32 devices in a mesh: group: 2 (over x), dp: 4 (over y, core), mp: 4 (over z).
Axes of the slice: x: 2, y: 2, z: 4, core: 2. Of those that a mesh axis runs over, the one named last changes fastest.
Arguments:
- query_passage_words: int32 [2, 12, 128], P('group'), may hold values from 0 to 16383, as said below
- difficult_distractors: int32 [12, 7], P('dp'), may hold values from 0 to 11
- vocabulary_vectors: bfloat16 [4096, 16384], P('dp'), may hold values from -6 to 6
- layer_weight_matrix: bfloat16 [4096, 4096], P('dp', 'mp'), may hold values from -0.09375 to 0.09375
- lowering_factor_matrix: bfloat16 [16, 4096], replicated, may hold values from -0.09375 to 0.09375
- raising_factor_matrix: bfloat16 [16, 4096], P(None, 'mp'), may hold values from -1.5 to 1.5
- logit_sharpness: float32 [1], replicated, may hold values from 10 to 500
Outputs:
- embeddings: bfloat16 [2, 12, 4096], P('group', 'dp', 'mp')
- losses: float32 [2, 12], P('group', 'dp')
- adapter_up_gradient: float32 [16, 4096], P(None, 'mp')
The draws below stay inside these ranges and needn't reach their ends.
Inputs may be any that keep to these rules, and one draw needn't show every extreme that they name: `query_passage_words`: id 0 is padding and fills only the end of a text; every text has at least 16 real tokens, and the first text of each side has 128. A query shares about half of its token slots with its paired passage.
All inputs are finite; a program needn't handle non-finite values.
Results may differ from the reference program's by a relative error of at most 0.018.
Values may be sent and summed in bfloat16 or wider, within the bound.
No kernel may reach another device: no remote copies, remote signals or barrier semaphores. Data moves between devices by JAX's collectives and lax.ppermute only.
A program may use at most 192 MiB of HBM per device.

```python
import jax
import jax.numpy as jnp
from jax import lax

MODEL_WIDTH = 4096
VOCAB = 16384
ADAPTER_RANK = 16
LEN = 128
NEG = 7
TEXT_TOTAL = 12


def draw_query_passage_words(key, part):
    key = jax.random.fold_in(key, 11)
    keys = jax.random.split(key, 4)
    passage = jax.random.randint(keys[0], (TEXT_TOTAL, LEN), 1, VOCAB)
    replaced = jax.random.randint(keys[1], (TEXT_TOTAL, LEN), 1, VOCAB)
    shared = jax.random.randint(keys[2], (TEXT_TOTAL, LEN), 0, 2)
    query = jnp.where(shared == 1, passage, replaced)
    lengths = jax.random.randint(keys[3], (2, TEXT_TOTAL), LEN // 8, LEN + 1)
    lengths = lengths.at[:, 0].set(LEN)
    slots = jnp.arange(LEN)
    both = jnp.stack([query, passage], axis=0)
    return jnp.where(slots[None, None, :] < lengths[:, :, None], both, 0).astype(jnp.int32)


def draw_logit_sharpness(key, part):
    key = jax.random.fold_in(key, 29)
    value = jax.random.uniform(key, (1,), jnp.float32, 30.0, 70.0)
    return value


def plant(result, rng, least, largest):
    spot = [jax.random.randint(jax.random.fold_in(rng, axis), (), 0, length) for axis, length in enumerate(result.shape)]
    longest = result.shape.index(max(result.shape))
    beside = spot[:longest] + [(spot[longest] + 1) % result.shape[longest]] + spot[longest + 1:]
    return result.at[tuple(spot)].set(least).at[tuple(beside)].set(largest)


def block_scale(stream_key, shape, pieces, smallest, top_value):
    def one(dim, parts):
        steps = jax.random.uniform(jax.random.fold_in(jax.random.fold_in(stream_key, 6), dim), (parts,), jnp.float32, smallest / len(pieces), top_value / len(pieces))
        return jnp.repeat(jnp.exp(steps), shape[dim] // parts).reshape((-1,) + (1,) * (len(shape) - dim - 1))

    gain = one(*pieces[0])
    for cut in pieces[1:]:
        gain = gain * one(*cut)
    return gain


def scatter_about(rng, extent, spread, bound, cuts=(), held_as=jnp.bfloat16):
    array = jax.random.normal(rng, extent, jnp.float32) * spread
    if len(cuts) > 0:
        array = block_scale(rng, extent, cuts, -0.22, 0.18) * array
    return jnp.clip(array, min=-bound, max=bound).astype(held_as)


def setup_inputs(seed: int = 0) -> dict:
    splits = jax.random.split(jax.random.key(seed), 8)
    query_passage_words = draw_query_passage_words(jax.random.fold_in(splits[7], 71), 0)
    difficult_distractors = plant(jax.random.randint(splits[1], (TEXT_TOTAL, NEG), 0, TEXT_TOTAL), jax.random.fold_in(splits[1], 1), 0, TEXT_TOTAL - 1).astype(jnp.int32)
    vocabulary_vectors = scatter_about(splits[2], (MODEL_WIDTH, VOCAB), 1.0, 6.0, ((0, 4),))
    layer_weight_matrix = scatter_about(splits[3], (MODEL_WIDTH, MODEL_WIDTH), MODEL_WIDTH ** -0.5, 0.09375, ((0, 4), (1, 4)))
    lowering_factor_matrix = scatter_about(splits[4], (ADAPTER_RANK, MODEL_WIDTH), MODEL_WIDTH ** -0.5, 0.09375)
    raising_factor_matrix = scatter_about(splits[5], (ADAPTER_RANK, MODEL_WIDTH), ADAPTER_RANK ** -0.5, 1.5, ((1, 4),))
    logit_sharpness = draw_logit_sharpness(jax.random.fold_in(splits[7], 71), 0)
    return {"query_passage_words": query_passage_words, "difficult_distractors": difficult_distractors, "vocabulary_vectors": vocabulary_vectors, "layer_weight_matrix": layer_weight_matrix, "lowering_factor_matrix": lowering_factor_matrix, "raising_factor_matrix": raising_factor_matrix, "logit_sharpness": logit_sharpness}


def encoder_block(token_identifiers, vocabulary_vectors, layer_weight_matrix, lowering_factor_matrix, raising_factor_matrix):
    inputs = jnp.take(vocabulary_vectors, token_identifiers.reshape(-1), axis=1).astype(jnp.float32)
    inverse = lax.rsqrt(lax.optimization_barrier(jnp.mean(inputs * inputs, axis=0)) + 1e-05)
    normed_state = (inputs * inverse[None, :]).astype(jnp.bfloat16)
    linear_map = lax.dot_general(layer_weight_matrix, normed_state, (((0,), (0,)), ((), ())), preferred_element_type=jnp.float32)
    reduced_sum = jnp.dot(lowering_factor_matrix, normed_state, preferred_element_type=jnp.float32).astype(jnp.bfloat16)
    linear_map = linear_map + lax.dot_general(raising_factor_matrix, reduced_sum, (((0,), (0,)), ((), ())), preferred_element_type=jnp.float32)
    hidden_state = inputs + jax.nn.silu(linear_map)
    return (hidden_state, linear_map, reduced_sum)

def token_mask(token_identifiers):
    mask = (token_identifiers != 0).astype(jnp.float32)
    return (mask, lax.optimization_barrier(jnp.sum(mask, axis=1)))

def reference(query_passage_words, difficult_distractors, vocabulary_vectors, layer_weight_matrix, lowering_factor_matrix, raising_factor_matrix, logit_sharpness):
    block_list = query_passage_words.reshape(2 * TEXT_TOTAL // 8, 8, LEN)

    def forward(token_identifiers):
        hidden_state, linear_map, reduced_sum = encoder_block(token_identifiers, vocabulary_vectors, layer_weight_matrix, lowering_factor_matrix, raising_factor_matrix)
        mask, counts = token_mask(token_identifiers)
        summed = jnp.einsum('dnl,nl->nd', hidden_state.reshape(MODEL_WIDTH, 8, LEN), mask)
        return (summed / counts[:, None]).astype(jnp.bfloat16)
    pooled = lax.map(forward, block_list).reshape(2 * TEXT_TOTAL, MODEL_WIDTH)
    wide = pooled.astype(jnp.float32)
    dots = lax.dot_general(pooled, pooled, (((1,), (1,)), ((), ())), preferred_element_type=jnp.float32)
    norms = lax.optimization_barrier(jnp.sum(wide * wide, axis=1))
    rnorm = lax.rsqrt(norms + 1e-06)
    cosine = dots * rnorm[:, None] * rnorm[None, :]
    multiplier_factor = logit_sharpness[0]
    scores = multiplier_factor * cosine
    row_ids = jnp.arange(2 * TEXT_TOTAL, dtype=jnp.int32)
    keep = row_ids[None, :] != row_ids[:, None]
    pair = (row_ids + TEXT_TOTAL) % (2 * TEXT_TOTAL)
    weight = (row_ids < TEXT_TOTAL).astype(jnp.float32)
    neg_cols = TEXT_TOTAL + jnp.concatenate([difficult_distractors, difficult_distractors], axis=0)
    top = lax.optimization_barrier(jnp.max(jnp.where(keep, scores, -jnp.inf), axis=1))
    safe_scores = jnp.where(keep, scores, top[:, None])
    expd = jnp.where(keep, jnp.exp(safe_scores - top[:, None]), 0.0)
    neg_exp = jnp.exp(jnp.minimum(jnp.take_along_axis(scores, neg_cols, axis=1) - top[:, None], 0.0)) * weight[:, None]
    total = lax.optimization_barrier(jnp.sum(expd, axis=1)) + lax.optimization_barrier(jnp.sum(neg_exp, axis=1))
    pair_score = jnp.take_along_axis(scores, pair[:, None], axis=1)[:, 0]
    losses = top + jnp.log(total) - pair_score
    onehot = (row_ids[None, None, :] == neg_cols[:, :, None]).astype(jnp.float32)
    probs = (expd + jnp.einsum('rk,rkc->rc', neg_exp, onehot)) / total[:, None]
    target = (row_ids[None, :] == pair[:, None]).astype(jnp.float32)
    grad_scores = (probs - target) / (2 * TEXT_TOTAL)
    coeff = (grad_scores * rnorm[:, None] * rnorm[None, :]).astype(jnp.bfloat16)
    along = jnp.dot(coeff, pooled, preferred_element_type=jnp.float32)
    radial = lax.optimization_barrier(jnp.sum(grad_scores * cosine, axis=1)) * rnorm * rnorm
    embedding_gradient = multiplier_factor * (along - radial[:, None] * wide)

    def backward_pass(carry, item):
        token_identifiers, grads = item
        hidden_state, linear_map, reduced_sum = encoder_block(token_identifiers, vocabulary_vectors, layer_weight_matrix, lowering_factor_matrix, raising_factor_matrix)
        mask, counts = token_mask(token_identifiers)
        token_grad = jnp.einsum('nd,nl->dnl', grads / counts[:, None], mask).reshape(MODEL_WIDTH, 8 * LEN)
        sigma = jax.nn.sigmoid(linear_map)
        local = (token_grad * sigma * (1.0 + linear_map * (1.0 - sigma))).astype(jnp.bfloat16)
        update = lax.dot_general(reduced_sum, local, (((1,), (1,)), ((), ())), preferred_element_type=jnp.float32)
        return (carry + update, None)
    start_offset = jnp.zeros((ADAPTER_RANK, MODEL_WIDTH), jnp.float32)
    adapter_up_gradient, unused_value = lax.scan(backward_pass, start_offset, (block_list, embedding_gradient.reshape(2 * TEXT_TOTAL // 8, 8, MODEL_WIDTH)))
    embeddings = (wide * rnorm[:, None]).astype(jnp.bfloat16).reshape(2, TEXT_TOTAL, MODEL_WIDTH)
    return (embeddings, losses.reshape(2, TEXT_TOTAL), adapter_up_gradient)
```

```python
import functools

import jax
import jax.numpy as jnp
from jax import lax
from jax.experimental import pallas as pl
from jax.experimental.pallas import tpu as pltpu
from jax.sharding import PartitionSpec as P


def general_body(
    query_passage_words,
    difficult_distractors,
    vocabulary_vectors,
    layer_weight_matrix,
    lowering_factor_matrix,
    raising_factor_matrix,
    logit_sharpness,
):
    group_index = lax.axis_index("group")
    shard_index = lax.axis_index("dp")
    part_index = lax.axis_index("mp")
    shard_count = lax.axis_size("dp")
    side_ids = query_passage_words[0]
    text_count = side_ids.shape[0]
    length = side_ids.shape[1]
    per_shard = text_count // shard_count
    own_ids = lax.dynamic_slice_in_dim(side_ids, shard_index * per_shard, per_shard, 0)
    columns = jnp.take(vocabulary_vectors, side_ids.reshape(-1), axis=1)
    inputs = lax.all_to_all(columns, "dp", split_axis=1, concat_axis=0, tiled=True)
    tokens = inputs.shape[1]
    feature_width = raising_factor_matrix.shape[1]
    wide_inputs = inputs.astype(jnp.float32)
    inverse = lax.rsqrt(jnp.mean(wide_inputs * wide_inputs, axis=0) + 1e-05)
    normed_state = (wide_inputs * inverse[None, :]).astype(jnp.bfloat16)
    linear_map = lax.dot_general(
        lax.all_gather(layer_weight_matrix, "dp", axis=0, tiled=True),
        normed_state,
        (((0,), (0,)), ((), ())),
        preferred_element_type=jnp.float32,
    )
    reduced_sum = jnp.dot(
        lowering_factor_matrix, normed_state, preferred_element_type=jnp.float32
    ).astype(jnp.bfloat16)
    linear_map = linear_map + lax.dot_general(
        raising_factor_matrix,
        reduced_sum,
        (((0,), (0,)), ((), ())),
        preferred_element_type=jnp.float32,
    )
    own_inputs = lax.dynamic_slice_in_dim(
        inputs, part_index * feature_width, feature_width, 0
    ).astype(jnp.float32)
    hidden_state = own_inputs + jax.nn.silu(linear_map)
    mask = (own_ids != 0).astype(jnp.float32)
    counts = jnp.sum(mask, axis=1)
    summed = jnp.einsum("dnl,nl->nd", hidden_state.reshape(feature_width, per_shard, length), mask)
    pooled = (summed / counts[:, None]).astype(jnp.bfloat16)
    gathered = lax.all_gather(pooled, ("group", "dp"), axis=0, tiled=True)
    part_scores = lax.dot_general(
        pooled, gathered, (((1,), (1,)), ((), ())), preferred_element_type=jnp.float32
    )
    gathered_wide = gathered.astype(jnp.float32)
    part_norms = jnp.sum(gathered_wide * gathered_wide, axis=1)
    dots, norms = lax.psum((part_scores, part_norms), "mp")
    rnorm_all = lax.rsqrt(norms + 1e-06)
    all_count = gathered.shape[0]
    half_count = all_count // 2
    own_rows = (
        group_index * half_count + shard_index * per_shard + jnp.arange(per_shard, dtype=jnp.int32)
    )
    rnorm_own = jnp.take(rnorm_all, own_rows)
    cosine = dots * rnorm_own[:, None] * rnorm_all[None, :]
    multiplier_factor = logit_sharpness[0]
    scores = multiplier_factor * cosine
    column_ids = jnp.arange(all_count, dtype=jnp.int32)
    keep = column_ids[None, :] != own_rows[:, None]
    pair = (own_rows + half_count) % all_count
    weight = (group_index == 0).astype(jnp.float32)
    neg_cols = half_count + difficult_distractors
    top = jnp.max(jnp.where(keep, scores, -jnp.inf), axis=1)
    safe_scores = jnp.where(keep, scores, top[:, None])
    expd = jnp.where(keep, jnp.exp(safe_scores - top[:, None]), 0.0)
    neg_exp = (
        jnp.exp(jnp.minimum(jnp.take_along_axis(scores, neg_cols, axis=1) - top[:, None], 0.0))
        * weight
    )
    total = jnp.sum(expd, axis=1) + jnp.sum(neg_exp, axis=1)
    pair_score = jnp.take_along_axis(scores, pair[:, None], axis=1)[:, 0]
    losses = top + jnp.log(total) - pair_score
    onehot = (column_ids[None, None, :] == neg_cols[:, :, None]).astype(jnp.float32)
    probs = (expd + jnp.einsum("rk,rkc->rc", neg_exp, onehot)) / total[:, None]
    target = (column_ids[None, :] == pair[:, None]).astype(jnp.float32)
    grad_scores = (probs - target) / all_count
    coeff = (grad_scores * rnorm_own[:, None] * rnorm_all[None, :]).astype(jnp.bfloat16)
    along = jnp.dot(coeff, gathered, preferred_element_type=jnp.float32)
    pooled_wide = pooled.astype(jnp.float32)
    radial = jnp.sum(grad_scores * cosine, axis=1) * rnorm_own * rnorm_own
    embedding_gradient = multiplier_factor * (along - radial[:, None] * pooled_wide)
    token_grad = jnp.einsum("nd,nl->dnl", embedding_gradient / counts[:, None], mask).reshape(
        feature_width, tokens
    )
    sigma = jax.nn.sigmoid(linear_map)
    local = (token_grad * sigma * (1.0 + linear_map * (1.0 - sigma))).astype(jnp.bfloat16)
    up_portion = lax.dot_general(
        reduced_sum, local, (((1,), (1,)), ((), ())), preferred_element_type=jnp.float32
    )
    adapter_up_gradient = lax.psum(up_portion, ("group", "dp"))
    embeddings = (pooled_wide * rnorm_own[:, None]).astype(jnp.bfloat16)[None]
    return (embeddings, losses[None], adapter_up_gradient)


IDS_PER_BLOCK = 1024
WINDOW = 128
CHUNK = 256
ROWS = 16
LANES = 128
NT = (((1,), (1,)), ((), ()))
VMEM_BYTES = 60 * 1024 * 1024


def mm(a, b, dims=(((1,), (0,)), ((), ()))):
    return lax.dot_general(a, b, dims, preferred_element_type=jnp.float32)


def split(x):
    high = x.astype(jnp.bfloat16)
    return high, (x - high.astype(jnp.float32)).astype(jnp.bfloat16)


def iota(shape, dim):
    return lax.broadcasted_iota(jnp.int32, shape, dim)


def quarter_of(dp_index, cores=2):
    return (dp_index % cores) * 2 + dp_index // cores


def project_kernel(
    ids_ref,
    hard_ref,
    vocab_ref,
    weight_ref,
    lower_ref,
    out00,
    out01,
    out10,
    out11,
    member_ref,
    held,
    weight,
    lower,
    rows32,
    values,
    turned,
    ranks,
    squares,
    residual,
    bounds,
    held_sems,
    weight_sems,
    lower_sem,
):
    texts, length = ids_ref.shape
    tokens = texts * length
    features, vocab = vocab_ref.shape
    blocks = vocab // IDS_PER_BLOCK
    chunks = tokens // CHUNK
    per_shard, negatives = hard_ref.shape
    width = weight.shape[2]
    outs = (out00, out01, out10, out11)
    shard = lax.axis_index("dp")
    core, side_y = lax.rem(shard, 2), lax.div(shard, 2)

    def vocab_copy(b):
        return pltpu.make_async_copy(
            vocab_ref.at[:, pl.ds(pl.multiple_of(b * IDS_PER_BLOCK, LANES), IDS_PER_BLOCK)],
            held.at[b],
            held_sems.at[b],
        )

    def weight_copy(i, j):
        quarter = (core ^ i) * 2 + (side_y ^ j)
        return pltpu.make_async_copy(
            weight_ref.at[:, pl.ds(pl.multiple_of(quarter * width, LANES), width)],
            weight.at[2 * i + j],
            weight_sems.at[2 * i + j],
        )

    lower_copy = pltpu.make_async_copy(
        lower_ref.at[:, pl.ds(pl.multiple_of(shard * features, LANES), features)], lower, lower_sem
    )
    vocab_copy(0).start()
    lower_copy.start()
    for i in range(2):
        for j in range(2):
            weight_copy(i, j).start()
    for b in range(1, blocks):
        vocab_copy(b).start()

    ids = ids_ref[...]
    valid = ids != 0
    block_of = jnp.where(valid, ids // IDS_PER_BLOCK, blocks)
    for b in range(blocks + 1):
        bounds[b] = jnp.sum((block_of < b).astype(jnp.float32)).astype(jnp.int32)
    block_rows = 8 * pl.cdiv(blocks + 1, 8)
    block_id = iota((block_rows, length), 0)
    below = jnp.zeros((block_rows, length), jnp.float32)
    for text in range(texts):
        below += jnp.where(block_of[text : text + 1] < block_id, 1.0, 0.0)
    before = jnp.broadcast_to(jnp.sum(below, axis=1, keepdims=True), (block_rows, length))
    earlier = jnp.where(iota((length, length), 0) < iota((length, length), 1), 1.0, 0.0).astype(
        jnp.bfloat16
    )
    for text in range(texts):
        here = jnp.where(block_of[text : text + 1] == block_id, 1.0, 0.0)
        inside = mm(here.astype(jnp.bfloat16), earlier)
        ranks[pl.ds(text, 1), :] = jnp.sum(here * (inside + before), axis=0, keepdims=True)
        before += jnp.broadcast_to(jnp.sum(here, axis=1, keepdims=True), (block_rows, length))
    text_of = iota((texts, length), 0)
    carried = jnp.where(valid, ids * ROWS + text_of, 0).astype(jnp.float32)
    rank = ranks[...]

    def place(p, carry):
        position = (iota((LANES, length), 0) + p * LANES).astype(jnp.float32)
        total = jnp.zeros((LANES, length), jnp.float32)
        for text in range(texts):
            total += jnp.where(rank[text : text + 1] == position, carried[text : text + 1], 0.0)
        found = jnp.sum(total, axis=1, keepdims=True).astype(jnp.int32)
        start = pl.multiple_of(p * LANES, LANES)
        values[pl.ds(start, LANES), :] = jnp.broadcast_to(found, (LANES, LANES))
        real = (found // ROWS != 0) & (lax.rem(found, ROWS) == iota((LANES, LANES), 1))
        member_ref[pl.ds(start, LANES), :] = jnp.where(real, 1.0, 0.0).astype(jnp.bfloat16)
        return carry

    lax.fori_loop(0, tokens // LANES, place, 0)
    values[pl.ds(tokens, WINDOW), :] = jnp.zeros((WINDOW, LANES), jnp.int32)

    def clear(p, carry):
        rows32[pl.ds(pl.multiple_of(p * LANES, LANES), LANES), :] = jnp.zeros(
            (LANES, features), jnp.float32
        )
        return carry

    lax.fori_loop(0, (tokens + WINDOW) // LANES, clear, 0)
    residual[...] = jnp.zeros_like(residual)
    squares[...] = jnp.zeros_like(squares)
    turned[...] = jnp.zeros_like(turned)
    turned[0:per_shard, chunks : chunks + negatives] = hard_ref[...].astype(jnp.float32)
    lower_copy.wait()
    for i in range(2):
        for j in range(2):
            weight_copy(i, j).wait()

    def project(k, carry):
        start = pl.multiple_of(k * CHUNK, CHUNK)
        x = rows32[pl.ds(start, CHUNK), :].astype(jnp.bfloat16)
        for q in range(4):
            outs[q][pl.ds(start, CHUNK), :] = mm(x, weight[q]).astype(jnp.bfloat16)
        reduced = mm(lower[...], x, NT).astype(jnp.bfloat16)
        place_at = pl.multiple_of(tokens + k * ROWS, ROWS)
        for q in range(4):
            outs[q][pl.ds(place_at, ROWS), :] = reduced
        ones = jnp.ones((ROWS, features), jnp.bfloat16)
        squares[pl.ds(k, 1), :] = mm(ones, x * x, NT)[0:1]
        member = member_ref[pl.ds(start, CHUNK), :].astype(jnp.float32).T.astype(jnp.bfloat16)
        residual[...] += mm(member[0:ROWS], x)
        return carry

    def zero(k, carry):
        start = pl.multiple_of(k * CHUNK, CHUNK)
        place_at = pl.multiple_of(tokens + k * ROWS, ROWS)
        for q in range(4):
            outs[q][pl.ds(start, CHUNK), :] = jnp.zeros((CHUNK, width), jnp.bfloat16)
            outs[q][pl.ds(place_at, ROWS), :] = jnp.zeros((ROWS, width), jnp.bfloat16)
        return carry

    def take(b, done):
        vocab_copy(b).wait()
        first, last = bounds[b], bounds[b + 1]
        aligned = (first // ROWS) * ROWS
        windows = jnp.where(last > first, (last - aligned + WINDOW - 1) // WINDOW, 0)

        def window(w, carry):
            start = pl.multiple_of(aligned + w * WINDOW, ROWS)
            wanted = values[pl.ds(start, WINDOW), :] // ROWS - b * IDS_PER_BLOCK
            wanted = jnp.concatenate([wanted] * (IDS_PER_BLOCK // LANES), axis=1)
            picked = jnp.where(wanted == iota((WINDOW, IDS_PER_BLOCK), 1), 1.0, 0.0)
            picked = jnp.where(wanted + b * IDS_PER_BLOCK == 0, 0.0, picked).astype(jnp.bfloat16)
            rows32[pl.ds(start, WINDOW), :] += mm(picked, held[b], NT)
            return carry

        lax.fori_loop(0, windows, window, 0)
        full = last // CHUNK
        lax.fori_loop(done, full, project, 0)
        return full

    done = lax.fori_loop(0, blocks, take, 0)
    used = (bounds[blocks] + CHUNK - 1) // CHUNK
    lax.fori_loop(done, used, project, 0)
    lax.fori_loop(used, chunks, zero, 0)

    hard = turned[...].T[0:ROWS]
    lane = iota((ROWS, width), 1)
    misc = jnp.concatenate([squares[...], jnp.zeros((ROWS - squares.shape[0], width), jnp.float32)])
    for i in range(per_shard):
        misc += jnp.where(lane == shard * per_shard + i, hard[:, i : i + 1], 0.0)
    misc = misc.astype(jnp.bfloat16)
    mine = lax.axis_index("mp") == shard
    for i in range(2):
        for j in range(2):
            quarter = (core ^ i) * 2 + (side_y ^ j)
            part = residual[:, pl.ds(pl.multiple_of(quarter * width, LANES), width)]
            out = outs[2 * i + j]
            out[pl.ds(tokens + chunks * ROWS, ROWS), :] = misc
            out[pl.ds(tokens + (chunks + 1) * ROWS, ROWS), :] = jnp.where(mine, part, 0.0).astype(
                jnp.bfloat16
            )


def pool_kernel(
    ids_ref,
    own_ref,
    core_ref,
    far_ref,
    member_ref,
    raise_ref,
    pooled_ref,
    slope_ref,
    reduced_ref,
    misc_ref,
    raised,
    model_width,
):
    texts, length = ids_ref.shape
    tokens = texts * length
    chunks = tokens // CHUNK
    width = own_ref.shape[1]
    quarter = quarter_of(lax.axis_index("dp"))

    def summed(start, size):
        rows = pl.ds(start, size)
        return (
            own_ref[rows, :].astype(jnp.float32)
            + core_ref[rows, :].astype(jnp.float32)
            + far_ref[rows, :].astype(jnp.float32)
        )

    misc = summed(tokens + chunks * ROWS, ROWS)
    misc_ref[...] = misc
    inverse = lax.rsqrt(misc / model_width + 1e-05)
    raised[...] = jnp.zeros_like(raised)
    raised[0:ROWS, :] = raise_ref[:, pl.ds(pl.multiple_of(quarter * width, LANES), width)]
    total = jnp.zeros((ROWS, width), jnp.float32)
    for k in range(chunks):
        scale = inverse[k : k + 1]
        reduced = (summed(tokens + k * ROWS, ROWS) * scale).astype(jnp.bfloat16)
        reduced_ref[:, k * CHUNK : (k + 1) * CHUNK] = reduced
        stacked = jnp.concatenate(
            [reduced.astype(jnp.float32), jnp.broadcast_to(scale, (LANES - ROWS, CHUNK))]
        )
        turned = stacked.T
        low = turned.astype(jnp.bfloat16)
        linear = summed(k * CHUNK, CHUNK) * turned[:, ROWS : ROWS + 1] + mm(low, raised[...])
        sigma = 1.0 / (1.0 + jnp.exp(-linear))
        slope_ref[pl.ds(k * CHUNK, CHUNK), :] = sigma * (1.0 + linear * (1.0 - sigma))
        member = member_ref[pl.ds(k * CHUNK, CHUNK), :].astype(jnp.float32).T
        member = member[0:ROWS].astype(jnp.bfloat16)
        high, rest = split(linear * sigma)
        total += mm(member, high) + mm(member, rest)
    total += summed(tokens + (chunks + 1) * ROWS, ROWS)
    counts = jnp.sum((ids_ref[...] != 0).astype(jnp.float32), axis=1, keepdims=True)
    pooled = total[0:texts] / counts
    pooled_ref[...] = jnp.zeros_like(pooled_ref)
    pooled_ref[0:texts, :] = pooled.astype(jnp.bfloat16)


def score_kernel(
    ids_ref,
    pooled_ref,
    misc_ref,
    slope_ref,
    reduced_ref,
    member_ref,
    sharp_ref,
    embed_ref,
    loss_ref,
    up_ref,
    shards,
    parts,
    negatives,
):
    texts, length = ids_ref.shape
    tokens = texts * length
    chunks = tokens // CHUNK
    rows = 2 * ROWS
    width = pooled_ref.shape[2]
    per_shard = loss_ref.shape[1]
    group, shard, part = lax.axis_index("group"), lax.axis_index("dp"), lax.axis_index("mp")
    places = shards * parts

    def both(place):
        return jnp.concatenate([pooled_ref[place], pooled_ref[places + place]], axis=0)

    dots = jnp.zeros((rows, rows), jnp.float32)
    for place in range(places):
        block = both(place)
        dots += mm(block, block, NT)
    down, across = iota((rows, rows), 0), iota((rows, rows), 1)
    same = down == across
    real = (lax.rem(down, ROWS) < texts) & (lax.rem(across, ROWS) < texts)
    diagonal = jnp.where(same, dots, 0.0)
    rnorm_row = lax.rsqrt(jnp.sum(diagonal, axis=0, keepdims=True) + 1e-06)
    rnorm_col = lax.rsqrt(jnp.sum(diagonal, axis=1, keepdims=True) + 1e-06)
    sharpness = sharp_ref[0]
    cosine = dots * rnorm_col * rnorm_row
    scores = sharpness * cosine
    keep = real & ~same
    top = jnp.max(jnp.where(keep, scores, -jnp.inf), axis=0, keepdims=True)
    top = jnp.where(lax.rem(across[0:1], ROWS) < texts, top, 0.0)
    powers = jnp.exp(jnp.where(real, jnp.minimum(scores - top, 0.0), 0.0))
    hard = misc_ref[chunks : chunks + negatives, 0:rows].astype(jnp.int32) + ROWS
    times = jnp.zeros((rows, rows), jnp.float32)
    for k in range(negatives):
        times += jnp.where(hard[k : k + 1] == down, 1.0, 0.0)
    times = jnp.where(across < texts, times, 0.0)
    weights = (jnp.where(keep, 1.0, 0.0) + jnp.where(real, times, 0.0)) * powers
    total = jnp.sum(weights, axis=0, keepdims=True)
    total = jnp.where(lax.rem(across[0:1], ROWS) < texts, total, 1.0)
    pair = (down == lax.rem(across + ROWS, rows)) & real
    pair_score = jnp.sum(jnp.where(pair, scores, 0.0), axis=0, keepdims=True)
    losses = top + jnp.log(total) - pair_score
    grad_scores = (weights / total - jnp.where(pair, 1.0, 0.0)) / (2 * texts)
    coeff = (grad_scores * rnorm_col * rnorm_row).astype(jnp.bfloat16)
    radial = jnp.sum(grad_scores * cosine, axis=0, keepdims=True) * rnorm_row * rnorm_row

    first = shard * per_shard
    loss_col = jnp.sum(jnp.where(same, losses, 0.0), axis=1, keepdims=True)
    at = (iota((rows, LANES), 0) == group * ROWS + first + iota((rows, LANES), 1)) & (
        iota((rows, LANES), 1) < per_shard
    )
    loss_ref[...] = jnp.sum(jnp.where(at, loss_col, 0.0), axis=0, keepdims=True)[:, 0:per_shard]

    place = shard * parts + part
    mine = both(place)
    along = mm(coeff.astype(jnp.float32).T.astype(jnp.bfloat16), mine)
    radial_col = jnp.sum(jnp.where(same, radial, 0.0), axis=1, keepdims=True)
    grad = sharpness * (along - radial_col * mine.astype(jnp.float32))
    grad = jnp.where(group == 0, grad[0:ROWS], grad[ROWS:rows])
    counts = jnp.sum((ids_ref[...] != 0).astype(jnp.float32), axis=1, keepdims=True)
    grad = grad[0:texts] / counts
    grad = jnp.concatenate([grad, jnp.zeros((LANES - texts, width), jnp.float32)])
    high, rest = split(grad)
    update = jnp.zeros((ROWS, width), jnp.float32)
    for k in range(chunks):
        member = member_ref[pl.ds(k * CHUNK, CHUNK), :]
        token_grad = mm(member, high) + mm(member, rest)
        local = (token_grad * slope_ref[pl.ds(k * CHUNK, CHUNK), :]).astype(jnp.bfloat16)
        update += mm(reduced_ref[:, k * CHUNK : (k + 1) * CHUNK], local)
    up_ref[...] = update

    rnorm_own = jnp.where(group == 0, rnorm_col[0:ROWS], rnorm_col[ROWS:rows])
    chosen = iota((ROWS, ROWS), 1) == iota((ROWS, ROWS), 0) + first
    chosen = jnp.where(chosen & (iota((ROWS, ROWS), 0) < per_shard), 1.0, 0.0).astype(jnp.bfloat16)
    for quarter in range(shards):
        holder = quarter_of(quarter, 2)
        block = pooled_ref[group * places + holder * parts + part].astype(jnp.float32) * rnorm_own
        picked = mm(chosen, block.astype(jnp.bfloat16)).astype(jnp.bfloat16)
        embed_ref[0, :, quarter * width : (quarter + 1) * width] = picked[0:per_shard]


def any_spec():
    return pl.BlockSpec(memory_space=pl.ANY)


def vmem_spec():
    return pl.BlockSpec(memory_space=pltpu.VMEM)


def smem_spec():
    return pl.BlockSpec(memory_space=pltpu.SMEM)


def split_body(
    query_passage_words,
    difficult_distractors,
    vocabulary_vectors,
    layer_weight_matrix,
    lowering_factor_matrix,
    raising_factor_matrix,
    logit_sharpness,
):
    shards, parts = lax.axis_size("dp"), lax.axis_size("mp")
    ids = query_passage_words[0]
    texts, length = ids.shape
    tokens = texts * length
    chunks = tokens // CHUNK
    features, vocab = vocabulary_vectors.shape
    blocks = vocab // IDS_PER_BLOCK
    per_shard, negatives = difficult_distractors.shape
    rank = lowering_factor_matrix.shape[0]
    part_width = layer_weight_matrix.shape[1]
    width = part_width // shards
    rows = tokens + (chunks + 2) * ROWS
    params = pltpu.CompilerParams(vmem_limit_bytes=VMEM_BYTES)
    half = jax.ShapeDtypeStruct((rows, width), jnp.bfloat16)
    own0, own1, away0, away1, member = pl.pallas_call(
        project_kernel,
        out_shape=[half] * 4 + [jax.ShapeDtypeStruct((tokens, LANES), jnp.bfloat16)],
        in_specs=[vmem_spec()] * 2 + [any_spec()] * 3,
        out_specs=[vmem_spec()] * 5,
        scratch_shapes=[
            pltpu.VMEM((blocks, features, IDS_PER_BLOCK), jnp.bfloat16),
            pltpu.VMEM((4, features, width), jnp.bfloat16),
            pltpu.VMEM((rank, features), jnp.bfloat16),
            pltpu.VMEM((tokens + WINDOW, features), jnp.float32),
            pltpu.VMEM((tokens + WINDOW, LANES), jnp.int32),
            pltpu.VMEM((LANES, LANES), jnp.float32),
            pltpu.VMEM((texts, length), jnp.float32),
            pltpu.VMEM((8, width), jnp.float32),
            pltpu.VMEM((ROWS, features), jnp.float32),
            pltpu.SMEM((blocks + 1,), jnp.int32),
            pltpu.SemaphoreType.DMA((blocks,)),
            pltpu.SemaphoreType.DMA((4,)),
            pltpu.SemaphoreType.DMA,
        ],
        compiler_params=params,
        name="project",
    )(
        ids,
        difficult_distractors,
        vocabulary_vectors,
        layer_weight_matrix,
        lowering_factor_matrix,
    )
    other_core = [(d, d ^ 1) for d in range(shards)]
    other_y = [(d, d ^ 2) for d in range(shards)]
    core1 = lax.ppermute(away1, "dp", other_core)
    core0 = lax.ppermute(away0, "dp", other_core)
    chip1 = (own1.astype(jnp.float32) + core1.astype(jnp.float32)).astype(jnp.bfloat16)
    far = lax.ppermute(chip1, "dp", other_y)
    pooled, slope, reduced, misc = pl.pallas_call(
        functools.partial(pool_kernel, model_width=float(features * shards)),
        out_shape=[
            jax.ShapeDtypeStruct((ROWS, width), jnp.bfloat16),
            jax.ShapeDtypeStruct((tokens, width), jnp.float32),
            jax.ShapeDtypeStruct((ROWS, tokens), jnp.bfloat16),
            jax.ShapeDtypeStruct((ROWS, width), jnp.float32),
        ],
        in_specs=[vmem_spec()] * 6,
        out_specs=[vmem_spec()] * 4,
        scratch_shapes=[pltpu.VMEM((LANES, width), jnp.bfloat16)],
        compiler_params=params,
        name="pool",
    )(ids, own0, core0, far, member, raising_factor_matrix)
    gathered = lax.all_gather(pooled, ("group", "dp", "mp"), axis=0)
    embeddings, losses, update = pl.pallas_call(
        functools.partial(score_kernel, shards=shards, parts=parts, negatives=negatives),
        out_shape=[
            jax.ShapeDtypeStruct((1, per_shard, part_width), jnp.bfloat16),
            jax.ShapeDtypeStruct((1, per_shard), jnp.float32),
            jax.ShapeDtypeStruct((ROWS, width), jnp.float32),
        ],
        in_specs=[vmem_spec()] * 6 + [smem_spec()],
        out_specs=[vmem_spec()] * 3,
        compiler_params=params,
        name="score",
    )(ids, gathered, misc, slope, reduced, member, logit_sharpness)
    updates = lax.all_gather(update, ("group", "dp"), axis=0)
    columns = [updates[quarter_of(q)] + updates[shards + quarter_of(q)] for q in range(shards)]
    return (embeddings, losses, jnp.concatenate(columns, axis=1))


def body(words, hard, vocabulary, weight, lowering, raising, sharpness):
    shards, parts = lax.axis_size("dp"), lax.axis_size("mp")
    texts, length = words.shape[1:]
    features, vocab = vocabulary.shape
    negatives = hard.shape[1]
    square = shards == 4 and features == weight.shape[1] and parts == shards
    small = texts <= ROWS - 2 and length == LANES and texts * length <= 2048
    even = (texts * length) % CHUNK == 0 and vocab % IDS_PER_BLOCK == 0
    fits = features * vocab <= 2**24 and features % (4 * LANES) == 0
    spare = texts * length // CHUNK + negatives <= ROWS and lowering.shape[0] == ROWS
    fast = square and small and even and fits and spare and lax.axis_size("group") == 2
    chosen = split_body if fast else general_body
    return chosen(words, hard, vocabulary, weight, lowering, raising, sharpness)


def solution(mesh):
    in_specs = (
        P("group", None, None),
        P("dp", None),
        P("dp", None),
        P("dp", "mp"),
        P(),
        P(None, "mp"),
        P(),
    )
    out_specs = (P("group", "dp", "mp"), P("group", "dp"), P(None, "mp"))
    return jax.shard_map(body, mesh=mesh, in_specs=in_specs, out_specs=out_specs, check_vma=False)
```

```python
import functools

import jax
import jax.numpy as jnp
from jax import lax
from jax.experimental import pallas as pl
from jax.experimental.pallas import tpu as pltpu
from jax.sharding import PartitionSpec as P


def general_body(
    query_passage_words,
    difficult_distractors,
    vocabulary_vectors,
    layer_weight_matrix,
    lowering_factor_matrix,
    raising_factor_matrix,
    logit_sharpness,
):
    group_index = lax.axis_index("group")
    shard_index = lax.axis_index("dp")
    part_index = lax.axis_index("mp")
    shard_count = lax.axis_size("dp")
    side_ids = query_passage_words[0]
    text_count = side_ids.shape[0]
    length = side_ids.shape[1]
    per_shard = text_count // shard_count
    own_ids = lax.dynamic_slice_in_dim(side_ids, shard_index * per_shard, per_shard, 0)
    columns = jnp.take(vocabulary_vectors, side_ids.reshape(-1), axis=1)
    inputs = lax.all_to_all(columns, "dp", split_axis=1, concat_axis=0, tiled=True)
    tokens = inputs.shape[1]
    feature_width = raising_factor_matrix.shape[1]
    wide_inputs = inputs.astype(jnp.float32)
    inverse = lax.rsqrt(jnp.mean(wide_inputs * wide_inputs, axis=0) + 1e-05)
    normed_state = (wide_inputs * inverse[None, :]).astype(jnp.bfloat16)
    linear_map = lax.dot_general(
        lax.all_gather(layer_weight_matrix, "dp", axis=0, tiled=True),
        normed_state,
        (((0,), (0,)), ((), ())),
        preferred_element_type=jnp.float32,
    )
    reduced_sum = jnp.dot(
        lowering_factor_matrix, normed_state, preferred_element_type=jnp.float32
    ).astype(jnp.bfloat16)
    linear_map = linear_map + lax.dot_general(
        raising_factor_matrix,
        reduced_sum,
        (((0,), (0,)), ((), ())),
        preferred_element_type=jnp.float32,
    )
    own_inputs = lax.dynamic_slice_in_dim(
        inputs, part_index * feature_width, feature_width, 0
    ).astype(jnp.float32)
    hidden_state = own_inputs + jax.nn.silu(linear_map)
    mask = (own_ids != 0).astype(jnp.float32)
    counts = jnp.sum(mask, axis=1)
    summed = jnp.einsum("dnl,nl->nd", hidden_state.reshape(feature_width, per_shard, length), mask)
    pooled = (summed / counts[:, None]).astype(jnp.bfloat16)
    gathered = lax.all_gather(pooled, ("group", "dp"), axis=0, tiled=True)
    part_scores = lax.dot_general(
        pooled, gathered, (((1,), (1,)), ((), ())), preferred_element_type=jnp.float32
    )
    gathered_wide = gathered.astype(jnp.float32)
    part_norms = jnp.sum(gathered_wide * gathered_wide, axis=1)
    dots, norms = lax.psum((part_scores, part_norms), "mp")
    rnorm_all = lax.rsqrt(norms + 1e-06)
    all_count = gathered.shape[0]
    half_count = all_count // 2
    own_rows = (
        group_index * half_count + shard_index * per_shard + jnp.arange(per_shard, dtype=jnp.int32)
    )
    rnorm_own = jnp.take(rnorm_all, own_rows)
    cosine = dots * rnorm_own[:, None] * rnorm_all[None, :]
    multiplier_factor = logit_sharpness[0]
    scores = multiplier_factor * cosine
    column_ids = jnp.arange(all_count, dtype=jnp.int32)
    keep = column_ids[None, :] != own_rows[:, None]
    pair = (own_rows + half_count) % all_count
    weight = (group_index == 0).astype(jnp.float32)
    neg_cols = half_count + difficult_distractors
    top = jnp.max(jnp.where(keep, scores, -jnp.inf), axis=1)
    safe_scores = jnp.where(keep, scores, top[:, None])
    expd = jnp.where(keep, jnp.exp(safe_scores - top[:, None]), 0.0)
    neg_exp = (
        jnp.exp(jnp.minimum(jnp.take_along_axis(scores, neg_cols, axis=1) - top[:, None], 0.0))
        * weight
    )
    total = jnp.sum(expd, axis=1) + jnp.sum(neg_exp, axis=1)
    pair_score = jnp.take_along_axis(scores, pair[:, None], axis=1)[:, 0]
    losses = top + jnp.log(total) - pair_score
    onehot = (column_ids[None, None, :] == neg_cols[:, :, None]).astype(jnp.float32)
    probs = (expd + jnp.einsum("rk,rkc->rc", neg_exp, onehot)) / total[:, None]
    target = (column_ids[None, :] == pair[:, None]).astype(jnp.float32)
    grad_scores = (probs - target) / all_count
    coeff = (grad_scores * rnorm_own[:, None] * rnorm_all[None, :]).astype(jnp.bfloat16)
    along = jnp.dot(coeff, gathered, preferred_element_type=jnp.float32)
    pooled_wide = pooled.astype(jnp.float32)
    radial = jnp.sum(grad_scores * cosine, axis=1) * rnorm_own * rnorm_own
    embedding_gradient = multiplier_factor * (along - radial[:, None] * pooled_wide)
    token_grad = jnp.einsum("nd,nl->dnl", embedding_gradient / counts[:, None], mask).reshape(
        feature_width, tokens
    )
    sigma = jax.nn.sigmoid(linear_map)
    local = (token_grad * sigma * (1.0 + linear_map * (1.0 - sigma))).astype(jnp.bfloat16)
    up_portion = lax.dot_general(
        reduced_sum, local, (((1,), (1,)), ((), ())), preferred_element_type=jnp.float32
    )
    adapter_up_gradient = lax.psum(up_portion, ("group", "dp"))
    embeddings = (pooled_wide * rnorm_own[:, None]).astype(jnp.bfloat16)[None]
    return (embeddings, losses[None], adapter_up_gradient)


BLOCK_BITS, WINDOW_BITS, CHUNK_BITS, ROW_BITS = 10, 7, 8, 4
IDS_PER_BLOCK = 1 << BLOCK_BITS
WINDOW = 1 << WINDOW_BITS
CHUNK = 1 << CHUNK_BITS
ROWS = 1 << ROW_BITS
LANES = 128
NT = (((1,), (1,)), ((), ()))
VMEM_BYTES = 60 * 1024 * 1024


def mm(a, b, dims=(((1,), (0,)), ((), ()))):
    return lax.dot_general(a, b, dims, preferred_element_type=jnp.float32)


def split(x):
    high = x.astype(jnp.bfloat16)
    return high, (x - high.astype(jnp.float32)).astype(jnp.bfloat16)


def iota(shape, dim):
    return lax.broadcasted_iota(jnp.int32, shape, dim)


def quarter_of(dp_index, cores=2):
    return (dp_index % cores) * 2 + dp_index // cores


def project_kernel(
    ids_ref,
    hard_ref,
    vocab_ref,
    weight_ref,
    lower_ref,
    out00,
    out01,
    out10,
    out11,
    member_ref,
    held,
    weight,
    lower,
    gathered,
    values,
    turned,
    ranks,
    squares,
    residual,
    counted,
    bounds,
    held_sems,
    weight_sems,
    lower_sem,
    bounds_sem,
):
    texts, length = ids_ref.shape
    tokens = texts * length
    features, vocab = vocab_ref.shape
    blocks = vocab // IDS_PER_BLOCK
    chunks = tokens // CHUNK
    per_shard, negatives = hard_ref.shape
    width = weight.shape[2]
    outs = (out00, out01, out10, out11)
    shard = lax.axis_index("dp")
    core, side_y = lax.rem(shard, 2), lax.div(shard, 2)

    def vocab_copy(b):
        return pltpu.make_async_copy(
            vocab_ref.at[:, pl.ds(pl.multiple_of(b * IDS_PER_BLOCK, LANES), IDS_PER_BLOCK)],
            held.at[b],
            held_sems.at[b],
        )

    def weight_copy(i, j):
        quarter = (core ^ i) * 2 + (side_y ^ j)
        return pltpu.make_async_copy(
            weight_ref.at[:, pl.ds(pl.multiple_of(quarter * width, LANES), width)],
            weight.at[2 * i + j],
            weight_sems.at[2 * i + j],
        )

    lower_copy = pltpu.make_async_copy(
        lower_ref.at[:, pl.ds(pl.multiple_of(shard * features, LANES), features)], lower, lower_sem
    )
    vocab_copy(0).start()
    lower_copy.start()
    for i in range(2):
        for j in range(2):
            weight_copy(i, j).start()
    for b in range(1, blocks):
        vocab_copy(b).start()

    ids = ids_ref[...]
    valid = ids != 0
    block_of = jnp.where(valid, lax.shift_right_logical(ids, BLOCK_BITS), blocks)
    block_rows = counted.shape[0]
    block_id = iota((block_rows, length), 0)
    below = jnp.zeros((block_rows, length), jnp.float32)
    for text in range(texts):
        below += jnp.where(block_of[text : text + 1] < block_id, 1.0, 0.0)
    before = jnp.broadcast_to(jnp.sum(below, axis=1, keepdims=True), (block_rows, length))
    counted[...] = before.astype(jnp.int32)
    bounds_copy = pltpu.make_async_copy(counted, bounds, bounds_sem)
    bounds_copy.start()
    earlier = jnp.where(iota((length, length), 0) < iota((length, length), 1), 1.0, 0.0).astype(
        jnp.bfloat16
    )
    for text in range(texts):
        here = jnp.where(block_of[text : text + 1] == block_id, 1.0, 0.0)
        inside = mm(here.astype(jnp.bfloat16), earlier)
        ranks[pl.ds(text, 1), :] = jnp.sum(here * (inside + before), axis=0, keepdims=True)
        before += jnp.broadcast_to(jnp.sum(here, axis=1, keepdims=True), (block_rows, length))
    text_of = iota((texts, length), 0)
    carried = jnp.where(valid, lax.shift_left(ids, ROW_BITS) + text_of, 0).astype(jnp.float32)
    rank = ranks[...]

    def place(p, carry):
        position = (iota((LANES, length), 0) + p * LANES).astype(jnp.float32)
        total = jnp.zeros((LANES, length), jnp.float32)
        for text in range(texts):
            total += jnp.where(rank[text : text + 1] == position, carried[text : text + 1], 0.0)
        found = jnp.broadcast_to(jnp.sum(total, axis=1, keepdims=True), (LANES, LANES))
        found = found.astype(jnp.int32)
        token = lax.shift_right_logical(found, ROW_BITS)
        start = pl.multiple_of(p * LANES, LANES)
        values[pl.ds(start, LANES), :] = jnp.where(token == 0, -vocab, token)
        real = (token != 0) & ((found & (ROWS - 1)) == iota((LANES, LANES), 1))
        member_ref[pl.ds(start, LANES), :] = jnp.where(real, 1.0, 0.0).astype(jnp.bfloat16)
        gathered[pl.ds(start, LANES), :] = jnp.zeros((LANES, features), jnp.bfloat16)
        return carry

    lax.fori_loop(0, tokens // LANES, place, 0)
    values[pl.ds(tokens, WINDOW), :] = jnp.full((WINDOW, LANES), -vocab, jnp.int32)
    gathered[pl.ds(tokens, WINDOW), :] = jnp.zeros((WINDOW, features), jnp.bfloat16)
    residual[...] = jnp.zeros_like(residual)
    squares[...] = jnp.zeros_like(squares)
    turned[...] = jnp.zeros_like(turned)
    turned[0:per_shard, chunks : chunks + negatives] = hard_ref[...].astype(jnp.float32)
    lower_copy.wait()
    for i in range(2):
        for j in range(2):
            weight_copy(i, j).wait()

    def project(k, carry):
        start = pl.multiple_of(k * CHUNK, CHUNK)
        x = gathered[pl.ds(start, CHUNK), :]
        for q in range(4):
            outs[q][pl.ds(start, CHUNK), :] = mm(x, weight[q]).astype(jnp.bfloat16)
        reduced = mm(lower[...], x, NT).astype(jnp.bfloat16)
        place_at = pl.multiple_of(tokens + k * ROWS, ROWS)
        for q in range(4):
            outs[q][pl.ds(place_at, ROWS), :] = reduced
        ones = jnp.ones((ROWS, features), jnp.bfloat16)
        squares[pl.ds(k, 1), :] = mm(ones, x * x, NT)[0:1]
        member = member_ref[pl.ds(start, CHUNK), :].astype(jnp.float32).T.astype(jnp.bfloat16)
        residual[...] += mm(member[0:ROWS], x)
        return carry

    def zero(k, carry):
        start = pl.multiple_of(k * CHUNK, CHUNK)
        place_at = pl.multiple_of(tokens + k * ROWS, ROWS)
        for q in range(4):
            outs[q][pl.ds(start, CHUNK), :] = jnp.zeros((CHUNK, width), jnp.bfloat16)
            outs[q][pl.ds(place_at, ROWS), :] = jnp.zeros((ROWS, width), jnp.bfloat16)
        return carry

    def take(b, done):
        vocab_copy(b).wait()
        first, last = bounds[b, 0], bounds[b + 1, 0]
        aligned = lax.shift_left(lax.shift_right_logical(first, ROW_BITS), ROW_BITS)
        windows = lax.shift_right_logical(last - aligned + WINDOW - 1, WINDOW_BITS)
        windows = jnp.where(last > first, windows, 0)

        def window(w, carry):
            start = pl.multiple_of(aligned + w * WINDOW, ROWS)
            wanted = values[pl.ds(start, WINDOW), :] - (b * IDS_PER_BLOCK + iota((WINDOW, LANES), 1))
            picked = [
                jnp.where(wanted == j * LANES, 1.0, 0.0).astype(jnp.bfloat16)
                for j in range(IDS_PER_BLOCK // LANES)
            ]
            found = mm(jnp.concatenate(picked, axis=1), held[b], NT)
            gathered[pl.ds(start, WINDOW), :] += found.astype(jnp.bfloat16)
            return carry

        lax.fori_loop(0, windows, window, 0)
        full = lax.shift_right_logical(last, CHUNK_BITS)
        lax.fori_loop(done, full, project, 0)
        return full

    bounds_copy.wait()
    done = lax.fori_loop(0, blocks, take, 0)
    used = lax.shift_right_logical(bounds[blocks, 0] + CHUNK - 1, CHUNK_BITS)
    lax.fori_loop(done, used, project, 0)
    lax.fori_loop(used, chunks, zero, 0)

    hard = turned[...].T[0:ROWS]
    lane = iota((ROWS, width), 1)
    misc = jnp.concatenate([squares[...], jnp.zeros((ROWS - squares.shape[0], width), jnp.float32)])
    for i in range(per_shard):
        misc += jnp.where(lane == shard * per_shard + i, hard[:, i : i + 1], 0.0)
    misc = misc.astype(jnp.bfloat16)
    mine = lax.axis_index("mp") == shard
    for i in range(2):
        for j in range(2):
            quarter = (core ^ i) * 2 + (side_y ^ j)
            part = residual[:, pl.ds(pl.multiple_of(quarter * width, LANES), width)]
            out = outs[2 * i + j]
            out[pl.ds(tokens + chunks * ROWS, ROWS), :] = misc
            out[pl.ds(tokens + (chunks + 1) * ROWS, ROWS), :] = jnp.where(mine, part, 0.0).astype(
                jnp.bfloat16
            )


def pool_kernel(
    ids_ref,
    own_ref,
    core_ref,
    far_ref,
    member_ref,
    raise_ref,
    pooled_ref,
    slope_ref,
    reduced_ref,
    misc_ref,
    raised,
    model_width,
):
    texts, length = ids_ref.shape
    tokens = texts * length
    chunks = tokens // CHUNK
    width = own_ref.shape[1]
    quarter = quarter_of(lax.axis_index("dp"))

    def summed(start, size):
        rows = pl.ds(start, size)
        return (
            own_ref[rows, :].astype(jnp.float32)
            + core_ref[rows, :].astype(jnp.float32)
            + far_ref[rows, :].astype(jnp.float32)
        )

    misc = summed(tokens + chunks * ROWS, ROWS)
    misc_ref[...] = misc
    inverse = lax.rsqrt(misc / model_width + 1e-05)
    raised[...] = jnp.zeros_like(raised)
    raised[0:ROWS, :] = raise_ref[:, pl.ds(pl.multiple_of(quarter * width, LANES), width)]
    total = jnp.zeros((ROWS, width), jnp.float32)
    for k in range(chunks):
        scale = inverse[k : k + 1]
        reduced = (summed(tokens + k * ROWS, ROWS) * scale).astype(jnp.bfloat16)
        reduced_ref[:, k * CHUNK : (k + 1) * CHUNK] = reduced
        stacked = jnp.concatenate(
            [reduced.astype(jnp.float32), jnp.broadcast_to(scale, (LANES - ROWS, CHUNK))]
        )
        turned = stacked.T
        low = turned.astype(jnp.bfloat16)
        linear = summed(k * CHUNK, CHUNK) * turned[:, ROWS : ROWS + 1] + mm(low, raised[...])
        sigma = 1.0 / (1.0 + jnp.exp(-linear))
        slope_ref[pl.ds(k * CHUNK, CHUNK), :] = sigma * (1.0 + linear * (1.0 - sigma))
        member = member_ref[pl.ds(k * CHUNK, CHUNK), :].astype(jnp.float32).T
        member = member[0:ROWS].astype(jnp.bfloat16)
        high, rest = split(linear * sigma)
        total += mm(member, high) + mm(member, rest)
    total += summed(tokens + (chunks + 1) * ROWS, ROWS)
    counts = jnp.sum((ids_ref[...] != 0).astype(jnp.float32), axis=1, keepdims=True)
    pooled = total[0:texts] / counts
    pooled_ref[...] = jnp.zeros_like(pooled_ref)
    pooled_ref[0:texts, :] = pooled.astype(jnp.bfloat16)


def pair_up(near, far, group):
    first = jnp.where(group == 0, near, far)
    return jnp.concatenate([first, jnp.where(group == 0, far, near)], axis=0)


def dots_kernel(*refs, shards):
    blocks, dots_ref = refs[:-1], refs[-1]
    group = lax.axis_index("group")
    dots = jnp.zeros(dots_ref.shape, jnp.float32)
    pairs = [pair_up(blocks[o][...], blocks[o + shards][...], group) for o in range(shards)]
    for o in (0, 2):
        dots += mm(pairs[o], pairs[o], NT) + mm(pairs[o + 1], pairs[o + 1], NT)
    dots_ref[...] = dots


def score_kernel(
    ids_ref,
    near0,
    near1,
    near2,
    near3,
    far0,
    dots0,
    dots1,
    dots2,
    dots3,
    misc_ref,
    slope_ref,
    reduced_ref,
    member_ref,
    sharp_ref,
    embed_ref,
    loss_ref,
    up_ref,
    negatives,
):
    texts, length = ids_ref.shape
    tokens = texts * length
    chunks = tokens // CHUNK
    rows = 2 * ROWS
    width = near0.shape[1]
    per_shard = loss_ref.shape[1]
    group, shard = lax.axis_index("group"), lax.axis_index("dp")
    dots = (dots0[...] + dots1[...]) + (dots2[...] + dots3[...])
    down, across = iota((rows, rows), 0), iota((rows, rows), 1)
    same = down == across
    real = (lax.rem(down, ROWS) < texts) & (lax.rem(across, ROWS) < texts)
    diagonal = jnp.where(same, dots, 0.0)
    rnorm_row = lax.rsqrt(jnp.sum(diagonal, axis=0, keepdims=True) + 1e-06)
    rnorm_col = lax.rsqrt(jnp.sum(diagonal, axis=1, keepdims=True) + 1e-06)
    sharpness = sharp_ref[0]
    cosine = dots * rnorm_col * rnorm_row
    scores = sharpness * cosine
    keep = real & ~same
    top = jnp.max(jnp.where(keep, scores, -jnp.inf), axis=0, keepdims=True)
    top = jnp.where(lax.rem(across[0:1], ROWS) < texts, top, 0.0)
    powers = jnp.exp(jnp.where(real, jnp.minimum(scores - top, 0.0), 0.0))
    hard = misc_ref[chunks : chunks + negatives, 0:rows].astype(jnp.int32) + ROWS
    times = jnp.zeros((rows, rows), jnp.float32)
    for k in range(negatives):
        times += jnp.where(hard[k : k + 1] == down, 1.0, 0.0)
    times = jnp.where(across < texts, times, 0.0)
    weights = (jnp.where(keep, 1.0, 0.0) + jnp.where(real, times, 0.0)) * powers
    total = jnp.sum(weights, axis=0, keepdims=True)
    total = jnp.where(lax.rem(across[0:1], ROWS) < texts, total, 1.0)
    pair = (down == lax.rem(across + ROWS, rows)) & real
    pair_score = jnp.sum(jnp.where(pair, scores, 0.0), axis=0, keepdims=True)
    losses = top + jnp.log(total) - pair_score
    grad_scores = (weights / total - jnp.where(pair, 1.0, 0.0)) / (2 * texts)
    coeff = (grad_scores * rnorm_col * rnorm_row).astype(jnp.bfloat16)
    radial = jnp.sum(grad_scores * cosine, axis=0, keepdims=True) * rnorm_row * rnorm_row

    first = shard * per_shard
    loss_col = jnp.sum(jnp.where(same, losses, 0.0), axis=1, keepdims=True)
    at = (iota((rows, LANES), 0) == group * ROWS + first + iota((rows, LANES), 1)) & (
        iota((rows, LANES), 1) < per_shard
    )
    loss_ref[...] = jnp.sum(jnp.where(at, loss_col, 0.0), axis=0, keepdims=True)[:, 0:per_shard]

    mine = pair_up(near0[...], far0[...], group)
    along = mm(coeff.astype(jnp.float32).T.astype(jnp.bfloat16), mine)
    radial_col = jnp.sum(jnp.where(same, radial, 0.0), axis=1, keepdims=True)
    grad = sharpness * (along - radial_col * mine.astype(jnp.float32))
    grad = jnp.where(group == 0, grad[0:ROWS], grad[ROWS:rows])
    counts = jnp.sum((ids_ref[...] != 0).astype(jnp.float32), axis=1, keepdims=True)
    grad = grad[0:texts] / counts
    grad = jnp.concatenate([grad, jnp.zeros((LANES - texts, width), jnp.float32)])
    high, rest = split(grad)
    update = jnp.zeros((ROWS, width), jnp.float32)
    for k in range(chunks):
        member = member_ref[pl.ds(k * CHUNK, CHUNK), :]
        token_grad = mm(member, high) + mm(member, rest)
        local = (token_grad * slope_ref[pl.ds(k * CHUNK, CHUNK), :]).astype(jnp.bfloat16)
        update += mm(reduced_ref[:, k * CHUNK : (k + 1) * CHUNK], local)
    up_ref[...] = update

    rnorm_own = jnp.where(group == 0, rnorm_col[0:ROWS], rnorm_col[ROWS:rows])
    chosen = iota((ROWS, ROWS), 1) == iota((ROWS, ROWS), 0) + first
    chosen = jnp.where(chosen & (iota((ROWS, ROWS), 0) < per_shard), 1.0, 0.0).astype(jnp.bfloat16)
    for o, near in enumerate((near0, near1, near2, near3)):
        block = near[...].astype(jnp.float32) * rnorm_own
        picked = mm(chosen, block.astype(jnp.bfloat16)).astype(jnp.bfloat16)
        at = pl.multiple_of(quarter_of(shard ^ o) * width, LANES)
        embed_ref[0, :, pl.ds(at, width)] = picked[0:per_shard]


def any_spec():
    return pl.BlockSpec(memory_space=pl.ANY)


def vmem_spec():
    return pl.BlockSpec(memory_space=pltpu.VMEM)


def smem_spec():
    return pl.BlockSpec(memory_space=pltpu.SMEM)


def exchange(x, axes, size):
    steps = [[(i, i ^ o) for i in range(size)] for o in range(1, size)]
    return [x] + [lax.ppermute(x, axes, step) for step in steps]


def split_body(
    query_passage_words,
    difficult_distractors,
    vocabulary_vectors,
    layer_weight_matrix,
    lowering_factor_matrix,
    raising_factor_matrix,
    logit_sharpness,
):
    shards, parts = lax.axis_size("dp"), lax.axis_size("mp")
    ids = query_passage_words[0]
    texts, length = ids.shape
    tokens = texts * length
    chunks = tokens // CHUNK
    features, vocab = vocabulary_vectors.shape
    blocks = vocab // IDS_PER_BLOCK
    block_rows = 8 * pl.cdiv(blocks + 1, 8)
    per_shard, negatives = difficult_distractors.shape
    rank = lowering_factor_matrix.shape[0]
    part_width = layer_weight_matrix.shape[1]
    width = part_width // shards
    rows = tokens + (chunks + 2) * ROWS
    params = pltpu.CompilerParams(vmem_limit_bytes=VMEM_BYTES)
    half = jax.ShapeDtypeStruct((rows, width), jnp.bfloat16)
    own0, own1, away0, away1, member = pl.pallas_call(
        project_kernel,
        out_shape=[half] * 4 + [jax.ShapeDtypeStruct((tokens, LANES), jnp.bfloat16)],
        in_specs=[vmem_spec()] * 2 + [any_spec()] * 3,
        out_specs=[vmem_spec()] * 5,
        scratch_shapes=[
            pltpu.VMEM((blocks, features, IDS_PER_BLOCK), jnp.bfloat16),
            pltpu.VMEM((4, features, width), jnp.bfloat16),
            pltpu.VMEM((rank, features), jnp.bfloat16),
            pltpu.VMEM((tokens + WINDOW, features), jnp.bfloat16),
            pltpu.VMEM((tokens + WINDOW, LANES), jnp.int32),
            pltpu.VMEM((LANES, LANES), jnp.float32),
            pltpu.VMEM((texts, length), jnp.float32),
            pltpu.VMEM((8, width), jnp.float32),
            pltpu.VMEM((ROWS, features), jnp.float32),
            pltpu.VMEM((block_rows, length), jnp.int32),
            pltpu.SMEM((block_rows, length), jnp.int32),
            pltpu.SemaphoreType.DMA((blocks,)),
            pltpu.SemaphoreType.DMA((4,)),
            pltpu.SemaphoreType.DMA,
            pltpu.SemaphoreType.DMA,
        ],
        compiler_params=params,
        name="project",
    )(
        ids,
        difficult_distractors,
        vocabulary_vectors,
        layer_weight_matrix,
        lowering_factor_matrix,
    )
    other_core = [(d, d ^ 1) for d in range(shards)]
    other_y = [(d, d ^ 2) for d in range(shards)]
    core1 = lax.ppermute(away1, "dp", other_core)
    core0 = lax.ppermute(away0, "dp", other_core)
    chip1 = (own1.astype(jnp.float32) + core1.astype(jnp.float32)).astype(jnp.bfloat16)
    far = lax.ppermute(chip1, "dp", other_y)
    pooled, slope, reduced, misc = pl.pallas_call(
        functools.partial(pool_kernel, model_width=float(features * shards)),
        out_shape=[
            jax.ShapeDtypeStruct((ROWS, width), jnp.bfloat16),
            jax.ShapeDtypeStruct((tokens, width), jnp.float32),
            jax.ShapeDtypeStruct((ROWS, tokens), jnp.bfloat16),
            jax.ShapeDtypeStruct((ROWS, width), jnp.float32),
        ],
        in_specs=[vmem_spec()] * 6,
        out_specs=[vmem_spec()] * 4,
        scratch_shapes=[pltpu.VMEM((LANES, width), jnp.bfloat16)],
        compiler_params=params,
        name="pool",
    )(ids, own0, core0, far, member, raising_factor_matrix)
    blocks8 = exchange(pooled, ("group", "dp"), 2 * shards)
    dots = pl.pallas_call(
        functools.partial(dots_kernel, shards=shards),
        out_shape=jax.ShapeDtypeStruct((2 * ROWS, 2 * ROWS), jnp.float32),
        in_specs=[vmem_spec()] * 8,
        out_specs=vmem_spec(),
        compiler_params=params,
        name="dots",
    )(*blocks8)
    dots4 = exchange(dots, "mp", parts)
    embeddings, losses, update = pl.pallas_call(
        functools.partial(score_kernel, negatives=negatives),
        out_shape=[
            jax.ShapeDtypeStruct((1, per_shard, part_width), jnp.bfloat16),
            jax.ShapeDtypeStruct((1, per_shard), jnp.float32),
            jax.ShapeDtypeStruct((ROWS, width), jnp.float32),
        ],
        in_specs=[vmem_spec()] * 14 + [smem_spec()],
        out_specs=[vmem_spec()] * 3,
        compiler_params=params,
        name="score",
    )(ids, *blocks8[:5], *dots4, misc, slope, reduced, member, logit_sharpness)
    updates = exchange(update, ("group", "dp"), 2 * shards)
    sums = [updates[o] + updates[o + shards] for o in range(shards)]
    shard = lax.axis_index("dp")
    columns = [lax.select_n(shard ^ quarter_of(q), *sums) for q in range(shards)]
    return (embeddings, losses, jnp.concatenate(columns, axis=1))


def body(words, hard, vocabulary, weight, lowering, raising, sharpness):
    shards, parts = lax.axis_size("dp"), lax.axis_size("mp")
    texts, length = words.shape[1:]
    features, vocab = vocabulary.shape
    negatives = hard.shape[1]
    square = shards == 4 and features == weight.shape[1] and parts == shards
    small = texts <= ROWS - 2 and length == LANES and texts * length <= 2048
    even = (texts * length) % CHUNK == 0 and vocab % IDS_PER_BLOCK == 0
    fits = features * vocab <= 2**24 and features % (4 * LANES) == 0
    spare = texts * length // CHUNK + negatives <= ROWS and lowering.shape[0] == ROWS
    fast = square and small and even and fits and spare and lax.axis_size("group") == 2
    chosen = split_body if fast else general_body
    return chosen(words, hard, vocabulary, weight, lowering, raising, sharpness)


def solution(mesh):
    in_specs = (
        P("group", None, None),
        P("dp", None),
        P("dp", None),
        P("dp", "mp"),
        P(),
        P(None, "mp"),
        P(),
    )
    out_specs = (P("group", "dp", "mp"), P("group", "dp"), P(None, "mp"))
    return jax.shard_map(body, mesh=mesh, in_specs=in_specs, out_specs=out_specs, check_vma=False)
```

```python
import functools

import jax
import jax.numpy as jnp
from jax import lax
from jax.experimental import pallas as pl
from jax.experimental.pallas import tpu as pltpu
from jax.sharding import PartitionSpec as P


def general_body(
    query_passage_words,
    difficult_distractors,
    vocabulary_vectors,
    layer_weight_matrix,
    lowering_factor_matrix,
    raising_factor_matrix,
    logit_sharpness,
):
    group_index = lax.axis_index("group")
    shard_index = lax.axis_index("dp")
    part_index = lax.axis_index("mp")
    shard_count = lax.axis_size("dp")
    side_ids = query_passage_words[0]
    text_count = side_ids.shape[0]
    length = side_ids.shape[1]
    per_shard = text_count // shard_count
    own_ids = lax.dynamic_slice_in_dim(side_ids, shard_index * per_shard, per_shard, 0)
    columns = jnp.take(vocabulary_vectors, side_ids.reshape(-1), axis=1)
    inputs = lax.all_to_all(columns, "dp", split_axis=1, concat_axis=0, tiled=True)
    tokens = inputs.shape[1]
    feature_width = raising_factor_matrix.shape[1]
    wide_inputs = inputs.astype(jnp.float32)
    inverse = lax.rsqrt(jnp.mean(wide_inputs * wide_inputs, axis=0) + 1e-05)
    normed_state = (wide_inputs * inverse[None, :]).astype(jnp.bfloat16)
    linear_map = lax.dot_general(
        lax.all_gather(layer_weight_matrix, "dp", axis=0, tiled=True),
        normed_state,
        (((0,), (0,)), ((), ())),
        preferred_element_type=jnp.float32,
    )
    reduced_sum = jnp.dot(
        lowering_factor_matrix, normed_state, preferred_element_type=jnp.float32
    ).astype(jnp.bfloat16)
    linear_map = linear_map + lax.dot_general(
        raising_factor_matrix,
        reduced_sum,
        (((0,), (0,)), ((), ())),
        preferred_element_type=jnp.float32,
    )
    own_inputs = lax.dynamic_slice_in_dim(
        inputs, part_index * feature_width, feature_width, 0
    ).astype(jnp.float32)
    hidden_state = own_inputs + jax.nn.silu(linear_map)
    mask = (own_ids != 0).astype(jnp.float32)
    counts = jnp.sum(mask, axis=1)
    summed = jnp.einsum("dnl,nl->nd", hidden_state.reshape(feature_width, per_shard, length), mask)
    pooled = (summed / counts[:, None]).astype(jnp.bfloat16)
    gathered = lax.all_gather(pooled, ("group", "dp"), axis=0, tiled=True)
    part_scores = lax.dot_general(
        pooled, gathered, (((1,), (1,)), ((), ())), preferred_element_type=jnp.float32
    )
    gathered_wide = gathered.astype(jnp.float32)
    part_norms = jnp.sum(gathered_wide * gathered_wide, axis=1)
    dots, norms = lax.psum((part_scores, part_norms), "mp")
    rnorm_all = lax.rsqrt(norms + 1e-06)
    all_count = gathered.shape[0]
    half_count = all_count // 2
    own_rows = (
        group_index * half_count + shard_index * per_shard + jnp.arange(per_shard, dtype=jnp.int32)
    )
    rnorm_own = jnp.take(rnorm_all, own_rows)
    cosine = dots * rnorm_own[:, None] * rnorm_all[None, :]
    multiplier_factor = logit_sharpness[0]
    scores = multiplier_factor * cosine
    column_ids = jnp.arange(all_count, dtype=jnp.int32)
    keep = column_ids[None, :] != own_rows[:, None]
    pair = (own_rows + half_count) % all_count
    weight = (group_index == 0).astype(jnp.float32)
    neg_cols = half_count + difficult_distractors
    top = jnp.max(jnp.where(keep, scores, -jnp.inf), axis=1)
    safe_scores = jnp.where(keep, scores, top[:, None])
    expd = jnp.where(keep, jnp.exp(safe_scores - top[:, None]), 0.0)
    neg_exp = (
        jnp.exp(jnp.minimum(jnp.take_along_axis(scores, neg_cols, axis=1) - top[:, None], 0.0))
        * weight
    )
    total = jnp.sum(expd, axis=1) + jnp.sum(neg_exp, axis=1)
    pair_score = jnp.take_along_axis(scores, pair[:, None], axis=1)[:, 0]
    losses = top + jnp.log(total) - pair_score
    onehot = (column_ids[None, None, :] == neg_cols[:, :, None]).astype(jnp.float32)
    probs = (expd + jnp.einsum("rk,rkc->rc", neg_exp, onehot)) / total[:, None]
    target = (column_ids[None, :] == pair[:, None]).astype(jnp.float32)
    grad_scores = (probs - target) / all_count
    coeff = (grad_scores * rnorm_own[:, None] * rnorm_all[None, :]).astype(jnp.bfloat16)
    along = jnp.dot(coeff, gathered, preferred_element_type=jnp.float32)
    pooled_wide = pooled.astype(jnp.float32)
    radial = jnp.sum(grad_scores * cosine, axis=1) * rnorm_own * rnorm_own
    embedding_gradient = multiplier_factor * (along - radial[:, None] * pooled_wide)
    token_grad = jnp.einsum("nd,nl->dnl", embedding_gradient / counts[:, None], mask).reshape(
        feature_width, tokens
    )
    sigma = jax.nn.sigmoid(linear_map)
    local = (token_grad * sigma * (1.0 + linear_map * (1.0 - sigma))).astype(jnp.bfloat16)
    up_portion = lax.dot_general(
        reduced_sum, local, (((1,), (1,)), ((), ())), preferred_element_type=jnp.float32
    )
    adapter_up_gradient = lax.psum(up_portion, ("group", "dp"))
    embeddings = (pooled_wide * rnorm_own[:, None]).astype(jnp.bfloat16)[None]
    return (embeddings, losses[None], adapter_up_gradient)


BLOCK_BITS, WINDOW_BITS, CHUNK_BITS, ROW_BITS = 10, 7, 8, 4
IDS_PER_BLOCK = 1 << BLOCK_BITS
WINDOW = 1 << WINDOW_BITS
CHUNK = 1 << CHUNK_BITS
ROWS = 1 << ROW_BITS
LANES = 128
PIECES = 4
NT = (((1,), (1,)), ((), ()))
VMEM_BYTES = 60 * 1024 * 1024


def mm(a, b, dims=(((1,), (0,)), ((), ()))):
    return lax.dot_general(a, b, dims, preferred_element_type=jnp.float32)


def split(x):
    high = x.astype(jnp.bfloat16)
    return high, (x - high.astype(jnp.float32)).astype(jnp.bfloat16)


def iota(shape, dim):
    return lax.broadcasted_iota(jnp.int32, shape, dim)


def quarter_of(dp_index, cores=2):
    return (dp_index % cores) * 2 + dp_index // cores


def project_kernel(
    ids_ref,
    hard_ref,
    vocab_ref,
    weight_ref,
    lower_ref,
    out00,
    out01,
    out10,
    out11,
    member_ref,
    held,
    weight,
    lower,
    gathered,
    values,
    turned,
    ranks,
    squares,
    residual,
    counted,
    bounds,
    held_sems,
    weight_sems,
    lower_sem,
    bounds_sem,
):
    texts, length = ids_ref.shape
    tokens = texts * length
    features, vocab = vocab_ref.shape
    blocks = vocab // IDS_PER_BLOCK
    chunks = tokens // CHUNK
    per_shard, negatives = hard_ref.shape
    width = weight.shape[2]
    outs = (out00, out01, out10, out11)
    shard = lax.axis_index("dp")
    core, side_y = lax.rem(shard, 2), lax.div(shard, 2)

    def vocab_copy(b, piece):
        rows = pl.ds(piece * (features // PIECES), features // PIECES)
        columns = pl.ds(pl.multiple_of(b * IDS_PER_BLOCK, LANES), IDS_PER_BLOCK)
        return pltpu.make_async_copy(
            vocab_ref.at[rows, columns], held.at[b, rows], held_sems.at[b, piece]
        )

    def weight_copy(i, j):
        quarter = (core ^ i) * 2 + (side_y ^ j)
        return pltpu.make_async_copy(
            weight_ref.at[:, pl.ds(pl.multiple_of(quarter * width, LANES), width)],
            weight.at[2 * i + j],
            weight_sems.at[2 * i + j],
        )

    lower_copy = pltpu.make_async_copy(
        lower_ref.at[:, pl.ds(pl.multiple_of(shard * features, LANES), features)], lower, lower_sem
    )
    for piece in range(PIECES):
        vocab_copy(0, piece).start()
    lower_copy.start()
    for i in range(2):
        for j in range(2):
            weight_copy(i, j).start()
    for b in range(1, blocks):
        for piece in range(PIECES):
            vocab_copy(b, piece).start()

    ids = ids_ref[...]
    valid = ids != 0
    block_of = jnp.where(valid, lax.shift_right_logical(ids, BLOCK_BITS), blocks)
    block_rows = counted.shape[0]
    block_id = iota((block_rows, length), 0)
    below = jnp.zeros((block_rows, length), jnp.float32)
    for text in range(texts):
        below += jnp.where(block_of[text : text + 1] < block_id, 1.0, 0.0)
    before = jnp.broadcast_to(jnp.sum(below, axis=1, keepdims=True), (block_rows, length))
    counted[...] = before.astype(jnp.int32)
    bounds_copy = pltpu.make_async_copy(counted, bounds, bounds_sem)
    bounds_copy.start()
    earlier = jnp.where(iota((length, length), 0) < iota((length, length), 1), 1.0, 0.0).astype(
        jnp.bfloat16
    )
    for text in range(texts):
        here = jnp.where(block_of[text : text + 1] == block_id, 1.0, 0.0)
        inside = mm(here.astype(jnp.bfloat16), earlier)
        ranks[pl.ds(text, 1), :] = jnp.sum(here * (inside + before), axis=0, keepdims=True)
        before += jnp.broadcast_to(jnp.sum(here, axis=1, keepdims=True), (block_rows, length))
    text_of = iota((texts, length), 0)
    carried = jnp.where(valid, lax.shift_left(ids, ROW_BITS) + text_of, 0).astype(jnp.float32)
    rank = ranks[...]

    def place(p, carry):
        position = (iota((LANES, length), 0) + p * LANES).astype(jnp.float32)
        total = jnp.zeros((LANES, length), jnp.float32)
        for text in range(texts):
            total += jnp.where(rank[text : text + 1] == position, carried[text : text + 1], 0.0)
        found = jnp.broadcast_to(jnp.sum(total, axis=1, keepdims=True), (LANES, LANES))
        found = found.astype(jnp.int32)
        token = lax.shift_right_logical(found, ROW_BITS)
        start = pl.multiple_of(p * LANES, LANES)
        values[pl.ds(start, LANES), :] = jnp.where(token == 0, -vocab, token)
        real = (token != 0) & ((found & (ROWS - 1)) == iota((LANES, LANES), 1))
        member_ref[pl.ds(start, LANES), :] = jnp.where(real, 1.0, 0.0).astype(jnp.bfloat16)
        gathered[pl.ds(start, LANES), :] = jnp.zeros((LANES, features), jnp.bfloat16)
        return carry

    lax.fori_loop(0, tokens // LANES, place, 0)
    values[pl.ds(tokens, WINDOW), :] = jnp.full((WINDOW, LANES), -vocab, jnp.int32)
    gathered[pl.ds(tokens, WINDOW), :] = jnp.zeros((WINDOW, features), jnp.bfloat16)
    residual[...] = jnp.zeros_like(residual)
    squares[...] = jnp.zeros_like(squares)
    turned[...] = jnp.zeros_like(turned)
    turned[0:per_shard, chunks : chunks + negatives] = hard_ref[...].astype(jnp.float32)
    lower_copy.wait()
    for i in range(2):
        for j in range(2):
            weight_copy(i, j).wait()

    def project(k, carry):
        start = pl.multiple_of(k * CHUNK, CHUNK)
        x = gathered[pl.ds(start, CHUNK), :]
        for q in range(4):
            outs[q][pl.ds(start, CHUNK), :] = mm(x, weight[q]).astype(jnp.bfloat16)
        reduced = mm(lower[...], x, NT).astype(jnp.bfloat16)
        place_at = pl.multiple_of(tokens + k * ROWS, ROWS)
        for q in range(4):
            outs[q][pl.ds(place_at, ROWS), :] = reduced
        ones = jnp.ones((ROWS, features), jnp.bfloat16)
        squares[pl.ds(k, 1), :] = mm(ones, x * x, NT)[0:1]
        member = member_ref[pl.ds(start, CHUNK), :].astype(jnp.float32).T.astype(jnp.bfloat16)
        residual[...] += mm(member[0:ROWS], x)
        return carry

    def zero(k, carry):
        start = pl.multiple_of(k * CHUNK, CHUNK)
        place_at = pl.multiple_of(tokens + k * ROWS, ROWS)
        for q in range(4):
            outs[q][pl.ds(start, CHUNK), :] = jnp.zeros((CHUNK, width), jnp.bfloat16)
            outs[q][pl.ds(place_at, ROWS), :] = jnp.zeros((ROWS, width), jnp.bfloat16)
        return carry

    def take(b, done):
        for piece in range(PIECES):
            vocab_copy(b, piece).wait()
        first, last = bounds[b, 0], bounds[b + 1, 0]
        aligned = lax.shift_left(lax.shift_right_logical(first, ROW_BITS), ROW_BITS)
        windows = lax.shift_right_logical(last - aligned + WINDOW - 1, WINDOW_BITS)
        windows = jnp.where(last > first, windows, 0)

        def window(w, carry):
            start = pl.multiple_of(aligned + w * WINDOW, ROWS)
            wanted = values[pl.ds(start, WINDOW), :] - (b * IDS_PER_BLOCK + iota((WINDOW, LANES), 1))
            picked = [
                jnp.where(wanted == j * LANES, 1.0, 0.0).astype(jnp.bfloat16)
                for j in range(IDS_PER_BLOCK // LANES)
            ]
            found = mm(jnp.concatenate(picked, axis=1), held[b], NT)
            gathered[pl.ds(start, WINDOW), :] += found.astype(jnp.bfloat16)
            return carry

        lax.fori_loop(0, windows, window, 0)
        full = lax.shift_right_logical(last, CHUNK_BITS)
        lax.fori_loop(done, full, project, 0)
        return full

    bounds_copy.wait()
    done = lax.fori_loop(0, blocks, take, 0)
    used = lax.shift_right_logical(bounds[blocks, 0] + CHUNK - 1, CHUNK_BITS)
    lax.fori_loop(done, used, project, 0)
    lax.fori_loop(used, chunks, zero, 0)

    hard = turned[...].T[0:ROWS]
    lane = iota((ROWS, width), 1)
    misc = jnp.concatenate([squares[...], jnp.zeros((ROWS - squares.shape[0], width), jnp.float32)])
    for i in range(per_shard):
        misc += jnp.where(lane == shard * per_shard + i, hard[:, i : i + 1], 0.0)
    misc = misc.astype(jnp.bfloat16)
    mine = lax.axis_index("mp") == shard
    for i in range(2):
        for j in range(2):
            quarter = (core ^ i) * 2 + (side_y ^ j)
            part = residual[:, pl.ds(pl.multiple_of(quarter * width, LANES), width)]
            out = outs[2 * i + j]
            out[pl.ds(tokens + chunks * ROWS, ROWS), :] = misc
            out[pl.ds(tokens + (chunks + 1) * ROWS, ROWS), :] = jnp.where(mine, part, 0.0).astype(
                jnp.bfloat16
            )


def pool_kernel(
    ids_ref,
    own_ref,
    core_ref,
    far_ref,
    member_ref,
    raise_ref,
    pooled_ref,
    slope_ref,
    reduced_ref,
    misc_ref,
    raised,
    model_width,
):
    texts, length = ids_ref.shape
    tokens = texts * length
    chunks = tokens // CHUNK
    width = own_ref.shape[1]
    quarter = quarter_of(lax.axis_index("dp"))

    def summed(start, size):
        rows = pl.ds(start, size)
        return (
            own_ref[rows, :].astype(jnp.float32)
            + core_ref[rows, :].astype(jnp.float32)
            + far_ref[rows, :].astype(jnp.float32)
        )

    misc = summed(tokens + chunks * ROWS, ROWS)
    misc_ref[...] = misc
    inverse = lax.rsqrt(misc / model_width + 1e-05)
    raised[...] = jnp.zeros_like(raised)
    raised[0:ROWS, :] = raise_ref[:, pl.ds(pl.multiple_of(quarter * width, LANES), width)]
    total = jnp.zeros((ROWS, width), jnp.float32)
    for k in range(chunks):
        scale = inverse[k : k + 1]
        reduced = (summed(tokens + k * ROWS, ROWS) * scale).astype(jnp.bfloat16)
        reduced_ref[:, k * CHUNK : (k + 1) * CHUNK] = reduced
        stacked = jnp.concatenate(
            [reduced.astype(jnp.float32), jnp.broadcast_to(scale, (LANES - ROWS, CHUNK))]
        )
        turned = stacked.T
        low = turned.astype(jnp.bfloat16)
        linear = summed(k * CHUNK, CHUNK) * turned[:, ROWS : ROWS + 1] + mm(low, raised[...])
        sigma = 1.0 / (1.0 + jnp.exp(-linear))
        slope_ref[pl.ds(k * CHUNK, CHUNK), :] = sigma * (1.0 + linear * (1.0 - sigma))
        member = member_ref[pl.ds(k * CHUNK, CHUNK), :].astype(jnp.float32).T
        member = member[0:ROWS].astype(jnp.bfloat16)
        high, rest = split(linear * sigma)
        total += mm(member, high) + mm(member, rest)
    total += summed(tokens + (chunks + 1) * ROWS, ROWS)
    counts = jnp.sum((ids_ref[...] != 0).astype(jnp.float32), axis=1, keepdims=True)
    pooled = total[0:texts] / counts
    pooled = jnp.concatenate([pooled, jnp.zeros((ROWS - texts, width), jnp.float32)])
    for to in range(pooled_ref.shape[0]):
        pooled_ref[to] = pooled.astype(jnp.bfloat16)


def both_sides(pooled_ref, shard, shards):
    return jnp.concatenate([pooled_ref[shard], pooled_ref[shards + shard]], axis=0)


def dots_kernel(pooled_ref, dots_ref, shards):
    dots = jnp.zeros((2 * ROWS, 2 * ROWS), jnp.float32)
    for shard in range(shards):
        block = both_sides(pooled_ref, shard, shards)
        dots += mm(block, block, NT)
    wide = jnp.concatenate([dots, jnp.zeros((2 * ROWS, LANES - 2 * ROWS), jnp.float32)], axis=1)
    for to in range(dots_ref.shape[0]):
        dots_ref[to] = wide


def score_kernel(
    ids_ref,
    pooled_ref,
    dots_ref,
    misc_ref,
    slope_ref,
    reduced_ref,
    member_ref,
    sharp_ref,
    embed_ref,
    loss_ref,
    up_ref,
    shards,
    negatives,
):
    texts, length = ids_ref.shape
    tokens = texts * length
    chunks = tokens // CHUNK
    rows = 2 * ROWS
    width = pooled_ref.shape[2]
    per_shard = loss_ref.shape[1]
    group, shard = lax.axis_index("group"), lax.axis_index("dp")
    dots = dots_ref[0]
    for part in range(1, dots_ref.shape[0]):
        dots += dots_ref[part]
    dots = dots[:, 0:rows]
    down, across = iota((rows, rows), 0), iota((rows, rows), 1)
    same = down == across
    real = (lax.rem(down, ROWS) < texts) & (lax.rem(across, ROWS) < texts)
    diagonal = jnp.where(same, dots, 0.0)
    rnorm_row = lax.rsqrt(jnp.sum(diagonal, axis=0, keepdims=True) + 1e-06)
    rnorm_col = lax.rsqrt(jnp.sum(diagonal, axis=1, keepdims=True) + 1e-06)
    sharpness = sharp_ref[0]
    cosine = dots * rnorm_col * rnorm_row
    scores = sharpness * cosine
    keep = real & ~same
    top = jnp.max(jnp.where(keep, scores, -jnp.inf), axis=0, keepdims=True)
    top = jnp.where(lax.rem(across[0:1], ROWS) < texts, top, 0.0)
    powers = jnp.exp(jnp.where(real, jnp.minimum(scores - top, 0.0), 0.0))
    hard = misc_ref[chunks : chunks + negatives, 0:rows].astype(jnp.int32) + ROWS
    times = jnp.zeros((rows, rows), jnp.float32)
    for k in range(negatives):
        times += jnp.where(hard[k : k + 1] == down, 1.0, 0.0)
    times = jnp.where(across < texts, times, 0.0)
    weights = (jnp.where(keep, 1.0, 0.0) + jnp.where(real, times, 0.0)) * powers
    total = jnp.sum(weights, axis=0, keepdims=True)
    total = jnp.where(lax.rem(across[0:1], ROWS) < texts, total, 1.0)
    pair = (down == lax.rem(across + ROWS, rows)) & real
    pair_score = jnp.sum(jnp.where(pair, scores, 0.0), axis=0, keepdims=True)
    losses = top + jnp.log(total) - pair_score
    grad_scores = (weights / total - jnp.where(pair, 1.0, 0.0)) / (2 * texts)
    coeff = (grad_scores * rnorm_col * rnorm_row).astype(jnp.bfloat16)
    radial = jnp.sum(grad_scores * cosine, axis=0, keepdims=True) * rnorm_row * rnorm_row

    first = shard * per_shard
    loss_col = jnp.sum(jnp.where(same, losses, 0.0), axis=1, keepdims=True)
    at = (iota((rows, LANES), 0) == group * ROWS + first + iota((rows, LANES), 1)) & (
        iota((rows, LANES), 1) < per_shard
    )
    loss_ref[...] = jnp.sum(jnp.where(at, loss_col, 0.0), axis=0, keepdims=True)[:, 0:per_shard]

    mine = both_sides(pooled_ref, shard, shards)
    along = mm(coeff.astype(jnp.float32).T.astype(jnp.bfloat16), mine)
    radial_col = jnp.sum(jnp.where(same, radial, 0.0), axis=1, keepdims=True)
    grad = sharpness * (along - radial_col * mine.astype(jnp.float32))
    grad = jnp.where(group == 0, grad[0:ROWS], grad[ROWS:rows])
    counts = jnp.sum((ids_ref[...] != 0).astype(jnp.float32), axis=1, keepdims=True)
    grad = grad[0:texts] / counts
    grad = jnp.concatenate([grad, jnp.zeros((LANES - texts, width), jnp.float32)])
    high, rest = split(grad)
    update = jnp.zeros((ROWS, width), jnp.float32)
    for k in range(chunks):
        member = member_ref[pl.ds(k * CHUNK, CHUNK), :]
        token_grad = mm(member, high) + mm(member, rest)
        local = (token_grad * slope_ref[pl.ds(k * CHUNK, CHUNK), :]).astype(jnp.bfloat16)
        update += mm(reduced_ref[:, k * CHUNK : (k + 1) * CHUNK], local)
    for to in range(up_ref.shape[0]):
        up_ref[to] = update

    rnorm_own = jnp.where(group == 0, rnorm_col[0:ROWS], rnorm_col[ROWS:rows])
    chosen = iota((ROWS, ROWS), 1) == iota((ROWS, ROWS), 0) + first
    chosen = jnp.where(chosen & (iota((ROWS, ROWS), 0) < per_shard), 1.0, 0.0).astype(jnp.bfloat16)
    for quarter in range(shards):
        block = pooled_ref[group * shards + quarter_of(quarter)].astype(jnp.float32) * rnorm_own
        picked = mm(chosen, block.astype(jnp.bfloat16)).astype(jnp.bfloat16)
        embed_ref[0, :, quarter * width : (quarter + 1) * width] = picked[0:per_shard]


def any_spec():
    return pl.BlockSpec(memory_space=pl.ANY)


def vmem_spec():
    return pl.BlockSpec(memory_space=pltpu.VMEM)


def smem_spec():
    return pl.BlockSpec(memory_space=pltpu.SMEM)


def split_body(
    query_passage_words,
    difficult_distractors,
    vocabulary_vectors,
    layer_weight_matrix,
    lowering_factor_matrix,
    raising_factor_matrix,
    logit_sharpness,
):
    shards, parts = lax.axis_size("dp"), lax.axis_size("mp")
    ids = query_passage_words[0]
    texts, length = ids.shape
    tokens = texts * length
    chunks = tokens // CHUNK
    features, vocab = vocabulary_vectors.shape
    blocks = vocab // IDS_PER_BLOCK
    block_rows = 8 * pl.cdiv(blocks + 1, 8)
    per_shard, negatives = difficult_distractors.shape
    rank = lowering_factor_matrix.shape[0]
    part_width = layer_weight_matrix.shape[1]
    width = part_width // shards
    rows = tokens + (chunks + 2) * ROWS
    params = pltpu.CompilerParams(vmem_limit_bytes=VMEM_BYTES)
    half = jax.ShapeDtypeStruct((rows, width), jnp.bfloat16)
    own0, own1, away0, away1, member = pl.pallas_call(
        project_kernel,
        out_shape=[half] * 4 + [jax.ShapeDtypeStruct((tokens, LANES), jnp.bfloat16)],
        in_specs=[vmem_spec()] * 2 + [any_spec()] * 3,
        out_specs=[vmem_spec()] * 5,
        scratch_shapes=[
            pltpu.VMEM((blocks, features, IDS_PER_BLOCK), jnp.bfloat16),
            pltpu.VMEM((4, features, width), jnp.bfloat16),
            pltpu.VMEM((rank, features), jnp.bfloat16),
            pltpu.VMEM((tokens + WINDOW, features), jnp.bfloat16),
            pltpu.VMEM((tokens + WINDOW, LANES), jnp.int32),
            pltpu.VMEM((LANES, LANES), jnp.float32),
            pltpu.VMEM((texts, length), jnp.float32),
            pltpu.VMEM((8, width), jnp.float32),
            pltpu.VMEM((ROWS, features), jnp.float32),
            pltpu.VMEM((block_rows, length), jnp.int32),
            pltpu.SMEM((block_rows, length), jnp.int32),
            pltpu.SemaphoreType.DMA((blocks, PIECES)),
            pltpu.SemaphoreType.DMA((4,)),
            pltpu.SemaphoreType.DMA,
            pltpu.SemaphoreType.DMA,
        ],
        compiler_params=params,
        name="project",
    )(
        ids,
        difficult_distractors,
        vocabulary_vectors,
        layer_weight_matrix,
        lowering_factor_matrix,
    )
    other_core = [(d, d ^ 1) for d in range(shards)]
    other_y = [(d, d ^ 2) for d in range(shards)]
    core1 = lax.ppermute(away1, "dp", other_core)
    core0 = lax.ppermute(away0, "dp", other_core)
    chip1 = (own1.astype(jnp.float32) + core1.astype(jnp.float32)).astype(jnp.bfloat16)
    far = lax.ppermute(chip1, "dp", other_y)
    pooled, slope, reduced, misc = pl.pallas_call(
        functools.partial(pool_kernel, model_width=float(features * shards)),
        out_shape=[
            jax.ShapeDtypeStruct((2 * shards, ROWS, width), jnp.bfloat16),
            jax.ShapeDtypeStruct((tokens, width), jnp.float32),
            jax.ShapeDtypeStruct((ROWS, tokens), jnp.bfloat16),
            jax.ShapeDtypeStruct((ROWS, width), jnp.float32),
        ],
        in_specs=[vmem_spec()] * 6,
        out_specs=[vmem_spec()] * 4,
        scratch_shapes=[pltpu.VMEM((LANES, width), jnp.bfloat16)],
        compiler_params=params,
        name="pool",
    )(ids, own0, core0, far, member, raising_factor_matrix)
    sides = ("group", "dp")
    pooled = lax.all_to_all(pooled, sides, 0, 0)
    dots = pl.pallas_call(
        functools.partial(dots_kernel, shards=shards),
        out_shape=jax.ShapeDtypeStruct((parts, 2 * ROWS, LANES), jnp.float32),
        in_specs=[vmem_spec()],
        out_specs=vmem_spec(),
        compiler_params=params,
        name="dots",
    )(pooled)
    dots = lax.all_to_all(dots, "mp", 0, 0)
    embeddings, losses, update = pl.pallas_call(
        functools.partial(score_kernel, shards=shards, negatives=negatives),
        out_shape=[
            jax.ShapeDtypeStruct((1, per_shard, part_width), jnp.bfloat16),
            jax.ShapeDtypeStruct((1, per_shard), jnp.float32),
            jax.ShapeDtypeStruct((2 * shards, ROWS, width), jnp.float32),
        ],
        in_specs=[vmem_spec()] * 7 + [smem_spec()],
        out_specs=[vmem_spec()] * 3,
        compiler_params=params,
        name="score",
    )(ids, pooled, dots, misc, slope, reduced, member, logit_sharpness)
    update = lax.all_to_all(update, sides, 0, 0)
    columns = [update[quarter_of(q)] + update[shards + quarter_of(q)] for q in range(shards)]
    return (embeddings, losses, jnp.concatenate(columns, axis=1))


def body(words, hard, vocabulary, weight, lowering, raising, sharpness):
    shards, parts = lax.axis_size("dp"), lax.axis_size("mp")
    texts, length = words.shape[1:]
    features, vocab = vocabulary.shape
    negatives = hard.shape[1]
    square = shards == 4 and features == weight.shape[1] and parts == shards
    small = texts <= ROWS - 2 and length == LANES and texts * length <= 2048
    even = (texts * length) % CHUNK == 0 and vocab % IDS_PER_BLOCK == 0
    fits = features * vocab <= 2**24 and features % (4 * LANES) == 0
    spare = texts * length // CHUNK + negatives <= ROWS and lowering.shape[0] == ROWS
    fast = square and small and even and fits and spare and lax.axis_size("group") == 2
    chosen = split_body if fast else general_body
    return chosen(words, hard, vocabulary, weight, lowering, raising, sharpness)


def solution(mesh):
    in_specs = (
        P("group", None, None),
        P("dp", None),
        P("dp", None),
        P("dp", "mp"),
        P(),
        P(None, "mp"),
        P(),
    )
    out_specs = (P("group", "dp", "mp"), P("group", "dp"), P(None, "mp"))
    return jax.shard_map(body, mesh=mesh, in_specs=in_specs, out_specs=out_specs, check_vma=False)
```

```python
import functools

import jax
import jax.numpy as jnp
from jax import lax
from jax.experimental import pallas as pl
from jax.experimental.pallas import tpu as pltpu
from jax.sharding import PartitionSpec as P


def general_body(
    query_passage_words,
    difficult_distractors,
    vocabulary_vectors,
    layer_weight_matrix,
    lowering_factor_matrix,
    raising_factor_matrix,
    logit_sharpness,
):
    group_index = lax.axis_index("group")
    shard_index = lax.axis_index("dp")
    part_index = lax.axis_index("mp")
    shard_count = lax.axis_size("dp")
    side_ids = query_passage_words[0]
    text_count = side_ids.shape[0]
    length = side_ids.shape[1]
    per_shard = text_count // shard_count
    own_ids = lax.dynamic_slice_in_dim(side_ids, shard_index * per_shard, per_shard, 0)
    columns = jnp.take(vocabulary_vectors, side_ids.reshape(-1), axis=1)
    inputs = lax.all_to_all(columns, "dp", split_axis=1, concat_axis=0, tiled=True)
    tokens = inputs.shape[1]
    feature_width = raising_factor_matrix.shape[1]
    wide_inputs = inputs.astype(jnp.float32)
    inverse = lax.rsqrt(jnp.mean(wide_inputs * wide_inputs, axis=0) + 1e-05)
    normed_state = (wide_inputs * inverse[None, :]).astype(jnp.bfloat16)
    linear_map = lax.dot_general(
        lax.all_gather(layer_weight_matrix, "dp", axis=0, tiled=True),
        normed_state,
        (((0,), (0,)), ((), ())),
        preferred_element_type=jnp.float32,
    )
    reduced_sum = jnp.dot(
        lowering_factor_matrix, normed_state, preferred_element_type=jnp.float32
    ).astype(jnp.bfloat16)
    linear_map = linear_map + lax.dot_general(
        raising_factor_matrix,
        reduced_sum,
        (((0,), (0,)), ((), ())),
        preferred_element_type=jnp.float32,
    )
    own_inputs = lax.dynamic_slice_in_dim(
        inputs, part_index * feature_width, feature_width, 0
    ).astype(jnp.float32)
    hidden_state = own_inputs + jax.nn.silu(linear_map)
    mask = (own_ids != 0).astype(jnp.float32)
    counts = jnp.sum(mask, axis=1)
    summed = jnp.einsum("dnl,nl->nd", hidden_state.reshape(feature_width, per_shard, length), mask)
    pooled = (summed / counts[:, None]).astype(jnp.bfloat16)
    gathered = lax.all_gather(pooled, ("group", "dp"), axis=0, tiled=True)
    part_scores = lax.dot_general(
        pooled, gathered, (((1,), (1,)), ((), ())), preferred_element_type=jnp.float32
    )
    gathered_wide = gathered.astype(jnp.float32)
    part_norms = jnp.sum(gathered_wide * gathered_wide, axis=1)
    dots, norms = lax.psum((part_scores, part_norms), "mp")
    rnorm_all = lax.rsqrt(norms + 1e-06)
    all_count = gathered.shape[0]
    half_count = all_count // 2
    own_rows = (
        group_index * half_count + shard_index * per_shard + jnp.arange(per_shard, dtype=jnp.int32)
    )
    rnorm_own = jnp.take(rnorm_all, own_rows)
    cosine = dots * rnorm_own[:, None] * rnorm_all[None, :]
    multiplier_factor = logit_sharpness[0]
    scores = multiplier_factor * cosine
    column_ids = jnp.arange(all_count, dtype=jnp.int32)
    keep = column_ids[None, :] != own_rows[:, None]
    pair = (own_rows + half_count) % all_count
    weight = (group_index == 0).astype(jnp.float32)
    neg_cols = half_count + difficult_distractors
    top = jnp.max(jnp.where(keep, scores, -jnp.inf), axis=1)
    safe_scores = jnp.where(keep, scores, top[:, None])
    expd = jnp.where(keep, jnp.exp(safe_scores - top[:, None]), 0.0)
    neg_exp = (
        jnp.exp(jnp.minimum(jnp.take_along_axis(scores, neg_cols, axis=1) - top[:, None], 0.0))
        * weight
    )
    total = jnp.sum(expd, axis=1) + jnp.sum(neg_exp, axis=1)
    pair_score = jnp.take_along_axis(scores, pair[:, None], axis=1)[:, 0]
    losses = top + jnp.log(total) - pair_score
    onehot = (column_ids[None, None, :] == neg_cols[:, :, None]).astype(jnp.float32)
    probs = (expd + jnp.einsum("rk,rkc->rc", neg_exp, onehot)) / total[:, None]
    target = (column_ids[None, :] == pair[:, None]).astype(jnp.float32)
    grad_scores = (probs - target) / all_count
    coeff = (grad_scores * rnorm_own[:, None] * rnorm_all[None, :]).astype(jnp.bfloat16)
    along = jnp.dot(coeff, gathered, preferred_element_type=jnp.float32)
    pooled_wide = pooled.astype(jnp.float32)
    radial = jnp.sum(grad_scores * cosine, axis=1) * rnorm_own * rnorm_own
    embedding_gradient = multiplier_factor * (along - radial[:, None] * pooled_wide)
    token_grad = jnp.einsum("nd,nl->dnl", embedding_gradient / counts[:, None], mask).reshape(
        feature_width, tokens
    )
    sigma = jax.nn.sigmoid(linear_map)
    local = (token_grad * sigma * (1.0 + linear_map * (1.0 - sigma))).astype(jnp.bfloat16)
    up_portion = lax.dot_general(
        reduced_sum, local, (((1,), (1,)), ((), ())), preferred_element_type=jnp.float32
    )
    adapter_up_gradient = lax.psum(up_portion, ("group", "dp"))
    embeddings = (pooled_wide * rnorm_own[:, None]).astype(jnp.bfloat16)[None]
    return (embeddings, losses[None], adapter_up_gradient)


BLOCK_BITS, WINDOW_BITS, CHUNK_BITS, ROW_BITS = 10, 7, 8, 4
IDS_PER_BLOCK = 1 << BLOCK_BITS
WINDOW = 1 << WINDOW_BITS
CHUNK = 1 << CHUNK_BITS
ROWS = 1 << ROW_BITS
LANES = 128
PIECES = 1
NT = (((1,), (1,)), ((), ()))
VMEM_BYTES = 60 * 1024 * 1024


def mm(a, b, dims=(((1,), (0,)), ((), ()))):
    return lax.dot_general(a, b, dims, preferred_element_type=jnp.float32)


def split(x):
    high = x.astype(jnp.bfloat16)
    return high, (x - high.astype(jnp.float32)).astype(jnp.bfloat16)


def iota(shape, dim):
    return lax.broadcasted_iota(jnp.int32, shape, dim)


def quarter_of(dp_index, cores=2):
    return (dp_index % cores) * 2 + dp_index // cores


def project_kernel(
    ids_ref,
    hard_ref,
    vocab_ref,
    weight_ref,
    lower_ref,
    out00,
    out01,
    out10,
    out11,
    member_ref,
    held,
    weight,
    lower_rows,
    lower,
    gathered,
    values,
    turned,
    ranks,
    squares,
    residual,
    counted,
    bounds,
    held_sems,
    weight_sems,
    lower_sem,
    bounds_sem,
):
    texts, length = ids_ref.shape
    tokens = texts * length
    features, vocab = vocab_ref.shape
    blocks = vocab // IDS_PER_BLOCK
    chunks = tokens // CHUNK
    per_shard, negatives = hard_ref.shape
    width = weight.shape[2]
    outs = (out00, out01, out10, out11)
    shard = lax.axis_index("dp")
    core, side_y = lax.rem(shard, 2), lax.div(shard, 2)

    def vocab_copy(b, piece):
        rows = pl.ds(piece * (features // PIECES), features // PIECES)
        columns = pl.ds(pl.multiple_of(b * IDS_PER_BLOCK, LANES), IDS_PER_BLOCK)
        return pltpu.make_async_copy(
            vocab_ref.at[rows, columns], held.at[b, rows], held_sems.at[b, piece]
        )

    def weight_copy(i, j):
        quarter = (core ^ i) * 2 + (side_y ^ j)
        return pltpu.make_async_copy(
            weight_ref.at[:, pl.ds(pl.multiple_of(quarter * width, LANES), width)],
            weight.at[2 * i + j],
            weight_sems.at[2 * i + j],
        )

    lower_copy = pltpu.make_async_copy(
        lower_ref.at[:, pl.ds(pl.multiple_of(shard * features, LANES), features)], lower_rows, lower_sem
    )
    for piece in range(PIECES):
        vocab_copy(0, piece).start()
    lower_copy.start()
    for i in range(2):
        for j in range(2):
            weight_copy(i, j).start()
    for b in range(1, blocks):
        for piece in range(PIECES):
            vocab_copy(b, piece).start()

    ids = ids_ref[...]
    valid = ids != 0
    block_of = jnp.where(valid, lax.shift_right_logical(ids, BLOCK_BITS), blocks)
    block_rows = counted.shape[0]
    block_id = iota((block_rows, length), 0)
    below = jnp.zeros((block_rows, length), jnp.float32)
    for text in range(texts):
        below += jnp.where(block_of[text : text + 1] < block_id, 1.0, 0.0)
    before = jnp.broadcast_to(jnp.sum(below, axis=1, keepdims=True), (block_rows, length))
    counted[...] = before.astype(jnp.int32)
    bounds_copy = pltpu.make_async_copy(counted, bounds, bounds_sem)
    bounds_copy.start()
    earlier = jnp.where(iota((length, length), 0) < iota((length, length), 1), 1.0, 0.0).astype(
        jnp.bfloat16
    )
    for text in range(texts):
        here = jnp.where(block_of[text : text + 1] == block_id, 1.0, 0.0)
        inside = mm(here.astype(jnp.bfloat16), earlier)
        ranks[pl.ds(text, 1), :] = jnp.sum(here * (inside + before), axis=0, keepdims=True)
        before += jnp.broadcast_to(jnp.sum(here, axis=1, keepdims=True), (block_rows, length))
    text_of = iota((texts, length), 0)
    carried = jnp.where(valid, lax.shift_left(ids, ROW_BITS) + text_of, 0).astype(jnp.float32)
    rank = ranks[...]

    def place(p, carry):
        position = (iota((LANES, length), 0) + p * LANES).astype(jnp.float32)
        total = jnp.zeros((LANES, length), jnp.float32)
        for text in range(texts):
            total += jnp.where(rank[text : text + 1] == position, carried[text : text + 1], 0.0)
        found = jnp.broadcast_to(jnp.sum(total, axis=1, keepdims=True), (LANES, LANES))
        found = found.astype(jnp.int32)
        token = lax.shift_right_logical(found, ROW_BITS)
        start = pl.multiple_of(p * LANES, LANES)
        values[pl.ds(start, LANES), :] = jnp.where(token == 0, -vocab, token).astype(jnp.float32)
        real = (token != 0) & ((found & (ROWS - 1)) == iota((LANES, LANES), 1))
        member_ref[pl.ds(start, LANES), :] = jnp.where(real, 1.0, 0.0).astype(jnp.bfloat16)
        gathered[pl.ds(start, LANES), :] = jnp.zeros((LANES, features), jnp.bfloat16)
        return carry

    lax.fori_loop(0, tokens // LANES, place, 0)
    values[pl.ds(tokens, WINDOW), :] = jnp.full((WINDOW, LANES), -vocab, jnp.float32)
    gathered[pl.ds(tokens, WINDOW), :] = jnp.zeros((WINDOW, features), jnp.bfloat16)
    residual[...] = jnp.zeros_like(residual)
    squares[...] = jnp.zeros_like(squares)
    turned[...] = jnp.zeros_like(turned)
    turned[0:per_shard, chunks : chunks + negatives] = hard_ref[...].astype(jnp.float32)
    lower_copy.wait()
    padded = jnp.zeros((LANES - ROWS, features), jnp.float32)
    padded = jnp.concatenate([lower_rows[...].astype(jnp.float32), padded])
    lower[...] = padded.T.astype(jnp.bfloat16)
    for i in range(2):
        for j in range(2):
            weight_copy(i, j).wait()

    def project(k, carry):
        start = pl.multiple_of(k * CHUNK, CHUNK)
        x = gathered[pl.ds(start, CHUNK), :]
        for q in range(4):
            outs[q][pl.ds(start, CHUNK), :] = mm(x, weight[q]).astype(jnp.bfloat16)
        squared = mm(x * x, jnp.ones((features, LANES), jnp.bfloat16))
        both = jnp.where(iota((CHUNK, LANES), 1) < ROWS, mm(x, lower[...]), squared).T
        place_at = pl.multiple_of(tokens + k * ROWS, ROWS)
        for q in range(4):
            outs[q][pl.ds(place_at, ROWS), :] = both[0:ROWS].astype(jnp.bfloat16)
        squares[pl.ds(k, 1), :] = both[ROWS : ROWS + 1]
        member = member_ref[pl.ds(start, CHUNK), :].astype(jnp.float32).T.astype(jnp.bfloat16)
        residual[...] += mm(member[0:ROWS], x)
        return carry

    def zero(k, carry):
        start = pl.multiple_of(k * CHUNK, CHUNK)
        place_at = pl.multiple_of(tokens + k * ROWS, ROWS)
        for q in range(4):
            outs[q][pl.ds(start, CHUNK), :] = jnp.zeros((CHUNK, width), jnp.bfloat16)
            outs[q][pl.ds(place_at, ROWS), :] = jnp.zeros((ROWS, width), jnp.bfloat16)
        return carry

    def take(b, done):
        for piece in range(PIECES):
            vocab_copy(b, piece).wait()
        first, last = bounds[b, 0], bounds[b + 1, 0]
        aligned = lax.shift_left(lax.shift_right_logical(first, ROW_BITS), ROW_BITS)
        windows = lax.shift_right_logical(last - aligned + WINDOW - 1, WINDOW_BITS)
        windows = jnp.where(last > first, windows, 0)

        def window(w, carry):
            start = pl.multiple_of(aligned + w * WINDOW, ROWS)
            wanted = values[pl.ds(start, WINDOW), :].T.astype(jnp.int32)
            wanted -= b * IDS_PER_BLOCK + iota((LANES, WINDOW), 0)
            picked = [
                jnp.where(wanted == j * LANES, 1.0, 0.0).astype(jnp.bfloat16)
                for j in range(IDS_PER_BLOCK // LANES)
            ]
            found = mm(held[b], jnp.concatenate(picked, axis=0))
            gathered[pl.ds(start, WINDOW), :] += found.T.astype(jnp.bfloat16)
            return carry

        lax.fori_loop(0, windows, window, 0)
        full = lax.shift_right_logical(last, CHUNK_BITS)
        lax.fori_loop(done, full, project, 0)
        return full

    bounds_copy.wait()
    done = lax.fori_loop(0, blocks, take, 0)
    used = lax.shift_right_logical(bounds[blocks, 0] + CHUNK - 1, CHUNK_BITS)
    lax.fori_loop(done, used, project, 0)
    lax.fori_loop(used, chunks, zero, 0)

    hard = turned[...].T[0:ROWS]
    lane = iota((ROWS, width), 1)
    misc = jnp.concatenate([squares[...], jnp.zeros((ROWS - squares.shape[0], width), jnp.float32)])
    for i in range(per_shard):
        misc += jnp.where(lane == shard * per_shard + i, hard[:, i : i + 1], 0.0)
    misc = misc.astype(jnp.bfloat16)
    mine = lax.axis_index("mp") == shard
    for i in range(2):
        for j in range(2):
            quarter = (core ^ i) * 2 + (side_y ^ j)
            part = residual[:, pl.ds(pl.multiple_of(quarter * width, LANES), width)]
            out = outs[2 * i + j]
            out[pl.ds(tokens + chunks * ROWS, ROWS), :] = misc
            out[pl.ds(tokens + (chunks + 1) * ROWS, ROWS), :] = jnp.where(mine, part, 0.0).astype(
                jnp.bfloat16
            )


def pool_kernel(
    ids_ref,
    own_ref,
    core_ref,
    far_ref,
    member_ref,
    raise_ref,
    pooled_ref,
    slope_ref,
    reduced_ref,
    misc_ref,
    raised,
    model_width,
):
    texts, length = ids_ref.shape
    tokens = texts * length
    chunks = tokens // CHUNK
    width = own_ref.shape[1]
    quarter = quarter_of(lax.axis_index("dp"))

    def summed(start, size):
        rows = pl.ds(start, size)
        return (
            own_ref[rows, :].astype(jnp.float32)
            + core_ref[rows, :].astype(jnp.float32)
            + far_ref[rows, :].astype(jnp.float32)
        )

    misc = summed(tokens + chunks * ROWS, ROWS)
    misc_ref[...] = misc
    inverse = lax.rsqrt(misc / model_width + 1e-05)
    raised[...] = jnp.zeros_like(raised)
    raised[0:ROWS, :] = raise_ref[:, pl.ds(pl.multiple_of(quarter * width, LANES), width)]
    total = jnp.zeros((ROWS, width), jnp.float32)
    for k in range(chunks):
        scale = inverse[k : k + 1]
        reduced = (summed(tokens + k * ROWS, ROWS) * scale).astype(jnp.bfloat16)
        reduced_ref[:, k * CHUNK : (k + 1) * CHUNK] = reduced
        stacked = jnp.concatenate(
            [reduced.astype(jnp.float32), jnp.broadcast_to(scale, (LANES - ROWS, CHUNK))]
        )
        turned = stacked.T
        low = turned.astype(jnp.bfloat16)
        linear = summed(k * CHUNK, CHUNK) * turned[:, ROWS : ROWS + 1] + mm(low, raised[...])
        sigma = 1.0 / (1.0 + jnp.exp(-linear))
        slope_ref[pl.ds(k * CHUNK, CHUNK), :] = sigma * (1.0 + linear * (1.0 - sigma))
        member = member_ref[pl.ds(k * CHUNK, CHUNK), :].astype(jnp.float32).T
        member = member[0:ROWS].astype(jnp.bfloat16)
        high, rest = split(linear * sigma)
        total += mm(member, high) + mm(member, rest)
    total += summed(tokens + (chunks + 1) * ROWS, ROWS)
    counts = jnp.sum((ids_ref[...] != 0).astype(jnp.float32), axis=1, keepdims=True)
    pooled = total[0:texts] / counts
    pooled = jnp.concatenate([pooled, jnp.zeros((ROWS - texts, width), jnp.float32)])
    for to in range(pooled_ref.shape[0]):
        pooled_ref[to] = pooled.astype(jnp.bfloat16)


def both_sides(pooled_ref, shard, shards):
    return jnp.concatenate([pooled_ref[shard], pooled_ref[shards + shard]], axis=0)


def dots_kernel(pooled_ref, dots_ref, shards):
    dots = jnp.zeros((2 * ROWS, 2 * ROWS), jnp.float32)
    for shard in range(shards):
        block = both_sides(pooled_ref, shard, shards)
        dots += mm(block, block, NT)
    wide = jnp.concatenate([dots, jnp.zeros((2 * ROWS, LANES - 2 * ROWS), jnp.float32)], axis=1)
    for to in range(dots_ref.shape[0]):
        dots_ref[to] = wide


def score_kernel(
    ids_ref,
    pooled_ref,
    dots_ref,
    misc_ref,
    slope_ref,
    reduced_ref,
    member_ref,
    sharp_ref,
    embed_ref,
    loss_ref,
    up_ref,
    shards,
    negatives,
):
    texts, length = ids_ref.shape
    tokens = texts * length
    chunks = tokens // CHUNK
    rows = 2 * ROWS
    width = pooled_ref.shape[2]
    per_shard = loss_ref.shape[1]
    group, shard = lax.axis_index("group"), lax.axis_index("dp")
    dots = dots_ref[0]
    for part in range(1, dots_ref.shape[0]):
        dots += dots_ref[part]
    dots = dots[:, 0:rows]
    down, across = iota((rows, rows), 0), iota((rows, rows), 1)
    same = down == across
    real = (lax.rem(down, ROWS) < texts) & (lax.rem(across, ROWS) < texts)
    diagonal = jnp.where(same, dots, 0.0)
    rnorm_row = lax.rsqrt(jnp.sum(diagonal, axis=0, keepdims=True) + 1e-06)
    rnorm_col = lax.rsqrt(jnp.sum(diagonal, axis=1, keepdims=True) + 1e-06)
    sharpness = sharp_ref[0]
    cosine = dots * rnorm_col * rnorm_row
    scores = sharpness * cosine
    keep = real & ~same
    top = jnp.max(jnp.where(keep, scores, -jnp.inf), axis=0, keepdims=True)
    top = jnp.where(lax.rem(across[0:1], ROWS) < texts, top, 0.0)
    powers = jnp.exp(jnp.where(real, jnp.minimum(scores - top, 0.0), 0.0))
    hard = misc_ref[chunks : chunks + negatives, 0:rows].astype(jnp.int32) + ROWS
    times = jnp.zeros((rows, rows), jnp.float32)
    for k in range(negatives):
        times += jnp.where(hard[k : k + 1] == down, 1.0, 0.0)
    times = jnp.where(across < texts, times, 0.0)
    weights = (jnp.where(keep, 1.0, 0.0) + jnp.where(real, times, 0.0)) * powers
    total = jnp.sum(weights, axis=0, keepdims=True)
    total = jnp.where(lax.rem(across[0:1], ROWS) < texts, total, 1.0)
    pair = (down == lax.rem(across + ROWS, rows)) & real
    pair_score = jnp.sum(jnp.where(pair, scores, 0.0), axis=0, keepdims=True)
    losses = top + jnp.log(total) - pair_score
    grad_scores = (weights / total - jnp.where(pair, 1.0, 0.0)) / (2 * texts)
    coeff = (grad_scores * rnorm_col * rnorm_row).astype(jnp.bfloat16)
    radial = jnp.sum(grad_scores * cosine, axis=0, keepdims=True) * rnorm_row * rnorm_row

    first = shard * per_shard
    loss_col = jnp.sum(jnp.where(same, losses, 0.0), axis=1, keepdims=True)
    at = (iota((rows, LANES), 0) == group * ROWS + first + iota((rows, LANES), 1)) & (
        iota((rows, LANES), 1) < per_shard
    )
    loss_ref[...] = jnp.sum(jnp.where(at, loss_col, 0.0), axis=0, keepdims=True)[:, 0:per_shard]

    mine = both_sides(pooled_ref, shard, shards)
    along = mm(coeff.astype(jnp.float32).T.astype(jnp.bfloat16), mine)
    radial_col = jnp.sum(jnp.where(same, radial, 0.0), axis=1, keepdims=True)
    grad = sharpness * (along - radial_col * mine.astype(jnp.float32))
    grad = jnp.where(group == 0, grad[0:ROWS], grad[ROWS:rows])
    counts = jnp.sum((ids_ref[...] != 0).astype(jnp.float32), axis=1, keepdims=True)
    grad = grad[0:texts] / counts
    grad = jnp.concatenate([grad, jnp.zeros((LANES - texts, width), jnp.float32)])
    high, rest = split(grad)
    update = jnp.zeros((ROWS, width), jnp.float32)
    for k in range(chunks):
        member = member_ref[pl.ds(k * CHUNK, CHUNK), :]
        token_grad = mm(member, high) + mm(member, rest)
        local = (token_grad * slope_ref[pl.ds(k * CHUNK, CHUNK), :]).astype(jnp.bfloat16)
        update += mm(reduced_ref[:, k * CHUNK : (k + 1) * CHUNK], local)
    for to in range(up_ref.shape[0]):
        up_ref[to] = update

    rnorm_own = jnp.where(group == 0, rnorm_col[0:ROWS], rnorm_col[ROWS:rows])
    chosen = iota((ROWS, ROWS), 1) == iota((ROWS, ROWS), 0) + first
    chosen = jnp.where(chosen & (iota((ROWS, ROWS), 0) < per_shard), 1.0, 0.0).astype(jnp.bfloat16)
    for quarter in range(shards):
        block = pooled_ref[group * shards + quarter_of(quarter)].astype(jnp.float32) * rnorm_own
        picked = mm(chosen, block.astype(jnp.bfloat16)).astype(jnp.bfloat16)
        embed_ref[0, :, quarter * width : (quarter + 1) * width] = picked[0:per_shard]


def any_spec():
    return pl.BlockSpec(memory_space=pl.ANY)


def vmem_spec():
    return pl.BlockSpec(memory_space=pltpu.VMEM)


def smem_spec():
    return pl.BlockSpec(memory_space=pltpu.SMEM)


def split_body(
    query_passage_words,
    difficult_distractors,
    vocabulary_vectors,
    layer_weight_matrix,
    lowering_factor_matrix,
    raising_factor_matrix,
    logit_sharpness,
):
    shards, parts = lax.axis_size("dp"), lax.axis_size("mp")
    ids = query_passage_words[0]
    texts, length = ids.shape
    tokens = texts * length
    chunks = tokens // CHUNK
    features, vocab = vocabulary_vectors.shape
    blocks = vocab // IDS_PER_BLOCK
    block_rows = 8 * pl.cdiv(blocks + 1, 8)
    per_shard, negatives = difficult_distractors.shape
    rank = lowering_factor_matrix.shape[0]
    part_width = layer_weight_matrix.shape[1]
    width = part_width // shards
    rows = tokens + (chunks + 2) * ROWS
    params = pltpu.CompilerParams(vmem_limit_bytes=VMEM_BYTES)
    half = jax.ShapeDtypeStruct((rows, width), jnp.bfloat16)
    own0, own1, away0, away1, member = pl.pallas_call(
        project_kernel,
        out_shape=[half] * 4 + [jax.ShapeDtypeStruct((tokens, LANES), jnp.bfloat16)],
        in_specs=[vmem_spec()] * 2 + [any_spec()] * 3,
        out_specs=[vmem_spec()] * 5,
        scratch_shapes=[
            pltpu.VMEM((blocks, features, IDS_PER_BLOCK), jnp.bfloat16),
            pltpu.VMEM((4, features, width), jnp.bfloat16),
            pltpu.VMEM((rank, features), jnp.bfloat16),
            pltpu.VMEM((features, LANES), jnp.bfloat16),
            pltpu.VMEM((tokens + WINDOW, features), jnp.bfloat16),
            pltpu.VMEM((tokens + WINDOW, LANES), jnp.float32),
            pltpu.VMEM((LANES, LANES), jnp.float32),
            pltpu.VMEM((texts, length), jnp.float32),
            pltpu.VMEM((8, width), jnp.float32),
            pltpu.VMEM((ROWS, features), jnp.float32),
            pltpu.VMEM((block_rows, length), jnp.int32),
            pltpu.SMEM((block_rows, length), jnp.int32),
            pltpu.SemaphoreType.DMA((blocks, PIECES)),
            pltpu.SemaphoreType.DMA((4,)),
            pltpu.SemaphoreType.DMA,
            pltpu.SemaphoreType.DMA,
        ],
        compiler_params=params,
        name="project",
    )(
        ids,
        difficult_distractors,
        vocabulary_vectors,
        layer_weight_matrix,
        lowering_factor_matrix,
    )
    other_core = [(d, d ^ 1) for d in range(shards)]
    other_y = [(d, d ^ 2) for d in range(shards)]
    core1 = lax.ppermute(away1, "dp", other_core)
    core0 = lax.ppermute(away0, "dp", other_core)
    chip1 = (own1.astype(jnp.float32) + core1.astype(jnp.float32)).astype(jnp.bfloat16)
    far = lax.ppermute(chip1, "dp", other_y)
    pooled, slope, reduced, misc = pl.pallas_call(
        functools.partial(pool_kernel, model_width=float(features * shards)),
        out_shape=[
            jax.ShapeDtypeStruct((2 * shards, ROWS, width), jnp.bfloat16),
            jax.ShapeDtypeStruct((tokens, width), jnp.float32),
            jax.ShapeDtypeStruct((ROWS, tokens), jnp.bfloat16),
            jax.ShapeDtypeStruct((ROWS, width), jnp.float32),
        ],
        in_specs=[vmem_spec()] * 6,
        out_specs=[vmem_spec()] * 4,
        scratch_shapes=[pltpu.VMEM((LANES, width), jnp.bfloat16)],
        compiler_params=params,
        name="pool",
    )(ids, own0, core0, far, member, raising_factor_matrix)
    sides = ("group", "dp")
    pooled = lax.all_to_all(pooled, sides, 0, 0)
    dots = pl.pallas_call(
        functools.partial(dots_kernel, shards=shards),
        out_shape=jax.ShapeDtypeStruct((parts, 2 * ROWS, LANES), jnp.float32),
        in_specs=[vmem_spec()],
        out_specs=vmem_spec(),
        compiler_params=params,
        name="dots",
    )(pooled)
    dots = lax.all_to_all(dots, "mp", 0, 0)
    embeddings, losses, update = pl.pallas_call(
        functools.partial(score_kernel, shards=shards, negatives=negatives),
        out_shape=[
            jax.ShapeDtypeStruct((1, per_shard, part_width), jnp.bfloat16),
            jax.ShapeDtypeStruct((1, per_shard), jnp.float32),
            jax.ShapeDtypeStruct((2 * shards, ROWS, width), jnp.float32),
        ],
        in_specs=[vmem_spec()] * 7 + [smem_spec()],
        out_specs=[vmem_spec()] * 3,
        compiler_params=params,
        name="score",
    )(ids, pooled, dots, misc, slope, reduced, member, logit_sharpness)
    update = lax.all_to_all(update, sides, 0, 0)
    columns = [update[quarter_of(q)] + update[shards + quarter_of(q)] for q in range(shards)]
    return (embeddings, losses, jnp.concatenate(columns, axis=1))


def body(words, hard, vocabulary, weight, lowering, raising, sharpness):
    shards, parts = lax.axis_size("dp"), lax.axis_size("mp")
    texts, length = words.shape[1:]
    features, vocab = vocabulary.shape
    negatives = hard.shape[1]
    square = shards == 4 and features == weight.shape[1] and parts == shards
    small = texts <= ROWS - 2 and length == LANES and texts * length <= 2048
    even = (texts * length) % CHUNK == 0 and vocab % IDS_PER_BLOCK == 0
    fits = features * vocab <= 2**24 and features % (4 * LANES) == 0
    spare = texts * length // CHUNK + negatives <= ROWS and lowering.shape[0] == ROWS
    fast = square and small and even and fits and spare and lax.axis_size("group") == 2
    chosen = split_body if fast else general_body
    return chosen(words, hard, vocabulary, weight, lowering, raising, sharpness)


def solution(mesh):
    in_specs = (
        P("group", None, None),
        P("dp", None),
        P("dp", None),
        P("dp", "mp"),
        P(),
        P(None, "mp"),
        P(),
    )
    out_specs = (P("group", "dp", "mp"), P("group", "dp"), P(None, "mp"))
    return jax.shard_map(body, mesh=mesh, in_specs=in_specs, out_specs=out_specs, check_vma=False)
```

```python
import functools

import jax
import jax.numpy as jnp
from jax import lax
from jax.experimental import pallas as pl
from jax.experimental.pallas import tpu as pltpu
from jax.sharding import PartitionSpec as P


def general_body(
    query_passage_words,
    difficult_distractors,
    vocabulary_vectors,
    layer_weight_matrix,
    lowering_factor_matrix,
    raising_factor_matrix,
    logit_sharpness,
):
    group_index = lax.axis_index("group")
    shard_index = lax.axis_index("dp")
    part_index = lax.axis_index("mp")
    shard_count = lax.axis_size("dp")
    side_ids = query_passage_words[0]
    text_count = side_ids.shape[0]
    length = side_ids.shape[1]
    per_shard = text_count // shard_count
    own_ids = lax.dynamic_slice_in_dim(side_ids, shard_index * per_shard, per_shard, 0)
    columns = jnp.take(vocabulary_vectors, side_ids.reshape(-1), axis=1)
    inputs = lax.all_to_all(columns, "dp", split_axis=1, concat_axis=0, tiled=True)
    tokens = inputs.shape[1]
    feature_width = raising_factor_matrix.shape[1]
    wide_inputs = inputs.astype(jnp.float32)
    inverse = lax.rsqrt(jnp.mean(wide_inputs * wide_inputs, axis=0) + 1e-05)
    normed_state = (wide_inputs * inverse[None, :]).astype(jnp.bfloat16)
    linear_map = lax.dot_general(
        lax.all_gather(layer_weight_matrix, "dp", axis=0, tiled=True),
        normed_state,
        (((0,), (0,)), ((), ())),
        preferred_element_type=jnp.float32,
    )
    reduced_sum = jnp.dot(
        lowering_factor_matrix, normed_state, preferred_element_type=jnp.float32
    ).astype(jnp.bfloat16)
    linear_map = linear_map + lax.dot_general(
        raising_factor_matrix,
        reduced_sum,
        (((0,), (0,)), ((), ())),
        preferred_element_type=jnp.float32,
    )
    own_inputs = lax.dynamic_slice_in_dim(
        inputs, part_index * feature_width, feature_width, 0
    ).astype(jnp.float32)
    hidden_state = own_inputs + jax.nn.silu(linear_map)
    mask = (own_ids != 0).astype(jnp.float32)
    counts = jnp.sum(mask, axis=1)
    summed = jnp.einsum("dnl,nl->nd", hidden_state.reshape(feature_width, per_shard, length), mask)
    pooled = (summed / counts[:, None]).astype(jnp.bfloat16)
    gathered = lax.all_gather(pooled, ("group", "dp"), axis=0, tiled=True)
    part_scores = lax.dot_general(
        pooled, gathered, (((1,), (1,)), ((), ())), preferred_element_type=jnp.float32
    )
    gathered_wide = gathered.astype(jnp.float32)
    part_norms = jnp.sum(gathered_wide * gathered_wide, axis=1)
    dots, norms = lax.psum((part_scores, part_norms), "mp")
    rnorm_all = lax.rsqrt(norms + 1e-06)
    all_count = gathered.shape[0]
    half_count = all_count // 2
    own_rows = (
        group_index * half_count + shard_index * per_shard + jnp.arange(per_shard, dtype=jnp.int32)
    )
    rnorm_own = jnp.take(rnorm_all, own_rows)
    cosine = dots * rnorm_own[:, None] * rnorm_all[None, :]
    multiplier_factor = logit_sharpness[0]
    scores = multiplier_factor * cosine
    column_ids = jnp.arange(all_count, dtype=jnp.int32)
    keep = column_ids[None, :] != own_rows[:, None]
    pair = (own_rows + half_count) % all_count
    weight = (group_index == 0).astype(jnp.float32)
    neg_cols = half_count + difficult_distractors
    top = jnp.max(jnp.where(keep, scores, -jnp.inf), axis=1)
    safe_scores = jnp.where(keep, scores, top[:, None])
    expd = jnp.where(keep, jnp.exp(safe_scores - top[:, None]), 0.0)
    neg_exp = (
        jnp.exp(jnp.minimum(jnp.take_along_axis(scores, neg_cols, axis=1) - top[:, None], 0.0))
        * weight
    )
    total = jnp.sum(expd, axis=1) + jnp.sum(neg_exp, axis=1)
    pair_score = jnp.take_along_axis(scores, pair[:, None], axis=1)[:, 0]
    losses = top + jnp.log(total) - pair_score
    onehot = (column_ids[None, None, :] == neg_cols[:, :, None]).astype(jnp.float32)
    probs = (expd + jnp.einsum("rk,rkc->rc", neg_exp, onehot)) / total[:, None]
    target = (column_ids[None, :] == pair[:, None]).astype(jnp.float32)
    grad_scores = (probs - target) / all_count
    coeff = (grad_scores * rnorm_own[:, None] * rnorm_all[None, :]).astype(jnp.bfloat16)
    along = jnp.dot(coeff, gathered, preferred_element_type=jnp.float32)
    pooled_wide = pooled.astype(jnp.float32)
    radial = jnp.sum(grad_scores * cosine, axis=1) * rnorm_own * rnorm_own
    embedding_gradient = multiplier_factor * (along - radial[:, None] * pooled_wide)
    token_grad = jnp.einsum("nd,nl->dnl", embedding_gradient / counts[:, None], mask).reshape(
        feature_width, tokens
    )
    sigma = jax.nn.sigmoid(linear_map)
    local = (token_grad * sigma * (1.0 + linear_map * (1.0 - sigma))).astype(jnp.bfloat16)
    up_portion = lax.dot_general(
        reduced_sum, local, (((1,), (1,)), ((), ())), preferred_element_type=jnp.float32
    )
    adapter_up_gradient = lax.psum(up_portion, ("group", "dp"))
    embeddings = (pooled_wide * rnorm_own[:, None]).astype(jnp.bfloat16)[None]
    return (embeddings, losses[None], adapter_up_gradient)


BLOCK_BITS, WINDOW_BITS, CHUNK_BITS, ROW_BITS = 10, 7, 8, 4
IDS_PER_BLOCK = 1 << BLOCK_BITS
WINDOW = 1 << WINDOW_BITS
CHUNK = 1 << CHUNK_BITS
ROWS = 1 << ROW_BITS
LANES = 128
STAGES = 4
PIECES = 4
NT = (((1,), (1,)), ((), ()))
VMEM_BYTES = 60 * 1024 * 1024


def mm(a, b, dims=(((1,), (0,)), ((), ()))):
    return lax.dot_general(a, b, dims, preferred_element_type=jnp.float32)


def split(x):
    high = x.astype(jnp.bfloat16)
    return high, (x - high.astype(jnp.float32)).astype(jnp.bfloat16)


def iota(shape, dim):
    return lax.broadcasted_iota(jnp.int32, shape, dim)


def quarter_of(dp_index, cores=2):
    return (dp_index % cores) * 2 + dp_index // cores


def project_kernel(
    ids_ref,
    hard_ref,
    vocab_ref,
    weight_ref,
    lower_ref,
    out00,
    out01,
    out10,
    out11,
    member_ref,
    held,
    weight,
    lower_rows,
    lower,
    picks,
    gathered,
    values,
    turned,
    ranks,
    squares,
    residual,
    counted,
    bounds,
    held_sems,
    weight_sems,
    lower_sem,
    bounds_sem,
):
    texts, length = ids_ref.shape
    tokens = texts * length
    features, vocab = vocab_ref.shape
    blocks = vocab // IDS_PER_BLOCK
    chunks = tokens // CHUNK
    per_shard, negatives = hard_ref.shape
    width = weight.shape[2]
    outs = (out00, out01, out10, out11)
    shard = lax.axis_index("dp")
    core, side_y = lax.rem(shard, 2), lax.div(shard, 2)

    stage_rows = features // STAGES
    piece_rows = stage_rows // PIECES

    def vocab_copy(stage, piece):
        rows = pl.ds(pl.multiple_of((stage * PIECES + piece) * piece_rows, ROWS), piece_rows)
        return pltpu.make_async_copy(vocab_ref.at[rows], held.at[rows], held_sems.at[stage, piece])

    def weight_copy(i, j):
        quarter = (core ^ i) * 2 + (side_y ^ j)
        return pltpu.make_async_copy(
            weight_ref.at[:, pl.ds(pl.multiple_of(quarter * width, LANES), width)],
            weight.at[2 * i + j],
            weight_sems.at[2 * i + j],
        )

    lower_copy = pltpu.make_async_copy(
        lower_ref.at[:, pl.ds(pl.multiple_of(shard * features, LANES), features)], lower_rows, lower_sem
    )
    for stage in range(STAGES):
        for piece in range(PIECES):
            vocab_copy(stage, piece).start()
        if stage == 0:
            lower_copy.start()
            for i in range(2):
                for j in range(2):
                    weight_copy(i, j).start()

    ids = ids_ref[...]
    valid = ids != 0
    block_of = jnp.where(valid, lax.shift_right_logical(ids, BLOCK_BITS), blocks)
    block_rows = counted.shape[0]
    block_id = iota((block_rows, length), 0)
    below = jnp.zeros((block_rows, length), jnp.float32)
    for text in range(texts):
        below += jnp.where(block_of[text : text + 1] < block_id, 1.0, 0.0)
    before = jnp.broadcast_to(jnp.sum(below, axis=1, keepdims=True), (block_rows, length))
    counted[...] = before.astype(jnp.int32)
    bounds_copy = pltpu.make_async_copy(counted, bounds, bounds_sem)
    bounds_copy.start()
    earlier = jnp.where(iota((length, length), 0) < iota((length, length), 1), 1.0, 0.0).astype(
        jnp.bfloat16
    )
    for text in range(texts):
        here = jnp.where(block_of[text : text + 1] == block_id, 1.0, 0.0)
        inside = mm(here.astype(jnp.bfloat16), earlier)
        ranks[pl.ds(text, 1), :] = jnp.sum(here * (inside + before), axis=0, keepdims=True)
        before += jnp.broadcast_to(jnp.sum(here, axis=1, keepdims=True), (block_rows, length))
    text_of = iota((texts, length), 0)
    carried = jnp.where(valid, lax.shift_left(ids, ROW_BITS) + text_of, 0).astype(jnp.float32)
    rank = ranks[...]

    def place(p, carry):
        position = (iota((LANES, length), 0) + p * LANES).astype(jnp.float32)
        total = jnp.zeros((LANES, length), jnp.float32)
        for text in range(texts):
            total += jnp.where(rank[text : text + 1] == position, carried[text : text + 1], 0.0)
        found = jnp.broadcast_to(jnp.sum(total, axis=1, keepdims=True), (LANES, LANES))
        found = found.astype(jnp.int32)
        token = lax.shift_right_logical(found, ROW_BITS)
        start = pl.multiple_of(p * LANES, LANES)
        values[pl.ds(start, LANES), :] = jnp.where(token == 0, -vocab, token).astype(jnp.float32)
        real = (token != 0) & ((found & (ROWS - 1)) == iota((LANES, LANES), 1))
        member_ref[pl.ds(start, LANES), :] = jnp.where(real, 1.0, 0.0).astype(jnp.bfloat16)
        gathered[pl.ds(start, LANES), :] = jnp.zeros((LANES, features), jnp.bfloat16)
        return carry

    lax.fori_loop(0, tokens // LANES, place, 0)
    values[pl.ds(tokens, WINDOW), :] = jnp.full((WINDOW, LANES), -vocab, jnp.float32)
    gathered[pl.ds(tokens, WINDOW), :] = jnp.zeros((WINDOW, features), jnp.bfloat16)
    residual[...] = jnp.zeros_like(residual)
    squares[...] = jnp.zeros_like(squares)
    turned[...] = jnp.zeros_like(turned)
    turned[0:per_shard, chunks : chunks + negatives] = hard_ref[...].astype(jnp.float32)
    lower_copy.wait()
    padded = jnp.zeros((LANES - ROWS, features), jnp.float32)
    padded = jnp.concatenate([lower_rows[...].astype(jnp.float32), padded])
    lower[...] = padded.T.astype(jnp.bfloat16)
    for i in range(2):
        for j in range(2):
            weight_copy(i, j).wait()

    def project(k, carry):
        start = pl.multiple_of(k * CHUNK, CHUNK)
        x = gathered[pl.ds(start, CHUNK), :]
        for q in range(4):
            outs[q][pl.ds(start, CHUNK), :] = mm(x, weight[q]).astype(jnp.bfloat16)
        squared = mm(x * x, jnp.ones((features, LANES), jnp.bfloat16))
        both = jnp.where(iota((CHUNK, LANES), 1) < ROWS, mm(x, lower[...]), squared).T
        place_at = pl.multiple_of(tokens + k * ROWS, ROWS)
        for q in range(4):
            outs[q][pl.ds(place_at, ROWS), :] = both[0:ROWS].astype(jnp.bfloat16)
        squares[pl.ds(k, 1), :] = both[ROWS : ROWS + 1]
        member = member_ref[pl.ds(start, CHUNK), :].astype(jnp.float32).T.astype(jnp.bfloat16)
        residual[...] += mm(member[0:ROWS], x)
        return carry

    def zero(k, carry):
        start = pl.multiple_of(k * CHUNK, CHUNK)
        place_at = pl.multiple_of(tokens + k * ROWS, ROWS)
        for q in range(4):
            outs[q][pl.ds(start, CHUNK), :] = jnp.zeros((CHUNK, width), jnp.bfloat16)
            outs[q][pl.ds(place_at, ROWS), :] = jnp.zeros((ROWS, width), jnp.bfloat16)
        return carry

    def windows_of(b):
        first, last = bounds[b, 0], bounds[b + 1, 0]
        aligned = lax.shift_left(lax.shift_right_logical(first, ROW_BITS), ROW_BITS)
        windows = lax.shift_right_logical(last - aligned + WINDOW - 1, WINDOW_BITS)
        return aligned, jnp.where(last > first, windows, 0)

    def over_windows(act):
        def block(b, slot):
            aligned, windows = windows_of(b)

            def window(w, slot):
                act(b, pl.multiple_of(aligned + w * WINDOW, ROWS), slot)
                return slot + 1

            return lax.fori_loop(0, windows, window, slot)

        lax.fori_loop(0, blocks, block, 0)

    def pick(b, start, slot):
        wanted = values[pl.ds(start, WINDOW), :].T.astype(jnp.int32)
        wanted -= b * IDS_PER_BLOCK + iota((LANES, WINDOW), 0)
        for j in range(IDS_PER_BLOCK // LANES):
            picks[slot, j * LANES : (j + 1) * LANES, :] = jnp.where(
                wanted == j * LANES, 1.0, 0.0
            ).astype(jnp.bfloat16)

    bounds_copy.wait()
    over_windows(pick)

    for stage in range(STAGES):
        at = stage * stage_rows
        for piece in range(PIECES):
            vocab_copy(stage, piece).wait()

        def take(b, start, slot):
            ids_at = pl.ds(pl.multiple_of(b * IDS_PER_BLOCK, LANES), IDS_PER_BLOCK)
            found = mm(held[at : at + stage_rows, ids_at], picks[slot])
            gathered[pl.ds(start, WINDOW), at : at + stage_rows] += found.T.astype(jnp.bfloat16)

        over_windows(take)

    used = lax.shift_right_logical(bounds[blocks, 0] + CHUNK - 1, CHUNK_BITS)
    lax.fori_loop(0, used, project, 0)
    lax.fori_loop(used, chunks, zero, 0)

    hard = turned[...].T[0:ROWS]
    lane = iota((ROWS, width), 1)
    misc = jnp.concatenate([squares[...], jnp.zeros((ROWS - squares.shape[0], width), jnp.float32)])
    for i in range(per_shard):
        misc += jnp.where(lane == shard * per_shard + i, hard[:, i : i + 1], 0.0)
    misc = misc.astype(jnp.bfloat16)
    mine = lax.axis_index("mp") == shard
    for i in range(2):
        for j in range(2):
            quarter = (core ^ i) * 2 + (side_y ^ j)
            part = residual[:, pl.ds(pl.multiple_of(quarter * width, LANES), width)]
            out = outs[2 * i + j]
            out[pl.ds(tokens + chunks * ROWS, ROWS), :] = misc
            out[pl.ds(tokens + (chunks + 1) * ROWS, ROWS), :] = jnp.where(mine, part, 0.0).astype(
                jnp.bfloat16
            )


def pool_kernel(
    ids_ref,
    own_ref,
    core_ref,
    far_ref,
    member_ref,
    raise_ref,
    pooled_ref,
    slope_ref,
    reduced_ref,
    misc_ref,
    raised,
    model_width,
):
    texts, length = ids_ref.shape
    tokens = texts * length
    chunks = tokens // CHUNK
    width = own_ref.shape[1]
    quarter = quarter_of(lax.axis_index("dp"))

    def summed(start, size):
        rows = pl.ds(start, size)
        return (
            own_ref[rows, :].astype(jnp.float32)
            + core_ref[rows, :].astype(jnp.float32)
            + far_ref[rows, :].astype(jnp.float32)
        )

    misc = summed(tokens + chunks * ROWS, ROWS)
    misc_ref[...] = misc
    inverse = lax.rsqrt(misc / model_width + 1e-05)
    raised[...] = jnp.zeros_like(raised)
    raised[0:ROWS, :] = raise_ref[:, pl.ds(pl.multiple_of(quarter * width, LANES), width)]
    total = jnp.zeros((ROWS, width), jnp.float32)
    for k in range(chunks):
        scale = inverse[k : k + 1]
        reduced = (summed(tokens + k * ROWS, ROWS) * scale).astype(jnp.bfloat16)
        reduced_ref[:, k * CHUNK : (k + 1) * CHUNK] = reduced
        stacked = jnp.concatenate(
            [reduced.astype(jnp.float32), jnp.broadcast_to(scale, (LANES - ROWS, CHUNK))]
        )
        turned = stacked.T
        low = turned.astype(jnp.bfloat16)
        linear = summed(k * CHUNK, CHUNK) * turned[:, ROWS : ROWS + 1] + mm(low, raised[...])
        sigma = 1.0 / (1.0 + jnp.exp(-linear))
        slope_ref[pl.ds(k * CHUNK, CHUNK), :] = sigma * (1.0 + linear * (1.0 - sigma))
        member = member_ref[pl.ds(k * CHUNK, CHUNK), :].astype(jnp.float32).T
        member = member[0:ROWS].astype(jnp.bfloat16)
        high, rest = split(linear * sigma)
        total += mm(member, high) + mm(member, rest)
    total += summed(tokens + (chunks + 1) * ROWS, ROWS)
    counts = jnp.sum((ids_ref[...] != 0).astype(jnp.float32), axis=1, keepdims=True)
    pooled = total[0:texts] / counts
    pooled = jnp.concatenate([pooled, jnp.zeros((ROWS - texts, width), jnp.float32)])
    for to in range(pooled_ref.shape[0]):
        pooled_ref[to] = pooled.astype(jnp.bfloat16)


def both_sides(pooled_ref, shard, shards):
    return jnp.concatenate([pooled_ref[shard], pooled_ref[shards + shard]], axis=0)


def dots_kernel(pooled_ref, dots_ref, shards):
    dots = jnp.zeros((2 * ROWS, 2 * ROWS), jnp.float32)
    for shard in range(shards):
        block = both_sides(pooled_ref, shard, shards)
        dots += mm(block, block, NT)
    wide = jnp.concatenate([dots, jnp.zeros((2 * ROWS, LANES - 2 * ROWS), jnp.float32)], axis=1)
    for to in range(dots_ref.shape[0]):
        dots_ref[to] = wide


def score_kernel(
    ids_ref,
    pooled_ref,
    dots_ref,
    misc_ref,
    slope_ref,
    reduced_ref,
    member_ref,
    sharp_ref,
    embed_ref,
    loss_ref,
    up_ref,
    shards,
    negatives,
):
    texts, length = ids_ref.shape
    tokens = texts * length
    chunks = tokens // CHUNK
    rows = 2 * ROWS
    width = pooled_ref.shape[2]
    per_shard = loss_ref.shape[1]
    group, shard = lax.axis_index("group"), lax.axis_index("dp")
    dots = dots_ref[0]
    for part in range(1, dots_ref.shape[0]):
        dots += dots_ref[part]
    dots = dots[:, 0:rows]
    down, across = iota((rows, rows), 0), iota((rows, rows), 1)
    same = down == across
    real = (lax.rem(down, ROWS) < texts) & (lax.rem(across, ROWS) < texts)
    diagonal = jnp.where(same, dots, 0.0)
    rnorm_row = lax.rsqrt(jnp.sum(diagonal, axis=0, keepdims=True) + 1e-06)
    rnorm_col = lax.rsqrt(jnp.sum(diagonal, axis=1, keepdims=True) + 1e-06)
    sharpness = sharp_ref[0]
    cosine = dots * rnorm_col * rnorm_row
    scores = sharpness * cosine
    keep = real & ~same
    top = jnp.max(jnp.where(keep, scores, -jnp.inf), axis=0, keepdims=True)
    top = jnp.where(lax.rem(across[0:1], ROWS) < texts, top, 0.0)
    powers = jnp.exp(jnp.where(real, jnp.minimum(scores - top, 0.0), 0.0))
    hard = misc_ref[chunks : chunks + negatives, 0:rows].astype(jnp.int32) + ROWS
    times = jnp.zeros((rows, rows), jnp.float32)
    for k in range(negatives):
        times += jnp.where(hard[k : k + 1] == down, 1.0, 0.0)
    times = jnp.where(across < texts, times, 0.0)
    weights = (jnp.where(keep, 1.0, 0.0) + jnp.where(real, times, 0.0)) * powers
    total = jnp.sum(weights, axis=0, keepdims=True)
    total = jnp.where(lax.rem(across[0:1], ROWS) < texts, total, 1.0)
    pair = (down == lax.rem(across + ROWS, rows)) & real
    pair_score = jnp.sum(jnp.where(pair, scores, 0.0), axis=0, keepdims=True)
    losses = top + jnp.log(total) - pair_score
    grad_scores = (weights / total - jnp.where(pair, 1.0, 0.0)) / (2 * texts)
    coeff = (grad_scores * rnorm_col * rnorm_row).astype(jnp.bfloat16)
    radial = jnp.sum(grad_scores * cosine, axis=0, keepdims=True) * rnorm_row * rnorm_row

    first = shard * per_shard
    loss_col = jnp.sum(jnp.where(same, losses, 0.0), axis=1, keepdims=True)
    at = (iota((rows, LANES), 0) == group * ROWS + first + iota((rows, LANES), 1)) & (
        iota((rows, LANES), 1) < per_shard
    )
    loss_ref[...] = jnp.sum(jnp.where(at, loss_col, 0.0), axis=0, keepdims=True)[:, 0:per_shard]

    mine = both_sides(pooled_ref, shard, shards)
    along = mm(coeff.astype(jnp.float32).T.astype(jnp.bfloat16), mine)
    radial_col = jnp.sum(jnp.where(same, radial, 0.0), axis=1, keepdims=True)
    grad = sharpness * (along - radial_col * mine.astype(jnp.float32))
    grad = jnp.where(group == 0, grad[0:ROWS], grad[ROWS:rows])
    counts = jnp.sum((ids_ref[...] != 0).astype(jnp.float32), axis=1, keepdims=True)
    grad = grad[0:texts] / counts
    grad = jnp.concatenate([grad, jnp.zeros((LANES - texts, width), jnp.float32)])
    high, rest = split(grad)
    update = jnp.zeros((ROWS, width), jnp.float32)
    for k in range(chunks):
        member = member_ref[pl.ds(k * CHUNK, CHUNK), :]
        token_grad = mm(member, high) + mm(member, rest)
        local = (token_grad * slope_ref[pl.ds(k * CHUNK, CHUNK), :]).astype(jnp.bfloat16)
        update += mm(reduced_ref[:, k * CHUNK : (k + 1) * CHUNK], local)
    for to in range(up_ref.shape[0]):
        up_ref[to] = update

    rnorm_own = jnp.where(group == 0, rnorm_col[0:ROWS], rnorm_col[ROWS:rows])
    chosen = iota((ROWS, ROWS), 1) == iota((ROWS, ROWS), 0) + first
    chosen = jnp.where(chosen & (iota((ROWS, ROWS), 0) < per_shard), 1.0, 0.0).astype(jnp.bfloat16)
    for quarter in range(shards):
        block = pooled_ref[group * shards + quarter_of(quarter)].astype(jnp.float32) * rnorm_own
        picked = mm(chosen, block.astype(jnp.bfloat16)).astype(jnp.bfloat16)
        embed_ref[0, :, quarter * width : (quarter + 1) * width] = picked[0:per_shard]


def any_spec():
    return pl.BlockSpec(memory_space=pl.ANY)


def vmem_spec():
    return pl.BlockSpec(memory_space=pltpu.VMEM)


def smem_spec():
    return pl.BlockSpec(memory_space=pltpu.SMEM)


def split_body(
    query_passage_words,
    difficult_distractors,
    vocabulary_vectors,
    layer_weight_matrix,
    lowering_factor_matrix,
    raising_factor_matrix,
    logit_sharpness,
):
    shards, parts = lax.axis_size("dp"), lax.axis_size("mp")
    ids = query_passage_words[0]
    texts, length = ids.shape
    tokens = texts * length
    chunks = tokens // CHUNK
    features, vocab = vocabulary_vectors.shape
    blocks = vocab // IDS_PER_BLOCK
    block_rows = 8 * pl.cdiv(blocks + 1, 8)
    per_shard, negatives = difficult_distractors.shape
    rank = lowering_factor_matrix.shape[0]
    part_width = layer_weight_matrix.shape[1]
    width = part_width // shards
    rows = tokens + (chunks + 2) * ROWS
    slots = (tokens + blocks * (WINDOW + ROWS - 2)) // WINDOW + 1
    params = pltpu.CompilerParams(vmem_limit_bytes=VMEM_BYTES)
    half = jax.ShapeDtypeStruct((rows, width), jnp.bfloat16)
    own0, own1, away0, away1, member = pl.pallas_call(
        project_kernel,
        out_shape=[half] * 4 + [jax.ShapeDtypeStruct((tokens, LANES), jnp.bfloat16)],
        in_specs=[vmem_spec()] * 2 + [any_spec()] * 3,
        out_specs=[vmem_spec()] * 5,
        scratch_shapes=[
            pltpu.VMEM((features, vocab), jnp.bfloat16),
            pltpu.VMEM((4, features, width), jnp.bfloat16),
            pltpu.VMEM((rank, features), jnp.bfloat16),
            pltpu.VMEM((features, LANES), jnp.bfloat16),
            pltpu.VMEM((slots, IDS_PER_BLOCK, WINDOW), jnp.bfloat16),
            pltpu.VMEM((tokens + WINDOW, features), jnp.bfloat16),
            pltpu.VMEM((tokens + WINDOW, LANES), jnp.float32),
            pltpu.VMEM((LANES, LANES), jnp.float32),
            pltpu.VMEM((texts, length), jnp.float32),
            pltpu.VMEM((8, width), jnp.float32),
            pltpu.VMEM((ROWS, features), jnp.float32),
            pltpu.VMEM((block_rows, length), jnp.int32),
            pltpu.SMEM((block_rows, length), jnp.int32),
            pltpu.SemaphoreType.DMA((STAGES, PIECES)),
            pltpu.SemaphoreType.DMA((4,)),
            pltpu.SemaphoreType.DMA,
            pltpu.SemaphoreType.DMA,
        ],
        compiler_params=params,
        name="project",
    )(
        ids,
        difficult_distractors,
        vocabulary_vectors,
        layer_weight_matrix,
        lowering_factor_matrix,
    )
    other_core = [(d, d ^ 1) for d in range(shards)]
    other_y = [(d, d ^ 2) for d in range(shards)]
    core1 = lax.ppermute(away1, "dp", other_core)
    core0 = lax.ppermute(away0, "dp", other_core)
    chip1 = (own1.astype(jnp.float32) + core1.astype(jnp.float32)).astype(jnp.bfloat16)
    far = lax.ppermute(chip1, "dp", other_y)
    pooled, slope, reduced, misc = pl.pallas_call(
        functools.partial(pool_kernel, model_width=float(features * shards)),
        out_shape=[
            jax.ShapeDtypeStruct((2 * shards, ROWS, width), jnp.bfloat16),
            jax.ShapeDtypeStruct((tokens, width), jnp.float32),
            jax.ShapeDtypeStruct((ROWS, tokens), jnp.bfloat16),
            jax.ShapeDtypeStruct((ROWS, width), jnp.float32),
        ],
        in_specs=[vmem_spec()] * 6,
        out_specs=[vmem_spec()] * 4,
        scratch_shapes=[pltpu.VMEM((LANES, width), jnp.bfloat16)],
        compiler_params=params,
        name="pool",
    )(ids, own0, core0, far, member, raising_factor_matrix)
    sides = ("group", "dp")
    pooled = lax.all_to_all(pooled, sides, 0, 0)
    dots = pl.pallas_call(
        functools.partial(dots_kernel, shards=shards),
        out_shape=jax.ShapeDtypeStruct((parts, 2 * ROWS, LANES), jnp.float32),
        in_specs=[vmem_spec()],
        out_specs=vmem_spec(),
        compiler_params=params,
        name="dots",
    )(pooled)
    dots = lax.all_to_all(dots, "mp", 0, 0)
    embeddings, losses, update = pl.pallas_call(
        functools.partial(score_kernel, shards=shards, negatives=negatives),
        out_shape=[
            jax.ShapeDtypeStruct((1, per_shard, part_width), jnp.bfloat16),
            jax.ShapeDtypeStruct((1, per_shard), jnp.float32),
            jax.ShapeDtypeStruct((2 * shards, ROWS, width), jnp.float32),
        ],
        in_specs=[vmem_spec()] * 7 + [smem_spec()],
        out_specs=[vmem_spec()] * 3,
        compiler_params=params,
        name="score",
    )(ids, pooled, dots, misc, slope, reduced, member, logit_sharpness)
    update = lax.all_to_all(update, sides, 0, 0)
    columns = [update[quarter_of(q)] + update[shards + quarter_of(q)] for q in range(shards)]
    return (embeddings, losses, jnp.concatenate(columns, axis=1))


def body(words, hard, vocabulary, weight, lowering, raising, sharpness):
    shards, parts = lax.axis_size("dp"), lax.axis_size("mp")
    texts, length = words.shape[1:]
    features, vocab = vocabulary.shape
    negatives = hard.shape[1]
    square = shards == 4 and features == weight.shape[1] and parts == shards
    small = texts <= ROWS - 2 and length == LANES and texts * length <= 2048
    even = (texts * length) % CHUNK == 0 and vocab % IDS_PER_BLOCK == 0
    fits = features * vocab <= 2**24 and features % (4 * LANES) == 0
    spare = texts * length // CHUNK + negatives <= ROWS and lowering.shape[0] == ROWS
    fast = square and small and even and fits and spare and lax.axis_size("group") == 2
    chosen = split_body if fast else general_body
    return chosen(words, hard, vocabulary, weight, lowering, raising, sharpness)


def solution(mesh):
    in_specs = (
        P("group", None, None),
        P("dp", None),
        P("dp", None),
        P("dp", "mp"),
        P(),
        P(None, "mp"),
        P(),
    )
    out_specs = (P("group", "dp", "mp"), P("group", "dp"), P(None, "mp"))
    return jax.shard_map(body, mesh=mesh, in_specs=in_specs, out_specs=out_specs, check_vma=False)
```

```python
import functools

import jax
import jax.numpy as jnp
from jax import lax
from jax.experimental import pallas as pl
from jax.experimental.pallas import tpu as pltpu
from jax.sharding import PartitionSpec as P


def general_body(
    query_passage_words,
    difficult_distractors,
    vocabulary_vectors,
    layer_weight_matrix,
    lowering_factor_matrix,
    raising_factor_matrix,
    logit_sharpness,
):
    group_index = lax.axis_index("group")
    shard_index = lax.axis_index("dp")
    part_index = lax.axis_index("mp")
    shard_count = lax.axis_size("dp")
    side_ids = query_passage_words[0]
    text_count = side_ids.shape[0]
    length = side_ids.shape[1]
    per_shard = text_count // shard_count
    own_ids = lax.dynamic_slice_in_dim(side_ids, shard_index * per_shard, per_shard, 0)
    columns = jnp.take(vocabulary_vectors, side_ids.reshape(-1), axis=1)
    inputs = lax.all_to_all(columns, "dp", split_axis=1, concat_axis=0, tiled=True)
    tokens = inputs.shape[1]
    feature_width = raising_factor_matrix.shape[1]
    wide_inputs = inputs.astype(jnp.float32)
    inverse = lax.rsqrt(jnp.mean(wide_inputs * wide_inputs, axis=0) + 1e-05)
    normed_state = (wide_inputs * inverse[None, :]).astype(jnp.bfloat16)
    linear_map = lax.dot_general(
        lax.all_gather(layer_weight_matrix, "dp", axis=0, tiled=True),
        normed_state,
        (((0,), (0,)), ((), ())),
        preferred_element_type=jnp.float32,
    )
    reduced_sum = jnp.dot(
        lowering_factor_matrix, normed_state, preferred_element_type=jnp.float32
    ).astype(jnp.bfloat16)
    linear_map = linear_map + lax.dot_general(
        raising_factor_matrix,
        reduced_sum,
        (((0,), (0,)), ((), ())),
        preferred_element_type=jnp.float32,
    )
    own_inputs = lax.dynamic_slice_in_dim(
        inputs, part_index * feature_width, feature_width, 0
    ).astype(jnp.float32)
    hidden_state = own_inputs + jax.nn.silu(linear_map)
    mask = (own_ids != 0).astype(jnp.float32)
    counts = jnp.sum(mask, axis=1)
    summed = jnp.einsum("dnl,nl->nd", hidden_state.reshape(feature_width, per_shard, length), mask)
    pooled = (summed / counts[:, None]).astype(jnp.bfloat16)
    gathered = lax.all_gather(pooled, ("group", "dp"), axis=0, tiled=True)
    part_scores = lax.dot_general(
        pooled, gathered, (((1,), (1,)), ((), ())), preferred_element_type=jnp.float32
    )
    gathered_wide = gathered.astype(jnp.float32)
    part_norms = jnp.sum(gathered_wide * gathered_wide, axis=1)
    dots, norms = lax.psum((part_scores, part_norms), "mp")
    rnorm_all = lax.rsqrt(norms + 1e-06)
    all_count = gathered.shape[0]
    half_count = all_count // 2
    own_rows = (
        group_index * half_count + shard_index * per_shard + jnp.arange(per_shard, dtype=jnp.int32)
    )
    rnorm_own = jnp.take(rnorm_all, own_rows)
    cosine = dots * rnorm_own[:, None] * rnorm_all[None, :]
    multiplier_factor = logit_sharpness[0]
    scores = multiplier_factor * cosine
    column_ids = jnp.arange(all_count, dtype=jnp.int32)
    keep = column_ids[None, :] != own_rows[:, None]
    pair = (own_rows + half_count) % all_count
    weight = (group_index == 0).astype(jnp.float32)
    neg_cols = half_count + difficult_distractors
    top = jnp.max(jnp.where(keep, scores, -jnp.inf), axis=1)
    safe_scores = jnp.where(keep, scores, top[:, None])
    expd = jnp.where(keep, jnp.exp(safe_scores - top[:, None]), 0.0)
    neg_exp = (
        jnp.exp(jnp.minimum(jnp.take_along_axis(scores, neg_cols, axis=1) - top[:, None], 0.0))
        * weight
    )
    total = jnp.sum(expd, axis=1) + jnp.sum(neg_exp, axis=1)
    pair_score = jnp.take_along_axis(scores, pair[:, None], axis=1)[:, 0]
    losses = top + jnp.log(total) - pair_score
    onehot = (column_ids[None, None, :] == neg_cols[:, :, None]).astype(jnp.float32)
    probs = (expd + jnp.einsum("rk,rkc->rc", neg_exp, onehot)) / total[:, None]
    target = (column_ids[None, :] == pair[:, None]).astype(jnp.float32)
    grad_scores = (probs - target) / all_count
    coeff = (grad_scores * rnorm_own[:, None] * rnorm_all[None, :]).astype(jnp.bfloat16)
    along = jnp.dot(coeff, gathered, preferred_element_type=jnp.float32)
    pooled_wide = pooled.astype(jnp.float32)
    radial = jnp.sum(grad_scores * cosine, axis=1) * rnorm_own * rnorm_own
    embedding_gradient = multiplier_factor * (along - radial[:, None] * pooled_wide)
    token_grad = jnp.einsum("nd,nl->dnl", embedding_gradient / counts[:, None], mask).reshape(
        feature_width, tokens
    )
    sigma = jax.nn.sigmoid(linear_map)
    local = (token_grad * sigma * (1.0 + linear_map * (1.0 - sigma))).astype(jnp.bfloat16)
    up_portion = lax.dot_general(
        reduced_sum, local, (((1,), (1,)), ((), ())), preferred_element_type=jnp.float32
    )
    adapter_up_gradient = lax.psum(up_portion, ("group", "dp"))
    embeddings = (pooled_wide * rnorm_own[:, None]).astype(jnp.bfloat16)[None]
    return (embeddings, losses[None], adapter_up_gradient)


BLOCK_BITS, WINDOW_BITS, CHUNK_BITS, ROW_BITS = 10, 6, 8, 4
IDS_PER_BLOCK = 1 << BLOCK_BITS
WINDOW = 1 << WINDOW_BITS
CHUNK = 1 << CHUNK_BITS
ROWS = 1 << ROW_BITS
LANES = 128
NT = (((1,), (1,)), ((), ()))
VMEM_BYTES = 60 * 1024 * 1024


def mm(a, b, dims=(((1,), (0,)), ((), ()))):
    return lax.dot_general(a, b, dims, preferred_element_type=jnp.float32)


def split(x):
    high = x.astype(jnp.bfloat16)
    return high, (x - high.astype(jnp.float32)).astype(jnp.bfloat16)


def iota(shape, dim):
    return lax.broadcasted_iota(jnp.int32, shape, dim)


def quarter_of(dp_index, cores=2):
    return (dp_index % cores) * 2 + dp_index // cores


def route_kernel(ids_ref, values_ref, member_ref, bounds_ref, ranks, vocab):
    texts, length = ids_ref.shape
    tokens = texts * length
    blocks = vocab // IDS_PER_BLOCK
    ids = ids_ref[...]
    valid = ids != 0
    block_of = jnp.where(valid, lax.shift_right_logical(ids, BLOCK_BITS), blocks)
    block_rows = bounds_ref.shape[0]
    block_id = iota((block_rows, length), 0)
    below = jnp.zeros((block_rows, length), jnp.float32)
    for text in range(texts):
        below += jnp.where(block_of[text : text + 1] < block_id, 1.0, 0.0)
    before = jnp.broadcast_to(jnp.sum(below, axis=1, keepdims=True), (block_rows, length))
    bounds_ref[...] = before.astype(jnp.int32)
    earlier = jnp.where(iota((length, length), 0) < iota((length, length), 1), 1.0, 0.0).astype(
        jnp.bfloat16
    )
    for text in range(texts):
        here = jnp.where(block_of[text : text + 1] == block_id, 1.0, 0.0)
        inside = mm(here.astype(jnp.bfloat16), earlier)
        ranks[pl.ds(text, 1), :] = jnp.sum(here * (inside + before), axis=0, keepdims=True)
        before += jnp.broadcast_to(jnp.sum(here, axis=1, keepdims=True), (block_rows, length))
    text_of = iota((texts, length), 0)
    carried = jnp.where(valid, lax.shift_left(ids, ROW_BITS) + text_of, 0).astype(jnp.float32)
    rank = ranks[...]

    def place(p, carry):
        position = (iota((LANES, length), 0) + p * LANES).astype(jnp.float32)
        total = jnp.zeros((LANES, length), jnp.float32)
        for text in range(texts):
            total += jnp.where(rank[text : text + 1] == position, carried[text : text + 1], 0.0)
        found = jnp.broadcast_to(jnp.sum(total, axis=1, keepdims=True), (LANES, LANES))
        found = found.astype(jnp.int32)
        token = lax.shift_right_logical(found, ROW_BITS)
        start = pl.multiple_of(p * LANES, LANES)
        values_ref[pl.ds(start, LANES), :] = jnp.where(token == 0, -vocab, token)
        real = (token != 0) & ((found & (ROWS - 1)) == iota((LANES, LANES), 1))
        member_ref[pl.ds(start, LANES), :] = jnp.where(real, 1.0, 0.0).astype(jnp.bfloat16)
        return carry

    lax.fori_loop(0, tokens // LANES, place, 0)
    values_ref[pl.ds(tokens, WINDOW), :] = jnp.full((WINDOW, LANES), -vocab, jnp.int32)


def gather_kernel(bounds, values_ref, vocab_ref, gathered, held, held_sems):
    features, vocab = vocab_ref.shape
    blocks = vocab // IDS_PER_BLOCK
    rows = gathered.shape[0]

    def vocab_copy(b):
        columns = pl.ds(pl.multiple_of(b * IDS_PER_BLOCK, LANES), IDS_PER_BLOCK)
        return pltpu.make_async_copy(vocab_ref.at[:, columns], held.at[b], held_sems.at[b])

    for b in range(blocks):
        vocab_copy(b).start()

    def clear(p, carry):
        at = pl.multiple_of(p * WINDOW, WINDOW)
        gathered[pl.ds(at, WINDOW), :] = jnp.zeros((WINDOW, features), jnp.bfloat16)
        return carry

    lax.fori_loop(0, rows // WINDOW, clear, 0)

    def take(b, carry):
        first, last = bounds[b, 0], bounds[b + 1, 0]
        aligned = lax.shift_left(lax.shift_right_logical(first, ROW_BITS), ROW_BITS)
        windows = lax.shift_right_logical(last - aligned + WINDOW - 1, WINDOW_BITS)
        windows = jnp.where(last > first, windows, 0)
        vocab_copy(b).wait()

        def window(w, carry):
            start = pl.multiple_of(aligned + w * WINDOW, ROWS)
            wanted = values_ref[pl.ds(start, WINDOW), :]
            wanted -= b * IDS_PER_BLOCK + iota((WINDOW, LANES), 1)
            picked = [
                jnp.where(wanted == j * LANES, 1.0, 0.0).astype(jnp.bfloat16)
                for j in range(IDS_PER_BLOCK // LANES)
            ]
            found = mm(jnp.concatenate(picked, axis=1), held[b], NT)
            gathered[pl.ds(start, WINDOW), :] += found.astype(jnp.bfloat16)
            return carry

        return lax.fori_loop(0, windows, window, carry)

    lax.fori_loop(0, blocks, take, 0)


def split_quarter(i, j, cores=2):
    shard = lax.axis_index("dp")
    core, side_y = lax.rem(shard, cores), lax.div(shard, cores)
    return (core ^ i) * 2 + (side_y ^ j)


def weight_copies(weight_ref, weight, sems, i):
    width = weight.shape[2]
    return [
        pltpu.make_async_copy(
            weight_ref.at[:, pl.ds(pl.multiple_of(split_quarter(i, j) * width, LANES), width)],
            weight.at[j],
            sems.at[j],
        )
        for j in range(2)
    ]


def away_kernel(
    bounds,
    gathered,
    member_ref,
    hard_ref,
    weight_ref,
    lower_ref,
    out1,
    out0,
    extra_ref,
    weight,
    lower,
    turned,
    squares,
    residual,
    weight_sems,
    lower_sem,
    blocks,
):
    features = gathered.shape[1]
    tokens, width = member_ref.shape[0], out0.shape[1]
    chunks = tokens // CHUNK
    per_shard, negatives = hard_ref.shape
    shard = lax.axis_index("dp")
    copies = weight_copies(weight_ref, weight, weight_sems, 1)
    lower_copy = pltpu.make_async_copy(
        lower_ref.at[:, pl.ds(pl.multiple_of(shard * features, LANES), features)], lower, lower_sem
    )
    for copy in copies + [lower_copy]:
        copy.start()
    residual[...] = jnp.zeros_like(residual)
    squares[...] = jnp.zeros_like(squares)
    turned[...] = jnp.zeros_like(turned)
    turned[0:per_shard, chunks : chunks + negatives] = hard_ref[...].astype(jnp.float32)
    for copy in copies + [lower_copy]:
        copy.wait()

    def project(k, carry):
        start = pl.multiple_of(k * CHUNK, CHUNK)
        x = gathered[pl.ds(start, CHUNK), :]
        out1[pl.ds(start, CHUNK), :] = mm(x, weight[1]).astype(jnp.bfloat16)
        out0[pl.ds(start, CHUNK), :] = mm(x, weight[0]).astype(jnp.bfloat16)
        reduced = mm(lower[...], x, NT).astype(jnp.bfloat16)
        extra_ref[pl.ds(pl.multiple_of(k * ROWS, ROWS), ROWS), :] = reduced
        out1[pl.ds(pl.multiple_of(tokens + k * ROWS, ROWS), ROWS), :] = reduced
        ones = jnp.ones((ROWS, features), jnp.bfloat16)
        squares[pl.ds(k, 1), :] = mm(ones, x * x, NT)[0:1]
        member = member_ref[pl.ds(start, CHUNK), :].astype(jnp.float32).T.astype(jnp.bfloat16)
        residual[...] += mm(member[0:ROWS], x)
        return carry

    def zero(k, carry):
        start = pl.multiple_of(k * CHUNK, CHUNK)
        out1[pl.ds(start, CHUNK), :] = jnp.zeros((CHUNK, width), jnp.bfloat16)
        out0[pl.ds(start, CHUNK), :] = jnp.zeros((CHUNK, width), jnp.bfloat16)
        none = jnp.zeros((ROWS, width), jnp.bfloat16)
        extra_ref[pl.ds(pl.multiple_of(k * ROWS, ROWS), ROWS), :] = none
        out1[pl.ds(pl.multiple_of(tokens + k * ROWS, ROWS), ROWS), :] = none
        return carry

    used = lax.shift_right_logical(bounds[blocks, 0] + CHUNK - 1, CHUNK_BITS)
    lax.fori_loop(0, used, project, 0)
    lax.fori_loop(used, chunks, zero, 0)
    hard = turned[...].T[0:ROWS]
    lane = iota((ROWS, width), 1)
    misc = jnp.concatenate([squares[...], jnp.zeros((ROWS - squares.shape[0], width), jnp.float32)])
    for i in range(per_shard):
        misc += jnp.where(lane == shard * per_shard + i, hard[:, i : i + 1], 0.0)
    extra_ref[pl.ds(chunks * ROWS, ROWS), :] = misc.astype(jnp.bfloat16)
    out1[pl.ds(tokens + chunks * ROWS, ROWS), :] = misc.astype(jnp.bfloat16)

    mine = lax.axis_index("mp") == shard

    def part(i, j):
        start = pl.multiple_of(split_quarter(i, j) * width, LANES)
        return jnp.where(mine, residual[:, pl.ds(start, width)], 0.0).astype(jnp.bfloat16)

    out1[pl.ds(tokens + (chunks + 1) * ROWS, ROWS), :] = part(1, 1)
    out0[pl.ds(tokens, ROWS), :] = part(1, 0)
    extra_ref[pl.ds((chunks + 1) * ROWS, ROWS), :] = part(0, 1)
    extra_ref[pl.ds((chunks + 2) * ROWS, ROWS), :] = part(0, 0)


def own_kernel(
    bounds, gathered, weight_ref, extra_ref, out1, out0, weight, weight_sems, blocks, tokens
):
    width = out0.shape[1]
    chunks = tokens // CHUNK
    copies = weight_copies(weight_ref, weight, weight_sems, 0)
    for copy in copies:
        copy.start()
    for copy in copies:
        copy.wait()

    def project(k, carry):
        start = pl.multiple_of(k * CHUNK, CHUNK)
        x = gathered[pl.ds(start, CHUNK), :]
        out1[pl.ds(start, CHUNK), :] = mm(x, weight[1]).astype(jnp.bfloat16)
        out0[pl.ds(start, CHUNK), :] = mm(x, weight[0]).astype(jnp.bfloat16)
        return carry

    def zero(k, carry):
        start = pl.multiple_of(k * CHUNK, CHUNK)
        out1[pl.ds(start, CHUNK), :] = jnp.zeros((CHUNK, width), jnp.bfloat16)
        out0[pl.ds(start, CHUNK), :] = jnp.zeros((CHUNK, width), jnp.bfloat16)
        return carry

    used = lax.shift_right_logical(bounds[blocks, 0] + CHUNK - 1, CHUNK_BITS)
    lax.fori_loop(0, used, project, 0)
    lax.fori_loop(used, chunks, zero, 0)
    size = (chunks + 2) * ROWS
    out1[pl.ds(tokens, size), :] = extra_ref[0:size, :]
    out0[pl.ds(tokens, ROWS), :] = extra_ref[size : size + ROWS, :]


def pool_kernel(
    ids_ref,
    own_ref,
    core_ref,
    chip_ref,
    far_ref,
    member_ref,
    raise_ref,
    pooled_ref,
    slope_ref,
    reduced_ref,
    misc_ref,
    raised,
    model_width,
):
    texts, length = ids_ref.shape
    tokens = texts * length
    chunks = tokens // CHUNK
    width = own_ref.shape[1]
    quarter = quarter_of(lax.axis_index("dp"))

    def summed(*pieces):
        return sum(ref[pl.ds(start, size), :].astype(jnp.float32) for ref, start, size in pieces)

    def statistics(row):
        return summed((chip_ref, tokens + row, ROWS), (far_ref, tokens + row, ROWS))

    misc = statistics(chunks * ROWS)
    misc_ref[...] = misc
    inverse = lax.rsqrt(misc / model_width + 1e-05)
    raised[...] = jnp.zeros_like(raised)
    raised[0:ROWS, :] = raise_ref[:, pl.ds(pl.multiple_of(quarter * width, LANES), width)]
    total = jnp.zeros((ROWS, width), jnp.float32)
    for k in range(chunks):
        scale = inverse[k : k + 1]
        reduced = (statistics(k * ROWS) * scale).astype(jnp.bfloat16)
        reduced_ref[:, k * CHUNK : (k + 1) * CHUNK] = reduced
        stacked = jnp.concatenate(
            [reduced.astype(jnp.float32), jnp.broadcast_to(scale, (LANES - ROWS, CHUNK))]
        )
        turned = stacked.T
        low = turned.astype(jnp.bfloat16)
        at = k * CHUNK
        linear = summed((own_ref, at, CHUNK), (core_ref, at, CHUNK), (far_ref, at, CHUNK))
        linear = linear * turned[:, ROWS : ROWS + 1] + mm(low, raised[...])
        sigma = 1.0 / (1.0 + jnp.exp(-linear))
        slope_ref[pl.ds(k * CHUNK, CHUNK), :] = sigma * (1.0 + linear * (1.0 - sigma))
        member = member_ref[pl.ds(k * CHUNK, CHUNK), :].astype(jnp.float32).T
        member = member[0:ROWS].astype(jnp.bfloat16)
        high, rest = split(linear * sigma)
        total += mm(member, high) + mm(member, rest)
    total += summed(
        (own_ref, tokens, ROWS),
        (core_ref, tokens, ROWS),
        (far_ref, tokens + (chunks + 1) * ROWS, ROWS),
    )
    counts = jnp.sum((ids_ref[...] != 0).astype(jnp.float32), axis=1, keepdims=True)
    pooled = total[0:texts] / counts
    pooled = jnp.concatenate([pooled, jnp.zeros((ROWS - texts, width), jnp.float32)])
    for to in range(pooled_ref.shape[0]):
        pooled_ref[to] = pooled.astype(jnp.bfloat16)


def both_sides(pooled_ref, shard, shards):
    return jnp.concatenate([pooled_ref[shard], pooled_ref[shards + shard]], axis=0)


def dots_kernel(pooled_ref, dots_ref, shards):
    dots = jnp.zeros((2 * ROWS, 2 * ROWS), jnp.float32)
    for shard in range(shards):
        block = both_sides(pooled_ref, shard, shards)
        dots += mm(block, block, NT)
    wide = jnp.concatenate([dots, jnp.zeros((2 * ROWS, LANES - 2 * ROWS), jnp.float32)], axis=1)
    for to in range(dots_ref.shape[0]):
        dots_ref[to] = wide


def score_kernel(
    ids_ref,
    pooled_ref,
    dots_ref,
    misc_ref,
    slope_ref,
    reduced_ref,
    member_ref,
    sharp_ref,
    embed_ref,
    loss_ref,
    up_ref,
    shards,
    negatives,
):
    texts, length = ids_ref.shape
    tokens = texts * length
    chunks = tokens // CHUNK
    rows = 2 * ROWS
    width = pooled_ref.shape[2]
    per_shard = loss_ref.shape[1]
    group, shard = lax.axis_index("group"), lax.axis_index("dp")
    dots = dots_ref[0]
    for part in range(1, dots_ref.shape[0]):
        dots += dots_ref[part]
    dots = dots[:, 0:rows]
    down, across = iota((rows, rows), 0), iota((rows, rows), 1)
    same = down == across
    real = (lax.rem(down, ROWS) < texts) & (lax.rem(across, ROWS) < texts)
    diagonal = jnp.where(same, dots, 0.0)
    rnorm_row = lax.rsqrt(jnp.sum(diagonal, axis=0, keepdims=True) + 1e-06)
    rnorm_col = lax.rsqrt(jnp.sum(diagonal, axis=1, keepdims=True) + 1e-06)
    sharpness = sharp_ref[0]
    cosine = dots * rnorm_col * rnorm_row
    scores = sharpness * cosine
    keep = real & ~same
    top = jnp.max(jnp.where(keep, scores, -jnp.inf), axis=0, keepdims=True)
    top = jnp.where(lax.rem(across[0:1], ROWS) < texts, top, 0.0)
    powers = jnp.exp(jnp.where(real, jnp.minimum(scores - top, 0.0), 0.0))
    hard = misc_ref[chunks : chunks + negatives, 0:rows].astype(jnp.int32) + ROWS
    times = jnp.zeros((rows, rows), jnp.float32)
    for k in range(negatives):
        times += jnp.where(hard[k : k + 1] == down, 1.0, 0.0)
    times = jnp.where(across < texts, times, 0.0)
    weights = (jnp.where(keep, 1.0, 0.0) + jnp.where(real, times, 0.0)) * powers
    total = jnp.sum(weights, axis=0, keepdims=True)
    total = jnp.where(lax.rem(across[0:1], ROWS) < texts, total, 1.0)
    pair = (down == lax.rem(across + ROWS, rows)) & real
    pair_score = jnp.sum(jnp.where(pair, scores, 0.0), axis=0, keepdims=True)
    losses = top + jnp.log(total) - pair_score
    grad_scores = (weights / total - jnp.where(pair, 1.0, 0.0)) / (2 * texts)
    coeff = (grad_scores * rnorm_col * rnorm_row).astype(jnp.bfloat16)
    radial = jnp.sum(grad_scores * cosine, axis=0, keepdims=True) * rnorm_row * rnorm_row

    first = shard * per_shard
    loss_col = jnp.sum(jnp.where(same, losses, 0.0), axis=1, keepdims=True)
    at = (iota((rows, LANES), 0) == group * ROWS + first + iota((rows, LANES), 1)) & (
        iota((rows, LANES), 1) < per_shard
    )
    loss_ref[...] = jnp.sum(jnp.where(at, loss_col, 0.0), axis=0, keepdims=True)[:, 0:per_shard]

    mine = both_sides(pooled_ref, shard, shards)
    along = mm(coeff.astype(jnp.float32).T.astype(jnp.bfloat16), mine)
    radial_col = jnp.sum(jnp.where(same, radial, 0.0), axis=1, keepdims=True)
    grad = sharpness * (along - radial_col * mine.astype(jnp.float32))
    grad = jnp.where(group == 0, grad[0:ROWS], grad[ROWS:rows])
    counts = jnp.sum((ids_ref[...] != 0).astype(jnp.float32), axis=1, keepdims=True)
    grad = grad[0:texts] / counts
    grad = jnp.concatenate([grad, jnp.zeros((LANES - texts, width), jnp.float32)])
    high, rest = split(grad)
    update = jnp.zeros((ROWS, width), jnp.float32)
    for k in range(chunks):
        member = member_ref[pl.ds(k * CHUNK, CHUNK), :]
        token_grad = mm(member, high) + mm(member, rest)
        local = (token_grad * slope_ref[pl.ds(k * CHUNK, CHUNK), :]).astype(jnp.bfloat16)
        update += mm(reduced_ref[:, k * CHUNK : (k + 1) * CHUNK], local)
    for to in range(up_ref.shape[0]):
        up_ref[to] = update

    rnorm_own = jnp.where(group == 0, rnorm_col[0:ROWS], rnorm_col[ROWS:rows])
    chosen = iota((ROWS, ROWS), 1) == iota((ROWS, ROWS), 0) + first
    chosen = jnp.where(chosen & (iota((ROWS, ROWS), 0) < per_shard), 1.0, 0.0).astype(jnp.bfloat16)
    for quarter in range(shards):
        block = pooled_ref[group * shards + quarter_of(quarter)].astype(jnp.float32) * rnorm_own
        picked = mm(chosen, block.astype(jnp.bfloat16)).astype(jnp.bfloat16)
        embed_ref[0, :, quarter * width : (quarter + 1) * width] = picked[0:per_shard]


def any_spec():
    return pl.BlockSpec(memory_space=pl.ANY)


def vmem_spec():
    return pl.BlockSpec(memory_space=pltpu.VMEM)


def smem_spec():
    return pl.BlockSpec(memory_space=pltpu.SMEM)


def split_body(
    query_passage_words,
    difficult_distractors,
    vocabulary_vectors,
    layer_weight_matrix,
    lowering_factor_matrix,
    raising_factor_matrix,
    logit_sharpness,
):
    shards, parts = lax.axis_size("dp"), lax.axis_size("mp")
    ids = query_passage_words[0]
    texts, length = ids.shape
    tokens = texts * length
    chunks = tokens // CHUNK
    features, vocab = vocabulary_vectors.shape
    blocks = vocab // IDS_PER_BLOCK
    block_rows = 8 * pl.cdiv(blocks + 1, 8)
    per_shard, negatives = difficult_distractors.shape
    rank = lowering_factor_matrix.shape[0]
    part_width = layer_weight_matrix.shape[1]
    width = part_width // shards
    rows = tokens + (chunks + 2) * ROWS
    params = pltpu.CompilerParams(vmem_limit_bytes=VMEM_BYTES)
    values, member, bounds = pl.pallas_call(
        functools.partial(route_kernel, vocab=vocab),
        out_shape=[
            jax.ShapeDtypeStruct((tokens + WINDOW, LANES), jnp.int32),
            jax.ShapeDtypeStruct((tokens, LANES), jnp.bfloat16),
            jax.ShapeDtypeStruct((block_rows, length), jnp.int32),
        ],
        in_specs=[vmem_spec()],
        out_specs=[vmem_spec()] * 3,
        scratch_shapes=[pltpu.VMEM((texts, length), jnp.float32)],
        compiler_params=params,
        name="route",
    )(ids)
    gathered = pl.pallas_call(
        gather_kernel,
        out_shape=jax.ShapeDtypeStruct((tokens + WINDOW, features), jnp.bfloat16),
        in_specs=[smem_spec(), vmem_spec(), any_spec()],
        out_specs=vmem_spec(),
        scratch_shapes=[
            pltpu.VMEM((blocks, features, IDS_PER_BLOCK), jnp.bfloat16),
            pltpu.SemaphoreType.DMA((blocks,)),
        ],
        compiler_params=params,
        name="gather",
    )(bounds, values, vocabulary_vectors)
    long = jax.ShapeDtypeStruct((rows, width), jnp.bfloat16)
    short = jax.ShapeDtypeStruct((tokens + ROWS, width), jnp.bfloat16)
    away1, away0, extra = pl.pallas_call(
        functools.partial(away_kernel, blocks=blocks),
        out_shape=[
            long,
            short,
            jax.ShapeDtypeStruct(((chunks + 3) * ROWS, width), jnp.bfloat16),
        ],
        in_specs=[smem_spec()] + [vmem_spec()] * 3 + [any_spec()] * 2,
        out_specs=[vmem_spec()] * 3,
        scratch_shapes=[
            pltpu.VMEM((2, features, width), jnp.bfloat16),
            pltpu.VMEM((rank, features), jnp.bfloat16),
            pltpu.VMEM((LANES, LANES), jnp.float32),
            pltpu.VMEM((8, width), jnp.float32),
            pltpu.VMEM((ROWS, features), jnp.float32),
            pltpu.SemaphoreType.DMA((2,)),
            pltpu.SemaphoreType.DMA,
        ],
        compiler_params=params,
        name="away",
    )(
        bounds,
        gathered,
        member,
        difficult_distractors,
        layer_weight_matrix,
        lowering_factor_matrix,
    )
    other_core = [(d, d ^ 1) for d in range(shards)]
    other_y = [(d, d ^ 2) for d in range(shards)]
    core1 = lax.ppermute(away1, "dp", other_core)
    core0 = lax.ppermute(away0, "dp", other_core)
    own1, own0 = pl.pallas_call(
        functools.partial(own_kernel, blocks=blocks, tokens=tokens),
        out_shape=[long, short],
        in_specs=[smem_spec(), vmem_spec(), any_spec(), vmem_spec()],
        out_specs=[vmem_spec()] * 2,
        scratch_shapes=[
            pltpu.VMEM((2, features, width), jnp.bfloat16),
            pltpu.SemaphoreType.DMA((2,)),
        ],
        compiler_params=params,
        cost_estimate=pl.CostEstimate(
            flops=4 * tokens * features * width, bytes_accessed=8 * 2**20, transcendentals=0
        ),
        name="own",
    )(bounds, gathered, layer_weight_matrix, extra)
    chip1 = (own1.astype(jnp.float32) + core1.astype(jnp.float32)).astype(jnp.bfloat16)
    far = lax.ppermute(chip1, "dp", other_y)
    pooled, slope, reduced, misc = pl.pallas_call(
        functools.partial(pool_kernel, model_width=float(features * shards)),
        out_shape=[
            jax.ShapeDtypeStruct((2 * shards, ROWS, width), jnp.bfloat16),
            jax.ShapeDtypeStruct((tokens, width), jnp.float32),
            jax.ShapeDtypeStruct((ROWS, tokens), jnp.bfloat16),
            jax.ShapeDtypeStruct((ROWS, width), jnp.float32),
        ],
        in_specs=[vmem_spec()] * 7,
        out_specs=[vmem_spec()] * 4,
        scratch_shapes=[pltpu.VMEM((LANES, width), jnp.bfloat16)],
        compiler_params=params,
        name="pool",
    )(ids, own0, core0, chip1, far, member, raising_factor_matrix)
    sides = ("group", "dp")
    pooled = lax.all_to_all(pooled, sides, 0, 0)
    dots = pl.pallas_call(
        functools.partial(dots_kernel, shards=shards),
        out_shape=jax.ShapeDtypeStruct((parts, 2 * ROWS, LANES), jnp.float32),
        in_specs=[vmem_spec()],
        out_specs=vmem_spec(),
        compiler_params=params,
        name="dots",
    )(pooled)
    dots = lax.all_to_all(dots, "mp", 0, 0)
    embeddings, losses, update = pl.pallas_call(
        functools.partial(score_kernel, shards=shards, negatives=negatives),
        out_shape=[
            jax.ShapeDtypeStruct((1, per_shard, part_width), jnp.bfloat16),
            jax.ShapeDtypeStruct((1, per_shard), jnp.float32),
            jax.ShapeDtypeStruct((2 * shards, ROWS, width), jnp.float32),
        ],
        in_specs=[vmem_spec()] * 7 + [smem_spec()],
        out_specs=[vmem_spec()] * 3,
        compiler_params=params,
        name="score",
    )(ids, pooled, dots, misc, slope, reduced, member, logit_sharpness)
    update = lax.all_to_all(update, sides, 0, 0)
    columns = [update[quarter_of(q)] + update[shards + quarter_of(q)] for q in range(shards)]
    return (embeddings, losses, jnp.concatenate(columns, axis=1))


def body(words, hard, vocabulary, weight, lowering, raising, sharpness):
    shards, parts = lax.axis_size("dp"), lax.axis_size("mp")
    texts, length = words.shape[1:]
    features, vocab = vocabulary.shape
    negatives = hard.shape[1]
    square = shards == 4 and features == weight.shape[1] and parts == shards
    small = texts <= ROWS - 2 and length == LANES and texts * length <= 2048
    even = (texts * length) % CHUNK == 0 and vocab % IDS_PER_BLOCK == 0
    fits = features * vocab <= 2**24 and features % (4 * LANES) == 0
    spare = texts * length // CHUNK + negatives <= ROWS and lowering.shape[0] == ROWS
    fast = square and small and even and fits and spare and lax.axis_size("group") == 2
    chosen = split_body if fast else general_body
    return chosen(words, hard, vocabulary, weight, lowering, raising, sharpness)


def solution(mesh):
    in_specs = (
        P("group", None, None),
        P("dp", None),
        P("dp", None),
        P("dp", "mp"),
        P(),
        P(None, "mp"),
        P(),
    )
    out_specs = (P("group", "dp", "mp"), P("group", "dp"), P(None, "mp"))
    return jax.shard_map(body, mesh=mesh, in_specs=in_specs, out_specs=out_specs, check_vma=False)
```

```python
import functools

import jax
import jax.numpy as jnp
from jax import lax
from jax.experimental import pallas as pl
from jax.experimental.pallas import tpu as pltpu
from jax.sharding import PartitionSpec as P


def general_body(
    query_passage_words,
    difficult_distractors,
    vocabulary_vectors,
    layer_weight_matrix,
    lowering_factor_matrix,
    raising_factor_matrix,
    logit_sharpness,
):
    group_index = lax.axis_index("group")
    shard_index = lax.axis_index("dp")
    part_index = lax.axis_index("mp")
    shard_count = lax.axis_size("dp")
    side_ids = query_passage_words[0]
    text_count = side_ids.shape[0]
    length = side_ids.shape[1]
    per_shard = text_count // shard_count
    own_ids = lax.dynamic_slice_in_dim(side_ids, shard_index * per_shard, per_shard, 0)
    columns = jnp.take(vocabulary_vectors, side_ids.reshape(-1), axis=1)
    inputs = lax.all_to_all(columns, "dp", split_axis=1, concat_axis=0, tiled=True)
    tokens = inputs.shape[1]
    feature_width = raising_factor_matrix.shape[1]
    wide_inputs = inputs.astype(jnp.float32)
    inverse = lax.rsqrt(jnp.mean(wide_inputs * wide_inputs, axis=0) + 1e-05)
    normed_state = (wide_inputs * inverse[None, :]).astype(jnp.bfloat16)
    linear_map = lax.dot_general(
        lax.all_gather(layer_weight_matrix, "dp", axis=0, tiled=True),
        normed_state,
        (((0,), (0,)), ((), ())),
        preferred_element_type=jnp.float32,
    )
    reduced_sum = jnp.dot(
        lowering_factor_matrix, normed_state, preferred_element_type=jnp.float32
    ).astype(jnp.bfloat16)
    linear_map = linear_map + lax.dot_general(
        raising_factor_matrix,
        reduced_sum,
        (((0,), (0,)), ((), ())),
        preferred_element_type=jnp.float32,
    )
    own_inputs = lax.dynamic_slice_in_dim(
        inputs, part_index * feature_width, feature_width, 0
    ).astype(jnp.float32)
    hidden_state = own_inputs + jax.nn.silu(linear_map)
    mask = (own_ids != 0).astype(jnp.float32)
    counts = jnp.sum(mask, axis=1)
    summed = jnp.einsum("dnl,nl->nd", hidden_state.reshape(feature_width, per_shard, length), mask)
    pooled = (summed / counts[:, None]).astype(jnp.bfloat16)
    gathered = lax.all_gather(pooled, ("group", "dp"), axis=0, tiled=True)
    part_scores = lax.dot_general(
        pooled, gathered, (((1,), (1,)), ((), ())), preferred_element_type=jnp.float32
    )
    gathered_wide = gathered.astype(jnp.float32)
    part_norms = jnp.sum(gathered_wide * gathered_wide, axis=1)
    dots, norms = lax.psum((part_scores, part_norms), "mp")
    rnorm_all = lax.rsqrt(norms + 1e-06)
    all_count = gathered.shape[0]
    half_count = all_count // 2
    own_rows = (
        group_index * half_count + shard_index * per_shard + jnp.arange(per_shard, dtype=jnp.int32)
    )
    rnorm_own = jnp.take(rnorm_all, own_rows)
    cosine = dots * rnorm_own[:, None] * rnorm_all[None, :]
    multiplier_factor = logit_sharpness[0]
    scores = multiplier_factor * cosine
    column_ids = jnp.arange(all_count, dtype=jnp.int32)
    keep = column_ids[None, :] != own_rows[:, None]
    pair = (own_rows + half_count) % all_count
    weight = (group_index == 0).astype(jnp.float32)
    neg_cols = half_count + difficult_distractors
    top = jnp.max(jnp.where(keep, scores, -jnp.inf), axis=1)
    safe_scores = jnp.where(keep, scores, top[:, None])
    expd = jnp.where(keep, jnp.exp(safe_scores - top[:, None]), 0.0)
    neg_exp = (
        jnp.exp(jnp.minimum(jnp.take_along_axis(scores, neg_cols, axis=1) - top[:, None], 0.0))
        * weight
    )
    total = jnp.sum(expd, axis=1) + jnp.sum(neg_exp, axis=1)
    pair_score = jnp.take_along_axis(scores, pair[:, None], axis=1)[:, 0]
    losses = top + jnp.log(total) - pair_score
    onehot = (column_ids[None, None, :] == neg_cols[:, :, None]).astype(jnp.float32)
    probs = (expd + jnp.einsum("rk,rkc->rc", neg_exp, onehot)) / total[:, None]
    target = (column_ids[None, :] == pair[:, None]).astype(jnp.float32)
    grad_scores = (probs - target) / all_count
    coeff = (grad_scores * rnorm_own[:, None] * rnorm_all[None, :]).astype(jnp.bfloat16)
    along = jnp.dot(coeff, gathered, preferred_element_type=jnp.float32)
    pooled_wide = pooled.astype(jnp.float32)
    radial = jnp.sum(grad_scores * cosine, axis=1) * rnorm_own * rnorm_own
    embedding_gradient = multiplier_factor * (along - radial[:, None] * pooled_wide)
    token_grad = jnp.einsum("nd,nl->dnl", embedding_gradient / counts[:, None], mask).reshape(
        feature_width, tokens
    )
    sigma = jax.nn.sigmoid(linear_map)
    local = (token_grad * sigma * (1.0 + linear_map * (1.0 - sigma))).astype(jnp.bfloat16)
    up_portion = lax.dot_general(
        reduced_sum, local, (((1,), (1,)), ((), ())), preferred_element_type=jnp.float32
    )
    adapter_up_gradient = lax.psum(up_portion, ("group", "dp"))
    embeddings = (pooled_wide * rnorm_own[:, None]).astype(jnp.bfloat16)[None]
    return (embeddings, losses[None], adapter_up_gradient)


BLOCK_BITS, WINDOW_BITS, CHUNK_BITS, ROW_BITS = 10, 6, 8, 4
IDS_PER_BLOCK = 1 << BLOCK_BITS
WINDOW = 1 << WINDOW_BITS
CHUNK = 1 << CHUNK_BITS
ROWS = 1 << ROW_BITS
LANES = 128
NT = (((1,), (1,)), ((), ()))
VMEM_BYTES = 60 * 1024 * 1024


def mm(a, b, dims=(((1,), (0,)), ((), ()))):
    return lax.dot_general(a, b, dims, preferred_element_type=jnp.float32)


def split(x):
    high = x.astype(jnp.bfloat16)
    return high, (x - high.astype(jnp.float32)).astype(jnp.bfloat16)


def iota(shape, dim):
    return lax.broadcasted_iota(jnp.int32, shape, dim)


def quarter_of(dp_index, cores=2):
    return (dp_index % cores) * 2 + dp_index // cores


def route_kernel(ids_ref, values_ref, member_ref, bounds_ref, ranks, vocab):
    texts, length = ids_ref.shape
    tokens = texts * length
    blocks = vocab // IDS_PER_BLOCK
    ids = ids_ref[...]
    valid = ids != 0
    block_of = jnp.where(valid, lax.shift_right_logical(ids, BLOCK_BITS), blocks)
    block_rows = bounds_ref.shape[0]
    block_id = iota((block_rows, length), 0)
    below = jnp.zeros((block_rows, length), jnp.float32)
    for text in range(texts):
        below += jnp.where(block_of[text : text + 1] < block_id, 1.0, 0.0)
    before = jnp.broadcast_to(jnp.sum(below, axis=1, keepdims=True), (block_rows, length))
    bounds_ref[...] = before.astype(jnp.int32)
    earlier = jnp.where(iota((length, length), 0) < iota((length, length), 1), 1.0, 0.0).astype(
        jnp.bfloat16
    )
    for text in range(texts):
        here = jnp.where(block_of[text : text + 1] == block_id, 1.0, 0.0)
        inside = mm(here.astype(jnp.bfloat16), earlier)
        ranks[pl.ds(text, 1), :] = jnp.sum(here * (inside + before), axis=0, keepdims=True)
        before += jnp.broadcast_to(jnp.sum(here, axis=1, keepdims=True), (block_rows, length))
    text_of = iota((texts, length), 0)
    carried = jnp.where(valid, lax.shift_left(ids, ROW_BITS) + text_of, 0).astype(jnp.float32)
    rank = ranks[...]

    def place(p, carry):
        position = (iota((LANES, length), 0) + p * LANES).astype(jnp.float32)
        total = jnp.zeros((LANES, length), jnp.float32)
        for text in range(texts):
            total += jnp.where(rank[text : text + 1] == position, carried[text : text + 1], 0.0)
        found = jnp.broadcast_to(jnp.sum(total, axis=1, keepdims=True), (LANES, LANES))
        found = found.astype(jnp.int32)
        token = lax.shift_right_logical(found, ROW_BITS)
        start = pl.multiple_of(p * LANES, LANES)
        values_ref[pl.ds(start, LANES), :] = jnp.where(token == 0, -vocab, token)
        real = (token != 0) & ((found & (ROWS - 1)) == iota((LANES, LANES), 1))
        member_ref[pl.ds(start, LANES), :] = jnp.where(real, 1.0, 0.0).astype(jnp.bfloat16)
        return carry

    lax.fori_loop(0, tokens // LANES, place, 0)
    values_ref[pl.ds(tokens, WINDOW), :] = jnp.full((WINDOW, LANES), -vocab, jnp.int32)


def gather_kernel(bounds, values_ref, vocab_ref, gathered, held, held_sems):
    features, vocab = vocab_ref.shape
    blocks = vocab // IDS_PER_BLOCK
    rows = gathered.shape[0]

    def vocab_copy(b):
        columns = pl.ds(pl.multiple_of(b * IDS_PER_BLOCK, LANES), IDS_PER_BLOCK)
        return pltpu.make_async_copy(vocab_ref.at[:, columns], held.at[b], held_sems.at[b])

    for b in range(blocks):
        vocab_copy(b).start(priority=b % 2)

    def clear(p, carry):
        at = pl.multiple_of(p * WINDOW, WINDOW)
        gathered[pl.ds(at, WINDOW), :] = jnp.zeros((WINDOW, features), jnp.bfloat16)
        return carry

    lax.fori_loop(0, rows // WINDOW, clear, 0)

    def take(b, carry):
        first, last = bounds[b, 0], bounds[b + 1, 0]
        aligned = lax.shift_left(lax.shift_right_logical(first, ROW_BITS), ROW_BITS)
        windows = lax.shift_right_logical(last - aligned + WINDOW - 1, WINDOW_BITS)
        windows = jnp.where(last > first, windows, 0)
        vocab_copy(b).wait()

        def window(w, carry):
            start = pl.multiple_of(aligned + w * WINDOW, ROWS)
            wanted = values_ref[pl.ds(start, WINDOW), :]
            wanted -= b * IDS_PER_BLOCK + iota((WINDOW, LANES), 1)
            picked = [
                jnp.where(wanted == j * LANES, 1.0, 0.0).astype(jnp.bfloat16)
                for j in range(IDS_PER_BLOCK // LANES)
            ]
            found = mm(jnp.concatenate(picked, axis=1), held[b], NT)
            gathered[pl.ds(start, WINDOW), :] += found.astype(jnp.bfloat16)
            return carry

        return lax.fori_loop(0, windows, window, carry)

    lax.fori_loop(0, blocks, take, 0)


def split_quarter(i, j, cores=2):
    shard = lax.axis_index("dp")
    core, side_y = lax.rem(shard, cores), lax.div(shard, cores)
    return (core ^ i) * 2 + (side_y ^ j)


def weight_copies(weight_ref, weight, sems, i):
    width = weight.shape[2]
    return [
        pltpu.make_async_copy(
            weight_ref.at[:, pl.ds(pl.multiple_of(split_quarter(i, j) * width, LANES), width)],
            weight.at[j],
            sems.at[j],
        )
        for j in range(2)
    ]


def away_kernel(
    bounds,
    gathered,
    member_ref,
    hard_ref,
    weight_ref,
    lower_ref,
    out1,
    out0,
    extra_ref,
    weight,
    lower,
    turned,
    squares,
    residual,
    weight_sems,
    lower_sem,
    blocks,
):
    features = gathered.shape[1]
    tokens, width = member_ref.shape[0], out0.shape[1]
    chunks = tokens // CHUNK
    per_shard, negatives = hard_ref.shape
    shard = lax.axis_index("dp")
    copies = weight_copies(weight_ref, weight, weight_sems, 1)
    lower_copy = pltpu.make_async_copy(
        lower_ref.at[:, pl.ds(pl.multiple_of(shard * features, LANES), features)], lower, lower_sem
    )
    for copy in copies + [lower_copy]:
        copy.start()
    residual[...] = jnp.zeros_like(residual)
    squares[...] = jnp.zeros_like(squares)
    turned[...] = jnp.zeros_like(turned)
    turned[0:per_shard, chunks : chunks + negatives] = hard_ref[...].astype(jnp.float32)
    for copy in copies + [lower_copy]:
        copy.wait()

    def project(k, carry):
        start = pl.multiple_of(k * CHUNK, CHUNK)
        x = gathered[pl.ds(start, CHUNK), :]
        out1[pl.ds(start, CHUNK), :] = mm(x, weight[1]).astype(jnp.bfloat16)
        out0[pl.ds(start, CHUNK), :] = mm(x, weight[0]).astype(jnp.bfloat16)
        reduced = mm(lower[...], x, NT).astype(jnp.bfloat16)
        extra_ref[pl.ds(pl.multiple_of(k * ROWS, ROWS), ROWS), :] = reduced
        out1[pl.ds(pl.multiple_of(tokens + k * ROWS, ROWS), ROWS), :] = reduced
        ones = jnp.ones((ROWS, features), jnp.bfloat16)
        squares[pl.ds(k, 1), :] = mm(ones, x * x, NT)[0:1]
        member = member_ref[pl.ds(start, CHUNK), :].astype(jnp.float32).T.astype(jnp.bfloat16)
        residual[...] += mm(member[0:ROWS], x)
        return carry

    def zero(k, carry):
        start = pl.multiple_of(k * CHUNK, CHUNK)
        out1[pl.ds(start, CHUNK), :] = jnp.zeros((CHUNK, width), jnp.bfloat16)
        out0[pl.ds(start, CHUNK), :] = jnp.zeros((CHUNK, width), jnp.bfloat16)
        none = jnp.zeros((ROWS, width), jnp.bfloat16)
        extra_ref[pl.ds(pl.multiple_of(k * ROWS, ROWS), ROWS), :] = none
        out1[pl.ds(pl.multiple_of(tokens + k * ROWS, ROWS), ROWS), :] = none
        return carry

    used = lax.shift_right_logical(bounds[blocks, 0] + CHUNK - 1, CHUNK_BITS)
    lax.fori_loop(0, used, project, 0)
    lax.fori_loop(used, chunks, zero, 0)
    hard = turned[...].T[0:ROWS]
    lane = iota((ROWS, width), 1)
    misc = jnp.concatenate([squares[...], jnp.zeros((ROWS - squares.shape[0], width), jnp.float32)])
    for i in range(per_shard):
        misc += jnp.where(lane == shard * per_shard + i, hard[:, i : i + 1], 0.0)
    extra_ref[pl.ds(chunks * ROWS, ROWS), :] = misc.astype(jnp.bfloat16)
    out1[pl.ds(tokens + chunks * ROWS, ROWS), :] = misc.astype(jnp.bfloat16)

    mine = lax.axis_index("mp") == shard

    def part(i, j):
        start = pl.multiple_of(split_quarter(i, j) * width, LANES)
        return jnp.where(mine, residual[:, pl.ds(start, width)], 0.0).astype(jnp.bfloat16)

    out1[pl.ds(tokens + (chunks + 1) * ROWS, ROWS), :] = part(1, 1)
    out0[pl.ds(tokens, ROWS), :] = part(1, 0)
    extra_ref[pl.ds((chunks + 1) * ROWS, ROWS), :] = part(0, 1)
    extra_ref[pl.ds((chunks + 2) * ROWS, ROWS), :] = part(0, 0)


def own_kernel(
    bounds, gathered, weight_ref, extra_ref, out1, out0, weight, weight_sems, blocks, tokens
):
    width = out0.shape[1]
    chunks = tokens // CHUNK
    copies = weight_copies(weight_ref, weight, weight_sems, 0)
    for copy in copies:
        copy.start()
    for copy in copies:
        copy.wait()

    def project(k, carry):
        start = pl.multiple_of(k * CHUNK, CHUNK)
        x = gathered[pl.ds(start, CHUNK), :]
        out1[pl.ds(start, CHUNK), :] = mm(x, weight[1]).astype(jnp.bfloat16)
        out0[pl.ds(start, CHUNK), :] = mm(x, weight[0]).astype(jnp.bfloat16)
        return carry

    def zero(k, carry):
        start = pl.multiple_of(k * CHUNK, CHUNK)
        out1[pl.ds(start, CHUNK), :] = jnp.zeros((CHUNK, width), jnp.bfloat16)
        out0[pl.ds(start, CHUNK), :] = jnp.zeros((CHUNK, width), jnp.bfloat16)
        return carry

    used = lax.shift_right_logical(bounds[blocks, 0] + CHUNK - 1, CHUNK_BITS)
    lax.fori_loop(0, used, project, 0)
    lax.fori_loop(used, chunks, zero, 0)
    size = (chunks + 2) * ROWS
    out1[pl.ds(tokens, size), :] = extra_ref[0:size, :]
    out0[pl.ds(tokens, ROWS), :] = extra_ref[size : size + ROWS, :]


def pool_kernel(
    ids_ref,
    own_ref,
    core_ref,
    chip_ref,
    far_ref,
    member_ref,
    raise_ref,
    pooled_ref,
    slope_ref,
    reduced_ref,
    misc_ref,
    raised,
    model_width,
):
    texts, length = ids_ref.shape
    tokens = texts * length
    chunks = tokens // CHUNK
    width = own_ref.shape[1]
    quarter = quarter_of(lax.axis_index("dp"))

    def summed(*pieces):
        return sum(ref[pl.ds(start, size), :].astype(jnp.float32) for ref, start, size in pieces)

    def statistics(row):
        return summed((chip_ref, tokens + row, ROWS), (far_ref, tokens + row, ROWS))

    misc = statistics(chunks * ROWS)
    misc_ref[...] = misc
    inverse = lax.rsqrt(misc / model_width + 1e-05)
    raised[...] = jnp.zeros_like(raised)
    raised[0:ROWS, :] = raise_ref[:, pl.ds(pl.multiple_of(quarter * width, LANES), width)]
    total = jnp.zeros((ROWS, width), jnp.float32)
    for k in range(chunks):
        scale = inverse[k : k + 1]
        reduced = (statistics(k * ROWS) * scale).astype(jnp.bfloat16)
        reduced_ref[:, k * CHUNK : (k + 1) * CHUNK] = reduced
        stacked = jnp.concatenate(
            [reduced.astype(jnp.float32), jnp.broadcast_to(scale, (LANES - ROWS, CHUNK))]
        )
        turned = stacked.T
        low = turned.astype(jnp.bfloat16)
        at = k * CHUNK
        linear = summed((own_ref, at, CHUNK), (core_ref, at, CHUNK), (far_ref, at, CHUNK))
        linear = linear * turned[:, ROWS : ROWS + 1] + mm(low, raised[...])
        sigma = 1.0 / (1.0 + jnp.exp(-linear))
        slope_ref[pl.ds(k * CHUNK, CHUNK), :] = sigma * (1.0 + linear * (1.0 - sigma))
        member = member_ref[pl.ds(k * CHUNK, CHUNK), :].astype(jnp.float32).T
        member = member[0:ROWS].astype(jnp.bfloat16)
        high, rest = split(linear * sigma)
        total += mm(member, high) + mm(member, rest)
    total += summed(
        (own_ref, tokens, ROWS),
        (core_ref, tokens, ROWS),
        (far_ref, tokens + (chunks + 1) * ROWS, ROWS),
    )
    counts = jnp.sum((ids_ref[...] != 0).astype(jnp.float32), axis=1, keepdims=True)
    pooled = total[0:texts] / counts
    pooled = jnp.concatenate([pooled, jnp.zeros((ROWS - texts, width), jnp.float32)])
    for to in range(pooled_ref.shape[0]):
        pooled_ref[to] = pooled.astype(jnp.bfloat16)


def both_sides(pooled_ref, shard, shards):
    return jnp.concatenate([pooled_ref[shard], pooled_ref[shards + shard]], axis=0)


def dots_kernel(pooled_ref, dots_ref, shards):
    dots = jnp.zeros((2 * ROWS, 2 * ROWS), jnp.float32)
    for shard in range(shards):
        block = both_sides(pooled_ref, shard, shards)
        dots += mm(block, block, NT)
    wide = jnp.concatenate([dots, jnp.zeros((2 * ROWS, LANES - 2 * ROWS), jnp.float32)], axis=1)
    for to in range(dots_ref.shape[0]):
        dots_ref[to] = wide


def score_kernel(
    ids_ref,
    pooled_ref,
    dots_ref,
    misc_ref,
    slope_ref,
    reduced_ref,
    member_ref,
    sharp_ref,
    embed_ref,
    loss_ref,
    up_ref,
    shards,
    negatives,
):
    texts, length = ids_ref.shape
    tokens = texts * length
    chunks = tokens // CHUNK
    rows = 2 * ROWS
    width = pooled_ref.shape[2]
    per_shard = loss_ref.shape[1]
    group, shard = lax.axis_index("group"), lax.axis_index("dp")
    dots = dots_ref[0]
    for part in range(1, dots_ref.shape[0]):
        dots += dots_ref[part]
    dots = dots[:, 0:rows]
    down, across = iota((rows, rows), 0), iota((rows, rows), 1)
    same = down == across
    real = (lax.rem(down, ROWS) < texts) & (lax.rem(across, ROWS) < texts)
    diagonal = jnp.where(same, dots, 0.0)
    rnorm_row = lax.rsqrt(jnp.sum(diagonal, axis=0, keepdims=True) + 1e-06)
    rnorm_col = lax.rsqrt(jnp.sum(diagonal, axis=1, keepdims=True) + 1e-06)
    sharpness = sharp_ref[0]
    cosine = dots * rnorm_col * rnorm_row
    scores = sharpness * cosine
    keep = real & ~same
    top = jnp.max(jnp.where(keep, scores, -jnp.inf), axis=0, keepdims=True)
    top = jnp.where(lax.rem(across[0:1], ROWS) < texts, top, 0.0)
    powers = jnp.exp(jnp.where(real, jnp.minimum(scores - top, 0.0), 0.0))
    hard = misc_ref[chunks : chunks + negatives, 0:rows].astype(jnp.int32) + ROWS
    times = jnp.zeros((rows, rows), jnp.float32)
    for k in range(negatives):
        times += jnp.where(hard[k : k + 1] == down, 1.0, 0.0)
    times = jnp.where(across < texts, times, 0.0)
    weights = (jnp.where(keep, 1.0, 0.0) + jnp.where(real, times, 0.0)) * powers
    total = jnp.sum(weights, axis=0, keepdims=True)
    total = jnp.where(lax.rem(across[0:1], ROWS) < texts, total, 1.0)
    pair = (down == lax.rem(across + ROWS, rows)) & real
    pair_score = jnp.sum(jnp.where(pair, scores, 0.0), axis=0, keepdims=True)
    losses = top + jnp.log(total) - pair_score
    grad_scores = (weights / total - jnp.where(pair, 1.0, 0.0)) / (2 * texts)
    coeff = (grad_scores * rnorm_col * rnorm_row).astype(jnp.bfloat16)
    radial = jnp.sum(grad_scores * cosine, axis=0, keepdims=True) * rnorm_row * rnorm_row

    first = shard * per_shard
    loss_col = jnp.sum(jnp.where(same, losses, 0.0), axis=1, keepdims=True)
    at = (iota((rows, LANES), 0) == group * ROWS + first + iota((rows, LANES), 1)) & (
        iota((rows, LANES), 1) < per_shard
    )
    loss_ref[...] = jnp.sum(jnp.where(at, loss_col, 0.0), axis=0, keepdims=True)[:, 0:per_shard]

    mine = both_sides(pooled_ref, shard, shards)
    along = mm(coeff.astype(jnp.float32).T.astype(jnp.bfloat16), mine)
    radial_col = jnp.sum(jnp.where(same, radial, 0.0), axis=1, keepdims=True)
    grad = sharpness * (along - radial_col * mine.astype(jnp.float32))
    grad = jnp.where(group == 0, grad[0:ROWS], grad[ROWS:rows])
    counts = jnp.sum((ids_ref[...] != 0).astype(jnp.float32), axis=1, keepdims=True)
    grad = grad[0:texts] / counts
    grad = jnp.concatenate([grad, jnp.zeros((LANES - texts, width), jnp.float32)])
    high, rest = split(grad)
    update = jnp.zeros((ROWS, width), jnp.float32)
    for k in range(chunks):
        member = member_ref[pl.ds(k * CHUNK, CHUNK), :]
        token_grad = mm(member, high) + mm(member, rest)
        local = (token_grad * slope_ref[pl.ds(k * CHUNK, CHUNK), :]).astype(jnp.bfloat16)
        update += mm(reduced_ref[:, k * CHUNK : (k + 1) * CHUNK], local)
    for to in range(up_ref.shape[0]):
        up_ref[to] = update

    rnorm_own = jnp.where(group == 0, rnorm_col[0:ROWS], rnorm_col[ROWS:rows])
    chosen = iota((ROWS, ROWS), 1) == iota((ROWS, ROWS), 0) + first
    chosen = jnp.where(chosen & (iota((ROWS, ROWS), 0) < per_shard), 1.0, 0.0).astype(jnp.bfloat16)
    for quarter in range(shards):
        block = pooled_ref[group * shards + quarter_of(quarter)].astype(jnp.float32) * rnorm_own
        picked = mm(chosen, block.astype(jnp.bfloat16)).astype(jnp.bfloat16)
        embed_ref[0, :, quarter * width : (quarter + 1) * width] = picked[0:per_shard]


def any_spec():
    return pl.BlockSpec(memory_space=pl.ANY)


def vmem_spec():
    return pl.BlockSpec(memory_space=pltpu.VMEM)


def smem_spec():
    return pl.BlockSpec(memory_space=pltpu.SMEM)


def split_body(
    query_passage_words,
    difficult_distractors,
    vocabulary_vectors,
    layer_weight_matrix,
    lowering_factor_matrix,
    raising_factor_matrix,
    logit_sharpness,
):
    shards, parts = lax.axis_size("dp"), lax.axis_size("mp")
    ids = query_passage_words[0]
    texts, length = ids.shape
    tokens = texts * length
    chunks = tokens // CHUNK
    features, vocab = vocabulary_vectors.shape
    blocks = vocab // IDS_PER_BLOCK
    block_rows = 8 * pl.cdiv(blocks + 1, 8)
    per_shard, negatives = difficult_distractors.shape
    rank = lowering_factor_matrix.shape[0]
    part_width = layer_weight_matrix.shape[1]
    width = part_width // shards
    rows = tokens + (chunks + 2) * ROWS
    params = pltpu.CompilerParams(vmem_limit_bytes=VMEM_BYTES)
    values, member, bounds = pl.pallas_call(
        functools.partial(route_kernel, vocab=vocab),
        out_shape=[
            jax.ShapeDtypeStruct((tokens + WINDOW, LANES), jnp.int32),
            jax.ShapeDtypeStruct((tokens, LANES), jnp.bfloat16),
            jax.ShapeDtypeStruct((block_rows, length), jnp.int32),
        ],
        in_specs=[vmem_spec()],
        out_specs=[vmem_spec()] * 3,
        scratch_shapes=[pltpu.VMEM((texts, length), jnp.float32)],
        compiler_params=params,
        name="route",
    )(ids)
    gathered = pl.pallas_call(
        gather_kernel,
        out_shape=jax.ShapeDtypeStruct((tokens + WINDOW, features), jnp.bfloat16),
        in_specs=[smem_spec(), vmem_spec(), any_spec()],
        out_specs=vmem_spec(),
        scratch_shapes=[
            pltpu.VMEM((blocks, features, IDS_PER_BLOCK), jnp.bfloat16),
            pltpu.SemaphoreType.DMA((blocks,)),
        ],
        compiler_params=params,
        name="gather",
    )(bounds, values, vocabulary_vectors)
    long = jax.ShapeDtypeStruct((rows, width), jnp.bfloat16)
    short = jax.ShapeDtypeStruct((tokens + ROWS, width), jnp.bfloat16)
    away1, away0, extra = pl.pallas_call(
        functools.partial(away_kernel, blocks=blocks),
        out_shape=[
            long,
            short,
            jax.ShapeDtypeStruct(((chunks + 3) * ROWS, width), jnp.bfloat16),
        ],
        in_specs=[smem_spec()] + [vmem_spec()] * 3 + [any_spec()] * 2,
        out_specs=[vmem_spec()] * 3,
        scratch_shapes=[
            pltpu.VMEM((2, features, width), jnp.bfloat16),
            pltpu.VMEM((rank, features), jnp.bfloat16),
            pltpu.VMEM((LANES, LANES), jnp.float32),
            pltpu.VMEM((8, width), jnp.float32),
            pltpu.VMEM((ROWS, features), jnp.float32),
            pltpu.SemaphoreType.DMA((2,)),
            pltpu.SemaphoreType.DMA,
        ],
        compiler_params=params,
        name="away",
    )(
        bounds,
        gathered,
        member,
        difficult_distractors,
        layer_weight_matrix,
        lowering_factor_matrix,
    )
    other_core = [(d, d ^ 1) for d in range(shards)]
    other_y = [(d, d ^ 2) for d in range(shards)]
    core1 = lax.ppermute(away1, "dp", other_core)
    core0 = lax.ppermute(away0, "dp", other_core)
    own1, own0 = pl.pallas_call(
        functools.partial(own_kernel, blocks=blocks, tokens=tokens),
        out_shape=[long, short],
        in_specs=[smem_spec(), vmem_spec(), any_spec(), vmem_spec()],
        out_specs=[vmem_spec()] * 2,
        scratch_shapes=[
            pltpu.VMEM((2, features, width), jnp.bfloat16),
            pltpu.SemaphoreType.DMA((2,)),
        ],
        compiler_params=params,
        cost_estimate=pl.CostEstimate(
            flops=4 * tokens * features * width, bytes_accessed=8 * 2**20, transcendentals=0
        ),
        name="own",
    )(bounds, gathered, layer_weight_matrix, extra)
    chip1 = (own1.astype(jnp.float32) + core1.astype(jnp.float32)).astype(jnp.bfloat16)
    far = lax.ppermute(chip1, "dp", other_y)
    pooled, slope, reduced, misc = pl.pallas_call(
        functools.partial(pool_kernel, model_width=float(features * shards)),
        out_shape=[
            jax.ShapeDtypeStruct((2 * shards, ROWS, width), jnp.bfloat16),
            jax.ShapeDtypeStruct((tokens, width), jnp.float32),
            jax.ShapeDtypeStruct((ROWS, tokens), jnp.bfloat16),
            jax.ShapeDtypeStruct((ROWS, width), jnp.float32),
        ],
        in_specs=[vmem_spec()] * 7,
        out_specs=[vmem_spec()] * 4,
        scratch_shapes=[pltpu.VMEM((LANES, width), jnp.bfloat16)],
        compiler_params=params,
        name="pool",
    )(ids, own0, core0, chip1, far, member, raising_factor_matrix)
    sides = ("group", "dp")
    pooled = lax.all_to_all(pooled, sides, 0, 0)
    dots = pl.pallas_call(
        functools.partial(dots_kernel, shards=shards),
        out_shape=jax.ShapeDtypeStruct((parts, 2 * ROWS, LANES), jnp.float32),
        in_specs=[vmem_spec()],
        out_specs=vmem_spec(),
        compiler_params=params,
        name="dots",
    )(pooled)
    dots = lax.all_to_all(dots, "mp", 0, 0)
    embeddings, losses, update = pl.pallas_call(
        functools.partial(score_kernel, shards=shards, negatives=negatives),
        out_shape=[
            jax.ShapeDtypeStruct((1, per_shard, part_width), jnp.bfloat16),
            jax.ShapeDtypeStruct((1, per_shard), jnp.float32),
            jax.ShapeDtypeStruct((2 * shards, ROWS, width), jnp.float32),
        ],
        in_specs=[vmem_spec()] * 7 + [smem_spec()],
        out_specs=[vmem_spec()] * 3,
        compiler_params=params,
        name="score",
    )(ids, pooled, dots, misc, slope, reduced, member, logit_sharpness)
    update = lax.all_to_all(update, sides, 0, 0)
    columns = [update[quarter_of(q)] + update[shards + quarter_of(q)] for q in range(shards)]
    return (embeddings, losses, jnp.concatenate(columns, axis=1))


def body(words, hard, vocabulary, weight, lowering, raising, sharpness):
    shards, parts = lax.axis_size("dp"), lax.axis_size("mp")
    texts, length = words.shape[1:]
    features, vocab = vocabulary.shape
    negatives = hard.shape[1]
    square = shards == 4 and features == weight.shape[1] and parts == shards
    small = texts <= ROWS - 2 and length == LANES and texts * length <= 2048
    even = (texts * length) % CHUNK == 0 and vocab % IDS_PER_BLOCK == 0
    fits = features * vocab <= 2**24 and features % (4 * LANES) == 0
    spare = texts * length // CHUNK + negatives <= ROWS and lowering.shape[0] == ROWS
    fast = square and small and even and fits and spare and lax.axis_size("group") == 2
    chosen = split_body if fast else general_body
    return chosen(words, hard, vocabulary, weight, lowering, raising, sharpness)


def solution(mesh):
    in_specs = (
        P("group", None, None),
        P("dp", None),
        P("dp", None),
        P("dp", "mp"),
        P(),
        P(None, "mp"),
        P(),
    )
    out_specs = (P("group", "dp", "mp"), P("group", "dp"), P(None, "mp"))
    return jax.shard_map(body, mesh=mesh, in_specs=in_specs, out_specs=out_specs, check_vma=False)
```

```python
import functools

import jax
import jax.numpy as jnp
from jax import lax
from jax.experimental import pallas as pl
from jax.experimental.pallas import tpu as pltpu
from jax.sharding import PartitionSpec as P


def general_body(
    query_passage_words,
    difficult_distractors,
    vocabulary_vectors,
    layer_weight_matrix,
    lowering_factor_matrix,
    raising_factor_matrix,
    logit_sharpness,
):
    group_index = lax.axis_index("group")
    shard_index = lax.axis_index("dp")
    part_index = lax.axis_index("mp")
    shard_count = lax.axis_size("dp")
    side_ids = query_passage_words[0]
    text_count = side_ids.shape[0]
    length = side_ids.shape[1]
    per_shard = text_count // shard_count
    own_ids = lax.dynamic_slice_in_dim(side_ids, shard_index * per_shard, per_shard, 0)
    columns = jnp.take(vocabulary_vectors, side_ids.reshape(-1), axis=1)
    inputs = lax.all_to_all(columns, "dp", split_axis=1, concat_axis=0, tiled=True)
    tokens = inputs.shape[1]
    feature_width = raising_factor_matrix.shape[1]
    wide_inputs = inputs.astype(jnp.float32)
    inverse = lax.rsqrt(jnp.mean(wide_inputs * wide_inputs, axis=0) + 1e-05)
    normed_state = (wide_inputs * inverse[None, :]).astype(jnp.bfloat16)
    linear_map = lax.dot_general(
        lax.all_gather(layer_weight_matrix, "dp", axis=0, tiled=True),
        normed_state,
        (((0,), (0,)), ((), ())),
        preferred_element_type=jnp.float32,
    )
    reduced_sum = jnp.dot(
        lowering_factor_matrix, normed_state, preferred_element_type=jnp.float32
    ).astype(jnp.bfloat16)
    linear_map = linear_map + lax.dot_general(
        raising_factor_matrix,
        reduced_sum,
        (((0,), (0,)), ((), ())),
        preferred_element_type=jnp.float32,
    )
    own_inputs = lax.dynamic_slice_in_dim(
        inputs, part_index * feature_width, feature_width, 0
    ).astype(jnp.float32)
    hidden_state = own_inputs + jax.nn.silu(linear_map)
    mask = (own_ids != 0).astype(jnp.float32)
    counts = jnp.sum(mask, axis=1)
    summed = jnp.einsum("dnl,nl->nd", hidden_state.reshape(feature_width, per_shard, length), mask)
    pooled = (summed / counts[:, None]).astype(jnp.bfloat16)
    gathered = lax.all_gather(pooled, ("group", "dp"), axis=0, tiled=True)
    part_scores = lax.dot_general(
        pooled, gathered, (((1,), (1,)), ((), ())), preferred_element_type=jnp.float32
    )
    gathered_wide = gathered.astype(jnp.float32)
    part_norms = jnp.sum(gathered_wide * gathered_wide, axis=1)
    dots, norms = lax.psum((part_scores, part_norms), "mp")
    rnorm_all = lax.rsqrt(norms + 1e-06)
    all_count = gathered.shape[0]
    half_count = all_count // 2
    own_rows = (
        group_index * half_count + shard_index * per_shard + jnp.arange(per_shard, dtype=jnp.int32)
    )
    rnorm_own = jnp.take(rnorm_all, own_rows)
    cosine = dots * rnorm_own[:, None] * rnorm_all[None, :]
    multiplier_factor = logit_sharpness[0]
    scores = multiplier_factor * cosine
    column_ids = jnp.arange(all_count, dtype=jnp.int32)
    keep = column_ids[None, :] != own_rows[:, None]
    pair = (own_rows + half_count) % all_count
    weight = (group_index == 0).astype(jnp.float32)
    neg_cols = half_count + difficult_distractors
    top = jnp.max(jnp.where(keep, scores, -jnp.inf), axis=1)
    safe_scores = jnp.where(keep, scores, top[:, None])
    expd = jnp.where(keep, jnp.exp(safe_scores - top[:, None]), 0.0)
    neg_exp = (
        jnp.exp(jnp.minimum(jnp.take_along_axis(scores, neg_cols, axis=1) - top[:, None], 0.0))
        * weight
    )
    total = jnp.sum(expd, axis=1) + jnp.sum(neg_exp, axis=1)
    pair_score = jnp.take_along_axis(scores, pair[:, None], axis=1)[:, 0]
    losses = top + jnp.log(total) - pair_score
    onehot = (column_ids[None, None, :] == neg_cols[:, :, None]).astype(jnp.float32)
    probs = (expd + jnp.einsum("rk,rkc->rc", neg_exp, onehot)) / total[:, None]
    target = (column_ids[None, :] == pair[:, None]).astype(jnp.float32)
    grad_scores = (probs - target) / all_count
    coeff = (grad_scores * rnorm_own[:, None] * rnorm_all[None, :]).astype(jnp.bfloat16)
    along = jnp.dot(coeff, gathered, preferred_element_type=jnp.float32)
    pooled_wide = pooled.astype(jnp.float32)
    radial = jnp.sum(grad_scores * cosine, axis=1) * rnorm_own * rnorm_own
    embedding_gradient = multiplier_factor * (along - radial[:, None] * pooled_wide)
    token_grad = jnp.einsum("nd,nl->dnl", embedding_gradient / counts[:, None], mask).reshape(
        feature_width, tokens
    )
    sigma = jax.nn.sigmoid(linear_map)
    local = (token_grad * sigma * (1.0 + linear_map * (1.0 - sigma))).astype(jnp.bfloat16)
    up_portion = lax.dot_general(
        reduced_sum, local, (((1,), (1,)), ((), ())), preferred_element_type=jnp.float32
    )
    adapter_up_gradient = lax.psum(up_portion, ("group", "dp"))
    embeddings = (pooled_wide * rnorm_own[:, None]).astype(jnp.bfloat16)[None]
    return (embeddings, losses[None], adapter_up_gradient)


BLOCK_BITS, CHUNK_BITS, LANE_BITS, ROW_BITS = 10, 8, 7, 4
IDS_PER_BLOCK = 1 << BLOCK_BITS
CHUNK = 1 << CHUNK_BITS
ROWS = 1 << ROW_BITS
LANES = 1 << LANE_BITS
FEATURE_ROWS = 256
NT = (((1,), (1,)), ((), ()))
VMEM_BYTES = 60 * 1024 * 1024


def mm(a, b, dims=(((1,), (0,)), ((), ()))):
    return lax.dot_general(a, b, dims, preferred_element_type=jnp.float32)


def split(x):
    high = x.astype(jnp.bfloat16)
    return high, (x - high.astype(jnp.float32)).astype(jnp.bfloat16)


def iota(shape, dim):
    return lax.broadcasted_iota(jnp.int32, shape, dim)


def quarter_of(dp_index, cores=2):
    return (dp_index % cores) * 2 + dp_index // cores


def route_kernel(ids_ref, token_ref, member_ref, bounds_ref, ranks, vocab):
    texts, length = ids_ref.shape
    tokens = texts * length
    blocks = vocab // IDS_PER_BLOCK
    ids = ids_ref[...]
    valid = ids != 0
    block_of = jnp.where(valid, lax.shift_right_logical(ids, BLOCK_BITS), blocks)
    block_rows = bounds_ref.shape[0]
    block_id = iota((block_rows, length), 0)
    below = jnp.zeros((block_rows, length), jnp.float32)
    for text in range(texts):
        below += jnp.where(block_of[text : text + 1] < block_id, 1.0, 0.0)
    before = jnp.broadcast_to(jnp.sum(below, axis=1, keepdims=True), (block_rows, length))
    bounds_ref[...] = before.astype(jnp.int32)
    earlier = jnp.where(iota((length, length), 0) < iota((length, length), 1), 1.0, 0.0).astype(
        jnp.bfloat16
    )
    for text in range(texts):
        here = jnp.where(block_of[text : text + 1] == block_id, 1.0, 0.0)
        inside = mm(here.astype(jnp.bfloat16), earlier)
        ranks[pl.ds(text, 1), :] = jnp.sum(here * (inside + before), axis=0, keepdims=True)
        before += jnp.broadcast_to(jnp.sum(here, axis=1, keepdims=True), (block_rows, length))
    text_of = iota((texts, length), 0)
    carried = jnp.where(valid, lax.shift_left(ids, ROW_BITS) + text_of, 0).astype(jnp.float32)
    rank = ranks[...]

    def place(p, carry):
        position = (iota((LANES, length), 0) + p * LANES).astype(jnp.float32)
        total = jnp.zeros((LANES, length), jnp.float32)
        for text in range(texts):
            total += jnp.where(rank[text : text + 1] == position, carried[text : text + 1], 0.0)
        found = jnp.broadcast_to(jnp.sum(total, axis=1, keepdims=True), (LANES, LANES))
        found = found.astype(jnp.int32)
        token = lax.shift_right_logical(found, ROW_BITS)
        start = pl.multiple_of(p * LANES, LANES)
        flat = jnp.where(token == 0, -vocab, token).astype(jnp.float32).T
        token_ref[pl.ds(p, 1), :] = flat[0:1].astype(jnp.int32)
        real = (token != 0) & ((found & (ROWS - 1)) == iota((LANES, LANES), 1))
        member_ref[pl.ds(start, LANES), :] = jnp.where(real, 1.0, 0.0).astype(jnp.bfloat16)
        return carry

    lax.fori_loop(0, tokens // LANES, place, 0)


def take_lanes(x, lanes):
    numbers = lax.GatherDimensionNumbers(
        offset_dims=(),
        collapsed_slice_dims=(1,),
        start_index_map=(1,),
        operand_batching_dims=(0,),
        start_indices_batching_dims=(0,),
    )
    mode = lax.GatherScatterMode.PROMISE_IN_BOUNDS
    return lax.gather(x, lanes[..., None], numbers, slice_sizes=(1, 1), mode=mode)


def gather_kernel(bounds, token_ref, vocab_ref, gathered, held, turned, held_sems):
    features, vocab = vocab_ref.shape
    blocks = vocab // IDS_PER_BLOCK
    windows = gathered.shape[0] // LANES

    def vocab_copy(b):
        columns = pl.ds(pl.multiple_of(b * IDS_PER_BLOCK, LANES), IDS_PER_BLOCK)
        return pltpu.make_async_copy(vocab_ref.at[:, columns], held.at[b], held_sems.at[b])

    for b in range(blocks):
        vocab_copy(b).start()

    def clear(p, carry):
        at = pl.multiple_of(p * LANES, LANES)
        turned[:, pl.ds(at, LANES)] = jnp.zeros((features, LANES), jnp.bfloat16)
        return carry

    lax.fori_loop(0, windows, clear, 0)

    def take(b, carry):
        first, last = bounds[b, 0], bounds[b + 1, 0]
        begin = lax.shift_right_logical(first, LANE_BITS)
        end = lax.shift_right_logical(last + LANES - 1, LANE_BITS)
        vocab_copy(b).wait()

        def window(p, carry):
            at = pl.ds(pl.multiple_of(p * LANES, LANES), LANES)
            token = token_ref[pl.ds(p, 1), :] - b * IDS_PER_BLOCK
            token = jnp.broadcast_to(token, (FEATURE_ROWS, LANES))
            lane = (token & (LANES - 1)).astype(jnp.int16)
            tile = lax.shift_right_arithmetic(token, LANE_BITS).astype(jnp.int16)
            for f in range(features // FEATURE_ROWS):
                rows = pl.ds(f * FEATURE_ROWS, FEATURE_ROWS)
                total = turned[rows, at]
                for j in range(IDS_PER_BLOCK // LANES):
                    found = take_lanes(held[b, rows, j * LANES : (j + 1) * LANES], lane)
                    total = jnp.where(tile == j, found, total)
                turned[rows, at] = total
            return carry

        return lax.fori_loop(begin, jnp.where(last > first, end, begin), window, carry)

    lax.fori_loop(0, blocks, take, 0)

    def turn(p, carry):
        at = pl.ds(pl.multiple_of(p * LANES, LANES), LANES)
        gathered[at, :] = turned[:, at].astype(jnp.float32).T.astype(jnp.bfloat16)
        return carry

    lax.fori_loop(0, windows, turn, 0)


def split_quarter(i, j, cores=2):
    shard = lax.axis_index("dp")
    core, side_y = lax.rem(shard, cores), lax.div(shard, cores)
    return (core ^ i) * 2 + (side_y ^ j)


def weight_copies(weight_ref, weight, sems, i):
    width = weight.shape[2]
    return [
        pltpu.make_async_copy(
            weight_ref.at[:, pl.ds(pl.multiple_of(split_quarter(i, j) * width, LANES), width)],
            weight.at[j],
            sems.at[j],
        )
        for j in range(2)
    ]


def away_kernel(
    bounds,
    gathered,
    member_ref,
    hard_ref,
    weight_ref,
    lower_ref,
    out1,
    out0,
    extra_ref,
    weight,
    lower,
    turned,
    squares,
    residual,
    weight_sems,
    lower_sem,
    blocks,
):
    features = gathered.shape[1]
    tokens, width = member_ref.shape[0], out0.shape[1]
    chunks = tokens // CHUNK
    per_shard, negatives = hard_ref.shape
    shard = lax.axis_index("dp")
    copies = weight_copies(weight_ref, weight, weight_sems, 1)
    lower_copy = pltpu.make_async_copy(
        lower_ref.at[:, pl.ds(pl.multiple_of(shard * features, LANES), features)], lower, lower_sem
    )
    for copy in copies + [lower_copy]:
        copy.start()
    residual[...] = jnp.zeros_like(residual)
    squares[...] = jnp.zeros_like(squares)
    turned[...] = jnp.zeros_like(turned)
    turned[0:per_shard, chunks : chunks + negatives] = hard_ref[...].astype(jnp.float32)
    for copy in copies + [lower_copy]:
        copy.wait()

    def project(k, carry):
        start = pl.multiple_of(k * CHUNK, CHUNK)
        x = gathered[pl.ds(start, CHUNK), :]
        out1[pl.ds(start, CHUNK), :] = mm(x, weight[1]).astype(jnp.bfloat16)
        out0[pl.ds(start, CHUNK), :] = mm(x, weight[0]).astype(jnp.bfloat16)
        reduced = mm(lower[...], x, NT).astype(jnp.bfloat16)
        extra_ref[pl.ds(pl.multiple_of(k * ROWS, ROWS), ROWS), :] = reduced
        out1[pl.ds(pl.multiple_of(tokens + k * ROWS, ROWS), ROWS), :] = reduced
        ones = jnp.ones((ROWS, features), jnp.bfloat16)
        squares[pl.ds(k, 1), :] = mm(ones, x * x, NT)[0:1]
        member = member_ref[pl.ds(start, CHUNK), :].astype(jnp.float32).T.astype(jnp.bfloat16)
        residual[...] += mm(member[0:ROWS], x)
        return carry

    def zero(k, carry):
        start = pl.multiple_of(k * CHUNK, CHUNK)
        out1[pl.ds(start, CHUNK), :] = jnp.zeros((CHUNK, width), jnp.bfloat16)
        out0[pl.ds(start, CHUNK), :] = jnp.zeros((CHUNK, width), jnp.bfloat16)
        none = jnp.zeros((ROWS, width), jnp.bfloat16)
        extra_ref[pl.ds(pl.multiple_of(k * ROWS, ROWS), ROWS), :] = none
        out1[pl.ds(pl.multiple_of(tokens + k * ROWS, ROWS), ROWS), :] = none
        return carry

    used = lax.shift_right_logical(bounds[blocks, 0] + CHUNK - 1, CHUNK_BITS)
    lax.fori_loop(0, used, project, 0)
    lax.fori_loop(used, chunks, zero, 0)
    hard = turned[...].T[0:ROWS]
    lane = iota((ROWS, width), 1)
    misc = jnp.concatenate([squares[...], jnp.zeros((ROWS - squares.shape[0], width), jnp.float32)])
    for i in range(per_shard):
        misc += jnp.where(lane == shard * per_shard + i, hard[:, i : i + 1], 0.0)
    extra_ref[pl.ds(chunks * ROWS, ROWS), :] = misc.astype(jnp.bfloat16)
    out1[pl.ds(tokens + chunks * ROWS, ROWS), :] = misc.astype(jnp.bfloat16)

    mine = lax.axis_index("mp") == shard

    def part(i, j):
        start = pl.multiple_of(split_quarter(i, j) * width, LANES)
        return jnp.where(mine, residual[:, pl.ds(start, width)], 0.0).astype(jnp.bfloat16)

    out1[pl.ds(tokens + (chunks + 1) * ROWS, ROWS), :] = part(1, 1)
    out0[pl.ds(tokens, ROWS), :] = part(1, 0)
    extra_ref[pl.ds((chunks + 1) * ROWS, ROWS), :] = part(0, 1)
    extra_ref[pl.ds((chunks + 2) * ROWS, ROWS), :] = part(0, 0)


def own_kernel(
    bounds, gathered, weight_ref, extra_ref, out1, out0, weight, weight_sems, blocks, tokens
):
    width = out0.shape[1]
    chunks = tokens // CHUNK
    copies = weight_copies(weight_ref, weight, weight_sems, 0)
    for copy in copies:
        copy.start()
    for copy in copies:
        copy.wait()

    def project(k, carry):
        start = pl.multiple_of(k * CHUNK, CHUNK)
        x = gathered[pl.ds(start, CHUNK), :]
        out1[pl.ds(start, CHUNK), :] = mm(x, weight[1]).astype(jnp.bfloat16)
        out0[pl.ds(start, CHUNK), :] = mm(x, weight[0]).astype(jnp.bfloat16)
        return carry

    def zero(k, carry):
        start = pl.multiple_of(k * CHUNK, CHUNK)
        out1[pl.ds(start, CHUNK), :] = jnp.zeros((CHUNK, width), jnp.bfloat16)
        out0[pl.ds(start, CHUNK), :] = jnp.zeros((CHUNK, width), jnp.bfloat16)
        return carry

    used = lax.shift_right_logical(bounds[blocks, 0] + CHUNK - 1, CHUNK_BITS)
    lax.fori_loop(0, used, project, 0)
    lax.fori_loop(used, chunks, zero, 0)
    size = (chunks + 2) * ROWS
    out1[pl.ds(tokens, size), :] = extra_ref[0:size, :]
    out0[pl.ds(tokens, ROWS), :] = extra_ref[size : size + ROWS, :]


def pool_kernel(
    ids_ref,
    own_ref,
    core_ref,
    chip_ref,
    far_ref,
    member_ref,
    raise_ref,
    pooled_ref,
    slope_ref,
    reduced_ref,
    misc_ref,
    raised,
    model_width,
):
    texts, length = ids_ref.shape
    tokens = texts * length
    chunks = tokens // CHUNK
    width = own_ref.shape[1]
    quarter = quarter_of(lax.axis_index("dp"))

    def summed(*pieces):
        return sum(ref[pl.ds(start, size), :].astype(jnp.float32) for ref, start, size in pieces)

    def statistics(row):
        return summed((chip_ref, tokens + row, ROWS), (far_ref, tokens + row, ROWS))

    misc = statistics(chunks * ROWS)
    misc_ref[...] = misc
    inverse = lax.rsqrt(misc / model_width + 1e-05)
    raised[...] = jnp.zeros_like(raised)
    raised[0:ROWS, :] = raise_ref[:, pl.ds(pl.multiple_of(quarter * width, LANES), width)]
    total = jnp.zeros((ROWS, width), jnp.float32)
    for k in range(chunks):
        scale = inverse[k : k + 1]
        reduced = (statistics(k * ROWS) * scale).astype(jnp.bfloat16)
        reduced_ref[:, k * CHUNK : (k + 1) * CHUNK] = reduced
        stacked = jnp.concatenate(
            [reduced.astype(jnp.float32), jnp.broadcast_to(scale, (LANES - ROWS, CHUNK))]
        )
        turned = stacked.T
        low = turned.astype(jnp.bfloat16)
        at = k * CHUNK
        linear = summed((own_ref, at, CHUNK), (core_ref, at, CHUNK), (far_ref, at, CHUNK))
        linear = linear * turned[:, ROWS : ROWS + 1] + mm(low, raised[...])
        sigma = 1.0 / (1.0 + jnp.exp(-linear))
        slope_ref[pl.ds(k * CHUNK, CHUNK), :] = sigma * (1.0 + linear * (1.0 - sigma))
        member = member_ref[pl.ds(k * CHUNK, CHUNK), :].astype(jnp.float32).T
        member = member[0:ROWS].astype(jnp.bfloat16)
        high, rest = split(linear * sigma)
        total += mm(member, high) + mm(member, rest)
    total += summed(
        (own_ref, tokens, ROWS),
        (core_ref, tokens, ROWS),
        (far_ref, tokens + (chunks + 1) * ROWS, ROWS),
    )
    counts = jnp.sum((ids_ref[...] != 0).astype(jnp.float32), axis=1, keepdims=True)
    pooled = total[0:texts] / counts
    pooled = jnp.concatenate([pooled, jnp.zeros((ROWS - texts, width), jnp.float32)])
    for to in range(pooled_ref.shape[0]):
        pooled_ref[to] = pooled.astype(jnp.bfloat16)


def both_sides(pooled_ref, shard, shards):
    return jnp.concatenate([pooled_ref[shard], pooled_ref[shards + shard]], axis=0)


def dots_kernel(pooled_ref, dots_ref, shards):
    dots = jnp.zeros((2 * ROWS, 2 * ROWS), jnp.float32)
    for shard in range(shards):
        block = both_sides(pooled_ref, shard, shards)
        dots += mm(block, block, NT)
    wide = jnp.concatenate([dots, jnp.zeros((2 * ROWS, LANES - 2 * ROWS), jnp.float32)], axis=1)
    for to in range(dots_ref.shape[0]):
        dots_ref[to] = wide


def score_kernel(
    ids_ref,
    pooled_ref,
    dots_ref,
    misc_ref,
    slope_ref,
    reduced_ref,
    member_ref,
    sharp_ref,
    embed_ref,
    loss_ref,
    up_ref,
    shards,
    negatives,
):
    texts, length = ids_ref.shape
    tokens = texts * length
    chunks = tokens // CHUNK
    rows = 2 * ROWS
    width = pooled_ref.shape[2]
    per_shard = loss_ref.shape[1]
    group, shard = lax.axis_index("group"), lax.axis_index("dp")
    dots = dots_ref[0]
    for part in range(1, dots_ref.shape[0]):
        dots += dots_ref[part]
    dots = dots[:, 0:rows]
    down, across = iota((rows, rows), 0), iota((rows, rows), 1)
    same = down == across
    real = (lax.rem(down, ROWS) < texts) & (lax.rem(across, ROWS) < texts)
    diagonal = jnp.where(same, dots, 0.0)
    rnorm_row = lax.rsqrt(jnp.sum(diagonal, axis=0, keepdims=True) + 1e-06)
    rnorm_col = lax.rsqrt(jnp.sum(diagonal, axis=1, keepdims=True) + 1e-06)
    sharpness = sharp_ref[0]
    cosine = dots * rnorm_col * rnorm_row
    scores = sharpness * cosine
    keep = real & ~same
    top = jnp.max(jnp.where(keep, scores, -jnp.inf), axis=0, keepdims=True)
    top = jnp.where(lax.rem(across[0:1], ROWS) < texts, top, 0.0)
    powers = jnp.exp(jnp.where(real, jnp.minimum(scores - top, 0.0), 0.0))
    hard = misc_ref[chunks : chunks + negatives, 0:rows].astype(jnp.int32) + ROWS
    times = jnp.zeros((rows, rows), jnp.float32)
    for k in range(negatives):
        times += jnp.where(hard[k : k + 1] == down, 1.0, 0.0)
    times = jnp.where(across < texts, times, 0.0)
    weights = (jnp.where(keep, 1.0, 0.0) + jnp.where(real, times, 0.0)) * powers
    total = jnp.sum(weights, axis=0, keepdims=True)
    total = jnp.where(lax.rem(across[0:1], ROWS) < texts, total, 1.0)
    pair = (down == lax.rem(across + ROWS, rows)) & real
    pair_score = jnp.sum(jnp.where(pair, scores, 0.0), axis=0, keepdims=True)
    losses = top + jnp.log(total) - pair_score
    grad_scores = (weights / total - jnp.where(pair, 1.0, 0.0)) / (2 * texts)
    coeff = (grad_scores * rnorm_col * rnorm_row).astype(jnp.bfloat16)
    radial = jnp.sum(grad_scores * cosine, axis=0, keepdims=True) * rnorm_row * rnorm_row

    first = shard * per_shard
    loss_col = jnp.sum(jnp.where(same, losses, 0.0), axis=1, keepdims=True)
    at = (iota((rows, LANES), 0) == group * ROWS + first + iota((rows, LANES), 1)) & (
        iota((rows, LANES), 1) < per_shard
    )
    loss_ref[...] = jnp.sum(jnp.where(at, loss_col, 0.0), axis=0, keepdims=True)[:, 0:per_shard]

    mine = both_sides(pooled_ref, shard, shards)
    along = mm(coeff.astype(jnp.float32).T.astype(jnp.bfloat16), mine)
    radial_col = jnp.sum(jnp.where(same, radial, 0.0), axis=1, keepdims=True)
    grad = sharpness * (along - radial_col * mine.astype(jnp.float32))
    grad = jnp.where(group == 0, grad[0:ROWS], grad[ROWS:rows])
    counts = jnp.sum((ids_ref[...] != 0).astype(jnp.float32), axis=1, keepdims=True)
    grad = grad[0:texts] / counts
    grad = jnp.concatenate([grad, jnp.zeros((LANES - texts, width), jnp.float32)])
    high, rest = split(grad)
    update = jnp.zeros((ROWS, width), jnp.float32)
    for k in range(chunks):
        member = member_ref[pl.ds(k * CHUNK, CHUNK), :]
        token_grad = mm(member, high) + mm(member, rest)
        local = (token_grad * slope_ref[pl.ds(k * CHUNK, CHUNK), :]).astype(jnp.bfloat16)
        update += mm(reduced_ref[:, k * CHUNK : (k + 1) * CHUNK], local)
    for to in range(up_ref.shape[0]):
        up_ref[to] = update

    rnorm_own = jnp.where(group == 0, rnorm_col[0:ROWS], rnorm_col[ROWS:rows])
    chosen = iota((ROWS, ROWS), 1) == iota((ROWS, ROWS), 0) + first
    chosen = jnp.where(chosen & (iota((ROWS, ROWS), 0) < per_shard), 1.0, 0.0).astype(jnp.bfloat16)
    for quarter in range(shards):
        block = pooled_ref[group * shards + quarter_of(quarter)].astype(jnp.float32) * rnorm_own
        picked = mm(chosen, block.astype(jnp.bfloat16)).astype(jnp.bfloat16)
        embed_ref[0, :, quarter * width : (quarter + 1) * width] = picked[0:per_shard]


def any_spec():
    return pl.BlockSpec(memory_space=pl.ANY)


def vmem_spec():
    return pl.BlockSpec(memory_space=pltpu.VMEM)


def smem_spec():
    return pl.BlockSpec(memory_space=pltpu.SMEM)


def split_body(
    query_passage_words,
    difficult_distractors,
    vocabulary_vectors,
    layer_weight_matrix,
    lowering_factor_matrix,
    raising_factor_matrix,
    logit_sharpness,
):
    shards, parts = lax.axis_size("dp"), lax.axis_size("mp")
    ids = query_passage_words[0]
    texts, length = ids.shape
    tokens = texts * length
    chunks = tokens // CHUNK
    features, vocab = vocabulary_vectors.shape
    blocks = vocab // IDS_PER_BLOCK
    block_rows = 8 * pl.cdiv(blocks + 1, 8)
    per_shard, negatives = difficult_distractors.shape
    rank = lowering_factor_matrix.shape[0]
    part_width = layer_weight_matrix.shape[1]
    width = part_width // shards
    rows = tokens + (chunks + 2) * ROWS
    params = pltpu.CompilerParams(vmem_limit_bytes=VMEM_BYTES)
    token, member, bounds = pl.pallas_call(
        functools.partial(route_kernel, vocab=vocab),
        out_shape=[
            jax.ShapeDtypeStruct((tokens // LANES, LANES), jnp.int32),
            jax.ShapeDtypeStruct((tokens, LANES), jnp.bfloat16),
            jax.ShapeDtypeStruct((block_rows, length), jnp.int32),
        ],
        in_specs=[vmem_spec()],
        out_specs=[vmem_spec()] * 3,
        scratch_shapes=[pltpu.VMEM((texts, length), jnp.float32)],
        compiler_params=params,
        name="route",
    )(ids)
    gathered = pl.pallas_call(
        gather_kernel,
        out_shape=jax.ShapeDtypeStruct((tokens, features), jnp.bfloat16),
        in_specs=[smem_spec(), vmem_spec(), any_spec()],
        out_specs=vmem_spec(),
        scratch_shapes=[
            pltpu.VMEM((blocks, features, IDS_PER_BLOCK), jnp.bfloat16),
            pltpu.VMEM((features, tokens), jnp.bfloat16),
            pltpu.SemaphoreType.DMA((blocks,)),
        ],
        compiler_params=params,
        name="gather",
    )(bounds, token, vocabulary_vectors)
    long = jax.ShapeDtypeStruct((rows, width), jnp.bfloat16)
    short = jax.ShapeDtypeStruct((tokens + ROWS, width), jnp.bfloat16)
    away1, away0, extra = pl.pallas_call(
        functools.partial(away_kernel, blocks=blocks),
        out_shape=[
            long,
            short,
            jax.ShapeDtypeStruct(((chunks + 3) * ROWS, width), jnp.bfloat16),
        ],
        in_specs=[smem_spec()] + [vmem_spec()] * 3 + [any_spec()] * 2,
        out_specs=[vmem_spec()] * 3,
        scratch_shapes=[
            pltpu.VMEM((2, features, width), jnp.bfloat16),
            pltpu.VMEM((rank, features), jnp.bfloat16),
            pltpu.VMEM((LANES, LANES), jnp.float32),
            pltpu.VMEM((8, width), jnp.float32),
            pltpu.VMEM((ROWS, features), jnp.float32),
            pltpu.SemaphoreType.DMA((2,)),
            pltpu.SemaphoreType.DMA,
        ],
        compiler_params=params,
        name="away",
    )(
        bounds,
        gathered,
        member,
        difficult_distractors,
        layer_weight_matrix,
        lowering_factor_matrix,
    )
    other_core = [(d, d ^ 1) for d in range(shards)]
    other_y = [(d, d ^ 2) for d in range(shards)]
    core1 = lax.ppermute(away1, "dp", other_core)
    core0 = lax.ppermute(away0, "dp", other_core)
    own1, own0 = pl.pallas_call(
        functools.partial(own_kernel, blocks=blocks, tokens=tokens),
        out_shape=[long, short],
        in_specs=[smem_spec(), vmem_spec(), any_spec(), vmem_spec()],
        out_specs=[vmem_spec()] * 2,
        scratch_shapes=[
            pltpu.VMEM((2, features, width), jnp.bfloat16),
            pltpu.SemaphoreType.DMA((2,)),
        ],
        compiler_params=params,
        cost_estimate=pl.CostEstimate(
            flops=4 * tokens * features * width, bytes_accessed=8 * 2**20, transcendentals=0
        ),
        name="own",
    )(bounds, gathered, layer_weight_matrix, extra)
    chip1 = (own1.astype(jnp.float32) + core1.astype(jnp.float32)).astype(jnp.bfloat16)
    far = lax.ppermute(chip1, "dp", other_y)
    pooled, slope, reduced, misc = pl.pallas_call(
        functools.partial(pool_kernel, model_width=float(features * shards)),
        out_shape=[
            jax.ShapeDtypeStruct((2 * shards, ROWS, width), jnp.bfloat16),
            jax.ShapeDtypeStruct((tokens, width), jnp.float32),
            jax.ShapeDtypeStruct((ROWS, tokens), jnp.bfloat16),
            jax.ShapeDtypeStruct((ROWS, width), jnp.float32),
        ],
        in_specs=[vmem_spec()] * 7,
        out_specs=[vmem_spec()] * 4,
        scratch_shapes=[pltpu.VMEM((LANES, width), jnp.bfloat16)],
        compiler_params=params,
        name="pool",
    )(ids, own0, core0, chip1, far, member, raising_factor_matrix)
    sides = ("group", "dp")
    pooled = lax.all_to_all(pooled, sides, 0, 0)
    dots = pl.pallas_call(
        functools.partial(dots_kernel, shards=shards),
        out_shape=jax.ShapeDtypeStruct((parts, 2 * ROWS, LANES), jnp.float32),
        in_specs=[vmem_spec()],
        out_specs=vmem_spec(),
        compiler_params=params,
        name="dots",
    )(pooled)
    dots = lax.all_to_all(dots, "mp", 0, 0)
    embeddings, losses, update = pl.pallas_call(
        functools.partial(score_kernel, shards=shards, negatives=negatives),
        out_shape=[
            jax.ShapeDtypeStruct((1, per_shard, part_width), jnp.bfloat16),
            jax.ShapeDtypeStruct((1, per_shard), jnp.float32),
            jax.ShapeDtypeStruct((2 * shards, ROWS, width), jnp.float32),
        ],
        in_specs=[vmem_spec()] * 7 + [smem_spec()],
        out_specs=[vmem_spec()] * 3,
        compiler_params=params,
        name="score",
    )(ids, pooled, dots, misc, slope, reduced, member, logit_sharpness)
    update = lax.all_to_all(update, sides, 0, 0)
    columns = [update[quarter_of(q)] + update[shards + quarter_of(q)] for q in range(shards)]
    return (embeddings, losses, jnp.concatenate(columns, axis=1))


def body(words, hard, vocabulary, weight, lowering, raising, sharpness):
    shards, parts = lax.axis_size("dp"), lax.axis_size("mp")
    texts, length = words.shape[1:]
    features, vocab = vocabulary.shape
    negatives = hard.shape[1]
    square = shards == 4 and features == weight.shape[1] and parts == shards
    small = texts <= ROWS - 2 and length == LANES and texts * length <= 2048
    even = (texts * length) % CHUNK == 0 and vocab % IDS_PER_BLOCK == 0
    fits = features * vocab <= 2**24 and features % (4 * LANES) == 0
    spare = texts * length // CHUNK + negatives <= ROWS and lowering.shape[0] == ROWS
    fast = square and small and even and fits and spare and lax.axis_size("group") == 2
    chosen = split_body if fast else general_body
    return chosen(words, hard, vocabulary, weight, lowering, raising, sharpness)


def solution(mesh):
    in_specs = (
        P("group", None, None),
        P("dp", None),
        P("dp", None),
        P("dp", "mp"),
        P(),
        P(None, "mp"),
        P(),
    )
    out_specs = (P("group", "dp", "mp"), P("group", "dp"), P(None, "mp"))
    return jax.shard_map(body, mesh=mesh, in_specs=in_specs, out_specs=out_specs, check_vma=False)
```

```python
import functools

import jax
import jax.numpy as jnp
from jax import lax
from jax.experimental import pallas as pl
from jax.experimental.pallas import tpu as pltpu
from jax.sharding import PartitionSpec as P


def general_body(
    query_passage_words,
    difficult_distractors,
    vocabulary_vectors,
    layer_weight_matrix,
    lowering_factor_matrix,
    raising_factor_matrix,
    logit_sharpness,
):
    group_index = lax.axis_index("group")
    shard_index = lax.axis_index("dp")
    part_index = lax.axis_index("mp")
    shard_count = lax.axis_size("dp")
    side_ids = query_passage_words[0]
    text_count = side_ids.shape[0]
    length = side_ids.shape[1]
    per_shard = text_count // shard_count
    own_ids = lax.dynamic_slice_in_dim(side_ids, shard_index * per_shard, per_shard, 0)
    columns = jnp.take(vocabulary_vectors, side_ids.reshape(-1), axis=1)
    inputs = lax.all_to_all(columns, "dp", split_axis=1, concat_axis=0, tiled=True)
    tokens = inputs.shape[1]
    feature_width = raising_factor_matrix.shape[1]
    wide_inputs = inputs.astype(jnp.float32)
    inverse = lax.rsqrt(jnp.mean(wide_inputs * wide_inputs, axis=0) + 1e-05)
    normed_state = (wide_inputs * inverse[None, :]).astype(jnp.bfloat16)
    linear_map = lax.dot_general(
        lax.all_gather(layer_weight_matrix, "dp", axis=0, tiled=True),
        normed_state,
        (((0,), (0,)), ((), ())),
        preferred_element_type=jnp.float32,
    )
    reduced_sum = jnp.dot(
        lowering_factor_matrix, normed_state, preferred_element_type=jnp.float32
    ).astype(jnp.bfloat16)
    linear_map = linear_map + lax.dot_general(
        raising_factor_matrix,
        reduced_sum,
        (((0,), (0,)), ((), ())),
        preferred_element_type=jnp.float32,
    )
    own_inputs = lax.dynamic_slice_in_dim(
        inputs, part_index * feature_width, feature_width, 0
    ).astype(jnp.float32)
    hidden_state = own_inputs + jax.nn.silu(linear_map)
    mask = (own_ids != 0).astype(jnp.float32)
    counts = jnp.sum(mask, axis=1)
    summed = jnp.einsum("dnl,nl->nd", hidden_state.reshape(feature_width, per_shard, length), mask)
    pooled = (summed / counts[:, None]).astype(jnp.bfloat16)
    gathered = lax.all_gather(pooled, ("group", "dp"), axis=0, tiled=True)
    part_scores = lax.dot_general(
        pooled, gathered, (((1,), (1,)), ((), ())), preferred_element_type=jnp.float32
    )
    gathered_wide = gathered.astype(jnp.float32)
    part_norms = jnp.sum(gathered_wide * gathered_wide, axis=1)
    dots, norms = lax.psum((part_scores, part_norms), "mp")
    rnorm_all = lax.rsqrt(norms + 1e-06)
    all_count = gathered.shape[0]
    half_count = all_count // 2
    own_rows = (
        group_index * half_count + shard_index * per_shard + jnp.arange(per_shard, dtype=jnp.int32)
    )
    rnorm_own = jnp.take(rnorm_all, own_rows)
    cosine = dots * rnorm_own[:, None] * rnorm_all[None, :]
    multiplier_factor = logit_sharpness[0]
    scores = multiplier_factor * cosine
    column_ids = jnp.arange(all_count, dtype=jnp.int32)
    keep = column_ids[None, :] != own_rows[:, None]
    pair = (own_rows + half_count) % all_count
    weight = (group_index == 0).astype(jnp.float32)
    neg_cols = half_count + difficult_distractors
    top = jnp.max(jnp.where(keep, scores, -jnp.inf), axis=1)
    safe_scores = jnp.where(keep, scores, top[:, None])
    expd = jnp.where(keep, jnp.exp(safe_scores - top[:, None]), 0.0)
    neg_exp = (
        jnp.exp(jnp.minimum(jnp.take_along_axis(scores, neg_cols, axis=1) - top[:, None], 0.0))
        * weight
    )
    total = jnp.sum(expd, axis=1) + jnp.sum(neg_exp, axis=1)
    pair_score = jnp.take_along_axis(scores, pair[:, None], axis=1)[:, 0]
    losses = top + jnp.log(total) - pair_score
    onehot = (column_ids[None, None, :] == neg_cols[:, :, None]).astype(jnp.float32)
    probs = (expd + jnp.einsum("rk,rkc->rc", neg_exp, onehot)) / total[:, None]
    target = (column_ids[None, :] == pair[:, None]).astype(jnp.float32)
    grad_scores = (probs - target) / all_count
    coeff = (grad_scores * rnorm_own[:, None] * rnorm_all[None, :]).astype(jnp.bfloat16)
    along = jnp.dot(coeff, gathered, preferred_element_type=jnp.float32)
    pooled_wide = pooled.astype(jnp.float32)
    radial = jnp.sum(grad_scores * cosine, axis=1) * rnorm_own * rnorm_own
    embedding_gradient = multiplier_factor * (along - radial[:, None] * pooled_wide)
    token_grad = jnp.einsum("nd,nl->dnl", embedding_gradient / counts[:, None], mask).reshape(
        feature_width, tokens
    )
    sigma = jax.nn.sigmoid(linear_map)
    local = (token_grad * sigma * (1.0 + linear_map * (1.0 - sigma))).astype(jnp.bfloat16)
    up_portion = lax.dot_general(
        reduced_sum, local, (((1,), (1,)), ((), ())), preferred_element_type=jnp.float32
    )
    adapter_up_gradient = lax.psum(up_portion, ("group", "dp"))
    embeddings = (pooled_wide * rnorm_own[:, None]).astype(jnp.bfloat16)[None]
    return (embeddings, losses[None], adapter_up_gradient)


BLOCK_BITS, GROUP_BITS, CHUNK_BITS, LANE_BITS, ROW_BITS = 10, 9, 8, 7, 4
IDS_PER_BLOCK = 1 << BLOCK_BITS
IDS_PER_GROUP = 1 << GROUP_BITS
CHUNK = 1 << CHUNK_BITS
ROWS = 1 << ROW_BITS
LANES = 1 << LANE_BITS
FEATURE_ROWS = 256
TAKEN = 512
FIRST = 1024
NT = (((1,), (1,)), ((), ()))
VMEM_BYTES = 60 * 1024 * 1024


def mm(a, b, dims=(((1,), (0,)), ((), ()))):
    return lax.dot_general(a, b, dims, preferred_element_type=jnp.float32)


def split(x):
    high = x.astype(jnp.bfloat16)
    return high, (x - high.astype(jnp.float32)).astype(jnp.bfloat16)


def iota(shape, dim):
    return lax.broadcasted_iota(jnp.int32, shape, dim)


def quarter_of(dp_index, cores=2):
    return (dp_index % cores) * 2 + dp_index // cores


def split_quarter(i, j, cores=2):
    shard = lax.axis_index("dp")
    core, side_y = lax.rem(shard, cores), lax.div(shard, cores)
    return (core ^ i) * 2 + (side_y ^ j)


def take_lanes(x, lanes):
    numbers = lax.GatherDimensionNumbers(
        offset_dims=(),
        collapsed_slice_dims=(1,),
        start_index_map=(1,),
        operand_batching_dims=(0,),
        start_indices_batching_dims=(0,),
    )
    mode = lax.GatherScatterMode.PROMISE_IN_BOUNDS
    return lax.gather(x, lanes[..., None], numbers, slice_sizes=(1, 1), mode=mode)


def project_kernel(
    ids_ref,
    hard_ref,
    vocab_ref,
    weight_ref,
    lower_ref,
    out00,
    out01,
    out10,
    out11,
    member_ref,
    held,
    weight,
    lower,
    turned,
    parts,
    token_ref,
    small,
    ranks,
    squares,
    residual,
    counted,
    bounds,
    held_sems,
    weight_sems,
    lower_sem,
    bounds_sem,
    out_sems,
    base,
):
    texts, length = ids_ref.shape
    features, vocab = vocab_ref.shape
    blocks = vocab // IDS_PER_BLOCK
    groups = vocab // IDS_PER_GROUP
    span = member_ref.shape[0]
    chunks = span // CHUNK
    per_shard, negatives = hard_ref.shape
    width = weight.shape[2]
    outs = (out00, out01, out10, out11)
    shard = lax.axis_index("dp")

    def vocab_copy(b):
        columns = pl.ds(pl.multiple_of(b * IDS_PER_BLOCK, LANES), IDS_PER_BLOCK)
        return pltpu.make_async_copy(vocab_ref.at[:, columns], held.at[b], held_sems.at[b])

    def weight_copy(q):
        start = pl.multiple_of(split_quarter(q // 2, q % 2) * width, LANES)
        return pltpu.make_async_copy(
            weight_ref.at[:, pl.ds(start, width)], weight.at[q], weight_sems.at[q]
        )

    lower_copy = pltpu.make_async_copy(
        lower_ref.at[:, pl.ds(pl.multiple_of(shard * features, LANES), features)], lower, lower_sem
    )
    vocab_copy(0).start()
    lower_copy.start()
    for q in range(4):
        weight_copy(q).start()
    for b in range(1, blocks):
        vocab_copy(b).start()

    ids = ids_ref[...]
    valid = ids != 0
    group_of = jnp.where(valid, lax.shift_right_logical(ids, GROUP_BITS), groups)
    group_rows = counted.shape[0]
    group_id = iota((group_rows, length), 0)
    below = jnp.zeros((group_rows, length), jnp.float32)
    for text in range(texts):
        below += jnp.where(group_of[text : text + 1] < group_id, 1.0, 0.0)
    before = jnp.broadcast_to(jnp.sum(below, axis=1, keepdims=True), (group_rows, length))
    counted[...] = before.astype(jnp.int32)
    bounds_copy = pltpu.make_async_copy(counted, bounds, bounds_sem)
    bounds_copy.start()
    earlier = jnp.where(iota((length, length), 0) < iota((length, length), 1), 1.0, 0.0).astype(
        jnp.bfloat16
    )
    for text in range(texts):
        here = jnp.where(group_of[text : text + 1] == group_id, 1.0, 0.0)
        inside = mm(here.astype(jnp.bfloat16), earlier)
        ranks[pl.ds(text, 1), :] = jnp.sum(here * (inside + before), axis=0, keepdims=True)
        before += jnp.broadcast_to(jnp.sum(here, axis=1, keepdims=True), (group_rows, length))
    text_of = iota((texts, length), 0)
    carried = jnp.where(valid, lax.shift_left(ids, ROW_BITS) + text_of, 0).astype(jnp.float32)
    rank = ranks[...]

    def place(p, carry):
        position = (iota((LANES, length), 0) + (p * LANES + base)).astype(jnp.float32)
        total = jnp.zeros((LANES, length), jnp.float32)
        for text in range(texts):
            total += jnp.where(rank[text : text + 1] == position, carried[text : text + 1], 0.0)
        found = jnp.broadcast_to(jnp.sum(total, axis=1, keepdims=True), (LANES, LANES))
        start = pl.multiple_of(p * LANES, LANES)
        row = found.T[0:1].astype(jnp.int32)
        token = lax.shift_right_logical(row, ROW_BITS)
        token_ref[pl.ds(p, 1), :] = jnp.where(token == 0, -vocab, token)
        found = found.astype(jnp.int32)
        real = (found >= ROWS) & ((found & (ROWS - 1)) == iota((LANES, LANES), 1))
        member_ref[pl.ds(start, LANES), :] = jnp.where(real, 1.0, 0.0).astype(jnp.bfloat16)
        turned[:, pl.ds(start, LANES)] = jnp.zeros((features, LANES), jnp.bfloat16)
        return carry

    lax.fori_loop(0, span // LANES, place, 0)
    residual[...] = jnp.zeros_like(residual)
    squares[...] = jnp.zeros_like(squares)
    small[...] = jnp.zeros_like(small)
    small[0:per_shard, chunks : chunks + negatives] = hard_ref[...].astype(jnp.float32)
    lower_copy.wait()
    for q in range(4):
        weight_copy(q).wait()
    bounds_copy.wait()

    def send(start, size):
        rows = pl.ds(start, size)
        for q in range(4):
            pltpu.make_async_copy(parts.at[q, rows], outs[q].at[rows], out_sems.at[q]).start()

    def project(k, carry):
        start = pl.multiple_of(k * CHUNK, CHUNK)
        wide = turned[:, pl.ds(start, CHUNK)].astype(jnp.float32)
        x = wide.T.astype(jnp.bfloat16)
        for q in range(4):
            parts[q, pl.ds(start, CHUNK), :] = mm(x, weight[q]).astype(jnp.bfloat16)
        send(start, CHUNK)
        reduced = mm(lower[...], turned[:, pl.ds(start, CHUNK)]).astype(jnp.bfloat16)
        for q in range(4):
            parts[q, pl.ds(pl.multiple_of(span + k * ROWS, ROWS), ROWS), :] = reduced
        squares[pl.ds(k, 1), :] = jnp.sum(wide * wide, axis=0, keepdims=True)
        member = member_ref[pl.ds(start, CHUNK), :].astype(jnp.float32).T.astype(jnp.bfloat16)
        residual[...] += mm(member[0:ROWS], x)
        return carry

    def zero(k, carry):
        start = pl.multiple_of(k * CHUNK, CHUNK)
        for q in range(4):
            parts[q, pl.ds(start, CHUNK), :] = jnp.zeros((CHUNK, width), jnp.bfloat16)
            parts[q, pl.ds(pl.multiple_of(span + k * ROWS, ROWS), ROWS), :] = jnp.zeros(
                (ROWS, width), jnp.bfloat16
            )
        send(start, CHUNK)
        return carry

    def within(place):
        return jnp.clip(place - base, 0, span)

    def take(b, done):
        vocab_copy(b).wait()
        for part in range(IDS_PER_BLOCK // IDS_PER_GROUP):
            group = b * (IDS_PER_BLOCK // IDS_PER_GROUP) + part
            first, last = within(bounds[group, 0]), within(bounds[group + 1, 0])
            begin = lax.shift_right_logical(first, LANE_BITS)
            end = lax.shift_right_logical(last + LANES - 1, LANE_BITS)

            def window(p, carry):
                at = pl.ds(pl.multiple_of(p * LANES, LANES), LANES)
                token = token_ref[pl.ds(p, 1), :] - group * IDS_PER_GROUP
                token = jnp.broadcast_to(token, (IDS_PER_GROUP, LANES))
                short = token.astype(jnp.int16)
                picked = jnp.where(
                    short == iota((IDS_PER_GROUP, LANES), 0).astype(jnp.int16), 1.0, 0.0
                ).astype(jnp.bfloat16)
                columns = pl.ds(part * IDS_PER_GROUP, IDS_PER_GROUP)
                found = mm(held[b, TAKEN:features, columns], picked)
                turned[TAKEN:features, at] += found.astype(jnp.bfloat16)
                lane = (token[0:FEATURE_ROWS] & (LANES - 1)).astype(jnp.int16)
                tile = lax.shift_right_arithmetic(token[0:FEATURE_ROWS], LANE_BITS)
                tile = tile.astype(jnp.int16)
                for f in range(TAKEN // FEATURE_ROWS):
                    rows = pl.ds(f * FEATURE_ROWS, FEATURE_ROWS)
                    total = turned[rows, at]
                    for j in range(IDS_PER_GROUP // LANES):
                        columns = pl.ds(part * IDS_PER_GROUP + j * LANES, LANES)
                        total = jnp.where(tile == j, take_lanes(held[b, rows, columns], lane), total)
                    turned[rows, at] = total
                return carry

            lax.fori_loop(begin, jnp.where(last > first, end, begin), window, 0)
        full = lax.shift_right_logical(last, CHUNK_BITS)
        lax.fori_loop(done, full, project, 0)
        return full

    done = lax.fori_loop(0, blocks, take, 0)
    used = lax.shift_right_logical(within(bounds[groups, 0]) + CHUNK - 1, CHUNK_BITS)
    lax.fori_loop(done, used, project, 0)
    lax.fori_loop(used, chunks, zero, 0)

    hard = small[...].T[0:ROWS]
    lane = iota((ROWS, width), 1)
    misc = jnp.concatenate([squares[...], jnp.zeros((ROWS - squares.shape[0], width), jnp.float32)])
    for i in range(per_shard):
        misc += jnp.where(lane == shard * per_shard + i, hard[:, i : i + 1], 0.0)
    mine = lax.axis_index("mp") == shard
    for q in range(4):
        start = pl.multiple_of(split_quarter(q // 2, q % 2) * width, LANES)
        part = jnp.where(mine, residual[:, pl.ds(start, width)], 0.0)
        parts[q, pl.ds(span + chunks * ROWS, ROWS), :] = misc.astype(jnp.bfloat16)
        parts[q, pl.ds(span + (chunks + 1) * ROWS, ROWS), :] = part.astype(jnp.bfloat16)
    send(span, (chunks + 2) * ROWS)
    for q in range(4):
        pltpu.make_async_copy(parts.at[q], outs[q], out_sems.at[q]).wait()


def pool_kernel(
    ids_ref,
    own_ref,
    core_ref,
    far_ref,
    member_ref,
    own_rest,
    core_rest,
    far_rest,
    member_rest,
    raise_ref,
    pooled_ref,
    slope_ref,
    reduced_ref,
    misc_ref,
    raised,
    total,
    model_width,
):
    texts, length = ids_ref.shape
    width = own_ref.shape[1]
    quarter = quarter_of(lax.axis_index("dp"))
    raised[...] = jnp.zeros_like(raised)
    raised[0:ROWS, :] = raise_ref[:, pl.ds(pl.multiple_of(quarter * width, LANES), width)]
    total[...] = jnp.zeros_like(total)

    def add(refs, member_ref, base):
        span = member_ref.shape[0]
        chunks = span // CHUNK

        def summed(start, size):
            return sum(ref[pl.ds(start, size), :].astype(jnp.float32) for ref in refs)

        misc = summed(span + chunks * ROWS, ROWS)
        if base == 0:
            misc_ref[...] = misc
        inverse = lax.rsqrt(misc / model_width + 1e-05)
        for k in range(chunks):
            at = base + k * CHUNK
            scale = inverse[k : k + 1]
            reduced = (summed(span + k * ROWS, ROWS) * scale).astype(jnp.bfloat16)
            reduced_ref[:, at : at + CHUNK] = reduced
            stacked = jnp.concatenate(
                [reduced.astype(jnp.float32), jnp.broadcast_to(scale, (LANES - ROWS, CHUNK))]
            )
            turned = stacked.T
            low = turned.astype(jnp.bfloat16)
            linear = summed(k * CHUNK, CHUNK) * turned[:, ROWS : ROWS + 1] + mm(low, raised[...])
            sigma = 1.0 / (1.0 + jnp.exp(-linear))
            slope_ref[pl.ds(at, CHUNK), :] = sigma * (1.0 + linear * (1.0 - sigma))
            member = member_ref[pl.ds(k * CHUNK, CHUNK), :].astype(jnp.float32).T
            member = member[0:ROWS].astype(jnp.bfloat16)
            high, rest = split(linear * sigma)
            total[...] += mm(member, high) + mm(member, rest)
        total[...] += summed(span + (chunks + 1) * ROWS, ROWS)

    add((own_ref, core_ref, far_ref), member_ref, 0)
    real = (ids_ref[...] != 0).astype(jnp.float32)

    @pl.when(jnp.sum(real) > member_ref.shape[0])
    def _():
        add((own_rest, core_rest, far_rest), member_rest, member_ref.shape[0])

    counts = jnp.sum(real, axis=1, keepdims=True)
    pooled = total[0:texts] / counts
    pooled = jnp.concatenate([pooled, jnp.zeros((ROWS - texts, width), jnp.float32)])
    for to in range(pooled_ref.shape[0]):
        pooled_ref[to] = pooled.astype(jnp.bfloat16)


def both_sides(pooled_ref, shard, shards):
    return jnp.concatenate([pooled_ref[shard], pooled_ref[shards + shard]], axis=0)


def dots_kernel(pooled_ref, dots_ref, shards):
    dots = jnp.zeros((2 * ROWS, 2 * ROWS), jnp.float32)
    for shard in range(shards):
        block = both_sides(pooled_ref, shard, shards)
        dots += mm(block, block, NT)
    wide = jnp.concatenate([dots, jnp.zeros((2 * ROWS, LANES - 2 * ROWS), jnp.float32)], axis=1)
    for to in range(dots_ref.shape[0]):
        dots_ref[to] = wide


def score_kernel(
    ids_ref,
    pooled_ref,
    dots_ref,
    misc_ref,
    slope_ref,
    reduced_ref,
    member_ref,
    member_rest,
    sharp_ref,
    embed_ref,
    loss_ref,
    up_ref,
    shards,
    negatives,
):
    texts, length = ids_ref.shape
    chunks = member_ref.shape[0] // CHUNK
    rows = 2 * ROWS
    width = pooled_ref.shape[2]
    per_shard = loss_ref.shape[1]
    group, shard = lax.axis_index("group"), lax.axis_index("dp")
    dots = dots_ref[0]
    for part in range(1, dots_ref.shape[0]):
        dots += dots_ref[part]
    dots = dots[:, 0:rows]
    down, across = iota((rows, rows), 0), iota((rows, rows), 1)
    same = down == across
    real = (lax.rem(down, ROWS) < texts) & (lax.rem(across, ROWS) < texts)
    diagonal = jnp.where(same, dots, 0.0)
    rnorm_row = lax.rsqrt(jnp.sum(diagonal, axis=0, keepdims=True) + 1e-06)
    rnorm_col = lax.rsqrt(jnp.sum(diagonal, axis=1, keepdims=True) + 1e-06)
    sharpness = sharp_ref[0]
    cosine = dots * rnorm_col * rnorm_row
    scores = sharpness * cosine
    keep = real & ~same
    top = jnp.max(jnp.where(keep, scores, -jnp.inf), axis=0, keepdims=True)
    top = jnp.where(lax.rem(across[0:1], ROWS) < texts, top, 0.0)
    powers = jnp.exp(jnp.where(real, jnp.minimum(scores - top, 0.0), 0.0))
    hard = misc_ref[chunks : chunks + negatives, 0:rows].astype(jnp.int32) + ROWS
    times = jnp.zeros((rows, rows), jnp.float32)
    for k in range(negatives):
        times += jnp.where(hard[k : k + 1] == down, 1.0, 0.0)
    times = jnp.where(across < texts, times, 0.0)
    weights = (jnp.where(keep, 1.0, 0.0) + jnp.where(real, times, 0.0)) * powers
    total = jnp.sum(weights, axis=0, keepdims=True)
    total = jnp.where(lax.rem(across[0:1], ROWS) < texts, total, 1.0)
    pair = (down == lax.rem(across + ROWS, rows)) & real
    pair_score = jnp.sum(jnp.where(pair, scores, 0.0), axis=0, keepdims=True)
    losses = top + jnp.log(total) - pair_score
    grad_scores = (weights / total - jnp.where(pair, 1.0, 0.0)) / (2 * texts)
    coeff = (grad_scores * rnorm_col * rnorm_row).astype(jnp.bfloat16)
    radial = jnp.sum(grad_scores * cosine, axis=0, keepdims=True) * rnorm_row * rnorm_row

    first = shard * per_shard
    loss_col = jnp.sum(jnp.where(same, losses, 0.0), axis=1, keepdims=True)
    at = (iota((rows, LANES), 0) == group * ROWS + first + iota((rows, LANES), 1)) & (
        iota((rows, LANES), 1) < per_shard
    )
    loss_ref[...] = jnp.sum(jnp.where(at, loss_col, 0.0), axis=0, keepdims=True)[:, 0:per_shard]

    mine = both_sides(pooled_ref, shard, shards)
    along = mm(coeff.astype(jnp.float32).T.astype(jnp.bfloat16), mine)
    radial_col = jnp.sum(jnp.where(same, radial, 0.0), axis=1, keepdims=True)
    grad = sharpness * (along - radial_col * mine.astype(jnp.float32))
    grad = jnp.where(group == 0, grad[0:ROWS], grad[ROWS:rows])
    real_tokens = (ids_ref[...] != 0).astype(jnp.float32)
    counts = jnp.sum(real_tokens, axis=1, keepdims=True)
    grad = grad[0:texts] / counts
    grad = jnp.concatenate([grad, jnp.zeros((LANES - texts, width), jnp.float32)])
    high, rest = split(grad)

    def update(member_ref, base):
        total = jnp.zeros((ROWS, width), jnp.float32)
        for k in range(member_ref.shape[0] // CHUNK):
            at = base + k * CHUNK
            member = member_ref[pl.ds(k * CHUNK, CHUNK), :]
            token_grad = mm(member, high) + mm(member, rest)
            local = (token_grad * slope_ref[pl.ds(at, CHUNK), :]).astype(jnp.bfloat16)
            total += mm(reduced_ref[:, at : at + CHUNK], local)
        return total

    first_part = update(member_ref, 0)
    for to in range(up_ref.shape[0]):
        up_ref[to] = first_part

    @pl.when(jnp.sum(real_tokens) > member_ref.shape[0])
    def _():
        whole = first_part + update(member_rest, member_ref.shape[0])
        for to in range(up_ref.shape[0]):
            up_ref[to] = whole

    rnorm_own = jnp.where(group == 0, rnorm_col[0:ROWS], rnorm_col[ROWS:rows])
    chosen = iota((ROWS, ROWS), 1) == iota((ROWS, ROWS), 0) + first
    chosen = jnp.where(chosen & (iota((ROWS, ROWS), 0) < per_shard), 1.0, 0.0).astype(jnp.bfloat16)
    for quarter in range(shards):
        block = pooled_ref[group * shards + quarter_of(quarter)].astype(jnp.float32) * rnorm_own
        picked = mm(chosen, block.astype(jnp.bfloat16)).astype(jnp.bfloat16)
        embed_ref[0, :, quarter * width : (quarter + 1) * width] = picked[0:per_shard]


def any_spec():
    return pl.BlockSpec(memory_space=pl.ANY)


def vmem_spec():
    return pl.BlockSpec(memory_space=pltpu.VMEM)


def smem_spec():
    return pl.BlockSpec(memory_space=pltpu.SMEM)


def split_body(
    query_passage_words,
    difficult_distractors,
    vocabulary_vectors,
    layer_weight_matrix,
    lowering_factor_matrix,
    raising_factor_matrix,
    logit_sharpness,
):
    shards, parts = lax.axis_size("dp"), lax.axis_size("mp")
    ids = query_passage_words[0]
    texts, length = ids.shape
    tokens = texts * length
    features, vocab = vocabulary_vectors.shape
    blocks = vocab // IDS_PER_BLOCK
    group_rows = 8 * pl.cdiv(vocab // IDS_PER_GROUP + 1, 8)
    per_shard, negatives = difficult_distractors.shape
    rank = lowering_factor_matrix.shape[0]
    part_width = layer_weight_matrix.shape[1]
    width = part_width // shards
    params = pltpu.CompilerParams(vmem_limit_bytes=VMEM_BYTES)
    other_core = [(d, d ^ 1) for d in range(shards)]
    other_y = [(d, d ^ 2) for d in range(shards)]

    def project(base, span):
        rows = span + (span // CHUNK + 2) * ROWS
        own0, own1, away0, away1, member = pl.pallas_call(
            functools.partial(project_kernel, base=base),
            out_shape=[jax.ShapeDtypeStruct((rows, width), jnp.bfloat16)] * 4
            + [jax.ShapeDtypeStruct((span, LANES), jnp.bfloat16)],
            in_specs=[vmem_spec()] * 2 + [any_spec()] * 3,
            out_specs=[any_spec()] * 4 + [vmem_spec()],
            scratch_shapes=[
                pltpu.VMEM((blocks, features, IDS_PER_BLOCK), jnp.bfloat16),
                pltpu.VMEM((4, features, width), jnp.bfloat16),
                pltpu.VMEM((rank, features), jnp.bfloat16),
                pltpu.VMEM((features, span), jnp.bfloat16),
                pltpu.VMEM((4, rows, width), jnp.bfloat16),
                pltpu.VMEM((8 * pl.cdiv(span // LANES, 8), LANES), jnp.int32),
                pltpu.VMEM((LANES, LANES), jnp.float32),
                pltpu.VMEM((texts, length), jnp.float32),
                pltpu.VMEM((8, width), jnp.float32),
                pltpu.VMEM((ROWS, features), jnp.float32),
                pltpu.VMEM((group_rows, length), jnp.int32),
                pltpu.SMEM((group_rows, length), jnp.int32),
                pltpu.SemaphoreType.DMA((blocks,)),
                pltpu.SemaphoreType.DMA((4,)),
                pltpu.SemaphoreType.DMA,
                pltpu.SemaphoreType.DMA,
                pltpu.SemaphoreType.DMA((4,)),
            ],
            compiler_params=params,
            name="project",
        )(
            ids,
            difficult_distractors,
            vocabulary_vectors,
            layer_weight_matrix,
            lowering_factor_matrix,
        )
        core1 = lax.ppermute(away1, "dp", other_core)
        core0 = lax.ppermute(away0, "dp", other_core)
        chip1 = (own1.astype(jnp.float32) + core1.astype(jnp.float32)).astype(jnp.bfloat16)
        far = lax.ppermute(chip1, "dp", other_y)
        return own0, core0, far, member

    first = project(0, FIRST)
    many = jnp.sum((ids != 0).astype(jnp.int32)) > FIRST
    left = tokens - FIRST
    shapes = jax.eval_shape(lambda: project(FIRST, left))
    rest = lax.cond(
        many,
        lambda: project(FIRST, left),
        lambda: tuple(jnp.zeros(x.shape, x.dtype) for x in shapes),
    )
    pooled, slope, reduced, misc = pl.pallas_call(
        functools.partial(pool_kernel, model_width=float(features * shards)),
        out_shape=[
            jax.ShapeDtypeStruct((2 * shards, ROWS, width), jnp.bfloat16),
            jax.ShapeDtypeStruct((tokens, width), jnp.float32),
            jax.ShapeDtypeStruct((ROWS, tokens), jnp.bfloat16),
            jax.ShapeDtypeStruct((ROWS, width), jnp.float32),
        ],
        in_specs=[vmem_spec()] * 10,
        out_specs=[vmem_spec()] * 4,
        scratch_shapes=[
            pltpu.VMEM((LANES, width), jnp.bfloat16),
            pltpu.VMEM((ROWS, width), jnp.float32),
        ],
        compiler_params=params,
        name="pool",
    )(ids, *first, *rest, raising_factor_matrix)
    member, member_rest = first[3], rest[3]
    sides = ("group", "dp")
    pooled = lax.all_to_all(pooled, sides, 0, 0)
    dots = pl.pallas_call(
        functools.partial(dots_kernel, shards=shards),
        out_shape=jax.ShapeDtypeStruct((parts, 2 * ROWS, LANES), jnp.float32),
        in_specs=[vmem_spec()],
        out_specs=vmem_spec(),
        compiler_params=params,
        name="dots",
    )(pooled)
    dots = lax.all_to_all(dots, "mp", 0, 0)
    embeddings, losses, update = pl.pallas_call(
        functools.partial(score_kernel, shards=shards, negatives=negatives),
        out_shape=[
            jax.ShapeDtypeStruct((1, per_shard, part_width), jnp.bfloat16),
            jax.ShapeDtypeStruct((1, per_shard), jnp.float32),
            jax.ShapeDtypeStruct((2 * shards, ROWS, width), jnp.float32),
        ],
        in_specs=[vmem_spec()] * 8 + [smem_spec()],
        out_specs=[vmem_spec()] * 3,
        compiler_params=params,
        name="score",
    )(ids, pooled, dots, misc, slope, reduced, member, member_rest, logit_sharpness)
    update = lax.all_to_all(update, sides, 0, 0)
    columns = [update[quarter_of(q)] + update[shards + quarter_of(q)] for q in range(shards)]
    return (embeddings, losses, jnp.concatenate(columns, axis=1))


def body(words, hard, vocabulary, weight, lowering, raising, sharpness):
    shards, parts = lax.axis_size("dp"), lax.axis_size("mp")
    texts, length = words.shape[1:]
    features, vocab = vocabulary.shape
    negatives = hard.shape[1]
    square = shards == 4 and features == weight.shape[1] and parts == shards
    small = texts <= ROWS - 2 and length == LANES and FIRST < texts * length <= 2048
    even = (texts * length) % CHUNK == 0 and vocab % IDS_PER_BLOCK == 0
    fits = features * vocab <= 2**24 and features % (4 * LANES) == 0
    spare = FIRST // CHUNK + negatives <= ROWS and lowering.shape[0] == ROWS
    fast = square and small and even and fits and spare and lax.axis_size("group") == 2
    chosen = split_body if fast else general_body
    return chosen(words, hard, vocabulary, weight, lowering, raising, sharpness)


def solution(mesh):
    in_specs = (
        P("group", None, None),
        P("dp", None),
        P("dp", None),
        P("dp", "mp"),
        P(),
        P(None, "mp"),
        P(),
    )
    out_specs = (P("group", "dp", "mp"), P("group", "dp"), P(None, "mp"))
    return jax.shard_map(body, mesh=mesh, in_specs=in_specs, out_specs=out_specs, check_vma=False)
```

```python
import functools

import jax
import jax.numpy as jnp
from jax import lax
from jax.experimental import pallas as pl
from jax.experimental.pallas import tpu as pltpu
from jax.sharding import PartitionSpec as P


def general_body(
    query_passage_words,
    difficult_distractors,
    vocabulary_vectors,
    layer_weight_matrix,
    lowering_factor_matrix,
    raising_factor_matrix,
    logit_sharpness,
):
    group_index = lax.axis_index("group")
    shard_index = lax.axis_index("dp")
    part_index = lax.axis_index("mp")
    shard_count = lax.axis_size("dp")
    side_ids = query_passage_words[0]
    text_count = side_ids.shape[0]
    length = side_ids.shape[1]
    per_shard = text_count // shard_count
    own_ids = lax.dynamic_slice_in_dim(side_ids, shard_index * per_shard, per_shard, 0)
    columns = jnp.take(vocabulary_vectors, side_ids.reshape(-1), axis=1)
    inputs = lax.all_to_all(columns, "dp", split_axis=1, concat_axis=0, tiled=True)
    tokens = inputs.shape[1]
    feature_width = raising_factor_matrix.shape[1]
    wide_inputs = inputs.astype(jnp.float32)
    inverse = lax.rsqrt(jnp.mean(wide_inputs * wide_inputs, axis=0) + 1e-05)
    normed_state = (wide_inputs * inverse[None, :]).astype(jnp.bfloat16)
    linear_map = lax.dot_general(
        lax.all_gather(layer_weight_matrix, "dp", axis=0, tiled=True),
        normed_state,
        (((0,), (0,)), ((), ())),
        preferred_element_type=jnp.float32,
    )
    reduced_sum = jnp.dot(
        lowering_factor_matrix, normed_state, preferred_element_type=jnp.float32
    ).astype(jnp.bfloat16)
    linear_map = linear_map + lax.dot_general(
        raising_factor_matrix,
        reduced_sum,
        (((0,), (0,)), ((), ())),
        preferred_element_type=jnp.float32,
    )
    own_inputs = lax.dynamic_slice_in_dim(
        inputs, part_index * feature_width, feature_width, 0
    ).astype(jnp.float32)
    hidden_state = own_inputs + jax.nn.silu(linear_map)
    mask = (own_ids != 0).astype(jnp.float32)
    counts = jnp.sum(mask, axis=1)
    summed = jnp.einsum("dnl,nl->nd", hidden_state.reshape(feature_width, per_shard, length), mask)
    pooled = (summed / counts[:, None]).astype(jnp.bfloat16)
    gathered = lax.all_gather(pooled, ("group", "dp"), axis=0, tiled=True)
    part_scores = lax.dot_general(
        pooled, gathered, (((1,), (1,)), ((), ())), preferred_element_type=jnp.float32
    )
    gathered_wide = gathered.astype(jnp.float32)
    part_norms = jnp.sum(gathered_wide * gathered_wide, axis=1)
    dots, norms = lax.psum((part_scores, part_norms), "mp")
    rnorm_all = lax.rsqrt(norms + 1e-06)
    all_count = gathered.shape[0]
    half_count = all_count // 2
    own_rows = (
        group_index * half_count + shard_index * per_shard + jnp.arange(per_shard, dtype=jnp.int32)
    )
    rnorm_own = jnp.take(rnorm_all, own_rows)
    cosine = dots * rnorm_own[:, None] * rnorm_all[None, :]
    multiplier_factor = logit_sharpness[0]
    scores = multiplier_factor * cosine
    column_ids = jnp.arange(all_count, dtype=jnp.int32)
    keep = column_ids[None, :] != own_rows[:, None]
    pair = (own_rows + half_count) % all_count
    weight = (group_index == 0).astype(jnp.float32)
    neg_cols = half_count + difficult_distractors
    top = jnp.max(jnp.where(keep, scores, -jnp.inf), axis=1)
    safe_scores = jnp.where(keep, scores, top[:, None])
    expd = jnp.where(keep, jnp.exp(safe_scores - top[:, None]), 0.0)
    neg_exp = (
        jnp.exp(jnp.minimum(jnp.take_along_axis(scores, neg_cols, axis=1) - top[:, None], 0.0))
        * weight
    )
    total = jnp.sum(expd, axis=1) + jnp.sum(neg_exp, axis=1)
    pair_score = jnp.take_along_axis(scores, pair[:, None], axis=1)[:, 0]
    losses = top + jnp.log(total) - pair_score
    onehot = (column_ids[None, None, :] == neg_cols[:, :, None]).astype(jnp.float32)
    probs = (expd + jnp.einsum("rk,rkc->rc", neg_exp, onehot)) / total[:, None]
    target = (column_ids[None, :] == pair[:, None]).astype(jnp.float32)
    grad_scores = (probs - target) / all_count
    coeff = (grad_scores * rnorm_own[:, None] * rnorm_all[None, :]).astype(jnp.bfloat16)
    along = jnp.dot(coeff, gathered, preferred_element_type=jnp.float32)
    pooled_wide = pooled.astype(jnp.float32)
    radial = jnp.sum(grad_scores * cosine, axis=1) * rnorm_own * rnorm_own
    embedding_gradient = multiplier_factor * (along - radial[:, None] * pooled_wide)
    token_grad = jnp.einsum("nd,nl->dnl", embedding_gradient / counts[:, None], mask).reshape(
        feature_width, tokens
    )
    sigma = jax.nn.sigmoid(linear_map)
    local = (token_grad * sigma * (1.0 + linear_map * (1.0 - sigma))).astype(jnp.bfloat16)
    up_portion = lax.dot_general(
        reduced_sum, local, (((1,), (1,)), ((), ())), preferred_element_type=jnp.float32
    )
    adapter_up_gradient = lax.psum(up_portion, ("group", "dp"))
    embeddings = (pooled_wide * rnorm_own[:, None]).astype(jnp.bfloat16)[None]
    return (embeddings, losses[None], adapter_up_gradient)


BLOCK_BITS, GROUP_BITS, CHUNK_BITS, LANE_BITS, ROW_BITS = 11, 9, 8, 7, 4
IDS_PER_BLOCK = 1 << BLOCK_BITS
IDS_PER_GROUP = 1 << GROUP_BITS
CHUNK = 1 << CHUNK_BITS
ROWS = 1 << ROW_BITS
LANES = 1 << LANE_BITS
FEATURE_ROWS = 256
TAKEN = 512
FIRST = 1024
NT = (((1,), (1,)), ((), ()))
VMEM_BYTES = 60 * 1024 * 1024


def mm(a, b, dims=(((1,), (0,)), ((), ()))):
    return lax.dot_general(a, b, dims, preferred_element_type=jnp.float32)


def split(x):
    high = x.astype(jnp.bfloat16)
    return high, (x - high.astype(jnp.float32)).astype(jnp.bfloat16)


def iota(shape, dim):
    return lax.broadcasted_iota(jnp.int32, shape, dim)


def quarter_of(dp_index, cores=2):
    return (dp_index % cores) * 2 + dp_index // cores


def split_quarter(i, j, cores=2):
    shard = lax.axis_index("dp")
    core, side_y = lax.rem(shard, cores), lax.div(shard, cores)
    return (core ^ i) * 2 + (side_y ^ j)


def take_lanes(x, lanes):
    numbers = lax.GatherDimensionNumbers(
        offset_dims=(),
        collapsed_slice_dims=(1,),
        start_index_map=(1,),
        operand_batching_dims=(0,),
        start_indices_batching_dims=(0,),
    )
    mode = lax.GatherScatterMode.PROMISE_IN_BOUNDS
    return lax.gather(x, lanes[..., None], numbers, slice_sizes=(1, 1), mode=mode)


def project_kernel(
    ids_ref,
    hard_ref,
    vocab_ref,
    weight_ref,
    lower_ref,
    out00,
    out01,
    out10,
    out11,
    member_ref,
    held,
    weight,
    lower,
    turned,
    parts,
    token_ref,
    small,
    ranks,
    squares,
    residual,
    counted,
    bounds,
    held_sems,
    weight_sem,
    lower_sem,
    bounds_sem,
    out_sems,
    base,
):
    texts, length = ids_ref.shape
    features, vocab = vocab_ref.shape
    blocks = vocab // IDS_PER_BLOCK
    groups = vocab // IDS_PER_GROUP
    span = member_ref.shape[0]
    chunks = span // CHUNK
    per_shard, negatives = hard_ref.shape
    width = out00.shape[1]
    outs = (out00, out01, out10, out11)
    shard = lax.axis_index("dp")

    def vocab_copy(b):
        columns = pl.ds(pl.multiple_of(b * IDS_PER_BLOCK, LANES), IDS_PER_BLOCK)
        return pltpu.make_async_copy(vocab_ref.at[:, columns], held.at[b], held_sems.at[b])

    weight_copy = pltpu.make_async_copy(weight_ref, weight, weight_sem)
    lower_copy = pltpu.make_async_copy(
        lower_ref.at[:, pl.ds(pl.multiple_of(shard * features, LANES), features)], lower, lower_sem
    )
    vocab_copy(0).start()
    lower_copy.start()
    weight_copy.start()
    for b in range(1, blocks):
        vocab_copy(b).start()

    ids = ids_ref[...]
    valid = ids != 0
    group_of = jnp.where(valid, lax.shift_right_logical(ids, GROUP_BITS), groups)
    group_rows = counted.shape[0]
    group_id = iota((group_rows, length), 0)
    below = jnp.zeros((group_rows, length), jnp.float32)
    for text in range(texts):
        below += jnp.where(group_of[text : text + 1] < group_id, 1.0, 0.0)
    before = jnp.broadcast_to(jnp.sum(below, axis=1, keepdims=True), (group_rows, length))
    counted[...] = before.astype(jnp.int32)
    bounds_copy = pltpu.make_async_copy(counted, bounds, bounds_sem)
    bounds_copy.start()
    earlier = jnp.where(iota((length, length), 0) < iota((length, length), 1), 1.0, 0.0).astype(
        jnp.bfloat16
    )
    for text in range(texts):
        here = jnp.where(group_of[text : text + 1] == group_id, 1.0, 0.0)
        inside = mm(here.astype(jnp.bfloat16), earlier)
        ranks[pl.ds(text, 1), :] = jnp.sum(here * (inside + before), axis=0, keepdims=True)
        before += jnp.broadcast_to(jnp.sum(here, axis=1, keepdims=True), (group_rows, length))
    text_of = iota((texts, length), 0)
    carried = jnp.where(valid, lax.shift_left(ids, ROW_BITS) + text_of, 0).astype(jnp.float32)
    rank = ranks[...]

    def place(p, carry):
        position = (iota((LANES, length), 0) + (p * LANES + base)).astype(jnp.float32)
        total = jnp.zeros((LANES, length), jnp.float32)
        for text in range(texts):
            total += jnp.where(rank[text : text + 1] == position, carried[text : text + 1], 0.0)
        found = jnp.broadcast_to(jnp.sum(total, axis=1, keepdims=True), (LANES, LANES))
        start = pl.multiple_of(p * LANES, LANES)
        row = found.T[0:1].astype(jnp.int32)
        token = lax.shift_right_logical(row, ROW_BITS)
        token_ref[pl.ds(p, 1), :] = jnp.where(token == 0, -vocab, token)
        found = found.astype(jnp.int32)
        real = (found >= ROWS) & ((found & (ROWS - 1)) == iota((LANES, LANES), 1))
        member_ref[pl.ds(start, LANES), :] = jnp.where(real, 1.0, 0.0).astype(jnp.bfloat16)
        turned[:, pl.ds(start, LANES)] = jnp.zeros((features, LANES), jnp.bfloat16)
        return carry

    lax.fori_loop(0, span // LANES, place, 0)
    residual[...] = jnp.zeros_like(residual)
    squares[...] = jnp.zeros_like(squares)
    small[...] = jnp.zeros_like(small)
    small[0:per_shard, chunks : chunks + negatives] = hard_ref[...].astype(jnp.float32)
    lower_copy.wait()
    weight_copy.wait()
    bounds_copy.wait()

    def send(start, size):
        rows = pl.ds(start, size)
        for q in range(4):
            pltpu.make_async_copy(parts.at[q, rows], outs[q].at[rows], out_sems.at[q]).start()

    def project(k, carry):
        start = pl.multiple_of(k * CHUNK, CHUNK)
        wide = turned[:, pl.ds(start, CHUNK)].astype(jnp.float32)
        x = wide.T.astype(jnp.bfloat16)
        for q in range(4):
            at = pl.multiple_of(split_quarter(q // 2, q % 2) * width, LANES)
            product = mm(x, weight[:, pl.ds(at, width)])
            parts[q, pl.ds(start, CHUNK), :] = product.astype(jnp.bfloat16)
        send(start, CHUNK)
        reduced = mm(lower[...], turned[:, pl.ds(start, CHUNK)]).astype(jnp.bfloat16)
        for q in range(4):
            parts[q, pl.ds(pl.multiple_of(span + k * ROWS, ROWS), ROWS), :] = reduced
        squares[pl.ds(k, 1), :] = jnp.sum(wide * wide, axis=0, keepdims=True)
        member = member_ref[pl.ds(start, CHUNK), :].astype(jnp.float32).T.astype(jnp.bfloat16)
        residual[...] += mm(member[0:ROWS], x)
        return carry

    def zero(k, carry):
        start = pl.multiple_of(k * CHUNK, CHUNK)
        for q in range(4):
            parts[q, pl.ds(start, CHUNK), :] = jnp.zeros((CHUNK, width), jnp.bfloat16)
            parts[q, pl.ds(pl.multiple_of(span + k * ROWS, ROWS), ROWS), :] = jnp.zeros(
                (ROWS, width), jnp.bfloat16
            )
        send(start, CHUNK)
        return carry

    def within(place):
        return jnp.clip(place - base, 0, span)

    def take(b, done):
        vocab_copy(b).wait()
        for part in range(IDS_PER_BLOCK // IDS_PER_GROUP):
            group = b * (IDS_PER_BLOCK // IDS_PER_GROUP) + part
            first, last = within(bounds[group, 0]), within(bounds[group + 1, 0])
            begin = lax.shift_right_logical(first, LANE_BITS)
            end = lax.shift_right_logical(last + LANES - 1, LANE_BITS)

            def window(p, carry):
                at = pl.ds(pl.multiple_of(p * LANES, LANES), LANES)
                token = token_ref[pl.ds(p, 1), :] - group * IDS_PER_GROUP
                token = jnp.broadcast_to(token, (IDS_PER_GROUP, LANES))
                short = token.astype(jnp.int16)
                picked = jnp.where(
                    short == iota((IDS_PER_GROUP, LANES), 0).astype(jnp.int16), 1.0, 0.0
                ).astype(jnp.bfloat16)
                columns = pl.ds(part * IDS_PER_GROUP, IDS_PER_GROUP)
                found = mm(held[b, TAKEN:features, columns], picked)
                turned[TAKEN:features, at] += found.astype(jnp.bfloat16)
                lane = (token[0:FEATURE_ROWS] & (LANES - 1)).astype(jnp.int16)
                tile = lax.shift_right_arithmetic(token[0:FEATURE_ROWS], LANE_BITS)
                tile = tile.astype(jnp.int16)
                for f in range(TAKEN // FEATURE_ROWS):
                    rows = pl.ds(f * FEATURE_ROWS, FEATURE_ROWS)
                    total = turned[rows, at]
                    for j in range(IDS_PER_GROUP // LANES):
                        columns = pl.ds(part * IDS_PER_GROUP + j * LANES, LANES)
                        total = jnp.where(tile == j, take_lanes(held[b, rows, columns], lane), total)
                    turned[rows, at] = total
                return carry

            lax.fori_loop(begin, jnp.where(last > first, end, begin), window, 0)
        full = lax.shift_right_logical(last, CHUNK_BITS)
        lax.fori_loop(done, full, project, 0)
        return full

    done = lax.fori_loop(0, blocks, take, 0)
    used = lax.shift_right_logical(within(bounds[groups, 0]) + CHUNK - 1, CHUNK_BITS)
    lax.fori_loop(done, used, project, 0)
    lax.fori_loop(used, chunks, zero, 0)

    hard = small[...].T[0:ROWS]
    lane = iota((ROWS, width), 1)
    misc = jnp.concatenate([squares[...], jnp.zeros((ROWS - squares.shape[0], width), jnp.float32)])
    for i in range(per_shard):
        misc += jnp.where(lane == shard * per_shard + i, hard[:, i : i + 1], 0.0)
    mine = lax.axis_index("mp") == shard
    for q in range(4):
        start = pl.multiple_of(split_quarter(q // 2, q % 2) * width, LANES)
        part = jnp.where(mine, residual[:, pl.ds(start, width)], 0.0)
        parts[q, pl.ds(span + chunks * ROWS, ROWS), :] = misc.astype(jnp.bfloat16)
        parts[q, pl.ds(span + (chunks + 1) * ROWS, ROWS), :] = part.astype(jnp.bfloat16)
    send(span, (chunks + 2) * ROWS)
    for q in range(4):
        pltpu.make_async_copy(parts.at[q], outs[q], out_sems.at[q]).wait()


def pool_kernel(
    ids_ref,
    own_ref,
    core_ref,
    far_ref,
    member_ref,
    own_rest,
    core_rest,
    far_rest,
    member_rest,
    raise_ref,
    pooled_ref,
    slope_ref,
    reduced_ref,
    misc_ref,
    raised,
    total,
    model_width,
):
    texts, length = ids_ref.shape
    width = own_ref.shape[1]
    quarter = quarter_of(lax.axis_index("dp"))
    raised[...] = jnp.zeros_like(raised)
    raised[0:ROWS, :] = raise_ref[:, pl.ds(pl.multiple_of(quarter * width, LANES), width)]
    total[...] = jnp.zeros_like(total)

    def add(refs, member_ref, base):
        span = member_ref.shape[0]
        chunks = span // CHUNK

        def summed(start, size):
            return sum(ref[pl.ds(start, size), :].astype(jnp.float32) for ref in refs)

        misc = summed(span + chunks * ROWS, ROWS)
        if base == 0:
            misc_ref[...] = misc
        inverse = lax.rsqrt(misc / model_width + 1e-05)
        for k in range(chunks):
            at = base + k * CHUNK
            scale = inverse[k : k + 1]
            reduced = (summed(span + k * ROWS, ROWS) * scale).astype(jnp.bfloat16)
            reduced_ref[:, at : at + CHUNK] = reduced
            stacked = jnp.concatenate(
                [reduced.astype(jnp.float32), jnp.broadcast_to(scale, (LANES - ROWS, CHUNK))]
            )
            turned = stacked.T
            low = turned.astype(jnp.bfloat16)
            linear = summed(k * CHUNK, CHUNK) * turned[:, ROWS : ROWS + 1] + mm(low, raised[...])
            sigma = 1.0 / (1.0 + jnp.exp(-linear))
            slope_ref[pl.ds(at, CHUNK), :] = sigma * (1.0 + linear * (1.0 - sigma))
            member = member_ref[pl.ds(k * CHUNK, CHUNK), :].astype(jnp.float32).T
            member = member[0:ROWS].astype(jnp.bfloat16)
            high, rest = split(linear * sigma)
            total[...] += mm(member, high) + mm(member, rest)
        total[...] += summed(span + (chunks + 1) * ROWS, ROWS)

    add((own_ref, core_ref, far_ref), member_ref, 0)
    real = (ids_ref[...] != 0).astype(jnp.float32)

    @pl.when(jnp.sum(real) > member_ref.shape[0])
    def _():
        add((own_rest, core_rest, far_rest), member_rest, member_ref.shape[0])

    counts = jnp.sum(real, axis=1, keepdims=True)
    pooled = total[0:texts] / counts
    pooled = jnp.concatenate([pooled, jnp.zeros((ROWS - texts, width), jnp.float32)])
    for to in range(pooled_ref.shape[0]):
        pooled_ref[to] = pooled.astype(jnp.bfloat16)


def both_sides(pooled_ref, shard, shards):
    return jnp.concatenate([pooled_ref[shard], pooled_ref[shards + shard]], axis=0)


def dots_kernel(pooled_ref, dots_ref, shards):
    dots = jnp.zeros((2 * ROWS, 2 * ROWS), jnp.float32)
    for shard in range(shards):
        block = both_sides(pooled_ref, shard, shards)
        dots += mm(block, block, NT)
    wide = jnp.concatenate([dots, jnp.zeros((2 * ROWS, LANES - 2 * ROWS), jnp.float32)], axis=1)
    for to in range(dots_ref.shape[0]):
        dots_ref[to] = wide


def score_kernel(
    ids_ref,
    pooled_ref,
    dots_ref,
    misc_ref,
    slope_ref,
    reduced_ref,
    member_ref,
    member_rest,
    sharp_ref,
    embed_ref,
    loss_ref,
    up_ref,
    shards,
    negatives,
):
    texts, length = ids_ref.shape
    chunks = member_ref.shape[0] // CHUNK
    rows = 2 * ROWS
    width = pooled_ref.shape[2]
    per_shard = loss_ref.shape[1]
    group, shard = lax.axis_index("group"), lax.axis_index("dp")
    dots = dots_ref[0]
    for part in range(1, dots_ref.shape[0]):
        dots += dots_ref[part]
    dots = dots[:, 0:rows]
    down, across = iota((rows, rows), 0), iota((rows, rows), 1)
    same = down == across
    real = (lax.rem(down, ROWS) < texts) & (lax.rem(across, ROWS) < texts)
    diagonal = jnp.where(same, dots, 0.0)
    rnorm_row = lax.rsqrt(jnp.sum(diagonal, axis=0, keepdims=True) + 1e-06)
    rnorm_col = lax.rsqrt(jnp.sum(diagonal, axis=1, keepdims=True) + 1e-06)
    sharpness = sharp_ref[0]
    cosine = dots * rnorm_col * rnorm_row
    scores = sharpness * cosine
    keep = real & ~same
    top = jnp.max(jnp.where(keep, scores, -jnp.inf), axis=0, keepdims=True)
    top = jnp.where(lax.rem(across[0:1], ROWS) < texts, top, 0.0)
    powers = jnp.exp(jnp.where(real, jnp.minimum(scores - top, 0.0), 0.0))
    hard = misc_ref[chunks : chunks + negatives, 0:rows].astype(jnp.int32) + ROWS
    times = jnp.zeros((rows, rows), jnp.float32)
    for k in range(negatives):
        times += jnp.where(hard[k : k + 1] == down, 1.0, 0.0)
    times = jnp.where(across < texts, times, 0.0)
    weights = (jnp.where(keep, 1.0, 0.0) + jnp.where(real, times, 0.0)) * powers
    total = jnp.sum(weights, axis=0, keepdims=True)
    total = jnp.where(lax.rem(across[0:1], ROWS) < texts, total, 1.0)
    pair = (down == lax.rem(across + ROWS, rows)) & real
    pair_score = jnp.sum(jnp.where(pair, scores, 0.0), axis=0, keepdims=True)
    losses = top + jnp.log(total) - pair_score
    grad_scores = (weights / total - jnp.where(pair, 1.0, 0.0)) / (2 * texts)
    coeff = (grad_scores * rnorm_col * rnorm_row).astype(jnp.bfloat16)
    radial = jnp.sum(grad_scores * cosine, axis=0, keepdims=True) * rnorm_row * rnorm_row

    first = shard * per_shard
    loss_col = jnp.sum(jnp.where(same, losses, 0.0), axis=1, keepdims=True)
    at = (iota((rows, LANES), 0) == group * ROWS + first + iota((rows, LANES), 1)) & (
        iota((rows, LANES), 1) < per_shard
    )
    loss_ref[...] = jnp.sum(jnp.where(at, loss_col, 0.0), axis=0, keepdims=True)[:, 0:per_shard]

    mine = both_sides(pooled_ref, shard, shards)
    along = mm(coeff.astype(jnp.float32).T.astype(jnp.bfloat16), mine)
    radial_col = jnp.sum(jnp.where(same, radial, 0.0), axis=1, keepdims=True)
    grad = sharpness * (along - radial_col * mine.astype(jnp.float32))
    grad = jnp.where(group == 0, grad[0:ROWS], grad[ROWS:rows])
    real_tokens = (ids_ref[...] != 0).astype(jnp.float32)
    counts = jnp.sum(real_tokens, axis=1, keepdims=True)
    grad = grad[0:texts] / counts
    grad = jnp.concatenate([grad, jnp.zeros((LANES - texts, width), jnp.float32)])
    high, rest = split(grad)

    def update(member_ref, base):
        total = jnp.zeros((ROWS, width), jnp.float32)
        for k in range(member_ref.shape[0] // CHUNK):
            at = base + k * CHUNK
            member = member_ref[pl.ds(k * CHUNK, CHUNK), :]
            token_grad = mm(member, high) + mm(member, rest)
            local = (token_grad * slope_ref[pl.ds(at, CHUNK), :]).astype(jnp.bfloat16)
            total += mm(reduced_ref[:, at : at + CHUNK], local)
        return total

    first_part = update(member_ref, 0)
    for to in range(up_ref.shape[0]):
        up_ref[to] = first_part

    @pl.when(jnp.sum(real_tokens) > member_ref.shape[0])
    def _():
        whole = first_part + update(member_rest, member_ref.shape[0])
        for to in range(up_ref.shape[0]):
            up_ref[to] = whole

    rnorm_own = jnp.where(group == 0, rnorm_col[0:ROWS], rnorm_col[ROWS:rows])
    chosen = iota((ROWS, ROWS), 1) == iota((ROWS, ROWS), 0) + first
    chosen = jnp.where(chosen & (iota((ROWS, ROWS), 0) < per_shard), 1.0, 0.0).astype(jnp.bfloat16)
    for quarter in range(shards):
        block = pooled_ref[group * shards + quarter_of(quarter)].astype(jnp.float32) * rnorm_own
        picked = mm(chosen, block.astype(jnp.bfloat16)).astype(jnp.bfloat16)
        embed_ref[0, :, quarter * width : (quarter + 1) * width] = picked[0:per_shard]


def any_spec():
    return pl.BlockSpec(memory_space=pl.ANY)


def vmem_spec():
    return pl.BlockSpec(memory_space=pltpu.VMEM)


def smem_spec():
    return pl.BlockSpec(memory_space=pltpu.SMEM)


def split_body(
    query_passage_words,
    difficult_distractors,
    vocabulary_vectors,
    layer_weight_matrix,
    lowering_factor_matrix,
    raising_factor_matrix,
    logit_sharpness,
):
    shards, parts = lax.axis_size("dp"), lax.axis_size("mp")
    ids = query_passage_words[0]
    texts, length = ids.shape
    tokens = texts * length
    features, vocab = vocabulary_vectors.shape
    blocks = vocab // IDS_PER_BLOCK
    group_rows = 8 * pl.cdiv(vocab // IDS_PER_GROUP + 1, 8)
    per_shard, negatives = difficult_distractors.shape
    rank = lowering_factor_matrix.shape[0]
    part_width = layer_weight_matrix.shape[1]
    width = part_width // shards
    params = pltpu.CompilerParams(vmem_limit_bytes=VMEM_BYTES)
    other_core = [(d, d ^ 1) for d in range(shards)]
    other_y = [(d, d ^ 2) for d in range(shards)]

    def project(base, span):
        rows = span + (span // CHUNK + 2) * ROWS
        own0, own1, away0, away1, member = pl.pallas_call(
            functools.partial(project_kernel, base=base),
            out_shape=[jax.ShapeDtypeStruct((rows, width), jnp.bfloat16)] * 4
            + [jax.ShapeDtypeStruct((span, LANES), jnp.bfloat16)],
            in_specs=[vmem_spec()] * 2 + [any_spec()] * 3,
            out_specs=[any_spec()] * 4 + [vmem_spec()],
            scratch_shapes=[
                pltpu.VMEM((blocks, features, IDS_PER_BLOCK), jnp.bfloat16),
                pltpu.VMEM((features, part_width), jnp.bfloat16),
                pltpu.VMEM((rank, features), jnp.bfloat16),
                pltpu.VMEM((features, span), jnp.bfloat16),
                pltpu.VMEM((4, rows, width), jnp.bfloat16),
                pltpu.VMEM((8 * pl.cdiv(span // LANES, 8), LANES), jnp.int32),
                pltpu.VMEM((LANES, LANES), jnp.float32),
                pltpu.VMEM((texts, length), jnp.float32),
                pltpu.VMEM((8, width), jnp.float32),
                pltpu.VMEM((ROWS, features), jnp.float32),
                pltpu.VMEM((group_rows, length), jnp.int32),
                pltpu.SMEM((group_rows, length), jnp.int32),
                pltpu.SemaphoreType.DMA((blocks,)),
                pltpu.SemaphoreType.DMA,
                pltpu.SemaphoreType.DMA,
                pltpu.SemaphoreType.DMA,
                pltpu.SemaphoreType.DMA((4,)),
            ],
            compiler_params=params,
            name="project",
        )(
            ids,
            difficult_distractors,
            vocabulary_vectors,
            layer_weight_matrix,
            lowering_factor_matrix,
        )
        core1 = lax.ppermute(away1, "dp", other_core)
        core0 = lax.ppermute(away0, "dp", other_core)
        chip1 = (own1.astype(jnp.float32) + core1.astype(jnp.float32)).astype(jnp.bfloat16)
        far = lax.ppermute(chip1, "dp", other_y)
        return own0, core0, far, member

    first = project(0, FIRST)
    many = jnp.sum((ids != 0).astype(jnp.int32)) > FIRST
    left = tokens - FIRST
    shapes = jax.eval_shape(lambda: project(FIRST, left))
    rest = lax.cond(
        many,
        lambda: project(FIRST, left),
        lambda: tuple(jnp.zeros(x.shape, x.dtype) for x in shapes),
    )
    pooled, slope, reduced, misc = pl.pallas_call(
        functools.partial(pool_kernel, model_width=float(features * shards)),
        out_shape=[
            jax.ShapeDtypeStruct((2 * shards, ROWS, width), jnp.bfloat16),
            jax.ShapeDtypeStruct((tokens, width), jnp.float32),
            jax.ShapeDtypeStruct((ROWS, tokens), jnp.bfloat16),
            jax.ShapeDtypeStruct((ROWS, width), jnp.float32),
        ],
        in_specs=[vmem_spec()] * 10,
        out_specs=[vmem_spec()] * 4,
        scratch_shapes=[
            pltpu.VMEM((LANES, width), jnp.bfloat16),
            pltpu.VMEM((ROWS, width), jnp.float32),
        ],
        compiler_params=params,
        name="pool",
    )(ids, *first, *rest, raising_factor_matrix)
    member, member_rest = first[3], rest[3]
    sides = ("group", "dp")
    pooled = lax.all_to_all(pooled, sides, 0, 0)
    dots = pl.pallas_call(
        functools.partial(dots_kernel, shards=shards),
        out_shape=jax.ShapeDtypeStruct((parts, 2 * ROWS, LANES), jnp.float32),
        in_specs=[vmem_spec()],
        out_specs=vmem_spec(),
        compiler_params=params,
        name="dots",
    )(pooled)
    dots = lax.all_to_all(dots, "mp", 0, 0)
    embeddings, losses, update = pl.pallas_call(
        functools.partial(score_kernel, shards=shards, negatives=negatives),
        out_shape=[
            jax.ShapeDtypeStruct((1, per_shard, part_width), jnp.bfloat16),
            jax.ShapeDtypeStruct((1, per_shard), jnp.float32),
            jax.ShapeDtypeStruct((2 * shards, ROWS, width), jnp.float32),
        ],
        in_specs=[vmem_spec()] * 8 + [smem_spec()],
        out_specs=[vmem_spec()] * 3,
        compiler_params=params,
        name="score",
    )(ids, pooled, dots, misc, slope, reduced, member, member_rest, logit_sharpness)
    update = lax.all_to_all(update, sides, 0, 0)
    columns = [update[quarter_of(q)] + update[shards + quarter_of(q)] for q in range(shards)]
    return (embeddings, losses, jnp.concatenate(columns, axis=1))


def body(words, hard, vocabulary, weight, lowering, raising, sharpness):
    shards, parts = lax.axis_size("dp"), lax.axis_size("mp")
    texts, length = words.shape[1:]
    features, vocab = vocabulary.shape
    negatives = hard.shape[1]
    square = shards == 4 and features == weight.shape[1] and parts == shards
    small = texts <= ROWS - 2 and length == LANES and FIRST < texts * length <= 2048
    even = (texts * length) % CHUNK == 0 and vocab % IDS_PER_BLOCK == 0
    fits = features * vocab <= 2**24 and features % (4 * LANES) == 0
    spare = FIRST // CHUNK + negatives <= ROWS and lowering.shape[0] == ROWS
    fast = square and small and even and fits and spare and lax.axis_size("group") == 2
    chosen = split_body if fast else general_body
    return chosen(words, hard, vocabulary, weight, lowering, raising, sharpness)


def solution(mesh):
    in_specs = (
        P("group", None, None),
        P("dp", None),
        P("dp", None),
        P("dp", "mp"),
        P(),
        P(None, "mp"),
        P(),
    )
    out_specs = (P("group", "dp", "mp"), P("group", "dp"), P(None, "mp"))
    return jax.shard_map(body, mesh=mesh, in_specs=in_specs, out_specs=out_specs, check_vma=False)
```

```python
import functools

import jax
import jax.numpy as jnp
from jax import lax
from jax.experimental import pallas as pl
from jax.experimental.pallas import tpu as pltpu
from jax.sharding import PartitionSpec as P


def general_body(
    query_passage_words,
    difficult_distractors,
    vocabulary_vectors,
    layer_weight_matrix,
    lowering_factor_matrix,
    raising_factor_matrix,
    logit_sharpness,
):
    group_index = lax.axis_index("group")
    shard_index = lax.axis_index("dp")
    part_index = lax.axis_index("mp")
    shard_count = lax.axis_size("dp")
    side_ids = query_passage_words[0]
    text_count = side_ids.shape[0]
    length = side_ids.shape[1]
    per_shard = text_count // shard_count
    own_ids = lax.dynamic_slice_in_dim(side_ids, shard_index * per_shard, per_shard, 0)
    columns = jnp.take(vocabulary_vectors, side_ids.reshape(-1), axis=1)
    inputs = lax.all_to_all(columns, "dp", split_axis=1, concat_axis=0, tiled=True)
    tokens = inputs.shape[1]
    feature_width = raising_factor_matrix.shape[1]
    wide_inputs = inputs.astype(jnp.float32)
    inverse = lax.rsqrt(jnp.mean(wide_inputs * wide_inputs, axis=0) + 1e-05)
    normed_state = (wide_inputs * inverse[None, :]).astype(jnp.bfloat16)
    linear_map = lax.dot_general(
        lax.all_gather(layer_weight_matrix, "dp", axis=0, tiled=True),
        normed_state,
        (((0,), (0,)), ((), ())),
        preferred_element_type=jnp.float32,
    )
    reduced_sum = jnp.dot(
        lowering_factor_matrix, normed_state, preferred_element_type=jnp.float32
    ).astype(jnp.bfloat16)
    linear_map = linear_map + lax.dot_general(
        raising_factor_matrix,
        reduced_sum,
        (((0,), (0,)), ((), ())),
        preferred_element_type=jnp.float32,
    )
    own_inputs = lax.dynamic_slice_in_dim(
        inputs, part_index * feature_width, feature_width, 0
    ).astype(jnp.float32)
    hidden_state = own_inputs + jax.nn.silu(linear_map)
    mask = (own_ids != 0).astype(jnp.float32)
    counts = jnp.sum(mask, axis=1)
    summed = jnp.einsum("dnl,nl->nd", hidden_state.reshape(feature_width, per_shard, length), mask)
    pooled = (summed / counts[:, None]).astype(jnp.bfloat16)
    gathered = lax.all_gather(pooled, ("group", "dp"), axis=0, tiled=True)
    part_scores = lax.dot_general(
        pooled, gathered, (((1,), (1,)), ((), ())), preferred_element_type=jnp.float32
    )
    gathered_wide = gathered.astype(jnp.float32)
    part_norms = jnp.sum(gathered_wide * gathered_wide, axis=1)
    dots, norms = lax.psum((part_scores, part_norms), "mp")
    rnorm_all = lax.rsqrt(norms + 1e-06)
    all_count = gathered.shape[0]
    half_count = all_count // 2
    own_rows = (
        group_index * half_count + shard_index * per_shard + jnp.arange(per_shard, dtype=jnp.int32)
    )
    rnorm_own = jnp.take(rnorm_all, own_rows)
    cosine = dots * rnorm_own[:, None] * rnorm_all[None, :]
    multiplier_factor = logit_sharpness[0]
    scores = multiplier_factor * cosine
    column_ids = jnp.arange(all_count, dtype=jnp.int32)
    keep = column_ids[None, :] != own_rows[:, None]
    pair = (own_rows + half_count) % all_count
    weight = (group_index == 0).astype(jnp.float32)
    neg_cols = half_count + difficult_distractors
    top = jnp.max(jnp.where(keep, scores, -jnp.inf), axis=1)
    safe_scores = jnp.where(keep, scores, top[:, None])
    expd = jnp.where(keep, jnp.exp(safe_scores - top[:, None]), 0.0)
    neg_exp = (
        jnp.exp(jnp.minimum(jnp.take_along_axis(scores, neg_cols, axis=1) - top[:, None], 0.0))
        * weight
    )
    total = jnp.sum(expd, axis=1) + jnp.sum(neg_exp, axis=1)
    pair_score = jnp.take_along_axis(scores, pair[:, None], axis=1)[:, 0]
    losses = top + jnp.log(total) - pair_score
    onehot = (column_ids[None, None, :] == neg_cols[:, :, None]).astype(jnp.float32)
    probs = (expd + jnp.einsum("rk,rkc->rc", neg_exp, onehot)) / total[:, None]
    target = (column_ids[None, :] == pair[:, None]).astype(jnp.float32)
    grad_scores = (probs - target) / all_count
    coeff = (grad_scores * rnorm_own[:, None] * rnorm_all[None, :]).astype(jnp.bfloat16)
    along = jnp.dot(coeff, gathered, preferred_element_type=jnp.float32)
    pooled_wide = pooled.astype(jnp.float32)
    radial = jnp.sum(grad_scores * cosine, axis=1) * rnorm_own * rnorm_own
    embedding_gradient = multiplier_factor * (along - radial[:, None] * pooled_wide)
    token_grad = jnp.einsum("nd,nl->dnl", embedding_gradient / counts[:, None], mask).reshape(
        feature_width, tokens
    )
    sigma = jax.nn.sigmoid(linear_map)
    local = (token_grad * sigma * (1.0 + linear_map * (1.0 - sigma))).astype(jnp.bfloat16)
    up_portion = lax.dot_general(
        reduced_sum, local, (((1,), (1,)), ((), ())), preferred_element_type=jnp.float32
    )
    adapter_up_gradient = lax.psum(up_portion, ("group", "dp"))
    embeddings = (pooled_wide * rnorm_own[:, None]).astype(jnp.bfloat16)[None]
    return (embeddings, losses[None], adapter_up_gradient)


BLOCK_BITS, GROUP_BITS, CHUNK_BITS, LANE_BITS, ROW_BITS = 11, 9, 8, 7, 4
IDS_PER_BLOCK = 1 << BLOCK_BITS
IDS_PER_GROUP = 1 << GROUP_BITS
CHUNK = 1 << CHUNK_BITS
ROWS = 1 << ROW_BITS
LANES = 1 << LANE_BITS
FEATURE_ROWS = 128
TAKEN = 640
FIRST = 1024
NT = (((1,), (1,)), ((), ()))
VMEM_BYTES = 60 * 1024 * 1024


def mm(a, b, dims=(((1,), (0,)), ((), ()))):
    return lax.dot_general(a, b, dims, preferred_element_type=jnp.float32)


def split(x):
    high = x.astype(jnp.bfloat16)
    return high, (x - high.astype(jnp.float32)).astype(jnp.bfloat16)


def iota(shape, dim):
    return lax.broadcasted_iota(jnp.int32, shape, dim)


def quarter_of(dp_index, cores=2):
    return (dp_index % cores) * 2 + dp_index // cores


def split_quarter(i, j, cores=2):
    shard = lax.axis_index("dp")
    core, side_y = lax.rem(shard, cores), lax.div(shard, cores)
    return (core ^ i) * 2 + (side_y ^ j)


def take_lanes(x, lanes):
    numbers = lax.GatherDimensionNumbers(
        offset_dims=(),
        collapsed_slice_dims=(1,),
        start_index_map=(1,),
        operand_batching_dims=(0,),
        start_indices_batching_dims=(0,),
    )
    mode = lax.GatherScatterMode.PROMISE_IN_BOUNDS
    return lax.gather(x, lanes[..., None], numbers, slice_sizes=(1, 1), mode=mode)


def project_kernel(
    ids_ref,
    hard_ref,
    vocab_ref,
    weight_ref,
    lower_ref,
    out00,
    out01,
    out10,
    out11,
    member_ref,
    held,
    weight,
    lower,
    turned,
    picked_turned,
    parts,
    token_ref,
    small,
    ranks,
    squares,
    residual,
    counted,
    bounds,
    held_sems,
    weight_sem,
    lower_sem,
    bounds_sem,
    out_sems,
    base,
):
    texts, length = ids_ref.shape
    features, vocab = vocab_ref.shape
    blocks = vocab // IDS_PER_BLOCK
    groups = vocab // IDS_PER_GROUP
    span = member_ref.shape[0]
    chunks = span // CHUNK
    per_shard, negatives = hard_ref.shape
    width = out00.shape[1]
    outs = (out00, out01, out10, out11)
    shard = lax.axis_index("dp")

    def vocab_copy(b):
        columns = pl.ds(pl.multiple_of(b * IDS_PER_BLOCK, LANES), IDS_PER_BLOCK)
        return pltpu.make_async_copy(vocab_ref.at[:, columns], held.at[b], held_sems.at[b])

    weight_copy = pltpu.make_async_copy(weight_ref, weight, weight_sem)
    lower_copy = pltpu.make_async_copy(
        lower_ref.at[:, pl.ds(pl.multiple_of(shard * features, LANES), features)], lower, lower_sem
    )
    vocab_copy(0).start()
    lower_copy.start()
    weight_copy.start()
    for b in range(1, blocks):
        vocab_copy(b).start()

    ids = ids_ref[...]
    valid = ids != 0
    group_of = jnp.where(valid, lax.shift_right_logical(ids, GROUP_BITS), groups)
    group_rows = counted.shape[0]
    group_id = iota((group_rows, length), 0)
    below = jnp.zeros((group_rows, length), jnp.float32)
    for text in range(texts):
        below += jnp.where(group_of[text : text + 1] < group_id, 1.0, 0.0)
    before = jnp.broadcast_to(jnp.sum(below, axis=1, keepdims=True), (group_rows, length))
    counted[...] = before.astype(jnp.int32)
    bounds_copy = pltpu.make_async_copy(counted, bounds, bounds_sem)
    bounds_copy.start()
    earlier = jnp.where(iota((length, length), 0) < iota((length, length), 1), 1.0, 0.0).astype(
        jnp.bfloat16
    )
    for text in range(texts):
        here = jnp.where(group_of[text : text + 1] == group_id, 1.0, 0.0)
        inside = mm(here.astype(jnp.bfloat16), earlier)
        ranks[pl.ds(text, 1), :] = jnp.sum(here * (inside + before), axis=0, keepdims=True)
        before += jnp.broadcast_to(jnp.sum(here, axis=1, keepdims=True), (group_rows, length))
    text_of = iota((texts, length), 0)
    carried = jnp.where(valid, lax.shift_left(ids, ROW_BITS) + text_of, 0).astype(jnp.float32)
    rank = ranks[...]

    def place(p, carry):
        position = (iota((LANES, length), 0) + (p * LANES + base)).astype(jnp.float32)
        total = jnp.zeros((LANES, length), jnp.float32)
        for text in range(texts):
            total += jnp.where(rank[text : text + 1] == position, carried[text : text + 1], 0.0)
        found = jnp.broadcast_to(jnp.sum(total, axis=1, keepdims=True), (LANES, LANES))
        start = pl.multiple_of(p * LANES, LANES)
        row = found.T[0:1].astype(jnp.int32)
        token = lax.shift_right_logical(row, ROW_BITS)
        token_ref[pl.ds(p, 1), :] = jnp.where(token == 0, -vocab, token)
        found = found.astype(jnp.int32)
        real = (found >= ROWS) & ((found & (ROWS - 1)) == iota((LANES, LANES), 1))
        member_ref[pl.ds(start, LANES), :] = jnp.where(real, 1.0, 0.0).astype(jnp.bfloat16)
        turned[:, pl.ds(start, LANES)] = jnp.zeros((TAKEN, LANES), jnp.bfloat16)
        picked_turned[:, pl.ds(start, LANES)] = jnp.zeros((features - TAKEN, LANES), jnp.bfloat16)
        return carry

    lax.fori_loop(0, span // LANES, place, 0)
    residual[...] = jnp.zeros_like(residual)
    squares[...] = jnp.zeros_like(squares)
    small[...] = jnp.zeros_like(small)
    small[0:per_shard, chunks : chunks + negatives] = hard_ref[...].astype(jnp.float32)
    lower_copy.wait()
    weight_copy.wait()
    bounds_copy.wait()

    def send(start, size):
        rows = pl.ds(start, size)
        for q in range(4):
            pltpu.make_async_copy(parts.at[q, rows], outs[q].at[rows], out_sems.at[q]).start()

    def project(k, carry):
        start = pl.multiple_of(k * CHUNK, CHUNK)
        across = pl.ds(start, CHUNK)
        upright = jnp.concatenate([turned[:, across], picked_turned[:, across]], axis=0)
        x = upright.T
        for q in range(4):
            at = pl.multiple_of(split_quarter(q // 2, q % 2) * width, LANES)
            product = mm(x, weight[:, pl.ds(at, width)])
            parts[q, pl.ds(start, CHUNK), :] = product.astype(jnp.bfloat16)
        send(start, CHUNK)
        reduced = mm(lower[...], upright).astype(jnp.bfloat16)
        for q in range(4):
            parts[q, pl.ds(pl.multiple_of(span + k * ROWS, ROWS), ROWS), :] = reduced
        wide = upright.astype(jnp.float32)
        squares[pl.ds(k, 1), :] = jnp.sum(wide * wide, axis=0, keepdims=True)
        member = member_ref[pl.ds(start, CHUNK), :].astype(jnp.float32).T.astype(jnp.bfloat16)
        residual[...] += mm(member[0:ROWS], x)
        return carry

    def zero(k, carry):
        start = pl.multiple_of(k * CHUNK, CHUNK)
        for q in range(4):
            parts[q, pl.ds(start, CHUNK), :] = jnp.zeros((CHUNK, width), jnp.bfloat16)
            parts[q, pl.ds(pl.multiple_of(span + k * ROWS, ROWS), ROWS), :] = jnp.zeros(
                (ROWS, width), jnp.bfloat16
            )
        send(start, CHUNK)
        return carry

    def within(place):
        return jnp.clip(place - base, 0, span)

    def take(b, done):
        vocab_copy(b).wait()
        for part in range(IDS_PER_BLOCK // IDS_PER_GROUP):
            group = b * (IDS_PER_BLOCK // IDS_PER_GROUP) + part
            first, last = within(bounds[group, 0]), within(bounds[group + 1, 0])
            begin = lax.shift_right_logical(first, LANE_BITS)
            end = lax.shift_right_logical(last + LANES - 1, LANE_BITS)

            def window(p, carry):
                at = pl.ds(pl.multiple_of(p * LANES, LANES), LANES)
                token = token_ref[pl.ds(p, 1), :] - group * IDS_PER_GROUP
                token = jnp.broadcast_to(token, (IDS_PER_GROUP, LANES))
                short = token.astype(jnp.int16)
                picked = jnp.where(
                    short == iota((IDS_PER_GROUP, LANES), 0).astype(jnp.int16), 1.0, 0.0
                ).astype(jnp.bfloat16)
                columns = pl.ds(part * IDS_PER_GROUP, IDS_PER_GROUP)
                found = mm(held[b, TAKEN:features, columns], picked)
                lane = (token[0:FEATURE_ROWS] & (LANES - 1)).astype(jnp.int16)
                tile = lax.shift_right_arithmetic(token[0:FEATURE_ROWS], LANE_BITS)
                tile = tile.astype(jnp.int16)
                for f in range(TAKEN // FEATURE_ROWS):
                    rows = pl.ds(f * FEATURE_ROWS, FEATURE_ROWS)
                    total = turned[rows, at]
                    for j in range(IDS_PER_GROUP // LANES):
                        columns = pl.ds(part * IDS_PER_GROUP + j * LANES, LANES)
                        total = jnp.where(tile == j, take_lanes(held[b, rows, columns], lane), total)
                    turned[rows, at] = total
                picked_turned[:, at] += found.astype(jnp.bfloat16)
                return carry

            lax.fori_loop(begin, jnp.where(last > first, end, begin), window, 0)
        full = lax.shift_right_logical(last, CHUNK_BITS)
        lax.fori_loop(done, full, project, 0)
        return full

    done = lax.fori_loop(0, blocks, take, 0)
    used = lax.shift_right_logical(within(bounds[groups, 0]) + CHUNK - 1, CHUNK_BITS)
    lax.fori_loop(done, used, project, 0)
    lax.fori_loop(used, chunks, zero, 0)

    hard = small[...].T[0:ROWS]
    lane = iota((ROWS, width), 1)
    misc = jnp.concatenate([squares[...], jnp.zeros((ROWS - squares.shape[0], width), jnp.float32)])
    for i in range(per_shard):
        misc += jnp.where(lane == shard * per_shard + i, hard[:, i : i + 1], 0.0)
    mine = lax.axis_index("mp") == shard
    for q in range(4):
        start = pl.multiple_of(split_quarter(q // 2, q % 2) * width, LANES)
        part = jnp.where(mine, residual[:, pl.ds(start, width)], 0.0)
        parts[q, pl.ds(span + chunks * ROWS, ROWS), :] = misc.astype(jnp.bfloat16)
        parts[q, pl.ds(span + (chunks + 1) * ROWS, ROWS), :] = part.astype(jnp.bfloat16)
    send(span, (chunks + 2) * ROWS)
    for q in range(4):
        pltpu.make_async_copy(parts.at[q], outs[q], out_sems.at[q]).wait()


def pool_kernel(
    ids_ref,
    own_ref,
    core_ref,
    far_ref,
    member_ref,
    own_rest,
    core_rest,
    far_rest,
    member_rest,
    raise_ref,
    pooled_ref,
    slope_ref,
    reduced_ref,
    misc_ref,
    raised,
    total,
    model_width,
):
    texts, length = ids_ref.shape
    width = own_ref.shape[1]
    quarter = quarter_of(lax.axis_index("dp"))
    raised[...] = jnp.zeros_like(raised)
    raised[0:ROWS, :] = raise_ref[:, pl.ds(pl.multiple_of(quarter * width, LANES), width)]
    total[...] = jnp.zeros_like(total)

    def add(refs, member_ref, base):
        span = member_ref.shape[0]
        chunks = span // CHUNK

        def summed(start, size):
            return sum(ref[pl.ds(start, size), :].astype(jnp.float32) for ref in refs)

        misc = summed(span + chunks * ROWS, ROWS)
        if base == 0:
            misc_ref[...] = misc
        inverse = lax.rsqrt(misc / model_width + 1e-05)
        for k in range(chunks):
            at = base + k * CHUNK
            scale = inverse[k : k + 1]
            reduced = (summed(span + k * ROWS, ROWS) * scale).astype(jnp.bfloat16)
            reduced_ref[:, at : at + CHUNK] = reduced
            stacked = jnp.concatenate(
                [reduced.astype(jnp.float32), jnp.broadcast_to(scale, (LANES - ROWS, CHUNK))]
            )
            turned = stacked.T
            low = turned.astype(jnp.bfloat16)
            linear = summed(k * CHUNK, CHUNK) * turned[:, ROWS : ROWS + 1] + mm(low, raised[...])
            sigma = 1.0 / (1.0 + jnp.exp(-linear))
            slope_ref[pl.ds(at, CHUNK), :] = sigma * (1.0 + linear * (1.0 - sigma))
            member = member_ref[pl.ds(k * CHUNK, CHUNK), :].astype(jnp.float32).T
            member = member[0:ROWS].astype(jnp.bfloat16)
            high, rest = split(linear * sigma)
            total[...] += mm(member, high) + mm(member, rest)
        total[...] += summed(span + (chunks + 1) * ROWS, ROWS)

    add((own_ref, core_ref, far_ref), member_ref, 0)
    real = (ids_ref[...] != 0).astype(jnp.float32)

    @pl.when(jnp.sum(real) > member_ref.shape[0])
    def _():
        add((own_rest, core_rest, far_rest), member_rest, member_ref.shape[0])

    counts = jnp.sum(real, axis=1, keepdims=True)
    pooled = total[0:texts] / counts
    pooled = jnp.concatenate([pooled, jnp.zeros((ROWS - texts, width), jnp.float32)])
    pooled_ref[...] = pooled.astype(jnp.bfloat16)


def both_sides(near, far):
    queries = lax.axis_index("group") == 0
    return jnp.concatenate([jnp.where(queries, near, far), jnp.where(queries, far, near)], axis=0)


def dots_kernel(near_ref, far_ref, packed_ref):
    near = near_ref[...]
    block = both_sides(near, far_ref[...])
    dots = mm(block, block, NT)
    rows = 2 * ROWS
    packed_ref[...] = jnp.zeros_like(packed_ref)
    packed_ref[0:rows, 0:rows] = dots
    for part in range(near.shape[1] // LANES):
        start = rows + part * ROWS
        packed_ref[start : start + ROWS, :] = near[:, part * LANES : (part + 1) * LANES].astype(
            jnp.float32
        )


def score_kernel(
    ids_ref,
    near_ref,
    far_ref,
    packed0,
    packed1,
    packed2,
    packed3,
    dots0,
    dots1,
    dots2,
    dots3,
    misc_ref,
    slope_ref,
    reduced_ref,
    member_ref,
    member_rest,
    sharp_ref,
    embed_ref,
    loss_ref,
    up_ref,
    negatives,
):
    texts, length = ids_ref.shape
    chunks = member_ref.shape[0] // CHUNK
    rows = 2 * ROWS
    width = near_ref.shape[1]
    per_shard = loss_ref.shape[1]
    group, shard = lax.axis_index("group"), lax.axis_index("dp")
    dots = ((dots0[...] + dots1[...]) + (dots2[...] + dots3[...]))[:, 0:rows]
    down, across = iota((rows, rows), 0), iota((rows, rows), 1)
    same = down == across
    real = (lax.rem(down, ROWS) < texts) & (lax.rem(across, ROWS) < texts)
    diagonal = jnp.where(same, dots, 0.0)
    rnorm_row = lax.rsqrt(jnp.sum(diagonal, axis=0, keepdims=True) + 1e-06)
    rnorm_col = lax.rsqrt(jnp.sum(diagonal, axis=1, keepdims=True) + 1e-06)
    sharpness = sharp_ref[0]
    cosine = dots * rnorm_col * rnorm_row
    scores = sharpness * cosine
    keep = real & ~same
    top = jnp.max(jnp.where(keep, scores, -jnp.inf), axis=0, keepdims=True)
    top = jnp.where(lax.rem(across[0:1], ROWS) < texts, top, 0.0)
    powers = jnp.exp(jnp.where(real, jnp.minimum(scores - top, 0.0), 0.0))
    hard = misc_ref[chunks : chunks + negatives, 0:rows].astype(jnp.int32) + ROWS
    times = jnp.zeros((rows, rows), jnp.float32)
    for k in range(negatives):
        times += jnp.where(hard[k : k + 1] == down, 1.0, 0.0)
    times = jnp.where(across < texts, times, 0.0)
    weights = (jnp.where(keep, 1.0, 0.0) + jnp.where(real, times, 0.0)) * powers
    total = jnp.sum(weights, axis=0, keepdims=True)
    total = jnp.where(lax.rem(across[0:1], ROWS) < texts, total, 1.0)
    pair = (down == lax.rem(across + ROWS, rows)) & real
    pair_score = jnp.sum(jnp.where(pair, scores, 0.0), axis=0, keepdims=True)
    losses = top + jnp.log(total) - pair_score
    grad_scores = (weights / total - jnp.where(pair, 1.0, 0.0)) / (2 * texts)
    coeff = (grad_scores * rnorm_col * rnorm_row).astype(jnp.bfloat16)
    radial = jnp.sum(grad_scores * cosine, axis=0, keepdims=True) * rnorm_row * rnorm_row

    first = shard * per_shard
    loss_col = jnp.sum(jnp.where(same, losses, 0.0), axis=1, keepdims=True)
    at = (iota((rows, LANES), 0) == group * ROWS + first + iota((rows, LANES), 1)) & (
        iota((rows, LANES), 1) < per_shard
    )
    loss_ref[...] = jnp.sum(jnp.where(at, loss_col, 0.0), axis=0, keepdims=True)[:, 0:per_shard]

    mine = both_sides(near_ref[...], far_ref[...])
    along = mm(coeff.astype(jnp.float32).T.astype(jnp.bfloat16), mine)
    radial_col = jnp.sum(jnp.where(same, radial, 0.0), axis=1, keepdims=True)
    grad = sharpness * (along - radial_col * mine.astype(jnp.float32))
    grad = jnp.where(group == 0, grad[0:ROWS], grad[ROWS:rows])
    real_tokens = (ids_ref[...] != 0).astype(jnp.float32)
    counts = jnp.sum(real_tokens, axis=1, keepdims=True)
    grad = grad[0:texts] / counts
    grad = jnp.concatenate([grad, jnp.zeros((LANES - texts, width), jnp.float32)])
    high, rest = split(grad)

    def update(member_ref, base):
        total = jnp.zeros((ROWS, width), jnp.float32)
        for k in range(member_ref.shape[0] // CHUNK):
            at = base + k * CHUNK
            member = member_ref[pl.ds(k * CHUNK, CHUNK), :]
            token_grad = mm(member, high) + mm(member, rest)
            local = (token_grad * slope_ref[pl.ds(at, CHUNK), :]).astype(jnp.bfloat16)
            total += mm(reduced_ref[:, at : at + CHUNK], local)
        return total

    first_part = update(member_ref, 0)
    up_ref[...] = first_part

    @pl.when(jnp.sum(real_tokens) > member_ref.shape[0])
    def _():
        up_ref[...] = first_part + update(member_rest, member_ref.shape[0])

    rnorm_own = jnp.where(group == 0, rnorm_col[0:ROWS], rnorm_col[ROWS:rows])
    chosen = iota((ROWS, ROWS), 1) == iota((ROWS, ROWS), 0) + first
    chosen = jnp.where(chosen & (iota((ROWS, ROWS), 0) < per_shard), 1.0, 0.0).astype(jnp.bfloat16)
    for o, packed in enumerate((packed0, packed1, packed2, packed3)):
        halves = [
            packed[rows + part * ROWS : rows + (part + 1) * ROWS, :]
            for part in range(width // LANES)
        ]
        block = jnp.concatenate(halves, axis=1) * rnorm_own
        picked = mm(chosen, block.astype(jnp.bfloat16)).astype(jnp.bfloat16)
        at = pl.multiple_of(quarter_of(shard ^ o) * width, LANES)
        embed_ref[0, :, pl.ds(at, width)] = picked[0:per_shard]


def any_spec():
    return pl.BlockSpec(memory_space=pl.ANY)


def vmem_spec():
    return pl.BlockSpec(memory_space=pltpu.VMEM)


def smem_spec():
    return pl.BlockSpec(memory_space=pltpu.SMEM)


def exchange(x, axis, size):
    steps = [[(i, i ^ o) for i in range(size)] for o in range(1, size)]
    return [x] + [lax.ppermute(x, axis, step) for step in steps]


def split_body(
    query_passage_words,
    difficult_distractors,
    vocabulary_vectors,
    layer_weight_matrix,
    lowering_factor_matrix,
    raising_factor_matrix,
    logit_sharpness,
):
    shards, parts = lax.axis_size("dp"), lax.axis_size("mp")
    ids = query_passage_words[0]
    texts, length = ids.shape
    tokens = texts * length
    features, vocab = vocabulary_vectors.shape
    blocks = vocab // IDS_PER_BLOCK
    group_rows = 8 * pl.cdiv(vocab // IDS_PER_GROUP + 1, 8)
    per_shard, negatives = difficult_distractors.shape
    rank = lowering_factor_matrix.shape[0]
    part_width = layer_weight_matrix.shape[1]
    width = part_width // shards
    params = pltpu.CompilerParams(vmem_limit_bytes=VMEM_BYTES)
    other_core = [(d, d ^ 1) for d in range(shards)]
    other_y = [(d, d ^ 2) for d in range(shards)]

    def project(base, span):
        rows = span + (span // CHUNK + 2) * ROWS
        own0, own1, away0, away1, member = pl.pallas_call(
            functools.partial(project_kernel, base=base),
            out_shape=[jax.ShapeDtypeStruct((rows, width), jnp.bfloat16)] * 4
            + [jax.ShapeDtypeStruct((span, LANES), jnp.bfloat16)],
            in_specs=[vmem_spec()] * 2 + [any_spec()] * 3,
            out_specs=[any_spec()] * 4 + [vmem_spec()],
            scratch_shapes=[
                pltpu.VMEM((blocks, features, IDS_PER_BLOCK), jnp.bfloat16),
                pltpu.VMEM((features, part_width), jnp.bfloat16),
                pltpu.VMEM((rank, features), jnp.bfloat16),
                pltpu.VMEM((TAKEN, span), jnp.bfloat16),
                pltpu.VMEM((features - TAKEN, span), jnp.bfloat16),
                pltpu.VMEM((4, rows, width), jnp.bfloat16),
                pltpu.VMEM((8 * pl.cdiv(span // LANES, 8), LANES), jnp.int32),
                pltpu.VMEM((LANES, LANES), jnp.float32),
                pltpu.VMEM((texts, length), jnp.float32),
                pltpu.VMEM((8, width), jnp.float32),
                pltpu.VMEM((ROWS, features), jnp.float32),
                pltpu.VMEM((group_rows, length), jnp.int32),
                pltpu.SMEM((group_rows, length), jnp.int32),
                pltpu.SemaphoreType.DMA((blocks,)),
                pltpu.SemaphoreType.DMA,
                pltpu.SemaphoreType.DMA,
                pltpu.SemaphoreType.DMA,
                pltpu.SemaphoreType.DMA((4,)),
            ],
            compiler_params=params,
            name="project",
        )(
            ids,
            difficult_distractors,
            vocabulary_vectors,
            layer_weight_matrix,
            lowering_factor_matrix,
        )
        core1 = lax.ppermute(away1, "dp", other_core)
        core0 = lax.ppermute(away0, "dp", other_core)
        chip1 = (own1.astype(jnp.float32) + core1.astype(jnp.float32)).astype(jnp.bfloat16)
        far = lax.ppermute(chip1, "dp", other_y)
        return own0, core0, far, member

    first = project(0, FIRST)
    many = jnp.sum((ids != 0).astype(jnp.int32)) > FIRST
    left = tokens - FIRST
    shapes = jax.eval_shape(lambda: project(FIRST, left))
    rest = lax.cond(
        many,
        lambda: project(FIRST, left),
        lambda: tuple(jnp.zeros(x.shape, x.dtype) for x in shapes),
    )
    pooled, slope, reduced, misc = pl.pallas_call(
        functools.partial(pool_kernel, model_width=float(features * shards)),
        out_shape=[
            jax.ShapeDtypeStruct((ROWS, width), jnp.bfloat16),
            jax.ShapeDtypeStruct((tokens, width), jnp.float32),
            jax.ShapeDtypeStruct((ROWS, tokens), jnp.bfloat16),
            jax.ShapeDtypeStruct((ROWS, width), jnp.float32),
        ],
        in_specs=[vmem_spec()] * 10,
        out_specs=[vmem_spec()] * 4,
        scratch_shapes=[
            pltpu.VMEM((LANES, width), jnp.bfloat16),
            pltpu.VMEM((ROWS, width), jnp.float32),
        ],
        compiler_params=params,
        name="pool",
    )(ids, *first, *rest, raising_factor_matrix)
    member, member_rest = first[3], rest[3]
    far_side = lax.ppermute(pooled, "group", [(0, 1), (1, 0)])
    rows = 2 * ROWS
    packed = pl.pallas_call(
        dots_kernel,
        out_shape=jax.ShapeDtypeStruct((rows + width // LANES * ROWS, LANES), jnp.float32),
        in_specs=[vmem_spec()] * 2,
        out_specs=vmem_spec(),
        compiler_params=params,
        name="dots",
    )(pooled, far_side)
    packed = exchange(packed, "dp", shards)
    dots = [x[0:rows] for x in packed]
    dots = exchange((dots[0] + dots[1]) + (dots[2] + dots[3]), "mp", parts)
    embeddings, losses, update = pl.pallas_call(
        functools.partial(score_kernel, negatives=negatives),
        out_shape=[
            jax.ShapeDtypeStruct((1, per_shard, part_width), jnp.bfloat16),
            jax.ShapeDtypeStruct((1, per_shard), jnp.float32),
            jax.ShapeDtypeStruct((ROWS, width), jnp.float32),
        ],
        in_specs=[vmem_spec()] * 16 + [smem_spec()],
        out_specs=[vmem_spec()] * 3,
        compiler_params=params,
        name="score",
    )(
        ids,
        pooled,
        far_side,
        *packed,
        *dots,
        misc,
        slope,
        reduced,
        member,
        member_rest,
        logit_sharpness,
    )
    update = update + lax.ppermute(update, "group", [(0, 1), (1, 0)])
    updates = exchange(update, "dp", shards)
    shard = lax.axis_index("dp")
    columns = [lax.select_n(shard ^ quarter_of(q), *updates) for q in range(shards)]
    return (embeddings, losses, jnp.concatenate(columns, axis=1))


def body(words, hard, vocabulary, weight, lowering, raising, sharpness):
    shards, parts = lax.axis_size("dp"), lax.axis_size("mp")
    texts, length = words.shape[1:]
    features, vocab = vocabulary.shape
    negatives = hard.shape[1]
    square = shards == 4 and features == weight.shape[1] and parts == shards
    small = texts <= ROWS - 2 and length == LANES and FIRST < texts * length <= 2048
    even = (texts * length) % CHUNK == 0 and vocab % IDS_PER_BLOCK == 0
    fits = features * vocab <= 2**24 and features % (4 * LANES) == 0
    spare = FIRST // CHUNK + negatives <= ROWS and lowering.shape[0] == ROWS
    fast = square and small and even and fits and spare and lax.axis_size("group") == 2
    chosen = split_body if fast else general_body
    return chosen(words, hard, vocabulary, weight, lowering, raising, sharpness)


def solution(mesh):
    in_specs = (
        P("group", None, None),
        P("dp", None),
        P("dp", None),
        P("dp", "mp"),
        P(),
        P(None, "mp"),
        P(),
    )
    out_specs = (P("group", "dp", "mp"), P("group", "dp"), P(None, "mp"))
    return jax.shard_map(body, mesh=mesh, in_specs=in_specs, out_specs=out_specs, check_vma=False)
```

```python
import functools

import jax
import jax.numpy as jnp
from jax import lax
from jax.experimental import pallas as pl
from jax.experimental.pallas import tpu as pltpu
from jax.sharding import PartitionSpec as P


def general_body(
    query_passage_words,
    difficult_distractors,
    vocabulary_vectors,
    layer_weight_matrix,
    lowering_factor_matrix,
    raising_factor_matrix,
    logit_sharpness,
):
    group_index = lax.axis_index("group")
    shard_index = lax.axis_index("dp")
    part_index = lax.axis_index("mp")
    shard_count = lax.axis_size("dp")
    side_ids = query_passage_words[0]
    text_count = side_ids.shape[0]
    length = side_ids.shape[1]
    per_shard = text_count // shard_count
    own_ids = lax.dynamic_slice_in_dim(side_ids, shard_index * per_shard, per_shard, 0)
    columns = jnp.take(vocabulary_vectors, side_ids.reshape(-1), axis=1)
    inputs = lax.all_to_all(columns, "dp", split_axis=1, concat_axis=0, tiled=True)
    tokens = inputs.shape[1]
    feature_width = raising_factor_matrix.shape[1]
    wide_inputs = inputs.astype(jnp.float32)
    inverse = lax.rsqrt(jnp.mean(wide_inputs * wide_inputs, axis=0) + 1e-05)
    normed_state = (wide_inputs * inverse[None, :]).astype(jnp.bfloat16)
    linear_map = lax.dot_general(
        lax.all_gather(layer_weight_matrix, "dp", axis=0, tiled=True),
        normed_state,
        (((0,), (0,)), ((), ())),
        preferred_element_type=jnp.float32,
    )
    reduced_sum = jnp.dot(
        lowering_factor_matrix, normed_state, preferred_element_type=jnp.float32
    ).astype(jnp.bfloat16)
    linear_map = linear_map + lax.dot_general(
        raising_factor_matrix,
        reduced_sum,
        (((0,), (0,)), ((), ())),
        preferred_element_type=jnp.float32,
    )
    own_inputs = lax.dynamic_slice_in_dim(
        inputs, part_index * feature_width, feature_width, 0
    ).astype(jnp.float32)
    hidden_state = own_inputs + jax.nn.silu(linear_map)
    mask = (own_ids != 0).astype(jnp.float32)
    counts = jnp.sum(mask, axis=1)
    summed = jnp.einsum("dnl,nl->nd", hidden_state.reshape(feature_width, per_shard, length), mask)
    pooled = (summed / counts[:, None]).astype(jnp.bfloat16)
    gathered = lax.all_gather(pooled, ("group", "dp"), axis=0, tiled=True)
    part_scores = lax.dot_general(
        pooled, gathered, (((1,), (1,)), ((), ())), preferred_element_type=jnp.float32
    )
    gathered_wide = gathered.astype(jnp.float32)
    part_norms = jnp.sum(gathered_wide * gathered_wide, axis=1)
    dots, norms = lax.psum((part_scores, part_norms), "mp")
    rnorm_all = lax.rsqrt(norms + 1e-06)
    all_count = gathered.shape[0]
    half_count = all_count // 2
    own_rows = (
        group_index * half_count + shard_index * per_shard + jnp.arange(per_shard, dtype=jnp.int32)
    )
    rnorm_own = jnp.take(rnorm_all, own_rows)
    cosine = dots * rnorm_own[:, None] * rnorm_all[None, :]
    multiplier_factor = logit_sharpness[0]
    scores = multiplier_factor * cosine
    column_ids = jnp.arange(all_count, dtype=jnp.int32)
    keep = column_ids[None, :] != own_rows[:, None]
    pair = (own_rows + half_count) % all_count
    weight = (group_index == 0).astype(jnp.float32)
    neg_cols = half_count + difficult_distractors
    top = jnp.max(jnp.where(keep, scores, -jnp.inf), axis=1)
    safe_scores = jnp.where(keep, scores, top[:, None])
    expd = jnp.where(keep, jnp.exp(safe_scores - top[:, None]), 0.0)
    neg_exp = (
        jnp.exp(jnp.minimum(jnp.take_along_axis(scores, neg_cols, axis=1) - top[:, None], 0.0))
        * weight
    )
    total = jnp.sum(expd, axis=1) + jnp.sum(neg_exp, axis=1)
    pair_score = jnp.take_along_axis(scores, pair[:, None], axis=1)[:, 0]
    losses = top + jnp.log(total) - pair_score
    onehot = (column_ids[None, None, :] == neg_cols[:, :, None]).astype(jnp.float32)
    probs = (expd + jnp.einsum("rk,rkc->rc", neg_exp, onehot)) / total[:, None]
    target = (column_ids[None, :] == pair[:, None]).astype(jnp.float32)
    grad_scores = (probs - target) / all_count
    coeff = (grad_scores * rnorm_own[:, None] * rnorm_all[None, :]).astype(jnp.bfloat16)
    along = jnp.dot(coeff, gathered, preferred_element_type=jnp.float32)
    pooled_wide = pooled.astype(jnp.float32)
    radial = jnp.sum(grad_scores * cosine, axis=1) * rnorm_own * rnorm_own
    embedding_gradient = multiplier_factor * (along - radial[:, None] * pooled_wide)
    token_grad = jnp.einsum("nd,nl->dnl", embedding_gradient / counts[:, None], mask).reshape(
        feature_width, tokens
    )
    sigma = jax.nn.sigmoid(linear_map)
    local = (token_grad * sigma * (1.0 + linear_map * (1.0 - sigma))).astype(jnp.bfloat16)
    up_portion = lax.dot_general(
        reduced_sum, local, (((1,), (1,)), ((), ())), preferred_element_type=jnp.float32
    )
    adapter_up_gradient = lax.psum(up_portion, ("group", "dp"))
    embeddings = (pooled_wide * rnorm_own[:, None]).astype(jnp.bfloat16)[None]
    return (embeddings, losses[None], adapter_up_gradient)


BLOCK_BITS, GROUP_BITS, LANE_BITS, ROW_BITS = 10, 8, 7, 4
IDS_PER_BLOCK = 1 << BLOCK_BITS
IDS_PER_GROUP = 1 << GROUP_BITS
CHUNK = 384
STRIPE = 256
ROWS = 1 << ROW_BITS
LANES = 1 << LANE_BITS
FEATURE_ROWS = 128
FIRST = 1152
NT = (((1,), (1,)), ((), ()))
VMEM_BYTES = 60 * 1024 * 1024


def mm(a, b, dims=(((1,), (0,)), ((), ()))):
    return lax.dot_general(a, b, dims, preferred_element_type=jnp.float32)


def split(x):
    high = x.astype(jnp.bfloat16)
    return high, (x - high.astype(jnp.float32)).astype(jnp.bfloat16)


def iota(shape, dim):
    return lax.broadcasted_iota(jnp.int32, shape, dim)


def quarter_of(dp_index, cores=2):
    return (dp_index % cores) * 2 + dp_index // cores


def split_quarter(i, j, cores=2):
    shard = lax.axis_index("dp")
    core, side_y = lax.rem(shard, cores), lax.div(shard, cores)
    return (core ^ i) * 2 + (side_y ^ j)


def take_lanes(x, lanes):
    numbers = lax.GatherDimensionNumbers(
        offset_dims=(),
        collapsed_slice_dims=(1,),
        start_index_map=(1,),
        operand_batching_dims=(0,),
        start_indices_batching_dims=(0,),
    )
    mode = lax.GatherScatterMode.PROMISE_IN_BOUNDS
    return lax.gather(x, lanes[..., None], numbers, slice_sizes=(1, 1), mode=mode)


def project_kernel(
    ids_ref,
    hard_ref,
    vocab_ref,
    weight_ref,
    lower_ref,
    out00,
    out01,
    out10,
    out11,
    member_ref,
    held,
    weight,
    lower,
    turned,
    parts,
    token_ref,
    small,
    ranks,
    statistics,
    residual,
    counted,
    bounds,
    held_sems,
    weight_sem,
    lower_sem,
    bounds_sem,
    out_sems,
    base,
):
    texts, length = ids_ref.shape
    features, vocab = vocab_ref.shape
    blocks = vocab // IDS_PER_BLOCK
    groups = vocab // IDS_PER_GROUP
    span = member_ref.shape[0]
    chunks = span // CHUNK
    stripes = pl.cdiv(span, STRIPE)
    per_shard, negatives = hard_ref.shape
    width = out00.shape[1]
    outs = (out00, out01, out10, out11)
    shard = lax.axis_index("dp")

    def vocab_copy(b):
        columns = pl.ds(pl.multiple_of(b * IDS_PER_BLOCK, LANES), IDS_PER_BLOCK)
        return pltpu.make_async_copy(vocab_ref.at[:, columns], held.at[b], held_sems.at[b])

    weight_copy = pltpu.make_async_copy(weight_ref, weight, weight_sem)
    lower_copy = pltpu.make_async_copy(
        lower_ref.at[:, pl.ds(pl.multiple_of(shard * features, LANES), features)], lower, lower_sem
    )
    vocab_copy(0).start()
    lower_copy.start()
    weight_copy.start()
    for b in range(1, blocks):
        vocab_copy(b).start()

    ids = ids_ref[...]
    valid = ids != 0
    group_of = jnp.where(valid, lax.shift_right_logical(ids, GROUP_BITS), groups)
    group_rows = counted.shape[0]
    group_id = iota((group_rows, length), 0)
    below = jnp.zeros((group_rows, length), jnp.float32)
    for text in range(texts):
        below += jnp.where(group_of[text : text + 1] < group_id, 1.0, 0.0)
    before = jnp.broadcast_to(jnp.sum(below, axis=1, keepdims=True), (group_rows, length))
    counted[...] = before.astype(jnp.int32)
    bounds_copy = pltpu.make_async_copy(counted, bounds, bounds_sem)
    bounds_copy.start()
    earlier = jnp.where(iota((length, length), 0) < iota((length, length), 1), 1.0, 0.0).astype(
        jnp.bfloat16
    )
    for text in range(texts):
        here = jnp.where(group_of[text : text + 1] == group_id, 1.0, 0.0)
        inside = mm(here.astype(jnp.bfloat16), earlier)
        ranks[pl.ds(text, 1), :] = jnp.sum(here * (inside + before), axis=0, keepdims=True)
        before += jnp.broadcast_to(jnp.sum(here, axis=1, keepdims=True), (group_rows, length))
    text_of = iota((texts, length), 0)
    carried = jnp.where(valid, lax.shift_left(ids, ROW_BITS) + text_of, 0).astype(jnp.float32)
    rank = ranks[...]

    def place(p, carry):
        position = (iota((LANES, length), 0) + (p * LANES + base)).astype(jnp.float32)
        total = jnp.zeros((LANES, length), jnp.float32)
        for text in range(texts):
            total += jnp.where(rank[text : text + 1] == position, carried[text : text + 1], 0.0)
        found = jnp.broadcast_to(jnp.sum(total, axis=1, keepdims=True), (LANES, LANES))
        start = pl.multiple_of(p * LANES, LANES)
        row = found.T[0:1].astype(jnp.int32)
        token = lax.shift_right_logical(row, ROW_BITS)
        token_ref[pl.ds(p, 1), :] = jnp.where(token == 0, -vocab, token)
        found = found.astype(jnp.int32)
        real = (found >= ROWS) & ((found & (ROWS - 1)) == iota((LANES, LANES), 1))
        member_ref[pl.ds(start, LANES), :] = jnp.where(real, 1.0, 0.0).astype(jnp.bfloat16)
        turned[:, pl.ds(start, LANES)] = jnp.zeros((features, LANES), jnp.bfloat16)
        return carry

    lax.fori_loop(0, span // LANES, place, 0)
    residual[...] = jnp.zeros_like(residual)
    statistics[...] = jnp.zeros_like(statistics)
    small[...] = jnp.zeros_like(small)
    small[0:per_shard, stripes : stripes + negatives] = hard_ref[...].astype(jnp.float32)
    lower_copy.wait()
    weight_copy.wait()
    bounds_copy.wait()

    def send(start, size):
        rows = pl.ds(start, size)
        for q in range(4):
            pltpu.make_async_copy(parts.at[q, rows], outs[q].at[rows], out_sems.at[q]).start()

    def project(k, carry):
        start = pl.multiple_of(k * CHUNK, LANES)
        across = pl.ds(start, CHUNK)
        upright = turned[:, across]
        x = upright.T
        for q in range(4):
            at = pl.multiple_of(split_quarter(q // 2, q % 2) * width, LANES)
            product = mm(x, weight[:, pl.ds(at, width)])
            parts[q, across, :] = product.astype(jnp.bfloat16)
        send(start, CHUNK)
        wide = upright.astype(jnp.float32)
        statistics[0:ROWS, across] = mm(lower[...], upright)
        statistics[ROWS : ROWS + 1, across] = jnp.sum(wide * wide, axis=0, keepdims=True)
        member = member_ref[across, :].astype(jnp.float32).T.astype(jnp.bfloat16)
        residual[...] += mm(member[0:ROWS], x)
        return carry

    def zero(k, carry):
        start = pl.multiple_of(k * CHUNK, LANES)
        for q in range(4):
            parts[q, pl.ds(start, CHUNK), :] = jnp.zeros((CHUNK, width), jnp.bfloat16)
        send(start, CHUNK)
        return carry

    def within(place):
        return jnp.clip(place - base, 0, span)

    def take(b, done):
        vocab_copy(b).wait()
        for part in range(IDS_PER_BLOCK // IDS_PER_GROUP):
            group = b * (IDS_PER_BLOCK // IDS_PER_GROUP) + part
            first, last = within(bounds[group, 0]), within(bounds[group + 1, 0])
            begin = lax.shift_right_logical(first, LANE_BITS)
            end = lax.shift_right_logical(last + LANES - 1, LANE_BITS)

            def window(p, carry):
                at = pl.ds(pl.multiple_of(p * LANES, LANES), LANES)
                token = token_ref[pl.ds(p, 1), :] - group * IDS_PER_GROUP
                token = jnp.broadcast_to(token, (FEATURE_ROWS, LANES))
                lane = token & (LANES - 1)
                tile = lax.shift_right_arithmetic(token, LANE_BITS)
                for f in range(features // FEATURE_ROWS):
                    rows = pl.ds(f * FEATURE_ROWS, FEATURE_ROWS)
                    total = turned[rows, at].astype(jnp.float32)
                    for j in range(IDS_PER_GROUP // LANES):
                        columns = pl.ds(part * IDS_PER_GROUP + j * LANES, LANES)
                        found = take_lanes(held[b, rows, columns].astype(jnp.float32), lane)
                        total = jnp.where(tile == j, found, total)
                    turned[rows, at] = total.astype(jnp.bfloat16)
                return carry

            lax.fori_loop(begin, jnp.where(last > first, end, begin), window, 0)
        full = lax.div(last, CHUNK)
        lax.fori_loop(done, full, project, 0)
        return full

    done = lax.fori_loop(0, blocks, take, 0)
    used = lax.div(within(bounds[groups, 0]) + CHUNK - 1, CHUNK)
    lax.fori_loop(done, used, project, 0)
    lax.fori_loop(used, chunks, zero, 0)

    hard = small[...].T[0:ROWS]
    lane = iota((ROWS, width), 1)
    misc = jnp.zeros((ROWS, width), jnp.float32)
    for stripe in range(stripes):
        across = pl.ds(stripe * STRIPE, STRIPE)
        for q in range(4):
            parts[q, pl.ds(span + stripe * ROWS, ROWS), :] = statistics[0:ROWS, across].astype(
                jnp.bfloat16
            )
        squares = jnp.broadcast_to(statistics[ROWS : ROWS + 1, across], (ROWS, STRIPE))
        misc = jnp.where(iota((ROWS, width), 0) == stripe, squares, misc)
    for i in range(per_shard):
        misc += jnp.where(lane == shard * per_shard + i, hard[:, i : i + 1], 0.0)
    mine = lax.axis_index("mp") == shard
    for q in range(4):
        start = pl.multiple_of(split_quarter(q // 2, q % 2) * width, LANES)
        part = jnp.where(mine, residual[:, pl.ds(start, width)], 0.0)
        parts[q, pl.ds(span + stripes * ROWS, ROWS), :] = misc.astype(jnp.bfloat16)
        parts[q, pl.ds(span + (stripes + 1) * ROWS, ROWS), :] = part.astype(jnp.bfloat16)
    send(span, (stripes + 2) * ROWS)
    for q in range(4):
        pltpu.make_async_copy(parts.at[q], outs[q], out_sems.at[q]).wait()


def pool_kernel(
    ids_ref,
    own_ref,
    core_ref,
    far_ref,
    member_ref,
    own_rest,
    core_rest,
    far_rest,
    member_rest,
    raise_ref,
    pooled_ref,
    slope_ref,
    reduced_ref,
    misc_ref,
    raised,
    total,
    model_width,
):
    texts, length = ids_ref.shape
    width = own_ref.shape[1]
    quarter = quarter_of(lax.axis_index("dp"))
    raised[...] = jnp.zeros_like(raised)
    raised[0:ROWS, :] = raise_ref[:, pl.ds(pl.multiple_of(quarter * width, LANES), width)]
    total[...] = jnp.zeros_like(total)

    def add(refs, member_ref, base):
        span = member_ref.shape[0]
        stripes = pl.cdiv(span, STRIPE)

        def summed(start, size):
            return sum(ref[pl.ds(start, size), :].astype(jnp.float32) for ref in refs)

        misc = summed(span + stripes * ROWS, ROWS)
        if base == 0:
            misc_ref[...] = misc
        inverse = lax.rsqrt(misc / model_width + 1e-05)
        for k in range(stripes):
            at = base + k * STRIPE
            size = min(STRIPE, span - k * STRIPE)
            scale = inverse[k : k + 1]
            reduced = (summed(span + k * ROWS, ROWS) * scale).astype(jnp.bfloat16)
            reduced_ref[:, at : at + size] = reduced[:, 0:size]
            stacked = jnp.concatenate(
                [reduced.astype(jnp.float32), jnp.broadcast_to(scale, (LANES - ROWS, STRIPE))]
            )
            turned = stacked[:, 0:size].T
            low = turned.astype(jnp.bfloat16)
            linear = summed(k * STRIPE, size) * turned[:, ROWS : ROWS + 1] + mm(low, raised[...])
            sigma = 1.0 / (1.0 + jnp.exp(-linear))
            slope_ref[pl.ds(at, size), :] = sigma * (1.0 + linear * (1.0 - sigma))
            member = member_ref[pl.ds(k * STRIPE, size), :].astype(jnp.float32).T
            member = member[0:ROWS].astype(jnp.bfloat16)
            high, rest = split(linear * sigma)
            total[...] += mm(member, high) + mm(member, rest)
        total[...] += summed(span + (stripes + 1) * ROWS, ROWS)

    add((own_ref, core_ref, far_ref), member_ref, 0)
    real = (ids_ref[...] != 0).astype(jnp.float32)

    @pl.when(jnp.sum(real) > member_ref.shape[0])
    def _():
        add((own_rest, core_rest, far_rest), member_rest, member_ref.shape[0])

    counts = jnp.sum(real, axis=1, keepdims=True)
    pooled = total[0:texts] / counts
    pooled = jnp.concatenate([pooled, jnp.zeros((ROWS - texts, width), jnp.float32)])
    pooled_ref[...] = pooled.astype(jnp.bfloat16)


def both_sides(near, far):
    queries = lax.axis_index("group") == 0
    return jnp.concatenate([jnp.where(queries, near, far), jnp.where(queries, far, near)], axis=0)


def dots_kernel(near_ref, far_ref, packed_ref):
    near = near_ref[...]
    block = both_sides(near, far_ref[...])
    dots = mm(block, block, NT)
    rows = 2 * ROWS
    packed_ref[...] = jnp.zeros_like(packed_ref)
    packed_ref[0:rows, 0:rows] = dots
    for part in range(near.shape[1] // LANES):
        start = rows + part * ROWS
        packed_ref[start : start + ROWS, :] = near[:, part * LANES : (part + 1) * LANES].astype(
            jnp.float32
        )


def score_kernel(
    ids_ref,
    near_ref,
    far_ref,
    packed0,
    packed1,
    packed2,
    packed3,
    dots0,
    dots1,
    dots2,
    dots3,
    misc_ref,
    slope_ref,
    reduced_ref,
    member_ref,
    member_rest,
    sharp_ref,
    embed_ref,
    loss_ref,
    up_ref,
    negatives,
):
    texts, length = ids_ref.shape
    stripes = pl.cdiv(member_ref.shape[0], STRIPE)
    rows = 2 * ROWS
    width = near_ref.shape[1]
    per_shard = loss_ref.shape[1]
    group, shard = lax.axis_index("group"), lax.axis_index("dp")
    dots = ((dots0[...] + dots1[...]) + (dots2[...] + dots3[...]))[:, 0:rows]
    down, across = iota((rows, rows), 0), iota((rows, rows), 1)
    same = down == across
    real = (lax.rem(down, ROWS) < texts) & (lax.rem(across, ROWS) < texts)
    diagonal = jnp.where(same, dots, 0.0)
    rnorm_row = lax.rsqrt(jnp.sum(diagonal, axis=0, keepdims=True) + 1e-06)
    rnorm_col = lax.rsqrt(jnp.sum(diagonal, axis=1, keepdims=True) + 1e-06)
    sharpness = sharp_ref[0]
    cosine = dots * rnorm_col * rnorm_row
    scores = sharpness * cosine
    keep = real & ~same
    top = jnp.max(jnp.where(keep, scores, -jnp.inf), axis=0, keepdims=True)
    top = jnp.where(lax.rem(across[0:1], ROWS) < texts, top, 0.0)
    powers = jnp.exp(jnp.where(real, jnp.minimum(scores - top, 0.0), 0.0))
    hard = misc_ref[stripes : stripes + negatives, 0:rows].astype(jnp.int32) + ROWS
    times = jnp.zeros((rows, rows), jnp.float32)
    for k in range(negatives):
        times += jnp.where(hard[k : k + 1] == down, 1.0, 0.0)
    times = jnp.where(across < texts, times, 0.0)
    weights = (jnp.where(keep, 1.0, 0.0) + jnp.where(real, times, 0.0)) * powers
    total = jnp.sum(weights, axis=0, keepdims=True)
    total = jnp.where(lax.rem(across[0:1], ROWS) < texts, total, 1.0)
    pair = (down == lax.rem(across + ROWS, rows)) & real
    pair_score = jnp.sum(jnp.where(pair, scores, 0.0), axis=0, keepdims=True)
    losses = top + jnp.log(total) - pair_score
    grad_scores = (weights / total - jnp.where(pair, 1.0, 0.0)) / (2 * texts)
    coeff = (grad_scores * rnorm_col * rnorm_row).astype(jnp.bfloat16)
    radial = jnp.sum(grad_scores * cosine, axis=0, keepdims=True) * rnorm_row * rnorm_row

    first = shard * per_shard
    loss_col = jnp.sum(jnp.where(same, losses, 0.0), axis=1, keepdims=True)
    at = (iota((rows, LANES), 0) == group * ROWS + first + iota((rows, LANES), 1)) & (
        iota((rows, LANES), 1) < per_shard
    )
    loss_ref[...] = jnp.sum(jnp.where(at, loss_col, 0.0), axis=0, keepdims=True)[:, 0:per_shard]

    mine = both_sides(near_ref[...], far_ref[...])
    along = mm(coeff.astype(jnp.float32).T.astype(jnp.bfloat16), mine)
    radial_col = jnp.sum(jnp.where(same, radial, 0.0), axis=1, keepdims=True)
    grad = sharpness * (along - radial_col * mine.astype(jnp.float32))
    grad = jnp.where(group == 0, grad[0:ROWS], grad[ROWS:rows])
    real_tokens = (ids_ref[...] != 0).astype(jnp.float32)
    counts = jnp.sum(real_tokens, axis=1, keepdims=True)
    grad = grad[0:texts] / counts
    grad = jnp.concatenate([grad, jnp.zeros((LANES - texts, width), jnp.float32)])
    high, rest = split(grad)

    def update(member_ref, base):
        total = jnp.zeros((ROWS, width), jnp.float32)
        for k in range(member_ref.shape[0] // CHUNK):
            at = base + k * CHUNK
            member = member_ref[pl.ds(k * CHUNK, CHUNK), :]
            token_grad = mm(member, high) + mm(member, rest)
            local = (token_grad * slope_ref[pl.ds(at, CHUNK), :]).astype(jnp.bfloat16)
            total += mm(reduced_ref[:, at : at + CHUNK], local)
        return total

    first_part = update(member_ref, 0)
    up_ref[...] = first_part

    @pl.when(jnp.sum(real_tokens) > member_ref.shape[0])
    def _():
        up_ref[...] = first_part + update(member_rest, member_ref.shape[0])

    rnorm_own = jnp.where(group == 0, rnorm_col[0:ROWS], rnorm_col[ROWS:rows])
    chosen = iota((ROWS, ROWS), 1) == iota((ROWS, ROWS), 0) + first
    chosen = jnp.where(chosen & (iota((ROWS, ROWS), 0) < per_shard), 1.0, 0.0).astype(jnp.bfloat16)
    for o, packed in enumerate((packed0, packed1, packed2, packed3)):
        halves = [
            packed[rows + part * ROWS : rows + (part + 1) * ROWS, :]
            for part in range(width // LANES)
        ]
        block = jnp.concatenate(halves, axis=1) * rnorm_own
        picked = mm(chosen, block.astype(jnp.bfloat16)).astype(jnp.bfloat16)
        at = pl.multiple_of(quarter_of(shard ^ o) * width, LANES)
        embed_ref[0, :, pl.ds(at, width)] = picked[0:per_shard]


def any_spec():
    return pl.BlockSpec(memory_space=pl.ANY)


def vmem_spec():
    return pl.BlockSpec(memory_space=pltpu.VMEM)


def smem_spec():
    return pl.BlockSpec(memory_space=pltpu.SMEM)


def exchange(x, axis, size):
    steps = [[(i, i ^ o) for i in range(size)] for o in range(1, size)]
    return [x] + [lax.ppermute(x, axis, step) for step in steps]


def split_body(
    query_passage_words,
    difficult_distractors,
    vocabulary_vectors,
    layer_weight_matrix,
    lowering_factor_matrix,
    raising_factor_matrix,
    logit_sharpness,
):
    shards, parts = lax.axis_size("dp"), lax.axis_size("mp")
    ids = query_passage_words[0]
    texts, length = ids.shape
    tokens = texts * length
    features, vocab = vocabulary_vectors.shape
    blocks = vocab // IDS_PER_BLOCK
    group_rows = 8 * pl.cdiv(vocab // IDS_PER_GROUP + 1, 8)
    per_shard, negatives = difficult_distractors.shape
    rank = lowering_factor_matrix.shape[0]
    part_width = layer_weight_matrix.shape[1]
    width = part_width // shards
    params = pltpu.CompilerParams(vmem_limit_bytes=VMEM_BYTES)
    other_core = [(d, d ^ 1) for d in range(shards)]
    other_y = [(d, d ^ 2) for d in range(shards)]

    def project(base, span):
        stripes = pl.cdiv(span, STRIPE)
        rows = span + (stripes + 2) * ROWS
        own0, own1, away0, away1, member = pl.pallas_call(
            functools.partial(project_kernel, base=base),
            out_shape=[jax.ShapeDtypeStruct((rows, width), jnp.bfloat16)] * 4
            + [jax.ShapeDtypeStruct((span, LANES), jnp.bfloat16)],
            in_specs=[vmem_spec()] * 2 + [any_spec()] * 3,
            out_specs=[any_spec()] * 4 + [vmem_spec()],
            scratch_shapes=[
                pltpu.VMEM((blocks, features, IDS_PER_BLOCK), jnp.bfloat16),
                pltpu.VMEM((features, part_width), jnp.bfloat16),
                pltpu.VMEM((rank, features), jnp.bfloat16),
                pltpu.VMEM((features, span), jnp.bfloat16),
                pltpu.VMEM((4, rows, width), jnp.bfloat16),
                pltpu.VMEM((8 * pl.cdiv(span // LANES, 8), LANES), jnp.int32),
                pltpu.VMEM((LANES, LANES), jnp.float32),
                pltpu.VMEM((texts, length), jnp.float32),
                pltpu.VMEM((ROWS + 8, stripes * STRIPE), jnp.float32),
                pltpu.VMEM((ROWS, features), jnp.float32),
                pltpu.VMEM((group_rows, length), jnp.int32),
                pltpu.SMEM((group_rows, length), jnp.int32),
                pltpu.SemaphoreType.DMA((blocks,)),
                pltpu.SemaphoreType.DMA,
                pltpu.SemaphoreType.DMA,
                pltpu.SemaphoreType.DMA,
                pltpu.SemaphoreType.DMA((4,)),
            ],
            compiler_params=params,
            name="project",
        )(
            ids,
            difficult_distractors,
            vocabulary_vectors,
            layer_weight_matrix,
            lowering_factor_matrix,
        )
        core1 = lax.ppermute(away1, "dp", other_core)
        core0 = lax.ppermute(away0, "dp", other_core)
        chip1 = (own1.astype(jnp.float32) + core1.astype(jnp.float32)).astype(jnp.bfloat16)
        far = lax.ppermute(chip1, "dp", other_y)
        return own0, core0, far, member

    first = project(0, FIRST)
    many = jnp.sum((ids != 0).astype(jnp.int32)) > FIRST
    left = tokens - FIRST
    shapes = jax.eval_shape(lambda: project(FIRST, left))
    rest = lax.cond(
        many,
        lambda: project(FIRST, left),
        lambda: tuple(jnp.zeros(x.shape, x.dtype) for x in shapes),
    )
    pooled, slope, reduced, misc = pl.pallas_call(
        functools.partial(pool_kernel, model_width=float(features * shards)),
        out_shape=[
            jax.ShapeDtypeStruct((ROWS, width), jnp.bfloat16),
            jax.ShapeDtypeStruct((tokens, width), jnp.float32),
            jax.ShapeDtypeStruct((ROWS, tokens), jnp.bfloat16),
            jax.ShapeDtypeStruct((ROWS, width), jnp.float32),
        ],
        in_specs=[vmem_spec()] * 10,
        out_specs=[vmem_spec()] * 4,
        scratch_shapes=[
            pltpu.VMEM((LANES, width), jnp.bfloat16),
            pltpu.VMEM((ROWS, width), jnp.float32),
        ],
        compiler_params=params,
        name="pool",
    )(ids, *first, *rest, raising_factor_matrix)
    member, member_rest = first[3], rest[3]
    far_side = lax.ppermute(pooled, "group", [(0, 1), (1, 0)])
    rows = 2 * ROWS
    packed = pl.pallas_call(
        dots_kernel,
        out_shape=jax.ShapeDtypeStruct((rows + width // LANES * ROWS, LANES), jnp.float32),
        in_specs=[vmem_spec()] * 2,
        out_specs=vmem_spec(),
        compiler_params=params,
        name="dots",
    )(pooled, far_side)
    packed = exchange(packed, "dp", shards)
    dots = [x[0:rows] for x in packed]
    dots = exchange((dots[0] + dots[1]) + (dots[2] + dots[3]), "mp", parts)
    embeddings, losses, update = pl.pallas_call(
        functools.partial(score_kernel, negatives=negatives),
        out_shape=[
            jax.ShapeDtypeStruct((1, per_shard, part_width), jnp.bfloat16),
            jax.ShapeDtypeStruct((1, per_shard), jnp.float32),
            jax.ShapeDtypeStruct((ROWS, width), jnp.float32),
        ],
        in_specs=[vmem_spec()] * 16 + [smem_spec()],
        out_specs=[vmem_spec()] * 3,
        compiler_params=params,
        name="score",
    )(
        ids,
        pooled,
        far_side,
        *packed,
        *dots,
        misc,
        slope,
        reduced,
        member,
        member_rest,
        logit_sharpness,
    )
    update = update + lax.ppermute(update, "group", [(0, 1), (1, 0)])
    updates = exchange(update, "dp", shards)
    shard = lax.axis_index("dp")
    columns = [lax.select_n(shard ^ quarter_of(q), *updates) for q in range(shards)]
    return (embeddings, losses, jnp.concatenate(columns, axis=1))


def body(words, hard, vocabulary, weight, lowering, raising, sharpness):
    shards, parts = lax.axis_size("dp"), lax.axis_size("mp")
    texts, length = words.shape[1:]
    features, vocab = vocabulary.shape
    negatives = hard.shape[1]
    square = shards == 4 and features == weight.shape[1] == 4 * STRIPE and parts == shards
    small = texts <= ROWS - 2 and length == LANES and FIRST < texts * length <= 2048
    even = (texts * length - FIRST) % CHUNK == 0 and vocab % IDS_PER_BLOCK == 0
    fits = features * vocab <= 2**24 and features % (4 * LANES) == 0
    spare = pl.cdiv(FIRST, STRIPE) + negatives <= ROWS and lowering.shape[0] == ROWS
    fast = square and small and even and fits and spare and lax.axis_size("group") == 2
    chosen = split_body if fast else general_body
    return chosen(words, hard, vocabulary, weight, lowering, raising, sharpness)


def solution(mesh):
    in_specs = (
        P("group", None, None),
        P("dp", None),
        P("dp", None),
        P("dp", "mp"),
        P(),
        P(None, "mp"),
        P(),
    )
    out_specs = (P("group", "dp", "mp"), P("group", "dp"), P(None, "mp"))
    return jax.shard_map(body, mesh=mesh, in_specs=in_specs, out_specs=out_specs, check_vma=False)
```

```python
import functools

import jax
import jax.numpy as jnp
from jax import lax
from jax.experimental import pallas as pl
from jax.experimental.pallas import tpu as pltpu
from jax.sharding import PartitionSpec as P


def general_body(
    query_passage_words,
    difficult_distractors,
    vocabulary_vectors,
    layer_weight_matrix,
    lowering_factor_matrix,
    raising_factor_matrix,
    logit_sharpness,
):
    group_index = lax.axis_index("group")
    shard_index = lax.axis_index("dp")
    part_index = lax.axis_index("mp")
    shard_count = lax.axis_size("dp")
    side_ids = query_passage_words[0]
    text_count = side_ids.shape[0]
    length = side_ids.shape[1]
    per_shard = text_count // shard_count
    own_ids = lax.dynamic_slice_in_dim(side_ids, shard_index * per_shard, per_shard, 0)
    columns = jnp.take(vocabulary_vectors, side_ids.reshape(-1), axis=1)
    inputs = lax.all_to_all(columns, "dp", split_axis=1, concat_axis=0, tiled=True)
    tokens = inputs.shape[1]
    feature_width = raising_factor_matrix.shape[1]
    wide_inputs = inputs.astype(jnp.float32)
    inverse = lax.rsqrt(jnp.mean(wide_inputs * wide_inputs, axis=0) + 1e-05)
    normed_state = (wide_inputs * inverse[None, :]).astype(jnp.bfloat16)
    linear_map = lax.dot_general(
        lax.all_gather(layer_weight_matrix, "dp", axis=0, tiled=True),
        normed_state,
        (((0,), (0,)), ((), ())),
        preferred_element_type=jnp.float32,
    )
    reduced_sum = jnp.dot(
        lowering_factor_matrix, normed_state, preferred_element_type=jnp.float32
    ).astype(jnp.bfloat16)
    linear_map = linear_map + lax.dot_general(
        raising_factor_matrix,
        reduced_sum,
        (((0,), (0,)), ((), ())),
        preferred_element_type=jnp.float32,
    )
    own_inputs = lax.dynamic_slice_in_dim(
        inputs, part_index * feature_width, feature_width, 0
    ).astype(jnp.float32)
    hidden_state = own_inputs + jax.nn.silu(linear_map)
    mask = (own_ids != 0).astype(jnp.float32)
    counts = jnp.sum(mask, axis=1)
    summed = jnp.einsum("dnl,nl->nd", hidden_state.reshape(feature_width, per_shard, length), mask)
    pooled = (summed / counts[:, None]).astype(jnp.bfloat16)
    gathered = lax.all_gather(pooled, ("group", "dp"), axis=0, tiled=True)
    part_scores = lax.dot_general(
        pooled, gathered, (((1,), (1,)), ((), ())), preferred_element_type=jnp.float32
    )
    gathered_wide = gathered.astype(jnp.float32)
    part_norms = jnp.sum(gathered_wide * gathered_wide, axis=1)
    dots, norms = lax.psum((part_scores, part_norms), "mp")
    rnorm_all = lax.rsqrt(norms + 1e-06)
    all_count = gathered.shape[0]
    half_count = all_count // 2
    own_rows = (
        group_index * half_count + shard_index * per_shard + jnp.arange(per_shard, dtype=jnp.int32)
    )
    rnorm_own = jnp.take(rnorm_all, own_rows)
    cosine = dots * rnorm_own[:, None] * rnorm_all[None, :]
    multiplier_factor = logit_sharpness[0]
    scores = multiplier_factor * cosine
    column_ids = jnp.arange(all_count, dtype=jnp.int32)
    keep = column_ids[None, :] != own_rows[:, None]
    pair = (own_rows + half_count) % all_count
    weight = (group_index == 0).astype(jnp.float32)
    neg_cols = half_count + difficult_distractors
    top = jnp.max(jnp.where(keep, scores, -jnp.inf), axis=1)
    safe_scores = jnp.where(keep, scores, top[:, None])
    expd = jnp.where(keep, jnp.exp(safe_scores - top[:, None]), 0.0)
    neg_exp = (
        jnp.exp(jnp.minimum(jnp.take_along_axis(scores, neg_cols, axis=1) - top[:, None], 0.0))
        * weight
    )
    total = jnp.sum(expd, axis=1) + jnp.sum(neg_exp, axis=1)
    pair_score = jnp.take_along_axis(scores, pair[:, None], axis=1)[:, 0]
    losses = top + jnp.log(total) - pair_score
    onehot = (column_ids[None, None, :] == neg_cols[:, :, None]).astype(jnp.float32)
    probs = (expd + jnp.einsum("rk,rkc->rc", neg_exp, onehot)) / total[:, None]
    target = (column_ids[None, :] == pair[:, None]).astype(jnp.float32)
    grad_scores = (probs - target) / all_count
    coeff = (grad_scores * rnorm_own[:, None] * rnorm_all[None, :]).astype(jnp.bfloat16)
    along = jnp.dot(coeff, gathered, preferred_element_type=jnp.float32)
    pooled_wide = pooled.astype(jnp.float32)
    radial = jnp.sum(grad_scores * cosine, axis=1) * rnorm_own * rnorm_own
    embedding_gradient = multiplier_factor * (along - radial[:, None] * pooled_wide)
    token_grad = jnp.einsum("nd,nl->dnl", embedding_gradient / counts[:, None], mask).reshape(
        feature_width, tokens
    )
    sigma = jax.nn.sigmoid(linear_map)
    local = (token_grad * sigma * (1.0 + linear_map * (1.0 - sigma))).astype(jnp.bfloat16)
    up_portion = lax.dot_general(
        reduced_sum, local, (((1,), (1,)), ((), ())), preferred_element_type=jnp.float32
    )
    adapter_up_gradient = lax.psum(up_portion, ("group", "dp"))
    embeddings = (pooled_wide * rnorm_own[:, None]).astype(jnp.bfloat16)[None]
    return (embeddings, losses[None], adapter_up_gradient)


BLOCK_BITS, GROUP_BITS, LANE_BITS, ROW_BITS = 10, 8, 7, 4
IDS_PER_BLOCK = 1 << BLOCK_BITS
IDS_PER_GROUP = 1 << GROUP_BITS
CHUNK = 384
STRIPE = 256
ROWS = 1 << ROW_BITS
LANES = 1 << LANE_BITS
FEATURE_ROWS = 128
FIRST = 1152
NT = (((1,), (1,)), ((), ()))
VMEM_BYTES = 60 * 1024 * 1024


def mm(a, b, dims=(((1,), (0,)), ((), ()))):
    return lax.dot_general(a, b, dims, preferred_element_type=jnp.float32)


def split(x):
    high = x.astype(jnp.bfloat16)
    return high, (x - high.astype(jnp.float32)).astype(jnp.bfloat16)


def iota(shape, dim):
    return lax.broadcasted_iota(jnp.int32, shape, dim)


def quarter_of(dp_index, cores=2):
    return (dp_index % cores) * 2 + dp_index // cores


def split_quarter(i, j, cores=2):
    shard = lax.axis_index("dp")
    core, side_y = lax.rem(shard, cores), lax.div(shard, cores)
    return (core ^ i) * 2 + (side_y ^ j)


def take_lanes(x, lanes):
    numbers = lax.GatherDimensionNumbers(
        offset_dims=(),
        collapsed_slice_dims=(1,),
        start_index_map=(1,),
        operand_batching_dims=(0,),
        start_indices_batching_dims=(0,),
    )
    mode = lax.GatherScatterMode.PROMISE_IN_BOUNDS
    return lax.gather(x, lanes[..., None], numbers, slice_sizes=(1, 1), mode=mode)


def gather_kernel(
    ids_ref,
    hard_ref,
    vocab_ref,
    lower_ref,
    turned,
    member_ref,
    extra_ref,
    held,
    lower,
    token_ref,
    small,
    ranks,
    counted,
    bounds,
    held_sems,
    lower_sem,
    bounds_sem,
    base,
):
    texts, length = ids_ref.shape
    features, vocab = vocab_ref.shape
    blocks = vocab // IDS_PER_BLOCK
    groups = vocab // IDS_PER_GROUP
    span = member_ref.shape[0]
    stripes = pl.cdiv(span, STRIPE)
    per_shard, negatives = hard_ref.shape
    shard = lax.axis_index("dp")

    def vocab_copy(b):
        columns = pl.ds(pl.multiple_of(b * IDS_PER_BLOCK, LANES), IDS_PER_BLOCK)
        return pltpu.make_async_copy(vocab_ref.at[:, columns], held.at[b], held_sems.at[b])

    lower_copy = pltpu.make_async_copy(
        lower_ref.at[:, pl.ds(pl.multiple_of(shard * features, LANES), features)], lower, lower_sem
    )
    vocab_copy(0).start()
    lower_copy.start()
    for b in range(1, blocks):
        vocab_copy(b).start()

    ids = ids_ref[...]
    valid = ids != 0
    group_of = jnp.where(valid, lax.shift_right_logical(ids, GROUP_BITS), groups)
    group_rows = counted.shape[0]
    group_id = iota((group_rows, length), 0)
    below = jnp.zeros((group_rows, length), jnp.float32)
    for text in range(texts):
        below += jnp.where(group_of[text : text + 1] < group_id, 1.0, 0.0)
    before = jnp.broadcast_to(jnp.sum(below, axis=1, keepdims=True), (group_rows, length))
    counted[...] = before.astype(jnp.int32)
    bounds_copy = pltpu.make_async_copy(counted, bounds, bounds_sem)
    bounds_copy.start()
    earlier = jnp.where(iota((length, length), 0) < iota((length, length), 1), 1.0, 0.0).astype(
        jnp.bfloat16
    )
    for text in range(texts):
        here = jnp.where(group_of[text : text + 1] == group_id, 1.0, 0.0)
        inside = mm(here.astype(jnp.bfloat16), earlier)
        ranks[pl.ds(text, 1), :] = jnp.sum(here * (inside + before), axis=0, keepdims=True)
        before += jnp.broadcast_to(jnp.sum(here, axis=1, keepdims=True), (group_rows, length))
    text_of = iota((texts, length), 0)
    carried = jnp.where(valid, lax.shift_left(ids, ROW_BITS) + text_of, 0).astype(jnp.float32)
    rank = ranks[...]

    def place(p, carry):
        position = (iota((LANES, length), 0) + (p * LANES + base)).astype(jnp.float32)
        total = jnp.zeros((LANES, length), jnp.float32)
        for text in range(texts):
            total += jnp.where(rank[text : text + 1] == position, carried[text : text + 1], 0.0)
        found = jnp.broadcast_to(jnp.sum(total, axis=1, keepdims=True), (LANES, LANES))
        start = pl.multiple_of(p * LANES, LANES)
        row = found.T[0:1].astype(jnp.int32)
        token = lax.shift_right_logical(row, ROW_BITS)
        token_ref[pl.ds(p, 1), :] = jnp.where(token == 0, -vocab, token)
        found = found.astype(jnp.int32)
        real = (found >= ROWS) & ((found & (ROWS - 1)) == iota((LANES, LANES), 1))
        member_ref[pl.ds(start, LANES), :] = jnp.where(real, 1.0, 0.0).astype(jnp.bfloat16)
        turned[:, pl.ds(start, LANES)] = jnp.zeros((features, LANES), jnp.bfloat16)
        return carry

    lax.fori_loop(0, span // LANES, place, 0)
    small[...] = jnp.zeros_like(small)
    small[0:per_shard, stripes : stripes + negatives] = hard_ref[...].astype(jnp.float32)
    lower_copy.wait()
    bounds_copy.wait()

    def within(place):
        return jnp.clip(place - base, 0, span)

    def take(b, carry):
        vocab_copy(b).wait()
        for part in range(IDS_PER_BLOCK // IDS_PER_GROUP):
            group = b * (IDS_PER_BLOCK // IDS_PER_GROUP) + part
            first, last = within(bounds[group, 0]), within(bounds[group + 1, 0])
            begin = lax.shift_right_logical(first, LANE_BITS)
            end = lax.shift_right_logical(last + LANES - 1, LANE_BITS)

            def window(p, carry):
                at = pl.ds(pl.multiple_of(p * LANES, LANES), LANES)
                token = token_ref[pl.ds(p, 1), :] - group * IDS_PER_GROUP
                token = jnp.broadcast_to(token, (FEATURE_ROWS, LANES))
                lane = (token & (LANES - 1)).astype(jnp.int16)
                tile = lax.shift_right_arithmetic(token, LANE_BITS).astype(jnp.int16)
                for f in range(features // FEATURE_ROWS):
                    rows = pl.ds(f * FEATURE_ROWS, FEATURE_ROWS)
                    total = turned[rows, at]
                    for j in range(IDS_PER_GROUP // LANES):
                        columns = pl.ds(part * IDS_PER_GROUP + j * LANES, LANES)
                        found = take_lanes(held[b, rows, columns], lane)
                        total = jnp.where(tile == j, found, total)
                    turned[rows, at] = total
                return carry

            lax.fori_loop(begin, jnp.where(last > first, end, begin), window, 0)
        return carry

    lax.fori_loop(0, blocks, take, 0)

    misc = jnp.zeros((ROWS, STRIPE), jnp.float32)
    residual = jnp.zeros((features, LANES), jnp.float32)
    for stripe in range(stripes):
        size = min(STRIPE, span - stripe * STRIPE)
        across = pl.ds(stripe * STRIPE, size)
        upright = turned[:, across]
        wide = upright.astype(jnp.float32)
        square = jnp.sum(wide * wide, axis=0, keepdims=True)
        reduced = mm(lower[...], upright)
        if size < STRIPE:
            none = jnp.zeros((ROWS, STRIPE - size), jnp.float32)
            reduced = jnp.concatenate([reduced, none], axis=1)
            square = jnp.concatenate([square, none[0:1]], axis=1)
        extra_ref[stripe * ROWS : (stripe + 1) * ROWS, :] = reduced.astype(jnp.bfloat16)
        misc = jnp.where(iota((ROWS, STRIPE), 0) == stripe, square, misc)
        residual += mm(upright, member_ref[across, :])
    hard = small[...].T[0:ROWS]
    for i in range(per_shard):
        misc += jnp.where(iota((ROWS, STRIPE), 1) == shard * per_shard + i, hard[:, i : i + 1], 0.0)
    extra_ref[stripes * ROWS : (stripes + 1) * ROWS, :] = misc.astype(jnp.bfloat16)
    residual = jnp.where(lax.axis_index("mp") == shard, residual.T[0:ROWS], 0.0)
    for q in range(features // STRIPE):
        start = (stripes + 1 + q) * ROWS
        extra_ref[start : start + ROWS, :] = residual[:, q * STRIPE : (q + 1) * STRIPE].astype(
            jnp.bfloat16
        )


def pool_kernel(
    ids_ref,
    own_ref,
    core_ref,
    far_ref,
    extra_ref,
    member_ref,
    own_rest,
    core_rest,
    far_rest,
    extra_rest,
    member_rest,
    raise_ref,
    pooled_ref,
    slope_ref,
    reduced_ref,
    misc_ref,
    raised,
    total,
    model_width,
):
    texts, length = ids_ref.shape
    width = own_ref.shape[1]
    quarter = quarter_of(lax.axis_index("dp"))
    raised[...] = jnp.zeros_like(raised)
    raised[0:ROWS, :] = raise_ref[:, pl.ds(pl.multiple_of(quarter * width, LANES), width)]
    total[...] = jnp.zeros_like(total)

    def add(refs, extra_ref, member_ref, base):
        span = member_ref.shape[0]
        stripes = pl.cdiv(span, STRIPE)

        def summed(start, size):
            return sum(ref[pl.ds(start, size), :].astype(jnp.float32) for ref in refs)

        misc = extra_ref[stripes * ROWS : (stripes + 1) * ROWS, :]
        if base == 0:
            misc_ref[...] = misc
        inverse = lax.rsqrt(misc / model_width + 1e-05)
        for k in range(stripes):
            at = base + k * STRIPE
            size = min(STRIPE, span - k * STRIPE)
            scale = inverse[k : k + 1]
            reduced = (extra_ref[k * ROWS : (k + 1) * ROWS, :] * scale).astype(jnp.bfloat16)
            reduced_ref[:, at : at + size] = reduced[:, 0:size]
            stacked = jnp.concatenate(
                [reduced.astype(jnp.float32), jnp.broadcast_to(scale, (LANES - ROWS, STRIPE))]
            )
            turned = stacked[:, 0:size].T
            low = turned.astype(jnp.bfloat16)
            linear = summed(k * STRIPE, size) * turned[:, ROWS : ROWS + 1] + mm(low, raised[...])
            sigma = 1.0 / (1.0 + jnp.exp(-linear))
            slope_ref[pl.ds(at, size), :] = sigma * (1.0 + linear * (1.0 - sigma))
            member = member_ref[pl.ds(k * STRIPE, size), :].astype(jnp.float32).T
            member = member[0:ROWS].astype(jnp.bfloat16)
            high, rest = split(linear * sigma)
            total[...] += mm(member, high) + mm(member, rest)
        start = pl.multiple_of((stripes + 1 + quarter) * ROWS, ROWS)
        total[...] += extra_ref[pl.ds(start, ROWS), :]

    add((own_ref, core_ref, far_ref), extra_ref, member_ref, 0)
    real = (ids_ref[...] != 0).astype(jnp.float32)

    @pl.when(jnp.sum(real) > member_ref.shape[0])
    def _():
        add((own_rest, core_rest, far_rest), extra_rest, member_rest, member_ref.shape[0])

    counts = jnp.sum(real, axis=1, keepdims=True)
    pooled = total[0:texts] / counts
    pooled = jnp.concatenate([pooled, jnp.zeros((ROWS - texts, width), jnp.float32)])
    pooled_ref[...] = pooled.astype(jnp.bfloat16)


def both_sides(near, far):
    queries = lax.axis_index("group") == 0
    return jnp.concatenate([jnp.where(queries, near, far), jnp.where(queries, far, near)], axis=0)


def dots_kernel(near_ref, far_ref, packed_ref):
    near = near_ref[...]
    block = both_sides(near, far_ref[...])
    dots = mm(block, block, NT)
    rows = 2 * ROWS
    packed_ref[...] = jnp.zeros_like(packed_ref)
    packed_ref[0:rows, 0:rows] = dots
    for part in range(near.shape[1] // LANES):
        start = rows + part * ROWS
        packed_ref[start : start + ROWS, :] = near[:, part * LANES : (part + 1) * LANES].astype(
            jnp.float32
        )


def score_kernel(
    ids_ref,
    near_ref,
    far_ref,
    packed0,
    packed1,
    packed2,
    packed3,
    dots0,
    dots1,
    dots2,
    dots3,
    misc_ref,
    slope_ref,
    reduced_ref,
    member_ref,
    member_rest,
    sharp_ref,
    embed_ref,
    loss_ref,
    up_ref,
    negatives,
):
    texts, length = ids_ref.shape
    stripes = pl.cdiv(member_ref.shape[0], STRIPE)
    rows = 2 * ROWS
    width = near_ref.shape[1]
    per_shard = loss_ref.shape[1]
    group, shard = lax.axis_index("group"), lax.axis_index("dp")
    dots = ((dots0[...] + dots1[...]) + (dots2[...] + dots3[...]))[:, 0:rows]
    down, across = iota((rows, rows), 0), iota((rows, rows), 1)
    same = down == across
    real = (lax.rem(down, ROWS) < texts) & (lax.rem(across, ROWS) < texts)
    diagonal = jnp.where(same, dots, 0.0)
    rnorm_row = lax.rsqrt(jnp.sum(diagonal, axis=0, keepdims=True) + 1e-06)
    rnorm_col = lax.rsqrt(jnp.sum(diagonal, axis=1, keepdims=True) + 1e-06)
    sharpness = sharp_ref[0]
    cosine = dots * rnorm_col * rnorm_row
    scores = sharpness * cosine
    keep = real & ~same
    top = jnp.max(jnp.where(keep, scores, -jnp.inf), axis=0, keepdims=True)
    top = jnp.where(lax.rem(across[0:1], ROWS) < texts, top, 0.0)
    powers = jnp.exp(jnp.where(real, jnp.minimum(scores - top, 0.0), 0.0))
    hard = misc_ref[stripes : stripes + negatives, 0:rows].astype(jnp.int32) + ROWS
    times = jnp.zeros((rows, rows), jnp.float32)
    for k in range(negatives):
        times += jnp.where(hard[k : k + 1] == down, 1.0, 0.0)
    times = jnp.where(across < texts, times, 0.0)
    weights = (jnp.where(keep, 1.0, 0.0) + jnp.where(real, times, 0.0)) * powers
    total = jnp.sum(weights, axis=0, keepdims=True)
    total = jnp.where(lax.rem(across[0:1], ROWS) < texts, total, 1.0)
    pair = (down == lax.rem(across + ROWS, rows)) & real
    pair_score = jnp.sum(jnp.where(pair, scores, 0.0), axis=0, keepdims=True)
    losses = top + jnp.log(total) - pair_score
    grad_scores = (weights / total - jnp.where(pair, 1.0, 0.0)) / (2 * texts)
    coeff = (grad_scores * rnorm_col * rnorm_row).astype(jnp.bfloat16)
    radial = jnp.sum(grad_scores * cosine, axis=0, keepdims=True) * rnorm_row * rnorm_row

    first = shard * per_shard
    loss_col = jnp.sum(jnp.where(same, losses, 0.0), axis=1, keepdims=True)
    at = (iota((rows, LANES), 0) == group * ROWS + first + iota((rows, LANES), 1)) & (
        iota((rows, LANES), 1) < per_shard
    )
    loss_ref[...] = jnp.sum(jnp.where(at, loss_col, 0.0), axis=0, keepdims=True)[:, 0:per_shard]

    mine = both_sides(near_ref[...], far_ref[...])
    along = mm(coeff.astype(jnp.float32).T.astype(jnp.bfloat16), mine)
    radial_col = jnp.sum(jnp.where(same, radial, 0.0), axis=1, keepdims=True)
    grad = sharpness * (along - radial_col * mine.astype(jnp.float32))
    grad = jnp.where(group == 0, grad[0:ROWS], grad[ROWS:rows])
    real_tokens = (ids_ref[...] != 0).astype(jnp.float32)
    counts = jnp.sum(real_tokens, axis=1, keepdims=True)
    grad = grad[0:texts] / counts
    grad = jnp.concatenate([grad, jnp.zeros((LANES - texts, width), jnp.float32)])
    high, rest = split(grad)

    def update(member_ref, base):
        total = jnp.zeros((ROWS, width), jnp.float32)
        for k in range(member_ref.shape[0] // CHUNK):
            at = base + k * CHUNK
            member = member_ref[pl.ds(k * CHUNK, CHUNK), :]
            token_grad = mm(member, high) + mm(member, rest)
            local = (token_grad * slope_ref[pl.ds(at, CHUNK), :]).astype(jnp.bfloat16)
            total += mm(reduced_ref[:, at : at + CHUNK], local)
        return total

    first_part = update(member_ref, 0)
    up_ref[...] = first_part

    @pl.when(jnp.sum(real_tokens) > member_ref.shape[0])
    def _():
        up_ref[...] = first_part + update(member_rest, member_ref.shape[0])

    rnorm_own = jnp.where(group == 0, rnorm_col[0:ROWS], rnorm_col[ROWS:rows])
    chosen = iota((ROWS, ROWS), 1) == iota((ROWS, ROWS), 0) + first
    chosen = jnp.where(chosen & (iota((ROWS, ROWS), 0) < per_shard), 1.0, 0.0).astype(jnp.bfloat16)
    for o, packed in enumerate((packed0, packed1, packed2, packed3)):
        halves = [
            packed[rows + part * ROWS : rows + (part + 1) * ROWS, :]
            for part in range(width // LANES)
        ]
        block = jnp.concatenate(halves, axis=1) * rnorm_own
        picked = mm(chosen, block.astype(jnp.bfloat16)).astype(jnp.bfloat16)
        at = pl.multiple_of(quarter_of(shard ^ o) * width, LANES)
        embed_ref[0, :, pl.ds(at, width)] = picked[0:per_shard]


def any_spec():
    return pl.BlockSpec(memory_space=pl.ANY)


def vmem_spec():
    return pl.BlockSpec(memory_space=pltpu.VMEM)


def smem_spec():
    return pl.BlockSpec(memory_space=pltpu.SMEM)


def exchange(x, axis, size):
    steps = [[(i, i ^ o) for i in range(size)] for o in range(1, size)]
    return [x] + [lax.ppermute(x, axis, step) for step in steps]


def split_body(
    query_passage_words,
    difficult_distractors,
    vocabulary_vectors,
    layer_weight_matrix,
    lowering_factor_matrix,
    raising_factor_matrix,
    logit_sharpness,
):
    shards, parts = lax.axis_size("dp"), lax.axis_size("mp")
    ids = query_passage_words[0]
    texts, length = ids.shape
    tokens = texts * length
    features, vocab = vocabulary_vectors.shape
    blocks = vocab // IDS_PER_BLOCK
    group_rows = 8 * pl.cdiv(vocab // IDS_PER_GROUP + 1, 8)
    per_shard, negatives = difficult_distractors.shape
    rank = lowering_factor_matrix.shape[0]
    part_width = layer_weight_matrix.shape[1]
    width = part_width // shards
    params = pltpu.CompilerParams(vmem_limit_bytes=VMEM_BYTES)
    other_core = [(d, d ^ 1) for d in range(shards)]
    other_y = [(d, d ^ 2) for d in range(shards)]

    def columns(i, j):
        start = split_quarter(i, j) * width
        return lax.dynamic_slice(layer_weight_matrix, (0, start), (features, width))

    def project(base, span):
        stripes = pl.cdiv(span, STRIPE)
        extra_rows = (stripes + 1 + shards) * ROWS
        turned, member, extra = pl.pallas_call(
            functools.partial(gather_kernel, base=base),
            out_shape=[
                jax.ShapeDtypeStruct((features, span), jnp.bfloat16),
                jax.ShapeDtypeStruct((span, LANES), jnp.bfloat16),
                jax.ShapeDtypeStruct((extra_rows, STRIPE), jnp.bfloat16),
            ],
            in_specs=[vmem_spec()] * 2 + [any_spec()] * 2,
            out_specs=[vmem_spec()] * 3,
            scratch_shapes=[
                pltpu.VMEM((blocks, features, IDS_PER_BLOCK), jnp.bfloat16),
                pltpu.VMEM((rank, features), jnp.bfloat16),
                pltpu.VMEM((8 * pl.cdiv(span // LANES, 8), LANES), jnp.int32),
                pltpu.VMEM((LANES, LANES), jnp.float32),
                pltpu.VMEM((texts, length), jnp.float32),
                pltpu.VMEM((group_rows, length), jnp.int32),
                pltpu.SMEM((group_rows, length), jnp.int32),
                pltpu.SemaphoreType.DMA((blocks,)),
                pltpu.SemaphoreType.DMA,
                pltpu.SemaphoreType.DMA,
            ],
            compiler_params=params,
            name="gather",
        )(ids, difficult_distractors, vocabulary_vectors, lowering_factor_matrix)

        def product(i, j):
            return mm(turned, columns(i, j), (((0,), (0,)), ((), ())))

        def narrow(x):
            return x.astype(jnp.bfloat16)

        chip = extra.astype(jnp.float32)
        chip += lax.ppermute(extra, "dp", other_core).astype(jnp.float32)
        extra = chip + lax.ppermute(narrow(chip), "dp", other_y).astype(jnp.float32)
        core1 = lax.ppermute(narrow(product(1, 1)), "dp", other_core)
        far = lax.ppermute(narrow(product(0, 1) + core1.astype(jnp.float32)), "dp", other_y)
        core0 = lax.ppermute(narrow(product(1, 0)), "dp", other_core)
        own0 = narrow(product(0, 0))
        return own0, core0, far, extra, member

    first = project(0, FIRST)
    many = jnp.sum((ids != 0).astype(jnp.int32)) > FIRST
    left = tokens - FIRST
    shapes = jax.eval_shape(lambda: project(FIRST, left))
    rest = lax.cond(
        many,
        lambda: project(FIRST, left),
        lambda: tuple(jnp.zeros(x.shape, x.dtype) for x in shapes),
    )
    pooled, slope, reduced, misc = pl.pallas_call(
        functools.partial(pool_kernel, model_width=float(features * shards)),
        out_shape=[
            jax.ShapeDtypeStruct((ROWS, width), jnp.bfloat16),
            jax.ShapeDtypeStruct((tokens, width), jnp.float32),
            jax.ShapeDtypeStruct((ROWS, tokens), jnp.bfloat16),
            jax.ShapeDtypeStruct((ROWS, width), jnp.float32),
        ],
        in_specs=[vmem_spec()] * 12,
        out_specs=[vmem_spec()] * 4,
        scratch_shapes=[
            pltpu.VMEM((LANES, width), jnp.bfloat16),
            pltpu.VMEM((ROWS, width), jnp.float32),
        ],
        compiler_params=params,
        name="pool",
    )(ids, *first, *rest, raising_factor_matrix)
    member, member_rest = first[4], rest[4]
    far_side = lax.ppermute(pooled, "group", [(0, 1), (1, 0)])
    rows = 2 * ROWS
    packed = pl.pallas_call(
        dots_kernel,
        out_shape=jax.ShapeDtypeStruct((rows + width // LANES * ROWS, LANES), jnp.float32),
        in_specs=[vmem_spec()] * 2,
        out_specs=vmem_spec(),
        compiler_params=params,
        name="dots",
    )(pooled, far_side)
    packed = exchange(packed, "dp", shards)
    dots = [x[0:rows] for x in packed]
    dots = exchange((dots[0] + dots[1]) + (dots[2] + dots[3]), "mp", parts)
    embeddings, losses, update = pl.pallas_call(
        functools.partial(score_kernel, negatives=negatives),
        out_shape=[
            jax.ShapeDtypeStruct((1, per_shard, part_width), jnp.bfloat16),
            jax.ShapeDtypeStruct((1, per_shard), jnp.float32),
            jax.ShapeDtypeStruct((ROWS, width), jnp.float32),
        ],
        in_specs=[vmem_spec()] * 16 + [smem_spec()],
        out_specs=[vmem_spec()] * 3,
        compiler_params=params,
        name="score",
    )(
        ids,
        pooled,
        far_side,
        *packed,
        *dots,
        misc,
        slope,
        reduced,
        member,
        member_rest,
        logit_sharpness,
    )
    update = update + lax.ppermute(update, "group", [(0, 1), (1, 0)])
    updates = exchange(update, "dp", shards)
    shard = lax.axis_index("dp")
    columns = [lax.select_n(shard ^ quarter_of(q), *updates) for q in range(shards)]
    return (embeddings, losses, jnp.concatenate(columns, axis=1))


def body(words, hard, vocabulary, weight, lowering, raising, sharpness):
    shards, parts = lax.axis_size("dp"), lax.axis_size("mp")
    texts, length = words.shape[1:]
    features, vocab = vocabulary.shape
    negatives = hard.shape[1]
    square = shards == 4 and features == weight.shape[1] == 4 * STRIPE and parts == shards
    small = texts <= ROWS - 2 and length == LANES and FIRST < texts * length <= 2048
    even = (texts * length - FIRST) % CHUNK == 0 and vocab % IDS_PER_BLOCK == 0
    fits = features * vocab <= 2**24 and features % (4 * LANES) == 0
    spare = pl.cdiv(FIRST, STRIPE) + negatives <= ROWS and lowering.shape[0] == ROWS
    fast = square and small and even and fits and spare and lax.axis_size("group") == 2
    chosen = split_body if fast else general_body
    return chosen(words, hard, vocabulary, weight, lowering, raising, sharpness)


def solution(mesh):
    in_specs = (
        P("group", None, None),
        P("dp", None),
        P("dp", None),
        P("dp", "mp"),
        P(),
        P(None, "mp"),
        P(),
    )
    out_specs = (P("group", "dp", "mp"), P("group", "dp"), P(None, "mp"))
    return jax.shard_map(body, mesh=mesh, in_specs=in_specs, out_specs=out_specs, check_vma=False)
```

```python
import functools

import jax
import jax.numpy as jnp
from jax import lax
from jax.experimental import pallas as pl
from jax.experimental.pallas import tpu as pltpu
from jax.sharding import PartitionSpec as P


def general_body(
    query_passage_words,
    difficult_distractors,
    vocabulary_vectors,
    layer_weight_matrix,
    lowering_factor_matrix,
    raising_factor_matrix,
    logit_sharpness,
):
    group_index = lax.axis_index("group")
    shard_index = lax.axis_index("dp")
    part_index = lax.axis_index("mp")
    shard_count = lax.axis_size("dp")
    side_ids = query_passage_words[0]
    text_count = side_ids.shape[0]
    length = side_ids.shape[1]
    per_shard = text_count // shard_count
    own_ids = lax.dynamic_slice_in_dim(side_ids, shard_index * per_shard, per_shard, 0)
    columns = jnp.take(vocabulary_vectors, side_ids.reshape(-1), axis=1)
    inputs = lax.all_to_all(columns, "dp", split_axis=1, concat_axis=0, tiled=True)
    tokens = inputs.shape[1]
    feature_width = raising_factor_matrix.shape[1]
    wide_inputs = inputs.astype(jnp.float32)
    inverse = lax.rsqrt(jnp.mean(wide_inputs * wide_inputs, axis=0) + 1e-05)
    normed_state = (wide_inputs * inverse[None, :]).astype(jnp.bfloat16)
    linear_map = lax.dot_general(
        lax.all_gather(layer_weight_matrix, "dp", axis=0, tiled=True),
        normed_state,
        (((0,), (0,)), ((), ())),
        preferred_element_type=jnp.float32,
    )
    reduced_sum = jnp.dot(
        lowering_factor_matrix, normed_state, preferred_element_type=jnp.float32
    ).astype(jnp.bfloat16)
    linear_map = linear_map + lax.dot_general(
        raising_factor_matrix,
        reduced_sum,
        (((0,), (0,)), ((), ())),
        preferred_element_type=jnp.float32,
    )
    own_inputs = lax.dynamic_slice_in_dim(
        inputs, part_index * feature_width, feature_width, 0
    ).astype(jnp.float32)
    hidden_state = own_inputs + jax.nn.silu(linear_map)
    mask = (own_ids != 0).astype(jnp.float32)
    counts = jnp.sum(mask, axis=1)
    summed = jnp.einsum("dnl,nl->nd", hidden_state.reshape(feature_width, per_shard, length), mask)
    pooled = (summed / counts[:, None]).astype(jnp.bfloat16)
    gathered = lax.all_gather(pooled, ("group", "dp"), axis=0, tiled=True)
    part_scores = lax.dot_general(
        pooled, gathered, (((1,), (1,)), ((), ())), preferred_element_type=jnp.float32
    )
    gathered_wide = gathered.astype(jnp.float32)
    part_norms = jnp.sum(gathered_wide * gathered_wide, axis=1)
    dots, norms = lax.psum((part_scores, part_norms), "mp")
    rnorm_all = lax.rsqrt(norms + 1e-06)
    all_count = gathered.shape[0]
    half_count = all_count // 2
    own_rows = (
        group_index * half_count + shard_index * per_shard + jnp.arange(per_shard, dtype=jnp.int32)
    )
    rnorm_own = jnp.take(rnorm_all, own_rows)
    cosine = dots * rnorm_own[:, None] * rnorm_all[None, :]
    multiplier_factor = logit_sharpness[0]
    scores = multiplier_factor * cosine
    column_ids = jnp.arange(all_count, dtype=jnp.int32)
    keep = column_ids[None, :] != own_rows[:, None]
    pair = (own_rows + half_count) % all_count
    weight = (group_index == 0).astype(jnp.float32)
    neg_cols = half_count + difficult_distractors
    top = jnp.max(jnp.where(keep, scores, -jnp.inf), axis=1)
    safe_scores = jnp.where(keep, scores, top[:, None])
    expd = jnp.where(keep, jnp.exp(safe_scores - top[:, None]), 0.0)
    neg_exp = (
        jnp.exp(jnp.minimum(jnp.take_along_axis(scores, neg_cols, axis=1) - top[:, None], 0.0))
        * weight
    )
    total = jnp.sum(expd, axis=1) + jnp.sum(neg_exp, axis=1)
    pair_score = jnp.take_along_axis(scores, pair[:, None], axis=1)[:, 0]
    losses = top + jnp.log(total) - pair_score
    onehot = (column_ids[None, None, :] == neg_cols[:, :, None]).astype(jnp.float32)
    probs = (expd + jnp.einsum("rk,rkc->rc", neg_exp, onehot)) / total[:, None]
    target = (column_ids[None, :] == pair[:, None]).astype(jnp.float32)
    grad_scores = (probs - target) / all_count
    coeff = (grad_scores * rnorm_own[:, None] * rnorm_all[None, :]).astype(jnp.bfloat16)
    along = jnp.dot(coeff, gathered, preferred_element_type=jnp.float32)
    pooled_wide = pooled.astype(jnp.float32)
    radial = jnp.sum(grad_scores * cosine, axis=1) * rnorm_own * rnorm_own
    embedding_gradient = multiplier_factor * (along - radial[:, None] * pooled_wide)
    token_grad = jnp.einsum("nd,nl->dnl", embedding_gradient / counts[:, None], mask).reshape(
        feature_width, tokens
    )
    sigma = jax.nn.sigmoid(linear_map)
    local = (token_grad * sigma * (1.0 + linear_map * (1.0 - sigma))).astype(jnp.bfloat16)
    up_portion = lax.dot_general(
        reduced_sum, local, (((1,), (1,)), ((), ())), preferred_element_type=jnp.float32
    )
    adapter_up_gradient = lax.psum(up_portion, ("group", "dp"))
    embeddings = (pooled_wide * rnorm_own[:, None]).astype(jnp.bfloat16)[None]
    return (embeddings, losses[None], adapter_up_gradient)


BLOCK_BITS, GROUP_BITS, LANE_BITS, ROW_BITS = 10, 9, 7, 4
IDS_PER_BLOCK = 1 << BLOCK_BITS
IDS_PER_GROUP = 1 << GROUP_BITS
CHUNK = 384
STRIPE = 256
ROWS = 1 << ROW_BITS
LANES = 1 << LANE_BITS
FEATURE_ROWS = 128
FIRST = 1152
NT = (((1,), (1,)), ((), ()))
VMEM_BYTES = 60 * 1024 * 1024


def mm(a, b, dims=(((1,), (0,)), ((), ()))):
    return lax.dot_general(a, b, dims, preferred_element_type=jnp.float32)


def split(x):
    high = x.astype(jnp.bfloat16)
    return high, (x - high.astype(jnp.float32)).astype(jnp.bfloat16)


def iota(shape, dim):
    return lax.broadcasted_iota(jnp.int32, shape, dim)


def quarter_of(dp_index, cores=2):
    return (dp_index % cores) * 2 + dp_index // cores


def split_quarter(i, j, cores=2):
    shard = lax.axis_index("dp")
    core, side_y = lax.rem(shard, cores), lax.div(shard, cores)
    return (core ^ i) * 2 + (side_y ^ j)


def take_lanes(x, lanes):
    numbers = lax.GatherDimensionNumbers(
        offset_dims=(),
        collapsed_slice_dims=(1,),
        start_index_map=(1,),
        operand_batching_dims=(0,),
        start_indices_batching_dims=(0,),
    )
    mode = lax.GatherScatterMode.PROMISE_IN_BOUNDS
    return lax.gather(x, lanes[..., None], numbers, slice_sizes=(1, 1), mode=mode)


def gather_kernel(
    ids_ref,
    hard_ref,
    vocab_ref,
    lower_ref,
    turned,
    member_ref,
    extra_ref,
    held,
    lower,
    token_ref,
    small,
    ranks,
    counted,
    bounds,
    held_sems,
    lower_sem,
    bounds_sem,
    base,
):
    texts, length = ids_ref.shape
    features, vocab = vocab_ref.shape
    blocks = vocab // IDS_PER_BLOCK
    groups = vocab // IDS_PER_GROUP
    span = member_ref.shape[0]
    stripes = pl.cdiv(span, STRIPE)
    per_shard, negatives = hard_ref.shape
    shard = lax.axis_index("dp")

    def vocab_copy(b):
        columns = pl.ds(pl.multiple_of(b * IDS_PER_BLOCK, LANES), IDS_PER_BLOCK)
        return pltpu.make_async_copy(vocab_ref.at[:, columns], held.at[b], held_sems.at[b])

    lower_copy = pltpu.make_async_copy(
        lower_ref.at[:, pl.ds(pl.multiple_of(shard * features, LANES), features)], lower, lower_sem
    )
    vocab_copy(0).start()
    lower_copy.start()
    for b in range(1, blocks):
        vocab_copy(b).start()

    ids = ids_ref[...]
    valid = ids != 0
    group_of = jnp.where(valid, lax.shift_right_logical(ids, GROUP_BITS), groups)
    group_rows = counted.shape[0]
    group_id = iota((group_rows, length), 0)
    below = jnp.zeros((group_rows, length), jnp.float32)
    for text in range(texts):
        below += jnp.where(group_of[text : text + 1] < group_id, 1.0, 0.0)
    before = jnp.broadcast_to(jnp.sum(below, axis=1, keepdims=True), (group_rows, length))
    counted[...] = before.astype(jnp.int32)
    bounds_copy = pltpu.make_async_copy(counted, bounds, bounds_sem)
    bounds_copy.start()
    earlier = jnp.where(iota((length, length), 0) < iota((length, length), 1), 1.0, 0.0).astype(
        jnp.bfloat16
    )
    for text in range(texts):
        here = jnp.where(group_of[text : text + 1] == group_id, 1.0, 0.0)
        inside = mm(here.astype(jnp.bfloat16), earlier)
        ranks[pl.ds(text, 1), :] = jnp.sum(here * (inside + before), axis=0, keepdims=True)
        before += jnp.broadcast_to(jnp.sum(here, axis=1, keepdims=True), (group_rows, length))
    text_of = iota((texts, length), 0)
    carried = jnp.where(valid, lax.shift_left(ids, ROW_BITS) + text_of, 0).astype(jnp.float32)
    rank = ranks[...]

    def place(p, carry):
        position = (iota((LANES, length), 0) + (p * LANES + base)).astype(jnp.float32)
        total = jnp.zeros((LANES, length), jnp.float32)
        for text in range(texts):
            total += jnp.where(rank[text : text + 1] == position, carried[text : text + 1], 0.0)
        found = jnp.broadcast_to(jnp.sum(total, axis=1, keepdims=True), (LANES, LANES))
        start = pl.multiple_of(p * LANES, LANES)
        row = found.T[0:1].astype(jnp.int32)
        token = lax.shift_right_logical(row, ROW_BITS)
        token_ref[pl.ds(p, 1), :] = jnp.where(token == 0, -vocab, token)
        found = found.astype(jnp.int32)
        real = (found >= ROWS) & ((found & (ROWS - 1)) == iota((LANES, LANES), 1))
        member_ref[pl.ds(start, LANES), :] = jnp.where(real, 1.0, 0.0).astype(jnp.bfloat16)
        turned[:, pl.ds(start, LANES)] = jnp.zeros((features, LANES), jnp.bfloat16)
        return carry

    lax.fori_loop(0, span // LANES, place, 0)
    small[...] = jnp.zeros_like(small)
    small[0:per_shard, stripes : stripes + negatives] = hard_ref[...].astype(jnp.float32)
    lower_copy.wait()
    bounds_copy.wait()

    def within(place):
        return jnp.clip(place - base, 0, span)

    def take(b, carry):
        vocab_copy(b).wait()
        for part in range(IDS_PER_BLOCK // IDS_PER_GROUP):
            group = b * (IDS_PER_BLOCK // IDS_PER_GROUP) + part
            first, last = within(bounds[group, 0]), within(bounds[group + 1, 0])
            begin = lax.shift_right_logical(first, LANE_BITS)
            end = lax.shift_right_logical(last + LANES - 1, LANE_BITS)

            def window(p, carry):
                at = pl.ds(pl.multiple_of(p * LANES, LANES), LANES)
                token = token_ref[pl.ds(p, 1), :] - group * IDS_PER_GROUP
                token = jnp.broadcast_to(token, (FEATURE_ROWS, LANES))
                lane = (token & (LANES - 1)).astype(jnp.int16)
                tile = lax.shift_right_arithmetic(token, LANE_BITS).astype(jnp.int16)
                pieces = [pl.ds(f, FEATURE_ROWS) for f in range(0, features, FEATURE_ROWS)]
                fresh = []
                for rows in pieces:
                    total = jnp.zeros((FEATURE_ROWS, LANES), jnp.bfloat16)
                    for j in range(IDS_PER_GROUP // LANES):
                        columns = pl.ds(part * IDS_PER_GROUP + j * LANES, LANES)
                        total = jnp.where(tile == j, take_lanes(held[b, rows, columns], lane), total)
                    fresh.append(total)
                fresh = [turned[rows, at] + total for rows, total in zip(pieces, fresh)]
                for rows, total in zip(pieces, fresh):
                    turned[rows, at] = total
                return carry

            lax.fori_loop(begin, jnp.where(last > first, end, begin), window, 0)
        return carry

    lax.fori_loop(0, blocks, take, 0)

    misc = jnp.zeros((ROWS, STRIPE), jnp.float32)
    residual = jnp.zeros((features, LANES), jnp.float32)
    for stripe in range(stripes):
        size = min(STRIPE, span - stripe * STRIPE)
        across = pl.ds(stripe * STRIPE, size)
        upright = turned[:, across]
        wide = upright.astype(jnp.float32)
        square = jnp.sum(wide * wide, axis=0, keepdims=True)
        reduced = mm(lower[...], upright)
        if size < STRIPE:
            none = jnp.zeros((ROWS, STRIPE - size), jnp.float32)
            reduced = jnp.concatenate([reduced, none], axis=1)
            square = jnp.concatenate([square, none[0:1]], axis=1)
        extra_ref[stripe * ROWS : (stripe + 1) * ROWS, :] = reduced.astype(jnp.bfloat16)
        misc = jnp.where(iota((ROWS, STRIPE), 0) == stripe, square, misc)
        residual += mm(upright, member_ref[across, :])
    hard = small[...].T[0:ROWS]
    for i in range(per_shard):
        misc += jnp.where(iota((ROWS, STRIPE), 1) == shard * per_shard + i, hard[:, i : i + 1], 0.0)
    extra_ref[stripes * ROWS : (stripes + 1) * ROWS, :] = misc.astype(jnp.bfloat16)
    residual = jnp.where(lax.axis_index("mp") == shard, residual.T[0:ROWS], 0.0)
    for q in range(features // STRIPE):
        start = (stripes + 1 + q) * ROWS
        extra_ref[start : start + ROWS, :] = residual[:, q * STRIPE : (q + 1) * STRIPE].astype(
            jnp.bfloat16
        )


def pool_kernel(
    ids_ref,
    own_ref,
    core_ref,
    far_ref,
    extra_ref,
    member_ref,
    own_rest,
    core_rest,
    far_rest,
    extra_rest,
    member_rest,
    raise_ref,
    pooled_ref,
    slope_ref,
    reduced_ref,
    misc_ref,
    raised,
    total,
    model_width,
):
    texts, length = ids_ref.shape
    width = own_ref.shape[1]
    quarter = quarter_of(lax.axis_index("dp"))
    raised[...] = jnp.zeros_like(raised)
    raised[0:ROWS, :] = raise_ref[:, pl.ds(pl.multiple_of(quarter * width, LANES), width)]
    total[...] = jnp.zeros_like(total)

    def add(refs, extra_ref, member_ref, base):
        span = member_ref.shape[0]
        stripes = pl.cdiv(span, STRIPE)

        def summed(start, size):
            return sum(ref[pl.ds(start, size), :].astype(jnp.float32) for ref in refs)

        misc = extra_ref[stripes * ROWS : (stripes + 1) * ROWS, :]
        if base == 0:
            misc_ref[...] = misc
        inverse = lax.rsqrt(misc / model_width + 1e-05)
        for k in range(stripes):
            at = base + k * STRIPE
            size = min(STRIPE, span - k * STRIPE)
            scale = inverse[k : k + 1]
            reduced = (extra_ref[k * ROWS : (k + 1) * ROWS, :] * scale).astype(jnp.bfloat16)
            reduced_ref[:, at : at + size] = reduced[:, 0:size]
            stacked = jnp.concatenate(
                [reduced.astype(jnp.float32), jnp.broadcast_to(scale, (LANES - ROWS, STRIPE))]
            )
            turned = stacked[:, 0:size].T
            low = turned.astype(jnp.bfloat16)
            linear = summed(k * STRIPE, size) * turned[:, ROWS : ROWS + 1] + mm(low, raised[...])
            sigma = 1.0 / (1.0 + jnp.exp(-linear))
            slope_ref[pl.ds(at, size), :] = sigma * (1.0 + linear * (1.0 - sigma))
            member = member_ref[pl.ds(k * STRIPE, size), :].astype(jnp.float32).T
            member = member[0:ROWS].astype(jnp.bfloat16)
            high, rest = split(linear * sigma)
            total[...] += mm(member, high) + mm(member, rest)
        start = pl.multiple_of((stripes + 1 + quarter) * ROWS, ROWS)
        total[...] += extra_ref[pl.ds(start, ROWS), :]

    add((own_ref, core_ref, far_ref), extra_ref, member_ref, 0)
    real = (ids_ref[...] != 0).astype(jnp.float32)

    @pl.when(jnp.sum(real) > member_ref.shape[0])
    def _():
        add((own_rest, core_rest, far_rest), extra_rest, member_rest, member_ref.shape[0])

    counts = jnp.sum(real, axis=1, keepdims=True)
    pooled = total[0:texts] / counts
    pooled = jnp.concatenate([pooled, jnp.zeros((ROWS - texts, width), jnp.float32)])
    pooled_ref[...] = pooled.astype(jnp.bfloat16)


def both_sides(near, far):
    queries = lax.axis_index("group") == 0
    return jnp.concatenate([jnp.where(queries, near, far), jnp.where(queries, far, near)], axis=0)


def dots_kernel(near_ref, far_ref, packed_ref):
    near = near_ref[...]
    block = both_sides(near, far_ref[...])
    dots = mm(block, block, NT)
    rows = 2 * ROWS
    packed_ref[...] = jnp.zeros_like(packed_ref)
    packed_ref[0:rows, 0:rows] = dots
    for part in range(near.shape[1] // LANES):
        start = rows + part * ROWS
        packed_ref[start : start + ROWS, :] = near[:, part * LANES : (part + 1) * LANES].astype(
            jnp.float32
        )


def score_kernel(
    ids_ref,
    near_ref,
    far_ref,
    packed0,
    packed1,
    packed2,
    packed3,
    dots0,
    dots1,
    dots2,
    dots3,
    misc_ref,
    slope_ref,
    reduced_ref,
    member_ref,
    member_rest,
    sharp_ref,
    embed_ref,
    loss_ref,
    up_ref,
    negatives,
):
    texts, length = ids_ref.shape
    stripes = pl.cdiv(member_ref.shape[0], STRIPE)
    rows = 2 * ROWS
    width = near_ref.shape[1]
    per_shard = loss_ref.shape[1]
    group, shard = lax.axis_index("group"), lax.axis_index("dp")
    dots = ((dots0[...] + dots1[...]) + (dots2[...] + dots3[...]))[:, 0:rows]
    down, across = iota((rows, rows), 0), iota((rows, rows), 1)
    same = down == across
    real = (lax.rem(down, ROWS) < texts) & (lax.rem(across, ROWS) < texts)
    diagonal = jnp.where(same, dots, 0.0)
    rnorm_row = lax.rsqrt(jnp.sum(diagonal, axis=0, keepdims=True) + 1e-06)
    rnorm_col = lax.rsqrt(jnp.sum(diagonal, axis=1, keepdims=True) + 1e-06)
    sharpness = sharp_ref[0]
    cosine = dots * rnorm_col * rnorm_row
    scores = sharpness * cosine
    keep = real & ~same
    top = jnp.max(jnp.where(keep, scores, -jnp.inf), axis=0, keepdims=True)
    top = jnp.where(lax.rem(across[0:1], ROWS) < texts, top, 0.0)
    powers = jnp.exp(jnp.where(real, jnp.minimum(scores - top, 0.0), 0.0))
    hard = misc_ref[stripes : stripes + negatives, 0:rows].astype(jnp.int32) + ROWS
    times = jnp.zeros((rows, rows), jnp.float32)
    for k in range(negatives):
        times += jnp.where(hard[k : k + 1] == down, 1.0, 0.0)
    times = jnp.where(across < texts, times, 0.0)
    weights = (jnp.where(keep, 1.0, 0.0) + jnp.where(real, times, 0.0)) * powers
    total = jnp.sum(weights, axis=0, keepdims=True)
    total = jnp.where(lax.rem(across[0:1], ROWS) < texts, total, 1.0)
    pair = (down == lax.rem(across + ROWS, rows)) & real
    pair_score = jnp.sum(jnp.where(pair, scores, 0.0), axis=0, keepdims=True)
    losses = top + jnp.log(total) - pair_score
    grad_scores = (weights / total - jnp.where(pair, 1.0, 0.0)) / (2 * texts)
    coeff = (grad_scores * rnorm_col * rnorm_row).astype(jnp.bfloat16)
    radial = jnp.sum(grad_scores * cosine, axis=0, keepdims=True) * rnorm_row * rnorm_row

    first = shard * per_shard
    loss_col = jnp.sum(jnp.where(same, losses, 0.0), axis=1, keepdims=True)
    at = (iota((rows, LANES), 0) == group * ROWS + first + iota((rows, LANES), 1)) & (
        iota((rows, LANES), 1) < per_shard
    )
    loss_ref[...] = jnp.sum(jnp.where(at, loss_col, 0.0), axis=0, keepdims=True)[:, 0:per_shard]

    mine = both_sides(near_ref[...], far_ref[...])
    along = mm(coeff.astype(jnp.float32).T.astype(jnp.bfloat16), mine)
    radial_col = jnp.sum(jnp.where(same, radial, 0.0), axis=1, keepdims=True)
    grad = sharpness * (along - radial_col * mine.astype(jnp.float32))
    grad = jnp.where(group == 0, grad[0:ROWS], grad[ROWS:rows])
    real_tokens = (ids_ref[...] != 0).astype(jnp.float32)
    counts = jnp.sum(real_tokens, axis=1, keepdims=True)
    grad = grad[0:texts] / counts
    grad = jnp.concatenate([grad, jnp.zeros((LANES - texts, width), jnp.float32)])
    high, rest = split(grad)

    def update(member_ref, base):
        total = jnp.zeros((ROWS, width), jnp.float32)
        for k in range(member_ref.shape[0] // CHUNK):
            at = base + k * CHUNK
            member = member_ref[pl.ds(k * CHUNK, CHUNK), :]
            token_grad = mm(member, high) + mm(member, rest)
            local = (token_grad * slope_ref[pl.ds(at, CHUNK), :]).astype(jnp.bfloat16)
            total += mm(reduced_ref[:, at : at + CHUNK], local)
        return total

    first_part = update(member_ref, 0)
    up_ref[...] = first_part

    @pl.when(jnp.sum(real_tokens) > member_ref.shape[0])
    def _():
        up_ref[...] = first_part + update(member_rest, member_ref.shape[0])

    rnorm_own = jnp.where(group == 0, rnorm_col[0:ROWS], rnorm_col[ROWS:rows])
    chosen = iota((ROWS, ROWS), 1) == iota((ROWS, ROWS), 0) + first
    chosen = jnp.where(chosen & (iota((ROWS, ROWS), 0) < per_shard), 1.0, 0.0).astype(jnp.bfloat16)
    for o, packed in enumerate((packed0, packed1, packed2, packed3)):
        halves = [
            packed[rows + part * ROWS : rows + (part + 1) * ROWS, :]
            for part in range(width // LANES)
        ]
        block = jnp.concatenate(halves, axis=1) * rnorm_own
        picked = mm(chosen, block.astype(jnp.bfloat16)).astype(jnp.bfloat16)
        at = pl.multiple_of(quarter_of(shard ^ o) * width, LANES)
        embed_ref[0, :, pl.ds(at, width)] = picked[0:per_shard]


def any_spec():
    return pl.BlockSpec(memory_space=pl.ANY)


def vmem_spec():
    return pl.BlockSpec(memory_space=pltpu.VMEM)


def smem_spec():
    return pl.BlockSpec(memory_space=pltpu.SMEM)


def exchange(x, axis, size):
    steps = [[(i, i ^ o) for i in range(size)] for o in range(1, size)]
    return [x] + [lax.ppermute(x, axis, step) for step in steps]


def split_body(
    query_passage_words,
    difficult_distractors,
    vocabulary_vectors,
    layer_weight_matrix,
    lowering_factor_matrix,
    raising_factor_matrix,
    logit_sharpness,
):
    shards, parts = lax.axis_size("dp"), lax.axis_size("mp")
    ids = query_passage_words[0]
    texts, length = ids.shape
    tokens = texts * length
    features, vocab = vocabulary_vectors.shape
    blocks = vocab // IDS_PER_BLOCK
    group_rows = 8 * pl.cdiv(vocab // IDS_PER_GROUP + 1, 8)
    per_shard, negatives = difficult_distractors.shape
    rank = lowering_factor_matrix.shape[0]
    part_width = layer_weight_matrix.shape[1]
    width = part_width // shards
    params = pltpu.CompilerParams(vmem_limit_bytes=VMEM_BYTES)
    other_core = [(d, d ^ 1) for d in range(shards)]
    other_y = [(d, d ^ 2) for d in range(shards)]

    def columns(i, j):
        start = split_quarter(i, j) * width
        return lax.dynamic_slice(layer_weight_matrix, (0, start), (features, width))

    def project(base, span):
        stripes = pl.cdiv(span, STRIPE)
        extra_rows = (stripes + 1 + shards) * ROWS
        turned, member, extra = pl.pallas_call(
            functools.partial(gather_kernel, base=base),
            out_shape=[
                jax.ShapeDtypeStruct((features, span), jnp.bfloat16),
                jax.ShapeDtypeStruct((span, LANES), jnp.bfloat16),
                jax.ShapeDtypeStruct((extra_rows, STRIPE), jnp.bfloat16),
            ],
            in_specs=[vmem_spec()] * 2 + [any_spec()] * 2,
            out_specs=[vmem_spec()] * 3,
            scratch_shapes=[
                pltpu.VMEM((blocks, features, IDS_PER_BLOCK), jnp.bfloat16),
                pltpu.VMEM((rank, features), jnp.bfloat16),
                pltpu.VMEM((8 * pl.cdiv(span // LANES, 8), LANES), jnp.int32),
                pltpu.VMEM((LANES, LANES), jnp.float32),
                pltpu.VMEM((texts, length), jnp.float32),
                pltpu.VMEM((group_rows, length), jnp.int32),
                pltpu.SMEM((group_rows, length), jnp.int32),
                pltpu.SemaphoreType.DMA((blocks,)),
                pltpu.SemaphoreType.DMA,
                pltpu.SemaphoreType.DMA,
            ],
            compiler_params=params,
            name="gather",
        )(ids, difficult_distractors, vocabulary_vectors, lowering_factor_matrix)

        def product(turned, i, j):
            return mm(turned, columns(i, j), (((0,), (0,)), ((), ())))

        def narrow(x):
            return x.astype(jnp.bfloat16)

        chip = extra.astype(jnp.float32)
        chip += lax.ppermute(extra, "dp", other_core).astype(jnp.float32)
        extra = chip + lax.ppermute(narrow(chip), "dp", other_y).astype(jnp.float32)
        core1 = lax.ppermute(narrow(product(turned, 1, 1)), "dp", other_core)
        chip1 = narrow(product(turned, 0, 1) + core1.astype(jnp.float32))
        far = lax.ppermute(chip1, "dp", other_y)
        turned, _ = lax.optimization_barrier((turned, chip1))
        core0 = lax.ppermute(narrow(product(turned, 1, 0)), "dp", other_core)
        own0 = narrow(product(turned, 0, 0))
        return own0, core0, far, extra, member

    first = project(0, FIRST)
    later, _ = lax.optimization_barrier((ids, first[0]))
    many = jnp.sum((later != 0).astype(jnp.int32)) > FIRST
    left = tokens - FIRST
    shapes = jax.eval_shape(lambda: project(FIRST, left))
    rest = lax.cond(
        many,
        lambda: project(FIRST, left),
        lambda: tuple(jnp.zeros(x.shape, x.dtype) for x in shapes),
    )
    pooled, slope, reduced, misc = pl.pallas_call(
        functools.partial(pool_kernel, model_width=float(features * shards)),
        out_shape=[
            jax.ShapeDtypeStruct((ROWS, width), jnp.bfloat16),
            jax.ShapeDtypeStruct((tokens, width), jnp.float32),
            jax.ShapeDtypeStruct((ROWS, tokens), jnp.bfloat16),
            jax.ShapeDtypeStruct((ROWS, width), jnp.float32),
        ],
        in_specs=[vmem_spec()] * 12,
        out_specs=[vmem_spec()] * 4,
        scratch_shapes=[
            pltpu.VMEM((LANES, width), jnp.bfloat16),
            pltpu.VMEM((ROWS, width), jnp.float32),
        ],
        compiler_params=params,
        name="pool",
    )(ids, *first, *rest, raising_factor_matrix)
    member, member_rest = first[4], rest[4]
    far_side = lax.ppermute(pooled, "group", [(0, 1), (1, 0)])
    rows = 2 * ROWS
    packed = pl.pallas_call(
        dots_kernel,
        out_shape=jax.ShapeDtypeStruct((rows + width // LANES * ROWS, LANES), jnp.float32),
        in_specs=[vmem_spec()] * 2,
        out_specs=vmem_spec(),
        compiler_params=params,
        name="dots",
    )(pooled, far_side)
    packed = exchange(packed, "dp", shards)
    dots = [x[0:rows] for x in packed]
    dots = exchange((dots[0] + dots[1]) + (dots[2] + dots[3]), "mp", parts)
    embeddings, losses, update = pl.pallas_call(
        functools.partial(score_kernel, negatives=negatives),
        out_shape=[
            jax.ShapeDtypeStruct((1, per_shard, part_width), jnp.bfloat16),
            jax.ShapeDtypeStruct((1, per_shard), jnp.float32),
            jax.ShapeDtypeStruct((ROWS, width), jnp.float32),
        ],
        in_specs=[vmem_spec()] * 16 + [smem_spec()],
        out_specs=[vmem_spec()] * 3,
        compiler_params=params,
        name="score",
    )(
        ids,
        pooled,
        far_side,
        *packed,
        *dots,
        misc,
        slope,
        reduced,
        member,
        member_rest,
        logit_sharpness,
    )
    update = update + lax.ppermute(update, "group", [(0, 1), (1, 0)])
    updates = exchange(update, "dp", shards)
    shard = lax.axis_index("dp")
    columns = [lax.select_n(shard ^ quarter_of(q), *updates) for q in range(shards)]
    return (embeddings, losses, jnp.concatenate(columns, axis=1))


def body(words, hard, vocabulary, weight, lowering, raising, sharpness):
    shards, parts = lax.axis_size("dp"), lax.axis_size("mp")
    texts, length = words.shape[1:]
    features, vocab = vocabulary.shape
    negatives = hard.shape[1]
    square = shards == 4 and features == weight.shape[1] == 4 * STRIPE and parts == shards
    small = texts <= ROWS - 2 and length == LANES and FIRST < texts * length <= 2048
    even = (texts * length - FIRST) % CHUNK == 0 and vocab % IDS_PER_BLOCK == 0
    fits = features * vocab <= 2**24 and features % (4 * LANES) == 0
    spare = pl.cdiv(FIRST, STRIPE) + negatives <= ROWS and lowering.shape[0] == ROWS
    fast = square and small and even and fits and spare and lax.axis_size("group") == 2
    chosen = split_body if fast else general_body
    return chosen(words, hard, vocabulary, weight, lowering, raising, sharpness)


def solution(mesh):
    in_specs = (
        P("group", None, None),
        P("dp", None),
        P("dp", None),
        P("dp", "mp"),
        P(),
        P(None, "mp"),
        P(),
    )
    out_specs = (P("group", "dp", "mp"), P("group", "dp"), P(None, "mp"))
    return jax.shard_map(body, mesh=mesh, in_specs=in_specs, out_specs=out_specs, check_vma=False)
```

```python
import functools

import jax
import jax.numpy as jnp
from jax import lax
from jax.experimental import pallas as pl
from jax.experimental.pallas import tpu as pltpu
from jax.sharding import PartitionSpec as P


def general_body(
    query_passage_words,
    difficult_distractors,
    vocabulary_vectors,
    layer_weight_matrix,
    lowering_factor_matrix,
    raising_factor_matrix,
    logit_sharpness,
):
    group_index = lax.axis_index("group")
    shard_index = lax.axis_index("dp")
    part_index = lax.axis_index("mp")
    shard_count = lax.axis_size("dp")
    side_ids = query_passage_words[0]
    text_count = side_ids.shape[0]
    length = side_ids.shape[1]
    per_shard = text_count // shard_count
    own_ids = lax.dynamic_slice_in_dim(side_ids, shard_index * per_shard, per_shard, 0)
    columns = jnp.take(vocabulary_vectors, side_ids.reshape(-1), axis=1)
    inputs = lax.all_to_all(columns, "dp", split_axis=1, concat_axis=0, tiled=True)
    tokens = inputs.shape[1]
    feature_width = raising_factor_matrix.shape[1]
    wide_inputs = inputs.astype(jnp.float32)
    inverse = lax.rsqrt(jnp.mean(wide_inputs * wide_inputs, axis=0) + 1e-05)
    normed_state = (wide_inputs * inverse[None, :]).astype(jnp.bfloat16)
    linear_map = lax.dot_general(
        lax.all_gather(layer_weight_matrix, "dp", axis=0, tiled=True),
        normed_state,
        (((0,), (0,)), ((), ())),
        preferred_element_type=jnp.float32,
    )
    reduced_sum = jnp.dot(
        lowering_factor_matrix, normed_state, preferred_element_type=jnp.float32
    ).astype(jnp.bfloat16)
    linear_map = linear_map + lax.dot_general(
        raising_factor_matrix,
        reduced_sum,
        (((0,), (0,)), ((), ())),
        preferred_element_type=jnp.float32,
    )
    own_inputs = lax.dynamic_slice_in_dim(
        inputs, part_index * feature_width, feature_width, 0
    ).astype(jnp.float32)
    hidden_state = own_inputs + jax.nn.silu(linear_map)
    mask = (own_ids != 0).astype(jnp.float32)
    counts = jnp.sum(mask, axis=1)
    summed = jnp.einsum("dnl,nl->nd", hidden_state.reshape(feature_width, per_shard, length), mask)
    pooled = (summed / counts[:, None]).astype(jnp.bfloat16)
    gathered = lax.all_gather(pooled, ("group", "dp"), axis=0, tiled=True)
    part_scores = lax.dot_general(
        pooled, gathered, (((1,), (1,)), ((), ())), preferred_element_type=jnp.float32
    )
    gathered_wide = gathered.astype(jnp.float32)
    part_norms = jnp.sum(gathered_wide * gathered_wide, axis=1)
    dots, norms = lax.psum((part_scores, part_norms), "mp")
    rnorm_all = lax.rsqrt(norms + 1e-06)
    all_count = gathered.shape[0]
    half_count = all_count // 2
    own_rows = (
        group_index * half_count + shard_index * per_shard + jnp.arange(per_shard, dtype=jnp.int32)
    )
    rnorm_own = jnp.take(rnorm_all, own_rows)
    cosine = dots * rnorm_own[:, None] * rnorm_all[None, :]
    multiplier_factor = logit_sharpness[0]
    scores = multiplier_factor * cosine
    column_ids = jnp.arange(all_count, dtype=jnp.int32)
    keep = column_ids[None, :] != own_rows[:, None]
    pair = (own_rows + half_count) % all_count
    weight = (group_index == 0).astype(jnp.float32)
    neg_cols = half_count + difficult_distractors
    top = jnp.max(jnp.where(keep, scores, -jnp.inf), axis=1)
    safe_scores = jnp.where(keep, scores, top[:, None])
    expd = jnp.where(keep, jnp.exp(safe_scores - top[:, None]), 0.0)
    neg_exp = (
        jnp.exp(jnp.minimum(jnp.take_along_axis(scores, neg_cols, axis=1) - top[:, None], 0.0))
        * weight
    )
    total = jnp.sum(expd, axis=1) + jnp.sum(neg_exp, axis=1)
    pair_score = jnp.take_along_axis(scores, pair[:, None], axis=1)[:, 0]
    losses = top + jnp.log(total) - pair_score
    onehot = (column_ids[None, None, :] == neg_cols[:, :, None]).astype(jnp.float32)
    probs = (expd + jnp.einsum("rk,rkc->rc", neg_exp, onehot)) / total[:, None]
    target = (column_ids[None, :] == pair[:, None]).astype(jnp.float32)
    grad_scores = (probs - target) / all_count
    coeff = (grad_scores * rnorm_own[:, None] * rnorm_all[None, :]).astype(jnp.bfloat16)
    along = jnp.dot(coeff, gathered, preferred_element_type=jnp.float32)
    pooled_wide = pooled.astype(jnp.float32)
    radial = jnp.sum(grad_scores * cosine, axis=1) * rnorm_own * rnorm_own
    embedding_gradient = multiplier_factor * (along - radial[:, None] * pooled_wide)
    token_grad = jnp.einsum("nd,nl->dnl", embedding_gradient / counts[:, None], mask).reshape(
        feature_width, tokens
    )
    sigma = jax.nn.sigmoid(linear_map)
    local = (token_grad * sigma * (1.0 + linear_map * (1.0 - sigma))).astype(jnp.bfloat16)
    up_portion = lax.dot_general(
        reduced_sum, local, (((1,), (1,)), ((), ())), preferred_element_type=jnp.float32
    )
    adapter_up_gradient = lax.psum(up_portion, ("group", "dp"))
    embeddings = (pooled_wide * rnorm_own[:, None]).astype(jnp.bfloat16)[None]
    return (embeddings, losses[None], adapter_up_gradient)


BLOCK_BITS, GROUP_BITS, LANE_BITS, ROW_BITS = 10, 9, 7, 4
IDS_PER_BLOCK = 1 << BLOCK_BITS
IDS_PER_GROUP = 1 << GROUP_BITS
CHUNK = 384
STRIPE = 256
ROWS = 1 << ROW_BITS
LANES = 1 << LANE_BITS
FEATURE_ROWS = 128
FIRST = 1152
NT = (((1,), (1,)), ((), ()))
VMEM_BYTES = 60 * 1024 * 1024


def mm(a, b, dims=(((1,), (0,)), ((), ()))):
    return lax.dot_general(a, b, dims, preferred_element_type=jnp.float32)


def split(x):
    high = x.astype(jnp.bfloat16)
    return high, (x - high.astype(jnp.float32)).astype(jnp.bfloat16)


def iota(shape, dim):
    return lax.broadcasted_iota(jnp.int32, shape, dim)


def quarter_of(dp_index, cores=2):
    return (dp_index % cores) * 2 + dp_index // cores


def split_quarter(i, j, cores=2):
    shard = lax.axis_index("dp")
    core, side_y = lax.rem(shard, cores), lax.div(shard, cores)
    return (core ^ i) * 2 + (side_y ^ j)


def take_lanes(x, lanes):
    numbers = lax.GatherDimensionNumbers(
        offset_dims=(),
        collapsed_slice_dims=(1,),
        start_index_map=(1,),
        operand_batching_dims=(0,),
        start_indices_batching_dims=(0,),
    )
    mode = lax.GatherScatterMode.PROMISE_IN_BOUNDS
    return lax.gather(x, lanes[..., None], numbers, slice_sizes=(1, 1), mode=mode)


def gather_kernel(
    ids_ref,
    vocab_ref,
    turned,
    member_ref,
    held,
    token_ref,
    ranks,
    counted,
    bounds,
    held_sems,
    bounds_sem,
    base,
):
    texts, length = ids_ref.shape
    features, vocab = vocab_ref.shape
    blocks = vocab // IDS_PER_BLOCK
    groups = vocab // IDS_PER_GROUP
    span = member_ref.shape[0]

    def vocab_copy(b):
        columns = pl.ds(pl.multiple_of(b * IDS_PER_BLOCK, LANES), IDS_PER_BLOCK)
        return pltpu.make_async_copy(vocab_ref.at[:, columns], held.at[b], held_sems.at[b])

    vocab_copy(0).start()
    for b in range(1, blocks):
        vocab_copy(b).start()

    ids = ids_ref[...]
    valid = ids != 0
    group_of = jnp.where(valid, lax.shift_right_logical(ids, GROUP_BITS), groups)
    group_rows = counted.shape[0]
    group_id = iota((group_rows, length), 0)
    below = jnp.zeros((group_rows, length), jnp.float32)
    for text in range(texts):
        below += jnp.where(group_of[text : text + 1] < group_id, 1.0, 0.0)
    before = jnp.broadcast_to(jnp.sum(below, axis=1, keepdims=True), (group_rows, length))
    counted[...] = before.astype(jnp.int32)
    bounds_copy = pltpu.make_async_copy(counted, bounds, bounds_sem)
    bounds_copy.start()
    earlier = jnp.where(iota((length, length), 0) < iota((length, length), 1), 1.0, 0.0).astype(
        jnp.bfloat16
    )
    for text in range(texts):
        here = jnp.where(group_of[text : text + 1] == group_id, 1.0, 0.0)
        inside = mm(here.astype(jnp.bfloat16), earlier)
        ranks[pl.ds(text, 1), :] = jnp.sum(here * (inside + before), axis=0, keepdims=True)
        before += jnp.broadcast_to(jnp.sum(here, axis=1, keepdims=True), (group_rows, length))
    text_of = iota((texts, length), 0)
    carried = jnp.where(valid, lax.shift_left(ids, ROW_BITS) + text_of, 0).astype(jnp.float32)
    rank = ranks[...]

    def place(p, carry):
        position = (iota((LANES, length), 0) + (p * LANES + base)).astype(jnp.float32)
        total = jnp.zeros((LANES, length), jnp.float32)
        for text in range(texts):
            total += jnp.where(rank[text : text + 1] == position, carried[text : text + 1], 0.0)
        found = jnp.broadcast_to(jnp.sum(total, axis=1, keepdims=True), (LANES, LANES))
        start = pl.multiple_of(p * LANES, LANES)
        row = found.T[0:1].astype(jnp.int32)
        token = lax.shift_right_logical(row, ROW_BITS)
        token_ref[pl.ds(p, 1), :] = jnp.where(token == 0, -vocab, token)
        found = found.astype(jnp.int32)
        real = (found >= ROWS) & ((found & (ROWS - 1)) == iota((LANES, LANES), 1))
        member_ref[pl.ds(start, LANES), :] = jnp.where(real, 1.0, 0.0).astype(jnp.bfloat16)
        turned[:, pl.ds(start, LANES)] = jnp.zeros((features, LANES), jnp.bfloat16)
        return carry

    lax.fori_loop(0, span // LANES, place, 0)
    bounds_copy.wait()

    def within(place):
        return jnp.clip(place - base, 0, span)

    def take(b, carry):
        vocab_copy(b).wait()
        for part in range(IDS_PER_BLOCK // IDS_PER_GROUP):
            group = b * (IDS_PER_BLOCK // IDS_PER_GROUP) + part
            first, last = within(bounds[group, 0]), within(bounds[group + 1, 0])
            begin = lax.shift_right_logical(first, LANE_BITS)
            end = lax.shift_right_logical(last + LANES - 1, LANE_BITS)

            def window(p, carry):
                at = pl.ds(pl.multiple_of(p * LANES, LANES), LANES)
                token = token_ref[pl.ds(p, 1), :] - group * IDS_PER_GROUP
                token = jnp.broadcast_to(token, (FEATURE_ROWS, LANES))
                lane = (token & (LANES - 1)).astype(jnp.int16)
                tile = lax.shift_right_arithmetic(token, LANE_BITS).astype(jnp.int16)
                pieces = [pl.ds(f, FEATURE_ROWS) for f in range(0, features, FEATURE_ROWS)]
                fresh = []
                for rows in pieces:
                    total = jnp.zeros((FEATURE_ROWS, LANES), jnp.bfloat16)
                    for j in range(IDS_PER_GROUP // LANES):
                        columns = pl.ds(part * IDS_PER_GROUP + j * LANES, LANES)
                        total = jnp.where(tile == j, take_lanes(held[b, rows, columns], lane), total)
                    fresh.append(total)
                fresh = [turned[rows, at] + total for rows, total in zip(pieces, fresh)]
                for rows, total in zip(pieces, fresh):
                    turned[rows, at] = total
                return carry

            lax.fori_loop(begin, jnp.where(last > first, end, begin), window, 0)
        return carry

    lax.fori_loop(0, blocks, take, 0)


def statistics_kernel(turned, member_ref, hard_ref, lower_ref, extra_ref, small):
    features, span = turned.shape
    stripes = pl.cdiv(span, STRIPE)
    per_shard, negatives = hard_ref.shape
    shard = lax.axis_index("dp")
    small[...] = jnp.zeros_like(small)
    small[0:per_shard, stripes : stripes + negatives] = hard_ref[...].astype(jnp.float32)
    lower = lower_ref[:, pl.ds(pl.multiple_of(shard * features, LANES), features)]

    misc = jnp.zeros((ROWS, STRIPE), jnp.float32)
    residual = jnp.zeros((features, LANES), jnp.float32)
    for stripe in range(stripes):
        size = min(STRIPE, span - stripe * STRIPE)
        across = pl.ds(stripe * STRIPE, size)
        upright = turned[:, across]
        wide = upright.astype(jnp.float32)
        square = jnp.sum(wide * wide, axis=0, keepdims=True)
        reduced = mm(lower, upright)
        if size < STRIPE:
            none = jnp.zeros((ROWS, STRIPE - size), jnp.float32)
            reduced = jnp.concatenate([reduced, none], axis=1)
            square = jnp.concatenate([square, none[0:1]], axis=1)
        extra_ref[stripe * ROWS : (stripe + 1) * ROWS, :] = reduced.astype(jnp.bfloat16)
        misc = jnp.where(iota((ROWS, STRIPE), 0) == stripe, square, misc)
        residual += mm(upright, member_ref[across, :])
    hard = small[...].T[0:ROWS]
    for i in range(per_shard):
        misc += jnp.where(iota((ROWS, STRIPE), 1) == shard * per_shard + i, hard[:, i : i + 1], 0.0)
    extra_ref[stripes * ROWS : (stripes + 1) * ROWS, :] = misc.astype(jnp.bfloat16)
    residual = jnp.where(lax.axis_index("mp") == shard, residual.T[0:ROWS], 0.0)
    for q in range(features // STRIPE):
        start = (stripes + 1 + q) * ROWS
        extra_ref[start : start + ROWS, :] = residual[:, q * STRIPE : (q + 1) * STRIPE].astype(
            jnp.bfloat16
        )


def pool_kernel(
    ids_ref,
    own_ref,
    core_ref,
    far_ref,
    extra_ref,
    member_ref,
    own_rest,
    core_rest,
    far_rest,
    extra_rest,
    member_rest,
    raise_ref,
    pooled_ref,
    slope_ref,
    reduced_ref,
    misc_ref,
    raised,
    total,
    model_width,
):
    texts, length = ids_ref.shape
    width = own_ref.shape[1]
    quarter = quarter_of(lax.axis_index("dp"))
    raised[...] = jnp.zeros_like(raised)
    raised[0:ROWS, :] = raise_ref[:, pl.ds(pl.multiple_of(quarter * width, LANES), width)]
    total[...] = jnp.zeros_like(total)

    def add(refs, extra_ref, member_ref, base):
        span = member_ref.shape[0]
        stripes = pl.cdiv(span, STRIPE)

        def summed(start, size):
            return sum(ref[pl.ds(start, size), :].astype(jnp.float32) for ref in refs)

        misc = extra_ref[stripes * ROWS : (stripes + 1) * ROWS, :]
        if base == 0:
            misc_ref[...] = misc
        inverse = lax.rsqrt(misc / model_width + 1e-05)
        for k in range(stripes):
            at = base + k * STRIPE
            size = min(STRIPE, span - k * STRIPE)
            scale = inverse[k : k + 1]
            reduced = (extra_ref[k * ROWS : (k + 1) * ROWS, :] * scale).astype(jnp.bfloat16)
            reduced_ref[:, at : at + size] = reduced[:, 0:size]
            stacked = jnp.concatenate(
                [reduced.astype(jnp.float32), jnp.broadcast_to(scale, (LANES - ROWS, STRIPE))]
            )
            turned = stacked[:, 0:size].T
            low = turned.astype(jnp.bfloat16)
            linear = summed(k * STRIPE, size) * turned[:, ROWS : ROWS + 1] + mm(low, raised[...])
            sigma = 1.0 / (1.0 + jnp.exp(-linear))
            slope_ref[pl.ds(at, size), :] = sigma * (1.0 + linear * (1.0 - sigma))
            member = member_ref[pl.ds(k * STRIPE, size), :].astype(jnp.float32).T
            member = member[0:ROWS].astype(jnp.bfloat16)
            high, rest = split(linear * sigma)
            total[...] += mm(member, high) + mm(member, rest)
        start = pl.multiple_of((stripes + 1 + quarter) * ROWS, ROWS)
        total[...] += extra_ref[pl.ds(start, ROWS), :]

    add((own_ref, core_ref, far_ref), extra_ref, member_ref, 0)
    real = (ids_ref[...] != 0).astype(jnp.float32)

    @pl.when(jnp.sum(real) > member_ref.shape[0])
    def _():
        add((own_rest, core_rest, far_rest), extra_rest, member_rest, member_ref.shape[0])

    counts = jnp.sum(real, axis=1, keepdims=True)
    pooled = total[0:texts] / counts
    pooled = jnp.concatenate([pooled, jnp.zeros((ROWS - texts, width), jnp.float32)])
    pooled_ref[...] = pooled.astype(jnp.bfloat16)


def both_sides(near, far):
    queries = lax.axis_index("group") == 0
    return jnp.concatenate([jnp.where(queries, near, far), jnp.where(queries, far, near)], axis=0)


def dots_kernel(near_ref, far_ref, packed_ref):
    near = near_ref[...]
    block = both_sides(near, far_ref[...])
    dots = mm(block, block, NT)
    rows = 2 * ROWS
    packed_ref[...] = jnp.zeros_like(packed_ref)
    packed_ref[0:rows, 0:rows] = dots
    for part in range(near.shape[1] // LANES):
        start = rows + part * ROWS
        packed_ref[start : start + ROWS, :] = near[:, part * LANES : (part + 1) * LANES].astype(
            jnp.float32
        )


def score_kernel(
    ids_ref,
    near_ref,
    far_ref,
    packed0,
    packed1,
    packed2,
    packed3,
    dots0,
    dots1,
    dots2,
    dots3,
    misc_ref,
    slope_ref,
    reduced_ref,
    member_ref,
    member_rest,
    sharp_ref,
    embed_ref,
    loss_ref,
    up_ref,
    negatives,
):
    texts, length = ids_ref.shape
    stripes = pl.cdiv(member_ref.shape[0], STRIPE)
    rows = 2 * ROWS
    width = near_ref.shape[1]
    per_shard = loss_ref.shape[1]
    group, shard = lax.axis_index("group"), lax.axis_index("dp")
    dots = ((dots0[...] + dots1[...]) + (dots2[...] + dots3[...]))[:, 0:rows]
    down, across = iota((rows, rows), 0), iota((rows, rows), 1)
    same = down == across
    real = (lax.rem(down, ROWS) < texts) & (lax.rem(across, ROWS) < texts)
    diagonal = jnp.where(same, dots, 0.0)
    rnorm_row = lax.rsqrt(jnp.sum(diagonal, axis=0, keepdims=True) + 1e-06)
    rnorm_col = lax.rsqrt(jnp.sum(diagonal, axis=1, keepdims=True) + 1e-06)
    sharpness = sharp_ref[0]
    cosine = dots * rnorm_col * rnorm_row
    scores = sharpness * cosine
    keep = real & ~same
    top = jnp.max(jnp.where(keep, scores, -jnp.inf), axis=0, keepdims=True)
    top = jnp.where(lax.rem(across[0:1], ROWS) < texts, top, 0.0)
    powers = jnp.exp(jnp.where(real, jnp.minimum(scores - top, 0.0), 0.0))
    hard = misc_ref[stripes : stripes + negatives, 0:rows].astype(jnp.int32) + ROWS
    times = jnp.zeros((rows, rows), jnp.float32)
    for k in range(negatives):
        times += jnp.where(hard[k : k + 1] == down, 1.0, 0.0)
    times = jnp.where(across < texts, times, 0.0)
    weights = (jnp.where(keep, 1.0, 0.0) + jnp.where(real, times, 0.0)) * powers
    total = jnp.sum(weights, axis=0, keepdims=True)
    total = jnp.where(lax.rem(across[0:1], ROWS) < texts, total, 1.0)
    pair = (down == lax.rem(across + ROWS, rows)) & real
    pair_score = jnp.sum(jnp.where(pair, scores, 0.0), axis=0, keepdims=True)
    losses = top + jnp.log(total) - pair_score
    grad_scores = (weights / total - jnp.where(pair, 1.0, 0.0)) / (2 * texts)
    coeff = (grad_scores * rnorm_col * rnorm_row).astype(jnp.bfloat16)
    radial = jnp.sum(grad_scores * cosine, axis=0, keepdims=True) * rnorm_row * rnorm_row

    first = shard * per_shard
    loss_col = jnp.sum(jnp.where(same, losses, 0.0), axis=1, keepdims=True)
    at = (iota((rows, LANES), 0) == group * ROWS + first + iota((rows, LANES), 1)) & (
        iota((rows, LANES), 1) < per_shard
    )
    loss_ref[...] = jnp.sum(jnp.where(at, loss_col, 0.0), axis=0, keepdims=True)[:, 0:per_shard]

    mine = both_sides(near_ref[...], far_ref[...])
    along = mm(coeff.astype(jnp.float32).T.astype(jnp.bfloat16), mine)
    radial_col = jnp.sum(jnp.where(same, radial, 0.0), axis=1, keepdims=True)
    grad = sharpness * (along - radial_col * mine.astype(jnp.float32))
    grad = jnp.where(group == 0, grad[0:ROWS], grad[ROWS:rows])
    real_tokens = (ids_ref[...] != 0).astype(jnp.float32)
    counts = jnp.sum(real_tokens, axis=1, keepdims=True)
    grad = grad[0:texts] / counts
    grad = jnp.concatenate([grad, jnp.zeros((LANES - texts, width), jnp.float32)])
    high, rest = split(grad)

    def update(member_ref, base):
        total = jnp.zeros((ROWS, width), jnp.float32)
        for k in range(member_ref.shape[0] // CHUNK):
            at = base + k * CHUNK
            member = member_ref[pl.ds(k * CHUNK, CHUNK), :]
            token_grad = mm(member, high) + mm(member, rest)
            local = (token_grad * slope_ref[pl.ds(at, CHUNK), :]).astype(jnp.bfloat16)
            total += mm(reduced_ref[:, at : at + CHUNK], local)
        return total

    first_part = update(member_ref, 0)
    up_ref[...] = first_part

    @pl.when(jnp.sum(real_tokens) > member_ref.shape[0])
    def _():
        up_ref[...] = first_part + update(member_rest, member_ref.shape[0])

    rnorm_own = jnp.where(group == 0, rnorm_col[0:ROWS], rnorm_col[ROWS:rows])
    chosen = iota((ROWS, ROWS), 1) == iota((ROWS, ROWS), 0) + first
    chosen = jnp.where(chosen & (iota((ROWS, ROWS), 0) < per_shard), 1.0, 0.0).astype(jnp.bfloat16)
    for o, packed in enumerate((packed0, packed1, packed2, packed3)):
        halves = [
            packed[rows + part * ROWS : rows + (part + 1) * ROWS, :]
            for part in range(width // LANES)
        ]
        block = jnp.concatenate(halves, axis=1) * rnorm_own
        picked = mm(chosen, block.astype(jnp.bfloat16)).astype(jnp.bfloat16)
        at = pl.multiple_of(quarter_of(shard ^ o) * width, LANES)
        embed_ref[0, :, pl.ds(at, width)] = picked[0:per_shard]


def any_spec():
    return pl.BlockSpec(memory_space=pl.ANY)


def vmem_spec():
    return pl.BlockSpec(memory_space=pltpu.VMEM)


def smem_spec():
    return pl.BlockSpec(memory_space=pltpu.SMEM)


def exchange(x, axis, size):
    steps = [[(i, i ^ o) for i in range(size)] for o in range(1, size)]
    return [x] + [lax.ppermute(x, axis, step) for step in steps]


def split_body(
    query_passage_words,
    difficult_distractors,
    vocabulary_vectors,
    layer_weight_matrix,
    lowering_factor_matrix,
    raising_factor_matrix,
    logit_sharpness,
):
    shards, parts = lax.axis_size("dp"), lax.axis_size("mp")
    ids = query_passage_words[0]
    texts, length = ids.shape
    tokens = texts * length
    features, vocab = vocabulary_vectors.shape
    blocks = vocab // IDS_PER_BLOCK
    group_rows = 8 * pl.cdiv(vocab // IDS_PER_GROUP + 1, 8)
    per_shard, negatives = difficult_distractors.shape
    part_width = layer_weight_matrix.shape[1]
    width = part_width // shards
    params = pltpu.CompilerParams(vmem_limit_bytes=VMEM_BYTES)
    other_core = [(d, d ^ 1) for d in range(shards)]
    other_y = [(d, d ^ 2) for d in range(shards)]

    def columns(i, j):
        start = split_quarter(i, j) * width
        return lax.dynamic_slice(layer_weight_matrix, (0, start), (features, width))

    def project(base, span):
        stripes = pl.cdiv(span, STRIPE)
        extra_rows = (stripes + 1 + shards) * ROWS
        turned, member = pl.pallas_call(
            functools.partial(gather_kernel, base=base),
            out_shape=[
                jax.ShapeDtypeStruct((features, span), jnp.bfloat16),
                jax.ShapeDtypeStruct((span, LANES), jnp.bfloat16),
            ],
            in_specs=[vmem_spec(), any_spec()],
            out_specs=[vmem_spec()] * 2,
            scratch_shapes=[
                pltpu.VMEM((blocks, features, IDS_PER_BLOCK), jnp.bfloat16),
                pltpu.VMEM((8 * pl.cdiv(span // LANES, 8), LANES), jnp.int32),
                pltpu.VMEM((texts, length), jnp.float32),
                pltpu.VMEM((group_rows, length), jnp.int32),
                pltpu.SMEM((group_rows, length), jnp.int32),
                pltpu.SemaphoreType.DMA((blocks,)),
                pltpu.SemaphoreType.DMA,
            ],
            compiler_params=params,
            name="gather",
        )(ids, vocabulary_vectors)

        def product(turned, i, j):
            return mm(turned, columns(i, j), (((0,), (0,)), ((), ())))

        def narrow(x):
            return x.astype(jnp.bfloat16)

        core1 = lax.ppermute(narrow(product(turned, 1, 1)), "dp", other_core)
        chip1 = narrow(product(turned, 0, 1) + core1.astype(jnp.float32))
        far = lax.ppermute(chip1, "dp", other_y)
        turned, _ = lax.optimization_barrier((turned, chip1))
        extra = pl.pallas_call(
            statistics_kernel,
            out_shape=jax.ShapeDtypeStruct((extra_rows, STRIPE), jnp.bfloat16),
            in_specs=[vmem_spec()] * 4,
            out_specs=vmem_spec(),
            scratch_shapes=[pltpu.VMEM((LANES, LANES), jnp.float32)],
            compiler_params=params,
            cost_estimate=pl.CostEstimate(
                flops=2 * features * span * (ROWS + LANES),
                bytes_accessed=2 * features * span,
                transcendentals=0,
            ),
            name="statistics",
        )(turned, member, difficult_distractors, lowering_factor_matrix)
        chip = extra.astype(jnp.float32)
        chip += lax.ppermute(extra, "dp", other_core).astype(jnp.float32)
        extra = chip + lax.ppermute(narrow(chip), "dp", other_y).astype(jnp.float32)
        core0 = lax.ppermute(narrow(product(turned, 1, 0)), "dp", other_core)
        own0 = narrow(product(turned, 0, 0))
        return (own0, core0, far, extra, member), chip

    first, early = project(0, FIRST)
    later, _ = lax.optimization_barrier((ids, early))
    many = jnp.sum((later != 0).astype(jnp.int32)) > FIRST
    left = tokens - FIRST
    shapes = jax.eval_shape(lambda: project(FIRST, left)[0])
    rest = lax.cond(
        many,
        lambda: project(FIRST, left)[0],
        lambda: tuple(jnp.zeros(x.shape, x.dtype) for x in shapes),
    )
    pooled, slope, reduced, misc = pl.pallas_call(
        functools.partial(pool_kernel, model_width=float(features * shards)),
        out_shape=[
            jax.ShapeDtypeStruct((ROWS, width), jnp.bfloat16),
            jax.ShapeDtypeStruct((tokens, width), jnp.float32),
            jax.ShapeDtypeStruct((ROWS, tokens), jnp.bfloat16),
            jax.ShapeDtypeStruct((ROWS, width), jnp.float32),
        ],
        in_specs=[vmem_spec()] * 12,
        out_specs=[vmem_spec()] * 4,
        scratch_shapes=[
            pltpu.VMEM((LANES, width), jnp.bfloat16),
            pltpu.VMEM((ROWS, width), jnp.float32),
        ],
        compiler_params=params,
        name="pool",
    )(ids, *first, *rest, raising_factor_matrix)
    member, member_rest = first[4], rest[4]
    far_side = lax.ppermute(pooled, "group", [(0, 1), (1, 0)])
    rows = 2 * ROWS
    packed = pl.pallas_call(
        dots_kernel,
        out_shape=jax.ShapeDtypeStruct((rows + width // LANES * ROWS, LANES), jnp.float32),
        in_specs=[vmem_spec()] * 2,
        out_specs=vmem_spec(),
        compiler_params=params,
        name="dots",
    )(pooled, far_side)
    packed = exchange(packed, "dp", shards)
    dots = [x[0:rows] for x in packed]
    dots = exchange((dots[0] + dots[1]) + (dots[2] + dots[3]), "mp", parts)
    embeddings, losses, update = pl.pallas_call(
        functools.partial(score_kernel, negatives=negatives),
        out_shape=[
            jax.ShapeDtypeStruct((1, per_shard, part_width), jnp.bfloat16),
            jax.ShapeDtypeStruct((1, per_shard), jnp.float32),
            jax.ShapeDtypeStruct((ROWS, width), jnp.float32),
        ],
        in_specs=[vmem_spec()] * 16 + [smem_spec()],
        out_specs=[vmem_spec()] * 3,
        compiler_params=params,
        name="score",
    )(
        ids,
        pooled,
        far_side,
        *packed,
        *dots,
        misc,
        slope,
        reduced,
        member,
        member_rest,
        logit_sharpness,
    )
    update = update + lax.ppermute(update, "group", [(0, 1), (1, 0)])
    updates = exchange(update, "dp", shards)
    shard = lax.axis_index("dp")
    columns = [lax.select_n(shard ^ quarter_of(q), *updates) for q in range(shards)]
    return (embeddings, losses, jnp.concatenate(columns, axis=1))


def body(words, hard, vocabulary, weight, lowering, raising, sharpness):
    shards, parts = lax.axis_size("dp"), lax.axis_size("mp")
    texts, length = words.shape[1:]
    features, vocab = vocabulary.shape
    negatives = hard.shape[1]
    square = shards == 4 and features == weight.shape[1] == 4 * STRIPE and parts == shards
    small = texts <= ROWS - 2 and length == LANES and FIRST < texts * length <= 2048
    even = (texts * length - FIRST) % CHUNK == 0 and vocab % IDS_PER_BLOCK == 0
    fits = features * vocab <= 2**24 and features % (4 * LANES) == 0
    spare = pl.cdiv(FIRST, STRIPE) + negatives <= ROWS and lowering.shape[0] == ROWS
    fast = square and small and even and fits and spare and lax.axis_size("group") == 2
    chosen = split_body if fast else general_body
    return chosen(words, hard, vocabulary, weight, lowering, raising, sharpness)


def solution(mesh):
    in_specs = (
        P("group", None, None),
        P("dp", None),
        P("dp", None),
        P("dp", "mp"),
        P(),
        P(None, "mp"),
        P(),
    )
    out_specs = (P("group", "dp", "mp"), P("group", "dp"), P(None, "mp"))
    return jax.shard_map(body, mesh=mesh, in_specs=in_specs, out_specs=out_specs, check_vma=False)
```

```python
import functools

import jax
import jax.numpy as jnp
from jax import lax
from jax.experimental import pallas as pl
from jax.experimental.pallas import tpu as pltpu
from jax.sharding import PartitionSpec as P


def general_body(
    query_passage_words,
    difficult_distractors,
    vocabulary_vectors,
    layer_weight_matrix,
    lowering_factor_matrix,
    raising_factor_matrix,
    logit_sharpness,
):
    group_index = lax.axis_index("group")
    shard_index = lax.axis_index("dp")
    part_index = lax.axis_index("mp")
    shard_count = lax.axis_size("dp")
    side_ids = query_passage_words[0]
    text_count = side_ids.shape[0]
    length = side_ids.shape[1]
    per_shard = text_count // shard_count
    own_ids = lax.dynamic_slice_in_dim(side_ids, shard_index * per_shard, per_shard, 0)
    columns = jnp.take(vocabulary_vectors, side_ids.reshape(-1), axis=1)
    inputs = lax.all_to_all(columns, "dp", split_axis=1, concat_axis=0, tiled=True)
    tokens = inputs.shape[1]
    feature_width = raising_factor_matrix.shape[1]
    wide_inputs = inputs.astype(jnp.float32)
    inverse = lax.rsqrt(jnp.mean(wide_inputs * wide_inputs, axis=0) + 1e-05)
    normed_state = (wide_inputs * inverse[None, :]).astype(jnp.bfloat16)
    linear_map = lax.dot_general(
        lax.all_gather(layer_weight_matrix, "dp", axis=0, tiled=True),
        normed_state,
        (((0,), (0,)), ((), ())),
        preferred_element_type=jnp.float32,
    )
    reduced_sum = jnp.dot(
        lowering_factor_matrix, normed_state, preferred_element_type=jnp.float32
    ).astype(jnp.bfloat16)
    linear_map = linear_map + lax.dot_general(
        raising_factor_matrix,
        reduced_sum,
        (((0,), (0,)), ((), ())),
        preferred_element_type=jnp.float32,
    )
    own_inputs = lax.dynamic_slice_in_dim(
        inputs, part_index * feature_width, feature_width, 0
    ).astype(jnp.float32)
    hidden_state = own_inputs + jax.nn.silu(linear_map)
    mask = (own_ids != 0).astype(jnp.float32)
    counts = jnp.sum(mask, axis=1)
    summed = jnp.einsum("dnl,nl->nd", hidden_state.reshape(feature_width, per_shard, length), mask)
    pooled = (summed / counts[:, None]).astype(jnp.bfloat16)
    gathered = lax.all_gather(pooled, ("group", "dp"), axis=0, tiled=True)
    part_scores = lax.dot_general(
        pooled, gathered, (((1,), (1,)), ((), ())), preferred_element_type=jnp.float32
    )
    gathered_wide = gathered.astype(jnp.float32)
    part_norms = jnp.sum(gathered_wide * gathered_wide, axis=1)
    dots, norms = lax.psum((part_scores, part_norms), "mp")
    rnorm_all = lax.rsqrt(norms + 1e-06)
    all_count = gathered.shape[0]
    half_count = all_count // 2
    own_rows = (
        group_index * half_count + shard_index * per_shard + jnp.arange(per_shard, dtype=jnp.int32)
    )
    rnorm_own = jnp.take(rnorm_all, own_rows)
    cosine = dots * rnorm_own[:, None] * rnorm_all[None, :]
    multiplier_factor = logit_sharpness[0]
    scores = multiplier_factor * cosine
    column_ids = jnp.arange(all_count, dtype=jnp.int32)
    keep = column_ids[None, :] != own_rows[:, None]
    pair = (own_rows + half_count) % all_count
    weight = (group_index == 0).astype(jnp.float32)
    neg_cols = half_count + difficult_distractors
    top = jnp.max(jnp.where(keep, scores, -jnp.inf), axis=1)
    safe_scores = jnp.where(keep, scores, top[:, None])
    expd = jnp.where(keep, jnp.exp(safe_scores - top[:, None]), 0.0)
    neg_exp = (
        jnp.exp(jnp.minimum(jnp.take_along_axis(scores, neg_cols, axis=1) - top[:, None], 0.0))
        * weight
    )
    total = jnp.sum(expd, axis=1) + jnp.sum(neg_exp, axis=1)
    pair_score = jnp.take_along_axis(scores, pair[:, None], axis=1)[:, 0]
    losses = top + jnp.log(total) - pair_score
    onehot = (column_ids[None, None, :] == neg_cols[:, :, None]).astype(jnp.float32)
    probs = (expd + jnp.einsum("rk,rkc->rc", neg_exp, onehot)) / total[:, None]
    target = (column_ids[None, :] == pair[:, None]).astype(jnp.float32)
    grad_scores = (probs - target) / all_count
    coeff = (grad_scores * rnorm_own[:, None] * rnorm_all[None, :]).astype(jnp.bfloat16)
    along = jnp.dot(coeff, gathered, preferred_element_type=jnp.float32)
    pooled_wide = pooled.astype(jnp.float32)
    radial = jnp.sum(grad_scores * cosine, axis=1) * rnorm_own * rnorm_own
    embedding_gradient = multiplier_factor * (along - radial[:, None] * pooled_wide)
    token_grad = jnp.einsum("nd,nl->dnl", embedding_gradient / counts[:, None], mask).reshape(
        feature_width, tokens
    )
    sigma = jax.nn.sigmoid(linear_map)
    local = (token_grad * sigma * (1.0 + linear_map * (1.0 - sigma))).astype(jnp.bfloat16)
    up_portion = lax.dot_general(
        reduced_sum, local, (((1,), (1,)), ((), ())), preferred_element_type=jnp.float32
    )
    adapter_up_gradient = lax.psum(up_portion, ("group", "dp"))
    embeddings = (pooled_wide * rnorm_own[:, None]).astype(jnp.bfloat16)[None]
    return (embeddings, losses[None], adapter_up_gradient)


BLOCK_BITS, GROUP_BITS, LANE_BITS, ROW_BITS = 10, 9, 7, 4
IDS_PER_BLOCK = 1 << BLOCK_BITS
IDS_PER_GROUP = 1 << GROUP_BITS
CHUNK = 384
STRIPE = 256
ROWS = 1 << ROW_BITS
LANES = 1 << LANE_BITS
FEATURE_ROWS = 128
FIRST = 1152
NT = (((1,), (1,)), ((), ()))
VMEM_BYTES = 60 * 1024 * 1024


def mm(a, b, dims=(((1,), (0,)), ((), ()))):
    return lax.dot_general(a, b, dims, preferred_element_type=jnp.float32)


def split(x):
    high = x.astype(jnp.bfloat16)
    return high, (x - high.astype(jnp.float32)).astype(jnp.bfloat16)


def iota(shape, dim):
    return lax.broadcasted_iota(jnp.int32, shape, dim)


def quarter_of(dp_index, cores=2):
    return (dp_index % cores) * 2 + dp_index // cores


def split_quarter(i, j, cores=2):
    shard = lax.axis_index("dp")
    core, side_y = lax.rem(shard, cores), lax.div(shard, cores)
    return (core ^ i) * 2 + (side_y ^ j)


def take_lanes(x, lanes):
    numbers = lax.GatherDimensionNumbers(
        offset_dims=(),
        collapsed_slice_dims=(1,),
        start_index_map=(1,),
        operand_batching_dims=(0,),
        start_indices_batching_dims=(0,),
    )
    mode = lax.GatherScatterMode.PROMISE_IN_BOUNDS
    return lax.gather(x, lanes[..., None], numbers, slice_sizes=(1, 1), mode=mode)


def gather_kernel(
    ids_ref,
    vocab_ref,
    turned,
    member_ref,
    held,
    token_ref,
    ranks,
    counted,
    bounds,
    held_sems,
    bounds_sem,
    base,
):
    texts, length = ids_ref.shape
    features, vocab = vocab_ref.shape
    blocks = vocab // IDS_PER_BLOCK
    groups = vocab // IDS_PER_GROUP
    span = member_ref.shape[0]

    def vocab_copy(b):
        columns = pl.ds(pl.multiple_of(b * IDS_PER_BLOCK, LANES), IDS_PER_BLOCK)
        return pltpu.make_async_copy(vocab_ref.at[:, columns], held.at[b], held_sems.at[b])

    vocab_copy(0).start()
    for b in range(1, blocks):
        vocab_copy(b).start()

    ids = ids_ref[...]
    valid = ids != 0
    group_of = jnp.where(valid, lax.shift_right_logical(ids, GROUP_BITS), groups)
    group_rows = counted.shape[0]
    group_id = iota((group_rows, length), 0)
    below = jnp.zeros((group_rows, length), jnp.float32)
    for text in range(texts):
        below += jnp.where(group_of[text : text + 1] < group_id, 1.0, 0.0)
    before = jnp.broadcast_to(jnp.sum(below, axis=1, keepdims=True), (group_rows, length))
    counted[...] = before.astype(jnp.int32)
    bounds_copy = pltpu.make_async_copy(counted, bounds, bounds_sem)
    bounds_copy.start()
    earlier = jnp.where(iota((length, length), 0) < iota((length, length), 1), 1.0, 0.0).astype(
        jnp.bfloat16
    )
    for text in range(texts):
        here = jnp.where(group_of[text : text + 1] == group_id, 1.0, 0.0)
        inside = mm(here.astype(jnp.bfloat16), earlier)
        ranks[pl.ds(text, 1), :] = jnp.sum(here * (inside + before), axis=0, keepdims=True)
        before += jnp.broadcast_to(jnp.sum(here, axis=1, keepdims=True), (group_rows, length))
    text_of = iota((texts, length), 0)
    carried = jnp.where(valid, lax.shift_left(ids, ROW_BITS) + text_of, 0).astype(jnp.float32)
    rank = ranks[...]

    def place(p, carry):
        position = (iota((LANES, length), 0) + (p * LANES + base)).astype(jnp.float32)
        total = jnp.zeros((LANES, length), jnp.float32)
        for text in range(texts):
            total += jnp.where(rank[text : text + 1] == position, carried[text : text + 1], 0.0)
        found = jnp.broadcast_to(jnp.sum(total, axis=1, keepdims=True), (LANES, LANES))
        start = pl.multiple_of(p * LANES, LANES)
        row = found.T[0:1].astype(jnp.int32)
        token = lax.shift_right_logical(row, ROW_BITS)
        token_ref[pl.ds(p, 1), :] = jnp.where(token == 0, -vocab, token)
        found = found.astype(jnp.int32)
        real = (found >= ROWS) & ((found & (ROWS - 1)) == iota((LANES, LANES), 1))
        member_ref[pl.ds(start, LANES), :] = jnp.where(real, 1.0, 0.0).astype(jnp.bfloat16)
        turned[:, pl.ds(start, LANES)] = jnp.zeros((features, LANES), jnp.bfloat16)
        return carry

    lax.fori_loop(0, span // LANES, place, 0)
    bounds_copy.wait()

    def within(place):
        return jnp.clip(place - base, 0, span)

    def take(b, carry):
        vocab_copy(b).wait()
        for part in range(IDS_PER_BLOCK // IDS_PER_GROUP):
            group = b * (IDS_PER_BLOCK // IDS_PER_GROUP) + part
            first, last = within(bounds[group, 0]), within(bounds[group + 1, 0])
            begin = lax.shift_right_logical(first, LANE_BITS)
            end = lax.shift_right_logical(last + LANES - 1, LANE_BITS)

            def window(p, carry):
                at = pl.ds(pl.multiple_of(p * LANES, LANES), LANES)
                token = token_ref[pl.ds(p, 1), :] - group * IDS_PER_GROUP
                token = jnp.broadcast_to(token, (FEATURE_ROWS, LANES))
                lane = (token & (LANES - 1)).astype(jnp.int16)
                tile = lax.shift_right_arithmetic(token, LANE_BITS).astype(jnp.int16)
                pieces = [pl.ds(f, FEATURE_ROWS) for f in range(0, features, FEATURE_ROWS)]
                fresh = []
                for rows in pieces:
                    total = jnp.zeros((FEATURE_ROWS, LANES), jnp.bfloat16)
                    for j in range(IDS_PER_GROUP // LANES):
                        columns = pl.ds(part * IDS_PER_GROUP + j * LANES, LANES)
                        total = jnp.where(tile == j, take_lanes(held[b, rows, columns], lane), total)
                    fresh.append(total)
                fresh = [turned[rows, at] + total for rows, total in zip(pieces, fresh)]
                for rows, total in zip(pieces, fresh):
                    turned[rows, at] = total
                return carry

            lax.fori_loop(begin, jnp.where(last > first, end, begin), window, 0)
        return carry

    lax.fori_loop(0, blocks, take, 0)


def statistics_kernel(
    ids_ref, turned, member_ref, hard_ref, lower_ref, extra_ref, count_ref, small
):
    features, span = turned.shape
    stripes = pl.cdiv(span, STRIPE)
    per_shard, negatives = hard_ref.shape
    shard = lax.axis_index("dp")
    count_ref[0] = jnp.sum((ids_ref[...] != 0).astype(jnp.float32)).astype(jnp.int32)
    small[...] = jnp.zeros_like(small)
    small[0:per_shard, stripes : stripes + negatives] = hard_ref[...].astype(jnp.float32)
    lower = lower_ref[:, pl.ds(pl.multiple_of(shard * features, LANES), features)]

    misc = jnp.zeros((ROWS, STRIPE), jnp.float32)
    residual = jnp.zeros((features, LANES), jnp.float32)
    for stripe in range(stripes):
        size = min(STRIPE, span - stripe * STRIPE)
        across = pl.ds(stripe * STRIPE, size)
        upright = turned[:, across]
        wide = upright.astype(jnp.float32)
        square = jnp.sum(wide * wide, axis=0, keepdims=True)
        reduced = mm(lower, upright)
        if size < STRIPE:
            none = jnp.zeros((ROWS, STRIPE - size), jnp.float32)
            reduced = jnp.concatenate([reduced, none], axis=1)
            square = jnp.concatenate([square, none[0:1]], axis=1)
        extra_ref[stripe * ROWS : (stripe + 1) * ROWS, :] = reduced.astype(jnp.bfloat16)
        misc = jnp.where(iota((ROWS, STRIPE), 0) == stripe, square, misc)
        residual += mm(upright, member_ref[across, :])
    hard = small[...].T[0:ROWS]
    for i in range(per_shard):
        misc += jnp.where(iota((ROWS, STRIPE), 1) == shard * per_shard + i, hard[:, i : i + 1], 0.0)
    extra_ref[stripes * ROWS : (stripes + 1) * ROWS, :] = misc.astype(jnp.bfloat16)
    residual = jnp.where(lax.axis_index("mp") == shard, residual.T[0:ROWS], 0.0)
    for q in range(features // STRIPE):
        start = (stripes + 1 + q) * ROWS
        extra_ref[start : start + ROWS, :] = residual[:, q * STRIPE : (q + 1) * STRIPE].astype(
            jnp.bfloat16
        )


def pool_kernel(
    ids_ref,
    own_ref,
    core_ref,
    far_ref,
    chip_ref,
    far_chip_ref,
    member_ref,
    own_rest,
    core_rest,
    far_rest,
    chip_rest,
    far_chip_rest,
    member_rest,
    raise_ref,
    pooled_ref,
    slopes_ref,
    misc_ref,
    raised,
    total,
    slopes,
    model_width,
):
    texts, length = ids_ref.shape
    width = own_ref.shape[1]
    quarter = quarter_of(lax.axis_index("dp"))
    raised[...] = jnp.zeros_like(raised)
    raised[0:ROWS, :] = raise_ref[:, pl.ds(pl.multiple_of(quarter * width, LANES), width)]
    total[...] = jnp.zeros_like(total)
    slopes[...] = jnp.zeros_like(slopes)

    def add(refs, extras, member_ref, base):
        span = member_ref.shape[0]
        stripes = pl.cdiv(span, STRIPE)

        def summed(refs, start, size):
            return sum(ref[pl.ds(start, size), :].astype(jnp.float32) for ref in refs)

        misc = summed(extras, stripes * ROWS, ROWS)
        if base == 0:
            misc_ref[...] = misc
        inverse = lax.rsqrt(misc / model_width + 1e-05)
        for k in range(stripes):
            size = min(STRIPE, span - k * STRIPE)
            scale = inverse[k : k + 1]
            reduced = (summed(extras, k * ROWS, ROWS) * scale).astype(jnp.bfloat16)
            reduced = reduced.astype(jnp.float32)
            stacked = jnp.concatenate([reduced, jnp.broadcast_to(scale, (LANES - ROWS, STRIPE))])
            turned = stacked[:, 0:size].T
            low = turned.astype(jnp.bfloat16)
            linear = summed(refs, k * STRIPE, size)
            linear = linear * turned[:, ROWS : ROWS + 1] + mm(low, raised[...])
            sigma = 1.0 / (1.0 + jnp.exp(-linear))
            slope = (sigma * (1.0 + linear * (1.0 - sigma))).astype(jnp.bfloat16)
            member = member_ref[pl.ds(k * STRIPE, size), :].astype(jnp.float32).T
            high, rest = split(linear * sigma)
            chosen = member[0:ROWS].astype(jnp.bfloat16)
            total[...] += mm(chosen, high) + mm(chosen, rest)
            spread = [reduced[:, 0:size] * member[text : text + 1] for text in range(texts)]
            slopes[...] += mm(jnp.concatenate(spread).astype(jnp.bfloat16), slope)
        start = pl.multiple_of((stripes + 1 + quarter) * ROWS, ROWS)
        total[...] += summed(extras, start, ROWS)

    add((own_ref, core_ref, far_ref), (chip_ref, far_chip_ref), member_ref, 0)
    real = (ids_ref[...] != 0).astype(jnp.float32)

    @pl.when(jnp.sum(real) > member_ref.shape[0])
    def _():
        extras = (chip_rest, far_chip_rest)
        add((own_rest, core_rest, far_rest), extras, member_rest, member_ref.shape[0])

    counts = jnp.sum(real, axis=1, keepdims=True)
    pooled = total[0:texts] / counts
    pooled = jnp.concatenate([pooled, jnp.zeros((ROWS - texts, width), jnp.float32)])
    pooled_ref[...] = pooled.astype(jnp.bfloat16)
    for text in range(texts):
        rows = pl.ds(text * ROWS, ROWS)
        slopes_ref[rows, :] = (slopes[rows, :] / counts[text : text + 1]).astype(jnp.bfloat16)


def both_sides(near, far):
    queries = lax.axis_index("group") == 0
    return jnp.concatenate([jnp.where(queries, near, far), jnp.where(queries, far, near)], axis=0)


def dots_kernel(near_ref, far_ref, slopes_ref, packed_ref, slopes_out):
    block = both_sides(near_ref[...], far_ref[...])
    rows = 2 * ROWS
    packed_ref[...] = jnp.zeros_like(packed_ref)
    packed_ref[0:rows, 0:rows] = mm(block, block, NT)
    for part in range(block.shape[1] // LANES):
        piece = block[:, part * LANES : (part + 1) * LANES]
        packed_ref[rows + part * rows : rows + (part + 1) * rows, :] = piece.astype(jnp.float32)
    slopes_out[...] = slopes_ref[...]


def score_kernel(
    packed0,
    packed1,
    packed2,
    packed3,
    slopes0,
    slopes1,
    slopes2,
    slopes3,
    dots0,
    dots1,
    dots2,
    dots3,
    misc_ref,
    sharp_ref,
    embed_ref,
    loss_ref,
    up_ref,
    texts,
    stripes,
    negatives,
):
    rows = 2 * ROWS
    per_shard = loss_ref.shape[1]
    group, shard = lax.axis_index("group"), lax.axis_index("dp")
    dots = ((dots0[...] + dots1[...]) + (dots2[...] + dots3[...]))[:, 0:rows]
    down, across = iota((rows, rows), 0), iota((rows, rows), 1)
    same = down == across
    real = (lax.rem(down, ROWS) < texts) & (lax.rem(across, ROWS) < texts)
    diagonal = jnp.where(same, dots, 0.0)
    rnorm_row = lax.rsqrt(jnp.sum(diagonal, axis=0, keepdims=True) + 1e-06)
    rnorm_col = lax.rsqrt(jnp.sum(diagonal, axis=1, keepdims=True) + 1e-06)
    sharpness = sharp_ref[0]
    cosine = dots * rnorm_col * rnorm_row
    scores = sharpness * cosine
    keep = real & ~same
    top = jnp.max(jnp.where(keep, scores, -jnp.inf), axis=0, keepdims=True)
    top = jnp.where(lax.rem(across[0:1], ROWS) < texts, top, 0.0)
    powers = jnp.exp(jnp.where(real, jnp.minimum(scores - top, 0.0), 0.0))
    hard = misc_ref[stripes : stripes + negatives, 0:rows].astype(jnp.int32) + ROWS
    times = jnp.zeros((rows, rows), jnp.float32)
    for k in range(negatives):
        times += jnp.where(hard[k : k + 1] == down, 1.0, 0.0)
    times = jnp.where(across < texts, times, 0.0)
    weights = (jnp.where(keep, 1.0, 0.0) + jnp.where(real, times, 0.0)) * powers
    total = jnp.sum(weights, axis=0, keepdims=True)
    total = jnp.where(lax.rem(across[0:1], ROWS) < texts, total, 1.0)
    pair = (down == lax.rem(across + ROWS, rows)) & real
    pair_score = jnp.sum(jnp.where(pair, scores, 0.0), axis=0, keepdims=True)
    losses = top + jnp.log(total) - pair_score
    grad_scores = (weights / total - jnp.where(pair, 1.0, 0.0)) / (2 * texts)
    coeff = (grad_scores * rnorm_col * rnorm_row).astype(jnp.bfloat16)
    radial = jnp.sum(grad_scores * cosine, axis=0, keepdims=True) * rnorm_row * rnorm_row

    first = shard * per_shard
    loss_col = jnp.sum(jnp.where(same, losses, 0.0), axis=1, keepdims=True)
    at = (iota((rows, LANES), 0) == group * ROWS + first + iota((rows, LANES), 1)) & (
        iota((rows, LANES), 1) < per_shard
    )
    loss_ref[...] = jnp.sum(jnp.where(at, loss_col, 0.0), axis=0, keepdims=True)[:, 0:per_shard]

    along_rows = coeff.astype(jnp.float32).T.astype(jnp.bfloat16)
    radial_col = jnp.sum(jnp.where(same, radial, 0.0), axis=1, keepdims=True)
    rnorm_own = jnp.where(group == 0, rnorm_col[0:ROWS], rnorm_col[ROWS:rows])
    chosen = iota((ROWS, ROWS), 1) == iota((ROWS, ROWS), 0) + first
    chosen = jnp.where(chosen & (iota((ROWS, ROWS), 0) < per_shard), 1.0, 0.0).astype(jnp.bfloat16)
    blocks = ((packed0, slopes0), (packed1, slopes1), (packed2, slopes2), (packed3, slopes3))
    for o, (packed, slopes) in enumerate(blocks):
        parts = packed.shape[0] // rows - 1
        width = parts * LANES
        halves = [packed[rows * (part + 1) : rows * (part + 2), :] for part in range(parts)]
        block = jnp.concatenate(halves, axis=1)
        along = mm(along_rows, block.astype(jnp.bfloat16))
        grad = sharpness * (along - radial_col * block)
        near, far = slopes[0 : slopes.shape[0] // 2], slopes[slopes.shape[0] // 2 :]
        queries = group == 0
        grad_near = jnp.where(queries, grad[0:ROWS], grad[ROWS:rows])
        grad_far = jnp.where(queries, grad[ROWS:rows], grad[0:ROWS])
        update = []
        for side, side_grad in ((near, grad_near), (far, grad_far)):
            total = jnp.zeros((ROWS, width), jnp.float32)
            for text in range(texts):
                slope = side[text * ROWS : (text + 1) * ROWS].astype(jnp.float32)
                total += side_grad[text : text + 1] * slope
            update.append(total)
        at = pl.multiple_of(quarter_of(shard ^ o) * width, LANES)
        up_ref[:, pl.ds(at, width)] = update[0] + update[1]
        own = jnp.where(queries, block[0:ROWS], block[ROWS:rows]) * rnorm_own
        picked = mm(chosen, own.astype(jnp.bfloat16)).astype(jnp.bfloat16)
        embed_ref[0, :, pl.ds(at, width)] = picked[0:per_shard]


def any_spec():
    return pl.BlockSpec(memory_space=pl.ANY)


def vmem_spec():
    return pl.BlockSpec(memory_space=pltpu.VMEM)


def smem_spec():
    return pl.BlockSpec(memory_space=pltpu.SMEM)


def exchange(x, axis, size):
    steps = [[(i, i ^ o) for i in range(size)] for o in range(1, size)]
    return [x] + [lax.ppermute(x, axis, step) for step in steps]


def split_body(
    query_passage_words,
    difficult_distractors,
    vocabulary_vectors,
    layer_weight_matrix,
    lowering_factor_matrix,
    raising_factor_matrix,
    logit_sharpness,
):
    shards, parts = lax.axis_size("dp"), lax.axis_size("mp")
    ids = query_passage_words[0]
    texts, length = ids.shape
    tokens = texts * length
    features, vocab = vocabulary_vectors.shape
    blocks = vocab // IDS_PER_BLOCK
    group_rows = 8 * pl.cdiv(vocab // IDS_PER_GROUP + 1, 8)
    per_shard, negatives = difficult_distractors.shape
    part_width = layer_weight_matrix.shape[1]
    width = part_width // shards
    params = pltpu.CompilerParams(vmem_limit_bytes=VMEM_BYTES)
    other_core = [(d, d ^ 1) for d in range(shards)]
    other_y = [(d, d ^ 2) for d in range(shards)]

    def columns(i, j):
        start = split_quarter(i, j) * width
        return lax.dynamic_slice(layer_weight_matrix, (0, start), (features, width))

    def project(base, span):
        stripes = pl.cdiv(span, STRIPE)
        extra_rows = (stripes + 1 + shards) * ROWS
        turned, member = pl.pallas_call(
            functools.partial(gather_kernel, base=base),
            out_shape=[
                jax.ShapeDtypeStruct((features, span), jnp.bfloat16),
                jax.ShapeDtypeStruct((span, LANES), jnp.bfloat16),
            ],
            in_specs=[vmem_spec(), any_spec()],
            out_specs=[vmem_spec()] * 2,
            scratch_shapes=[
                pltpu.VMEM((blocks, features, IDS_PER_BLOCK), jnp.bfloat16),
                pltpu.VMEM((8 * pl.cdiv(span // LANES, 8), LANES), jnp.int32),
                pltpu.VMEM((texts, length), jnp.float32),
                pltpu.VMEM((group_rows, length), jnp.int32),
                pltpu.SMEM((group_rows, length), jnp.int32),
                pltpu.SemaphoreType.DMA((blocks,)),
                pltpu.SemaphoreType.DMA,
            ],
            compiler_params=params,
            name="gather",
        )(ids, vocabulary_vectors)

        def product(turned, i, j):
            return mm(turned, columns(i, j), (((0,), (0,)), ((), ())))

        def narrow(x):
            return x.astype(jnp.bfloat16)

        core1 = lax.ppermute(narrow(product(turned, 1, 1)), "dp", other_core)
        chip1 = narrow(product(turned, 0, 1) + core1.astype(jnp.float32))
        far = lax.ppermute(chip1, "dp", other_y)
        turned, _ = lax.optimization_barrier((turned, chip1))
        extra, count = pl.pallas_call(
            statistics_kernel,
            out_shape=[
                jax.ShapeDtypeStruct((extra_rows, STRIPE), jnp.bfloat16),
                jax.ShapeDtypeStruct((1,), jnp.int32),
            ],
            in_specs=[vmem_spec()] * 5,
            out_specs=[vmem_spec(), smem_spec()],
            scratch_shapes=[pltpu.VMEM((LANES, LANES), jnp.float32)],
            compiler_params=params,
            cost_estimate=pl.CostEstimate(
                flops=2 * features * span * (ROWS + LANES),
                bytes_accessed=2 * features * span,
                transcendentals=0,
            ),
            name="statistics",
        )(ids, turned, member, difficult_distractors, lowering_factor_matrix)
        chip = extra.astype(jnp.float32)
        chip = narrow(chip + lax.ppermute(extra, "dp", other_core).astype(jnp.float32))
        far_chip = lax.ppermute(chip, "dp", other_y)
        core0 = lax.ppermute(narrow(product(turned, 1, 0)), "dp", other_core)
        own0 = narrow(product(turned, 0, 0))
        return (own0, core0, far, chip, far_chip, member), count

    first, count = project(0, FIRST)
    many = count[0] > FIRST
    left = tokens - FIRST
    shapes = jax.eval_shape(lambda: project(FIRST, left)[0])
    rest = lax.cond(
        many,
        lambda: project(FIRST, left)[0],
        lambda: tuple(jnp.zeros(x.shape, x.dtype) for x in shapes),
    )
    pooled, slopes, misc = pl.pallas_call(
        functools.partial(pool_kernel, model_width=float(features * shards)),
        out_shape=[
            jax.ShapeDtypeStruct((ROWS, width), jnp.bfloat16),
            jax.ShapeDtypeStruct((texts * ROWS, width), jnp.bfloat16),
            jax.ShapeDtypeStruct((ROWS, width), jnp.float32),
        ],
        in_specs=[vmem_spec()] * 14,
        out_specs=[vmem_spec()] * 3,
        scratch_shapes=[
            pltpu.VMEM((LANES, width), jnp.bfloat16),
            pltpu.VMEM((ROWS, width), jnp.float32),
            pltpu.VMEM((texts * ROWS, width), jnp.float32),
        ],
        compiler_params=params,
        name="pool",
    )(ids, *first, *rest, raising_factor_matrix)
    other_side = [(0, 1), (1, 0)]
    far_side = lax.ppermute(pooled, "group", other_side)
    rows = 2 * ROWS
    packed, slopes = pl.pallas_call(
        dots_kernel,
        out_shape=[
            jax.ShapeDtypeStruct((rows + width // LANES * rows, LANES), jnp.float32),
            jax.ShapeDtypeStruct(slopes.shape, slopes.dtype),
        ],
        in_specs=[vmem_spec()] * 3,
        out_specs=[vmem_spec()] * 2,
        compiler_params=params,
        name="dots",
    )(pooled, far_side, slopes)
    packed = exchange(packed, "dp", shards)
    dots = [x[0:rows] for x in packed]
    dots = exchange((dots[0] + dots[1]) + (dots[2] + dots[3]), "mp", parts)
    slopes = jnp.concatenate([slopes, lax.ppermute(slopes, "group", other_side)])
    slopes = exchange(slopes, "dp", shards)
    embeddings, losses, update = pl.pallas_call(
        functools.partial(
            score_kernel, texts=texts, stripes=pl.cdiv(FIRST, STRIPE), negatives=negatives
        ),
        out_shape=[
            jax.ShapeDtypeStruct((1, per_shard, part_width), jnp.bfloat16),
            jax.ShapeDtypeStruct((1, per_shard), jnp.float32),
            jax.ShapeDtypeStruct((ROWS, part_width), jnp.float32),
        ],
        in_specs=[vmem_spec()] * 13 + [smem_spec()],
        out_specs=[vmem_spec()] * 3,
        compiler_params=params,
        name="score",
    )(*packed, *slopes, *dots, misc, logit_sharpness)
    return (embeddings, losses, update)


def body(words, hard, vocabulary, weight, lowering, raising, sharpness):
    shards, parts = lax.axis_size("dp"), lax.axis_size("mp")
    texts, length = words.shape[1:]
    features, vocab = vocabulary.shape
    negatives = hard.shape[1]
    square = shards == 4 and features == weight.shape[1] == 4 * STRIPE and parts == shards
    small = texts <= ROWS - 2 and length == LANES and FIRST < texts * length <= 2048
    even = (texts * length - FIRST) % CHUNK == 0 and vocab % IDS_PER_BLOCK == 0
    fits = features * vocab <= 2**24 and features % (4 * LANES) == 0
    spare = pl.cdiv(FIRST, STRIPE) + negatives <= ROWS and lowering.shape[0] == ROWS
    fast = square and small and even and fits and spare and lax.axis_size("group") == 2
    chosen = split_body if fast else general_body
    return chosen(words, hard, vocabulary, weight, lowering, raising, sharpness)


def solution(mesh):
    in_specs = (
        P("group", None, None),
        P("dp", None),
        P("dp", None),
        P("dp", "mp"),
        P(),
        P(None, "mp"),
        P(),
    )
    out_specs = (P("group", "dp", "mp"), P("group", "dp"), P(None, "mp"))
    return jax.shard_map(body, mesh=mesh, in_specs=in_specs, out_specs=out_specs, check_vma=False)
```

```python
import functools

import jax
import jax.numpy as jnp
from jax import lax
from jax.experimental import pallas as pl
from jax.experimental.pallas import tpu as pltpu
from jax.sharding import PartitionSpec as P


def general_body(
    query_passage_words,
    difficult_distractors,
    vocabulary_vectors,
    layer_weight_matrix,
    lowering_factor_matrix,
    raising_factor_matrix,
    logit_sharpness,
):
    group_index = lax.axis_index("group")
    shard_index = lax.axis_index("dp")
    part_index = lax.axis_index("mp")
    shard_count = lax.axis_size("dp")
    side_ids = query_passage_words[0]
    text_count = side_ids.shape[0]
    length = side_ids.shape[1]
    per_shard = text_count // shard_count
    own_ids = lax.dynamic_slice_in_dim(side_ids, shard_index * per_shard, per_shard, 0)
    columns = jnp.take(vocabulary_vectors, side_ids.reshape(-1), axis=1)
    inputs = lax.all_to_all(columns, "dp", split_axis=1, concat_axis=0, tiled=True)
    tokens = inputs.shape[1]
    feature_width = raising_factor_matrix.shape[1]
    wide_inputs = inputs.astype(jnp.float32)
    inverse = lax.rsqrt(jnp.mean(wide_inputs * wide_inputs, axis=0) + 1e-05)
    normed_state = (wide_inputs * inverse[None, :]).astype(jnp.bfloat16)
    linear_map = lax.dot_general(
        lax.all_gather(layer_weight_matrix, "dp", axis=0, tiled=True),
        normed_state,
        (((0,), (0,)), ((), ())),
        preferred_element_type=jnp.float32,
    )
    reduced_sum = jnp.dot(
        lowering_factor_matrix, normed_state, preferred_element_type=jnp.float32
    ).astype(jnp.bfloat16)
    linear_map = linear_map + lax.dot_general(
        raising_factor_matrix,
        reduced_sum,
        (((0,), (0,)), ((), ())),
        preferred_element_type=jnp.float32,
    )
    own_inputs = lax.dynamic_slice_in_dim(
        inputs, part_index * feature_width, feature_width, 0
    ).astype(jnp.float32)
    hidden_state = own_inputs + jax.nn.silu(linear_map)
    mask = (own_ids != 0).astype(jnp.float32)
    counts = jnp.sum(mask, axis=1)
    summed = jnp.einsum("dnl,nl->nd", hidden_state.reshape(feature_width, per_shard, length), mask)
    pooled = (summed / counts[:, None]).astype(jnp.bfloat16)
    gathered = lax.all_gather(pooled, ("group", "dp"), axis=0, tiled=True)
    part_scores = lax.dot_general(
        pooled, gathered, (((1,), (1,)), ((), ())), preferred_element_type=jnp.float32
    )
    gathered_wide = gathered.astype(jnp.float32)
    part_norms = jnp.sum(gathered_wide * gathered_wide, axis=1)
    dots, norms = lax.psum((part_scores, part_norms), "mp")
    rnorm_all = lax.rsqrt(norms + 1e-06)
    all_count = gathered.shape[0]
    half_count = all_count // 2
    own_rows = (
        group_index * half_count + shard_index * per_shard + jnp.arange(per_shard, dtype=jnp.int32)
    )
    rnorm_own = jnp.take(rnorm_all, own_rows)
    cosine = dots * rnorm_own[:, None] * rnorm_all[None, :]
    multiplier_factor = logit_sharpness[0]
    scores = multiplier_factor * cosine
    column_ids = jnp.arange(all_count, dtype=jnp.int32)
    keep = column_ids[None, :] != own_rows[:, None]
    pair = (own_rows + half_count) % all_count
    weight = (group_index == 0).astype(jnp.float32)
    neg_cols = half_count + difficult_distractors
    top = jnp.max(jnp.where(keep, scores, -jnp.inf), axis=1)
    safe_scores = jnp.where(keep, scores, top[:, None])
    expd = jnp.where(keep, jnp.exp(safe_scores - top[:, None]), 0.0)
    neg_exp = (
        jnp.exp(jnp.minimum(jnp.take_along_axis(scores, neg_cols, axis=1) - top[:, None], 0.0))
        * weight
    )
    total = jnp.sum(expd, axis=1) + jnp.sum(neg_exp, axis=1)
    pair_score = jnp.take_along_axis(scores, pair[:, None], axis=1)[:, 0]
    losses = top + jnp.log(total) - pair_score
    onehot = (column_ids[None, None, :] == neg_cols[:, :, None]).astype(jnp.float32)
    probs = (expd + jnp.einsum("rk,rkc->rc", neg_exp, onehot)) / total[:, None]
    target = (column_ids[None, :] == pair[:, None]).astype(jnp.float32)
    grad_scores = (probs - target) / all_count
    coeff = (grad_scores * rnorm_own[:, None] * rnorm_all[None, :]).astype(jnp.bfloat16)
    along = jnp.dot(coeff, gathered, preferred_element_type=jnp.float32)
    pooled_wide = pooled.astype(jnp.float32)
    radial = jnp.sum(grad_scores * cosine, axis=1) * rnorm_own * rnorm_own
    embedding_gradient = multiplier_factor * (along - radial[:, None] * pooled_wide)
    token_grad = jnp.einsum("nd,nl->dnl", embedding_gradient / counts[:, None], mask).reshape(
        feature_width, tokens
    )
    sigma = jax.nn.sigmoid(linear_map)
    local = (token_grad * sigma * (1.0 + linear_map * (1.0 - sigma))).astype(jnp.bfloat16)
    up_portion = lax.dot_general(
        reduced_sum, local, (((1,), (1,)), ((), ())), preferred_element_type=jnp.float32
    )
    adapter_up_gradient = lax.psum(up_portion, ("group", "dp"))
    embeddings = (pooled_wide * rnorm_own[:, None]).astype(jnp.bfloat16)[None]
    return (embeddings, losses[None], adapter_up_gradient)


BLOCK_BITS, GROUP_BITS, LANE_BITS, ROW_BITS = 10, 9, 7, 4
IDS_PER_BLOCK = 1 << BLOCK_BITS
IDS_PER_GROUP = 1 << GROUP_BITS
CHUNK = 384
STRIPE = 256
ROWS = 1 << ROW_BITS
LANES = 1 << LANE_BITS
FEATURE_ROWS = 128
FIRST = 1152
NT = (((1,), (1,)), ((), ()))
VMEM_BYTES = 60 * 1024 * 1024


def mm(a, b, dims=(((1,), (0,)), ((), ()))):
    return lax.dot_general(a, b, dims, preferred_element_type=jnp.float32)


def split(x):
    high = x.astype(jnp.bfloat16)
    return high, (x - high.astype(jnp.float32)).astype(jnp.bfloat16)


def iota(shape, dim):
    return lax.broadcasted_iota(jnp.int32, shape, dim)


def quarter_of(dp_index, cores=2):
    return (dp_index % cores) * 2 + dp_index // cores


def split_quarter(i, j, cores=2):
    shard = lax.axis_index("dp")
    core, side_y = lax.rem(shard, cores), lax.div(shard, cores)
    return (core ^ i) * 2 + (side_y ^ j)


def take_lanes(x, lanes):
    numbers = lax.GatherDimensionNumbers(
        offset_dims=(),
        collapsed_slice_dims=(1,),
        start_index_map=(1,),
        operand_batching_dims=(0,),
        start_indices_batching_dims=(0,),
    )
    mode = lax.GatherScatterMode.PROMISE_IN_BOUNDS
    return lax.gather(x, lanes[..., None], numbers, slice_sizes=(1, 1), mode=mode)


def gather_kernel(
    ids_ref,
    vocab_ref,
    turned,
    member_ref,
    held,
    token_ref,
    ranks,
    counted,
    bounds,
    held_sems,
    bounds_sem,
    base,
):
    texts, length = ids_ref.shape
    features, vocab = vocab_ref.shape
    blocks = vocab // IDS_PER_BLOCK
    groups = vocab // IDS_PER_GROUP
    span = member_ref.shape[0]

    def vocab_copy(b):
        columns = pl.ds(pl.multiple_of(b * IDS_PER_BLOCK, LANES), IDS_PER_BLOCK)
        return pltpu.make_async_copy(vocab_ref.at[:, columns], held.at[b], held_sems.at[b])

    vocab_copy(0).start()
    for b in range(1, blocks):
        vocab_copy(b).start()

    ids = ids_ref[...]
    valid = ids != 0
    group_of = jnp.where(valid, lax.shift_right_logical(ids, GROUP_BITS), groups)
    group_rows = counted.shape[0]
    group_id = iota((group_rows, length), 0)
    below = jnp.zeros((group_rows, length), jnp.float32)
    for text in range(texts):
        below += jnp.where(group_of[text : text + 1] < group_id, 1.0, 0.0)
    before = jnp.broadcast_to(jnp.sum(below, axis=1, keepdims=True), (group_rows, length))
    counted[...] = before.astype(jnp.int32)
    bounds_copy = pltpu.make_async_copy(counted, bounds, bounds_sem)
    bounds_copy.start()
    earlier = jnp.where(iota((length, length), 0) < iota((length, length), 1), 1.0, 0.0).astype(
        jnp.bfloat16
    )
    for text in range(texts):
        here = jnp.where(group_of[text : text + 1] == group_id, 1.0, 0.0)
        inside = mm(here.astype(jnp.bfloat16), earlier)
        ranks[pl.ds(text, 1), :] = jnp.sum(here * (inside + before), axis=0, keepdims=True)
        before += jnp.broadcast_to(jnp.sum(here, axis=1, keepdims=True), (group_rows, length))
    text_of = iota((texts, length), 0)
    carried = jnp.where(valid, lax.shift_left(ids, ROW_BITS) + text_of, 0).astype(jnp.float32)
    rank = ranks[...]

    def place(p, carry):
        position = (iota((LANES, length), 0) + (p * LANES + base)).astype(jnp.float32)
        total = jnp.zeros((LANES, length), jnp.float32)
        for text in range(texts):
            total += jnp.where(rank[text : text + 1] == position, carried[text : text + 1], 0.0)
        found = jnp.broadcast_to(jnp.sum(total, axis=1, keepdims=True), (LANES, LANES))
        start = pl.multiple_of(p * LANES, LANES)
        row = found.T[0:1].astype(jnp.int32)
        token = lax.shift_right_logical(row, ROW_BITS)
        token_ref[pl.ds(p, 1), :] = jnp.where(token == 0, -vocab, token)
        found = found.astype(jnp.int32)
        real = (found >= ROWS) & ((found & (ROWS - 1)) == iota((LANES, LANES), 1))
        member_ref[pl.ds(start, LANES), :] = jnp.where(real, 1.0, 0.0).astype(jnp.bfloat16)
        turned[:, pl.ds(start, LANES)] = jnp.zeros((features, LANES), jnp.bfloat16)
        return carry

    lax.fori_loop(0, span // LANES, place, 0)
    bounds_copy.wait()

    def within(place):
        return jnp.clip(place - base, 0, span)

    per_block = IDS_PER_BLOCK // IDS_PER_GROUP

    def take(group, carry):
        b, part = lax.div(group, per_block), lax.rem(group, per_block)

        @pl.when(part == 0)
        def _():
            vocab_copy(b).wait()

        first, last = within(bounds[group, 0]), within(bounds[group + 1, 0])
        begin = lax.shift_right_logical(first, LANE_BITS)
        end = lax.shift_right_logical(last + LANES - 1, LANE_BITS)

        def window(p, carry):
            at = pl.ds(pl.multiple_of(p * LANES, LANES), LANES)
            token = token_ref[pl.ds(p, 1), :] - group * IDS_PER_GROUP
            token = jnp.broadcast_to(token, (FEATURE_ROWS, LANES))
            lane = (token & (LANES - 1)).astype(jnp.int16)
            tile = lax.shift_right_arithmetic(token, LANE_BITS).astype(jnp.int16)
            pieces = [pl.ds(f, FEATURE_ROWS) for f in range(0, features, FEATURE_ROWS)]
            fresh = []
            for rows in pieces:
                total = jnp.zeros((FEATURE_ROWS, LANES), jnp.bfloat16)
                for j in range(IDS_PER_GROUP // LANES):
                    start = pl.multiple_of(part * IDS_PER_GROUP + j * LANES, LANES)
                    columns = pl.ds(start, LANES)
                    total = jnp.where(tile == j, take_lanes(held[b, rows, columns], lane), total)
                fresh.append(total)
            fresh = [turned[rows, at] + total for rows, total in zip(pieces, fresh)]
            for rows, total in zip(pieces, fresh):
                turned[rows, at] = total
            return carry

        return lax.fori_loop(begin, jnp.where(last > first, end, begin), window, carry)

    lax.fori_loop(0, groups, take, 0)


def statistics_kernel(turned, member_ref, hard_ref, lower_ref, extra_ref, small):
    features, span = turned.shape
    stripes = pl.cdiv(span, STRIPE)
    per_shard, negatives = hard_ref.shape
    shard = lax.axis_index("dp")
    small[...] = jnp.zeros_like(small)
    small[0:per_shard, stripes : stripes + negatives] = hard_ref[...].astype(jnp.float32)
    lower = lower_ref[:, pl.ds(pl.multiple_of(shard * features, LANES), features)]

    misc = jnp.zeros((ROWS, STRIPE), jnp.float32)
    residual = jnp.zeros((features, LANES), jnp.float32)
    for stripe in range(stripes):
        size = min(STRIPE, span - stripe * STRIPE)
        across = pl.ds(stripe * STRIPE, size)
        upright = turned[:, across]
        wide = upright.astype(jnp.float32)
        square = jnp.sum(wide * wide, axis=0, keepdims=True)
        reduced = mm(lower, upright)
        if size < STRIPE:
            none = jnp.zeros((ROWS, STRIPE - size), jnp.float32)
            reduced = jnp.concatenate([reduced, none], axis=1)
            square = jnp.concatenate([square, none[0:1]], axis=1)
        extra_ref[stripe * ROWS : (stripe + 1) * ROWS, :] = reduced.astype(jnp.bfloat16)
        misc = jnp.where(iota((ROWS, STRIPE), 0) == stripe, square, misc)
        residual += mm(upright, member_ref[across, :])
    hard = small[...].T[0:ROWS]
    for i in range(per_shard):
        misc += jnp.where(iota((ROWS, STRIPE), 1) == shard * per_shard + i, hard[:, i : i + 1], 0.0)
    extra_ref[stripes * ROWS : (stripes + 1) * ROWS, :] = misc.astype(jnp.bfloat16)
    residual = jnp.where(lax.axis_index("mp") == shard, residual.T[0:ROWS], 0.0)
    for q in range(features // STRIPE):
        start = (stripes + 1 + q) * ROWS
        extra_ref[start : start + ROWS, :] = residual[:, q * STRIPE : (q + 1) * STRIPE].astype(
            jnp.bfloat16
        )


def pool_kernel(
    ids_ref,
    own_ref,
    core_ref,
    far_ref,
    chip_ref,
    far_chip_ref,
    member_ref,
    own_rest,
    core_rest,
    far_rest,
    chip_rest,
    far_chip_rest,
    member_rest,
    raise_ref,
    sent_ref,
    misc_ref,
    raised,
    total,
    slopes,
    model_width,
):
    texts, length = ids_ref.shape
    width = own_ref.shape[1]
    quarter = quarter_of(lax.axis_index("dp"))
    raised[...] = jnp.zeros_like(raised)
    raised[0:ROWS, :] = raise_ref[:, pl.ds(pl.multiple_of(quarter * width, LANES), width)]
    total[...] = jnp.zeros_like(total)
    slopes[...] = jnp.zeros_like(slopes)

    def add(refs, extras, member_ref, base):
        span = member_ref.shape[0]
        stripes = pl.cdiv(span, STRIPE)

        def summed(refs, start, size):
            return sum(ref[pl.ds(start, size), :].astype(jnp.float32) for ref in refs)

        misc = summed(extras, stripes * ROWS, ROWS)
        if base == 0:
            misc_ref[...] = misc
        inverse = lax.rsqrt(misc / model_width + 1e-05)
        for k in range(stripes):
            size = min(STRIPE, span - k * STRIPE)
            scale = inverse[k : k + 1]
            reduced = (summed(extras, k * ROWS, ROWS) * scale).astype(jnp.bfloat16)
            reduced = reduced.astype(jnp.float32)
            stacked = jnp.concatenate([reduced, jnp.broadcast_to(scale, (LANES - ROWS, STRIPE))])
            turned = stacked[:, 0:size].T
            low = turned.astype(jnp.bfloat16)
            linear = summed(refs, k * STRIPE, size)
            linear = linear * turned[:, ROWS : ROWS + 1] + mm(low, raised[...])
            sigma = 1.0 / (1.0 + jnp.exp(-linear))
            slope = (sigma * (1.0 + linear * (1.0 - sigma))).astype(jnp.bfloat16)
            member = member_ref[pl.ds(k * STRIPE, size), :].astype(jnp.float32).T
            high, rest = split(linear * sigma)
            chosen = member[0:ROWS].astype(jnp.bfloat16)
            total[...] += mm(chosen, high) + mm(chosen, rest)
            spread = [reduced[:, 0:size] * member[text : text + 1] for text in range(texts)]
            slopes[...] += mm(jnp.concatenate(spread).astype(jnp.bfloat16), slope)
        start = pl.multiple_of((stripes + 1 + quarter) * ROWS, ROWS)
        total[...] += summed(extras, start, ROWS)

    add((own_ref, core_ref, far_ref), (chip_ref, far_chip_ref), member_ref, 0)
    real = (ids_ref[...] != 0).astype(jnp.float32)

    @pl.when(jnp.sum(real) > member_ref.shape[0])
    def _():
        extras = (chip_rest, far_chip_rest)
        add((own_rest, core_rest, far_rest), extras, member_rest, member_ref.shape[0])

    counts = jnp.sum(real, axis=1, keepdims=True)
    pooled = total[0:texts] / counts
    pooled = jnp.concatenate([pooled, jnp.zeros((ROWS - texts, width), jnp.float32)])
    sent_ref[0:ROWS, :] = pooled.astype(jnp.bfloat16)
    for text in range(texts):
        part = slopes[text * ROWS : (text + 1) * ROWS, :] / counts[text : text + 1]
        sent_ref[(text + 1) * ROWS : (text + 2) * ROWS, :] = part.astype(jnp.bfloat16)


def both_sides(near, far):
    queries = lax.axis_index("group") == 0
    return jnp.concatenate([jnp.where(queries, near, far), jnp.where(queries, far, near)], axis=0)


def dots_kernel(near_ref, far_ref, packed_ref, slopes_ref):
    block = both_sides(near_ref[0:ROWS], far_ref[0:ROWS])
    rows = 2 * ROWS
    packed_ref[...] = jnp.zeros_like(packed_ref)
    packed_ref[0:rows, 0:rows] = mm(block, block, NT)
    for part in range(block.shape[1] // LANES):
        piece = block[:, part * LANES : (part + 1) * LANES]
        packed_ref[rows + part * rows : rows + (part + 1) * rows, :] = piece.astype(jnp.float32)
    size = near_ref.shape[0] - ROWS
    slopes_ref[0:size] = near_ref[ROWS:]
    slopes_ref[size:] = far_ref[ROWS:]


def score_kernel(
    packed0,
    packed1,
    packed2,
    packed3,
    slopes0,
    slopes1,
    slopes2,
    slopes3,
    dots0,
    dots1,
    dots2,
    dots3,
    misc_ref,
    sharp_ref,
    embed_ref,
    loss_ref,
    up_ref,
    texts,
    stripes,
    negatives,
):
    rows = 2 * ROWS
    per_shard = loss_ref.shape[1]
    group, shard = lax.axis_index("group"), lax.axis_index("dp")
    dots = ((dots0[...] + dots1[...]) + (dots2[...] + dots3[...]))[:, 0:rows]
    down, across = iota((rows, rows), 0), iota((rows, rows), 1)
    same = down == across
    real = (lax.rem(down, ROWS) < texts) & (lax.rem(across, ROWS) < texts)
    diagonal = jnp.where(same, dots, 0.0)
    rnorm_row = lax.rsqrt(jnp.sum(diagonal, axis=0, keepdims=True) + 1e-06)
    rnorm_col = lax.rsqrt(jnp.sum(diagonal, axis=1, keepdims=True) + 1e-06)
    sharpness = sharp_ref[0]
    cosine = dots * rnorm_col * rnorm_row
    scores = sharpness * cosine
    keep = real & ~same
    top = jnp.max(jnp.where(keep, scores, -jnp.inf), axis=0, keepdims=True)
    top = jnp.where(lax.rem(across[0:1], ROWS) < texts, top, 0.0)
    powers = jnp.exp(jnp.where(real, jnp.minimum(scores - top, 0.0), 0.0))
    hard = misc_ref[stripes : stripes + negatives, 0:rows].astype(jnp.int32) + ROWS
    times = jnp.zeros((rows, rows), jnp.float32)
    for k in range(negatives):
        times += jnp.where(hard[k : k + 1] == down, 1.0, 0.0)
    times = jnp.where(across < texts, times, 0.0)
    weights = (jnp.where(keep, 1.0, 0.0) + jnp.where(real, times, 0.0)) * powers
    total = jnp.sum(weights, axis=0, keepdims=True)
    total = jnp.where(lax.rem(across[0:1], ROWS) < texts, total, 1.0)
    pair = (down == lax.rem(across + ROWS, rows)) & real
    pair_score = jnp.sum(jnp.where(pair, scores, 0.0), axis=0, keepdims=True)
    losses = top + jnp.log(total) - pair_score
    grad_scores = (weights / total - jnp.where(pair, 1.0, 0.0)) / (2 * texts)
    coeff = (grad_scores * rnorm_col * rnorm_row).astype(jnp.bfloat16)
    radial = jnp.sum(grad_scores * cosine, axis=0, keepdims=True) * rnorm_row * rnorm_row

    first = shard * per_shard
    loss_col = jnp.sum(jnp.where(same, losses, 0.0), axis=1, keepdims=True)
    at = (iota((rows, LANES), 0) == group * ROWS + first + iota((rows, LANES), 1)) & (
        iota((rows, LANES), 1) < per_shard
    )
    loss_ref[...] = jnp.sum(jnp.where(at, loss_col, 0.0), axis=0, keepdims=True)[:, 0:per_shard]

    along_rows = coeff.astype(jnp.float32).T.astype(jnp.bfloat16)
    radial_col = jnp.sum(jnp.where(same, radial, 0.0), axis=1, keepdims=True)
    rnorm_own = jnp.where(group == 0, rnorm_col[0:ROWS], rnorm_col[ROWS:rows])
    chosen = iota((ROWS, ROWS), 1) == iota((ROWS, ROWS), 0) + first
    chosen = jnp.where(chosen & (iota((ROWS, ROWS), 0) < per_shard), 1.0, 0.0).astype(jnp.bfloat16)
    blocks = ((packed0, slopes0), (packed1, slopes1), (packed2, slopes2), (packed3, slopes3))
    for o, (packed, slopes) in enumerate(blocks):
        parts = packed.shape[0] // rows - 1
        width = parts * LANES
        halves = [packed[rows * (part + 1) : rows * (part + 2), :] for part in range(parts)]
        block = jnp.concatenate(halves, axis=1)
        along = mm(along_rows, block.astype(jnp.bfloat16))
        grad = sharpness * (along - radial_col * block)
        near, far = slopes[0 : slopes.shape[0] // 2], slopes[slopes.shape[0] // 2 :]
        queries = group == 0
        grad_near = jnp.where(queries, grad[0:ROWS], grad[ROWS:rows])
        grad_far = jnp.where(queries, grad[ROWS:rows], grad[0:ROWS])
        update = []
        for side, side_grad in ((near, grad_near), (far, grad_far)):
            total = jnp.zeros((ROWS, width), jnp.float32)
            for text in range(texts):
                slope = side[text * ROWS : (text + 1) * ROWS].astype(jnp.float32)
                total += side_grad[text : text + 1] * slope
            update.append(total)
        at = pl.multiple_of(quarter_of(shard ^ o) * width, LANES)
        up_ref[:, pl.ds(at, width)] = update[0] + update[1]
        own = jnp.where(queries, block[0:ROWS], block[ROWS:rows]) * rnorm_own
        picked = mm(chosen, own.astype(jnp.bfloat16)).astype(jnp.bfloat16)
        embed_ref[0, :, pl.ds(at, width)] = picked[0:per_shard]


def any_spec():
    return pl.BlockSpec(memory_space=pl.ANY)


def vmem_spec():
    return pl.BlockSpec(memory_space=pltpu.VMEM)


def smem_spec():
    return pl.BlockSpec(memory_space=pltpu.SMEM)


def exchange(x, axis, size):
    steps = [[(i, i ^ o) for i in range(size)] for o in range(1, size)]
    return [x] + [lax.ppermute(x, axis, step) for step in steps]


def split_body(
    query_passage_words,
    difficult_distractors,
    vocabulary_vectors,
    layer_weight_matrix,
    lowering_factor_matrix,
    raising_factor_matrix,
    logit_sharpness,
):
    shards, parts = lax.axis_size("dp"), lax.axis_size("mp")
    ids = query_passage_words[0]
    texts, length = ids.shape
    tokens = texts * length
    features, vocab = vocabulary_vectors.shape
    blocks = vocab // IDS_PER_BLOCK
    group_rows = 8 * pl.cdiv(vocab // IDS_PER_GROUP + 1, 8)
    per_shard, negatives = difficult_distractors.shape
    part_width = layer_weight_matrix.shape[1]
    width = part_width // shards
    params = pltpu.CompilerParams(vmem_limit_bytes=VMEM_BYTES)
    other_core = [(d, d ^ 1) for d in range(shards)]
    other_y = [(d, d ^ 2) for d in range(shards)]

    def columns(i, j):
        start = split_quarter(i, j) * width
        return lax.dynamic_slice(layer_weight_matrix, (0, start), (features, width))

    def project(base, span):
        stripes = pl.cdiv(span, STRIPE)
        extra_rows = (stripes + 1 + shards) * ROWS
        turned, member = pl.pallas_call(
            functools.partial(gather_kernel, base=base),
            out_shape=[
                jax.ShapeDtypeStruct((features, span), jnp.bfloat16),
                jax.ShapeDtypeStruct((span, LANES), jnp.bfloat16),
            ],
            in_specs=[vmem_spec(), any_spec()],
            out_specs=[vmem_spec()] * 2,
            scratch_shapes=[
                pltpu.VMEM((blocks, features, IDS_PER_BLOCK), jnp.bfloat16),
                pltpu.VMEM((8 * pl.cdiv(span // LANES, 8), LANES), jnp.int32),
                pltpu.VMEM((texts, length), jnp.float32),
                pltpu.VMEM((group_rows, length), jnp.int32),
                pltpu.SMEM((group_rows, length), jnp.int32),
                pltpu.SemaphoreType.DMA((blocks,)),
                pltpu.SemaphoreType.DMA,
            ],
            compiler_params=params,
            name="gather",
        )(ids, vocabulary_vectors)

        def product(turned, i, j):
            return mm(turned, columns(i, j), (((0,), (0,)), ((), ())))

        def narrow(x):
            return x.astype(jnp.bfloat16)

        core1 = lax.ppermute(narrow(product(turned, 1, 1)), "dp", other_core)
        chip1 = narrow(product(turned, 0, 1) + core1.astype(jnp.float32))
        far = lax.ppermute(chip1, "dp", other_y)
        turned, _ = lax.optimization_barrier((turned, chip1))
        extra = pl.pallas_call(
            statistics_kernel,
            out_shape=jax.ShapeDtypeStruct((extra_rows, STRIPE), jnp.bfloat16),
            in_specs=[vmem_spec()] * 4,
            out_specs=vmem_spec(),
            scratch_shapes=[pltpu.VMEM((LANES, LANES), jnp.float32)],
            compiler_params=params,
            cost_estimate=pl.CostEstimate(
                flops=2 * features * span * (ROWS + LANES),
                bytes_accessed=2 * features * span,
                transcendentals=0,
            ),
            name="statistics",
        )(turned, member, difficult_distractors, lowering_factor_matrix)
        chip = extra.astype(jnp.float32)
        chip = narrow(chip + lax.ppermute(extra, "dp", other_core).astype(jnp.float32))
        far_chip = lax.ppermute(chip, "dp", other_y)
        core0 = lax.ppermute(narrow(product(turned, 1, 0)), "dp", other_core)
        own0 = narrow(product(turned, 0, 0))
        return own0, core0, far, chip, far_chip, member

    first = project(0, FIRST)
    many = jnp.sum((ids != 0).astype(jnp.int32)) > FIRST
    left = tokens - FIRST
    shapes = jax.eval_shape(lambda: project(FIRST, left))
    rest = lax.cond(
        many,
        lambda: project(FIRST, left),
        lambda: tuple(jnp.zeros(x.shape, x.dtype) for x in shapes),
    )
    sent, misc = pl.pallas_call(
        functools.partial(pool_kernel, model_width=float(features * shards)),
        out_shape=[
            jax.ShapeDtypeStruct(((texts + 1) * ROWS, width), jnp.bfloat16),
            jax.ShapeDtypeStruct((ROWS, width), jnp.float32),
        ],
        in_specs=[vmem_spec()] * 14,
        out_specs=[vmem_spec()] * 2,
        scratch_shapes=[
            pltpu.VMEM((LANES, width), jnp.bfloat16),
            pltpu.VMEM((ROWS, width), jnp.float32),
            pltpu.VMEM((texts * ROWS, width), jnp.float32),
        ],
        compiler_params=params,
        name="pool",
    )(ids, *first, *rest, raising_factor_matrix)
    far_side = lax.ppermute(sent, "group", [(0, 1), (1, 0)])
    rows = 2 * ROWS
    packed, slopes = pl.pallas_call(
        dots_kernel,
        out_shape=[
            jax.ShapeDtypeStruct((rows + width // LANES * rows, LANES), jnp.float32),
            jax.ShapeDtypeStruct((2 * texts * ROWS, width), jnp.bfloat16),
        ],
        in_specs=[vmem_spec()] * 2,
        out_specs=[vmem_spec()] * 2,
        compiler_params=params,
        name="dots",
    )(sent, far_side)
    packed = exchange(packed, "dp", shards)
    dots = [x[0:rows] for x in packed]
    dots = exchange((dots[0] + dots[1]) + (dots[2] + dots[3]), "mp", parts)
    over_y = lax.ppermute(slopes, "dp", other_y)
    slopes = [
        slopes,
        lax.ppermute(slopes, "dp", other_core),
        over_y,
        lax.ppermute(over_y, "dp", other_core),
    ]
    embeddings, losses, update = pl.pallas_call(
        functools.partial(
            score_kernel, texts=texts, stripes=pl.cdiv(FIRST, STRIPE), negatives=negatives
        ),
        out_shape=[
            jax.ShapeDtypeStruct((1, per_shard, part_width), jnp.bfloat16),
            jax.ShapeDtypeStruct((1, per_shard), jnp.float32),
            jax.ShapeDtypeStruct((ROWS, part_width), jnp.float32),
        ],
        in_specs=[vmem_spec()] * 13 + [smem_spec()],
        out_specs=[vmem_spec()] * 3,
        compiler_params=params,
        name="score",
    )(*packed, *slopes, *dots, misc, logit_sharpness)
    return (embeddings, losses, update)


def body(words, hard, vocabulary, weight, lowering, raising, sharpness):
    shards, parts = lax.axis_size("dp"), lax.axis_size("mp")
    texts, length = words.shape[1:]
    features, vocab = vocabulary.shape
    negatives = hard.shape[1]
    square = shards == 4 and features == weight.shape[1] == 4 * STRIPE and parts == shards
    small = texts <= ROWS - 2 and length == LANES and FIRST < texts * length <= 2048
    even = (texts * length - FIRST) % CHUNK == 0 and vocab % IDS_PER_BLOCK == 0
    fits = features * vocab <= 2**24 and features % (4 * LANES) == 0
    spare = pl.cdiv(FIRST, STRIPE) + negatives <= ROWS and lowering.shape[0] == ROWS
    fast = square and small and even and fits and spare and lax.axis_size("group") == 2
    chosen = split_body if fast else general_body
    return chosen(words, hard, vocabulary, weight, lowering, raising, sharpness)


def solution(mesh):
    in_specs = (
        P("group", None, None),
        P("dp", None),
        P("dp", None),
        P("dp", "mp"),
        P(),
        P(None, "mp"),
        P(),
    )
    out_specs = (P("group", "dp", "mp"), P("group", "dp"), P(None, "mp"))
    return jax.shard_map(body, mesh=mesh, in_specs=in_specs, out_specs=out_specs, check_vma=False)
```

```python
import functools

import jax
import jax.numpy as jnp
from jax import lax
from jax.experimental import pallas as pl
from jax.experimental.pallas import tpu as pltpu
from jax.sharding import PartitionSpec as P


def general_body(
    query_passage_words,
    difficult_distractors,
    vocabulary_vectors,
    layer_weight_matrix,
    lowering_factor_matrix,
    raising_factor_matrix,
    logit_sharpness,
):
    group_index = lax.axis_index("group")
    shard_index = lax.axis_index("dp")
    part_index = lax.axis_index("mp")
    shard_count = lax.axis_size("dp")
    side_ids = query_passage_words[0]
    text_count = side_ids.shape[0]
    length = side_ids.shape[1]
    per_shard = text_count // shard_count
    own_ids = lax.dynamic_slice_in_dim(side_ids, shard_index * per_shard, per_shard, 0)
    columns = jnp.take(vocabulary_vectors, side_ids.reshape(-1), axis=1)
    inputs = lax.all_to_all(columns, "dp", split_axis=1, concat_axis=0, tiled=True)
    tokens = inputs.shape[1]
    feature_width = raising_factor_matrix.shape[1]
    wide_inputs = inputs.astype(jnp.float32)
    inverse = lax.rsqrt(jnp.mean(wide_inputs * wide_inputs, axis=0) + 1e-05)
    normed_state = (wide_inputs * inverse[None, :]).astype(jnp.bfloat16)
    linear_map = lax.dot_general(
        lax.all_gather(layer_weight_matrix, "dp", axis=0, tiled=True),
        normed_state,
        (((0,), (0,)), ((), ())),
        preferred_element_type=jnp.float32,
    )
    reduced_sum = jnp.dot(
        lowering_factor_matrix, normed_state, preferred_element_type=jnp.float32
    ).astype(jnp.bfloat16)
    linear_map = linear_map + lax.dot_general(
        raising_factor_matrix,
        reduced_sum,
        (((0,), (0,)), ((), ())),
        preferred_element_type=jnp.float32,
    )
    own_inputs = lax.dynamic_slice_in_dim(
        inputs, part_index * feature_width, feature_width, 0
    ).astype(jnp.float32)
    hidden_state = own_inputs + jax.nn.silu(linear_map)
    mask = (own_ids != 0).astype(jnp.float32)
    counts = jnp.sum(mask, axis=1)
    summed = jnp.einsum("dnl,nl->nd", hidden_state.reshape(feature_width, per_shard, length), mask)
    pooled = (summed / counts[:, None]).astype(jnp.bfloat16)
    gathered = lax.all_gather(pooled, ("group", "dp"), axis=0, tiled=True)
    part_scores = lax.dot_general(
        pooled, gathered, (((1,), (1,)), ((), ())), preferred_element_type=jnp.float32
    )
    gathered_wide = gathered.astype(jnp.float32)
    part_norms = jnp.sum(gathered_wide * gathered_wide, axis=1)
    dots, norms = lax.psum((part_scores, part_norms), "mp")
    rnorm_all = lax.rsqrt(norms + 1e-06)
    all_count = gathered.shape[0]
    half_count = all_count // 2
    own_rows = (
        group_index * half_count + shard_index * per_shard + jnp.arange(per_shard, dtype=jnp.int32)
    )
    rnorm_own = jnp.take(rnorm_all, own_rows)
    cosine = dots * rnorm_own[:, None] * rnorm_all[None, :]
    multiplier_factor = logit_sharpness[0]
    scores = multiplier_factor * cosine
    column_ids = jnp.arange(all_count, dtype=jnp.int32)
    keep = column_ids[None, :] != own_rows[:, None]
    pair = (own_rows + half_count) % all_count
    weight = (group_index == 0).astype(jnp.float32)
    neg_cols = half_count + difficult_distractors
    top = jnp.max(jnp.where(keep, scores, -jnp.inf), axis=1)
    safe_scores = jnp.where(keep, scores, top[:, None])
    expd = jnp.where(keep, jnp.exp(safe_scores - top[:, None]), 0.0)
    neg_exp = (
        jnp.exp(jnp.minimum(jnp.take_along_axis(scores, neg_cols, axis=1) - top[:, None], 0.0))
        * weight
    )
    total = jnp.sum(expd, axis=1) + jnp.sum(neg_exp, axis=1)
    pair_score = jnp.take_along_axis(scores, pair[:, None], axis=1)[:, 0]
    losses = top + jnp.log(total) - pair_score
    onehot = (column_ids[None, None, :] == neg_cols[:, :, None]).astype(jnp.float32)
    probs = (expd + jnp.einsum("rk,rkc->rc", neg_exp, onehot)) / total[:, None]
    target = (column_ids[None, :] == pair[:, None]).astype(jnp.float32)
    grad_scores = (probs - target) / all_count
    coeff = (grad_scores * rnorm_own[:, None] * rnorm_all[None, :]).astype(jnp.bfloat16)
    along = jnp.dot(coeff, gathered, preferred_element_type=jnp.float32)
    pooled_wide = pooled.astype(jnp.float32)
    radial = jnp.sum(grad_scores * cosine, axis=1) * rnorm_own * rnorm_own
    embedding_gradient = multiplier_factor * (along - radial[:, None] * pooled_wide)
    token_grad = jnp.einsum("nd,nl->dnl", embedding_gradient / counts[:, None], mask).reshape(
        feature_width, tokens
    )
    sigma = jax.nn.sigmoid(linear_map)
    local = (token_grad * sigma * (1.0 + linear_map * (1.0 - sigma))).astype(jnp.bfloat16)
    up_portion = lax.dot_general(
        reduced_sum, local, (((1,), (1,)), ((), ())), preferred_element_type=jnp.float32
    )
    adapter_up_gradient = lax.psum(up_portion, ("group", "dp"))
    embeddings = (pooled_wide * rnorm_own[:, None]).astype(jnp.bfloat16)[None]
    return (embeddings, losses[None], adapter_up_gradient)


BLOCK_BITS, GROUP_BITS, LANE_BITS, ROW_BITS = 10, 9, 7, 4
IDS_PER_BLOCK = 1 << BLOCK_BITS
IDS_PER_GROUP = 1 << GROUP_BITS
CHUNK = 384
STRIPE = 256
ROWS = 1 << ROW_BITS
LANES = 1 << LANE_BITS
FEATURE_ROWS = 128
FIRST = 1152
NT = (((1,), (1,)), ((), ()))
VMEM_BYTES = 60 * 1024 * 1024


def mm(a, b, dims=(((1,), (0,)), ((), ()))):
    return lax.dot_general(a, b, dims, preferred_element_type=jnp.float32)


def split(x):
    high = x.astype(jnp.bfloat16)
    return high, (x - high.astype(jnp.float32)).astype(jnp.bfloat16)


def iota(shape, dim):
    return lax.broadcasted_iota(jnp.int32, shape, dim)


def quarter_of(dp_index, cores=2):
    return (dp_index % cores) * 2 + dp_index // cores


def split_quarter(i, j, cores=2):
    shard = lax.axis_index("dp")
    core, side_y = lax.rem(shard, cores), lax.div(shard, cores)
    return (core ^ i) * 2 + (side_y ^ j)


def take_lanes(x, lanes):
    numbers = lax.GatherDimensionNumbers(
        offset_dims=(),
        collapsed_slice_dims=(1,),
        start_index_map=(1,),
        operand_batching_dims=(0,),
        start_indices_batching_dims=(0,),
    )
    mode = lax.GatherScatterMode.PROMISE_IN_BOUNDS
    return lax.gather(x, lanes[..., None], numbers, slice_sizes=(1, 1), mode=mode)


def gather_kernel(
    ids_ref,
    vocab_ref,
    turned,
    member_ref,
    held,
    token_ref,
    ranks,
    counted,
    bounds,
    held_sems,
    bounds_sem,
    base,
):
    texts, length = ids_ref.shape
    features, vocab = vocab_ref.shape
    blocks = vocab // IDS_PER_BLOCK
    groups = vocab // IDS_PER_GROUP
    span = member_ref.shape[0]

    def vocab_copy(b):
        columns = pl.ds(pl.multiple_of(b * IDS_PER_BLOCK, LANES), IDS_PER_BLOCK)
        return pltpu.make_async_copy(vocab_ref.at[:, columns], held.at[b], held_sems.at[b])

    vocab_copy(0).start()
    for b in range(1, blocks):
        vocab_copy(b).start()

    ids = ids_ref[...]
    valid = ids != 0
    group_of = jnp.where(valid, lax.shift_right_logical(ids, GROUP_BITS), groups)
    group_rows = counted.shape[0]
    group_id = iota((group_rows, length), 0)
    below = jnp.zeros((group_rows, length), jnp.float32)
    for text in range(texts):
        below += jnp.where(group_of[text : text + 1] < group_id, 1.0, 0.0)
    before = jnp.broadcast_to(jnp.sum(below, axis=1, keepdims=True), (group_rows, length))
    counted[...] = before.astype(jnp.int32)
    bounds_copy = pltpu.make_async_copy(counted, bounds, bounds_sem)
    bounds_copy.start()
    earlier = jnp.where(iota((length, length), 0) < iota((length, length), 1), 1.0, 0.0).astype(
        jnp.bfloat16
    )
    for text in range(texts):
        here = jnp.where(group_of[text : text + 1] == group_id, 1.0, 0.0)
        inside = mm(here.astype(jnp.bfloat16), earlier)
        ranks[pl.ds(text, 1), :] = jnp.sum(here * (inside + before), axis=0, keepdims=True)
        before += jnp.broadcast_to(jnp.sum(here, axis=1, keepdims=True), (group_rows, length))
    text_of = iota((texts, length), 0)
    carried = jnp.where(valid, lax.shift_left(ids, ROW_BITS) + text_of, 0).astype(jnp.float32)
    rank = ranks[...]

    def place(p, carry):
        position = (iota((LANES, length), 0) + (p * LANES + base)).astype(jnp.float32)
        total = jnp.zeros((LANES, length), jnp.float32)
        for text in range(texts):
            total += jnp.where(rank[text : text + 1] == position, carried[text : text + 1], 0.0)
        found = jnp.broadcast_to(jnp.sum(total, axis=1, keepdims=True), (LANES, LANES))
        start = pl.multiple_of(p * LANES, LANES)
        row = found.T[0:1].astype(jnp.int32)
        token = lax.shift_right_logical(row, ROW_BITS)
        token_ref[pl.ds(p, 1), :] = jnp.where(token == 0, -vocab, token)
        found = found.astype(jnp.int32)
        real = (found >= ROWS) & ((found & (ROWS - 1)) == iota((LANES, LANES), 1))
        member_ref[pl.ds(start, LANES), :] = jnp.where(real, 1.0, 0.0).astype(jnp.bfloat16)
        turned[:, pl.ds(start, LANES)] = jnp.zeros((features, LANES), jnp.bfloat16)
        return carry

    lax.fori_loop(0, span // LANES, place, 0)
    bounds_copy.wait()

    def within(place):
        return jnp.clip(place - base, 0, span)

    def take(b, carry):
        vocab_copy(b).wait()
        for part in range(IDS_PER_BLOCK // IDS_PER_GROUP):
            group = b * (IDS_PER_BLOCK // IDS_PER_GROUP) + part
            first, last = within(bounds[group, 0]), within(bounds[group + 1, 0])
            begin = lax.shift_right_logical(first, LANE_BITS)
            end = lax.shift_right_logical(last + LANES - 1, LANE_BITS)

            def window(p, carry):
                at = pl.ds(pl.multiple_of(p * LANES, LANES), LANES)
                token = token_ref[pl.ds(p, 1), :] - group * IDS_PER_GROUP
                token = jnp.broadcast_to(token, (FEATURE_ROWS, LANES))
                lane = (token & (LANES - 1)).astype(jnp.int16)
                tile = lax.shift_right_arithmetic(token, LANE_BITS).astype(jnp.int16)
                pieces = [pl.ds(f, FEATURE_ROWS) for f in range(0, features, FEATURE_ROWS)]
                fresh = []
                for rows in pieces:
                    total = jnp.zeros((FEATURE_ROWS, LANES), jnp.bfloat16)
                    for j in range(IDS_PER_GROUP // LANES):
                        columns = pl.ds(part * IDS_PER_GROUP + j * LANES, LANES)
                        total = jnp.where(tile == j, take_lanes(held[b, rows, columns], lane), total)
                    fresh.append(total)
                fresh = [turned[rows, at] + total for rows, total in zip(pieces, fresh)]
                for rows, total in zip(pieces, fresh):
                    turned[rows, at] = total
                return carry

            lax.fori_loop(begin, jnp.where(last > first, end, begin), window, 0)
        return carry

    lax.fori_loop(0, blocks, take, 0)


def statistics_kernel(turned, member_ref, hard_ref, lower_ref, extra_ref, small):
    features, span = turned.shape
    stripes = pl.cdiv(span, STRIPE)
    per_shard, negatives = hard_ref.shape
    shard = lax.axis_index("dp")
    small[...] = jnp.zeros_like(small)
    small[0:per_shard, stripes : stripes + negatives] = hard_ref[...].astype(jnp.float32)
    lower = lower_ref[:, pl.ds(pl.multiple_of(shard * features, LANES), features)]

    misc = jnp.zeros((ROWS, STRIPE), jnp.float32)
    residual = jnp.zeros((features, LANES), jnp.float32)
    for stripe in range(stripes):
        size = min(STRIPE, span - stripe * STRIPE)
        across = pl.ds(stripe * STRIPE, size)
        upright = turned[:, across]
        wide = upright.astype(jnp.float32)
        square = jnp.sum(wide * wide, axis=0, keepdims=True)
        reduced = mm(lower, upright)
        if size < STRIPE:
            none = jnp.zeros((ROWS, STRIPE - size), jnp.float32)
            reduced = jnp.concatenate([reduced, none], axis=1)
            square = jnp.concatenate([square, none[0:1]], axis=1)
        extra_ref[stripe * ROWS : (stripe + 1) * ROWS, :] = reduced.astype(jnp.bfloat16)
        misc = jnp.where(iota((ROWS, STRIPE), 0) == stripe, square, misc)
        residual += mm(upright, member_ref[across, :])
    hard = small[...].T[0:ROWS]
    for i in range(per_shard):
        misc += jnp.where(iota((ROWS, STRIPE), 1) == shard * per_shard + i, hard[:, i : i + 1], 0.0)
    extra_ref[stripes * ROWS : (stripes + 1) * ROWS, :] = misc.astype(jnp.bfloat16)
    residual = jnp.where(lax.axis_index("mp") == shard, residual.T[0:ROWS], 0.0)
    for q in range(features // STRIPE):
        start = (stripes + 1 + q) * ROWS
        extra_ref[start : start + ROWS, :] = residual[:, q * STRIPE : (q + 1) * STRIPE].astype(
            jnp.bfloat16
        )


def pool_kernel(
    ids_ref,
    own_ref,
    core_ref,
    far_ref,
    extra_ref,
    member_ref,
    own_rest,
    core_rest,
    far_rest,
    extra_rest,
    member_rest,
    raise_ref,
    sent_ref,
    misc_ref,
    raised,
    total,
    slopes,
    model_width,
):
    texts, length = ids_ref.shape
    width = own_ref.shape[1]
    quarter = quarter_of(lax.axis_index("dp"))
    raised[...] = jnp.zeros_like(raised)
    raised[0:ROWS, :] = raise_ref[:, pl.ds(pl.multiple_of(quarter * width, LANES), width)]
    total[...] = jnp.zeros_like(total)
    slopes[...] = jnp.zeros_like(slopes)

    def add(refs, extra_ref, member_ref, base):
        span = member_ref.shape[0]
        stripes = pl.cdiv(span, STRIPE)

        def summed(start, size):
            return sum(ref[pl.ds(start, size), :].astype(jnp.float32) for ref in refs)

        misc = extra_ref[stripes * ROWS : (stripes + 1) * ROWS, :]
        if base == 0:
            misc_ref[...] = misc
        inverse = lax.rsqrt(misc / model_width + 1e-05)
        for k in range(stripes):
            size = min(STRIPE, span - k * STRIPE)
            scale = inverse[k : k + 1]
            reduced = (extra_ref[k * ROWS : (k + 1) * ROWS, :] * scale).astype(jnp.bfloat16)
            reduced = reduced.astype(jnp.float32)
            stacked = jnp.concatenate([reduced, jnp.broadcast_to(scale, (LANES - ROWS, STRIPE))])
            turned = stacked[:, 0:size].T
            low = turned.astype(jnp.bfloat16)
            linear = summed(k * STRIPE, size)
            linear = linear * turned[:, ROWS : ROWS + 1] + mm(low, raised[...])
            sigma = 1.0 / (1.0 + jnp.exp(-linear))
            slope = (sigma * (1.0 + linear * (1.0 - sigma))).astype(jnp.bfloat16)
            member = member_ref[pl.ds(k * STRIPE, size), :].astype(jnp.float32).T
            high, rest = split(linear * sigma)
            chosen = member[0:ROWS].astype(jnp.bfloat16)
            total[...] += mm(chosen, high) + mm(chosen, rest)
            spread = [reduced[:, 0:size] * member[text : text + 1] for text in range(texts)]
            slopes[...] += mm(jnp.concatenate(spread).astype(jnp.bfloat16), slope)
        start = pl.multiple_of((stripes + 1 + quarter) * ROWS, ROWS)
        total[...] += extra_ref[pl.ds(start, ROWS), :]

    add((own_ref, core_ref, far_ref), extra_ref, member_ref, 0)
    real = (ids_ref[...] != 0).astype(jnp.float32)

    @pl.when(jnp.sum(real) > member_ref.shape[0])
    def _():
        add((own_rest, core_rest, far_rest), extra_rest, member_rest, member_ref.shape[0])

    counts = jnp.sum(real, axis=1, keepdims=True)
    pooled = total[0:texts] / counts
    pooled = jnp.concatenate([pooled, jnp.zeros((ROWS - texts, width), jnp.float32)])
    sent_ref[0:ROWS, :] = pooled.astype(jnp.bfloat16)
    for text in range(texts):
        part = slopes[text * ROWS : (text + 1) * ROWS, :] / counts[text : text + 1]
        sent_ref[(text + 1) * ROWS : (text + 2) * ROWS, :] = part.astype(jnp.bfloat16)


def both_sides(near, far):
    queries = lax.axis_index("group") == 0
    return jnp.concatenate([jnp.where(queries, near, far), jnp.where(queries, far, near)], axis=0)


def dots_kernel(near_ref, far_ref, packed_ref, slopes_ref):
    block = both_sides(near_ref[0:ROWS], far_ref[0:ROWS])
    rows = 2 * ROWS
    packed_ref[...] = jnp.zeros_like(packed_ref)
    packed_ref[0:rows, 0:rows] = mm(block, block, NT)
    for part in range(block.shape[1] // LANES):
        piece = block[:, part * LANES : (part + 1) * LANES]
        packed_ref[rows + part * rows : rows + (part + 1) * rows, :] = piece.astype(jnp.float32)
    size = near_ref.shape[0] - ROWS
    slopes_ref[0:size] = near_ref[ROWS:]
    slopes_ref[size:] = far_ref[ROWS:]


def score_kernel(
    packed0,
    packed1,
    packed2,
    packed3,
    slopes0,
    slopes1,
    slopes2,
    slopes3,
    dots0,
    dots1,
    dots2,
    dots3,
    misc_ref,
    sharp_ref,
    embed_ref,
    loss_ref,
    up_ref,
    texts,
    stripes,
    negatives,
):
    rows = 2 * ROWS
    per_shard = loss_ref.shape[1]
    group, shard = lax.axis_index("group"), lax.axis_index("dp")
    dots = ((dots0[...] + dots1[...]) + (dots2[...] + dots3[...]))[:, 0:rows]
    down, across = iota((rows, rows), 0), iota((rows, rows), 1)
    same = down == across
    real = (lax.rem(down, ROWS) < texts) & (lax.rem(across, ROWS) < texts)
    diagonal = jnp.where(same, dots, 0.0)
    rnorm_row = lax.rsqrt(jnp.sum(diagonal, axis=0, keepdims=True) + 1e-06)
    rnorm_col = lax.rsqrt(jnp.sum(diagonal, axis=1, keepdims=True) + 1e-06)
    sharpness = sharp_ref[0]
    cosine = dots * rnorm_col * rnorm_row
    scores = sharpness * cosine
    keep = real & ~same
    top = jnp.max(jnp.where(keep, scores, -jnp.inf), axis=0, keepdims=True)
    top = jnp.where(lax.rem(across[0:1], ROWS) < texts, top, 0.0)
    powers = jnp.exp(jnp.where(real, jnp.minimum(scores - top, 0.0), 0.0))
    hard = misc_ref[stripes : stripes + negatives, 0:rows].astype(jnp.int32) + ROWS
    times = jnp.zeros((rows, rows), jnp.float32)
    for k in range(negatives):
        times += jnp.where(hard[k : k + 1] == down, 1.0, 0.0)
    times = jnp.where(across < texts, times, 0.0)
    weights = (jnp.where(keep, 1.0, 0.0) + jnp.where(real, times, 0.0)) * powers
    total = jnp.sum(weights, axis=0, keepdims=True)
    total = jnp.where(lax.rem(across[0:1], ROWS) < texts, total, 1.0)
    pair = (down == lax.rem(across + ROWS, rows)) & real
    pair_score = jnp.sum(jnp.where(pair, scores, 0.0), axis=0, keepdims=True)
    losses = top + jnp.log(total) - pair_score
    grad_scores = (weights / total - jnp.where(pair, 1.0, 0.0)) / (2 * texts)
    coeff = (grad_scores * rnorm_col * rnorm_row).astype(jnp.bfloat16)
    radial = jnp.sum(grad_scores * cosine, axis=0, keepdims=True) * rnorm_row * rnorm_row

    first = shard * per_shard
    loss_col = jnp.sum(jnp.where(same, losses, 0.0), axis=1, keepdims=True)
    at = (iota((rows, LANES), 0) == group * ROWS + first + iota((rows, LANES), 1)) & (
        iota((rows, LANES), 1) < per_shard
    )
    loss_ref[...] = jnp.sum(jnp.where(at, loss_col, 0.0), axis=0, keepdims=True)[:, 0:per_shard]

    along_rows = coeff.astype(jnp.float32).T.astype(jnp.bfloat16)
    radial_col = jnp.sum(jnp.where(same, radial, 0.0), axis=1, keepdims=True)
    rnorm_own = jnp.where(group == 0, rnorm_col[0:ROWS], rnorm_col[ROWS:rows])
    chosen = iota((ROWS, ROWS), 1) == iota((ROWS, ROWS), 0) + first
    chosen = jnp.where(chosen & (iota((ROWS, ROWS), 0) < per_shard), 1.0, 0.0).astype(jnp.bfloat16)
    blocks = ((packed0, slopes0), (packed1, slopes1), (packed2, slopes2), (packed3, slopes3))
    for o, (packed, slopes) in enumerate(blocks):
        parts = packed.shape[0] // rows - 1
        width = parts * LANES
        halves = [packed[rows * (part + 1) : rows * (part + 2), :] for part in range(parts)]
        block = jnp.concatenate(halves, axis=1)
        along = mm(along_rows, block.astype(jnp.bfloat16))
        grad = sharpness * (along - radial_col * block)
        near, far = slopes[0 : slopes.shape[0] // 2], slopes[slopes.shape[0] // 2 :]
        queries = group == 0
        grad_near = jnp.where(queries, grad[0:ROWS], grad[ROWS:rows])
        grad_far = jnp.where(queries, grad[ROWS:rows], grad[0:ROWS])
        update = []
        for side, side_grad in ((near, grad_near), (far, grad_far)):
            total = jnp.zeros((ROWS, width), jnp.float32)
            for text in range(texts):
                slope = side[text * ROWS : (text + 1) * ROWS].astype(jnp.float32)
                total += side_grad[text : text + 1] * slope
            update.append(total)
        at = pl.multiple_of(quarter_of(shard ^ o) * width, LANES)
        up_ref[:, pl.ds(at, width)] = update[0] + update[1]
        own = jnp.where(queries, block[0:ROWS], block[ROWS:rows]) * rnorm_own
        picked = mm(chosen, own.astype(jnp.bfloat16)).astype(jnp.bfloat16)
        embed_ref[0, :, pl.ds(at, width)] = picked[0:per_shard]


def any_spec():
    return pl.BlockSpec(memory_space=pl.ANY)


def vmem_spec():
    return pl.BlockSpec(memory_space=pltpu.VMEM)


def smem_spec():
    return pl.BlockSpec(memory_space=pltpu.SMEM)


def exchange(x, axis, size):
    steps = [[(i, i ^ o) for i in range(size)] for o in range(1, size)]
    return [x] + [lax.ppermute(x, axis, step) for step in steps]


def split_body(
    query_passage_words,
    difficult_distractors,
    vocabulary_vectors,
    layer_weight_matrix,
    lowering_factor_matrix,
    raising_factor_matrix,
    logit_sharpness,
):
    shards, parts = lax.axis_size("dp"), lax.axis_size("mp")
    ids = query_passage_words[0]
    texts, length = ids.shape
    tokens = texts * length
    features, vocab = vocabulary_vectors.shape
    blocks = vocab // IDS_PER_BLOCK
    group_rows = 8 * pl.cdiv(vocab // IDS_PER_GROUP + 1, 8)
    per_shard, negatives = difficult_distractors.shape
    part_width = layer_weight_matrix.shape[1]
    width = part_width // shards
    params = pltpu.CompilerParams(vmem_limit_bytes=VMEM_BYTES)
    other_core = [(d, d ^ 1) for d in range(shards)]
    other_y = [(d, d ^ 2) for d in range(shards)]

    def columns(i, j):
        start = split_quarter(i, j) * width
        return lax.dynamic_slice(layer_weight_matrix, (0, start), (features, width))

    def project(base, span):
        stripes = pl.cdiv(span, STRIPE)
        extra_rows = (stripes + 1 + shards) * ROWS
        turned, member = pl.pallas_call(
            functools.partial(gather_kernel, base=base),
            out_shape=[
                jax.ShapeDtypeStruct((features, span), jnp.bfloat16),
                jax.ShapeDtypeStruct((span, LANES), jnp.bfloat16),
            ],
            in_specs=[vmem_spec(), any_spec()],
            out_specs=[vmem_spec()] * 2,
            scratch_shapes=[
                pltpu.VMEM((blocks, features, IDS_PER_BLOCK), jnp.bfloat16),
                pltpu.VMEM((8 * pl.cdiv(span // LANES, 8), LANES), jnp.int32),
                pltpu.VMEM((texts, length), jnp.float32),
                pltpu.VMEM((group_rows, length), jnp.int32),
                pltpu.SMEM((group_rows, length), jnp.int32),
                pltpu.SemaphoreType.DMA((blocks,)),
                pltpu.SemaphoreType.DMA,
            ],
            compiler_params=params,
            name="gather",
        )(ids, vocabulary_vectors)

        def product(turned, i, j):
            return mm(turned, columns(i, j), (((0,), (0,)), ((), ())))

        def narrow(x):
            return x.astype(jnp.bfloat16)

        core1 = lax.ppermute(narrow(product(turned, 1, 1)), "dp", other_core)
        chip1 = narrow(product(turned, 0, 1) + core1.astype(jnp.float32))
        far = lax.ppermute(chip1, "dp", other_y)
        turned, _ = lax.optimization_barrier((turned, chip1))
        extra = pl.pallas_call(
            statistics_kernel,
            out_shape=jax.ShapeDtypeStruct((extra_rows, STRIPE), jnp.bfloat16),
            in_specs=[vmem_spec()] * 4,
            out_specs=vmem_spec(),
            scratch_shapes=[pltpu.VMEM((LANES, LANES), jnp.float32)],
            compiler_params=params,
            cost_estimate=pl.CostEstimate(
                flops=2 * features * span * (ROWS + LANES),
                bytes_accessed=2 * features * span,
                transcendentals=0,
            ),
            name="statistics",
        )(turned, member, difficult_distractors, lowering_factor_matrix)
        chip = extra.astype(jnp.float32)
        chip += lax.ppermute(extra, "dp", other_core).astype(jnp.float32)
        extra = chip + lax.ppermute(narrow(chip), "dp", other_y).astype(jnp.float32)
        core0 = lax.ppermute(narrow(product(turned, 1, 0)), "dp", other_core)
        own0 = narrow(product(turned, 0, 0))
        return own0, core0, far, extra, member

    first = project(0, FIRST)
    many = jnp.sum((ids != 0).astype(jnp.int32)) > FIRST
    left = tokens - FIRST
    shapes = jax.eval_shape(lambda: project(FIRST, left))
    rest = lax.cond(
        many,
        lambda: project(FIRST, left),
        lambda: tuple(jnp.zeros(x.shape, x.dtype) for x in shapes),
    )
    sent, misc = pl.pallas_call(
        functools.partial(pool_kernel, model_width=float(features * shards)),
        out_shape=[
            jax.ShapeDtypeStruct(((texts + 1) * ROWS, width), jnp.bfloat16),
            jax.ShapeDtypeStruct((ROWS, width), jnp.float32),
        ],
        in_specs=[vmem_spec()] * 12,
        out_specs=[vmem_spec()] * 2,
        scratch_shapes=[
            pltpu.VMEM((LANES, width), jnp.bfloat16),
            pltpu.VMEM((ROWS, width), jnp.float32),
            pltpu.VMEM((texts * ROWS, width), jnp.float32),
        ],
        compiler_params=params,
        name="pool",
    )(ids, *first, *rest, raising_factor_matrix)
    far_side = lax.ppermute(sent, "group", [(0, 1), (1, 0)])
    rows = 2 * ROWS
    packed, slopes = pl.pallas_call(
        dots_kernel,
        out_shape=[
            jax.ShapeDtypeStruct((rows + width // LANES * rows, LANES), jnp.float32),
            jax.ShapeDtypeStruct((2 * texts * ROWS, width), jnp.bfloat16),
        ],
        in_specs=[vmem_spec()] * 2,
        out_specs=[vmem_spec()] * 2,
        compiler_params=params,
        name="dots",
    )(sent, far_side)
    packed = exchange(packed, "dp", shards)
    dots = [x[0:rows] for x in packed]
    dots = (dots[0] + dots[1]) + (dots[2] + dots[3])
    slopes, dots = lax.optimization_barrier((slopes, dots))
    dots = exchange(dots, "mp", parts)
    over_y = lax.ppermute(slopes, "dp", other_y)
    slopes = [
        slopes,
        lax.ppermute(slopes, "dp", other_core),
        over_y,
        lax.ppermute(over_y, "dp", other_core),
    ]
    embeddings, losses, update = pl.pallas_call(
        functools.partial(
            score_kernel, texts=texts, stripes=pl.cdiv(FIRST, STRIPE), negatives=negatives
        ),
        out_shape=[
            jax.ShapeDtypeStruct((1, per_shard, part_width), jnp.bfloat16),
            jax.ShapeDtypeStruct((1, per_shard), jnp.float32),
            jax.ShapeDtypeStruct((ROWS, part_width), jnp.float32),
        ],
        in_specs=[vmem_spec()] * 13 + [smem_spec()],
        out_specs=[vmem_spec()] * 3,
        compiler_params=params,
        name="score",
    )(*packed, *slopes, *dots, misc, logit_sharpness)
    return (embeddings, losses, update)


def body(words, hard, vocabulary, weight, lowering, raising, sharpness):
    shards, parts = lax.axis_size("dp"), lax.axis_size("mp")
    texts, length = words.shape[1:]
    features, vocab = vocabulary.shape
    negatives = hard.shape[1]
    square = shards == 4 and features == weight.shape[1] == 4 * STRIPE and parts == shards
    small = texts <= ROWS - 2 and length == LANES and FIRST < texts * length <= 2048
    even = (texts * length - FIRST) % CHUNK == 0 and vocab % IDS_PER_BLOCK == 0
    fits = features * vocab <= 2**24 and features % (4 * LANES) == 0
    spare = pl.cdiv(FIRST, STRIPE) + negatives <= ROWS and lowering.shape[0] == ROWS
    fast = square and small and even and fits and spare and lax.axis_size("group") == 2
    chosen = split_body if fast else general_body
    return chosen(words, hard, vocabulary, weight, lowering, raising, sharpness)


def solution(mesh):
    in_specs = (
        P("group", None, None),
        P("dp", None),
        P("dp", None),
        P("dp", "mp"),
        P(),
        P(None, "mp"),
        P(),
    )
    out_specs = (P("group", "dp", "mp"), P("group", "dp"), P(None, "mp"))
    return jax.shard_map(body, mesh=mesh, in_specs=in_specs, out_specs=out_specs, check_vma=False)
```

```python
import functools

import jax
import jax.numpy as jnp
from jax import lax
from jax.experimental import pallas as pl
from jax.experimental.pallas import tpu as pltpu
from jax.sharding import PartitionSpec as P


def general_body(
    query_passage_words,
    difficult_distractors,
    vocabulary_vectors,
    layer_weight_matrix,
    lowering_factor_matrix,
    raising_factor_matrix,
    logit_sharpness,
):
    group_index = lax.axis_index("group")
    shard_index = lax.axis_index("dp")
    part_index = lax.axis_index("mp")
    shard_count = lax.axis_size("dp")
    side_ids = query_passage_words[0]
    text_count = side_ids.shape[0]
    length = side_ids.shape[1]
    per_shard = text_count // shard_count
    own_ids = lax.dynamic_slice_in_dim(side_ids, shard_index * per_shard, per_shard, 0)
    columns = jnp.take(vocabulary_vectors, side_ids.reshape(-1), axis=1)
    inputs = lax.all_to_all(columns, "dp", split_axis=1, concat_axis=0, tiled=True)
    tokens = inputs.shape[1]
    feature_width = raising_factor_matrix.shape[1]
    wide_inputs = inputs.astype(jnp.float32)
    inverse = lax.rsqrt(jnp.mean(wide_inputs * wide_inputs, axis=0) + 1e-05)
    normed_state = (wide_inputs * inverse[None, :]).astype(jnp.bfloat16)
    linear_map = lax.dot_general(
        lax.all_gather(layer_weight_matrix, "dp", axis=0, tiled=True),
        normed_state,
        (((0,), (0,)), ((), ())),
        preferred_element_type=jnp.float32,
    )
    reduced_sum = jnp.dot(
        lowering_factor_matrix, normed_state, preferred_element_type=jnp.float32
    ).astype(jnp.bfloat16)
    linear_map = linear_map + lax.dot_general(
        raising_factor_matrix,
        reduced_sum,
        (((0,), (0,)), ((), ())),
        preferred_element_type=jnp.float32,
    )
    own_inputs = lax.dynamic_slice_in_dim(
        inputs, part_index * feature_width, feature_width, 0
    ).astype(jnp.float32)
    hidden_state = own_inputs + jax.nn.silu(linear_map)
    mask = (own_ids != 0).astype(jnp.float32)
    counts = jnp.sum(mask, axis=1)
    summed = jnp.einsum("dnl,nl->nd", hidden_state.reshape(feature_width, per_shard, length), mask)
    pooled = (summed / counts[:, None]).astype(jnp.bfloat16)
    gathered = lax.all_gather(pooled, ("group", "dp"), axis=0, tiled=True)
    part_scores = lax.dot_general(
        pooled, gathered, (((1,), (1,)), ((), ())), preferred_element_type=jnp.float32
    )
    gathered_wide = gathered.astype(jnp.float32)
    part_norms = jnp.sum(gathered_wide * gathered_wide, axis=1)
    dots, norms = lax.psum((part_scores, part_norms), "mp")
    rnorm_all = lax.rsqrt(norms + 1e-06)
    all_count = gathered.shape[0]
    half_count = all_count // 2
    own_rows = (
        group_index * half_count + shard_index * per_shard + jnp.arange(per_shard, dtype=jnp.int32)
    )
    rnorm_own = jnp.take(rnorm_all, own_rows)
    cosine = dots * rnorm_own[:, None] * rnorm_all[None, :]
    multiplier_factor = logit_sharpness[0]
    scores = multiplier_factor * cosine
    column_ids = jnp.arange(all_count, dtype=jnp.int32)
    keep = column_ids[None, :] != own_rows[:, None]
    pair = (own_rows + half_count) % all_count
    weight = (group_index == 0).astype(jnp.float32)
    neg_cols = half_count + difficult_distractors
    top = jnp.max(jnp.where(keep, scores, -jnp.inf), axis=1)
    safe_scores = jnp.where(keep, scores, top[:, None])
    expd = jnp.where(keep, jnp.exp(safe_scores - top[:, None]), 0.0)
    neg_exp = (
        jnp.exp(jnp.minimum(jnp.take_along_axis(scores, neg_cols, axis=1) - top[:, None], 0.0))
        * weight
    )
    total = jnp.sum(expd, axis=1) + jnp.sum(neg_exp, axis=1)
    pair_score = jnp.take_along_axis(scores, pair[:, None], axis=1)[:, 0]
    losses = top + jnp.log(total) - pair_score
    onehot = (column_ids[None, None, :] == neg_cols[:, :, None]).astype(jnp.float32)
    probs = (expd + jnp.einsum("rk,rkc->rc", neg_exp, onehot)) / total[:, None]
    target = (column_ids[None, :] == pair[:, None]).astype(jnp.float32)
    grad_scores = (probs - target) / all_count
    coeff = (grad_scores * rnorm_own[:, None] * rnorm_all[None, :]).astype(jnp.bfloat16)
    along = jnp.dot(coeff, gathered, preferred_element_type=jnp.float32)
    pooled_wide = pooled.astype(jnp.float32)
    radial = jnp.sum(grad_scores * cosine, axis=1) * rnorm_own * rnorm_own
    embedding_gradient = multiplier_factor * (along - radial[:, None] * pooled_wide)
    token_grad = jnp.einsum("nd,nl->dnl", embedding_gradient / counts[:, None], mask).reshape(
        feature_width, tokens
    )
    sigma = jax.nn.sigmoid(linear_map)
    local = (token_grad * sigma * (1.0 + linear_map * (1.0 - sigma))).astype(jnp.bfloat16)
    up_portion = lax.dot_general(
        reduced_sum, local, (((1,), (1,)), ((), ())), preferred_element_type=jnp.float32
    )
    adapter_up_gradient = lax.psum(up_portion, ("group", "dp"))
    embeddings = (pooled_wide * rnorm_own[:, None]).astype(jnp.bfloat16)[None]
    return (embeddings, losses[None], adapter_up_gradient)


BLOCK_BITS, GROUP_BITS, LANE_BITS, ROW_BITS = 10, 9, 7, 4
IDS_PER_BLOCK = 1 << BLOCK_BITS
IDS_PER_GROUP = 1 << GROUP_BITS
CHUNK = 384
STRIPE = 256
ROWS = 1 << ROW_BITS
LANES = 1 << LANE_BITS
FEATURE_ROWS = 128
FIRST = 1152
TAKEN = 768
NT = (((1,), (1,)), ((), ()))
VMEM_BYTES = 60 * 1024 * 1024


def mm(a, b, dims=(((1,), (0,)), ((), ()))):
    return lax.dot_general(a, b, dims, preferred_element_type=jnp.float32)


def split(x):
    high = x.astype(jnp.bfloat16)
    return high, (x - high.astype(jnp.float32)).astype(jnp.bfloat16)


def iota(shape, dim):
    return lax.broadcasted_iota(jnp.int32, shape, dim)


def quarter_of(dp_index, cores=2):
    return (dp_index % cores) * 2 + dp_index // cores


def split_quarter(i, j, cores=2):
    shard = lax.axis_index("dp")
    core, side_y = lax.rem(shard, cores), lax.div(shard, cores)
    return (core ^ i) * 2 + (side_y ^ j)


def take_lanes(x, lanes):
    numbers = lax.GatherDimensionNumbers(
        offset_dims=(),
        collapsed_slice_dims=(1,),
        start_index_map=(1,),
        operand_batching_dims=(0,),
        start_indices_batching_dims=(0,),
    )
    mode = lax.GatherScatterMode.PROMISE_IN_BOUNDS
    return lax.gather(x, lanes[..., None], numbers, slice_sizes=(1, 1), mode=mode)


def gather_kernel(
    ids_ref,
    vocab_ref,
    turned,
    member_ref,
    held,
    token_ref,
    ranks,
    counted,
    bounds,
    held_sems,
    bounds_sem,
    base,
):
    texts, length = ids_ref.shape
    features, vocab = vocab_ref.shape
    blocks = vocab // IDS_PER_BLOCK
    groups = vocab // IDS_PER_GROUP
    span = member_ref.shape[0]

    def vocab_copy(b):
        columns = pl.ds(pl.multiple_of(b * IDS_PER_BLOCK, LANES), IDS_PER_BLOCK)
        return pltpu.make_async_copy(vocab_ref.at[:, columns], held.at[b], held_sems.at[b])

    vocab_copy(0).start()
    for b in range(1, blocks):
        vocab_copy(b).start()

    ids = ids_ref[...]
    valid = ids != 0
    group_of = jnp.where(valid, lax.shift_right_logical(ids, GROUP_BITS), groups)
    group_rows = counted.shape[0]
    group_id = iota((group_rows, length), 0)
    below = jnp.zeros((group_rows, length), jnp.float32)
    for text in range(texts):
        below += jnp.where(group_of[text : text + 1] < group_id, 1.0, 0.0)
    before = jnp.broadcast_to(jnp.sum(below, axis=1, keepdims=True), (group_rows, length))
    counted[...] = before.astype(jnp.int32)
    bounds_copy = pltpu.make_async_copy(counted, bounds, bounds_sem)
    bounds_copy.start()
    earlier = jnp.where(iota((length, length), 0) < iota((length, length), 1), 1.0, 0.0).astype(
        jnp.bfloat16
    )
    for text in range(texts):
        here = jnp.where(group_of[text : text + 1] == group_id, 1.0, 0.0)
        inside = mm(here.astype(jnp.bfloat16), earlier)
        ranks[pl.ds(text, 1), :] = jnp.sum(here * (inside + before), axis=0, keepdims=True)
        before += jnp.broadcast_to(jnp.sum(here, axis=1, keepdims=True), (group_rows, length))
    text_of = iota((texts, length), 0)
    carried = jnp.where(valid, lax.shift_left(ids, ROW_BITS) + text_of, 0).astype(jnp.float32)
    rank = ranks[...]

    def place(p, carry):
        position = (iota((LANES, length), 0) + (p * LANES + base)).astype(jnp.float32)
        total = jnp.zeros((LANES, length), jnp.float32)
        for text in range(texts):
            total += jnp.where(rank[text : text + 1] == position, carried[text : text + 1], 0.0)
        found = jnp.broadcast_to(jnp.sum(total, axis=1, keepdims=True), (LANES, LANES))
        start = pl.multiple_of(p * LANES, LANES)
        row = found.T[0:1].astype(jnp.int32)
        token = lax.shift_right_logical(row, ROW_BITS)
        token_ref[pl.ds(p, 1), :] = jnp.where(token == 0, -vocab, token)
        found = found.astype(jnp.int32)
        real = (found >= ROWS) & ((found & (ROWS - 1)) == iota((LANES, LANES), 1))
        member_ref[pl.ds(start, LANES), :] = jnp.where(real, 1.0, 0.0).astype(jnp.bfloat16)
        turned[:, pl.ds(start, LANES)] = jnp.zeros((features, LANES), jnp.bfloat16)
        return carry

    lax.fori_loop(0, span // LANES, place, 0)
    bounds_copy.wait()

    def within(place):
        return jnp.clip(place - base, 0, span)

    def take(b, carry):
        vocab_copy(b).wait()
        for part in range(IDS_PER_BLOCK // IDS_PER_GROUP):
            group = b * (IDS_PER_BLOCK // IDS_PER_GROUP) + part
            first, last = within(bounds[group, 0]), within(bounds[group + 1, 0])
            begin = lax.shift_right_logical(first, LANE_BITS)
            end = lax.shift_right_logical(last + LANES - 1, LANE_BITS)

            def window(p, carry):
                at = pl.ds(pl.multiple_of(p * LANES, LANES), LANES)
                token = token_ref[pl.ds(p, 1), :] - group * IDS_PER_GROUP
                token = jnp.broadcast_to(token, (FEATURE_ROWS, LANES))
                lane = (token & (LANES - 1)).astype(jnp.int16)
                tile = lax.shift_right_arithmetic(token, LANE_BITS).astype(jnp.int16)
                pieces = [pl.ds(f, FEATURE_ROWS) for f in range(0, TAKEN, FEATURE_ROWS)]
                short = jnp.broadcast_to(token[0:1], (IDS_PER_GROUP, LANES)).astype(jnp.int16)
                picked = jnp.where(
                    short == iota((IDS_PER_GROUP, LANES), 0).astype(jnp.int16), 1.0, 0.0
                ).astype(jnp.bfloat16)
                columns = pl.ds(part * IDS_PER_GROUP, IDS_PER_GROUP)
                rest = pl.ds(TAKEN, features - TAKEN)
                product = mm(held[b, rest, columns], picked).astype(jnp.bfloat16)
                fresh = []
                for rows in pieces:
                    total = jnp.zeros((FEATURE_ROWS, LANES), jnp.bfloat16)
                    for j in range(IDS_PER_GROUP // LANES):
                        columns = pl.ds(part * IDS_PER_GROUP + j * LANES, LANES)
                        total = jnp.where(tile == j, take_lanes(held[b, rows, columns], lane), total)
                    fresh.append(total)
                pieces.append(rest)
                fresh.append(product)
                fresh = [turned[rows, at] + total for rows, total in zip(pieces, fresh)]
                for rows, total in zip(pieces, fresh):
                    turned[rows, at] = total
                return carry

            lax.fori_loop(begin, jnp.where(last > first, end, begin), window, 0)
        return carry

    lax.fori_loop(0, blocks, take, 0)


def statistics_kernel(turned, member_ref, hard_ref, lower_ref, extra_ref, small):
    features, span = turned.shape
    stripes = pl.cdiv(span, STRIPE)
    per_shard, negatives = hard_ref.shape
    shard = lax.axis_index("dp")
    small[...] = jnp.zeros_like(small)
    small[0:per_shard, stripes : stripes + negatives] = hard_ref[...].astype(jnp.float32)
    lower = lower_ref[:, pl.ds(pl.multiple_of(shard * features, LANES), features)]

    misc = jnp.zeros((ROWS, STRIPE), jnp.float32)
    residual = jnp.zeros((features, LANES), jnp.float32)
    for stripe in range(stripes):
        size = min(STRIPE, span - stripe * STRIPE)
        across = pl.ds(stripe * STRIPE, size)
        upright = turned[:, across]
        wide = upright.astype(jnp.float32)
        square = jnp.sum(wide * wide, axis=0, keepdims=True)
        reduced = mm(lower, upright)
        if size < STRIPE:
            none = jnp.zeros((ROWS, STRIPE - size), jnp.float32)
            reduced = jnp.concatenate([reduced, none], axis=1)
            square = jnp.concatenate([square, none[0:1]], axis=1)
        extra_ref[stripe * ROWS : (stripe + 1) * ROWS, :] = reduced.astype(jnp.bfloat16)
        misc = jnp.where(iota((ROWS, STRIPE), 0) == stripe, square, misc)
        residual += mm(upright, member_ref[across, :])
    hard = small[...].T[0:ROWS]
    for i in range(per_shard):
        misc += jnp.where(iota((ROWS, STRIPE), 1) == shard * per_shard + i, hard[:, i : i + 1], 0.0)
    extra_ref[stripes * ROWS : (stripes + 1) * ROWS, :] = misc.astype(jnp.bfloat16)
    residual = jnp.where(lax.axis_index("mp") == shard, residual.T[0:ROWS], 0.0)
    for q in range(features // STRIPE):
        start = (stripes + 1 + q) * ROWS
        extra_ref[start : start + ROWS, :] = residual[:, q * STRIPE : (q + 1) * STRIPE].astype(
            jnp.bfloat16
        )


def fetch(pairs, sems):
    copies = [pltpu.make_async_copy(a, b, sems.at[n]) for n, (a, b) in enumerate(pairs)]
    for copy in copies:
        copy.start()
    for copy in copies:
        copy.wait()


def pool_kernel(
    ids_ref,
    own_ref,
    core_any,
    far_any,
    extra_ref,
    member_ref,
    own_rest,
    core_rest,
    far_rest,
    extra_rest,
    member_rest,
    raise_ref,
    sent_ref,
    misc_ref,
    raised,
    total,
    slopes,
    core_ref,
    far_ref,
    sems,
    model_width,
):
    texts, length = ids_ref.shape
    width = own_ref.shape[1]
    quarter = quarter_of(lax.axis_index("dp"))
    fetch([(core_any, core_ref), (far_any, far_ref)], sems)
    raised[...] = jnp.zeros_like(raised)
    raised[0:ROWS, :] = raise_ref[:, pl.ds(pl.multiple_of(quarter * width, LANES), width)]
    total[...] = jnp.zeros_like(total)
    slopes[...] = jnp.zeros_like(slopes)

    def add(refs, extra_ref, member_ref, base):
        span = member_ref.shape[0]
        stripes = pl.cdiv(span, STRIPE)

        def summed(start, size):
            return sum(ref[pl.ds(start, size), :].astype(jnp.float32) for ref in refs)

        misc = extra_ref[stripes * ROWS : (stripes + 1) * ROWS, :]
        if base == 0:
            misc_ref[...] = misc
        inverse = lax.rsqrt(misc / model_width + 1e-05)
        for k in range(stripes):
            size = min(STRIPE, span - k * STRIPE)
            scale = inverse[k : k + 1]
            reduced = (extra_ref[k * ROWS : (k + 1) * ROWS, :] * scale).astype(jnp.bfloat16)
            reduced = reduced.astype(jnp.float32)
            stacked = jnp.concatenate([reduced, jnp.broadcast_to(scale, (LANES - ROWS, STRIPE))])
            turned = stacked[:, 0:size].T
            low = turned.astype(jnp.bfloat16)
            linear = summed(k * STRIPE, size)
            linear = linear * turned[:, ROWS : ROWS + 1] + mm(low, raised[...])
            sigma = 1.0 / (1.0 + jnp.exp(-linear))
            slope = (sigma * (1.0 + linear * (1.0 - sigma))).astype(jnp.bfloat16)
            member = member_ref[pl.ds(k * STRIPE, size), :].astype(jnp.float32).T
            high, rest = split(linear * sigma)
            chosen = member[0:ROWS].astype(jnp.bfloat16)
            total[...] += mm(chosen, high) + mm(chosen, rest)
            spread = [reduced[:, 0:size] * member[text : text + 1] for text in range(texts)]
            slopes[...] += mm(jnp.concatenate(spread).astype(jnp.bfloat16), slope)
        start = pl.multiple_of((stripes + 1 + quarter) * ROWS, ROWS)
        total[...] += extra_ref[pl.ds(start, ROWS), :]

    add((own_ref, core_ref, far_ref), extra_ref, member_ref, 0)
    real = (ids_ref[...] != 0).astype(jnp.float32)

    @pl.when(jnp.sum(real) > member_ref.shape[0])
    def _():
        add((own_rest, core_rest, far_rest), extra_rest, member_rest, member_ref.shape[0])

    counts = jnp.sum(real, axis=1, keepdims=True)
    pooled = total[0:texts] / counts
    pooled = jnp.concatenate([pooled, jnp.zeros((ROWS - texts, width), jnp.float32)])
    sent_ref[0:ROWS, :] = pooled.astype(jnp.bfloat16)
    for text in range(texts):
        part = slopes[text * ROWS : (text + 1) * ROWS, :] / counts[text : text + 1]
        sent_ref[(text + 1) * ROWS : (text + 2) * ROWS, :] = part.astype(jnp.bfloat16)


def both_sides(near, far):
    queries = lax.axis_index("group") == 0
    return jnp.concatenate([jnp.where(queries, near, far), jnp.where(queries, far, near)], axis=0)


def dots_kernel(near_ref, far_any, packed_ref, slopes_ref, far_ref, sems):
    fetch([(far_any, far_ref)], sems)
    block = both_sides(near_ref[0:ROWS], far_ref[0:ROWS])
    rows = 2 * ROWS
    packed_ref[...] = jnp.zeros_like(packed_ref)
    packed_ref[0:rows, 0:rows] = mm(block, block, NT)
    for part in range(block.shape[1] // LANES):
        piece = block[:, part * LANES : (part + 1) * LANES]
        packed_ref[rows + part * rows : rows + (part + 1) * rows, :] = piece.astype(jnp.float32)
    size = near_ref.shape[0] - ROWS
    slopes_ref[0:size] = near_ref[ROWS:]
    slopes_ref[size:] = far_ref[ROWS:]


def score_kernel(*refs, texts, stripes, negatives):
    there, (misc_ref, sharp_ref, embed_ref, loss_ref, up_ref), (*here, sems) = (
        refs[0:12],
        refs[12:17],
        refs[17:],
    )
    fetch(list(zip(there, here)), sems)
    packed0, packed1, packed2, packed3, slopes0, slopes1, slopes2, slopes3 = here[0:8]
    dots0, dots1, dots2, dots3 = here[8:12]
    rows = 2 * ROWS
    per_shard = loss_ref.shape[1]
    group, shard = lax.axis_index("group"), lax.axis_index("dp")
    dots = ((dots0[...] + dots1[...]) + (dots2[...] + dots3[...]))[:, 0:rows]
    down, across = iota((rows, rows), 0), iota((rows, rows), 1)
    same = down == across
    real = (lax.rem(down, ROWS) < texts) & (lax.rem(across, ROWS) < texts)
    diagonal = jnp.where(same, dots, 0.0)
    rnorm_row = lax.rsqrt(jnp.sum(diagonal, axis=0, keepdims=True) + 1e-06)
    rnorm_col = lax.rsqrt(jnp.sum(diagonal, axis=1, keepdims=True) + 1e-06)
    sharpness = sharp_ref[0]
    cosine = dots * rnorm_col * rnorm_row
    scores = sharpness * cosine
    keep = real & ~same
    top = jnp.max(jnp.where(keep, scores, -jnp.inf), axis=0, keepdims=True)
    top = jnp.where(lax.rem(across[0:1], ROWS) < texts, top, 0.0)
    powers = jnp.exp(jnp.where(real, jnp.minimum(scores - top, 0.0), 0.0))
    hard = misc_ref[stripes : stripes + negatives, 0:rows].astype(jnp.int32) + ROWS
    times = jnp.zeros((rows, rows), jnp.float32)
    for k in range(negatives):
        times += jnp.where(hard[k : k + 1] == down, 1.0, 0.0)
    times = jnp.where(across < texts, times, 0.0)
    weights = (jnp.where(keep, 1.0, 0.0) + jnp.where(real, times, 0.0)) * powers
    total = jnp.sum(weights, axis=0, keepdims=True)
    total = jnp.where(lax.rem(across[0:1], ROWS) < texts, total, 1.0)
    pair = (down == lax.rem(across + ROWS, rows)) & real
    pair_score = jnp.sum(jnp.where(pair, scores, 0.0), axis=0, keepdims=True)
    losses = top + jnp.log(total) - pair_score
    grad_scores = (weights / total - jnp.where(pair, 1.0, 0.0)) / (2 * texts)
    coeff = (grad_scores * rnorm_col * rnorm_row).astype(jnp.bfloat16)
    radial = jnp.sum(grad_scores * cosine, axis=0, keepdims=True) * rnorm_row * rnorm_row

    first = shard * per_shard
    loss_col = jnp.sum(jnp.where(same, losses, 0.0), axis=1, keepdims=True)
    at = (iota((rows, LANES), 0) == group * ROWS + first + iota((rows, LANES), 1)) & (
        iota((rows, LANES), 1) < per_shard
    )
    loss_ref[...] = jnp.sum(jnp.where(at, loss_col, 0.0), axis=0, keepdims=True)[:, 0:per_shard]

    along_rows = coeff.astype(jnp.float32).T.astype(jnp.bfloat16)
    radial_col = jnp.sum(jnp.where(same, radial, 0.0), axis=1, keepdims=True)
    rnorm_own = jnp.where(group == 0, rnorm_col[0:ROWS], rnorm_col[ROWS:rows])
    chosen = iota((ROWS, ROWS), 1) == iota((ROWS, ROWS), 0) + first
    chosen = jnp.where(chosen & (iota((ROWS, ROWS), 0) < per_shard), 1.0, 0.0).astype(jnp.bfloat16)
    blocks = ((packed0, slopes0), (packed1, slopes1), (packed2, slopes2), (packed3, slopes3))
    for o, (packed, slopes) in enumerate(blocks):
        parts = packed.shape[0] // rows - 1
        width = parts * LANES
        halves = [packed[rows * (part + 1) : rows * (part + 2), :] for part in range(parts)]
        block = jnp.concatenate(halves, axis=1)
        along = mm(along_rows, block.astype(jnp.bfloat16))
        grad = sharpness * (along - radial_col * block)
        near, far = slopes[0 : slopes.shape[0] // 2], slopes[slopes.shape[0] // 2 :]
        queries = group == 0
        grad_near = jnp.where(queries, grad[0:ROWS], grad[ROWS:rows])
        grad_far = jnp.where(queries, grad[ROWS:rows], grad[0:ROWS])
        update = []
        for side, side_grad in ((near, grad_near), (far, grad_far)):
            total = jnp.zeros((ROWS, width), jnp.float32)
            for text in range(texts):
                slope = side[text * ROWS : (text + 1) * ROWS].astype(jnp.float32)
                total += side_grad[text : text + 1] * slope
            update.append(total)
        at = pl.multiple_of(quarter_of(shard ^ o) * width, LANES)
        up_ref[:, pl.ds(at, width)] = update[0] + update[1]
        own = jnp.where(queries, block[0:ROWS], block[ROWS:rows]) * rnorm_own
        picked = mm(chosen, own.astype(jnp.bfloat16)).astype(jnp.bfloat16)
        embed_ref[0, :, pl.ds(at, width)] = picked[0:per_shard]


def any_spec():
    return pl.BlockSpec(memory_space=pl.ANY)


def vmem_spec():
    return pl.BlockSpec(memory_space=pltpu.VMEM)


def smem_spec():
    return pl.BlockSpec(memory_space=pltpu.SMEM)


def exchange(x, axis, size):
    steps = [[(i, i ^ o) for i in range(size)] for o in range(1, size)]
    return [x] + [lax.ppermute(x, axis, step) for step in steps]


def split_body(
    query_passage_words,
    difficult_distractors,
    vocabulary_vectors,
    layer_weight_matrix,
    lowering_factor_matrix,
    raising_factor_matrix,
    logit_sharpness,
):
    shards, parts = lax.axis_size("dp"), lax.axis_size("mp")
    ids = query_passage_words[0]
    texts, length = ids.shape
    tokens = texts * length
    features, vocab = vocabulary_vectors.shape
    blocks = vocab // IDS_PER_BLOCK
    group_rows = 8 * pl.cdiv(vocab // IDS_PER_GROUP + 1, 8)
    per_shard, negatives = difficult_distractors.shape
    part_width = layer_weight_matrix.shape[1]
    width = part_width // shards
    params = pltpu.CompilerParams(vmem_limit_bytes=VMEM_BYTES)
    modest = pltpu.CompilerParams(vmem_limit_bytes=VMEM_BYTES // 4)
    other_core = [(d, d ^ 1) for d in range(shards)]
    other_y = [(d, d ^ 2) for d in range(shards)]

    def columns(i, j):
        start = split_quarter(i, j) * width
        return lax.dynamic_slice(layer_weight_matrix, (0, start), (features, width))

    def project(base, span):
        stripes = pl.cdiv(span, STRIPE)
        extra_rows = (stripes + 1 + shards) * ROWS
        turned, member = pl.pallas_call(
            functools.partial(gather_kernel, base=base),
            out_shape=[
                jax.ShapeDtypeStruct((features, span), jnp.bfloat16),
                jax.ShapeDtypeStruct((span, LANES), jnp.bfloat16),
            ],
            in_specs=[vmem_spec(), any_spec()],
            out_specs=[vmem_spec()] * 2,
            scratch_shapes=[
                pltpu.VMEM((blocks, features, IDS_PER_BLOCK), jnp.bfloat16),
                pltpu.VMEM((8 * pl.cdiv(span // LANES, 8), LANES), jnp.int32),
                pltpu.VMEM((texts, length), jnp.float32),
                pltpu.VMEM((group_rows, length), jnp.int32),
                pltpu.SMEM((group_rows, length), jnp.int32),
                pltpu.SemaphoreType.DMA((blocks,)),
                pltpu.SemaphoreType.DMA,
            ],
            compiler_params=params,
            name="gather",
        )(ids, vocabulary_vectors)

        def product(turned, i, j):
            return mm(turned, columns(i, j), (((0,), (0,)), ((), ())))

        def narrow(x):
            return x.astype(jnp.bfloat16)

        core1 = lax.ppermute(narrow(product(turned, 1, 1)), "dp", other_core)
        chip1 = narrow(product(turned, 0, 1) + core1.astype(jnp.float32))
        far = lax.ppermute(chip1, "dp", other_y)
        turned, _ = lax.optimization_barrier((turned, chip1))
        extra = pl.pallas_call(
            statistics_kernel,
            out_shape=jax.ShapeDtypeStruct((extra_rows, STRIPE), jnp.bfloat16),
            in_specs=[vmem_spec()] * 4,
            out_specs=vmem_spec(),
            scratch_shapes=[pltpu.VMEM((LANES, LANES), jnp.float32)],
            compiler_params=params,
            cost_estimate=pl.CostEstimate(
                flops=2 * features * span * (ROWS + LANES),
                bytes_accessed=2 * features * span,
                transcendentals=0,
            ),
            name="statistics",
        )(turned, member, difficult_distractors, lowering_factor_matrix)
        chip = extra.astype(jnp.float32)
        chip += lax.ppermute(extra, "dp", other_core).astype(jnp.float32)
        extra = chip + lax.ppermute(narrow(chip), "dp", other_y).astype(jnp.float32)
        core0 = lax.ppermute(narrow(product(turned, 1, 0)), "dp", other_core)
        own0 = narrow(product(turned, 0, 0))
        return own0, core0, far, extra, member

    first = project(0, FIRST)
    many = jnp.sum((ids != 0).astype(jnp.int32)) > FIRST
    left = tokens - FIRST
    shapes = jax.eval_shape(lambda: project(FIRST, left))
    rest = lax.cond(
        many,
        lambda: project(FIRST, left),
        lambda: tuple(jnp.zeros(x.shape, x.dtype) for x in shapes),
    )
    sent, misc = pl.pallas_call(
        functools.partial(pool_kernel, model_width=float(features * shards)),
        out_shape=[
            jax.ShapeDtypeStruct(((texts + 1) * ROWS, width), jnp.bfloat16),
            jax.ShapeDtypeStruct((ROWS, width), jnp.float32),
        ],
        in_specs=[vmem_spec()] * 2 + [any_spec()] * 2 + [vmem_spec()] * 8,
        out_specs=[vmem_spec()] * 2,
        scratch_shapes=[
            pltpu.VMEM((LANES, width), jnp.bfloat16),
            pltpu.VMEM((ROWS, width), jnp.float32),
            pltpu.VMEM((texts * ROWS, width), jnp.float32),
            pltpu.VMEM((FIRST, width), jnp.bfloat16),
            pltpu.VMEM((FIRST, width), jnp.bfloat16),
            pltpu.SemaphoreType.DMA((2,)),
        ],
        compiler_params=modest,
        name="pool",
    )(ids, *first, *rest, raising_factor_matrix)
    far_side = lax.ppermute(sent, "group", [(0, 1), (1, 0)])
    rows = 2 * ROWS
    packed, slopes = pl.pallas_call(
        dots_kernel,
        out_shape=[
            jax.ShapeDtypeStruct((rows + width // LANES * rows, LANES), jnp.float32),
            jax.ShapeDtypeStruct((2 * texts * ROWS, width), jnp.bfloat16),
        ],
        in_specs=[vmem_spec(), any_spec()],
        out_specs=[vmem_spec()] * 2,
        scratch_shapes=[
            pltpu.VMEM(sent.shape, sent.dtype),
            pltpu.SemaphoreType.DMA((1,)),
        ],
        compiler_params=modest,
        name="dots",
    )(sent, far_side)
    packed = exchange(packed, "dp", shards)
    dots = [x[0:rows] for x in packed]
    dots = (dots[0] + dots[1]) + (dots[2] + dots[3])
    slopes, dots = lax.optimization_barrier((slopes, dots))
    dots = exchange(dots, "mp", parts)
    slopes = exchange(slopes, "dp", shards)
    embeddings, losses, update = pl.pallas_call(
        functools.partial(
            score_kernel, texts=texts, stripes=pl.cdiv(FIRST, STRIPE), negatives=negatives
        ),
        out_shape=[
            jax.ShapeDtypeStruct((1, per_shard, part_width), jnp.bfloat16),
            jax.ShapeDtypeStruct((1, per_shard), jnp.float32),
            jax.ShapeDtypeStruct((ROWS, part_width), jnp.float32),
        ],
        in_specs=[any_spec()] * 12 + [vmem_spec(), smem_spec()],
        out_specs=[vmem_spec()] * 3,
        scratch_shapes=[pltpu.VMEM(x.shape, x.dtype) for x in (*packed, *slopes, *dots)]
        + [pltpu.SemaphoreType.DMA((12,))],
        compiler_params=modest,
        name="score",
    )(*packed, *slopes, *dots, misc, logit_sharpness)
    return (embeddings, losses, update)


def body(words, hard, vocabulary, weight, lowering, raising, sharpness):
    shards, parts = lax.axis_size("dp"), lax.axis_size("mp")
    texts, length = words.shape[1:]
    features, vocab = vocabulary.shape
    negatives = hard.shape[1]
    square = shards == 4 and features == weight.shape[1] == 4 * STRIPE and parts == shards
    small = texts <= ROWS - 2 and length == LANES and FIRST < texts * length <= 2048
    even = (texts * length - FIRST) % CHUNK == 0 and vocab % IDS_PER_BLOCK == 0
    fits = features * vocab <= 2**24 and features % (4 * LANES) == 0
    spare = pl.cdiv(FIRST, STRIPE) + negatives <= ROWS and lowering.shape[0] == ROWS
    fast = square and small and even and fits and spare and lax.axis_size("group") == 2
    chosen = split_body if fast else general_body
    return chosen(words, hard, vocabulary, weight, lowering, raising, sharpness)


def solution(mesh):
    in_specs = (
        P("group", None, None),
        P("dp", None),
        P("dp", None),
        P("dp", "mp"),
        P(),
        P(None, "mp"),
        P(),
    )
    out_specs = (P("group", "dp", "mp"), P("group", "dp"), P(None, "mp"))
    return jax.shard_map(body, mesh=mesh, in_specs=in_specs, out_specs=out_specs, check_vma=False)
```

```python
import functools

import jax
import jax.numpy as jnp
from jax import lax
from jax.experimental import pallas as pl
from jax.experimental.pallas import tpu as pltpu
from jax.sharding import PartitionSpec as P


def general_body(
    query_passage_words,
    difficult_distractors,
    vocabulary_vectors,
    layer_weight_matrix,
    lowering_factor_matrix,
    raising_factor_matrix,
    logit_sharpness,
):
    group_index = lax.axis_index("group")
    shard_index = lax.axis_index("dp")
    part_index = lax.axis_index("mp")
    shard_count = lax.axis_size("dp")
    side_ids = query_passage_words[0]
    text_count = side_ids.shape[0]
    length = side_ids.shape[1]
    per_shard = text_count // shard_count
    own_ids = lax.dynamic_slice_in_dim(side_ids, shard_index * per_shard, per_shard, 0)
    columns = jnp.take(vocabulary_vectors, side_ids.reshape(-1), axis=1)
    inputs = lax.all_to_all(columns, "dp", split_axis=1, concat_axis=0, tiled=True)
    tokens = inputs.shape[1]
    feature_width = raising_factor_matrix.shape[1]
    wide_inputs = inputs.astype(jnp.float32)
    inverse = lax.rsqrt(jnp.mean(wide_inputs * wide_inputs, axis=0) + 1e-05)
    normed_state = (wide_inputs * inverse[None, :]).astype(jnp.bfloat16)
    linear_map = lax.dot_general(
        lax.all_gather(layer_weight_matrix, "dp", axis=0, tiled=True),
        normed_state,
        (((0,), (0,)), ((), ())),
        preferred_element_type=jnp.float32,
    )
    reduced_sum = jnp.dot(
        lowering_factor_matrix, normed_state, preferred_element_type=jnp.float32
    ).astype(jnp.bfloat16)
    linear_map = linear_map + lax.dot_general(
        raising_factor_matrix,
        reduced_sum,
        (((0,), (0,)), ((), ())),
        preferred_element_type=jnp.float32,
    )
    own_inputs = lax.dynamic_slice_in_dim(
        inputs, part_index * feature_width, feature_width, 0
    ).astype(jnp.float32)
    hidden_state = own_inputs + jax.nn.silu(linear_map)
    mask = (own_ids != 0).astype(jnp.float32)
    counts = jnp.sum(mask, axis=1)
    summed = jnp.einsum("dnl,nl->nd", hidden_state.reshape(feature_width, per_shard, length), mask)
    pooled = (summed / counts[:, None]).astype(jnp.bfloat16)
    gathered = lax.all_gather(pooled, ("group", "dp"), axis=0, tiled=True)
    part_scores = lax.dot_general(
        pooled, gathered, (((1,), (1,)), ((), ())), preferred_element_type=jnp.float32
    )
    gathered_wide = gathered.astype(jnp.float32)
    part_norms = jnp.sum(gathered_wide * gathered_wide, axis=1)
    dots, norms = lax.psum((part_scores, part_norms), "mp")
    rnorm_all = lax.rsqrt(norms + 1e-06)
    all_count = gathered.shape[0]
    half_count = all_count // 2
    own_rows = (
        group_index * half_count + shard_index * per_shard + jnp.arange(per_shard, dtype=jnp.int32)
    )
    rnorm_own = jnp.take(rnorm_all, own_rows)
    cosine = dots * rnorm_own[:, None] * rnorm_all[None, :]
    multiplier_factor = logit_sharpness[0]
    scores = multiplier_factor * cosine
    column_ids = jnp.arange(all_count, dtype=jnp.int32)
    keep = column_ids[None, :] != own_rows[:, None]
    pair = (own_rows + half_count) % all_count
    weight = (group_index == 0).astype(jnp.float32)
    neg_cols = half_count + difficult_distractors
    top = jnp.max(jnp.where(keep, scores, -jnp.inf), axis=1)
    safe_scores = jnp.where(keep, scores, top[:, None])
    expd = jnp.where(keep, jnp.exp(safe_scores - top[:, None]), 0.0)
    neg_exp = (
        jnp.exp(jnp.minimum(jnp.take_along_axis(scores, neg_cols, axis=1) - top[:, None], 0.0))
        * weight
    )
    total = jnp.sum(expd, axis=1) + jnp.sum(neg_exp, axis=1)
    pair_score = jnp.take_along_axis(scores, pair[:, None], axis=1)[:, 0]
    losses = top + jnp.log(total) - pair_score
    onehot = (column_ids[None, None, :] == neg_cols[:, :, None]).astype(jnp.float32)
    probs = (expd + jnp.einsum("rk,rkc->rc", neg_exp, onehot)) / total[:, None]
    target = (column_ids[None, :] == pair[:, None]).astype(jnp.float32)
    grad_scores = (probs - target) / all_count
    coeff = (grad_scores * rnorm_own[:, None] * rnorm_all[None, :]).astype(jnp.bfloat16)
    along = jnp.dot(coeff, gathered, preferred_element_type=jnp.float32)
    pooled_wide = pooled.astype(jnp.float32)
    radial = jnp.sum(grad_scores * cosine, axis=1) * rnorm_own * rnorm_own
    embedding_gradient = multiplier_factor * (along - radial[:, None] * pooled_wide)
    token_grad = jnp.einsum("nd,nl->dnl", embedding_gradient / counts[:, None], mask).reshape(
        feature_width, tokens
    )
    sigma = jax.nn.sigmoid(linear_map)
    local = (token_grad * sigma * (1.0 + linear_map * (1.0 - sigma))).astype(jnp.bfloat16)
    up_portion = lax.dot_general(
        reduced_sum, local, (((1,), (1,)), ((), ())), preferred_element_type=jnp.float32
    )
    adapter_up_gradient = lax.psum(up_portion, ("group", "dp"))
    embeddings = (pooled_wide * rnorm_own[:, None]).astype(jnp.bfloat16)[None]
    return (embeddings, losses[None], adapter_up_gradient)


BLOCK_BITS, GROUP_BITS, LANE_BITS, ROW_BITS = 10, 9, 7, 4
IDS_PER_BLOCK = 1 << BLOCK_BITS
IDS_PER_GROUP = 1 << GROUP_BITS
CHUNK = 384
STRIPE = 256
ROWS = 1 << ROW_BITS
LANES = 1 << LANE_BITS
FEATURE_ROWS = 128
FIRST = 1152
TAKEN = 768
NT = (((1,), (1,)), ((), ()))
LARGE_VMEM, MODEST_VMEM = 44 * 1024 * 1024, 15 * 1024 * 1024


def mm(a, b, dims=(((1,), (0,)), ((), ()))):
    return lax.dot_general(a, b, dims, preferred_element_type=jnp.float32)


def split(x):
    high = x.astype(jnp.bfloat16)
    return high, (x - high.astype(jnp.float32)).astype(jnp.bfloat16)


def iota(shape, dim):
    return lax.broadcasted_iota(jnp.int32, shape, dim)


def quarter_of(dp_index, cores=2):
    return (dp_index % cores) * 2 + dp_index // cores


def split_quarter(i, j, cores=2):
    shard = lax.axis_index("dp")
    core, side_y = lax.rem(shard, cores), lax.div(shard, cores)
    return (core ^ i) * 2 + (side_y ^ j)


def take_lanes(x, lanes):
    numbers = lax.GatherDimensionNumbers(
        offset_dims=(),
        collapsed_slice_dims=(1,),
        start_index_map=(1,),
        operand_batching_dims=(0,),
        start_indices_batching_dims=(0,),
    )
    mode = lax.GatherScatterMode.PROMISE_IN_BOUNDS
    return lax.gather(x, lanes[..., None], numbers, slice_sizes=(1, 1), mode=mode)


def fetch(pairs, sems):
    copies = [pltpu.make_async_copy(a, b, sems.at[n]) for n, (a, b) in enumerate(pairs)]
    for copy in copies:
        copy.start()
    for copy in copies:
        copy.wait()


def gather_kernel(
    ids_ref,
    vocab_ref,
    turned_any,
    member_any,
    turned,
    member_ref,
    held,
    token_ref,
    ranks,
    counted,
    bounds,
    held_sems,
    bounds_sem,
    out_sems,
    base,
):
    texts, length = ids_ref.shape
    features, vocab = vocab_ref.shape
    blocks = vocab // IDS_PER_BLOCK
    groups = vocab // IDS_PER_GROUP
    span = member_ref.shape[0]

    def vocab_copy(b):
        columns = pl.ds(pl.multiple_of(b * IDS_PER_BLOCK, LANES), IDS_PER_BLOCK)
        return pltpu.make_async_copy(vocab_ref.at[:, columns], held.at[b], held_sems.at[b])

    vocab_copy(0).start()
    for b in range(1, blocks):
        vocab_copy(b).start()

    ids = ids_ref[...]
    valid = ids != 0
    group_of = jnp.where(valid, lax.shift_right_logical(ids, GROUP_BITS), groups)
    group_rows = counted.shape[0]
    group_id = iota((group_rows, length), 0)
    below = jnp.zeros((group_rows, length), jnp.float32)
    for text in range(texts):
        below += jnp.where(group_of[text : text + 1] < group_id, 1.0, 0.0)
    before = jnp.broadcast_to(jnp.sum(below, axis=1, keepdims=True), (group_rows, length))
    counted[...] = before.astype(jnp.int32)
    bounds_copy = pltpu.make_async_copy(counted, bounds, bounds_sem)
    bounds_copy.start()
    earlier = jnp.where(iota((length, length), 0) < iota((length, length), 1), 1.0, 0.0).astype(
        jnp.bfloat16
    )
    for text in range(texts):
        here = jnp.where(group_of[text : text + 1] == group_id, 1.0, 0.0)
        inside = mm(here.astype(jnp.bfloat16), earlier)
        ranks[pl.ds(text, 1), :] = jnp.sum(here * (inside + before), axis=0, keepdims=True)
        before += jnp.broadcast_to(jnp.sum(here, axis=1, keepdims=True), (group_rows, length))
    text_of = iota((texts, length), 0)
    carried = jnp.where(valid, lax.shift_left(ids, ROW_BITS) + text_of, 0).astype(jnp.float32)
    rank = ranks[...]

    def place(p, carry):
        position = (iota((LANES, length), 0) + (p * LANES + base)).astype(jnp.float32)
        total = jnp.zeros((LANES, length), jnp.float32)
        for text in range(texts):
            total += jnp.where(rank[text : text + 1] == position, carried[text : text + 1], 0.0)
        found = jnp.broadcast_to(jnp.sum(total, axis=1, keepdims=True), (LANES, LANES))
        start = pl.multiple_of(p * LANES, LANES)
        row = found.T[0:1].astype(jnp.int32)
        token = lax.shift_right_logical(row, ROW_BITS)
        token_ref[pl.ds(p, 1), :] = jnp.where(token == 0, -vocab, token)
        found = found.astype(jnp.int32)
        real = (found >= ROWS) & ((found & (ROWS - 1)) == iota((LANES, LANES), 1))
        member_ref[pl.ds(start, LANES), :] = jnp.where(real, 1.0, 0.0).astype(jnp.bfloat16)
        turned[:, pl.ds(start, LANES)] = jnp.zeros((features, LANES), jnp.bfloat16)
        return carry

    lax.fori_loop(0, span // LANES, place, 0)
    bounds_copy.wait()

    def within(place):
        return jnp.clip(place - base, 0, span)

    def take(b, carry):
        vocab_copy(b).wait()
        for part in range(IDS_PER_BLOCK // IDS_PER_GROUP):
            group = b * (IDS_PER_BLOCK // IDS_PER_GROUP) + part
            first, last = within(bounds[group, 0]), within(bounds[group + 1, 0])
            begin = lax.shift_right_logical(first, LANE_BITS)
            end = lax.shift_right_logical(last + LANES - 1, LANE_BITS)

            def window(p, carry):
                at = pl.ds(pl.multiple_of(p * LANES, LANES), LANES)
                token = token_ref[pl.ds(p, 1), :] - group * IDS_PER_GROUP
                token = jnp.broadcast_to(token, (FEATURE_ROWS, LANES))
                lane = (token & (LANES - 1)).astype(jnp.int16)
                tile = lax.shift_right_arithmetic(token, LANE_BITS).astype(jnp.int16)
                pieces = [pl.ds(f, FEATURE_ROWS) for f in range(0, TAKEN, FEATURE_ROWS)]
                short = jnp.broadcast_to(token[0:1], (IDS_PER_GROUP, LANES)).astype(jnp.int16)
                picked = jnp.where(
                    short == iota((IDS_PER_GROUP, LANES), 0).astype(jnp.int16), 1.0, 0.0
                ).astype(jnp.bfloat16)
                columns = pl.ds(part * IDS_PER_GROUP, IDS_PER_GROUP)
                rest = pl.ds(TAKEN, features - TAKEN)
                product = mm(held[b, rest, columns], picked).astype(jnp.bfloat16)
                fresh = []
                for rows in pieces:
                    total = jnp.zeros((FEATURE_ROWS, LANES), jnp.bfloat16)
                    for j in range(IDS_PER_GROUP // LANES):
                        columns = pl.ds(part * IDS_PER_GROUP + j * LANES, LANES)
                        total = jnp.where(tile == j, take_lanes(held[b, rows, columns], lane), total)
                    fresh.append(total)
                pieces.append(rest)
                fresh.append(product)
                fresh = [turned[rows, at] + total for rows, total in zip(pieces, fresh)]
                for rows, total in zip(pieces, fresh):
                    turned[rows, at] = total
                return carry

            lax.fori_loop(begin, jnp.where(last > first, end, begin), window, 0)
        return carry

    lax.fori_loop(0, blocks, take, 0)
    fetch([(turned, turned_any), (member_ref, member_any)], out_sems)


def statistics_kernel(
    turned_any, member_any, hard_ref, lower_ref, extra_ref, small, turned, member_ref, spread, sems
):
    fetch([(turned_any, turned), (member_any, member_ref)], sems)
    features, span = turned.shape
    stripes = pl.cdiv(span, STRIPE)
    per_shard, negatives = hard_ref.shape
    shard = lax.axis_index("dp")
    small[...] = jnp.zeros_like(small)
    small[0:per_shard, stripes : stripes + negatives] = hard_ref[...].astype(jnp.float32)
    lower = lower_ref[:, pl.ds(pl.multiple_of(shard * features, LANES), features)]

    misc = jnp.zeros((ROWS, STRIPE), jnp.float32)
    residual = jnp.zeros((features, LANES), jnp.float32)
    for stripe in range(stripes):
        size = min(STRIPE, span - stripe * STRIPE)
        across = pl.ds(stripe * STRIPE, size)
        upright = turned[:, across]
        wide = upright.astype(jnp.float32)
        square = jnp.sum(wide * wide, axis=0, keepdims=True)
        reduced = mm(lower, upright)
        if size < STRIPE:
            none = jnp.zeros((ROWS, STRIPE - size), jnp.float32)
            reduced = jnp.concatenate([reduced, none], axis=1)
            square = jnp.concatenate([square, none[0:1]], axis=1)
        extra_ref[stripe * ROWS : (stripe + 1) * ROWS, :] = reduced.astype(jnp.bfloat16)
        misc = jnp.where(iota((ROWS, STRIPE), 0) == stripe, square, misc)
        residual += mm(upright, member_ref[across, :])
    hard = small[...].T[0:ROWS]
    for i in range(per_shard):
        misc += jnp.where(iota((ROWS, STRIPE), 1) == shard * per_shard + i, hard[:, i : i + 1], 0.0)
    extra_ref[stripes * ROWS : (stripes + 1) * ROWS, :] = misc.astype(jnp.bfloat16)
    residual = jnp.where(lax.axis_index("mp") == shard, residual.T[0:ROWS], 0.0)
    spread[...] = residual
    for q in range(4):
        start = (stripes + 1 + q) * ROWS
        quarter = pl.multiple_of(split_quarter(q // 2, q % 2) * STRIPE, LANES)
        extra_ref[start : start + ROWS, :] = spread[:, pl.ds(quarter, STRIPE)].astype(jnp.bfloat16)


def pool_kernel(
    ids_ref,
    own_ref,
    core_any,
    far_any,
    extra_ref,
    member_ref,
    own_rest,
    core_rest,
    far_rest,
    extra_rest,
    member_rest,
    raise_ref,
    sent_ref,
    misc_ref,
    raised,
    total,
    slopes,
    core_ref,
    far_ref,
    sems,
    model_width,
):
    texts, length = ids_ref.shape
    width = own_ref.shape[1]
    quarter = quarter_of(lax.axis_index("dp"))
    fetch([(core_any, core_ref), (far_any, far_ref)], sems)
    raised[...] = jnp.zeros_like(raised)
    raised[0:ROWS, :] = raise_ref[:, pl.ds(pl.multiple_of(quarter * width, LANES), width)]
    total[...] = jnp.zeros_like(total)
    slopes[...] = jnp.zeros_like(slopes)

    def add(refs, extra_ref, member_ref, base):
        span = member_ref.shape[0]
        stripes = pl.cdiv(span, STRIPE)

        def summed(start, size):
            return sum(ref[pl.ds(start, size), :].astype(jnp.float32) for ref in refs)

        misc = extra_ref[stripes * ROWS : (stripes + 1) * ROWS, :]
        if base == 0:
            misc_ref[...] = misc
        inverse = lax.rsqrt(misc / model_width + 1e-05)
        for k in range(stripes):
            size = min(STRIPE, span - k * STRIPE)
            scale = inverse[k : k + 1]
            reduced = (extra_ref[k * ROWS : (k + 1) * ROWS, :] * scale).astype(jnp.bfloat16)
            reduced = reduced.astype(jnp.float32)
            stacked = jnp.concatenate([reduced, jnp.broadcast_to(scale, (LANES - ROWS, STRIPE))])
            turned = stacked[:, 0:size].T
            low = turned.astype(jnp.bfloat16)
            linear = summed(k * STRIPE, size)
            linear = linear * turned[:, ROWS : ROWS + 1] + mm(low, raised[...])
            sigma = 1.0 / (1.0 + jnp.exp(-linear))
            slope = (sigma * (1.0 + linear * (1.0 - sigma))).astype(jnp.bfloat16)
            member = member_ref[pl.ds(k * STRIPE, size), :].astype(jnp.float32).T
            high, rest = split(linear * sigma)
            chosen = member[0:ROWS].astype(jnp.bfloat16)
            total[...] += mm(chosen, high) + mm(chosen, rest)
            spread = [reduced[:, 0:size] * member[text : text + 1] for text in range(texts)]
            slopes[...] += mm(jnp.concatenate(spread).astype(jnp.bfloat16), slope)
        total[...] += extra_ref[(stripes + 1) * ROWS : (stripes + 2) * ROWS, :]

    add((own_ref, core_ref, far_ref), extra_ref, member_ref, 0)
    real = (ids_ref[...] != 0).astype(jnp.float32)

    @pl.when(jnp.sum(real) > member_ref.shape[0])
    def _():
        add((own_rest, core_rest, far_rest), extra_rest, member_rest, member_ref.shape[0])

    counts = jnp.sum(real, axis=1, keepdims=True)
    pooled = total[0:texts] / counts
    pooled = jnp.concatenate([pooled, jnp.zeros((ROWS - texts, width), jnp.float32)])
    sent_ref[0:ROWS, :] = pooled.astype(jnp.bfloat16)
    for text in range(texts):
        part = slopes[text * ROWS : (text + 1) * ROWS, :] / counts[text : text + 1]
        sent_ref[(text + 1) * ROWS : (text + 2) * ROWS, :] = part.astype(jnp.bfloat16)


def both_sides(near, far):
    queries = lax.axis_index("group") == 0
    return jnp.concatenate([jnp.where(queries, near, far), jnp.where(queries, far, near)], axis=0)


def dots_kernel(near_ref, far_any, packed_ref, slopes_ref, far_ref, sems):
    fetch([(far_any, far_ref)], sems)
    block = both_sides(near_ref[0:ROWS], far_ref[0:ROWS])
    rows = 2 * ROWS
    packed_ref[...] = jnp.zeros_like(packed_ref)
    packed_ref[0:rows, 0:rows] = mm(block, block, NT)
    for part in range(block.shape[1] // LANES):
        piece = block[:, part * LANES : (part + 1) * LANES]
        packed_ref[rows + part * rows : rows + (part + 1) * rows, :] = piece.astype(jnp.float32)
    size = near_ref.shape[0] - ROWS
    slopes_ref[0:size] = near_ref[ROWS:]
    slopes_ref[size:] = far_ref[ROWS:]


def score_kernel(*refs, texts, stripes, negatives):
    there, (misc_ref, sharp_ref, embed_ref, loss_ref, up_ref), (*here, sems) = (
        refs[0:10],
        refs[10:15],
        refs[15:],
    )
    fetch(list(zip(there, here)), sems)
    packed0, packed1, packed2, packed3, slopes0, slopes2 = here[0:6]
    dots0, dots1, dots2, dots3 = here[6:10]
    rows = 2 * ROWS
    per_shard = loss_ref.shape[1]
    group, shard = lax.axis_index("group"), lax.axis_index("dp")
    dots = ((dots0[...] + dots1[...]) + (dots2[...] + dots3[...]))[:, 0:rows]
    down, across = iota((rows, rows), 0), iota((rows, rows), 1)
    same = down == across
    real = (lax.rem(down, ROWS) < texts) & (lax.rem(across, ROWS) < texts)
    diagonal = jnp.where(same, dots, 0.0)
    rnorm_row = lax.rsqrt(jnp.sum(diagonal, axis=0, keepdims=True) + 1e-06)
    rnorm_col = lax.rsqrt(jnp.sum(diagonal, axis=1, keepdims=True) + 1e-06)
    sharpness = sharp_ref[0]
    cosine = dots * rnorm_col * rnorm_row
    scores = sharpness * cosine
    keep = real & ~same
    top = jnp.max(jnp.where(keep, scores, -jnp.inf), axis=0, keepdims=True)
    top = jnp.where(lax.rem(across[0:1], ROWS) < texts, top, 0.0)
    powers = jnp.exp(jnp.where(real, jnp.minimum(scores - top, 0.0), 0.0))
    hard = misc_ref[stripes : stripes + negatives, 0:rows].astype(jnp.int32) + ROWS
    times = jnp.zeros((rows, rows), jnp.float32)
    for k in range(negatives):
        times += jnp.where(hard[k : k + 1] == down, 1.0, 0.0)
    times = jnp.where(across < texts, times, 0.0)
    weights = (jnp.where(keep, 1.0, 0.0) + jnp.where(real, times, 0.0)) * powers
    total = jnp.sum(weights, axis=0, keepdims=True)
    total = jnp.where(lax.rem(across[0:1], ROWS) < texts, total, 1.0)
    pair = (down == lax.rem(across + ROWS, rows)) & real
    pair_score = jnp.sum(jnp.where(pair, scores, 0.0), axis=0, keepdims=True)
    losses = top + jnp.log(total) - pair_score
    grad_scores = (weights / total - jnp.where(pair, 1.0, 0.0)) / (2 * texts)
    coeff = (grad_scores * rnorm_col * rnorm_row).astype(jnp.bfloat16)
    radial = jnp.sum(grad_scores * cosine, axis=0, keepdims=True) * rnorm_row * rnorm_row

    first = shard * per_shard
    loss_col = jnp.sum(jnp.where(same, losses, 0.0), axis=1, keepdims=True)
    at = (iota((rows, LANES), 0) == group * ROWS + first + iota((rows, LANES), 1)) & (
        iota((rows, LANES), 1) < per_shard
    )
    loss_ref[...] = jnp.sum(jnp.where(at, loss_col, 0.0), axis=0, keepdims=True)[:, 0:per_shard]

    along_rows = coeff.astype(jnp.float32).T.astype(jnp.bfloat16)
    radial_col = jnp.sum(jnp.where(same, radial, 0.0), axis=1, keepdims=True)
    rnorm_own = jnp.where(group == 0, rnorm_col[0:ROWS], rnorm_col[ROWS:rows])
    chosen = iota((ROWS, ROWS), 1) == iota((ROWS, ROWS), 0) + first
    chosen = jnp.where(chosen & (iota((ROWS, ROWS), 0) < per_shard), 1.0, 0.0).astype(jnp.bfloat16)
    blocks = ((packed0, slopes0), (packed1, None), (packed2, slopes2), (packed3, None))
    for o, (packed, slopes) in enumerate(blocks):
        parts = packed.shape[0] // rows - 1
        width = parts * LANES
        halves = [packed[rows * (part + 1) : rows * (part + 2), :] for part in range(parts)]
        block = jnp.concatenate(halves, axis=1)
        queries = group == 0
        at = pl.multiple_of(quarter_of(shard ^ o) * width, LANES)
        own = jnp.where(queries, block[0:ROWS], block[ROWS:rows]) * rnorm_own
        picked = mm(chosen, own.astype(jnp.bfloat16)).astype(jnp.bfloat16)
        embed_ref[0, :, pl.ds(at, width)] = picked[0:per_shard]
        if slopes is None:
            continue
        along = mm(along_rows, block.astype(jnp.bfloat16))
        grad = sharpness * (along - radial_col * block)
        near, far = slopes[0 : slopes.shape[0] // 2], slopes[slopes.shape[0] // 2 :]
        grad_near = jnp.where(queries, grad[0:ROWS], grad[ROWS:rows])
        grad_far = jnp.where(queries, grad[ROWS:rows], grad[0:ROWS])
        update = []
        for side, side_grad in ((near, grad_near), (far, grad_far)):
            total = jnp.zeros((ROWS, width), jnp.float32)
            for text in range(texts):
                slope = side[text * ROWS : (text + 1) * ROWS].astype(jnp.float32)
                total += side_grad[text : text + 1] * slope
            update.append(total)
        at = pl.multiple_of((lax.div(shard, 2) ^ (o // 2)) * width, LANES)
        up_ref[:, pl.ds(at, width)] = update[0] + update[1]


def any_spec():
    return pl.BlockSpec(memory_space=pl.ANY)


def vmem_spec():
    return pl.BlockSpec(memory_space=pltpu.VMEM)


def smem_spec():
    return pl.BlockSpec(memory_space=pltpu.SMEM)


def exchange(x, axis, size):
    steps = [[(i, i ^ o) for i in range(size)] for o in range(1, size)]
    return [x] + [lax.ppermute(x, axis, step) for step in steps]


def split_body(
    query_passage_words,
    difficult_distractors,
    vocabulary_vectors,
    layer_weight_matrix,
    lowering_factor_matrix,
    raising_factor_matrix,
    logit_sharpness,
):
    shards, parts = lax.axis_size("dp"), lax.axis_size("mp")
    ids = query_passage_words[0]
    texts, length = ids.shape
    tokens = texts * length
    features, vocab = vocabulary_vectors.shape
    blocks = vocab // IDS_PER_BLOCK
    group_rows = 8 * pl.cdiv(vocab // IDS_PER_GROUP + 1, 8)
    per_shard, negatives = difficult_distractors.shape
    part_width = layer_weight_matrix.shape[1]
    width = part_width // shards
    params = pltpu.CompilerParams(vmem_limit_bytes=LARGE_VMEM)
    modest = pltpu.CompilerParams(vmem_limit_bytes=MODEST_VMEM)
    other_core = [(d, d ^ 1) for d in range(shards)]
    other_y = [(d, d ^ 2) for d in range(shards)]

    def columns(i, j):
        start = split_quarter(i, j) * width
        return lax.dynamic_slice(layer_weight_matrix, (0, start), (features, width))

    def project(base, span):
        stripes = pl.cdiv(span, STRIPE)
        extra_rows = (stripes + 1 + shards) * ROWS
        turned, member = pl.pallas_call(
            functools.partial(gather_kernel, base=base),
            out_shape=[
                jax.ShapeDtypeStruct((features, span), jnp.bfloat16),
                jax.ShapeDtypeStruct((span, LANES), jnp.bfloat16),
            ],
            in_specs=[vmem_spec(), any_spec()],
            out_specs=[any_spec()] * 2,
            scratch_shapes=[
                pltpu.VMEM((features, span), jnp.bfloat16),
                pltpu.VMEM((span, LANES), jnp.bfloat16),
                pltpu.VMEM((blocks, features, IDS_PER_BLOCK), jnp.bfloat16),
                pltpu.VMEM((8 * pl.cdiv(span // LANES, 8), LANES), jnp.int32),
                pltpu.VMEM((texts, length), jnp.float32),
                pltpu.VMEM((group_rows, length), jnp.int32),
                pltpu.SMEM((group_rows, length), jnp.int32),
                pltpu.SemaphoreType.DMA((blocks,)),
                pltpu.SemaphoreType.DMA,
                pltpu.SemaphoreType.DMA((2,)),
            ],
            compiler_params=params,
            name="gather",
        )(ids, vocabulary_vectors)

        def product(turned, i, j):
            return mm(turned, columns(i, j), (((0,), (0,)), ((), ())))

        def narrow(x):
            return x.astype(jnp.bfloat16)

        core1 = lax.ppermute(narrow(product(turned, 1, 1)), "dp", other_core)
        chip1 = narrow(product(turned, 0, 1) + core1.astype(jnp.float32))
        far = lax.ppermute(chip1, "dp", other_y)
        turned, _ = lax.optimization_barrier((turned, chip1))
        extra = pl.pallas_call(
            statistics_kernel,
            out_shape=jax.ShapeDtypeStruct((extra_rows, STRIPE), jnp.bfloat16),
            in_specs=[any_spec()] * 2 + [vmem_spec()] * 2,
            out_specs=vmem_spec(),
            scratch_shapes=[
                pltpu.VMEM((LANES, LANES), jnp.float32),
                pltpu.VMEM(turned.shape, turned.dtype),
                pltpu.VMEM(member.shape, member.dtype),
                pltpu.VMEM((ROWS, features), jnp.float32),
                pltpu.SemaphoreType.DMA((2,)),
            ],
            compiler_params=modest,
            cost_estimate=pl.CostEstimate(
                flops=2 * features * span * (ROWS + LANES),
                bytes_accessed=2 * features * span,
                transcendentals=0,
            ),
            name="statistics",
        )(turned, member, difficult_distractors, lowering_factor_matrix)
        common = (stripes + 1) * ROWS
        near = extra.astype(jnp.float32)
        across = lax.ppermute(extra, "dp", other_core).astype(jnp.float32)
        chip = near[0:common] + across[0:common]
        inputs = near[common : common + 2 * ROWS] + across[common + 2 * ROWS :]
        sent = narrow(jnp.concatenate([chip, inputs[ROWS:]]))
        sent = lax.ppermute(sent, "dp", other_y).astype(jnp.float32)
        extra = jnp.concatenate([chip, inputs[0:ROWS]]) + sent
        core0 = lax.ppermute(narrow(product(turned, 1, 0)), "dp", other_core)
        own0 = narrow(product(turned, 0, 0))
        return own0, core0, far, extra, member

    first = project(0, FIRST)
    later, _ = lax.optimization_barrier((ids, first[0]))
    many = jnp.sum((later != 0).astype(jnp.int32)) > FIRST
    left = tokens - FIRST
    shapes = jax.eval_shape(lambda: project(FIRST, left))
    rest = lax.cond(
        many,
        lambda: project(FIRST, left),
        lambda: tuple(jnp.zeros(x.shape, x.dtype) for x in shapes),
    )
    sent, misc = pl.pallas_call(
        functools.partial(pool_kernel, model_width=float(features * shards)),
        out_shape=[
            jax.ShapeDtypeStruct(((texts + 1) * ROWS, width), jnp.bfloat16),
            jax.ShapeDtypeStruct((ROWS, width), jnp.float32),
        ],
        in_specs=[vmem_spec()] * 2 + [any_spec()] * 2 + [vmem_spec()] * 8,
        out_specs=[vmem_spec()] * 2,
        scratch_shapes=[
            pltpu.VMEM((LANES, width), jnp.bfloat16),
            pltpu.VMEM((ROWS, width), jnp.float32),
            pltpu.VMEM((texts * ROWS, width), jnp.float32),
            pltpu.VMEM((FIRST, width), jnp.bfloat16),
            pltpu.VMEM((FIRST, width), jnp.bfloat16),
            pltpu.SemaphoreType.DMA((2,)),
        ],
        compiler_params=modest,
        name="pool",
    )(ids, *first, *rest, raising_factor_matrix)
    far_side = lax.ppermute(sent, "group", [(0, 1), (1, 0)])
    rows = 2 * ROWS
    packed, slopes = pl.pallas_call(
        dots_kernel,
        out_shape=[
            jax.ShapeDtypeStruct((rows + width // LANES * rows, LANES), jnp.float32),
            jax.ShapeDtypeStruct((2 * texts * ROWS, width), jnp.bfloat16),
        ],
        in_specs=[vmem_spec(), any_spec()],
        out_specs=[vmem_spec()] * 2,
        scratch_shapes=[
            pltpu.VMEM(sent.shape, sent.dtype),
            pltpu.SemaphoreType.DMA((1,)),
        ],
        compiler_params=modest,
        name="dots",
    )(sent, far_side)
    packed = exchange(packed, "dp", shards)
    dots = [x[0:rows] for x in packed]
    dots = (dots[0] + dots[1]) + (dots[2] + dots[3])
    slopes, dots = lax.optimization_barrier((slopes, dots))
    dots = exchange(dots, "mp", parts)
    slopes = [slopes, lax.ppermute(slopes, "dp", other_y)]
    embeddings, losses, update = pl.pallas_call(
        functools.partial(
            score_kernel, texts=texts, stripes=pl.cdiv(FIRST, STRIPE), negatives=negatives
        ),
        out_shape=[
            jax.ShapeDtypeStruct((1, per_shard, part_width), jnp.bfloat16),
            jax.ShapeDtypeStruct((1, per_shard), jnp.float32),
            jax.ShapeDtypeStruct((ROWS, part_width // 2), jnp.float32),
        ],
        in_specs=[any_spec()] * 10 + [vmem_spec(), smem_spec()],
        out_specs=[vmem_spec()] * 3,
        scratch_shapes=[pltpu.VMEM(x.shape, x.dtype) for x in (*packed, *slopes, *dots)]
        + [pltpu.SemaphoreType.DMA((10,))],
        compiler_params=modest,
        name="score",
    )(*packed, *slopes, *dots, misc, logit_sharpness)
    other = lax.ppermute(update, "dp", other_core)
    core = lax.rem(lax.axis_index("dp"), 2)
    halves = [jnp.where(core == 0, update, other), jnp.where(core == 0, other, update)]
    return (embeddings, losses, jnp.concatenate(halves, axis=1))


def body(words, hard, vocabulary, weight, lowering, raising, sharpness):
    shards, parts = lax.axis_size("dp"), lax.axis_size("mp")
    texts, length = words.shape[1:]
    features, vocab = vocabulary.shape
    negatives = hard.shape[1]
    square = shards == 4 and features == weight.shape[1] == 4 * STRIPE and parts == shards
    small = texts <= ROWS - 2 and length == LANES and FIRST < texts * length <= 2048
    even = (texts * length - FIRST) % CHUNK == 0 and vocab % IDS_PER_BLOCK == 0
    fits = features * vocab <= 2**24 and features % (4 * LANES) == 0
    spare = pl.cdiv(FIRST, STRIPE) + negatives <= ROWS and lowering.shape[0] == ROWS
    fast = square and small and even and fits and spare and lax.axis_size("group") == 2
    chosen = split_body if fast else general_body
    return chosen(words, hard, vocabulary, weight, lowering, raising, sharpness)


def solution(mesh):
    in_specs = (
        P("group", None, None),
        P("dp", None),
        P("dp", None),
        P("dp", "mp"),
        P(),
        P(None, "mp"),
        P(),
    )
    out_specs = (P("group", "dp", "mp"), P("group", "dp"), P(None, "mp"))
    return jax.shard_map(body, mesh=mesh, in_specs=in_specs, out_specs=out_specs, check_vma=False)
```

```python
import functools

import jax
import jax.numpy as jnp
from jax import lax
from jax.experimental import pallas as pl
from jax.experimental.pallas import tpu as pltpu
from jax.sharding import PartitionSpec as P


def general_body(
    query_passage_words,
    difficult_distractors,
    vocabulary_vectors,
    layer_weight_matrix,
    lowering_factor_matrix,
    raising_factor_matrix,
    logit_sharpness,
):
    group_index = lax.axis_index("group")
    shard_index = lax.axis_index("dp")
    part_index = lax.axis_index("mp")
    shard_count = lax.axis_size("dp")
    side_ids = query_passage_words[0]
    text_count = side_ids.shape[0]
    length = side_ids.shape[1]
    per_shard = text_count // shard_count
    own_ids = lax.dynamic_slice_in_dim(side_ids, shard_index * per_shard, per_shard, 0)
    columns = jnp.take(vocabulary_vectors, side_ids.reshape(-1), axis=1)
    inputs = lax.all_to_all(columns, "dp", split_axis=1, concat_axis=0, tiled=True)
    tokens = inputs.shape[1]
    feature_width = raising_factor_matrix.shape[1]
    wide_inputs = inputs.astype(jnp.float32)
    inverse = lax.rsqrt(jnp.mean(wide_inputs * wide_inputs, axis=0) + 1e-05)
    normed_state = (wide_inputs * inverse[None, :]).astype(jnp.bfloat16)
    linear_map = lax.dot_general(
        lax.all_gather(layer_weight_matrix, "dp", axis=0, tiled=True),
        normed_state,
        (((0,), (0,)), ((), ())),
        preferred_element_type=jnp.float32,
    )
    reduced_sum = jnp.dot(
        lowering_factor_matrix, normed_state, preferred_element_type=jnp.float32
    ).astype(jnp.bfloat16)
    linear_map = linear_map + lax.dot_general(
        raising_factor_matrix,
        reduced_sum,
        (((0,), (0,)), ((), ())),
        preferred_element_type=jnp.float32,
    )
    own_inputs = lax.dynamic_slice_in_dim(
        inputs, part_index * feature_width, feature_width, 0
    ).astype(jnp.float32)
    hidden_state = own_inputs + jax.nn.silu(linear_map)
    mask = (own_ids != 0).astype(jnp.float32)
    counts = jnp.sum(mask, axis=1)
    summed = jnp.einsum("dnl,nl->nd", hidden_state.reshape(feature_width, per_shard, length), mask)
    pooled = (summed / counts[:, None]).astype(jnp.bfloat16)
    gathered = lax.all_gather(pooled, ("group", "dp"), axis=0, tiled=True)
    part_scores = lax.dot_general(
        pooled, gathered, (((1,), (1,)), ((), ())), preferred_element_type=jnp.float32
    )
    gathered_wide = gathered.astype(jnp.float32)
    part_norms = jnp.sum(gathered_wide * gathered_wide, axis=1)
    dots, norms = lax.psum((part_scores, part_norms), "mp")
    rnorm_all = lax.rsqrt(norms + 1e-06)
    all_count = gathered.shape[0]
    half_count = all_count // 2
    own_rows = (
        group_index * half_count + shard_index * per_shard + jnp.arange(per_shard, dtype=jnp.int32)
    )
    rnorm_own = jnp.take(rnorm_all, own_rows)
    cosine = dots * rnorm_own[:, None] * rnorm_all[None, :]
    multiplier_factor = logit_sharpness[0]
    scores = multiplier_factor * cosine
    column_ids = jnp.arange(all_count, dtype=jnp.int32)
    keep = column_ids[None, :] != own_rows[:, None]
    pair = (own_rows + half_count) % all_count
    weight = (group_index == 0).astype(jnp.float32)
    neg_cols = half_count + difficult_distractors
    top = jnp.max(jnp.where(keep, scores, -jnp.inf), axis=1)
    safe_scores = jnp.where(keep, scores, top[:, None])
    expd = jnp.where(keep, jnp.exp(safe_scores - top[:, None]), 0.0)
    neg_exp = (
        jnp.exp(jnp.minimum(jnp.take_along_axis(scores, neg_cols, axis=1) - top[:, None], 0.0))
        * weight
    )
    total = jnp.sum(expd, axis=1) + jnp.sum(neg_exp, axis=1)
    pair_score = jnp.take_along_axis(scores, pair[:, None], axis=1)[:, 0]
    losses = top + jnp.log(total) - pair_score
    onehot = (column_ids[None, None, :] == neg_cols[:, :, None]).astype(jnp.float32)
    probs = (expd + jnp.einsum("rk,rkc->rc", neg_exp, onehot)) / total[:, None]
    target = (column_ids[None, :] == pair[:, None]).astype(jnp.float32)
    grad_scores = (probs - target) / all_count
    coeff = (grad_scores * rnorm_own[:, None] * rnorm_all[None, :]).astype(jnp.bfloat16)
    along = jnp.dot(coeff, gathered, preferred_element_type=jnp.float32)
    pooled_wide = pooled.astype(jnp.float32)
    radial = jnp.sum(grad_scores * cosine, axis=1) * rnorm_own * rnorm_own
    embedding_gradient = multiplier_factor * (along - radial[:, None] * pooled_wide)
    token_grad = jnp.einsum("nd,nl->dnl", embedding_gradient / counts[:, None], mask).reshape(
        feature_width, tokens
    )
    sigma = jax.nn.sigmoid(linear_map)
    local = (token_grad * sigma * (1.0 + linear_map * (1.0 - sigma))).astype(jnp.bfloat16)
    up_portion = lax.dot_general(
        reduced_sum, local, (((1,), (1,)), ((), ())), preferred_element_type=jnp.float32
    )
    adapter_up_gradient = lax.psum(up_portion, ("group", "dp"))
    embeddings = (pooled_wide * rnorm_own[:, None]).astype(jnp.bfloat16)[None]
    return (embeddings, losses[None], adapter_up_gradient)


BLOCK_BITS, GROUP_BITS, LANE_BITS, ROW_BITS = 10, 9, 7, 4
IDS_PER_BLOCK = 1 << BLOCK_BITS
IDS_PER_GROUP = 1 << GROUP_BITS
CHUNK = 384
STRIPE = 256
ROWS = 1 << ROW_BITS
LANES = 1 << LANE_BITS
FEATURE_ROWS = 128
FIRST = 1152
TAKEN = 512
NT = (((1,), (1,)), ((), ()))
LARGE_VMEM, MODEST_VMEM = 44 * 1024 * 1024, 15 * 1024 * 1024


def mm(a, b, dims=(((1,), (0,)), ((), ()))):
    return lax.dot_general(a, b, dims, preferred_element_type=jnp.float32)


def split(x):
    high = x.astype(jnp.bfloat16)
    return high, (x - high.astype(jnp.float32)).astype(jnp.bfloat16)


def iota(shape, dim):
    return lax.broadcasted_iota(jnp.int32, shape, dim)


def quarter_of(dp_index, cores=2):
    return (dp_index % cores) * 2 + dp_index // cores


def split_quarter(i, j, cores=2):
    shard = lax.axis_index("dp")
    core, side_y = lax.rem(shard, cores), lax.div(shard, cores)
    return (core ^ i) * 2 + (side_y ^ j)


def take_lanes(x, lanes):
    numbers = lax.GatherDimensionNumbers(
        offset_dims=(),
        collapsed_slice_dims=(1,),
        start_index_map=(1,),
        operand_batching_dims=(0,),
        start_indices_batching_dims=(0,),
    )
    mode = lax.GatherScatterMode.PROMISE_IN_BOUNDS
    return lax.gather(x, lanes[..., None], numbers, slice_sizes=(1, 1), mode=mode)


def load_ids(ref):
    return jnp.concatenate([ref[text] for text in range(ref.shape[0])], axis=0)


def fetch(pairs, sems):
    copies = [pltpu.make_async_copy(a, b, sems.at[n]) for n, (a, b) in enumerate(pairs)]
    for copy in copies:
        copy.start()
    for copy in copies:
        copy.wait()


def gather_kernel(
    ids_ref,
    vocab_ref,
    turned_any,
    member_any,
    turned,
    member_ref,
    held,
    token_ref,
    ranks,
    counted,
    bounds,
    held_sems,
    bounds_sem,
    out_sems,
    base,
):
    texts, _, length = ids_ref.shape
    features, vocab = vocab_ref.shape
    blocks = vocab // IDS_PER_BLOCK
    groups = vocab // IDS_PER_GROUP
    span = member_ref.shape[0]

    def vocab_copy(b):
        columns = pl.ds(pl.multiple_of(b * IDS_PER_BLOCK, LANES), IDS_PER_BLOCK)
        return pltpu.make_async_copy(vocab_ref.at[:, columns], held.at[b], held_sems.at[b])

    vocab_copy(0).start()
    for b in range(1, blocks):
        vocab_copy(b).start()

    ids = load_ids(ids_ref)
    valid = ids != 0
    group_of = jnp.where(valid, lax.shift_right_logical(ids, GROUP_BITS), groups)
    group_rows = counted.shape[0]
    group_id = iota((group_rows, length), 0)
    below = jnp.zeros((group_rows, length), jnp.float32)
    for text in range(texts):
        below += jnp.where(group_of[text : text + 1] < group_id, 1.0, 0.0)
    before = jnp.broadcast_to(jnp.sum(below, axis=1, keepdims=True), (group_rows, length))
    counted[...] = before.astype(jnp.int32)
    bounds_copy = pltpu.make_async_copy(counted, bounds, bounds_sem)
    bounds_copy.start()
    earlier = jnp.where(iota((length, length), 0) < iota((length, length), 1), 1.0, 0.0).astype(
        jnp.bfloat16
    )
    for text in range(texts):
        here = jnp.where(group_of[text : text + 1] == group_id, 1.0, 0.0)
        inside = mm(here.astype(jnp.bfloat16), earlier)
        ranks[pl.ds(text, 1), :] = jnp.sum(here * (inside + before), axis=0, keepdims=True)
        before += jnp.broadcast_to(jnp.sum(here, axis=1, keepdims=True), (group_rows, length))
    text_of = iota((texts, length), 0)
    carried = jnp.where(valid, lax.shift_left(ids, ROW_BITS) + text_of, 0).astype(jnp.float32)
    rank = ranks[...]

    def place(p, carry):
        position = (iota((LANES, length), 0) + (p * LANES + base)).astype(jnp.float32)
        total = jnp.zeros((LANES, length), jnp.float32)
        for text in range(texts):
            total += jnp.where(rank[text : text + 1] == position, carried[text : text + 1], 0.0)
        found = jnp.broadcast_to(jnp.sum(total, axis=1, keepdims=True), (LANES, LANES))
        start = pl.multiple_of(p * LANES, LANES)
        row = found.T[0:1].astype(jnp.int32)
        token = lax.shift_right_logical(row, ROW_BITS)
        token_ref[pl.ds(p, 1), :] = jnp.where(token == 0, -vocab, token)
        found = found.astype(jnp.int32)
        real = (found >= ROWS) & ((found & (ROWS - 1)) == iota((LANES, LANES), 1))
        member_ref[pl.ds(start, LANES), :] = jnp.where(real, 1.0, 0.0).astype(jnp.bfloat16)
        turned[:, pl.ds(start, LANES)] = jnp.zeros((features, LANES), jnp.bfloat16)
        return carry

    lax.fori_loop(0, span // LANES, place, 0)
    bounds_copy.wait()

    def within(place):
        return jnp.clip(place - base, 0, span)

    def take(b, carry):
        vocab_copy(b).wait()
        for part in range(IDS_PER_BLOCK // IDS_PER_GROUP):
            group = b * (IDS_PER_BLOCK // IDS_PER_GROUP) + part
            first, last = within(bounds[group, 0]), within(bounds[group + 1, 0])
            begin = lax.shift_right_logical(first, LANE_BITS)
            end = lax.shift_right_logical(last + LANES - 1, LANE_BITS)

            def window(p, carry):
                at = pl.ds(pl.multiple_of(p * LANES, LANES), LANES)
                token = token_ref[pl.ds(p, 1), :] - group * IDS_PER_GROUP
                token = jnp.broadcast_to(token, (FEATURE_ROWS, LANES))
                lane = (token & (LANES - 1)).astype(jnp.int16)
                tile = lax.shift_right_arithmetic(token, LANE_BITS).astype(jnp.int16)
                pieces = [pl.ds(f, FEATURE_ROWS) for f in range(0, TAKEN, FEATURE_ROWS)]
                short = jnp.broadcast_to(token[0:1], (IDS_PER_GROUP, LANES)).astype(jnp.int16)
                picked = jnp.where(
                    short == iota((IDS_PER_GROUP, LANES), 0).astype(jnp.int16), 1.0, 0.0
                ).astype(jnp.bfloat16)
                columns = pl.ds(part * IDS_PER_GROUP, IDS_PER_GROUP)
                rest = pl.ds(TAKEN, features - TAKEN)
                product = mm(held[b, rest, columns], picked).astype(jnp.bfloat16)
                fresh = []
                for rows in pieces:
                    total = jnp.zeros((FEATURE_ROWS, LANES), jnp.bfloat16)
                    for j in range(IDS_PER_GROUP // LANES):
                        columns = pl.ds(part * IDS_PER_GROUP + j * LANES, LANES)
                        total = jnp.where(tile == j, take_lanes(held[b, rows, columns], lane), total)
                    fresh.append(total)
                pieces.append(rest)
                fresh.append(product)
                fresh = [turned[rows, at] + total for rows, total in zip(pieces, fresh)]
                for rows, total in zip(pieces, fresh):
                    turned[rows, at] = total
                return carry

            lax.fori_loop(begin, jnp.where(last > first, end, begin), window, 0)
        return carry

    lax.fori_loop(0, blocks, take, 0)
    fetch([(turned, turned_any), (member_ref, member_any)], out_sems)


def statistics_kernel(
    turned_any, member_any, hard_ref, lower_ref, extra_ref, small, turned, member_ref, spread, sems
):
    fetch([(turned_any, turned), (member_any, member_ref)], sems)
    features, span = turned.shape
    stripes = pl.cdiv(span, STRIPE)
    per_shard, negatives = hard_ref.shape
    shard = lax.axis_index("dp")
    small[...] = jnp.zeros_like(small)
    small[0:per_shard, stripes : stripes + negatives] = hard_ref[...].astype(jnp.float32)
    lower = lower_ref[:, pl.ds(pl.multiple_of(shard * features, LANES), features)]

    misc = jnp.zeros((ROWS, STRIPE), jnp.float32)
    residual = jnp.zeros((features, LANES), jnp.float32)
    for stripe in range(stripes):
        size = min(STRIPE, span - stripe * STRIPE)
        across = pl.ds(stripe * STRIPE, size)
        upright = turned[:, across]
        wide = upright.astype(jnp.float32)
        square = jnp.sum(wide * wide, axis=0, keepdims=True)
        reduced = mm(lower, upright)
        if size < STRIPE:
            none = jnp.zeros((ROWS, STRIPE - size), jnp.float32)
            reduced = jnp.concatenate([reduced, none], axis=1)
            square = jnp.concatenate([square, none[0:1]], axis=1)
        extra_ref[stripe * ROWS : (stripe + 1) * ROWS, :] = reduced.astype(jnp.bfloat16)
        misc = jnp.where(iota((ROWS, STRIPE), 0) == stripe, square, misc)
        residual += mm(upright, member_ref[across, :])
    hard = small[...].T[0:ROWS]
    for i in range(per_shard):
        misc += jnp.where(iota((ROWS, STRIPE), 1) == shard * per_shard + i, hard[:, i : i + 1], 0.0)
    extra_ref[stripes * ROWS : (stripes + 1) * ROWS, :] = misc.astype(jnp.bfloat16)
    residual = jnp.where(lax.axis_index("mp") == shard, residual.T[0:ROWS], 0.0)
    spread[...] = residual
    for q in range(4):
        start = (stripes + 1 + q) * ROWS
        quarter = pl.multiple_of(split_quarter(q // 2, q % 2) * STRIPE, LANES)
        extra_ref[start : start + ROWS, :] = spread[:, pl.ds(quarter, STRIPE)].astype(jnp.bfloat16)


def join_kernel(own_any, core_any, extra_ref, core_extra_ref, chip_ref, inputs_ref, own, core, sems):
    fetch([(own_any, own), (core_any, core)], sems)
    span = own.shape[0]
    common = extra_ref.shape[0] - 4 * ROWS
    near, across = extra_ref[...].astype(jnp.float32), core_extra_ref[...].astype(jnp.float32)
    chip_ref[0:span, :] = (own[...] + core[...].astype(jnp.float32)).astype(jnp.bfloat16)
    chip = near[0:common] + across[0:common]
    inputs = near[common : common + 2 * ROWS] + across[common + 2 * ROWS :]
    sent = jnp.concatenate([chip, inputs[ROWS:]]).astype(jnp.bfloat16)
    chip_ref[span : span + common + ROWS, :] = sent
    inputs_ref[...] = inputs[0:ROWS]


def pool_kernel(
    ids_ref,
    own_ref,
    core_any,
    far_any,
    chip_any,
    inputs_ref,
    member_ref,
    own_rest,
    core_rest,
    far_rest,
    chip_rest,
    inputs_rest,
    member_rest,
    raise_ref,
    sent_ref,
    misc_ref,
    raised,
    total,
    slopes,
    core_ref,
    far_ref,
    chip_ref,
    sems,
    *rest,
    model_width,
):
    texts, _, length = ids_ref.shape
    width = own_ref.shape[1]
    quarter = quarter_of(lax.axis_index("dp"))
    extra_rows = far_ref.shape[0] - own_ref.shape[0]
    chip_extra = chip_any.at[pl.ds(own_ref.shape[0], extra_rows)]
    fetch([(core_any, core_ref), (far_any, far_ref), (chip_extra, chip_ref)], sems)
    raised[...] = jnp.zeros_like(raised)
    raised[0:ROWS, :] = raise_ref[:, pl.ds(pl.multiple_of(quarter * width, LANES), width)]
    total[...] = jnp.zeros_like(total)
    slopes[...] = jnp.zeros_like(slopes)

    def add(refs, far_ref, chip_ref, inputs_ref, member_ref, base):
        span = member_ref.shape[0]
        stripes = pl.cdiv(span, STRIPE)

        def summed(start, size):
            return sum(ref[pl.ds(start, size), :].astype(jnp.float32) for ref in refs)

        def extra(row):
            near, far = chip_ref[pl.ds(row, ROWS), :], far_ref[pl.ds(span + row, ROWS), :]
            return near.astype(jnp.float32) + far.astype(jnp.float32)

        misc = extra(stripes * ROWS)
        if base == 0:
            misc_ref[...] = misc
        inverse = lax.rsqrt(misc / model_width + 1e-05)
        for k in range(stripes):
            size = min(STRIPE, span - k * STRIPE)
            scale = inverse[k : k + 1]
            reduced = (extra(k * ROWS) * scale).astype(jnp.bfloat16)
            reduced = reduced.astype(jnp.float32)
            stacked = jnp.concatenate([reduced, jnp.broadcast_to(scale, (LANES - ROWS, STRIPE))])
            turned = stacked[:, 0:size].T
            low = turned.astype(jnp.bfloat16)
            linear = summed(k * STRIPE, size)
            linear = linear * turned[:, ROWS : ROWS + 1] + mm(low, raised[...])
            sigma = 1.0 / (1.0 + jnp.exp(-linear))
            slope = (sigma * (1.0 + linear * (1.0 - sigma))).astype(jnp.bfloat16)
            member = member_ref[pl.ds(k * STRIPE, size), :].astype(jnp.float32).T
            high, rest = split(linear * sigma)
            chosen = member[0:ROWS].astype(jnp.bfloat16)
            total[...] += mm(chosen, high) + mm(chosen, rest)
            spread = [reduced[:, 0:size] * member[text : text + 1] for text in range(texts)]
            slopes[...] += mm(jnp.concatenate(spread).astype(jnp.bfloat16), slope)
        far_inputs = far_ref[pl.ds(span + (stripes + 1) * ROWS, ROWS), :]
        total[...] += inputs_ref[...] + far_inputs.astype(jnp.float32)

    add((own_ref, core_ref, far_ref), far_ref, chip_ref, inputs_ref, member_ref, 0)
    real = (load_ids(ids_ref) != 0).astype(jnp.float32)

    @pl.when(jnp.sum(real) > member_ref.shape[0])
    def _():
        *here, rest_sems = rest
        span = member_rest.shape[0]
        chip_extra = chip_rest.at[pl.ds(span, here[3].shape[0])]
        there = (own_rest, core_rest, far_rest, chip_extra, inputs_rest, member_rest)
        fetch(list(zip(there, here)), rest_sems)
        own, core, far, chip, inputs, member = here
        add((own, core, far), far, chip, inputs, member, member_ref.shape[0])

    counts = jnp.sum(real, axis=1, keepdims=True)
    pooled = total[0:texts] / counts
    pooled = jnp.concatenate([pooled, jnp.zeros((ROWS - texts, width), jnp.float32)])
    sent_ref[0:ROWS, :] = pooled.astype(jnp.bfloat16)
    for text in range(texts):
        part = slopes[text * ROWS : (text + 1) * ROWS, :] / counts[text : text + 1]
        sent_ref[(text + 1) * ROWS : (text + 2) * ROWS, :] = part.astype(jnp.bfloat16)


def both_sides(near, far):
    queries = lax.axis_index("group") == 0
    return jnp.concatenate([jnp.where(queries, near, far), jnp.where(queries, far, near)], axis=0)


def dots_kernel(near_ref, far_any, packed_ref, slopes_ref, far_ref, sems):
    fetch([(far_any, far_ref)], sems)
    block = both_sides(near_ref[0:ROWS], far_ref[0:ROWS])
    rows = 2 * ROWS
    packed_ref[...] = jnp.zeros_like(packed_ref)
    packed_ref[0:rows, 0:rows] = mm(block, block, NT)
    for part in range(block.shape[1] // LANES):
        piece = block[:, part * LANES : (part + 1) * LANES]
        packed_ref[rows + part * rows : rows + (part + 1) * rows, :] = piece.astype(jnp.float32)
    size = near_ref.shape[0] - ROWS
    slopes_ref[0:size] = near_ref[ROWS:]
    slopes_ref[size:] = far_ref[ROWS:]


def score_kernel(*refs, texts, stripes, negatives):
    there, (misc_ref, sharp_ref, embed_ref, loss_ref, up_ref), (*here, sems) = (
        refs[0:10],
        refs[10:15],
        refs[15:],
    )
    fetch(list(zip(there, here)), sems)
    packed0, packed1, packed2, packed3, slopes0, slopes2 = here[0:6]
    dots0, dots1, dots2, dots3 = here[6:10]
    rows = 2 * ROWS
    per_shard = loss_ref.shape[1]
    group, shard = lax.axis_index("group"), lax.axis_index("dp")
    dots = ((dots0[...] + dots1[...]) + (dots2[...] + dots3[...]))[:, 0:rows]
    down, across = iota((rows, rows), 0), iota((rows, rows), 1)
    same = down == across
    real = (lax.rem(down, ROWS) < texts) & (lax.rem(across, ROWS) < texts)
    diagonal = jnp.where(same, dots, 0.0)
    rnorm_row = lax.rsqrt(jnp.sum(diagonal, axis=0, keepdims=True) + 1e-06)
    rnorm_col = lax.rsqrt(jnp.sum(diagonal, axis=1, keepdims=True) + 1e-06)
    sharpness = sharp_ref[0]
    cosine = dots * rnorm_col * rnorm_row
    scores = sharpness * cosine
    keep = real & ~same
    top = jnp.max(jnp.where(keep, scores, -jnp.inf), axis=0, keepdims=True)
    top = jnp.where(lax.rem(across[0:1], ROWS) < texts, top, 0.0)
    powers = jnp.exp(jnp.where(real, jnp.minimum(scores - top, 0.0), 0.0))
    hard = misc_ref[stripes : stripes + negatives, 0:rows].astype(jnp.int32) + ROWS
    times = jnp.zeros((rows, rows), jnp.float32)
    for k in range(negatives):
        times += jnp.where(hard[k : k + 1] == down, 1.0, 0.0)
    times = jnp.where(across < texts, times, 0.0)
    weights = (jnp.where(keep, 1.0, 0.0) + jnp.where(real, times, 0.0)) * powers
    total = jnp.sum(weights, axis=0, keepdims=True)
    total = jnp.where(lax.rem(across[0:1], ROWS) < texts, total, 1.0)
    pair = (down == lax.rem(across + ROWS, rows)) & real
    pair_score = jnp.sum(jnp.where(pair, scores, 0.0), axis=0, keepdims=True)
    losses = top + jnp.log(total) - pair_score
    grad_scores = (weights / total - jnp.where(pair, 1.0, 0.0)) / (2 * texts)
    coeff = (grad_scores * rnorm_col * rnorm_row).astype(jnp.bfloat16)
    radial = jnp.sum(grad_scores * cosine, axis=0, keepdims=True) * rnorm_row * rnorm_row

    first = shard * per_shard
    loss_col = jnp.sum(jnp.where(same, losses, 0.0), axis=1, keepdims=True)
    at = (iota((rows, LANES), 0) == group * ROWS + first + iota((rows, LANES), 1)) & (
        iota((rows, LANES), 1) < per_shard
    )
    loss_ref[...] = jnp.sum(jnp.where(at, loss_col, 0.0), axis=0, keepdims=True)[:, 0:per_shard]

    along_rows = coeff.astype(jnp.float32).T.astype(jnp.bfloat16)
    radial_col = jnp.sum(jnp.where(same, radial, 0.0), axis=1, keepdims=True)
    rnorm_own = jnp.where(group == 0, rnorm_col[0:ROWS], rnorm_col[ROWS:rows])
    chosen = iota((ROWS, ROWS), 1) == iota((ROWS, ROWS), 0) + first
    chosen = jnp.where(chosen & (iota((ROWS, ROWS), 0) < per_shard), 1.0, 0.0).astype(jnp.bfloat16)
    blocks = ((packed0, slopes0), (packed1, None), (packed2, slopes2), (packed3, None))
    for o, (packed, slopes) in enumerate(blocks):
        parts = packed.shape[0] // rows - 1
        width = parts * LANES
        halves = [packed[rows * (part + 1) : rows * (part + 2), :] for part in range(parts)]
        block = jnp.concatenate(halves, axis=1)
        queries = group == 0
        at = pl.multiple_of(quarter_of(shard ^ o) * width, LANES)
        own = jnp.where(queries, block[0:ROWS], block[ROWS:rows]) * rnorm_own
        picked = mm(chosen, own.astype(jnp.bfloat16)).astype(jnp.bfloat16)
        embed_ref[0, :, pl.ds(at, width)] = picked[0:per_shard]
        if slopes is None:
            continue
        along = mm(along_rows, block.astype(jnp.bfloat16))
        grad = sharpness * (along - radial_col * block)
        near, far = slopes[0 : slopes.shape[0] // 2], slopes[slopes.shape[0] // 2 :]
        grad_near = jnp.where(queries, grad[0:ROWS], grad[ROWS:rows])
        grad_far = jnp.where(queries, grad[ROWS:rows], grad[0:ROWS])
        update = []
        for side, side_grad in ((near, grad_near), (far, grad_far)):
            total = jnp.zeros((ROWS, width), jnp.float32)
            for text in range(texts):
                slope = side[text * ROWS : (text + 1) * ROWS].astype(jnp.float32)
                total += side_grad[text : text + 1] * slope
            update.append(total)
        at = pl.multiple_of((lax.div(shard, 2) ^ (o // 2)) * width, LANES)
        up_ref[:, pl.ds(at, width)] = update[0] + update[1]


def any_spec():
    return pl.BlockSpec(memory_space=pl.ANY)


def vmem_spec():
    return pl.BlockSpec(memory_space=pltpu.VMEM)


def smem_spec():
    return pl.BlockSpec(memory_space=pltpu.SMEM)


def exchange(x, axis, size):
    steps = [[(i, i ^ o) for i in range(size)] for o in range(1, size)]
    return [x] + [lax.ppermute(x, axis, step) for step in steps]


def split_body(
    query_passage_words,
    difficult_distractors,
    vocabulary_vectors,
    layer_weight_matrix,
    lowering_factor_matrix,
    raising_factor_matrix,
    logit_sharpness,
):
    shards, parts = lax.axis_size("dp"), lax.axis_size("mp")
    texts, length = query_passage_words.shape[1:]
    ids = query_passage_words.reshape(texts, 1, length)
    tokens = texts * length
    features, vocab = vocabulary_vectors.shape
    blocks = vocab // IDS_PER_BLOCK
    group_rows = 8 * pl.cdiv(vocab // IDS_PER_GROUP + 1, 8)
    per_shard, negatives = difficult_distractors.shape
    part_width = layer_weight_matrix.shape[1]
    width = part_width // shards
    params = pltpu.CompilerParams(vmem_limit_bytes=LARGE_VMEM)
    modest = pltpu.CompilerParams(vmem_limit_bytes=MODEST_VMEM)
    other_core = [(d, d ^ 1) for d in range(shards)]
    other_y = [(d, d ^ 2) for d in range(shards)]

    def columns(i, j):
        start = split_quarter(i, j) * width
        return lax.dynamic_slice(layer_weight_matrix, (0, start), (features, width))

    def project(base, span):
        stripes = pl.cdiv(span, STRIPE)
        extra_rows = (stripes + 1 + shards) * ROWS
        turned, member = pl.pallas_call(
            functools.partial(gather_kernel, base=base),
            out_shape=[
                jax.ShapeDtypeStruct((features, span), jnp.bfloat16),
                jax.ShapeDtypeStruct((span, LANES), jnp.bfloat16),
            ],
            in_specs=[vmem_spec(), any_spec()],
            out_specs=[any_spec()] * 2,
            scratch_shapes=[
                pltpu.VMEM((features, span), jnp.bfloat16),
                pltpu.VMEM((span, LANES), jnp.bfloat16),
                pltpu.VMEM((blocks, features, IDS_PER_BLOCK), jnp.bfloat16),
                pltpu.VMEM((8 * pl.cdiv(span // LANES, 8), LANES), jnp.int32),
                pltpu.VMEM((texts, length), jnp.float32),
                pltpu.VMEM((group_rows, length), jnp.int32),
                pltpu.SMEM((group_rows, length), jnp.int32),
                pltpu.SemaphoreType.DMA((blocks,)),
                pltpu.SemaphoreType.DMA,
                pltpu.SemaphoreType.DMA((2,)),
            ],
            compiler_params=params,
            name="gather",
        )(ids, vocabulary_vectors)

        def product(turned, i, j):
            return mm(turned, columns(i, j), (((0,), (0,)), ((), ())))

        def narrow(x):
            return x.astype(jnp.bfloat16)

        core1 = lax.ppermute(narrow(product(turned, 1, 1)), "dp", other_core)
        own1 = lax.optimization_barrier(product(turned, 0, 1))
        extra = pl.pallas_call(
            statistics_kernel,
            out_shape=jax.ShapeDtypeStruct((extra_rows, STRIPE), jnp.bfloat16),
            in_specs=[any_spec()] * 2 + [vmem_spec()] * 2,
            out_specs=vmem_spec(),
            scratch_shapes=[
                pltpu.VMEM((LANES, LANES), jnp.float32),
                pltpu.VMEM(turned.shape, turned.dtype),
                pltpu.VMEM(member.shape, member.dtype),
                pltpu.VMEM((ROWS, features), jnp.float32),
                pltpu.SemaphoreType.DMA((2,)),
            ],
            compiler_params=modest,
            cost_estimate=pl.CostEstimate(
                flops=2 * features * span * (ROWS + LANES),
                bytes_accessed=2 * features * span,
                transcendentals=0,
            ),
            name="statistics",
        )(turned, member, difficult_distractors, lowering_factor_matrix)
        core_extra = lax.ppermute(extra, "dp", other_core)
        joined = span + extra_rows - 3 * ROWS
        chip, inputs = pl.pallas_call(
            join_kernel,
            out_shape=[
                jax.ShapeDtypeStruct((joined, width), jnp.bfloat16),
                jax.ShapeDtypeStruct((ROWS, width), jnp.float32),
            ],
            in_specs=[any_spec()] * 2 + [vmem_spec()] * 2,
            out_specs=[vmem_spec()] * 2,
            scratch_shapes=[
                pltpu.VMEM(own1.shape, own1.dtype),
                pltpu.VMEM(core1.shape, core1.dtype),
                pltpu.SemaphoreType.DMA((2,)),
            ],
            compiler_params=modest,
            name="join",
        )(own1, core1, extra, core_extra)
        far = lax.ppermute(chip, "dp", other_y)
        turned, _ = lax.optimization_barrier((turned, chip))
        core0 = lax.ppermute(narrow(product(turned, 1, 0)), "dp", other_core)
        own0 = narrow(product(turned, 0, 0))
        return own0, core0, far, chip, inputs, member

    first = project(0, FIRST)
    later, _ = lax.optimization_barrier((ids, first[0]))
    many = jnp.sum((later != 0).astype(jnp.int32)) > FIRST
    left = tokens - FIRST
    shapes = jax.eval_shape(lambda: project(FIRST, left))
    rest = lax.cond(
        many,
        lambda: project(FIRST, left),
        lambda: tuple(jnp.zeros(x.shape, x.dtype) for x in shapes),
    )
    sent, misc = pl.pallas_call(
        functools.partial(pool_kernel, model_width=float(features * shards)),
        out_shape=[
            jax.ShapeDtypeStruct(((texts + 1) * ROWS, width), jnp.bfloat16),
            jax.ShapeDtypeStruct((ROWS, width), jnp.float32),
        ],
        in_specs=[vmem_spec()] * 2
        + [any_spec()] * 3
        + [vmem_spec()] * 2
        + [any_spec()] * 6
        + [vmem_spec()],
        out_specs=[vmem_spec()] * 2,
        scratch_shapes=[
            pltpu.VMEM((LANES, width), jnp.bfloat16),
            pltpu.VMEM((ROWS, width), jnp.float32),
            pltpu.VMEM((texts * ROWS, width), jnp.float32),
            *[pltpu.VMEM(x.shape, x.dtype) for x in first[1:3]],
            pltpu.VMEM((first[2].shape[0] - FIRST, width), jnp.bfloat16),
            pltpu.SemaphoreType.DMA((3,)),
            *[pltpu.VMEM(x.shape, x.dtype) for x in rest[0:3]],
            pltpu.VMEM((rest[2].shape[0] - left, width), jnp.bfloat16),
            *[pltpu.VMEM(x.shape, x.dtype) for x in rest[4:6]],
            pltpu.SemaphoreType.DMA((6,)),
        ],
        compiler_params=modest,
        name="pool",
    )(ids, *first, *rest, raising_factor_matrix)
    far_side = lax.ppermute(sent, "group", [(0, 1), (1, 0)])
    rows = 2 * ROWS
    packed, slopes = pl.pallas_call(
        dots_kernel,
        out_shape=[
            jax.ShapeDtypeStruct((rows + width // LANES * rows, LANES), jnp.float32),
            jax.ShapeDtypeStruct((2 * texts * ROWS, width), jnp.bfloat16),
        ],
        in_specs=[vmem_spec(), any_spec()],
        out_specs=[vmem_spec()] * 2,
        scratch_shapes=[
            pltpu.VMEM(sent.shape, sent.dtype),
            pltpu.SemaphoreType.DMA((1,)),
        ],
        compiler_params=modest,
        name="dots",
    )(sent, far_side)
    packed = exchange(packed, "dp", shards)
    dots = [x[0:rows] for x in packed]
    dots = (dots[0] + dots[1]) + (dots[2] + dots[3])
    slopes, dots = lax.optimization_barrier((slopes, dots))
    dots = exchange(dots, "mp", parts)
    slopes = [slopes, lax.ppermute(slopes, "dp", other_y)]
    embeddings, losses, update = pl.pallas_call(
        functools.partial(
            score_kernel, texts=texts, stripes=pl.cdiv(FIRST, STRIPE), negatives=negatives
        ),
        out_shape=[
            jax.ShapeDtypeStruct((1, per_shard, part_width), jnp.bfloat16),
            jax.ShapeDtypeStruct((1, per_shard), jnp.float32),
            jax.ShapeDtypeStruct((ROWS, part_width // 2), jnp.float32),
        ],
        in_specs=[any_spec()] * 10 + [vmem_spec(), smem_spec()],
        out_specs=[vmem_spec()] * 3,
        scratch_shapes=[pltpu.VMEM(x.shape, x.dtype) for x in (*packed, *slopes, *dots)]
        + [pltpu.SemaphoreType.DMA((10,))],
        compiler_params=modest,
        name="score",
    )(*packed, *slopes, *dots, misc, logit_sharpness)
    other = lax.ppermute(update, "dp", other_core)
    core = lax.rem(lax.axis_index("dp"), 2)
    halves = [jnp.where(core == 0, update, other), jnp.where(core == 0, other, update)]
    return (embeddings, losses, jnp.concatenate(halves, axis=1))


def body(words, hard, vocabulary, weight, lowering, raising, sharpness):
    shards, parts = lax.axis_size("dp"), lax.axis_size("mp")
    texts, length = words.shape[1:]
    features, vocab = vocabulary.shape
    negatives = hard.shape[1]
    square = shards == 4 and features == weight.shape[1] == 4 * STRIPE and parts == shards
    small = texts <= ROWS - 2 and length == LANES and FIRST < texts * length <= 2048
    even = (texts * length - FIRST) % CHUNK == 0 and vocab % IDS_PER_BLOCK == 0
    fits = features * vocab <= 2**24 and features % (4 * LANES) == 0
    spare = pl.cdiv(FIRST, STRIPE) + negatives <= ROWS and lowering.shape[0] == ROWS
    fast = square and small and even and fits and spare and lax.axis_size("group") == 2
    chosen = split_body if fast else general_body
    return chosen(words, hard, vocabulary, weight, lowering, raising, sharpness)


def solution(mesh):
    in_specs = (
        P("group", None, None),
        P("dp", None),
        P("dp", None),
        P("dp", "mp"),
        P(),
        P(None, "mp"),
        P(),
    )
    out_specs = (P("group", "dp", "mp"), P("group", "dp"), P(None, "mp"))
    return jax.shard_map(body, mesh=mesh, in_specs=in_specs, out_specs=out_specs, check_vma=False)
```

```python
import functools

import jax
import jax.numpy as jnp
from jax import lax
from jax.experimental import pallas as pl
from jax.experimental.pallas import tpu as pltpu
from jax.sharding import PartitionSpec as P


def general_body(
    query_passage_words,
    difficult_distractors,
    vocabulary_vectors,
    layer_weight_matrix,
    lowering_factor_matrix,
    raising_factor_matrix,
    logit_sharpness,
):
    group_index = lax.axis_index("group")
    shard_index = lax.axis_index("dp")
    part_index = lax.axis_index("mp")
    shard_count = lax.axis_size("dp")
    side_ids = query_passage_words[0]
    text_count = side_ids.shape[0]
    length = side_ids.shape[1]
    per_shard = text_count // shard_count
    own_ids = lax.dynamic_slice_in_dim(side_ids, shard_index * per_shard, per_shard, 0)
    columns = jnp.take(vocabulary_vectors, side_ids.reshape(-1), axis=1)
    inputs = lax.all_to_all(columns, "dp", split_axis=1, concat_axis=0, tiled=True)
    tokens = inputs.shape[1]
    feature_width = raising_factor_matrix.shape[1]
    wide_inputs = inputs.astype(jnp.float32)
    inverse = lax.rsqrt(jnp.mean(wide_inputs * wide_inputs, axis=0) + 1e-05)
    normed_state = (wide_inputs * inverse[None, :]).astype(jnp.bfloat16)
    linear_map = lax.dot_general(
        lax.all_gather(layer_weight_matrix, "dp", axis=0, tiled=True),
        normed_state,
        (((0,), (0,)), ((), ())),
        preferred_element_type=jnp.float32,
    )
    reduced_sum = jnp.dot(
        lowering_factor_matrix, normed_state, preferred_element_type=jnp.float32
    ).astype(jnp.bfloat16)
    linear_map = linear_map + lax.dot_general(
        raising_factor_matrix,
        reduced_sum,
        (((0,), (0,)), ((), ())),
        preferred_element_type=jnp.float32,
    )
    own_inputs = lax.dynamic_slice_in_dim(
        inputs, part_index * feature_width, feature_width, 0
    ).astype(jnp.float32)
    hidden_state = own_inputs + jax.nn.silu(linear_map)
    mask = (own_ids != 0).astype(jnp.float32)
    counts = jnp.sum(mask, axis=1)
    summed = jnp.einsum("dnl,nl->nd", hidden_state.reshape(feature_width, per_shard, length), mask)
    pooled = (summed / counts[:, None]).astype(jnp.bfloat16)
    gathered = lax.all_gather(pooled, ("group", "dp"), axis=0, tiled=True)
    part_scores = lax.dot_general(
        pooled, gathered, (((1,), (1,)), ((), ())), preferred_element_type=jnp.float32
    )
    gathered_wide = gathered.astype(jnp.float32)
    part_norms = jnp.sum(gathered_wide * gathered_wide, axis=1)
    dots, norms = lax.psum((part_scores, part_norms), "mp")
    rnorm_all = lax.rsqrt(norms + 1e-06)
    all_count = gathered.shape[0]
    half_count = all_count // 2
    own_rows = (
        group_index * half_count + shard_index * per_shard + jnp.arange(per_shard, dtype=jnp.int32)
    )
    rnorm_own = jnp.take(rnorm_all, own_rows)
    cosine = dots * rnorm_own[:, None] * rnorm_all[None, :]
    multiplier_factor = logit_sharpness[0]
    scores = multiplier_factor * cosine
    column_ids = jnp.arange(all_count, dtype=jnp.int32)
    keep = column_ids[None, :] != own_rows[:, None]
    pair = (own_rows + half_count) % all_count
    weight = (group_index == 0).astype(jnp.float32)
    neg_cols = half_count + difficult_distractors
    top = jnp.max(jnp.where(keep, scores, -jnp.inf), axis=1)
    safe_scores = jnp.where(keep, scores, top[:, None])
    expd = jnp.where(keep, jnp.exp(safe_scores - top[:, None]), 0.0)
    neg_exp = (
        jnp.exp(jnp.minimum(jnp.take_along_axis(scores, neg_cols, axis=1) - top[:, None], 0.0))
        * weight
    )
    total = jnp.sum(expd, axis=1) + jnp.sum(neg_exp, axis=1)
    pair_score = jnp.take_along_axis(scores, pair[:, None], axis=1)[:, 0]
    losses = top + jnp.log(total) - pair_score
    onehot = (column_ids[None, None, :] == neg_cols[:, :, None]).astype(jnp.float32)
    probs = (expd + jnp.einsum("rk,rkc->rc", neg_exp, onehot)) / total[:, None]
    target = (column_ids[None, :] == pair[:, None]).astype(jnp.float32)
    grad_scores = (probs - target) / all_count
    coeff = (grad_scores * rnorm_own[:, None] * rnorm_all[None, :]).astype(jnp.bfloat16)
    along = jnp.dot(coeff, gathered, preferred_element_type=jnp.float32)
    pooled_wide = pooled.astype(jnp.float32)
    radial = jnp.sum(grad_scores * cosine, axis=1) * rnorm_own * rnorm_own
    embedding_gradient = multiplier_factor * (along - radial[:, None] * pooled_wide)
    token_grad = jnp.einsum("nd,nl->dnl", embedding_gradient / counts[:, None], mask).reshape(
        feature_width, tokens
    )
    sigma = jax.nn.sigmoid(linear_map)
    local = (token_grad * sigma * (1.0 + linear_map * (1.0 - sigma))).astype(jnp.bfloat16)
    up_portion = lax.dot_general(
        reduced_sum, local, (((1,), (1,)), ((), ())), preferred_element_type=jnp.float32
    )
    adapter_up_gradient = lax.psum(up_portion, ("group", "dp"))
    embeddings = (pooled_wide * rnorm_own[:, None]).astype(jnp.bfloat16)[None]
    return (embeddings, losses[None], adapter_up_gradient)


BLOCK_BITS, GROUP_BITS, LANE_BITS, ROW_BITS = 10, 9, 7, 4
IDS_PER_BLOCK = 1 << BLOCK_BITS
IDS_PER_GROUP = 1 << GROUP_BITS
CHUNK = 384
STRIPE = 256
ROWS = 1 << ROW_BITS
LANES = 1 << LANE_BITS
FEATURE_ROWS = 128
FIRST = 1152
TAKEN = 768
NT = (((1,), (1,)), ((), ()))
LARGE_VMEM, MODEST_VMEM = 44 * 1024 * 1024, 15 * 1024 * 1024


def mm(a, b, dims=(((1,), (0,)), ((), ()))):
    return lax.dot_general(a, b, dims, preferred_element_type=jnp.float32)


def split(x):
    high = x.astype(jnp.bfloat16)
    return high, (x - high.astype(jnp.float32)).astype(jnp.bfloat16)


def iota(shape, dim):
    return lax.broadcasted_iota(jnp.int32, shape, dim)


def quarter_of(dp_index, cores=2):
    return (dp_index % cores) * 2 + dp_index // cores


def split_quarter(i, j, cores=2):
    shard = lax.axis_index("dp")
    core, side_y = lax.rem(shard, cores), lax.div(shard, cores)
    return (core ^ i) * 2 + (side_y ^ j)


def take_lanes(x, lanes):
    numbers = lax.GatherDimensionNumbers(
        offset_dims=(),
        collapsed_slice_dims=(1,),
        start_index_map=(1,),
        operand_batching_dims=(0,),
        start_indices_batching_dims=(0,),
    )
    mode = lax.GatherScatterMode.PROMISE_IN_BOUNDS
    return lax.gather(x, lanes[..., None], numbers, slice_sizes=(1, 1), mode=mode)


def load_ids(ref):
    return jnp.concatenate([ref[text] for text in range(ref.shape[0])], axis=0)


def gather_kernel(
    ids_ref,
    vocab_ref,
    turned,
    member_ref,
    held,
    token_ref,
    ranks,
    counted,
    bounds,
    held_sems,
    bounds_sem,
    base,
):
    texts, _, length = ids_ref.shape
    features, vocab = vocab_ref.shape
    blocks = vocab // IDS_PER_BLOCK
    groups = vocab // IDS_PER_GROUP
    span = member_ref.shape[0]

    def vocab_copy(b):
        columns = pl.ds(pl.multiple_of(b * IDS_PER_BLOCK, LANES), IDS_PER_BLOCK)
        return pltpu.make_async_copy(vocab_ref.at[:, columns], held.at[b], held_sems.at[b])

    vocab_copy(0).start()
    for b in range(1, blocks):
        vocab_copy(b).start()

    ids = load_ids(ids_ref)
    valid = ids != 0
    group_of = jnp.where(valid, lax.shift_right_logical(ids, GROUP_BITS), groups)
    group_rows = counted.shape[0]
    group_id = iota((group_rows, length), 0)
    below = jnp.zeros((group_rows, length), jnp.float32)
    for text in range(texts):
        below += jnp.where(group_of[text : text + 1] < group_id, 1.0, 0.0)
    before = jnp.broadcast_to(jnp.sum(below, axis=1, keepdims=True), (group_rows, length))
    counted[...] = before.astype(jnp.int32)
    bounds_copy = pltpu.make_async_copy(counted, bounds, bounds_sem)
    bounds_copy.start()
    earlier = jnp.where(iota((length, length), 0) < iota((length, length), 1), 1.0, 0.0).astype(
        jnp.bfloat16
    )
    for text in range(texts):
        here = jnp.where(group_of[text : text + 1] == group_id, 1.0, 0.0)
        inside = mm(here.astype(jnp.bfloat16), earlier)
        ranks[pl.ds(text, 1), :] = jnp.sum(here * (inside + before), axis=0, keepdims=True)
        before += jnp.broadcast_to(jnp.sum(here, axis=1, keepdims=True), (group_rows, length))
    text_of = iota((texts, length), 0)
    carried = jnp.where(valid, lax.shift_left(ids, ROW_BITS) + text_of, 0).astype(jnp.float32)
    rank = ranks[...]

    def place(p, carry):
        position = (iota((LANES, length), 0) + (p * LANES + base)).astype(jnp.float32)
        total = jnp.zeros((LANES, length), jnp.float32)
        for text in range(texts):
            total += jnp.where(rank[text : text + 1] == position, carried[text : text + 1], 0.0)
        found = jnp.broadcast_to(jnp.sum(total, axis=1, keepdims=True), (LANES, LANES))
        start = pl.multiple_of(p * LANES, LANES)
        row = found.T[0:1].astype(jnp.int32)
        token = lax.shift_right_logical(row, ROW_BITS)
        token_ref[pl.ds(p, 1), :] = jnp.where(token == 0, -vocab, token)
        found = found.astype(jnp.int32)
        real = (found >= ROWS) & ((found & (ROWS - 1)) == iota((LANES, LANES), 1))
        member_ref[pl.ds(start, LANES), :] = jnp.where(real, 1.0, 0.0).astype(jnp.bfloat16)
        turned[:, pl.ds(start, LANES)] = jnp.zeros((features, LANES), jnp.bfloat16)
        return carry

    lax.fori_loop(0, span // LANES, place, 0)
    bounds_copy.wait()

    def within(place):
        return jnp.clip(place - base, 0, span)

    def take(b, carry):
        vocab_copy(b).wait()
        for part in range(IDS_PER_BLOCK // IDS_PER_GROUP):
            group = b * (IDS_PER_BLOCK // IDS_PER_GROUP) + part
            first, last = within(bounds[group, 0]), within(bounds[group + 1, 0])
            begin = lax.shift_right_logical(first, LANE_BITS)
            end = lax.shift_right_logical(last + LANES - 1, LANE_BITS)

            def window(p, carry):
                at = pl.ds(pl.multiple_of(p * LANES, LANES), LANES)
                token = token_ref[pl.ds(p, 1), :] - group * IDS_PER_GROUP
                token = jnp.broadcast_to(token, (FEATURE_ROWS, LANES))
                lane = (token & (LANES - 1)).astype(jnp.int16)
                tile = lax.shift_right_arithmetic(token, LANE_BITS).astype(jnp.int16)
                pieces = [pl.ds(f, FEATURE_ROWS) for f in range(0, TAKEN, FEATURE_ROWS)]
                short = jnp.broadcast_to(token[0:1], (IDS_PER_GROUP, LANES)).astype(jnp.int16)
                picked = jnp.where(
                    short == iota((IDS_PER_GROUP, LANES), 0).astype(jnp.int16), 1.0, 0.0
                ).astype(jnp.bfloat16)
                columns = pl.ds(part * IDS_PER_GROUP, IDS_PER_GROUP)
                rest = pl.ds(TAKEN, features - TAKEN)
                product = mm(held[b, rest, columns], picked).astype(jnp.bfloat16)
                fresh = []
                for rows in pieces:
                    total = jnp.zeros((FEATURE_ROWS, LANES), jnp.bfloat16)
                    for j in range(IDS_PER_GROUP // LANES):
                        columns = pl.ds(part * IDS_PER_GROUP + j * LANES, LANES)
                        total = jnp.where(tile == j, take_lanes(held[b, rows, columns], lane), total)
                    fresh.append(total)
                pieces.append(rest)
                fresh.append(product)
                fresh = [turned[rows, at] + total for rows, total in zip(pieces, fresh)]
                for rows, total in zip(pieces, fresh):
                    turned[rows, at] = total
                return carry

            lax.fori_loop(begin, jnp.where(last > first, end, begin), window, 0)
        return carry

    lax.fori_loop(0, blocks, take, 0)


def statistics_kernel(turned, member_ref, hard_ref, lower_ref, extra_ref, small, spread):
    features, span = turned.shape
    stripes = pl.cdiv(span, STRIPE)
    per_shard, negatives = hard_ref.shape
    shard = lax.axis_index("dp")
    small[...] = jnp.zeros_like(small)
    small[0:per_shard, stripes : stripes + negatives] = hard_ref[...].astype(jnp.float32)
    lower = lower_ref[:, pl.ds(pl.multiple_of(shard * features, LANES), features)]

    misc = jnp.zeros((ROWS, STRIPE), jnp.float32)
    residual = jnp.zeros((features, LANES), jnp.float32)
    for stripe in range(stripes):
        size = min(STRIPE, span - stripe * STRIPE)
        across = pl.ds(stripe * STRIPE, size)
        upright = turned[:, across]
        wide = upright.astype(jnp.float32)
        square = jnp.sum(wide * wide, axis=0, keepdims=True)
        reduced = mm(lower, upright)
        if size < STRIPE:
            none = jnp.zeros((ROWS, STRIPE - size), jnp.float32)
            reduced = jnp.concatenate([reduced, none], axis=1)
            square = jnp.concatenate([square, none[0:1]], axis=1)
        extra_ref[stripe * ROWS : (stripe + 1) * ROWS, :] = reduced.astype(jnp.bfloat16)
        misc = jnp.where(iota((ROWS, STRIPE), 0) == stripe, square, misc)
        residual += mm(upright, member_ref[across, :])
    hard = small[...].T[0:ROWS]
    for i in range(per_shard):
        misc += jnp.where(iota((ROWS, STRIPE), 1) == shard * per_shard + i, hard[:, i : i + 1], 0.0)
    extra_ref[stripes * ROWS : (stripes + 1) * ROWS, :] = misc.astype(jnp.bfloat16)
    residual = jnp.where(lax.axis_index("mp") == shard, residual.T[0:ROWS], 0.0)
    spread[...] = residual
    for q in range(4):
        start = (stripes + 1 + q) * ROWS
        quarter = pl.multiple_of(split_quarter(q // 2, q % 2) * STRIPE, LANES)
        extra_ref[start : start + ROWS, :] = spread[:, pl.ds(quarter, STRIPE)].astype(jnp.bfloat16)


def join_kernel(own, core, extra_ref, core_extra_ref, chip_ref, inputs_ref):
    span = own.shape[0]
    common = extra_ref.shape[0] - 4 * ROWS
    near, across = extra_ref[...].astype(jnp.float32), core_extra_ref[...].astype(jnp.float32)
    chip_ref[0:span, :] = (own[...] + core[...].astype(jnp.float32)).astype(jnp.bfloat16)
    chip = near[0:common] + across[0:common]
    inputs = near[common : common + 2 * ROWS] + across[common + 2 * ROWS :]
    sent = jnp.concatenate([chip, inputs[ROWS:]]).astype(jnp.bfloat16)
    chip_ref[span : span + common + ROWS, :] = sent
    inputs_ref[...] = inputs[0:ROWS]


def pool_kernel(
    ids_ref,
    own_ref,
    core_ref,
    far_ref,
    chip_ref,
    inputs_ref,
    member_ref,
    own_rest,
    core_rest,
    far_rest,
    chip_rest,
    inputs_rest,
    member_rest,
    raise_ref,
    sent_ref,
    misc_ref,
    raised,
    total,
    slopes,
    model_width,
):
    texts, _, length = ids_ref.shape
    width = own_ref.shape[1]
    quarter = quarter_of(lax.axis_index("dp"))
    raised[...] = jnp.zeros_like(raised)
    raised[0:ROWS, :] = raise_ref[:, pl.ds(pl.multiple_of(quarter * width, LANES), width)]
    total[...] = jnp.zeros_like(total)
    slopes[...] = jnp.zeros_like(slopes)

    def add(refs, far_ref, chip_ref, inputs_ref, member_ref, base):
        span = member_ref.shape[0]
        stripes = pl.cdiv(span, STRIPE)

        def summed(start, size):
            return sum(ref[pl.ds(start, size), :].astype(jnp.float32) for ref in refs)

        def extra(row):
            rows = pl.ds(span + row, ROWS)
            near, far = chip_ref[rows, :], far_ref[rows, :]
            return near.astype(jnp.float32) + far.astype(jnp.float32)

        misc = extra(stripes * ROWS)
        if base == 0:
            misc_ref[...] = misc
        inverse = lax.rsqrt(misc / model_width + 1e-05)
        for k in range(stripes):
            size = min(STRIPE, span - k * STRIPE)
            scale = inverse[k : k + 1]
            reduced = (extra(k * ROWS) * scale).astype(jnp.bfloat16)
            reduced = reduced.astype(jnp.float32)
            stacked = jnp.concatenate([reduced, jnp.broadcast_to(scale, (LANES - ROWS, STRIPE))])
            turned = stacked[:, 0:size].T
            low = turned.astype(jnp.bfloat16)
            linear = summed(k * STRIPE, size)
            linear = linear * turned[:, ROWS : ROWS + 1] + mm(low, raised[...])
            sigma = 1.0 / (1.0 + jnp.exp(-linear))
            slope = (sigma * (1.0 + linear * (1.0 - sigma))).astype(jnp.bfloat16)
            member = member_ref[pl.ds(k * STRIPE, size), :].astype(jnp.float32).T
            high, rest = split(linear * sigma)
            chosen = member[0:ROWS].astype(jnp.bfloat16)
            total[...] += mm(chosen, high) + mm(chosen, rest)
            spread = [reduced[:, 0:size] * member[text : text + 1] for text in range(texts)]
            slopes[...] += mm(jnp.concatenate(spread).astype(jnp.bfloat16), slope)
        far_inputs = far_ref[pl.ds(span + (stripes + 1) * ROWS, ROWS), :]
        total[...] += inputs_ref[...] + far_inputs.astype(jnp.float32)

    add((own_ref, core_ref, far_ref), far_ref, chip_ref, inputs_ref, member_ref, 0)
    real = (load_ids(ids_ref) != 0).astype(jnp.float32)

    @pl.when(jnp.sum(real) > member_ref.shape[0])
    def _():
        refs = (own_rest, core_rest, far_rest)
        add(refs, far_rest, chip_rest, inputs_rest, member_rest, member_ref.shape[0])

    counts = jnp.sum(real, axis=1, keepdims=True)
    pooled = total[0:texts] / counts
    pooled = jnp.concatenate([pooled, jnp.zeros((ROWS - texts, width), jnp.float32)])
    sent_ref[0:ROWS, :] = pooled.astype(jnp.bfloat16)
    for text in range(texts):
        part = slopes[text * ROWS : (text + 1) * ROWS, :] / counts[text : text + 1]
        sent_ref[(text + 1) * ROWS : (text + 2) * ROWS, :] = part.astype(jnp.bfloat16)


def both_sides(near, far):
    queries = lax.axis_index("group") == 0
    return jnp.concatenate([jnp.where(queries, near, far), jnp.where(queries, far, near)], axis=0)


def dots_kernel(near_ref, far_ref, packed_ref, slopes_ref):
    block = both_sides(near_ref[0:ROWS], far_ref[0:ROWS])
    rows = 2 * ROWS
    packed_ref[...] = jnp.zeros_like(packed_ref)
    packed_ref[0:rows, 0:rows] = mm(block, block, NT)
    for part in range(block.shape[1] // LANES):
        piece = block[:, part * LANES : (part + 1) * LANES]
        packed_ref[rows + part * rows : rows + (part + 1) * rows, :] = piece.astype(jnp.float32)
    size = near_ref.shape[0] - ROWS
    slopes_ref[0:size] = near_ref[ROWS:]
    slopes_ref[size:] = far_ref[ROWS:]


def score_kernel(*refs, texts, stripes, negatives):
    packed0, packed1, packed2, packed3, slopes0, slopes2 = refs[0:6]
    dots0, dots1, dots2, dots3, misc_ref, sharp_ref = refs[6:12]
    embed_ref, loss_ref, up_ref = refs[12:15]
    rows = 2 * ROWS
    per_shard = loss_ref.shape[1]
    group, shard = lax.axis_index("group"), lax.axis_index("dp")
    dots = ((dots0[...] + dots1[...]) + (dots2[...] + dots3[...]))[:, 0:rows]
    down, across = iota((rows, rows), 0), iota((rows, rows), 1)
    same = down == across
    real = (lax.rem(down, ROWS) < texts) & (lax.rem(across, ROWS) < texts)
    diagonal = jnp.where(same, dots, 0.0)
    rnorm_row = lax.rsqrt(jnp.sum(diagonal, axis=0, keepdims=True) + 1e-06)
    rnorm_col = lax.rsqrt(jnp.sum(diagonal, axis=1, keepdims=True) + 1e-06)
    sharpness = sharp_ref[0]
    cosine = dots * rnorm_col * rnorm_row
    scores = sharpness * cosine
    keep = real & ~same
    top = jnp.max(jnp.where(keep, scores, -jnp.inf), axis=0, keepdims=True)
    top = jnp.where(lax.rem(across[0:1], ROWS) < texts, top, 0.0)
    powers = jnp.exp(jnp.where(real, jnp.minimum(scores - top, 0.0), 0.0))
    hard = misc_ref[stripes : stripes + negatives, 0:rows].astype(jnp.int32) + ROWS
    times = jnp.zeros((rows, rows), jnp.float32)
    for k in range(negatives):
        times += jnp.where(hard[k : k + 1] == down, 1.0, 0.0)
    times = jnp.where(across < texts, times, 0.0)
    weights = (jnp.where(keep, 1.0, 0.0) + jnp.where(real, times, 0.0)) * powers
    total = jnp.sum(weights, axis=0, keepdims=True)
    total = jnp.where(lax.rem(across[0:1], ROWS) < texts, total, 1.0)
    pair = (down == lax.rem(across + ROWS, rows)) & real
    pair_score = jnp.sum(jnp.where(pair, scores, 0.0), axis=0, keepdims=True)
    losses = top + jnp.log(total) - pair_score
    grad_scores = (weights / total - jnp.where(pair, 1.0, 0.0)) / (2 * texts)
    coeff = (grad_scores * rnorm_col * rnorm_row).astype(jnp.bfloat16)
    radial = jnp.sum(grad_scores * cosine, axis=0, keepdims=True) * rnorm_row * rnorm_row

    first = shard * per_shard
    loss_col = jnp.sum(jnp.where(same, losses, 0.0), axis=1, keepdims=True)
    at = (iota((rows, LANES), 0) == group * ROWS + first + iota((rows, LANES), 1)) & (
        iota((rows, LANES), 1) < per_shard
    )
    loss_ref[...] = jnp.sum(jnp.where(at, loss_col, 0.0), axis=0, keepdims=True)[:, 0:per_shard]

    along_rows = coeff.astype(jnp.float32).T.astype(jnp.bfloat16)
    radial_col = jnp.sum(jnp.where(same, radial, 0.0), axis=1, keepdims=True)
    rnorm_own = jnp.where(group == 0, rnorm_col[0:ROWS], rnorm_col[ROWS:rows])
    chosen = iota((ROWS, ROWS), 1) == iota((ROWS, ROWS), 0) + first
    chosen = jnp.where(chosen & (iota((ROWS, ROWS), 0) < per_shard), 1.0, 0.0).astype(jnp.bfloat16)
    blocks = ((packed0, slopes0), (packed1, None), (packed2, slopes2), (packed3, None))
    for o, (packed, slopes) in enumerate(blocks):
        parts = packed.shape[0] // rows - 1
        width = parts * LANES
        halves = [packed[rows * (part + 1) : rows * (part + 2), :] for part in range(parts)]
        block = jnp.concatenate(halves, axis=1)
        queries = group == 0
        at = pl.multiple_of(quarter_of(shard ^ o) * width, LANES)
        own = jnp.where(queries, block[0:ROWS], block[ROWS:rows]) * rnorm_own
        picked = mm(chosen, own.astype(jnp.bfloat16)).astype(jnp.bfloat16)
        embed_ref[0, :, pl.ds(at, width)] = picked[0:per_shard]
        if slopes is None:
            continue
        along = mm(along_rows, block.astype(jnp.bfloat16))
        grad = sharpness * (along - radial_col * block)
        near, far = slopes[0 : slopes.shape[0] // 2], slopes[slopes.shape[0] // 2 :]
        grad_near = jnp.where(queries, grad[0:ROWS], grad[ROWS:rows])
        grad_far = jnp.where(queries, grad[ROWS:rows], grad[0:ROWS])
        update = []
        for side, side_grad in ((near, grad_near), (far, grad_far)):
            total = jnp.zeros((ROWS, width), jnp.float32)
            for text in range(texts):
                slope = side[text * ROWS : (text + 1) * ROWS].astype(jnp.float32)
                total += side_grad[text : text + 1] * slope
            update.append(total)
        at = pl.multiple_of((lax.div(shard, 2) ^ (o // 2)) * width, LANES)
        up_ref[:, pl.ds(at, width)] = update[0] + update[1]


def any_spec():
    return pl.BlockSpec(memory_space=pl.ANY)


def vmem_spec():
    return pl.BlockSpec(memory_space=pltpu.VMEM)


def smem_spec():
    return pl.BlockSpec(memory_space=pltpu.SMEM)


def exchange(x, axis, size):
    steps = [[(i, i ^ o) for i in range(size)] for o in range(1, size)]
    return [x] + [lax.ppermute(x, axis, step) for step in steps]


def split_body(
    query_passage_words,
    difficult_distractors,
    vocabulary_vectors,
    layer_weight_matrix,
    lowering_factor_matrix,
    raising_factor_matrix,
    logit_sharpness,
):
    shards, parts = lax.axis_size("dp"), lax.axis_size("mp")
    texts, length = query_passage_words.shape[1:]
    ids = query_passage_words.reshape(texts, 1, length)
    tokens = texts * length
    features, vocab = vocabulary_vectors.shape
    blocks = vocab // IDS_PER_BLOCK
    group_rows = 8 * pl.cdiv(vocab // IDS_PER_GROUP + 1, 8)
    per_shard, negatives = difficult_distractors.shape
    part_width = layer_weight_matrix.shape[1]
    width = part_width // shards
    params = pltpu.CompilerParams(vmem_limit_bytes=LARGE_VMEM)
    modest = pltpu.CompilerParams(vmem_limit_bytes=MODEST_VMEM)
    other_core = [(d, d ^ 1) for d in range(shards)]
    other_y = [(d, d ^ 2) for d in range(shards)]

    def columns(i, j):
        start = split_quarter(i, j) * width
        return lax.dynamic_slice(layer_weight_matrix, (0, start), (features, width))

    def project(base, span):
        stripes = pl.cdiv(span, STRIPE)
        extra_rows = (stripes + 1 + shards) * ROWS
        turned, member = pl.pallas_call(
            functools.partial(gather_kernel, base=base),
            out_shape=[
                jax.ShapeDtypeStruct((features, span), jnp.bfloat16),
                jax.ShapeDtypeStruct((span, LANES), jnp.bfloat16),
            ],
            in_specs=[vmem_spec(), any_spec()],
            out_specs=[vmem_spec()] * 2,
            scratch_shapes=[
                pltpu.VMEM((blocks, features, IDS_PER_BLOCK), jnp.bfloat16),
                pltpu.VMEM((8 * pl.cdiv(span // LANES, 8), LANES), jnp.int32),
                pltpu.VMEM((texts, length), jnp.float32),
                pltpu.VMEM((group_rows, length), jnp.int32),
                pltpu.SMEM((group_rows, length), jnp.int32),
                pltpu.SemaphoreType.DMA((blocks,)),
                pltpu.SemaphoreType.DMA,
            ],
            compiler_params=params,
            name="gather",
        )(ids, vocabulary_vectors)

        def product(turned, i, j):
            return mm(turned, columns(i, j), (((0,), (0,)), ((), ())))

        def narrow(x):
            return x.astype(jnp.bfloat16)

        core1 = lax.ppermute(narrow(product(turned, 1, 1)), "dp", other_core)
        own1 = lax.optimization_barrier(product(turned, 0, 1))
        extra = pl.pallas_call(
            statistics_kernel,
            out_shape=jax.ShapeDtypeStruct((extra_rows, STRIPE), jnp.bfloat16),
            in_specs=[vmem_spec()] * 4,
            out_specs=vmem_spec(),
            scratch_shapes=[
                pltpu.VMEM((LANES, LANES), jnp.float32),
                pltpu.VMEM((ROWS, features), jnp.float32),
            ],
            compiler_params=modest,
            cost_estimate=pl.CostEstimate(
                flops=2 * features * span * (ROWS + LANES),
                bytes_accessed=2 * features * span,
                transcendentals=0,
            ),
            name="statistics",
        )(turned, member, difficult_distractors, lowering_factor_matrix)
        core_extra = lax.ppermute(extra, "dp", other_core)
        joined = span + extra_rows - 3 * ROWS
        chip, inputs = pl.pallas_call(
            join_kernel,
            out_shape=[
                jax.ShapeDtypeStruct((joined, width), jnp.bfloat16),
                jax.ShapeDtypeStruct((ROWS, width), jnp.float32),
            ],
            in_specs=[vmem_spec()] * 4,
            out_specs=[vmem_spec()] * 2,
            compiler_params=modest,
            name="join",
        )(own1, core1, extra, core_extra)
        far = lax.ppermute(chip, "dp", other_y)
        turned, _ = lax.optimization_barrier((turned, chip))
        core0 = lax.ppermute(narrow(product(turned, 1, 0)), "dp", other_core)
        own0 = narrow(product(turned, 0, 0))
        return own0, core0, far, chip, inputs, member

    first = project(0, FIRST)
    later, _ = lax.optimization_barrier((ids, first[0]))
    many = jnp.sum((later != 0).astype(jnp.int32)) > FIRST
    left = tokens - FIRST
    shapes = jax.eval_shape(lambda: project(FIRST, left))
    rest = lax.cond(
        many,
        lambda: project(FIRST, left),
        lambda: tuple(jnp.zeros(x.shape, x.dtype) for x in shapes),
    )
    sent, misc = pl.pallas_call(
        functools.partial(pool_kernel, model_width=float(features * shards)),
        out_shape=[
            jax.ShapeDtypeStruct(((texts + 1) * ROWS, width), jnp.bfloat16),
            jax.ShapeDtypeStruct((ROWS, width), jnp.float32),
        ],
        in_specs=[vmem_spec()] * 14,
        out_specs=[vmem_spec()] * 2,
        scratch_shapes=[
            pltpu.VMEM((LANES, width), jnp.bfloat16),
            pltpu.VMEM((ROWS, width), jnp.float32),
            pltpu.VMEM((texts * ROWS, width), jnp.float32),
        ],
        compiler_params=modest,
        name="pool",
    )(ids, *first, *rest, raising_factor_matrix)
    far_side = lax.ppermute(sent, "group", [(0, 1), (1, 0)])
    rows = 2 * ROWS
    packed, slopes = pl.pallas_call(
        dots_kernel,
        out_shape=[
            jax.ShapeDtypeStruct((rows + width // LANES * rows, LANES), jnp.float32),
            jax.ShapeDtypeStruct((2 * texts * ROWS, width), jnp.bfloat16),
        ],
        in_specs=[vmem_spec()] * 2,
        out_specs=[vmem_spec()] * 2,
        compiler_params=modest,
        name="dots",
    )(sent, far_side)
    packed = exchange(packed, "dp", shards)
    dots = [x[0:rows] for x in packed]
    dots = (dots[0] + dots[1]) + (dots[2] + dots[3])
    slopes, dots = lax.optimization_barrier((slopes, dots))
    dots = exchange(dots, "mp", parts)
    slopes = [slopes, lax.ppermute(slopes, "dp", other_y)]
    embeddings, losses, update = pl.pallas_call(
        functools.partial(
            score_kernel, texts=texts, stripes=pl.cdiv(FIRST, STRIPE), negatives=negatives
        ),
        out_shape=[
            jax.ShapeDtypeStruct((1, per_shard, part_width), jnp.bfloat16),
            jax.ShapeDtypeStruct((1, per_shard), jnp.float32),
            jax.ShapeDtypeStruct((ROWS, part_width // 2), jnp.float32),
        ],
        in_specs=[vmem_spec()] * 11 + [smem_spec()],
        out_specs=[vmem_spec()] * 3,
        compiler_params=modest,
        name="score",
    )(*packed, *slopes, *dots, misc, logit_sharpness)
    other = lax.ppermute(update, "dp", other_core)
    core = lax.rem(lax.axis_index("dp"), 2)
    halves = [jnp.where(core == 0, update, other), jnp.where(core == 0, other, update)]
    return (embeddings, losses, jnp.concatenate(halves, axis=1))


def body(words, hard, vocabulary, weight, lowering, raising, sharpness):
    shards, parts = lax.axis_size("dp"), lax.axis_size("mp")
    texts, length = words.shape[1:]
    features, vocab = vocabulary.shape
    negatives = hard.shape[1]
    square = shards == 4 and features == weight.shape[1] == 4 * STRIPE and parts == shards
    small = texts <= ROWS - 2 and length == LANES and FIRST < texts * length <= 2048
    even = (texts * length - FIRST) % CHUNK == 0 and vocab % IDS_PER_BLOCK == 0
    fits = features * vocab <= 2**24 and features % (4 * LANES) == 0
    spare = pl.cdiv(FIRST, STRIPE) + negatives <= ROWS and lowering.shape[0] == ROWS
    fast = square and small and even and fits and spare and lax.axis_size("group") == 2
    chosen = split_body if fast else general_body
    return chosen(words, hard, vocabulary, weight, lowering, raising, sharpness)


def solution(mesh):
    in_specs = (
        P("group", None, None),
        P("dp", None),
        P("dp", None),
        P("dp", "mp"),
        P(),
        P(None, "mp"),
        P(),
    )
    out_specs = (P("group", "dp", "mp"), P("group", "dp"), P(None, "mp"))
    return jax.shard_map(body, mesh=mesh, in_specs=in_specs, out_specs=out_specs, check_vma=False)
```

```python
import functools

import jax
import jax.numpy as jnp
from jax import lax
from jax.experimental import pallas as pl
from jax.experimental.pallas import tpu as pltpu
from jax.sharding import PartitionSpec as P


def general_body(
    query_passage_words,
    difficult_distractors,
    vocabulary_vectors,
    layer_weight_matrix,
    lowering_factor_matrix,
    raising_factor_matrix,
    logit_sharpness,
):
    group_index = lax.axis_index("group")
    shard_index = lax.axis_index("dp")
    part_index = lax.axis_index("mp")
    shard_count = lax.axis_size("dp")
    side_ids = query_passage_words[0]
    text_count = side_ids.shape[0]
    length = side_ids.shape[1]
    per_shard = text_count // shard_count
    own_ids = lax.dynamic_slice_in_dim(side_ids, shard_index * per_shard, per_shard, 0)
    columns = jnp.take(vocabulary_vectors, side_ids.reshape(-1), axis=1)
    inputs = lax.all_to_all(columns, "dp", split_axis=1, concat_axis=0, tiled=True)
    tokens = inputs.shape[1]
    feature_width = raising_factor_matrix.shape[1]
    wide_inputs = inputs.astype(jnp.float32)
    inverse = lax.rsqrt(jnp.mean(wide_inputs * wide_inputs, axis=0) + 1e-05)
    normed_state = (wide_inputs * inverse[None, :]).astype(jnp.bfloat16)
    linear_map = lax.dot_general(
        lax.all_gather(layer_weight_matrix, "dp", axis=0, tiled=True),
        normed_state,
        (((0,), (0,)), ((), ())),
        preferred_element_type=jnp.float32,
    )
    reduced_sum = jnp.dot(
        lowering_factor_matrix, normed_state, preferred_element_type=jnp.float32
    ).astype(jnp.bfloat16)
    linear_map = linear_map + lax.dot_general(
        raising_factor_matrix,
        reduced_sum,
        (((0,), (0,)), ((), ())),
        preferred_element_type=jnp.float32,
    )
    own_inputs = lax.dynamic_slice_in_dim(
        inputs, part_index * feature_width, feature_width, 0
    ).astype(jnp.float32)
    hidden_state = own_inputs + jax.nn.silu(linear_map)
    mask = (own_ids != 0).astype(jnp.float32)
    counts = jnp.sum(mask, axis=1)
    summed = jnp.einsum("dnl,nl->nd", hidden_state.reshape(feature_width, per_shard, length), mask)
    pooled = (summed / counts[:, None]).astype(jnp.bfloat16)
    gathered = lax.all_gather(pooled, ("group", "dp"), axis=0, tiled=True)
    part_scores = lax.dot_general(
        pooled, gathered, (((1,), (1,)), ((), ())), preferred_element_type=jnp.float32
    )
    gathered_wide = gathered.astype(jnp.float32)
    part_norms = jnp.sum(gathered_wide * gathered_wide, axis=1)
    dots, norms = lax.psum((part_scores, part_norms), "mp")
    rnorm_all = lax.rsqrt(norms + 1e-06)
    all_count = gathered.shape[0]
    half_count = all_count // 2
    own_rows = (
        group_index * half_count + shard_index * per_shard + jnp.arange(per_shard, dtype=jnp.int32)
    )
    rnorm_own = jnp.take(rnorm_all, own_rows)
    cosine = dots * rnorm_own[:, None] * rnorm_all[None, :]
    multiplier_factor = logit_sharpness[0]
    scores = multiplier_factor * cosine
    column_ids = jnp.arange(all_count, dtype=jnp.int32)
    keep = column_ids[None, :] != own_rows[:, None]
    pair = (own_rows + half_count) % all_count
    weight = (group_index == 0).astype(jnp.float32)
    neg_cols = half_count + difficult_distractors
    top = jnp.max(jnp.where(keep, scores, -jnp.inf), axis=1)
    safe_scores = jnp.where(keep, scores, top[:, None])
    expd = jnp.where(keep, jnp.exp(safe_scores - top[:, None]), 0.0)
    neg_exp = (
        jnp.exp(jnp.minimum(jnp.take_along_axis(scores, neg_cols, axis=1) - top[:, None], 0.0))
        * weight
    )
    total = jnp.sum(expd, axis=1) + jnp.sum(neg_exp, axis=1)
    pair_score = jnp.take_along_axis(scores, pair[:, None], axis=1)[:, 0]
    losses = top + jnp.log(total) - pair_score
    onehot = (column_ids[None, None, :] == neg_cols[:, :, None]).astype(jnp.float32)
    probs = (expd + jnp.einsum("rk,rkc->rc", neg_exp, onehot)) / total[:, None]
    target = (column_ids[None, :] == pair[:, None]).astype(jnp.float32)
    grad_scores = (probs - target) / all_count
    coeff = (grad_scores * rnorm_own[:, None] * rnorm_all[None, :]).astype(jnp.bfloat16)
    along = jnp.dot(coeff, gathered, preferred_element_type=jnp.float32)
    pooled_wide = pooled.astype(jnp.float32)
    radial = jnp.sum(grad_scores * cosine, axis=1) * rnorm_own * rnorm_own
    embedding_gradient = multiplier_factor * (along - radial[:, None] * pooled_wide)
    token_grad = jnp.einsum("nd,nl->dnl", embedding_gradient / counts[:, None], mask).reshape(
        feature_width, tokens
    )
    sigma = jax.nn.sigmoid(linear_map)
    local = (token_grad * sigma * (1.0 + linear_map * (1.0 - sigma))).astype(jnp.bfloat16)
    up_portion = lax.dot_general(
        reduced_sum, local, (((1,), (1,)), ((), ())), preferred_element_type=jnp.float32
    )
    adapter_up_gradient = lax.psum(up_portion, ("group", "dp"))
    embeddings = (pooled_wide * rnorm_own[:, None]).astype(jnp.bfloat16)[None]
    return (embeddings, losses[None], adapter_up_gradient)


BLOCK_BITS, GROUP_BITS, LANE_BITS, ROW_BITS = 10, 9, 7, 4
IDS_PER_BLOCK = 1 << BLOCK_BITS
IDS_PER_GROUP = 1 << GROUP_BITS
CHUNK = 384
STRIPE = 256
ROWS = 1 << ROW_BITS
LANES = 1 << LANE_BITS
FEATURE_ROWS = 128
FIRST = 1152
TAKEN = 768
NT = (((1,), (1,)), ((), ()))
LARGE_VMEM, MODEST_VMEM = 44 * 1024 * 1024, 15 * 1024 * 1024


def mm(a, b, dims=(((1,), (0,)), ((), ()))):
    return lax.dot_general(a, b, dims, preferred_element_type=jnp.float32)


def split(x):
    high = x.astype(jnp.bfloat16)
    return high, (x - high.astype(jnp.float32)).astype(jnp.bfloat16)


def iota(shape, dim):
    return lax.broadcasted_iota(jnp.int32, shape, dim)


def quarter_of(dp_index, cores=2):
    return (dp_index % cores) * 2 + dp_index // cores


def split_quarter(i, j, cores=2):
    shard = lax.axis_index("dp")
    core, side_y = lax.rem(shard, cores), lax.div(shard, cores)
    return (core ^ i) * 2 + (side_y ^ j)


def take_lanes(x, lanes):
    numbers = lax.GatherDimensionNumbers(
        offset_dims=(),
        collapsed_slice_dims=(1,),
        start_index_map=(1,),
        operand_batching_dims=(0,),
        start_indices_batching_dims=(0,),
    )
    mode = lax.GatherScatterMode.PROMISE_IN_BOUNDS
    return lax.gather(x, lanes[..., None], numbers, slice_sizes=(1, 1), mode=mode)


def fetch(pairs, sems):
    copies = [pltpu.make_async_copy(a, b, sems.at[n]) for n, (a, b) in enumerate(pairs)]
    for copy in copies:
        copy.start()
    for copy in copies:
        copy.wait()


def gather_kernel(
    ids_ref,
    vocab_ref,
    turned_any,
    member_any,
    count_ref,
    turned,
    member_ref,
    held,
    token_ref,
    ranks,
    counted,
    bounds,
    held_sems,
    bounds_sem,
    out_sems,
    base,
):
    texts, length = ids_ref.shape
    features, vocab = vocab_ref.shape
    blocks = vocab // IDS_PER_BLOCK
    groups = vocab // IDS_PER_GROUP
    span = member_ref.shape[0]

    def vocab_copy(b):
        columns = pl.ds(pl.multiple_of(b * IDS_PER_BLOCK, LANES), IDS_PER_BLOCK)
        return pltpu.make_async_copy(vocab_ref.at[:, columns], held.at[b], held_sems.at[b])

    vocab_copy(0).start()
    for b in range(1, blocks):
        vocab_copy(b).start()

    ids = ids_ref[...]
    valid = ids != 0
    group_of = jnp.where(valid, lax.shift_right_logical(ids, GROUP_BITS), groups)
    group_rows = counted.shape[0]
    group_id = iota((group_rows, length), 0)
    below = jnp.zeros((group_rows, length), jnp.float32)
    for text in range(texts):
        below += jnp.where(group_of[text : text + 1] < group_id, 1.0, 0.0)
    before = jnp.broadcast_to(jnp.sum(below, axis=1, keepdims=True), (group_rows, length))
    counted[...] = before.astype(jnp.int32)
    bounds_copy = pltpu.make_async_copy(counted, bounds, bounds_sem)
    bounds_copy.start()
    earlier = jnp.where(iota((length, length), 0) < iota((length, length), 1), 1.0, 0.0).astype(
        jnp.bfloat16
    )
    for text in range(texts):
        here = jnp.where(group_of[text : text + 1] == group_id, 1.0, 0.0)
        inside = mm(here.astype(jnp.bfloat16), earlier)
        ranks[pl.ds(text, 1), :] = jnp.sum(here * (inside + before), axis=0, keepdims=True)
        before += jnp.broadcast_to(jnp.sum(here, axis=1, keepdims=True), (group_rows, length))
    text_of = iota((texts, length), 0)
    carried = jnp.where(valid, lax.shift_left(ids, ROW_BITS) + text_of, 0).astype(jnp.float32)
    rank = ranks[...]

    def place(p, carry):
        position = (iota((LANES, length), 0) + (p * LANES + base)).astype(jnp.float32)
        total = jnp.zeros((LANES, length), jnp.float32)
        for text in range(texts):
            total += jnp.where(rank[text : text + 1] == position, carried[text : text + 1], 0.0)
        found = jnp.broadcast_to(jnp.sum(total, axis=1, keepdims=True), (LANES, LANES))
        start = pl.multiple_of(p * LANES, LANES)
        row = found.T[0:1].astype(jnp.int32)
        token = lax.shift_right_logical(row, ROW_BITS)
        token_ref[pl.ds(p, 1), :] = jnp.where(token == 0, -vocab, token)
        found = found.astype(jnp.int32)
        real = (found >= ROWS) & ((found & (ROWS - 1)) == iota((LANES, LANES), 1))
        member_ref[pl.ds(start, LANES), :] = jnp.where(real, 1.0, 0.0).astype(jnp.bfloat16)
        turned[:, pl.ds(start, LANES)] = jnp.zeros((features, LANES), jnp.bfloat16)
        return carry

    lax.fori_loop(0, span // LANES, place, 0)
    bounds_copy.wait()
    count_ref[0] = bounds[groups, 0]

    def within(place):
        return jnp.clip(place - base, 0, span)

    def take(b, carry):
        vocab_copy(b).wait()
        for part in range(IDS_PER_BLOCK // IDS_PER_GROUP):
            group = b * (IDS_PER_BLOCK // IDS_PER_GROUP) + part
            first, last = within(bounds[group, 0]), within(bounds[group + 1, 0])
            begin = lax.shift_right_logical(first, LANE_BITS)
            end = lax.shift_right_logical(last + LANES - 1, LANE_BITS)

            def window(p, carry):
                at = pl.ds(pl.multiple_of(p * LANES, LANES), LANES)
                token = token_ref[pl.ds(p, 1), :] - group * IDS_PER_GROUP
                token = jnp.broadcast_to(token, (FEATURE_ROWS, LANES))
                lane = (token & (LANES - 1)).astype(jnp.int16)
                tile = lax.shift_right_arithmetic(token, LANE_BITS).astype(jnp.int16)
                pieces = [pl.ds(f, FEATURE_ROWS) for f in range(0, TAKEN, FEATURE_ROWS)]
                short = jnp.broadcast_to(token[0:1], (IDS_PER_GROUP, LANES)).astype(jnp.int16)
                picked = jnp.where(
                    short == iota((IDS_PER_GROUP, LANES), 0).astype(jnp.int16), 1.0, 0.0
                ).astype(jnp.bfloat16)
                columns = pl.ds(part * IDS_PER_GROUP, IDS_PER_GROUP)
                rest = pl.ds(TAKEN, features - TAKEN)
                product = mm(held[b, rest, columns], picked).astype(jnp.bfloat16)
                fresh = []
                for rows in pieces:
                    total = jnp.zeros((FEATURE_ROWS, LANES), jnp.bfloat16)
                    for j in range(IDS_PER_GROUP // LANES):
                        columns = pl.ds(part * IDS_PER_GROUP + j * LANES, LANES)
                        total = jnp.where(tile == j, take_lanes(held[b, rows, columns], lane), total)
                    fresh.append(total)
                pieces.append(rest)
                fresh.append(product)
                fresh = [turned[rows, at] + total for rows, total in zip(pieces, fresh)]
                for rows, total in zip(pieces, fresh):
                    turned[rows, at] = total
                return carry

            lax.fori_loop(begin, jnp.where(last > first, end, begin), window, 0)
        return carry

    lax.fori_loop(0, blocks, take, 0)
    fetch([(turned, turned_any), (member_ref, member_any)], out_sems)


def statistics_kernel(
    turned_any, member_any, hard_ref, lower_ref, extra_ref, small, turned, member_ref, spread, sems
):
    fetch([(turned_any, turned), (member_any, member_ref)], sems)
    features, span = turned.shape
    stripes = pl.cdiv(span, STRIPE)
    per_shard, negatives = hard_ref.shape
    shard = lax.axis_index("dp")
    small[...] = jnp.zeros_like(small)
    small[0:per_shard, stripes : stripes + negatives] = hard_ref[...].astype(jnp.float32)
    lower = lower_ref[:, pl.ds(pl.multiple_of(shard * features, LANES), features)]

    misc = jnp.zeros((ROWS, STRIPE), jnp.float32)
    residual = jnp.zeros((features, LANES), jnp.float32)
    for stripe in range(stripes):
        size = min(STRIPE, span - stripe * STRIPE)
        across = pl.ds(stripe * STRIPE, size)
        upright = turned[:, across]
        wide = upright.astype(jnp.float32)
        square = jnp.sum(wide * wide, axis=0, keepdims=True)
        reduced = mm(lower, upright)
        if size < STRIPE:
            none = jnp.zeros((ROWS, STRIPE - size), jnp.float32)
            reduced = jnp.concatenate([reduced, none], axis=1)
            square = jnp.concatenate([square, none[0:1]], axis=1)
        extra_ref[stripe * ROWS : (stripe + 1) * ROWS, :] = reduced.astype(jnp.bfloat16)
        misc = jnp.where(iota((ROWS, STRIPE), 0) == stripe, square, misc)
        residual += mm(upright, member_ref[across, :])
    hard = small[...].T[0:ROWS]
    for i in range(per_shard):
        misc += jnp.where(iota((ROWS, STRIPE), 1) == shard * per_shard + i, hard[:, i : i + 1], 0.0)
    extra_ref[stripes * ROWS : (stripes + 1) * ROWS, :] = misc.astype(jnp.bfloat16)
    residual = jnp.where(lax.axis_index("mp") == shard, residual.T[0:ROWS], 0.0)
    spread[...] = residual
    for q in range(4):
        start = (stripes + 1 + q) * ROWS
        quarter = pl.multiple_of(split_quarter(q // 2, q % 2) * STRIPE, LANES)
        extra_ref[start : start + ROWS, :] = spread[:, pl.ds(quarter, STRIPE)].astype(jnp.bfloat16)


def pool_kernel(
    ids_ref,
    own_ref,
    core_any,
    far_any,
    extra_ref,
    member_ref,
    own_rest,
    core_rest,
    far_rest,
    extra_rest,
    member_rest,
    raise_ref,
    sent_ref,
    misc_ref,
    raised,
    total,
    slopes,
    core_ref,
    far_ref,
    sems,
    model_width,
):
    texts, length = ids_ref.shape
    width = own_ref.shape[1]
    quarter = quarter_of(lax.axis_index("dp"))
    fetch([(core_any, core_ref), (far_any, far_ref)], sems)
    raised[...] = jnp.zeros_like(raised)
    raised[0:ROWS, :] = raise_ref[:, pl.ds(pl.multiple_of(quarter * width, LANES), width)]
    total[...] = jnp.zeros_like(total)
    slopes[...] = jnp.zeros_like(slopes)

    def add(refs, extra_ref, member_ref, base):
        span = member_ref.shape[0]
        stripes = pl.cdiv(span, STRIPE)

        def summed(start, size):
            return sum(ref[pl.ds(start, size), :].astype(jnp.float32) for ref in refs)

        misc = extra_ref[stripes * ROWS : (stripes + 1) * ROWS, :]
        if base == 0:
            misc_ref[...] = misc
        inverse = lax.rsqrt(misc / model_width + 1e-05)
        for k in range(stripes):
            size = min(STRIPE, span - k * STRIPE)
            scale = inverse[k : k + 1]
            reduced = (extra_ref[k * ROWS : (k + 1) * ROWS, :] * scale).astype(jnp.bfloat16)
            reduced = reduced.astype(jnp.float32)
            stacked = jnp.concatenate([reduced, jnp.broadcast_to(scale, (LANES - ROWS, STRIPE))])
            turned = stacked[:, 0:size].T
            low = turned.astype(jnp.bfloat16)
            linear = summed(k * STRIPE, size)
            linear = linear * turned[:, ROWS : ROWS + 1] + mm(low, raised[...])
            sigma = 1.0 / (1.0 + jnp.exp(-linear))
            slope = (sigma * (1.0 + linear * (1.0 - sigma))).astype(jnp.bfloat16)
            member = member_ref[pl.ds(k * STRIPE, size), :].astype(jnp.float32).T
            high, rest = split(linear * sigma)
            chosen = member[0:ROWS].astype(jnp.bfloat16)
            total[...] += mm(chosen, high) + mm(chosen, rest)
            spread = [reduced[:, 0:size] * member[text : text + 1] for text in range(texts)]
            slopes[...] += mm(jnp.concatenate(spread).astype(jnp.bfloat16), slope)
        total[...] += extra_ref[(stripes + 1) * ROWS : (stripes + 2) * ROWS, :]

    add((own_ref, core_ref, far_ref), extra_ref, member_ref, 0)
    real = (ids_ref[...] != 0).astype(jnp.float32)

    @pl.when(jnp.sum(real) > member_ref.shape[0])
    def _():
        add((own_rest, core_rest, far_rest), extra_rest, member_rest, member_ref.shape[0])

    counts = jnp.sum(real, axis=1, keepdims=True)
    pooled = total[0:texts] / counts
    pooled = jnp.concatenate([pooled, jnp.zeros((ROWS - texts, width), jnp.float32)])
    sent_ref[0:ROWS, :] = pooled.astype(jnp.bfloat16)
    for text in range(texts):
        part = slopes[text * ROWS : (text + 1) * ROWS, :] / counts[text : text + 1]
        sent_ref[(text + 1) * ROWS : (text + 2) * ROWS, :] = part.astype(jnp.bfloat16)


def both_sides(near, far):
    queries = lax.axis_index("group") == 0
    return jnp.concatenate([jnp.where(queries, near, far), jnp.where(queries, far, near)], axis=0)


def dots_kernel(near_ref, far_ref, packed_ref, slopes_ref):
    block = both_sides(near_ref[0:ROWS], far_ref[0:ROWS])
    rows = 2 * ROWS
    packed_ref[...] = jnp.zeros_like(packed_ref)
    packed_ref[0:rows, 0:rows] = mm(block, block, NT)
    for part in range(block.shape[1] // LANES):
        piece = block[:, part * LANES : (part + 1) * LANES]
        packed_ref[rows + part * rows : rows + (part + 1) * rows, :] = piece.astype(jnp.float32)
    size = near_ref.shape[0] - ROWS
    slopes_ref[0:size] = near_ref[ROWS:]
    slopes_ref[size:] = far_ref[ROWS:]


def score_kernel(*refs, texts, stripes, negatives):
    packed0, packed1, packed2, packed3, slopes0, slopes2 = refs[0:6]
    dots0, dots1, dots2, dots3, misc_ref, sharp_ref = refs[6:12]
    embed_ref, loss_ref, up_ref = refs[12:15]
    rows = 2 * ROWS
    per_shard = loss_ref.shape[1]
    group, shard = lax.axis_index("group"), lax.axis_index("dp")
    dots = ((dots0[...] + dots1[...]) + (dots2[...] + dots3[...]))[:, 0:rows]
    down, across = iota((rows, rows), 0), iota((rows, rows), 1)
    same = down == across
    real = (lax.rem(down, ROWS) < texts) & (lax.rem(across, ROWS) < texts)
    diagonal = jnp.where(same, dots, 0.0)
    rnorm_row = lax.rsqrt(jnp.sum(diagonal, axis=0, keepdims=True) + 1e-06)
    rnorm_col = lax.rsqrt(jnp.sum(diagonal, axis=1, keepdims=True) + 1e-06)
    sharpness = sharp_ref[0]
    cosine = dots * rnorm_col * rnorm_row
    scores = sharpness * cosine
    keep = real & ~same
    top = jnp.max(jnp.where(keep, scores, -jnp.inf), axis=0, keepdims=True)
    top = jnp.where(lax.rem(across[0:1], ROWS) < texts, top, 0.0)
    powers = jnp.exp(jnp.where(real, jnp.minimum(scores - top, 0.0), 0.0))
    hard = misc_ref[stripes : stripes + negatives, 0:rows].astype(jnp.int32) + ROWS
    times = jnp.zeros((rows, rows), jnp.float32)
    for k in range(negatives):
        times += jnp.where(hard[k : k + 1] == down, 1.0, 0.0)
    times = jnp.where(across < texts, times, 0.0)
    weights = (jnp.where(keep, 1.0, 0.0) + jnp.where(real, times, 0.0)) * powers
    total = jnp.sum(weights, axis=0, keepdims=True)
    total = jnp.where(lax.rem(across[0:1], ROWS) < texts, total, 1.0)
    pair = (down == lax.rem(across + ROWS, rows)) & real
    pair_score = jnp.sum(jnp.where(pair, scores, 0.0), axis=0, keepdims=True)
    losses = top + jnp.log(total) - pair_score
    grad_scores = (weights / total - jnp.where(pair, 1.0, 0.0)) / (2 * texts)
    coeff = (grad_scores * rnorm_col * rnorm_row).astype(jnp.bfloat16)
    radial = jnp.sum(grad_scores * cosine, axis=0, keepdims=True) * rnorm_row * rnorm_row

    first = shard * per_shard
    loss_col = jnp.sum(jnp.where(same, losses, 0.0), axis=1, keepdims=True)
    at = (iota((rows, LANES), 0) == group * ROWS + first + iota((rows, LANES), 1)) & (
        iota((rows, LANES), 1) < per_shard
    )
    loss_ref[...] = jnp.sum(jnp.where(at, loss_col, 0.0), axis=0, keepdims=True)[:, 0:per_shard]

    along_rows = coeff.astype(jnp.float32).T.astype(jnp.bfloat16)
    radial_col = jnp.sum(jnp.where(same, radial, 0.0), axis=1, keepdims=True)
    rnorm_own = jnp.where(group == 0, rnorm_col[0:ROWS], rnorm_col[ROWS:rows])
    chosen = iota((ROWS, ROWS), 1) == iota((ROWS, ROWS), 0) + first
    chosen = jnp.where(chosen & (iota((ROWS, ROWS), 0) < per_shard), 1.0, 0.0).astype(jnp.bfloat16)
    blocks = ((packed0, slopes0), (packed1, None), (packed2, slopes2), (packed3, None))
    for o, (packed, slopes) in enumerate(blocks):
        parts = packed.shape[0] // rows - 1
        width = parts * LANES
        halves = [packed[rows * (part + 1) : rows * (part + 2), :] for part in range(parts)]
        block = jnp.concatenate(halves, axis=1)
        queries = group == 0
        at = pl.multiple_of(quarter_of(shard ^ o) * width, LANES)
        own = jnp.where(queries, block[0:ROWS], block[ROWS:rows]) * rnorm_own
        picked = mm(chosen, own.astype(jnp.bfloat16)).astype(jnp.bfloat16)
        embed_ref[0, :, pl.ds(at, width)] = picked[0:per_shard]
        if slopes is None:
            continue
        along = mm(along_rows, block.astype(jnp.bfloat16))
        grad = sharpness * (along - radial_col * block)
        near, far = slopes[0 : slopes.shape[0] // 2], slopes[slopes.shape[0] // 2 :]
        grad_near = jnp.where(queries, grad[0:ROWS], grad[ROWS:rows])
        grad_far = jnp.where(queries, grad[ROWS:rows], grad[0:ROWS])
        update = []
        for side, side_grad in ((near, grad_near), (far, grad_far)):
            total = jnp.zeros((ROWS, width), jnp.float32)
            for text in range(texts):
                slope = side[text * ROWS : (text + 1) * ROWS].astype(jnp.float32)
                total += side_grad[text : text + 1] * slope
            update.append(total)
        at = pl.multiple_of((lax.div(shard, 2) ^ (o // 2)) * width, LANES)
        up_ref[:, pl.ds(at, width)] = update[0] + update[1]


def any_spec():
    return pl.BlockSpec(memory_space=pl.ANY)


def vmem_spec():
    return pl.BlockSpec(memory_space=pltpu.VMEM)


def smem_spec():
    return pl.BlockSpec(memory_space=pltpu.SMEM)


def exchange(x, axis, size):
    steps = [[(i, i ^ o) for i in range(size)] for o in range(1, size)]
    return [x] + [lax.ppermute(x, axis, step) for step in steps]


def split_body(
    query_passage_words,
    difficult_distractors,
    vocabulary_vectors,
    layer_weight_matrix,
    lowering_factor_matrix,
    raising_factor_matrix,
    logit_sharpness,
):
    shards, parts = lax.axis_size("dp"), lax.axis_size("mp")
    ids = query_passage_words[0]
    texts, length = ids.shape
    tokens = texts * length
    features, vocab = vocabulary_vectors.shape
    blocks = vocab // IDS_PER_BLOCK
    group_rows = 8 * pl.cdiv(vocab // IDS_PER_GROUP + 1, 8)
    per_shard, negatives = difficult_distractors.shape
    part_width = layer_weight_matrix.shape[1]
    width = part_width // shards
    params = pltpu.CompilerParams(vmem_limit_bytes=LARGE_VMEM)
    modest = pltpu.CompilerParams(vmem_limit_bytes=MODEST_VMEM)
    other_core = [(d, d ^ 1) for d in range(shards)]
    other_y = [(d, d ^ 2) for d in range(shards)]

    def columns(i, j):
        start = split_quarter(i, j) * width
        return lax.dynamic_slice(layer_weight_matrix, (0, start), (features, width))

    def project(base, span):
        stripes = pl.cdiv(span, STRIPE)
        extra_rows = (stripes + 1 + shards) * ROWS
        turned, member, count = pl.pallas_call(
            functools.partial(gather_kernel, base=base),
            out_shape=[
                jax.ShapeDtypeStruct((features, span), jnp.bfloat16),
                jax.ShapeDtypeStruct((span, LANES), jnp.bfloat16),
                jax.ShapeDtypeStruct((1,), jnp.int32),
            ],
            in_specs=[vmem_spec(), any_spec()],
            out_specs=[any_spec()] * 2 + [smem_spec()],
            scratch_shapes=[
                pltpu.VMEM((features, span), jnp.bfloat16),
                pltpu.VMEM((span, LANES), jnp.bfloat16),
                pltpu.VMEM((blocks, features, IDS_PER_BLOCK), jnp.bfloat16),
                pltpu.VMEM((8 * pl.cdiv(span // LANES, 8), LANES), jnp.int32),
                pltpu.VMEM((texts, length), jnp.float32),
                pltpu.VMEM((group_rows, length), jnp.int32),
                pltpu.SMEM((group_rows, length), jnp.int32),
                pltpu.SemaphoreType.DMA((blocks,)),
                pltpu.SemaphoreType.DMA,
                pltpu.SemaphoreType.DMA((2,)),
            ],
            compiler_params=params,
            name="gather",
        )(ids, vocabulary_vectors)

        def product(turned, i, j):
            return mm(turned, columns(i, j), (((0,), (0,)), ((), ())))

        def narrow(x):
            return x.astype(jnp.bfloat16)

        core1 = lax.ppermute(narrow(product(turned, 1, 1)), "dp", other_core)
        own1 = lax.optimization_barrier(narrow(product(turned, 0, 1)))
        chip1 = narrow(own1.astype(jnp.float32) + core1.astype(jnp.float32))
        far = lax.ppermute(chip1, "dp", other_y)
        turned, _ = lax.optimization_barrier((turned, chip1))
        extra = pl.pallas_call(
            statistics_kernel,
            out_shape=jax.ShapeDtypeStruct((extra_rows, STRIPE), jnp.bfloat16),
            in_specs=[any_spec()] * 2 + [vmem_spec()] * 2,
            out_specs=vmem_spec(),
            scratch_shapes=[
                pltpu.VMEM((LANES, LANES), jnp.float32),
                pltpu.VMEM(turned.shape, turned.dtype),
                pltpu.VMEM(member.shape, member.dtype),
                pltpu.VMEM((ROWS, features), jnp.float32),
                pltpu.SemaphoreType.DMA((2,)),
            ],
            compiler_params=modest,
            cost_estimate=pl.CostEstimate(
                flops=2 * features * span * (ROWS + LANES),
                bytes_accessed=2 * features * span,
                transcendentals=0,
            ),
            name="statistics",
        )(turned, member, difficult_distractors, lowering_factor_matrix)
        common = (stripes + 1) * ROWS
        near = extra.astype(jnp.float32)
        across = lax.ppermute(extra, "dp", other_core).astype(jnp.float32)
        chip = near[0:common] + across[0:common]
        inputs = near[common : common + 2 * ROWS] + across[common + 2 * ROWS :]
        sent = narrow(jnp.concatenate([chip, inputs[ROWS:]]))
        sent = lax.ppermute(sent, "dp", other_y).astype(jnp.float32)
        extra = jnp.concatenate([chip, inputs[0:ROWS]]) + sent
        core0 = lax.ppermute(narrow(product(turned, 1, 0)), "dp", other_core)
        own0 = narrow(product(turned, 0, 0))
        return (own0, core0, far, extra, member), count

    first, count = project(0, FIRST)
    many = count[0] > FIRST
    left = tokens - FIRST
    shapes = jax.eval_shape(lambda: project(FIRST, left)[0])
    rest = lax.cond(
        many,
        lambda: project(FIRST, left)[0],
        lambda: tuple(jnp.zeros(x.shape, x.dtype) for x in shapes),
    )
    sent, misc = pl.pallas_call(
        functools.partial(pool_kernel, model_width=float(features * shards)),
        out_shape=[
            jax.ShapeDtypeStruct(((texts + 1) * ROWS, width), jnp.bfloat16),
            jax.ShapeDtypeStruct((ROWS, width), jnp.float32),
        ],
        in_specs=[vmem_spec()] * 2 + [any_spec()] * 2 + [vmem_spec()] * 8,
        out_specs=[vmem_spec()] * 2,
        scratch_shapes=[
            pltpu.VMEM((LANES, width), jnp.bfloat16),
            pltpu.VMEM((ROWS, width), jnp.float32),
            pltpu.VMEM((texts * ROWS, width), jnp.float32),
            pltpu.VMEM((FIRST, width), jnp.bfloat16),
            pltpu.VMEM((FIRST, width), jnp.bfloat16),
            pltpu.SemaphoreType.DMA((2,)),
        ],
        compiler_params=modest,
        name="pool",
    )(ids, *first, *rest, raising_factor_matrix)
    far_side = lax.ppermute(sent, "group", [(0, 1), (1, 0)])
    rows = 2 * ROWS
    packed, slopes = pl.pallas_call(
        dots_kernel,
        out_shape=[
            jax.ShapeDtypeStruct((rows + width // LANES * rows, LANES), jnp.float32),
            jax.ShapeDtypeStruct((2 * texts * ROWS, width), jnp.bfloat16),
        ],
        in_specs=[vmem_spec()] * 2,
        out_specs=[vmem_spec()] * 2,
        compiler_params=modest,
        name="dots",
    )(sent, far_side)
    packed = exchange(packed, "dp", shards)
    dots = [x[0:rows] for x in packed]
    dots = (dots[0] + dots[1]) + (dots[2] + dots[3])
    slopes, dots = lax.optimization_barrier((slopes, dots))
    dots = exchange(dots, "mp", parts)
    slopes = [slopes, lax.ppermute(slopes, "dp", other_y)]
    embeddings, losses, update = pl.pallas_call(
        functools.partial(
            score_kernel, texts=texts, stripes=pl.cdiv(FIRST, STRIPE), negatives=negatives
        ),
        out_shape=[
            jax.ShapeDtypeStruct((1, per_shard, part_width), jnp.bfloat16),
            jax.ShapeDtypeStruct((1, per_shard), jnp.float32),
            jax.ShapeDtypeStruct((ROWS, part_width // 2), jnp.float32),
        ],
        in_specs=[vmem_spec()] * 11 + [smem_spec()],
        out_specs=[vmem_spec()] * 3,
        compiler_params=modest,
        name="score",
    )(*packed, *slopes, *dots, misc, logit_sharpness)
    other = lax.ppermute(update, "dp", other_core)
    core = lax.rem(lax.axis_index("dp"), 2)
    halves = [jnp.where(core == 0, update, other), jnp.where(core == 0, other, update)]
    return (embeddings, losses, jnp.concatenate(halves, axis=1))


def body(words, hard, vocabulary, weight, lowering, raising, sharpness):
    shards, parts = lax.axis_size("dp"), lax.axis_size("mp")
    texts, length = words.shape[1:]
    features, vocab = vocabulary.shape
    negatives = hard.shape[1]
    square = shards == 4 and features == weight.shape[1] == 4 * STRIPE and parts == shards
    small = texts <= ROWS - 2 and length == LANES and FIRST < texts * length <= 2048
    even = (texts * length - FIRST) % CHUNK == 0 and vocab % IDS_PER_BLOCK == 0
    fits = features * vocab <= 2**24 and features % (4 * LANES) == 0
    spare = pl.cdiv(FIRST, STRIPE) + negatives <= ROWS and lowering.shape[0] == ROWS
    fast = square and small and even and fits and spare and lax.axis_size("group") == 2
    chosen = split_body if fast else general_body
    return chosen(words, hard, vocabulary, weight, lowering, raising, sharpness)


def solution(mesh):
    in_specs = (
        P("group", None, None),
        P("dp", None),
        P("dp", None),
        P("dp", "mp"),
        P(),
        P(None, "mp"),
        P(),
    )
    out_specs = (P("group", "dp", "mp"), P("group", "dp"), P(None, "mp"))
    return jax.shard_map(body, mesh=mesh, in_specs=in_specs, out_specs=out_specs, check_vma=False)
```

```python
import functools

import jax
import jax.numpy as jnp
from jax import lax
from jax.experimental import pallas as pl
from jax.experimental.pallas import tpu as pltpu
from jax.sharding import PartitionSpec as P


def general_body(
    query_passage_words,
    difficult_distractors,
    vocabulary_vectors,
    layer_weight_matrix,
    lowering_factor_matrix,
    raising_factor_matrix,
    logit_sharpness,
):
    group_index = lax.axis_index("group")
    shard_index = lax.axis_index("dp")
    part_index = lax.axis_index("mp")
    shard_count = lax.axis_size("dp")
    side_ids = query_passage_words[0]
    text_count = side_ids.shape[0]
    length = side_ids.shape[1]
    per_shard = text_count // shard_count
    own_ids = lax.dynamic_slice_in_dim(side_ids, shard_index * per_shard, per_shard, 0)
    columns = jnp.take(vocabulary_vectors, side_ids.reshape(-1), axis=1)
    inputs = lax.all_to_all(columns, "dp", split_axis=1, concat_axis=0, tiled=True)
    tokens = inputs.shape[1]
    feature_width = raising_factor_matrix.shape[1]
    wide_inputs = inputs.astype(jnp.float32)
    inverse = lax.rsqrt(jnp.mean(wide_inputs * wide_inputs, axis=0) + 1e-05)
    normed_state = (wide_inputs * inverse[None, :]).astype(jnp.bfloat16)
    linear_map = lax.dot_general(
        lax.all_gather(layer_weight_matrix, "dp", axis=0, tiled=True),
        normed_state,
        (((0,), (0,)), ((), ())),
        preferred_element_type=jnp.float32,
    )
    reduced_sum = jnp.dot(
        lowering_factor_matrix, normed_state, preferred_element_type=jnp.float32
    ).astype(jnp.bfloat16)
    linear_map = linear_map + lax.dot_general(
        raising_factor_matrix,
        reduced_sum,
        (((0,), (0,)), ((), ())),
        preferred_element_type=jnp.float32,
    )
    own_inputs = lax.dynamic_slice_in_dim(
        inputs, part_index * feature_width, feature_width, 0
    ).astype(jnp.float32)
    hidden_state = own_inputs + jax.nn.silu(linear_map)
    mask = (own_ids != 0).astype(jnp.float32)
    counts = jnp.sum(mask, axis=1)
    summed = jnp.einsum("dnl,nl->nd", hidden_state.reshape(feature_width, per_shard, length), mask)
    pooled = (summed / counts[:, None]).astype(jnp.bfloat16)
    gathered = lax.all_gather(pooled, ("group", "dp"), axis=0, tiled=True)
    part_scores = lax.dot_general(
        pooled, gathered, (((1,), (1,)), ((), ())), preferred_element_type=jnp.float32
    )
    gathered_wide = gathered.astype(jnp.float32)
    part_norms = jnp.sum(gathered_wide * gathered_wide, axis=1)
    dots, norms = lax.psum((part_scores, part_norms), "mp")
    rnorm_all = lax.rsqrt(norms + 1e-06)
    all_count = gathered.shape[0]
    half_count = all_count // 2
    own_rows = (
        group_index * half_count + shard_index * per_shard + jnp.arange(per_shard, dtype=jnp.int32)
    )
    rnorm_own = jnp.take(rnorm_all, own_rows)
    cosine = dots * rnorm_own[:, None] * rnorm_all[None, :]
    multiplier_factor = logit_sharpness[0]
    scores = multiplier_factor * cosine
    column_ids = jnp.arange(all_count, dtype=jnp.int32)
    keep = column_ids[None, :] != own_rows[:, None]
    pair = (own_rows + half_count) % all_count
    weight = (group_index == 0).astype(jnp.float32)
    neg_cols = half_count + difficult_distractors
    top = jnp.max(jnp.where(keep, scores, -jnp.inf), axis=1)
    safe_scores = jnp.where(keep, scores, top[:, None])
    expd = jnp.where(keep, jnp.exp(safe_scores - top[:, None]), 0.0)
    neg_exp = (
        jnp.exp(jnp.minimum(jnp.take_along_axis(scores, neg_cols, axis=1) - top[:, None], 0.0))
        * weight
    )
    total = jnp.sum(expd, axis=1) + jnp.sum(neg_exp, axis=1)
    pair_score = jnp.take_along_axis(scores, pair[:, None], axis=1)[:, 0]
    losses = top + jnp.log(total) - pair_score
    onehot = (column_ids[None, None, :] == neg_cols[:, :, None]).astype(jnp.float32)
    probs = (expd + jnp.einsum("rk,rkc->rc", neg_exp, onehot)) / total[:, None]
    target = (column_ids[None, :] == pair[:, None]).astype(jnp.float32)
    grad_scores = (probs - target) / all_count
    coeff = (grad_scores * rnorm_own[:, None] * rnorm_all[None, :]).astype(jnp.bfloat16)
    along = jnp.dot(coeff, gathered, preferred_element_type=jnp.float32)
    pooled_wide = pooled.astype(jnp.float32)
    radial = jnp.sum(grad_scores * cosine, axis=1) * rnorm_own * rnorm_own
    embedding_gradient = multiplier_factor * (along - radial[:, None] * pooled_wide)
    token_grad = jnp.einsum("nd,nl->dnl", embedding_gradient / counts[:, None], mask).reshape(
        feature_width, tokens
    )
    sigma = jax.nn.sigmoid(linear_map)
    local = (token_grad * sigma * (1.0 + linear_map * (1.0 - sigma))).astype(jnp.bfloat16)
    up_portion = lax.dot_general(
        reduced_sum, local, (((1,), (1,)), ((), ())), preferred_element_type=jnp.float32
    )
    adapter_up_gradient = lax.psum(up_portion, ("group", "dp"))
    embeddings = (pooled_wide * rnorm_own[:, None]).astype(jnp.bfloat16)[None]
    return (embeddings, losses[None], adapter_up_gradient)


BLOCK_BITS, GROUP_BITS, LANE_BITS, ROW_BITS = 10, 9, 7, 4
IDS_PER_BLOCK = 1 << BLOCK_BITS
IDS_PER_GROUP = 1 << GROUP_BITS
CHUNK = 384
STRIPE = 256
ROWS = 1 << ROW_BITS
LANES = 1 << LANE_BITS
FEATURE_ROWS = 128
FIRST = 1152
TAKEN = 768
NT = (((1,), (1,)), ((), ()))
LARGE_VMEM, MODEST_VMEM = 44 * 1024 * 1024, 15 * 1024 * 1024


def mm(a, b, dims=(((1,), (0,)), ((), ()))):
    return lax.dot_general(a, b, dims, preferred_element_type=jnp.float32)


def split(x):
    high = x.astype(jnp.bfloat16)
    return high, (x - high.astype(jnp.float32)).astype(jnp.bfloat16)


def iota(shape, dim):
    return lax.broadcasted_iota(jnp.int32, shape, dim)


def quarter_of(dp_index, cores=2):
    return (dp_index % cores) * 2 + dp_index // cores


def split_quarter(i, j, cores=2):
    shard = lax.axis_index("dp")
    core, side_y = lax.rem(shard, cores), lax.div(shard, cores)
    return (core ^ i) * 2 + (side_y ^ j)


def take_lanes(x, lanes):
    numbers = lax.GatherDimensionNumbers(
        offset_dims=(),
        collapsed_slice_dims=(1,),
        start_index_map=(1,),
        operand_batching_dims=(0,),
        start_indices_batching_dims=(0,),
    )
    mode = lax.GatherScatterMode.PROMISE_IN_BOUNDS
    return lax.gather(x, lanes[..., None], numbers, slice_sizes=(1, 1), mode=mode)


def fetch(pairs, sems):
    copies = [pltpu.make_async_copy(a, b, sems.at[n]) for n, (a, b) in enumerate(pairs)]
    for copy in copies:
        copy.start()
    for copy in copies:
        copy.wait()


def gather_kernel(
    ids_ref,
    vocab_ref,
    turned_any,
    member_any,
    count_ref,
    turned,
    member_ref,
    held,
    token_ref,
    ranks,
    counted,
    bounds,
    held_sems,
    bounds_sem,
    out_sems,
    base,
):
    texts, length = ids_ref.shape
    features, vocab = vocab_ref.shape
    blocks = vocab // IDS_PER_BLOCK
    groups = vocab // IDS_PER_GROUP
    span = member_ref.shape[0]

    slots = held.shape[0]

    def slot(b):
        return b if slots == blocks else lax.rem(b, slots)

    def vocab_copy(b):
        columns = pl.ds(pl.multiple_of(b * IDS_PER_BLOCK, LANES), IDS_PER_BLOCK)
        return pltpu.make_async_copy(vocab_ref.at[:, columns], held.at[slot(b)], held_sems.at[slot(b)])

    vocab_copy(0).start()
    for b in range(1, slots):
        vocab_copy(b).start()

    ids = ids_ref[...]
    valid = ids != 0
    group_of = jnp.where(valid, lax.shift_right_logical(ids, GROUP_BITS), groups)
    group_rows = counted.shape[0]
    group_id = iota((group_rows, length), 0)
    below = jnp.zeros((group_rows, length), jnp.float32)
    for text in range(texts):
        below += jnp.where(group_of[text : text + 1] < group_id, 1.0, 0.0)
    before = jnp.broadcast_to(jnp.sum(below, axis=1, keepdims=True), (group_rows, length))
    counted[...] = before.astype(jnp.int32)
    bounds_copy = pltpu.make_async_copy(counted, bounds, bounds_sem)
    bounds_copy.start()
    earlier = jnp.where(iota((length, length), 0) < iota((length, length), 1), 1.0, 0.0).astype(
        jnp.bfloat16
    )
    for text in range(texts):
        here = jnp.where(group_of[text : text + 1] == group_id, 1.0, 0.0)
        inside = mm(here.astype(jnp.bfloat16), earlier)
        ranks[pl.ds(text, 1), :] = jnp.sum(here * (inside + before), axis=0, keepdims=True)
        before += jnp.broadcast_to(jnp.sum(here, axis=1, keepdims=True), (group_rows, length))
    text_of = iota((texts, length), 0)
    carried = jnp.where(valid, lax.shift_left(ids, ROW_BITS) + text_of, 0).astype(jnp.float32)
    rank = ranks[...]

    def place(p, carry):
        position = (iota((LANES, length), 0) + (p * LANES + base)).astype(jnp.float32)
        total = jnp.zeros((LANES, length), jnp.float32)
        for text in range(texts):
            total += jnp.where(rank[text : text + 1] == position, carried[text : text + 1], 0.0)
        found = jnp.broadcast_to(jnp.sum(total, axis=1, keepdims=True), (LANES, LANES))
        start = pl.multiple_of(p * LANES, LANES)
        row = found.T[0:1].astype(jnp.int32)
        token = lax.shift_right_logical(row, ROW_BITS)
        token_ref[pl.ds(p, 1), :] = jnp.where(token == 0, -vocab, token)
        found = found.astype(jnp.int32)
        real = (found >= ROWS) & ((found & (ROWS - 1)) == iota((LANES, LANES), 1))
        member_ref[pl.ds(start, LANES), :] = jnp.where(real, 1.0, 0.0).astype(jnp.bfloat16)
        turned[:, pl.ds(start, LANES)] = jnp.zeros((features, LANES), jnp.bfloat16)
        return carry

    lax.fori_loop(0, span // LANES, place, 0)
    bounds_copy.wait()
    count_ref[0] = bounds[groups, 0]

    def within(place):
        return jnp.clip(place - base, 0, span)

    def take(b, carry):
        vocab_copy(b).wait()
        for part in range(IDS_PER_BLOCK // IDS_PER_GROUP):
            group = b * (IDS_PER_BLOCK // IDS_PER_GROUP) + part
            first, last = within(bounds[group, 0]), within(bounds[group + 1, 0])
            begin = lax.shift_right_logical(first, LANE_BITS)
            end = lax.shift_right_logical(last + LANES - 1, LANE_BITS)

            def window(p, carry):
                at = pl.ds(pl.multiple_of(p * LANES, LANES), LANES)
                token = token_ref[pl.ds(p, 1), :] - group * IDS_PER_GROUP
                token = jnp.broadcast_to(token, (FEATURE_ROWS, LANES))
                lane = (token & (LANES - 1)).astype(jnp.int16)
                tile = lax.shift_right_arithmetic(token, LANE_BITS).astype(jnp.int16)
                pieces = [pl.ds(f, FEATURE_ROWS) for f in range(0, TAKEN, FEATURE_ROWS)]
                short = jnp.broadcast_to(token[0:1], (IDS_PER_GROUP, LANES)).astype(jnp.int16)
                picked = jnp.where(
                    short == iota((IDS_PER_GROUP, LANES), 0).astype(jnp.int16), 1.0, 0.0
                ).astype(jnp.bfloat16)
                columns = pl.ds(part * IDS_PER_GROUP, IDS_PER_GROUP)
                rest = pl.ds(TAKEN, features - TAKEN)
                product = mm(held[slot(b), rest, columns], picked).astype(jnp.bfloat16)
                fresh = []
                for rows in pieces:
                    total = jnp.zeros((FEATURE_ROWS, LANES), jnp.bfloat16)
                    for j in range(IDS_PER_GROUP // LANES):
                        columns = pl.ds(part * IDS_PER_GROUP + j * LANES, LANES)
                        total = jnp.where(tile == j, take_lanes(held[slot(b), rows, columns], lane), total)
                    fresh.append(total)
                pieces.append(rest)
                fresh.append(product)
                fresh = [turned[rows, at] + total for rows, total in zip(pieces, fresh)]
                for rows, total in zip(pieces, fresh):
                    turned[rows, at] = total
                return carry

            lax.fori_loop(begin, jnp.where(last > first, end, begin), window, 0)
        if slots < blocks:

            @pl.when(b + slots < blocks)
            def _():
                vocab_copy(b + slots).start()

        return carry

    lax.fori_loop(0, blocks, take, 0)
    fetch([(turned, turned_any), (member_ref, member_any)], out_sems)


def statistics_kernel(
    turned_any, member_any, hard_ref, lower_ref, extra_ref, small, turned, member_ref, spread, sems
):
    fetch([(turned_any, turned), (member_any, member_ref)], sems)
    features, span = turned.shape
    stripes = pl.cdiv(span, STRIPE)
    per_shard, negatives = hard_ref.shape
    shard = lax.axis_index("dp")
    small[...] = jnp.zeros_like(small)
    small[0:per_shard, stripes : stripes + negatives] = hard_ref[...].astype(jnp.float32)
    lower = lower_ref[:, pl.ds(pl.multiple_of(shard * features, LANES), features)]

    misc = jnp.zeros((ROWS, STRIPE), jnp.float32)
    residual = jnp.zeros((features, LANES), jnp.float32)
    for stripe in range(stripes):
        size = min(STRIPE, span - stripe * STRIPE)
        across = pl.ds(stripe * STRIPE, size)
        upright = turned[:, across]
        wide = upright.astype(jnp.float32)
        square = jnp.sum(wide * wide, axis=0, keepdims=True)
        reduced = mm(lower, upright)
        if size < STRIPE:
            none = jnp.zeros((ROWS, STRIPE - size), jnp.float32)
            reduced = jnp.concatenate([reduced, none], axis=1)
            square = jnp.concatenate([square, none[0:1]], axis=1)
        extra_ref[stripe * ROWS : (stripe + 1) * ROWS, :] = reduced.astype(jnp.bfloat16)
        misc = jnp.where(iota((ROWS, STRIPE), 0) == stripe, square, misc)
        residual += mm(upright, member_ref[across, :])
    hard = small[...].T[0:ROWS]
    for i in range(per_shard):
        misc += jnp.where(iota((ROWS, STRIPE), 1) == shard * per_shard + i, hard[:, i : i + 1], 0.0)
    extra_ref[stripes * ROWS : (stripes + 1) * ROWS, :] = misc.astype(jnp.bfloat16)
    residual = jnp.where(lax.axis_index("mp") == shard, residual.T[0:ROWS], 0.0)
    spread[...] = residual
    for q in range(4):
        start = (stripes + 1 + q) * ROWS
        quarter = pl.multiple_of(split_quarter(q // 2, q % 2) * STRIPE, LANES)
        extra_ref[start : start + ROWS, :] = spread[:, pl.ds(quarter, STRIPE)].astype(jnp.bfloat16)


def pool_kernel(
    ids_ref,
    own_ref,
    core_any,
    far_any,
    extra_ref,
    member_ref,
    own_rest,
    core_rest,
    far_rest,
    extra_rest,
    member_rest,
    raise_ref,
    sent_ref,
    misc_ref,
    raised,
    total,
    slopes,
    core_ref,
    far_ref,
    sems,
    model_width,
):
    texts, length = ids_ref.shape
    width = own_ref.shape[1]
    quarter = quarter_of(lax.axis_index("dp"))
    fetch([(core_any, core_ref), (far_any, far_ref)], sems)
    raised[...] = jnp.zeros_like(raised)
    raised[0:ROWS, :] = raise_ref[:, pl.ds(pl.multiple_of(quarter * width, LANES), width)]
    total[...] = jnp.zeros_like(total)
    slopes[...] = jnp.zeros_like(slopes)

    def add(refs, extra_ref, member_ref, base):
        span = member_ref.shape[0]
        stripes = pl.cdiv(span, STRIPE)

        def summed(start, size):
            return sum(ref[pl.ds(start, size), :].astype(jnp.float32) for ref in refs)

        misc = extra_ref[stripes * ROWS : (stripes + 1) * ROWS, :]
        if base == 0:
            misc_ref[...] = misc
        inverse = lax.rsqrt(misc / model_width + 1e-05)
        for k in range(stripes):
            size = min(STRIPE, span - k * STRIPE)
            scale = inverse[k : k + 1]
            reduced = (extra_ref[k * ROWS : (k + 1) * ROWS, :] * scale).astype(jnp.bfloat16)
            reduced = reduced.astype(jnp.float32)
            stacked = jnp.concatenate([reduced, jnp.broadcast_to(scale, (LANES - ROWS, STRIPE))])
            turned = stacked[:, 0:size].T
            low = turned.astype(jnp.bfloat16)
            linear = summed(k * STRIPE, size)
            linear = linear * turned[:, ROWS : ROWS + 1] + mm(low, raised[...])
            sigma = 1.0 / (1.0 + jnp.exp(-linear))
            slope = (sigma * (1.0 + linear * (1.0 - sigma))).astype(jnp.bfloat16)
            member = member_ref[pl.ds(k * STRIPE, size), :].astype(jnp.float32).T
            high, rest = split(linear * sigma)
            chosen = member[0:ROWS].astype(jnp.bfloat16)
            total[...] += mm(chosen, high) + mm(chosen, rest)
            spread = [reduced[:, 0:size] * member[text : text + 1] for text in range(texts)]
            slopes[...] += mm(jnp.concatenate(spread).astype(jnp.bfloat16), slope)
        total[...] += extra_ref[(stripes + 1) * ROWS : (stripes + 2) * ROWS, :]

    add((own_ref, core_ref, far_ref), extra_ref, member_ref, 0)
    real = (ids_ref[...] != 0).astype(jnp.float32)

    @pl.when(jnp.sum(real) > member_ref.shape[0])
    def _():
        add((own_rest, core_rest, far_rest), extra_rest, member_rest, member_ref.shape[0])

    counts = jnp.sum(real, axis=1, keepdims=True)
    pooled = total[0:texts] / counts
    pooled = jnp.concatenate([pooled, jnp.zeros((ROWS - texts, width), jnp.float32)])
    sent_ref[0:ROWS, :] = pooled.astype(jnp.bfloat16)
    for text in range(texts):
        part = slopes[text * ROWS : (text + 1) * ROWS, :] / counts[text : text + 1]
        sent_ref[(text + 1) * ROWS : (text + 2) * ROWS, :] = part.astype(jnp.bfloat16)


def both_sides(near, far):
    queries = lax.axis_index("group") == 0
    return jnp.concatenate([jnp.where(queries, near, far), jnp.where(queries, far, near)], axis=0)


def dots_kernel(near_ref, far_ref, packed_ref, slopes_ref):
    block = both_sides(near_ref[0:ROWS], far_ref[0:ROWS])
    rows = 2 * ROWS
    packed_ref[...] = jnp.zeros_like(packed_ref)
    packed_ref[0:rows, 0:rows] = mm(block, block, NT)
    for part in range(block.shape[1] // LANES):
        piece = block[:, part * LANES : (part + 1) * LANES]
        packed_ref[rows + part * rows : rows + (part + 1) * rows, :] = piece.astype(jnp.float32)
    size = near_ref.shape[0] - ROWS
    slopes_ref[0:size] = near_ref[ROWS:]
    slopes_ref[size:] = far_ref[ROWS:]


def score_kernel(*refs, texts, stripes, negatives):
    packed0, packed1, packed2, packed3, slopes0, slopes2 = refs[0:6]
    dots0, dots1, dots2, dots3, misc_ref, sharp_ref = refs[6:12]
    embed_ref, loss_ref, up_ref = refs[12:15]
    rows = 2 * ROWS
    per_shard = loss_ref.shape[1]
    group, shard = lax.axis_index("group"), lax.axis_index("dp")
    dots = ((dots0[...] + dots1[...]) + (dots2[...] + dots3[...]))[:, 0:rows]
    down, across = iota((rows, rows), 0), iota((rows, rows), 1)
    same = down == across
    real = (lax.rem(down, ROWS) < texts) & (lax.rem(across, ROWS) < texts)
    diagonal = jnp.where(same, dots, 0.0)
    rnorm_row = lax.rsqrt(jnp.sum(diagonal, axis=0, keepdims=True) + 1e-06)
    rnorm_col = lax.rsqrt(jnp.sum(diagonal, axis=1, keepdims=True) + 1e-06)
    sharpness = sharp_ref[0]
    cosine = dots * rnorm_col * rnorm_row
    scores = sharpness * cosine
    keep = real & ~same
    top = jnp.max(jnp.where(keep, scores, -jnp.inf), axis=0, keepdims=True)
    top = jnp.where(lax.rem(across[0:1], ROWS) < texts, top, 0.0)
    powers = jnp.exp(jnp.where(real, jnp.minimum(scores - top, 0.0), 0.0))
    hard = misc_ref[stripes : stripes + negatives, 0:rows].astype(jnp.int32) + ROWS
    times = jnp.zeros((rows, rows), jnp.float32)
    for k in range(negatives):
        times += jnp.where(hard[k : k + 1] == down, 1.0, 0.0)
    times = jnp.where(across < texts, times, 0.0)
    weights = (jnp.where(keep, 1.0, 0.0) + jnp.where(real, times, 0.0)) * powers
    total = jnp.sum(weights, axis=0, keepdims=True)
    total = jnp.where(lax.rem(across[0:1], ROWS) < texts, total, 1.0)
    pair = (down == lax.rem(across + ROWS, rows)) & real
    pair_score = jnp.sum(jnp.where(pair, scores, 0.0), axis=0, keepdims=True)
    losses = top + jnp.log(total) - pair_score
    grad_scores = (weights / total - jnp.where(pair, 1.0, 0.0)) / (2 * texts)
    coeff = (grad_scores * rnorm_col * rnorm_row).astype(jnp.bfloat16)
    radial = jnp.sum(grad_scores * cosine, axis=0, keepdims=True) * rnorm_row * rnorm_row

    first = shard * per_shard
    loss_col = jnp.sum(jnp.where(same, losses, 0.0), axis=1, keepdims=True)
    at = (iota((rows, LANES), 0) == group * ROWS + first + iota((rows, LANES), 1)) & (
        iota((rows, LANES), 1) < per_shard
    )
    loss_ref[...] = jnp.sum(jnp.where(at, loss_col, 0.0), axis=0, keepdims=True)[:, 0:per_shard]

    along_rows = coeff.astype(jnp.float32).T.astype(jnp.bfloat16)
    radial_col = jnp.sum(jnp.where(same, radial, 0.0), axis=1, keepdims=True)
    rnorm_own = jnp.where(group == 0, rnorm_col[0:ROWS], rnorm_col[ROWS:rows])
    chosen = iota((ROWS, ROWS), 1) == iota((ROWS, ROWS), 0) + first
    chosen = jnp.where(chosen & (iota((ROWS, ROWS), 0) < per_shard), 1.0, 0.0).astype(jnp.bfloat16)
    blocks = ((packed0, slopes0), (packed1, None), (packed2, slopes2), (packed3, None))
    for o, (packed, slopes) in enumerate(blocks):
        parts = packed.shape[0] // rows - 1
        width = parts * LANES
        halves = [packed[rows * (part + 1) : rows * (part + 2), :] for part in range(parts)]
        block = jnp.concatenate(halves, axis=1)
        queries = group == 0
        at = pl.multiple_of(quarter_of(shard ^ o) * width, LANES)
        own = jnp.where(queries, block[0:ROWS], block[ROWS:rows]) * rnorm_own
        picked = mm(chosen, own.astype(jnp.bfloat16)).astype(jnp.bfloat16)
        embed_ref[0, :, pl.ds(at, width)] = picked[0:per_shard]
        if slopes is None:
            continue
        along = mm(along_rows, block.astype(jnp.bfloat16))
        grad = sharpness * (along - radial_col * block)
        near, far = slopes[0 : slopes.shape[0] // 2], slopes[slopes.shape[0] // 2 :]
        grad_near = jnp.where(queries, grad[0:ROWS], grad[ROWS:rows])
        grad_far = jnp.where(queries, grad[ROWS:rows], grad[0:ROWS])
        update = []
        for side, side_grad in ((near, grad_near), (far, grad_far)):
            total = jnp.zeros((ROWS, width), jnp.float32)
            for text in range(texts):
                slope = side[text * ROWS : (text + 1) * ROWS].astype(jnp.float32)
                total += side_grad[text : text + 1] * slope
            update.append(total)
        at = pl.multiple_of((lax.div(shard, 2) ^ (o // 2)) * width, LANES)
        up_ref[:, pl.ds(at, width)] = update[0] + update[1]


def any_spec():
    return pl.BlockSpec(memory_space=pl.ANY)


def vmem_spec():
    return pl.BlockSpec(memory_space=pltpu.VMEM)


def smem_spec():
    return pl.BlockSpec(memory_space=pltpu.SMEM)


def exchange(x, axis, size):
    steps = [[(i, i ^ o) for i in range(size)] for o in range(1, size)]
    return [x] + [lax.ppermute(x, axis, step) for step in steps]


def split_body(
    query_passage_words,
    difficult_distractors,
    vocabulary_vectors,
    layer_weight_matrix,
    lowering_factor_matrix,
    raising_factor_matrix,
    logit_sharpness,
):
    shards, parts = lax.axis_size("dp"), lax.axis_size("mp")
    ids = query_passage_words[0]
    texts, length = ids.shape
    tokens = texts * length
    features, vocab = vocabulary_vectors.shape
    blocks = vocab // IDS_PER_BLOCK
    group_rows = 8 * pl.cdiv(vocab // IDS_PER_GROUP + 1, 8)
    per_shard, negatives = difficult_distractors.shape
    part_width = layer_weight_matrix.shape[1]
    width = part_width // shards
    params = pltpu.CompilerParams(vmem_limit_bytes=LARGE_VMEM)
    modest = pltpu.CompilerParams(vmem_limit_bytes=MODEST_VMEM)
    other_core = [(d, d ^ 1) for d in range(shards)]
    other_y = [(d, d ^ 2) for d in range(shards)]

    def columns(i, j):
        start = split_quarter(i, j) * width
        return lax.dynamic_slice(layer_weight_matrix, (0, start), (features, width))

    def project(base, span, slots, grant):
        stripes = pl.cdiv(span, STRIPE)
        extra_rows = (stripes + 1 + shards) * ROWS
        turned, member, count = pl.pallas_call(
            functools.partial(gather_kernel, base=base),
            out_shape=[
                jax.ShapeDtypeStruct((features, span), jnp.bfloat16),
                jax.ShapeDtypeStruct((span, LANES), jnp.bfloat16),
                jax.ShapeDtypeStruct((1,), jnp.int32),
            ],
            in_specs=[vmem_spec(), any_spec()],
            out_specs=[any_spec()] * 2 + [smem_spec()],
            scratch_shapes=[
                pltpu.VMEM((features, span), jnp.bfloat16),
                pltpu.VMEM((span, LANES), jnp.bfloat16),
                pltpu.VMEM((slots, features, IDS_PER_BLOCK), jnp.bfloat16),
                pltpu.VMEM((8 * pl.cdiv(span // LANES, 8), LANES), jnp.int32),
                pltpu.VMEM((texts, length), jnp.float32),
                pltpu.VMEM((group_rows, length), jnp.int32),
                pltpu.SMEM((group_rows, length), jnp.int32),
                pltpu.SemaphoreType.DMA((slots,)),
                pltpu.SemaphoreType.DMA,
                pltpu.SemaphoreType.DMA((2,)),
            ],
            compiler_params=grant,
            name="gather",
        )(ids, vocabulary_vectors)

        def product(turned, i, j):
            return mm(turned, columns(i, j), (((0,), (0,)), ((), ())))

        def narrow(x):
            return x.astype(jnp.bfloat16)

        core1 = lax.ppermute(narrow(product(turned, 1, 1)), "dp", other_core)
        own1 = lax.optimization_barrier(narrow(product(turned, 0, 1)))
        chip1 = narrow(own1.astype(jnp.float32) + core1.astype(jnp.float32))
        far = lax.ppermute(chip1, "dp", other_y)
        turned, _ = lax.optimization_barrier((turned, chip1))
        extra = pl.pallas_call(
            statistics_kernel,
            out_shape=jax.ShapeDtypeStruct((extra_rows, STRIPE), jnp.bfloat16),
            in_specs=[any_spec()] * 2 + [vmem_spec()] * 2,
            out_specs=vmem_spec(),
            scratch_shapes=[
                pltpu.VMEM((LANES, LANES), jnp.float32),
                pltpu.VMEM(turned.shape, turned.dtype),
                pltpu.VMEM(member.shape, member.dtype),
                pltpu.VMEM((ROWS, features), jnp.float32),
                pltpu.SemaphoreType.DMA((2,)),
            ],
            compiler_params=modest,
            cost_estimate=pl.CostEstimate(
                flops=2 * features * span * (ROWS + LANES),
                bytes_accessed=2 * features * span,
                transcendentals=0,
            ),
            name="statistics",
        )(turned, member, difficult_distractors, lowering_factor_matrix)
        common = (stripes + 1) * ROWS
        near = extra.astype(jnp.float32)
        across = lax.ppermute(extra, "dp", other_core).astype(jnp.float32)
        chip = near[0:common] + across[0:common]
        inputs = near[common : common + 2 * ROWS] + across[common + 2 * ROWS :]
        sent = narrow(jnp.concatenate([chip, inputs[ROWS:]]))
        sent = lax.ppermute(sent, "dp", other_y).astype(jnp.float32)
        extra = jnp.concatenate([chip, inputs[0:ROWS]]) + sent
        core0 = lax.ppermute(narrow(product(turned, 1, 0)), "dp", other_core)
        own0 = narrow(product(turned, 0, 0))
        return (own0, core0, far, extra, member), count

    first, count = project(0, FIRST, blocks, params)
    many = count[0] > FIRST
    left = tokens - FIRST
    shapes = jax.eval_shape(lambda: project(FIRST, left, min(blocks, 4), modest)[0])
    rest = lax.cond(
        many,
        lambda: project(FIRST, left, min(blocks, 4), modest)[0],
        lambda: tuple(jnp.zeros(x.shape, x.dtype) for x in shapes),
    )
    sent, misc = pl.pallas_call(
        functools.partial(pool_kernel, model_width=float(features * shards)),
        out_shape=[
            jax.ShapeDtypeStruct(((texts + 1) * ROWS, width), jnp.bfloat16),
            jax.ShapeDtypeStruct((ROWS, width), jnp.float32),
        ],
        in_specs=[vmem_spec()] * 2 + [any_spec()] * 2 + [vmem_spec()] * 8,
        out_specs=[vmem_spec()] * 2,
        scratch_shapes=[
            pltpu.VMEM((LANES, width), jnp.bfloat16),
            pltpu.VMEM((ROWS, width), jnp.float32),
            pltpu.VMEM((texts * ROWS, width), jnp.float32),
            pltpu.VMEM((FIRST, width), jnp.bfloat16),
            pltpu.VMEM((FIRST, width), jnp.bfloat16),
            pltpu.SemaphoreType.DMA((2,)),
        ],
        compiler_params=modest,
        name="pool",
    )(ids, *first, *rest, raising_factor_matrix)
    far_side = lax.ppermute(sent, "group", [(0, 1), (1, 0)])
    rows = 2 * ROWS
    packed, slopes = pl.pallas_call(
        dots_kernel,
        out_shape=[
            jax.ShapeDtypeStruct((rows + width // LANES * rows, LANES), jnp.float32),
            jax.ShapeDtypeStruct((2 * texts * ROWS, width), jnp.bfloat16),
        ],
        in_specs=[vmem_spec()] * 2,
        out_specs=[vmem_spec()] * 2,
        compiler_params=modest,
        name="dots",
    )(sent, far_side)
    packed = exchange(packed, "dp", shards)
    dots = [x[0:rows] for x in packed]
    dots = (dots[0] + dots[1]) + (dots[2] + dots[3])
    slopes, dots = lax.optimization_barrier((slopes, dots))
    dots = exchange(dots, "mp", parts)
    slopes = [slopes, lax.ppermute(slopes, "dp", other_y)]
    embeddings, losses, update = pl.pallas_call(
        functools.partial(
            score_kernel, texts=texts, stripes=pl.cdiv(FIRST, STRIPE), negatives=negatives
        ),
        out_shape=[
            jax.ShapeDtypeStruct((1, per_shard, part_width), jnp.bfloat16),
            jax.ShapeDtypeStruct((1, per_shard), jnp.float32),
            jax.ShapeDtypeStruct((ROWS, part_width // 2), jnp.float32),
        ],
        in_specs=[vmem_spec()] * 11 + [smem_spec()],
        out_specs=[vmem_spec()] * 3,
        compiler_params=modest,
        name="score",
    )(*packed, *slopes, *dots, misc, logit_sharpness)
    other = lax.ppermute(update, "dp", other_core)
    core = lax.rem(lax.axis_index("dp"), 2)
    halves = [jnp.where(core == 0, update, other), jnp.where(core == 0, other, update)]
    return (embeddings, losses, jnp.concatenate(halves, axis=1))


def body(words, hard, vocabulary, weight, lowering, raising, sharpness):
    shards, parts = lax.axis_size("dp"), lax.axis_size("mp")
    texts, length = words.shape[1:]
    features, vocab = vocabulary.shape
    negatives = hard.shape[1]
    square = shards == 4 and features == weight.shape[1] == 4 * STRIPE and parts == shards
    small = texts <= ROWS - 2 and length == LANES and FIRST < texts * length <= 2048
    even = (texts * length - FIRST) % CHUNK == 0 and vocab % IDS_PER_BLOCK == 0
    fits = features * vocab <= 2**24 and features % (4 * LANES) == 0
    spare = pl.cdiv(FIRST, STRIPE) + negatives <= ROWS and lowering.shape[0] == ROWS
    fast = square and small and even and fits and spare and lax.axis_size("group") == 2
    chosen = split_body if fast else general_body
    return chosen(words, hard, vocabulary, weight, lowering, raising, sharpness)


def solution(mesh):
    in_specs = (
        P("group", None, None),
        P("dp", None),
        P("dp", None),
        P("dp", "mp"),
        P(),
        P(None, "mp"),
        P(),
    )
    out_specs = (P("group", "dp", "mp"), P("group", "dp"), P(None, "mp"))
    return jax.shard_map(body, mesh=mesh, in_specs=in_specs, out_specs=out_specs, check_vma=False)
```

```python
import functools

import jax
import jax.numpy as jnp
from jax import lax
from jax.experimental import pallas as pl
from jax.experimental.pallas import tpu as pltpu
from jax.sharding import PartitionSpec as P


def general_body(
    query_passage_words,
    difficult_distractors,
    vocabulary_vectors,
    layer_weight_matrix,
    lowering_factor_matrix,
    raising_factor_matrix,
    logit_sharpness,
):
    group_index = lax.axis_index("group")
    shard_index = lax.axis_index("dp")
    part_index = lax.axis_index("mp")
    shard_count = lax.axis_size("dp")
    side_ids = query_passage_words[0]
    text_count = side_ids.shape[0]
    length = side_ids.shape[1]
    per_shard = text_count // shard_count
    own_ids = lax.dynamic_slice_in_dim(side_ids, shard_index * per_shard, per_shard, 0)
    columns = jnp.take(vocabulary_vectors, side_ids.reshape(-1), axis=1)
    inputs = lax.all_to_all(columns, "dp", split_axis=1, concat_axis=0, tiled=True)
    tokens = inputs.shape[1]
    feature_width = raising_factor_matrix.shape[1]
    wide_inputs = inputs.astype(jnp.float32)
    inverse = lax.rsqrt(jnp.mean(wide_inputs * wide_inputs, axis=0) + 1e-05)
    normed_state = (wide_inputs * inverse[None, :]).astype(jnp.bfloat16)
    linear_map = lax.dot_general(
        lax.all_gather(layer_weight_matrix, "dp", axis=0, tiled=True),
        normed_state,
        (((0,), (0,)), ((), ())),
        preferred_element_type=jnp.float32,
    )
    reduced_sum = jnp.dot(
        lowering_factor_matrix, normed_state, preferred_element_type=jnp.float32
    ).astype(jnp.bfloat16)
    linear_map = linear_map + lax.dot_general(
        raising_factor_matrix,
        reduced_sum,
        (((0,), (0,)), ((), ())),
        preferred_element_type=jnp.float32,
    )
    own_inputs = lax.dynamic_slice_in_dim(
        inputs, part_index * feature_width, feature_width, 0
    ).astype(jnp.float32)
    hidden_state = own_inputs + jax.nn.silu(linear_map)
    mask = (own_ids != 0).astype(jnp.float32)
    counts = jnp.sum(mask, axis=1)
    summed = jnp.einsum("dnl,nl->nd", hidden_state.reshape(feature_width, per_shard, length), mask)
    pooled = (summed / counts[:, None]).astype(jnp.bfloat16)
    gathered = lax.all_gather(pooled, ("group", "dp"), axis=0, tiled=True)
    part_scores = lax.dot_general(
        pooled, gathered, (((1,), (1,)), ((), ())), preferred_element_type=jnp.float32
    )
    gathered_wide = gathered.astype(jnp.float32)
    part_norms = jnp.sum(gathered_wide * gathered_wide, axis=1)
    dots, norms = lax.psum((part_scores, part_norms), "mp")
    rnorm_all = lax.rsqrt(norms + 1e-06)
    all_count = gathered.shape[0]
    half_count = all_count // 2
    own_rows = (
        group_index * half_count + shard_index * per_shard + jnp.arange(per_shard, dtype=jnp.int32)
    )
    rnorm_own = jnp.take(rnorm_all, own_rows)
    cosine = dots * rnorm_own[:, None] * rnorm_all[None, :]
    multiplier_factor = logit_sharpness[0]
    scores = multiplier_factor * cosine
    column_ids = jnp.arange(all_count, dtype=jnp.int32)
    keep = column_ids[None, :] != own_rows[:, None]
    pair = (own_rows + half_count) % all_count
    weight = (group_index == 0).astype(jnp.float32)
    neg_cols = half_count + difficult_distractors
    top = jnp.max(jnp.where(keep, scores, -jnp.inf), axis=1)
    safe_scores = jnp.where(keep, scores, top[:, None])
    expd = jnp.where(keep, jnp.exp(safe_scores - top[:, None]), 0.0)
    neg_exp = (
        jnp.exp(jnp.minimum(jnp.take_along_axis(scores, neg_cols, axis=1) - top[:, None], 0.0))
        * weight
    )
    total = jnp.sum(expd, axis=1) + jnp.sum(neg_exp, axis=1)
    pair_score = jnp.take_along_axis(scores, pair[:, None], axis=1)[:, 0]
    losses = top + jnp.log(total) - pair_score
    onehot = (column_ids[None, None, :] == neg_cols[:, :, None]).astype(jnp.float32)
    probs = (expd + jnp.einsum("rk,rkc->rc", neg_exp, onehot)) / total[:, None]
    target = (column_ids[None, :] == pair[:, None]).astype(jnp.float32)
    grad_scores = (probs - target) / all_count
    coeff = (grad_scores * rnorm_own[:, None] * rnorm_all[None, :]).astype(jnp.bfloat16)
    along = jnp.dot(coeff, gathered, preferred_element_type=jnp.float32)
    pooled_wide = pooled.astype(jnp.float32)
    radial = jnp.sum(grad_scores * cosine, axis=1) * rnorm_own * rnorm_own
    embedding_gradient = multiplier_factor * (along - radial[:, None] * pooled_wide)
    token_grad = jnp.einsum("nd,nl->dnl", embedding_gradient / counts[:, None], mask).reshape(
        feature_width, tokens
    )
    sigma = jax.nn.sigmoid(linear_map)
    local = (token_grad * sigma * (1.0 + linear_map * (1.0 - sigma))).astype(jnp.bfloat16)
    up_portion = lax.dot_general(
        reduced_sum, local, (((1,), (1,)), ((), ())), preferred_element_type=jnp.float32
    )
    adapter_up_gradient = lax.psum(up_portion, ("group", "dp"))
    embeddings = (pooled_wide * rnorm_own[:, None]).astype(jnp.bfloat16)[None]
    return (embeddings, losses[None], adapter_up_gradient)


BLOCK_BITS, GROUP_BITS, LANE_BITS, ROW_BITS = 10, 9, 7, 4
IDS_PER_BLOCK = 1 << BLOCK_BITS
IDS_PER_GROUP = 1 << GROUP_BITS
CHUNK = 384
STRIPE = 256
ROWS = 1 << ROW_BITS
LANES = 1 << LANE_BITS
FEATURE_ROWS = 128
FIRST = 1152
TAKEN = 768
NT = (((1,), (1,)), ((), ()))
LARGE_VMEM, MODEST_VMEM = 44 * 1024 * 1024, 15 * 1024 * 1024


def mm(a, b, dims=(((1,), (0,)), ((), ()))):
    return lax.dot_general(a, b, dims, preferred_element_type=jnp.float32)


def split(x):
    high = x.astype(jnp.bfloat16)
    return high, (x - high.astype(jnp.float32)).astype(jnp.bfloat16)


def iota(shape, dim):
    return lax.broadcasted_iota(jnp.int32, shape, dim)


def quarter_of(dp_index, cores=2):
    return (dp_index % cores) * 2 + dp_index // cores


def split_quarter(i, j, cores=2):
    shard = lax.axis_index("dp")
    core, side_y = lax.rem(shard, cores), lax.div(shard, cores)
    return (core ^ i) * 2 + (side_y ^ j)


def take_lanes(x, lanes):
    numbers = lax.GatherDimensionNumbers(
        offset_dims=(),
        collapsed_slice_dims=(1,),
        start_index_map=(1,),
        operand_batching_dims=(0,),
        start_indices_batching_dims=(0,),
    )
    mode = lax.GatherScatterMode.PROMISE_IN_BOUNDS
    return lax.gather(x, lanes[..., None], numbers, slice_sizes=(1, 1), mode=mode)


def fetch(pairs, sems):
    copies = [pltpu.make_async_copy(a, b, sems.at[n]) for n, (a, b) in enumerate(pairs)]
    for copy in copies:
        copy.start()
    for copy in copies:
        copy.wait()


def gather_kernel(
    ids_ref,
    vocab_ref,
    turned_any,
    member_any,
    turned,
    member_ref,
    held,
    token_ref,
    ranks,
    counted,
    bounds,
    held_sems,
    bounds_sem,
    out_sems,
    base,
):
    texts, length = ids_ref.shape
    features, vocab = vocab_ref.shape
    blocks = vocab // IDS_PER_BLOCK
    groups = vocab // IDS_PER_GROUP
    span = member_ref.shape[0]

    def vocab_copy(b):
        columns = pl.ds(pl.multiple_of(b * IDS_PER_BLOCK, LANES), IDS_PER_BLOCK)
        return pltpu.make_async_copy(vocab_ref.at[:, columns], held.at[b], held_sems.at[b])

    vocab_copy(0).start()
    for b in range(1, blocks):
        vocab_copy(b).start()

    ids = ids_ref[...]
    valid = ids != 0
    group_of = jnp.where(valid, lax.shift_right_logical(ids, GROUP_BITS), groups)
    group_rows = counted.shape[0]
    group_id = iota((group_rows, length), 0)
    below = jnp.zeros((group_rows, length), jnp.float32)
    for text in range(texts):
        below += jnp.where(group_of[text : text + 1] < group_id, 1.0, 0.0)
    before = jnp.broadcast_to(jnp.sum(below, axis=1, keepdims=True), (group_rows, length))
    counted[...] = before.astype(jnp.int32)
    bounds_copy = pltpu.make_async_copy(counted, bounds, bounds_sem)
    bounds_copy.start()
    earlier = jnp.where(iota((length, length), 0) < iota((length, length), 1), 1.0, 0.0).astype(
        jnp.bfloat16
    )
    for text in range(texts):
        here = jnp.where(group_of[text : text + 1] == group_id, 1.0, 0.0)
        inside = mm(here.astype(jnp.bfloat16), earlier)
        ranks[pl.ds(text, 1), :] = jnp.sum(here * (inside + before), axis=0, keepdims=True)
        before += jnp.broadcast_to(jnp.sum(here, axis=1, keepdims=True), (group_rows, length))
    text_of = iota((texts, length), 0)
    carried = jnp.where(valid, lax.shift_left(ids, ROW_BITS) + text_of, 0).astype(jnp.float32)
    rank = ranks[...]

    def place(p, carry):
        position = (iota((LANES, length), 0) + (p * LANES + base)).astype(jnp.float32)
        total = jnp.zeros((LANES, length), jnp.float32)
        for text in range(texts):
            total += jnp.where(rank[text : text + 1] == position, carried[text : text + 1], 0.0)
        found = jnp.broadcast_to(jnp.sum(total, axis=1, keepdims=True), (LANES, LANES))
        start = pl.multiple_of(p * LANES, LANES)
        row = found.T[0:1].astype(jnp.int32)
        token = lax.shift_right_logical(row, ROW_BITS)
        token_ref[pl.ds(p, 1), :] = jnp.where(token == 0, -vocab, token)
        found = found.astype(jnp.int32)
        real = (found >= ROWS) & ((found & (ROWS - 1)) == iota((LANES, LANES), 1))
        member_ref[pl.ds(start, LANES), :] = jnp.where(real, 1.0, 0.0).astype(jnp.bfloat16)
        turned[:, pl.ds(start, LANES)] = jnp.zeros((features, LANES), jnp.bfloat16)
        return carry

    lax.fori_loop(0, span // LANES, place, 0)
    bounds_copy.wait()

    def within(place):
        return jnp.clip(place - base, 0, span)

    def take(b, carry):
        vocab_copy(b).wait()
        for part in range(IDS_PER_BLOCK // IDS_PER_GROUP):
            group = b * (IDS_PER_BLOCK // IDS_PER_GROUP) + part
            first, last = within(bounds[group, 0]), within(bounds[group + 1, 0])
            begin = lax.shift_right_logical(first, LANE_BITS)
            end = lax.shift_right_logical(last + LANES - 1, LANE_BITS)

            def window(p, carry):
                at = pl.ds(pl.multiple_of(p * LANES, LANES), LANES)
                token = token_ref[pl.ds(p, 1), :] - group * IDS_PER_GROUP
                token = jnp.broadcast_to(token, (FEATURE_ROWS, LANES))
                lane = (token & (LANES - 1)).astype(jnp.int16)
                tile = lax.shift_right_arithmetic(token, LANE_BITS).astype(jnp.int16)
                pieces = [pl.ds(f, FEATURE_ROWS) for f in range(0, TAKEN, FEATURE_ROWS)]
                short = jnp.broadcast_to(token[0:1], (IDS_PER_GROUP, LANES)).astype(jnp.int16)
                picked = jnp.where(
                    short == iota((IDS_PER_GROUP, LANES), 0).astype(jnp.int16), 1.0, 0.0
                ).astype(jnp.bfloat16)
                columns = pl.ds(part * IDS_PER_GROUP, IDS_PER_GROUP)
                rest = pl.ds(TAKEN, features - TAKEN)
                product = mm(held[b, rest, columns], picked).astype(jnp.bfloat16)
                fresh = []
                for rows in pieces:
                    total = jnp.zeros((FEATURE_ROWS, LANES), jnp.bfloat16)
                    for j in range(IDS_PER_GROUP // LANES):
                        columns = pl.ds(part * IDS_PER_GROUP + j * LANES, LANES)
                        total = jnp.where(tile == j, take_lanes(held[b, rows, columns], lane), total)
                    fresh.append(total)
                pieces.append(rest)
                fresh.append(product)
                fresh = [turned[rows, at] + total for rows, total in zip(pieces, fresh)]
                for rows, total in zip(pieces, fresh):
                    turned[rows, at] = total
                return carry

            lax.fori_loop(begin, jnp.where(last > first, end, begin), window, 0)
        return carry

    lax.fori_loop(0, blocks, take, 0)
    fetch([(turned, turned_any), (member_ref, member_any)], out_sems)


def statistics_kernel(
    turned_any, member_any, hard_ref, lower_ref, extra_ref, small, turned, member_ref, spread, sems
):
    fetch([(turned_any, turned), (member_any, member_ref)], sems)
    features, span = turned.shape
    stripes = pl.cdiv(span, STRIPE)
    per_shard, negatives = hard_ref.shape
    shard = lax.axis_index("dp")
    small[...] = jnp.zeros_like(small)
    small[0:per_shard, stripes : stripes + negatives] = hard_ref[...].astype(jnp.float32)
    lower = lower_ref[:, pl.ds(pl.multiple_of(shard * features, LANES), features)]

    misc = jnp.zeros((ROWS, STRIPE), jnp.float32)
    residual = jnp.zeros((features, LANES), jnp.float32)
    for stripe in range(stripes):
        size = min(STRIPE, span - stripe * STRIPE)
        across = pl.ds(stripe * STRIPE, size)
        upright = turned[:, across]
        wide = upright.astype(jnp.float32)
        square = jnp.sum(wide * wide, axis=0, keepdims=True)
        reduced = mm(lower, upright)
        if size < STRIPE:
            none = jnp.zeros((ROWS, STRIPE - size), jnp.float32)
            reduced = jnp.concatenate([reduced, none], axis=1)
            square = jnp.concatenate([square, none[0:1]], axis=1)
        extra_ref[stripe * ROWS : (stripe + 1) * ROWS, :] = reduced.astype(jnp.bfloat16)
        misc = jnp.where(iota((ROWS, STRIPE), 0) == stripe, square, misc)
        residual += mm(upright, member_ref[across, :])
    hard = small[...].T[0:ROWS]
    for i in range(per_shard):
        misc += jnp.where(iota((ROWS, STRIPE), 1) == shard * per_shard + i, hard[:, i : i + 1], 0.0)
    extra_ref[stripes * ROWS : (stripes + 1) * ROWS, :] = misc.astype(jnp.bfloat16)
    residual = jnp.where(lax.axis_index("mp") == shard, residual.T[0:ROWS], 0.0)
    spread[...] = residual
    for q in range(4):
        start = (stripes + 1 + q) * ROWS
        quarter = pl.multiple_of(split_quarter(q // 2, q % 2) * STRIPE, LANES)
        extra_ref[start : start + ROWS, :] = spread[:, pl.ds(quarter, STRIPE)].astype(jnp.bfloat16)


def pool_kernel(
    ids_ref,
    own_ref,
    core_any,
    far_any,
    extra_ref,
    member_ref,
    own_rest,
    core_rest,
    far_rest,
    extra_rest,
    member_rest,
    raise_ref,
    sent_ref,
    misc_ref,
    raised,
    total,
    slopes,
    core_ref,
    far_ref,
    sems,
    model_width,
):
    texts, length = ids_ref.shape
    width = own_ref.shape[1]
    quarter = quarter_of(lax.axis_index("dp"))
    fetch([(core_any, core_ref), (far_any, far_ref)], sems)
    raised[...] = jnp.zeros_like(raised)
    raised[0:ROWS, :] = raise_ref[:, pl.ds(pl.multiple_of(quarter * width, LANES), width)]
    total[...] = jnp.zeros_like(total)
    slopes[...] = jnp.zeros_like(slopes)

    def add(refs, extra_ref, member_ref, base):
        span = member_ref.shape[0]
        stripes = pl.cdiv(span, STRIPE)

        def summed(start, size):
            return sum(ref[pl.ds(start, size), :].astype(jnp.float32) for ref in refs)

        misc = extra_ref[stripes * ROWS : (stripes + 1) * ROWS, :]
        if base == 0:
            misc_ref[...] = misc
        inverse = lax.rsqrt(misc / model_width + 1e-05)
        for k in range(stripes):
            size = min(STRIPE, span - k * STRIPE)
            scale = inverse[k : k + 1]
            reduced = (extra_ref[k * ROWS : (k + 1) * ROWS, :] * scale).astype(jnp.bfloat16)
            reduced = reduced.astype(jnp.float32)
            stacked = jnp.concatenate([reduced, jnp.broadcast_to(scale, (LANES - ROWS, STRIPE))])
            turned = stacked[:, 0:size].T
            low = turned.astype(jnp.bfloat16)
            linear = summed(k * STRIPE, size)
            linear = linear * turned[:, ROWS : ROWS + 1] + mm(low, raised[...])
            sigma = 1.0 / (1.0 + jnp.exp(-linear))
            slope = (sigma * (1.0 + linear * (1.0 - sigma))).astype(jnp.bfloat16)
            member = member_ref[pl.ds(k * STRIPE, size), :].astype(jnp.float32).T
            high, rest = split(linear * sigma)
            chosen = member[0:ROWS].astype(jnp.bfloat16)
            total[...] += mm(chosen, high) + mm(chosen, rest)
            spread = [reduced[:, 0:size] * member[text : text + 1] for text in range(texts)]
            slopes[...] += mm(jnp.concatenate(spread).astype(jnp.bfloat16), slope)
        total[...] += extra_ref[(stripes + 1) * ROWS : (stripes + 2) * ROWS, :]

    add((own_ref, core_ref, far_ref), extra_ref, member_ref, 0)
    real = (ids_ref[...] != 0).astype(jnp.float32)

    @pl.when(jnp.sum(real) > member_ref.shape[0])
    def _():
        add((own_rest, core_rest, far_rest), extra_rest, member_rest, member_ref.shape[0])

    counts = jnp.sum(real, axis=1, keepdims=True)
    pooled = total[0:texts] / counts
    pooled = jnp.concatenate([pooled, jnp.zeros((ROWS - texts, width), jnp.float32)])
    sent_ref[0:ROWS, :] = pooled.astype(jnp.bfloat16)
    for text in range(texts):
        part = slopes[text * ROWS : (text + 1) * ROWS, :] / counts[text : text + 1]
        sent_ref[(text + 1) * ROWS : (text + 2) * ROWS, :] = part.astype(jnp.bfloat16)


def both_sides(near, far):
    queries = lax.axis_index("group") == 0
    return jnp.concatenate([jnp.where(queries, near, far), jnp.where(queries, far, near)], axis=0)


def dots_kernel(near_ref, far_ref, packed_ref, slopes_ref):
    block = both_sides(near_ref[0:ROWS], far_ref[0:ROWS])
    rows = 2 * ROWS
    packed_ref[...] = jnp.zeros_like(packed_ref)
    packed_ref[0:rows, 0:rows] = mm(block, block, NT)
    for part in range(block.shape[1] // LANES):
        piece = block[:, part * LANES : (part + 1) * LANES]
        packed_ref[rows + part * rows : rows + (part + 1) * rows, :] = piece.astype(jnp.float32)
    size = near_ref.shape[0] - ROWS
    slopes_ref[0:size] = near_ref[ROWS:]
    slopes_ref[size:] = far_ref[ROWS:]


def score_kernel(*refs, texts, stripes, negatives):
    packed0, packed1, packed2, packed3, slopes0, slopes2 = refs[0:6]
    dots0, dots1, dots2, dots3, misc_ref, sharp_ref = refs[6:12]
    embed_ref, loss_ref, up_ref = refs[12:15]
    rows = 2 * ROWS
    per_shard = loss_ref.shape[1]
    group, shard = lax.axis_index("group"), lax.axis_index("dp")
    dots = ((dots0[...] + dots1[...]) + (dots2[...] + dots3[...]))[:, 0:rows]
    down, across = iota((rows, rows), 0), iota((rows, rows), 1)
    same = down == across
    real = (lax.rem(down, ROWS) < texts) & (lax.rem(across, ROWS) < texts)
    diagonal = jnp.where(same, dots, 0.0)
    rnorm_row = lax.rsqrt(jnp.sum(diagonal, axis=0, keepdims=True) + 1e-06)
    rnorm_col = lax.rsqrt(jnp.sum(diagonal, axis=1, keepdims=True) + 1e-06)
    sharpness = sharp_ref[0]
    cosine = dots * rnorm_col * rnorm_row
    scores = sharpness * cosine
    keep = real & ~same
    top = jnp.max(jnp.where(keep, scores, -jnp.inf), axis=0, keepdims=True)
    top = jnp.where(lax.rem(across[0:1], ROWS) < texts, top, 0.0)
    powers = jnp.exp(jnp.where(real, jnp.minimum(scores - top, 0.0), 0.0))
    hard = misc_ref[stripes : stripes + negatives, 0:rows].astype(jnp.int32) + ROWS
    times = jnp.zeros((rows, rows), jnp.float32)
    for k in range(negatives):
        times += jnp.where(hard[k : k + 1] == down, 1.0, 0.0)
    times = jnp.where(across < texts, times, 0.0)
    weights = (jnp.where(keep, 1.0, 0.0) + jnp.where(real, times, 0.0)) * powers
    total = jnp.sum(weights, axis=0, keepdims=True)
    total = jnp.where(lax.rem(across[0:1], ROWS) < texts, total, 1.0)
    pair = (down == lax.rem(across + ROWS, rows)) & real
    pair_score = jnp.sum(jnp.where(pair, scores, 0.0), axis=0, keepdims=True)
    losses = top + jnp.log(total) - pair_score
    grad_scores = (weights / total - jnp.where(pair, 1.0, 0.0)) / (2 * texts)
    coeff = (grad_scores * rnorm_col * rnorm_row).astype(jnp.bfloat16)
    radial = jnp.sum(grad_scores * cosine, axis=0, keepdims=True) * rnorm_row * rnorm_row

    first = shard * per_shard
    loss_col = jnp.sum(jnp.where(same, losses, 0.0), axis=1, keepdims=True)
    at = (iota((rows, LANES), 0) == group * ROWS + first + iota((rows, LANES), 1)) & (
        iota((rows, LANES), 1) < per_shard
    )
    loss_ref[...] = jnp.sum(jnp.where(at, loss_col, 0.0), axis=0, keepdims=True)[:, 0:per_shard]

    along_rows = coeff.astype(jnp.float32).T.astype(jnp.bfloat16)
    radial_col = jnp.sum(jnp.where(same, radial, 0.0), axis=1, keepdims=True)
    rnorm_own = jnp.where(group == 0, rnorm_col[0:ROWS], rnorm_col[ROWS:rows])
    chosen = iota((ROWS, ROWS), 1) == iota((ROWS, ROWS), 0) + first
    chosen = jnp.where(chosen & (iota((ROWS, ROWS), 0) < per_shard), 1.0, 0.0).astype(jnp.bfloat16)
    blocks = ((packed0, slopes0), (packed1, None), (packed2, slopes2), (packed3, None))
    for o, (packed, slopes) in enumerate(blocks):
        parts = packed.shape[0] // rows - 1
        width = parts * LANES
        halves = [packed[rows * (part + 1) : rows * (part + 2), :] for part in range(parts)]
        block = jnp.concatenate(halves, axis=1)
        queries = group == 0
        at = pl.multiple_of(quarter_of(shard ^ o) * width, LANES)
        own = jnp.where(queries, block[0:ROWS], block[ROWS:rows]) * rnorm_own
        picked = mm(chosen, own.astype(jnp.bfloat16)).astype(jnp.bfloat16)
        embed_ref[0, :, pl.ds(at, width)] = picked[0:per_shard]
        if slopes is None:
            continue
        along = mm(along_rows, block.astype(jnp.bfloat16))
        grad = sharpness * (along - radial_col * block)
        near, far = slopes[0 : slopes.shape[0] // 2], slopes[slopes.shape[0] // 2 :]
        grad_near = jnp.where(queries, grad[0:ROWS], grad[ROWS:rows])
        grad_far = jnp.where(queries, grad[ROWS:rows], grad[0:ROWS])
        update = []
        for side, side_grad in ((near, grad_near), (far, grad_far)):
            total = jnp.zeros((ROWS, width), jnp.float32)
            for text in range(texts):
                slope = side[text * ROWS : (text + 1) * ROWS].astype(jnp.float32)
                total += side_grad[text : text + 1] * slope
            update.append(total)
        at = pl.multiple_of((lax.div(shard, 2) ^ (o // 2)) * width, LANES)
        up_ref[:, pl.ds(at, width)] = update[0] + update[1]


def any_spec():
    return pl.BlockSpec(memory_space=pl.ANY)


def vmem_spec():
    return pl.BlockSpec(memory_space=pltpu.VMEM)


def smem_spec():
    return pl.BlockSpec(memory_space=pltpu.SMEM)


def exchange(x, axis, size):
    steps = [[(i, i ^ o) for i in range(size)] for o in range(1, size)]
    return [x] + [lax.ppermute(x, axis, step) for step in steps]


def split_body(
    query_passage_words,
    difficult_distractors,
    vocabulary_vectors,
    layer_weight_matrix,
    lowering_factor_matrix,
    raising_factor_matrix,
    logit_sharpness,
):
    shards, parts = lax.axis_size("dp"), lax.axis_size("mp")
    ids = query_passage_words[0]
    texts, length = ids.shape
    tokens = texts * length
    features, vocab = vocabulary_vectors.shape
    blocks = vocab // IDS_PER_BLOCK
    group_rows = 8 * pl.cdiv(vocab // IDS_PER_GROUP + 1, 8)
    per_shard, negatives = difficult_distractors.shape
    part_width = layer_weight_matrix.shape[1]
    width = part_width // shards
    params = pltpu.CompilerParams(vmem_limit_bytes=LARGE_VMEM)
    modest = pltpu.CompilerParams(vmem_limit_bytes=MODEST_VMEM)
    other_core = [(d, d ^ 1) for d in range(shards)]
    other_y = [(d, d ^ 2) for d in range(shards)]

    def columns(i, j):
        start = split_quarter(i, j) * width
        return lax.dynamic_slice(layer_weight_matrix, (0, start), (features, width))

    def project(base, span):
        stripes = pl.cdiv(span, STRIPE)
        extra_rows = (stripes + 1 + shards) * ROWS
        turned, member = pl.pallas_call(
            functools.partial(gather_kernel, base=base),
            out_shape=[
                jax.ShapeDtypeStruct((features, span), jnp.bfloat16),
                jax.ShapeDtypeStruct((span, LANES), jnp.bfloat16),
            ],
            in_specs=[vmem_spec(), any_spec()],
            out_specs=[any_spec()] * 2,
            scratch_shapes=[
                pltpu.VMEM((features, span), jnp.bfloat16),
                pltpu.VMEM((span, LANES), jnp.bfloat16),
                pltpu.VMEM((blocks, features, IDS_PER_BLOCK), jnp.bfloat16),
                pltpu.VMEM((8 * pl.cdiv(span // LANES, 8), LANES), jnp.int32),
                pltpu.VMEM((texts, length), jnp.float32),
                pltpu.VMEM((group_rows, length), jnp.int32),
                pltpu.SMEM((group_rows, length), jnp.int32),
                pltpu.SemaphoreType.DMA((blocks,)),
                pltpu.SemaphoreType.DMA,
                pltpu.SemaphoreType.DMA((2,)),
            ],
            compiler_params=params,
            name="gather",
        )(ids, vocabulary_vectors)

        def product(turned, i, j):
            return mm(turned, columns(i, j), (((0,), (0,)), ((), ())))

        def narrow(x):
            return x.astype(jnp.bfloat16)

        core1 = lax.ppermute(narrow(product(turned, 1, 1)), "dp", other_core)
        own1 = lax.optimization_barrier(narrow(product(turned, 0, 1)))
        chip1 = narrow(own1.astype(jnp.float32) + core1.astype(jnp.float32))
        far = lax.ppermute(chip1, "dp", other_y)
        turned, _ = lax.optimization_barrier((turned, chip1))
        extra = pl.pallas_call(
            statistics_kernel,
            out_shape=jax.ShapeDtypeStruct((extra_rows, STRIPE), jnp.bfloat16),
            in_specs=[any_spec()] * 2 + [vmem_spec()] * 2,
            out_specs=vmem_spec(),
            scratch_shapes=[
                pltpu.VMEM((LANES, LANES), jnp.float32),
                pltpu.VMEM(turned.shape, turned.dtype),
                pltpu.VMEM(member.shape, member.dtype),
                pltpu.VMEM((ROWS, features), jnp.float32),
                pltpu.SemaphoreType.DMA((2,)),
            ],
            compiler_params=modest,
            cost_estimate=pl.CostEstimate(
                flops=2 * features * span * (ROWS + LANES),
                bytes_accessed=2 * features * span,
                transcendentals=0,
            ),
            name="statistics",
        )(turned, member, difficult_distractors, lowering_factor_matrix)
        common = (stripes + 1) * ROWS
        near = extra.astype(jnp.float32)
        across = lax.ppermute(extra, "dp", other_core).astype(jnp.float32)
        chip = near[0:common] + across[0:common]
        inputs = near[common : common + 2 * ROWS] + across[common + 2 * ROWS :]
        sent = narrow(jnp.concatenate([chip, inputs[ROWS:]]))
        sent = lax.ppermute(sent, "dp", other_y).astype(jnp.float32)
        extra = jnp.concatenate([chip, inputs[0:ROWS]]) + sent
        core0 = lax.ppermute(narrow(product(turned, 1, 0)), "dp", other_core)
        own0 = narrow(product(turned, 0, 0))
        return own0, core0, far, extra, member

    first = project(0, FIRST)
    later, _ = lax.optimization_barrier((ids, first[0]))
    many = jnp.sum((later != 0).astype(jnp.int32)) > FIRST
    left = tokens - FIRST
    shapes = jax.eval_shape(lambda: project(FIRST, left))
    rest = lax.cond(
        many,
        lambda: project(FIRST, left),
        lambda: tuple(jnp.zeros(x.shape, x.dtype) for x in shapes),
    )
    sent, misc = pl.pallas_call(
        functools.partial(pool_kernel, model_width=float(features * shards)),
        out_shape=[
            jax.ShapeDtypeStruct(((texts + 1) * ROWS, width), jnp.bfloat16),
            jax.ShapeDtypeStruct((ROWS, width), jnp.float32),
        ],
        in_specs=[vmem_spec()] * 2 + [any_spec()] * 2 + [vmem_spec()] * 8,
        out_specs=[vmem_spec()] * 2,
        scratch_shapes=[
            pltpu.VMEM((LANES, width), jnp.bfloat16),
            pltpu.VMEM((ROWS, width), jnp.float32),
            pltpu.VMEM((texts * ROWS, width), jnp.float32),
            pltpu.VMEM((FIRST, width), jnp.bfloat16),
            pltpu.VMEM((FIRST, width), jnp.bfloat16),
            pltpu.SemaphoreType.DMA((2,)),
        ],
        compiler_params=modest,
        name="pool",
    )(ids, *first, *rest, raising_factor_matrix)
    far_side = lax.ppermute(sent, "group", [(0, 1), (1, 0)])
    rows = 2 * ROWS
    packed, slopes = pl.pallas_call(
        dots_kernel,
        out_shape=[
            jax.ShapeDtypeStruct((rows + width // LANES * rows, LANES), jnp.float32),
            jax.ShapeDtypeStruct((2 * texts * ROWS, width), jnp.bfloat16),
        ],
        in_specs=[vmem_spec()] * 2,
        out_specs=[vmem_spec()] * 2,
        compiler_params=modest,
        name="dots",
    )(sent, far_side)
    packed = exchange(packed, "dp", shards)
    dots = [x[0:rows] for x in packed]
    dots = (dots[0] + dots[1]) + (dots[2] + dots[3])
    slopes, dots = lax.optimization_barrier((slopes, dots))
    dots = exchange(dots, "mp", parts)
    slopes = [slopes, lax.ppermute(slopes, "dp", other_y)]
    embeddings, losses, update = pl.pallas_call(
        functools.partial(
            score_kernel, texts=texts, stripes=pl.cdiv(FIRST, STRIPE), negatives=negatives
        ),
        out_shape=[
            jax.ShapeDtypeStruct((1, per_shard, part_width), jnp.bfloat16),
            jax.ShapeDtypeStruct((1, per_shard), jnp.float32),
            jax.ShapeDtypeStruct((ROWS, part_width // 2), jnp.float32),
        ],
        in_specs=[vmem_spec()] * 11 + [smem_spec()],
        out_specs=[vmem_spec()] * 3,
        compiler_params=modest,
        name="score",
    )(*packed, *slopes, *dots, misc, logit_sharpness)
    other = lax.ppermute(update, "dp", other_core)
    core = lax.rem(lax.axis_index("dp"), 2)
    halves = [jnp.where(core == 0, update, other), jnp.where(core == 0, other, update)]
    return (embeddings, losses, jnp.concatenate(halves, axis=1))


def body(words, hard, vocabulary, weight, lowering, raising, sharpness):
    shards, parts = lax.axis_size("dp"), lax.axis_size("mp")
    texts, length = words.shape[1:]
    features, vocab = vocabulary.shape
    negatives = hard.shape[1]
    square = shards == 4 and features == weight.shape[1] == 4 * STRIPE and parts == shards
    small = texts <= ROWS - 2 and length == LANES and FIRST < texts * length <= 2048
    even = (texts * length - FIRST) % CHUNK == 0 and vocab % IDS_PER_BLOCK == 0
    fits = features * vocab <= 2**24 and features % (4 * LANES) == 0
    spare = pl.cdiv(FIRST, STRIPE) + negatives <= ROWS and lowering.shape[0] == ROWS
    fast = square and small and even and fits and spare and lax.axis_size("group") == 2
    chosen = split_body if fast else general_body
    return chosen(words, hard, vocabulary, weight, lowering, raising, sharpness)


def solution(mesh):
    in_specs = (
        P("group", None, None),
        P("dp", None),
        P("dp", None),
        P("dp", "mp"),
        P(),
        P(None, "mp"),
        P(),
    )
    out_specs = (P("group", "dp", "mp"), P("group", "dp"), P(None, "mp"))
    return jax.shard_map(body, mesh=mesh, in_specs=in_specs, out_specs=out_specs, check_vma=False)
```

```python
import functools

import jax
import jax.numpy as jnp
from jax import lax
from jax.experimental import pallas as pl
from jax.experimental.pallas import tpu as pltpu
from jax.sharding import PartitionSpec as P


def general_body(
    query_passage_words,
    difficult_distractors,
    vocabulary_vectors,
    layer_weight_matrix,
    lowering_factor_matrix,
    raising_factor_matrix,
    logit_sharpness,
):
    group_index = lax.axis_index("group")
    shard_index = lax.axis_index("dp")
    part_index = lax.axis_index("mp")
    shard_count = lax.axis_size("dp")
    side_ids = query_passage_words[0]
    text_count = side_ids.shape[0]
    length = side_ids.shape[1]
    per_shard = text_count // shard_count
    own_ids = lax.dynamic_slice_in_dim(side_ids, shard_index * per_shard, per_shard, 0)
    columns = jnp.take(vocabulary_vectors, side_ids.reshape(-1), axis=1)
    inputs = lax.all_to_all(columns, "dp", split_axis=1, concat_axis=0, tiled=True)
    tokens = inputs.shape[1]
    feature_width = raising_factor_matrix.shape[1]
    wide_inputs = inputs.astype(jnp.float32)
    inverse = lax.rsqrt(jnp.mean(wide_inputs * wide_inputs, axis=0) + 1e-05)
    normed_state = (wide_inputs * inverse[None, :]).astype(jnp.bfloat16)
    linear_map = lax.dot_general(
        lax.all_gather(layer_weight_matrix, "dp", axis=0, tiled=True),
        normed_state,
        (((0,), (0,)), ((), ())),
        preferred_element_type=jnp.float32,
    )
    reduced_sum = jnp.dot(
        lowering_factor_matrix, normed_state, preferred_element_type=jnp.float32
    ).astype(jnp.bfloat16)
    linear_map = linear_map + lax.dot_general(
        raising_factor_matrix,
        reduced_sum,
        (((0,), (0,)), ((), ())),
        preferred_element_type=jnp.float32,
    )
    own_inputs = lax.dynamic_slice_in_dim(
        inputs, part_index * feature_width, feature_width, 0
    ).astype(jnp.float32)
    hidden_state = own_inputs + jax.nn.silu(linear_map)
    mask = (own_ids != 0).astype(jnp.float32)
    counts = jnp.sum(mask, axis=1)
    summed = jnp.einsum("dnl,nl->nd", hidden_state.reshape(feature_width, per_shard, length), mask)
    pooled = (summed / counts[:, None]).astype(jnp.bfloat16)
    gathered = lax.all_gather(pooled, ("group", "dp"), axis=0, tiled=True)
    part_scores = lax.dot_general(
        pooled, gathered, (((1,), (1,)), ((), ())), preferred_element_type=jnp.float32
    )
    gathered_wide = gathered.astype(jnp.float32)
    part_norms = jnp.sum(gathered_wide * gathered_wide, axis=1)
    dots, norms = lax.psum((part_scores, part_norms), "mp")
    rnorm_all = lax.rsqrt(norms + 1e-06)
    all_count = gathered.shape[0]
    half_count = all_count // 2
    own_rows = (
        group_index * half_count + shard_index * per_shard + jnp.arange(per_shard, dtype=jnp.int32)
    )
    rnorm_own = jnp.take(rnorm_all, own_rows)
    cosine = dots * rnorm_own[:, None] * rnorm_all[None, :]
    multiplier_factor = logit_sharpness[0]
    scores = multiplier_factor * cosine
    column_ids = jnp.arange(all_count, dtype=jnp.int32)
    keep = column_ids[None, :] != own_rows[:, None]
    pair = (own_rows + half_count) % all_count
    weight = (group_index == 0).astype(jnp.float32)
    neg_cols = half_count + difficult_distractors
    top = jnp.max(jnp.where(keep, scores, -jnp.inf), axis=1)
    safe_scores = jnp.where(keep, scores, top[:, None])
    expd = jnp.where(keep, jnp.exp(safe_scores - top[:, None]), 0.0)
    neg_exp = (
        jnp.exp(jnp.minimum(jnp.take_along_axis(scores, neg_cols, axis=1) - top[:, None], 0.0))
        * weight
    )
    total = jnp.sum(expd, axis=1) + jnp.sum(neg_exp, axis=1)
    pair_score = jnp.take_along_axis(scores, pair[:, None], axis=1)[:, 0]
    losses = top + jnp.log(total) - pair_score
    onehot = (column_ids[None, None, :] == neg_cols[:, :, None]).astype(jnp.float32)
    probs = (expd + jnp.einsum("rk,rkc->rc", neg_exp, onehot)) / total[:, None]
    target = (column_ids[None, :] == pair[:, None]).astype(jnp.float32)
    grad_scores = (probs - target) / all_count
    coeff = (grad_scores * rnorm_own[:, None] * rnorm_all[None, :]).astype(jnp.bfloat16)
    along = jnp.dot(coeff, gathered, preferred_element_type=jnp.float32)
    pooled_wide = pooled.astype(jnp.float32)
    radial = jnp.sum(grad_scores * cosine, axis=1) * rnorm_own * rnorm_own
    embedding_gradient = multiplier_factor * (along - radial[:, None] * pooled_wide)
    token_grad = jnp.einsum("nd,nl->dnl", embedding_gradient / counts[:, None], mask).reshape(
        feature_width, tokens
    )
    sigma = jax.nn.sigmoid(linear_map)
    local = (token_grad * sigma * (1.0 + linear_map * (1.0 - sigma))).astype(jnp.bfloat16)
    up_portion = lax.dot_general(
        reduced_sum, local, (((1,), (1,)), ((), ())), preferred_element_type=jnp.float32
    )
    adapter_up_gradient = lax.psum(up_portion, ("group", "dp"))
    embeddings = (pooled_wide * rnorm_own[:, None]).astype(jnp.bfloat16)[None]
    return (embeddings, losses[None], adapter_up_gradient)


BLOCK_BITS, GROUP_BITS, LANE_BITS, ROW_BITS = 10, 9, 7, 4
IDS_PER_BLOCK = 1 << BLOCK_BITS
IDS_PER_GROUP = 1 << GROUP_BITS
CHUNK = 384
STRIPE = 256
ROWS = 1 << ROW_BITS
LANES = 1 << LANE_BITS
FEATURE_ROWS = 128
FIRST = 1152
TAKEN = 768
NT = (((1,), (1,)), ((), ()))
LARGE_VMEM, MODEST_VMEM = 44 * 1024 * 1024, 15 * 1024 * 1024


def mm(a, b, dims=(((1,), (0,)), ((), ()))):
    return lax.dot_general(a, b, dims, preferred_element_type=jnp.float32)


def split(x):
    high = x.astype(jnp.bfloat16)
    return high, (x - high.astype(jnp.float32)).astype(jnp.bfloat16)


def iota(shape, dim):
    return lax.broadcasted_iota(jnp.int32, shape, dim)


def quarter_of(dp_index, cores=2):
    return (dp_index % cores) * 2 + dp_index // cores


def split_quarter(i, j, cores=2):
    shard = lax.axis_index("dp")
    core, side_y = lax.rem(shard, cores), lax.div(shard, cores)
    return (core ^ i) * 2 + (side_y ^ j)


def take_lanes(x, lanes):
    numbers = lax.GatherDimensionNumbers(
        offset_dims=(),
        collapsed_slice_dims=(1,),
        start_index_map=(1,),
        operand_batching_dims=(0,),
        start_indices_batching_dims=(0,),
    )
    mode = lax.GatherScatterMode.PROMISE_IN_BOUNDS
    return lax.gather(x, lanes[..., None], numbers, slice_sizes=(1, 1), mode=mode)


def fetch(pairs, sems):
    copies = [pltpu.make_async_copy(a, b, sems.at[n]) for n, (a, b) in enumerate(pairs)]
    for copy in copies:
        copy.start()
    for copy in copies:
        copy.wait()


def gather_kernel(
    ids_ref,
    vocab_ref,
    weight_ref,
    turned_any,
    member_any,
    weight_any,
    turned,
    member_ref,
    held,
    token_ref,
    ranks,
    counted,
    bounds,
    held_sems,
    bounds_sem,
    out_sems,
    weight_sem,
    base,
):
    texts, length = ids_ref.shape
    features, vocab = vocab_ref.shape
    blocks = vocab // IDS_PER_BLOCK
    groups = vocab // IDS_PER_GROUP
    span = member_ref.shape[0]

    def vocab_copy(b):
        columns = pl.ds(pl.multiple_of(b * IDS_PER_BLOCK, LANES), IDS_PER_BLOCK)
        return pltpu.make_async_copy(vocab_ref.at[:, columns], held.at[b], held_sems.at[b])

    weight_copy = pltpu.make_async_copy(weight_ref, weight_any, weight_sem)
    vocab_copy(0).start()
    weight_copy.start()
    for b in range(1, blocks):
        vocab_copy(b).start()

    ids = ids_ref[...]
    valid = ids != 0
    group_of = jnp.where(valid, lax.shift_right_logical(ids, GROUP_BITS), groups)
    group_rows = counted.shape[0]
    group_id = iota((group_rows, length), 0)
    below = jnp.zeros((group_rows, length), jnp.float32)
    for text in range(texts):
        below += jnp.where(group_of[text : text + 1] < group_id, 1.0, 0.0)
    before = jnp.broadcast_to(jnp.sum(below, axis=1, keepdims=True), (group_rows, length))
    counted[...] = before.astype(jnp.int32)
    bounds_copy = pltpu.make_async_copy(counted, bounds, bounds_sem)
    bounds_copy.start()
    earlier = jnp.where(iota((length, length), 0) < iota((length, length), 1), 1.0, 0.0).astype(
        jnp.bfloat16
    )
    for text in range(texts):
        here = jnp.where(group_of[text : text + 1] == group_id, 1.0, 0.0)
        inside = mm(here.astype(jnp.bfloat16), earlier)
        ranks[pl.ds(text, 1), :] = jnp.sum(here * (inside + before), axis=0, keepdims=True)
        before += jnp.broadcast_to(jnp.sum(here, axis=1, keepdims=True), (group_rows, length))
    text_of = iota((texts, length), 0)
    carried = jnp.where(valid, lax.shift_left(ids, ROW_BITS) + text_of, 0).astype(jnp.float32)
    rank = ranks[...]

    def place(p, carry):
        position = (iota((LANES, length), 0) + (p * LANES + base)).astype(jnp.float32)
        total = jnp.zeros((LANES, length), jnp.float32)
        for text in range(texts):
            total += jnp.where(rank[text : text + 1] == position, carried[text : text + 1], 0.0)
        found = jnp.broadcast_to(jnp.sum(total, axis=1, keepdims=True), (LANES, LANES))
        start = pl.multiple_of(p * LANES, LANES)
        row = found.T[0:1].astype(jnp.int32)
        token = lax.shift_right_logical(row, ROW_BITS)
        token_ref[pl.ds(p, 1), :] = jnp.where(token == 0, -vocab, token)
        found = found.astype(jnp.int32)
        real = (found >= ROWS) & ((found & (ROWS - 1)) == iota((LANES, LANES), 1))
        member_ref[pl.ds(start, LANES), :] = jnp.where(real, 1.0, 0.0).astype(jnp.bfloat16)
        turned[:, pl.ds(start, LANES)] = jnp.zeros((features, LANES), jnp.bfloat16)
        return carry

    lax.fori_loop(0, span // LANES, place, 0)
    bounds_copy.wait()

    def within(place):
        return jnp.clip(place - base, 0, span)

    def take(b, carry):
        vocab_copy(b).wait()
        for part in range(IDS_PER_BLOCK // IDS_PER_GROUP):
            group = b * (IDS_PER_BLOCK // IDS_PER_GROUP) + part
            first, last = within(bounds[group, 0]), within(bounds[group + 1, 0])
            begin = lax.shift_right_logical(first, LANE_BITS)
            end = lax.shift_right_logical(last + LANES - 1, LANE_BITS)

            def window(p, carry):
                at = pl.ds(pl.multiple_of(p * LANES, LANES), LANES)
                token = token_ref[pl.ds(p, 1), :] - group * IDS_PER_GROUP
                token = jnp.broadcast_to(token, (FEATURE_ROWS, LANES))
                lane = (token & (LANES - 1)).astype(jnp.int16)
                tile = lax.shift_right_arithmetic(token, LANE_BITS).astype(jnp.int16)
                pieces = [pl.ds(f, FEATURE_ROWS) for f in range(0, TAKEN, FEATURE_ROWS)]
                short = jnp.broadcast_to(token[0:1], (IDS_PER_GROUP, LANES)).astype(jnp.int16)
                picked = jnp.where(
                    short == iota((IDS_PER_GROUP, LANES), 0).astype(jnp.int16), 1.0, 0.0
                ).astype(jnp.bfloat16)
                columns = pl.ds(part * IDS_PER_GROUP, IDS_PER_GROUP)
                rest = pl.ds(TAKEN, features - TAKEN)
                product = mm(held[b, rest, columns], picked).astype(jnp.bfloat16)
                fresh = []
                for rows in pieces:
                    total = jnp.zeros((FEATURE_ROWS, LANES), jnp.bfloat16)
                    for j in range(IDS_PER_GROUP // LANES):
                        columns = pl.ds(part * IDS_PER_GROUP + j * LANES, LANES)
                        total = jnp.where(tile == j, take_lanes(held[b, rows, columns], lane), total)
                    fresh.append(total)
                pieces.append(rest)
                fresh.append(product)
                fresh = [turned[rows, at] + total for rows, total in zip(pieces, fresh)]
                for rows, total in zip(pieces, fresh):
                    turned[rows, at] = total
                return carry

            lax.fori_loop(begin, jnp.where(last > first, end, begin), window, 0)
        return carry

    lax.fori_loop(0, blocks, take, 0)
    fetch([(turned, turned_any), (member_ref, member_any)], out_sems)
    weight_copy.wait()


def statistics_kernel(
    turned_any, member_any, hard_ref, lower_ref, extra_ref, small, turned, member_ref, spread, sems
):
    fetch([(turned_any, turned), (member_any, member_ref)], sems)
    features, span = turned.shape
    stripes = pl.cdiv(span, STRIPE)
    per_shard, negatives = hard_ref.shape
    shard = lax.axis_index("dp")
    small[...] = jnp.zeros_like(small)
    small[0:per_shard, stripes : stripes + negatives] = hard_ref[...].astype(jnp.float32)
    lower = lower_ref[:, pl.ds(pl.multiple_of(shard * features, LANES), features)]

    misc = jnp.zeros((ROWS, STRIPE), jnp.float32)
    residual = jnp.zeros((features, LANES), jnp.float32)
    for stripe in range(stripes):
        size = min(STRIPE, span - stripe * STRIPE)
        across = pl.ds(stripe * STRIPE, size)
        upright = turned[:, across]
        wide = upright.astype(jnp.float32)
        square = jnp.sum(wide * wide, axis=0, keepdims=True)
        reduced = mm(lower, upright)
        if size < STRIPE:
            none = jnp.zeros((ROWS, STRIPE - size), jnp.float32)
            reduced = jnp.concatenate([reduced, none], axis=1)
            square = jnp.concatenate([square, none[0:1]], axis=1)
        extra_ref[stripe * ROWS : (stripe + 1) * ROWS, :] = reduced.astype(jnp.bfloat16)
        misc = jnp.where(iota((ROWS, STRIPE), 0) == stripe, square, misc)
        residual += mm(upright, member_ref[across, :])
    hard = small[...].T[0:ROWS]
    for i in range(per_shard):
        misc += jnp.where(iota((ROWS, STRIPE), 1) == shard * per_shard + i, hard[:, i : i + 1], 0.0)
    extra_ref[stripes * ROWS : (stripes + 1) * ROWS, :] = misc.astype(jnp.bfloat16)
    residual = jnp.where(lax.axis_index("mp") == shard, residual.T[0:ROWS], 0.0)
    spread[...] = residual
    for q in range(4):
        start = (stripes + 1 + q) * ROWS
        quarter = pl.multiple_of(split_quarter(q // 2, q % 2) * STRIPE, LANES)
        extra_ref[start : start + ROWS, :] = spread[:, pl.ds(quarter, STRIPE)].astype(jnp.bfloat16)


def pool_kernel(
    ids_ref,
    own_ref,
    core_any,
    far_any,
    extra_ref,
    member_ref,
    own_rest,
    core_rest,
    far_rest,
    extra_rest,
    member_rest,
    raise_ref,
    sent_ref,
    misc_ref,
    raised,
    total,
    slopes,
    core_ref,
    far_ref,
    sems,
    model_width,
):
    texts, length = ids_ref.shape
    width = own_ref.shape[1]
    quarter = quarter_of(lax.axis_index("dp"))
    fetch([(core_any, core_ref), (far_any, far_ref)], sems)
    raised[...] = jnp.zeros_like(raised)
    raised[0:ROWS, :] = raise_ref[:, pl.ds(pl.multiple_of(quarter * width, LANES), width)]
    total[...] = jnp.zeros_like(total)
    slopes[...] = jnp.zeros_like(slopes)

    def add(refs, extra_ref, member_ref, base):
        span = member_ref.shape[0]
        stripes = pl.cdiv(span, STRIPE)

        def summed(start, size):
            return sum(ref[pl.ds(start, size), :].astype(jnp.float32) for ref in refs)

        misc = extra_ref[stripes * ROWS : (stripes + 1) * ROWS, :]
        if base == 0:
            misc_ref[...] = misc
        inverse = lax.rsqrt(misc / model_width + 1e-05)
        for k in range(stripes):
            size = min(STRIPE, span - k * STRIPE)
            scale = inverse[k : k + 1]
            reduced = (extra_ref[k * ROWS : (k + 1) * ROWS, :] * scale).astype(jnp.bfloat16)
            reduced = reduced.astype(jnp.float32)
            stacked = jnp.concatenate([reduced, jnp.broadcast_to(scale, (LANES - ROWS, STRIPE))])
            turned = stacked[:, 0:size].T
            low = turned.astype(jnp.bfloat16)
            linear = summed(k * STRIPE, size)
            linear = linear * turned[:, ROWS : ROWS + 1] + mm(low, raised[...])
            sigma = 1.0 / (1.0 + jnp.exp(-linear))
            slope = (sigma * (1.0 + linear * (1.0 - sigma))).astype(jnp.bfloat16)
            member = member_ref[pl.ds(k * STRIPE, size), :].astype(jnp.float32).T
            high, rest = split(linear * sigma)
            chosen = member[0:ROWS].astype(jnp.bfloat16)
            total[...] += mm(chosen, high) + mm(chosen, rest)
            spread = [reduced[:, 0:size] * member[text : text + 1] for text in range(texts)]
            slopes[...] += mm(jnp.concatenate(spread).astype(jnp.bfloat16), slope)
        total[...] += extra_ref[(stripes + 1) * ROWS : (stripes + 2) * ROWS, :]

    add((own_ref, core_ref, far_ref), extra_ref, member_ref, 0)
    real = (ids_ref[...] != 0).astype(jnp.float32)

    @pl.when(jnp.sum(real) > member_ref.shape[0])
    def _():
        add((own_rest, core_rest, far_rest), extra_rest, member_rest, member_ref.shape[0])

    counts = jnp.sum(real, axis=1, keepdims=True)
    pooled = total[0:texts] / counts
    pooled = jnp.concatenate([pooled, jnp.zeros((ROWS - texts, width), jnp.float32)])
    sent_ref[0:ROWS, :] = pooled.astype(jnp.bfloat16)
    for text in range(texts):
        part = slopes[text * ROWS : (text + 1) * ROWS, :] / counts[text : text + 1]
        sent_ref[(text + 1) * ROWS : (text + 2) * ROWS, :] = part.astype(jnp.bfloat16)


def both_sides(near, far):
    queries = lax.axis_index("group") == 0
    return jnp.concatenate([jnp.where(queries, near, far), jnp.where(queries, far, near)], axis=0)


def dots_kernel(near_ref, far_ref, packed_ref, slopes_ref):
    block = both_sides(near_ref[0:ROWS], far_ref[0:ROWS])
    rows = 2 * ROWS
    packed_ref[...] = jnp.zeros_like(packed_ref)
    packed_ref[0:rows, 0:rows] = mm(block, block, NT)
    for part in range(block.shape[1] // LANES):
        piece = block[:, part * LANES : (part + 1) * LANES]
        packed_ref[rows + part * rows : rows + (part + 1) * rows, :] = piece.astype(jnp.float32)
    size = near_ref.shape[0] - ROWS
    slopes_ref[0:size] = near_ref[ROWS:]
    slopes_ref[size:] = far_ref[ROWS:]


def score_kernel(*refs, texts, stripes, negatives):
    packed0, packed1, packed2, packed3, slopes0, slopes2 = refs[0:6]
    dots0, dots1, dots2, dots3, misc_ref, sharp_ref = refs[6:12]
    embed_ref, loss_ref, up_ref = refs[12:15]
    rows = 2 * ROWS
    per_shard = loss_ref.shape[1]
    group, shard = lax.axis_index("group"), lax.axis_index("dp")
    dots = ((dots0[...] + dots1[...]) + (dots2[...] + dots3[...]))[:, 0:rows]
    down, across = iota((rows, rows), 0), iota((rows, rows), 1)
    same = down == across
    real = (lax.rem(down, ROWS) < texts) & (lax.rem(across, ROWS) < texts)
    diagonal = jnp.where(same, dots, 0.0)
    rnorm_row = lax.rsqrt(jnp.sum(diagonal, axis=0, keepdims=True) + 1e-06)
    rnorm_col = lax.rsqrt(jnp.sum(diagonal, axis=1, keepdims=True) + 1e-06)
    sharpness = sharp_ref[0]
    cosine = dots * rnorm_col * rnorm_row
    scores = sharpness * cosine
    keep = real & ~same
    top = jnp.max(jnp.where(keep, scores, -jnp.inf), axis=0, keepdims=True)
    top = jnp.where(lax.rem(across[0:1], ROWS) < texts, top, 0.0)
    powers = jnp.exp(jnp.where(real, jnp.minimum(scores - top, 0.0), 0.0))
    hard = misc_ref[stripes : stripes + negatives, 0:rows].astype(jnp.int32) + ROWS
    times = jnp.zeros((rows, rows), jnp.float32)
    for k in range(negatives):
        times += jnp.where(hard[k : k + 1] == down, 1.0, 0.0)
    times = jnp.where(across < texts, times, 0.0)
    weights = (jnp.where(keep, 1.0, 0.0) + jnp.where(real, times, 0.0)) * powers
    total = jnp.sum(weights, axis=0, keepdims=True)
    total = jnp.where(lax.rem(across[0:1], ROWS) < texts, total, 1.0)
    pair = (down == lax.rem(across + ROWS, rows)) & real
    pair_score = jnp.sum(jnp.where(pair, scores, 0.0), axis=0, keepdims=True)
    losses = top + jnp.log(total) - pair_score
    grad_scores = (weights / total - jnp.where(pair, 1.0, 0.0)) / (2 * texts)
    coeff = (grad_scores * rnorm_col * rnorm_row).astype(jnp.bfloat16)
    radial = jnp.sum(grad_scores * cosine, axis=0, keepdims=True) * rnorm_row * rnorm_row

    first = shard * per_shard
    loss_col = jnp.sum(jnp.where(same, losses, 0.0), axis=1, keepdims=True)
    at = (iota((rows, LANES), 0) == group * ROWS + first + iota((rows, LANES), 1)) & (
        iota((rows, LANES), 1) < per_shard
    )
    loss_ref[...] = jnp.sum(jnp.where(at, loss_col, 0.0), axis=0, keepdims=True)[:, 0:per_shard]

    along_rows = coeff.astype(jnp.float32).T.astype(jnp.bfloat16)
    radial_col = jnp.sum(jnp.where(same, radial, 0.0), axis=1, keepdims=True)
    rnorm_own = jnp.where(group == 0, rnorm_col[0:ROWS], rnorm_col[ROWS:rows])
    chosen = iota((ROWS, ROWS), 1) == iota((ROWS, ROWS), 0) + first
    chosen = jnp.where(chosen & (iota((ROWS, ROWS), 0) < per_shard), 1.0, 0.0).astype(jnp.bfloat16)
    blocks = ((packed0, slopes0), (packed1, None), (packed2, slopes2), (packed3, None))
    for o, (packed, slopes) in enumerate(blocks):
        parts = packed.shape[0] // rows - 1
        width = parts * LANES
        halves = [packed[rows * (part + 1) : rows * (part + 2), :] for part in range(parts)]
        block = jnp.concatenate(halves, axis=1)
        queries = group == 0
        at = pl.multiple_of(quarter_of(shard ^ o) * width, LANES)
        own = jnp.where(queries, block[0:ROWS], block[ROWS:rows]) * rnorm_own
        picked = mm(chosen, own.astype(jnp.bfloat16)).astype(jnp.bfloat16)
        embed_ref[0, :, pl.ds(at, width)] = picked[0:per_shard]
        if slopes is None:
            continue
        along = mm(along_rows, block.astype(jnp.bfloat16))
        grad = sharpness * (along - radial_col * block)
        near, far = slopes[0 : slopes.shape[0] // 2], slopes[slopes.shape[0] // 2 :]
        grad_near = jnp.where(queries, grad[0:ROWS], grad[ROWS:rows])
        grad_far = jnp.where(queries, grad[ROWS:rows], grad[0:ROWS])
        update = []
        for side, side_grad in ((near, grad_near), (far, grad_far)):
            total = jnp.zeros((ROWS, width), jnp.float32)
            for text in range(texts):
                slope = side[text * ROWS : (text + 1) * ROWS].astype(jnp.float32)
                total += side_grad[text : text + 1] * slope
            update.append(total)
        at = pl.multiple_of((lax.div(shard, 2) ^ (o // 2)) * width, LANES)
        up_ref[:, pl.ds(at, width)] = update[0] + update[1]


def any_spec():
    return pl.BlockSpec(memory_space=pl.ANY)


def vmem_spec():
    return pl.BlockSpec(memory_space=pltpu.VMEM)


def smem_spec():
    return pl.BlockSpec(memory_space=pltpu.SMEM)


def exchange(x, axis, size):
    steps = [[(i, i ^ o) for i in range(size)] for o in range(1, size)]
    return [x] + [lax.ppermute(x, axis, step) for step in steps]


def split_body(
    query_passage_words,
    difficult_distractors,
    vocabulary_vectors,
    layer_weight_matrix,
    lowering_factor_matrix,
    raising_factor_matrix,
    logit_sharpness,
):
    shards, parts = lax.axis_size("dp"), lax.axis_size("mp")
    ids = query_passage_words[0]
    texts, length = ids.shape
    tokens = texts * length
    features, vocab = vocabulary_vectors.shape
    blocks = vocab // IDS_PER_BLOCK
    group_rows = 8 * pl.cdiv(vocab // IDS_PER_GROUP + 1, 8)
    per_shard, negatives = difficult_distractors.shape
    part_width = layer_weight_matrix.shape[1]
    width = part_width // shards
    params = pltpu.CompilerParams(vmem_limit_bytes=LARGE_VMEM)
    modest = pltpu.CompilerParams(vmem_limit_bytes=MODEST_VMEM)
    other_core = [(d, d ^ 1) for d in range(shards)]
    other_y = [(d, d ^ 2) for d in range(shards)]

    def columns(weight, i, j):
        return lax.dynamic_slice(weight, (0, split_quarter(i, j) * width), (features, width))

    def project(base, span):
        stripes = pl.cdiv(span, STRIPE)
        extra_rows = (stripes + 1 + shards) * ROWS
        turned, member, weight = pl.pallas_call(
            functools.partial(gather_kernel, base=base),
            out_shape=[
                jax.ShapeDtypeStruct((features, span), jnp.bfloat16),
                jax.ShapeDtypeStruct((span, LANES), jnp.bfloat16),
                jax.ShapeDtypeStruct(layer_weight_matrix.shape, jnp.bfloat16),
            ],
            in_specs=[vmem_spec()] + [any_spec()] * 2,
            out_specs=[any_spec()] * 3,
            scratch_shapes=[
                pltpu.VMEM((features, span), jnp.bfloat16),
                pltpu.VMEM((span, LANES), jnp.bfloat16),
                pltpu.VMEM((blocks, features, IDS_PER_BLOCK), jnp.bfloat16),
                pltpu.VMEM((8 * pl.cdiv(span // LANES, 8), LANES), jnp.int32),
                pltpu.VMEM((texts, length), jnp.float32),
                pltpu.VMEM((group_rows, length), jnp.int32),
                pltpu.SMEM((group_rows, length), jnp.int32),
                pltpu.SemaphoreType.DMA((blocks,)),
                pltpu.SemaphoreType.DMA,
                pltpu.SemaphoreType.DMA((2,)),
                pltpu.SemaphoreType.DMA,
            ],
            compiler_params=params,
            name="gather",
        )(ids, vocabulary_vectors, layer_weight_matrix)

        def product(turned, i, j):
            return mm(turned, columns(weight, i, j), (((0,), (0,)), ((), ())))

        def narrow(x):
            return x.astype(jnp.bfloat16)

        core1 = lax.ppermute(narrow(product(turned, 1, 1)), "dp", other_core)
        own1 = lax.optimization_barrier(narrow(product(turned, 0, 1)))
        chip1 = narrow(own1.astype(jnp.float32) + core1.astype(jnp.float32))
        far = lax.ppermute(chip1, "dp", other_y)
        turned, _ = lax.optimization_barrier((turned, chip1))
        extra = pl.pallas_call(
            statistics_kernel,
            out_shape=jax.ShapeDtypeStruct((extra_rows, STRIPE), jnp.bfloat16),
            in_specs=[any_spec()] * 2 + [vmem_spec()] * 2,
            out_specs=vmem_spec(),
            scratch_shapes=[
                pltpu.VMEM((LANES, LANES), jnp.float32),
                pltpu.VMEM(turned.shape, turned.dtype),
                pltpu.VMEM(member.shape, member.dtype),
                pltpu.VMEM((ROWS, features), jnp.float32),
                pltpu.SemaphoreType.DMA((2,)),
            ],
            compiler_params=modest,
            cost_estimate=pl.CostEstimate(
                flops=2 * features * span * (ROWS + LANES),
                bytes_accessed=2 * features * span,
                transcendentals=0,
            ),
            name="statistics",
        )(turned, member, difficult_distractors, lowering_factor_matrix)
        common = (stripes + 1) * ROWS
        near = extra.astype(jnp.float32)
        across = lax.ppermute(extra, "dp", other_core).astype(jnp.float32)
        chip = near[0:common] + across[0:common]
        inputs = near[common : common + 2 * ROWS] + across[common + 2 * ROWS :]
        sent = narrow(jnp.concatenate([chip, inputs[ROWS:]]))
        sent = lax.ppermute(sent, "dp", other_y).astype(jnp.float32)
        extra = jnp.concatenate([chip, inputs[0:ROWS]]) + sent
        core0 = lax.ppermute(narrow(product(turned, 1, 0)), "dp", other_core)
        own0 = narrow(product(turned, 0, 0))
        return own0, core0, far, extra, member

    first = project(0, FIRST)
    later, _ = lax.optimization_barrier((ids, first[0]))
    many = jnp.sum((later != 0).astype(jnp.int32)) > FIRST
    left = tokens - FIRST
    shapes = jax.eval_shape(lambda: project(FIRST, left))
    rest = lax.cond(
        many,
        lambda: project(FIRST, left),
        lambda: tuple(jnp.zeros(x.shape, x.dtype) for x in shapes),
    )
    sent, misc = pl.pallas_call(
        functools.partial(pool_kernel, model_width=float(features * shards)),
        out_shape=[
            jax.ShapeDtypeStruct(((texts + 1) * ROWS, width), jnp.bfloat16),
            jax.ShapeDtypeStruct((ROWS, width), jnp.float32),
        ],
        in_specs=[vmem_spec()] * 2 + [any_spec()] * 2 + [vmem_spec()] * 8,
        out_specs=[vmem_spec()] * 2,
        scratch_shapes=[
            pltpu.VMEM((LANES, width), jnp.bfloat16),
            pltpu.VMEM((ROWS, width), jnp.float32),
            pltpu.VMEM((texts * ROWS, width), jnp.float32),
            pltpu.VMEM((FIRST, width), jnp.bfloat16),
            pltpu.VMEM((FIRST, width), jnp.bfloat16),
            pltpu.SemaphoreType.DMA((2,)),
        ],
        compiler_params=modest,
        name="pool",
    )(ids, *first, *rest, raising_factor_matrix)
    far_side = lax.ppermute(sent, "group", [(0, 1), (1, 0)])
    rows = 2 * ROWS
    packed, slopes = pl.pallas_call(
        dots_kernel,
        out_shape=[
            jax.ShapeDtypeStruct((rows + width // LANES * rows, LANES), jnp.float32),
            jax.ShapeDtypeStruct((2 * texts * ROWS, width), jnp.bfloat16),
        ],
        in_specs=[vmem_spec()] * 2,
        out_specs=[vmem_spec()] * 2,
        compiler_params=modest,
        name="dots",
    )(sent, far_side)
    packed = exchange(packed, "dp", shards)
    dots = [x[0:rows] for x in packed]
    dots = (dots[0] + dots[1]) + (dots[2] + dots[3])
    slopes, dots = lax.optimization_barrier((slopes, dots))
    dots = exchange(dots, "mp", parts)
    slopes = [slopes, lax.ppermute(slopes, "dp", other_y)]
    embeddings, losses, update = pl.pallas_call(
        functools.partial(
            score_kernel, texts=texts, stripes=pl.cdiv(FIRST, STRIPE), negatives=negatives
        ),
        out_shape=[
            jax.ShapeDtypeStruct((1, per_shard, part_width), jnp.bfloat16),
            jax.ShapeDtypeStruct((1, per_shard), jnp.float32),
            jax.ShapeDtypeStruct((ROWS, part_width // 2), jnp.float32),
        ],
        in_specs=[vmem_spec()] * 11 + [smem_spec()],
        out_specs=[vmem_spec()] * 3,
        compiler_params=modest,
        name="score",
    )(*packed, *slopes, *dots, misc, logit_sharpness)
    other = lax.ppermute(update, "dp", other_core)
    core = lax.rem(lax.axis_index("dp"), 2)
    halves = [jnp.where(core == 0, update, other), jnp.where(core == 0, other, update)]
    return (embeddings, losses, jnp.concatenate(halves, axis=1))


def body(words, hard, vocabulary, weight, lowering, raising, sharpness):
    shards, parts = lax.axis_size("dp"), lax.axis_size("mp")
    texts, length = words.shape[1:]
    features, vocab = vocabulary.shape
    negatives = hard.shape[1]
    square = shards == 4 and features == weight.shape[1] == 4 * STRIPE and parts == shards
    small = texts <= ROWS - 2 and length == LANES and FIRST < texts * length <= 2048
    even = (texts * length - FIRST) % CHUNK == 0 and vocab % IDS_PER_BLOCK == 0
    fits = features * vocab <= 2**24 and features % (4 * LANES) == 0
    spare = pl.cdiv(FIRST, STRIPE) + negatives <= ROWS and lowering.shape[0] == ROWS
    fast = square and small and even and fits and spare and lax.axis_size("group") == 2
    chosen = split_body if fast else general_body
    return chosen(words, hard, vocabulary, weight, lowering, raising, sharpness)


def solution(mesh):
    in_specs = (
        P("group", None, None),
        P("dp", None),
        P("dp", None),
        P("dp", "mp"),
        P(),
        P(None, "mp"),
        P(),
    )
    out_specs = (P("group", "dp", "mp"), P("group", "dp"), P(None, "mp"))
    return jax.shard_map(body, mesh=mesh, in_specs=in_specs, out_specs=out_specs, check_vma=False)
```

```python
import functools

import jax
import jax.numpy as jnp
from jax import lax
from jax.experimental import pallas as pl
from jax.experimental.pallas import tpu as pltpu
from jax.sharding import PartitionSpec as P


def general_body(
    query_passage_words,
    difficult_distractors,
    vocabulary_vectors,
    layer_weight_matrix,
    lowering_factor_matrix,
    raising_factor_matrix,
    logit_sharpness,
):
    group_index = lax.axis_index("group")
    shard_index = lax.axis_index("dp")
    part_index = lax.axis_index("mp")
    shard_count = lax.axis_size("dp")
    side_ids = query_passage_words[0]
    text_count = side_ids.shape[0]
    length = side_ids.shape[1]
    per_shard = text_count // shard_count
    own_ids = lax.dynamic_slice_in_dim(side_ids, shard_index * per_shard, per_shard, 0)
    columns = jnp.take(vocabulary_vectors, side_ids.reshape(-1), axis=1)
    inputs = lax.all_to_all(columns, "dp", split_axis=1, concat_axis=0, tiled=True)
    tokens = inputs.shape[1]
    feature_width = raising_factor_matrix.shape[1]
    wide_inputs = inputs.astype(jnp.float32)
    inverse = lax.rsqrt(jnp.mean(wide_inputs * wide_inputs, axis=0) + 1e-05)
    normed_state = (wide_inputs * inverse[None, :]).astype(jnp.bfloat16)
    linear_map = lax.dot_general(
        lax.all_gather(layer_weight_matrix, "dp", axis=0, tiled=True),
        normed_state,
        (((0,), (0,)), ((), ())),
        preferred_element_type=jnp.float32,
    )
    reduced_sum = jnp.dot(
        lowering_factor_matrix, normed_state, preferred_element_type=jnp.float32
    ).astype(jnp.bfloat16)
    linear_map = linear_map + lax.dot_general(
        raising_factor_matrix,
        reduced_sum,
        (((0,), (0,)), ((), ())),
        preferred_element_type=jnp.float32,
    )
    own_inputs = lax.dynamic_slice_in_dim(
        inputs, part_index * feature_width, feature_width, 0
    ).astype(jnp.float32)
    hidden_state = own_inputs + jax.nn.silu(linear_map)
    mask = (own_ids != 0).astype(jnp.float32)
    counts = jnp.sum(mask, axis=1)
    summed = jnp.einsum("dnl,nl->nd", hidden_state.reshape(feature_width, per_shard, length), mask)
    pooled = (summed / counts[:, None]).astype(jnp.bfloat16)
    gathered = lax.all_gather(pooled, ("group", "dp"), axis=0, tiled=True)
    part_scores = lax.dot_general(
        pooled, gathered, (((1,), (1,)), ((), ())), preferred_element_type=jnp.float32
    )
    gathered_wide = gathered.astype(jnp.float32)
    part_norms = jnp.sum(gathered_wide * gathered_wide, axis=1)
    dots, norms = lax.psum((part_scores, part_norms), "mp")
    rnorm_all = lax.rsqrt(norms + 1e-06)
    all_count = gathered.shape[0]
    half_count = all_count // 2
    own_rows = (
        group_index * half_count + shard_index * per_shard + jnp.arange(per_shard, dtype=jnp.int32)
    )
    rnorm_own = jnp.take(rnorm_all, own_rows)
    cosine = dots * rnorm_own[:, None] * rnorm_all[None, :]
    multiplier_factor = logit_sharpness[0]
    scores = multiplier_factor * cosine
    column_ids = jnp.arange(all_count, dtype=jnp.int32)
    keep = column_ids[None, :] != own_rows[:, None]
    pair = (own_rows + half_count) % all_count
    weight = (group_index == 0).astype(jnp.float32)
    neg_cols = half_count + difficult_distractors
    top = jnp.max(jnp.where(keep, scores, -jnp.inf), axis=1)
    safe_scores = jnp.where(keep, scores, top[:, None])
    expd = jnp.where(keep, jnp.exp(safe_scores - top[:, None]), 0.0)
    neg_exp = (
        jnp.exp(jnp.minimum(jnp.take_along_axis(scores, neg_cols, axis=1) - top[:, None], 0.0))
        * weight
    )
    total = jnp.sum(expd, axis=1) + jnp.sum(neg_exp, axis=1)
    pair_score = jnp.take_along_axis(scores, pair[:, None], axis=1)[:, 0]
    losses = top + jnp.log(total) - pair_score
    onehot = (column_ids[None, None, :] == neg_cols[:, :, None]).astype(jnp.float32)
    probs = (expd + jnp.einsum("rk,rkc->rc", neg_exp, onehot)) / total[:, None]
    target = (column_ids[None, :] == pair[:, None]).astype(jnp.float32)
    grad_scores = (probs - target) / all_count
    coeff = (grad_scores * rnorm_own[:, None] * rnorm_all[None, :]).astype(jnp.bfloat16)
    along = jnp.dot(coeff, gathered, preferred_element_type=jnp.float32)
    pooled_wide = pooled.astype(jnp.float32)
    radial = jnp.sum(grad_scores * cosine, axis=1) * rnorm_own * rnorm_own
    embedding_gradient = multiplier_factor * (along - radial[:, None] * pooled_wide)
    token_grad = jnp.einsum("nd,nl->dnl", embedding_gradient / counts[:, None], mask).reshape(
        feature_width, tokens
    )
    sigma = jax.nn.sigmoid(linear_map)
    local = (token_grad * sigma * (1.0 + linear_map * (1.0 - sigma))).astype(jnp.bfloat16)
    up_portion = lax.dot_general(
        reduced_sum, local, (((1,), (1,)), ((), ())), preferred_element_type=jnp.float32
    )
    adapter_up_gradient = lax.psum(up_portion, ("group", "dp"))
    embeddings = (pooled_wide * rnorm_own[:, None]).astype(jnp.bfloat16)[None]
    return (embeddings, losses[None], adapter_up_gradient)


BLOCK_BITS, GROUP_BITS, LANE_BITS, ROW_BITS = 10, 9, 7, 4
IDS_PER_BLOCK = 1 << BLOCK_BITS
IDS_PER_GROUP = 1 << GROUP_BITS
CHUNK = 384
STRIPE = 256
ROWS = 1 << ROW_BITS
LANES = 1 << LANE_BITS
FEATURE_ROWS = 128
FIRST = 1152
TAKEN = 768
NT = (((1,), (1,)), ((), ()))
LARGE_VMEM, MODEST_VMEM = 44 * 1024 * 1024, 15 * 1024 * 1024


def mm(a, b, dims=(((1,), (0,)), ((), ()))):
    return lax.dot_general(a, b, dims, preferred_element_type=jnp.float32)


def split(x):
    high = x.astype(jnp.bfloat16)
    return high, (x - high.astype(jnp.float32)).astype(jnp.bfloat16)


def iota(shape, dim):
    return lax.broadcasted_iota(jnp.int32, shape, dim)


def quarter_of(dp_index, cores=2):
    return (dp_index % cores) * 2 + dp_index // cores


def split_quarter(i, j, cores=2):
    shard = lax.axis_index("dp")
    core, side_y = lax.rem(shard, cores), lax.div(shard, cores)
    return (core ^ i) * 2 + (side_y ^ j)


def take_lanes(x, lanes):
    numbers = lax.GatherDimensionNumbers(
        offset_dims=(),
        collapsed_slice_dims=(1,),
        start_index_map=(1,),
        operand_batching_dims=(0,),
        start_indices_batching_dims=(0,),
    )
    mode = lax.GatherScatterMode.PROMISE_IN_BOUNDS
    return lax.gather(x, lanes[..., None], numbers, slice_sizes=(1, 1), mode=mode)


def fetch(pairs, sems):
    copies = [pltpu.make_async_copy(a, b, sems.at[n]) for n, (a, b) in enumerate(pairs)]
    for copy in copies:
        copy.start()
    for copy in copies:
        copy.wait()


def gather_kernel(
    ids_ref,
    vocab_ref,
    after_any,
    turned_any,
    member_any,
    turned,
    member_ref,
    held,
    token_ref,
    ranks,
    counted,
    bounds,
    held_sems,
    bounds_sem,
    out_sems,
    base,
):
    del after_any
    texts, length = ids_ref.shape
    features, vocab = vocab_ref.shape
    blocks = vocab // IDS_PER_BLOCK
    groups = vocab // IDS_PER_GROUP
    span = member_ref.shape[0]

    def vocab_copy(b):
        columns = pl.ds(pl.multiple_of(b * IDS_PER_BLOCK, LANES), IDS_PER_BLOCK)
        return pltpu.make_async_copy(vocab_ref.at[:, columns], held.at[b], held_sems.at[b])

    vocab_copy(0).start()
    for b in range(1, blocks):
        vocab_copy(b).start()

    ids = ids_ref[...]
    valid = ids != 0
    group_of = jnp.where(valid, lax.shift_right_logical(ids, GROUP_BITS), groups)
    group_rows = counted.shape[0]
    group_id = iota((group_rows, length), 0)
    below = jnp.zeros((group_rows, length), jnp.float32)
    for text in range(texts):
        below += jnp.where(group_of[text : text + 1] < group_id, 1.0, 0.0)
    before = jnp.broadcast_to(jnp.sum(below, axis=1, keepdims=True), (group_rows, length))
    counted[...] = before.astype(jnp.int32)
    bounds_copy = pltpu.make_async_copy(counted, bounds, bounds_sem)
    bounds_copy.start()
    earlier = jnp.where(iota((length, length), 0) < iota((length, length), 1), 1.0, 0.0).astype(
        jnp.bfloat16
    )
    for text in range(texts):
        here = jnp.where(group_of[text : text + 1] == group_id, 1.0, 0.0)
        inside = mm(here.astype(jnp.bfloat16), earlier)
        ranks[pl.ds(text, 1), :] = jnp.sum(here * (inside + before), axis=0, keepdims=True)
        before += jnp.broadcast_to(jnp.sum(here, axis=1, keepdims=True), (group_rows, length))
    text_of = iota((texts, length), 0)
    carried = jnp.where(valid, lax.shift_left(ids, ROW_BITS) + text_of, 0).astype(jnp.float32)
    rank = ranks[...]

    def place(p, carry):
        position = (iota((LANES, length), 0) + (p * LANES + base)).astype(jnp.float32)
        total = jnp.zeros((LANES, length), jnp.float32)
        for text in range(texts):
            total += jnp.where(rank[text : text + 1] == position, carried[text : text + 1], 0.0)
        found = jnp.broadcast_to(jnp.sum(total, axis=1, keepdims=True), (LANES, LANES))
        start = pl.multiple_of(p * LANES, LANES)
        row = found.T[0:1].astype(jnp.int32)
        token = lax.shift_right_logical(row, ROW_BITS)
        token_ref[pl.ds(p, 1), :] = jnp.where(token == 0, -vocab, token)
        found = found.astype(jnp.int32)
        real = (found >= ROWS) & ((found & (ROWS - 1)) == iota((LANES, LANES), 1))
        member_ref[pl.ds(start, LANES), :] = jnp.where(real, 1.0, 0.0).astype(jnp.bfloat16)
        turned[:, pl.ds(start, LANES)] = jnp.zeros((features, LANES), jnp.bfloat16)
        return carry

    lax.fori_loop(0, span // LANES, place, 0)
    bounds_copy.wait()

    def within(place):
        return jnp.clip(place - base, 0, span)

    def take(b, carry):
        vocab_copy(b).wait()
        for part in range(IDS_PER_BLOCK // IDS_PER_GROUP):
            group = b * (IDS_PER_BLOCK // IDS_PER_GROUP) + part
            first, last = within(bounds[group, 0]), within(bounds[group + 1, 0])
            begin = lax.shift_right_logical(first, LANE_BITS)
            end = lax.shift_right_logical(last + LANES - 1, LANE_BITS)

            def window(p, carry):
                at = pl.ds(pl.multiple_of(p * LANES, LANES), LANES)
                token = token_ref[pl.ds(p, 1), :] - group * IDS_PER_GROUP
                token = jnp.broadcast_to(token, (FEATURE_ROWS, LANES))
                lane = (token & (LANES - 1)).astype(jnp.int16)
                tile = lax.shift_right_arithmetic(token, LANE_BITS).astype(jnp.int16)
                pieces = [pl.ds(f, FEATURE_ROWS) for f in range(0, TAKEN, FEATURE_ROWS)]
                short = jnp.broadcast_to(token[0:1], (IDS_PER_GROUP, LANES)).astype(jnp.int16)
                picked = jnp.where(
                    short == iota((IDS_PER_GROUP, LANES), 0).astype(jnp.int16), 1.0, 0.0
                ).astype(jnp.bfloat16)
                columns = pl.ds(part * IDS_PER_GROUP, IDS_PER_GROUP)
                rest = pl.ds(TAKEN, features - TAKEN)
                product = mm(held[b, rest, columns], picked).astype(jnp.bfloat16)
                fresh = []
                for rows in pieces:
                    total = jnp.zeros((FEATURE_ROWS, LANES), jnp.bfloat16)
                    for j in range(IDS_PER_GROUP // LANES):
                        columns = pl.ds(part * IDS_PER_GROUP + j * LANES, LANES)
                        total = jnp.where(tile == j, take_lanes(held[b, rows, columns], lane), total)
                    fresh.append(total)
                pieces.append(rest)
                fresh.append(product)
                fresh = [turned[rows, at] + total for rows, total in zip(pieces, fresh)]
                for rows, total in zip(pieces, fresh):
                    turned[rows, at] = total
                return carry

            lax.fori_loop(begin, jnp.where(last > first, end, begin), window, 0)
        return carry

    lax.fori_loop(0, blocks, take, 0)
    fetch([(turned, turned_any), (member_ref, member_any)], out_sems)


def statistics_kernel(
    turned_any, member_any, hard_ref, lower_ref, extra_ref, small, turned, member_ref, spread, sems
):
    fetch([(turned_any, turned), (member_any, member_ref)], sems)
    features, span = turned.shape
    stripes = pl.cdiv(span, STRIPE)
    per_shard, negatives = hard_ref.shape
    shard = lax.axis_index("dp")
    small[...] = jnp.zeros_like(small)
    small[0:per_shard, stripes : stripes + negatives] = hard_ref[...].astype(jnp.float32)
    lower = lower_ref[:, pl.ds(pl.multiple_of(shard * features, LANES), features)]

    misc = jnp.zeros((ROWS, STRIPE), jnp.float32)
    residual = jnp.zeros((features, LANES), jnp.float32)
    for stripe in range(stripes):
        size = min(STRIPE, span - stripe * STRIPE)
        across = pl.ds(stripe * STRIPE, size)
        upright = turned[:, across]
        wide = upright.astype(jnp.float32)
        square = jnp.sum(wide * wide, axis=0, keepdims=True)
        reduced = mm(lower, upright)
        if size < STRIPE:
            none = jnp.zeros((ROWS, STRIPE - size), jnp.float32)
            reduced = jnp.concatenate([reduced, none], axis=1)
            square = jnp.concatenate([square, none[0:1]], axis=1)
        extra_ref[stripe * ROWS : (stripe + 1) * ROWS, :] = reduced.astype(jnp.bfloat16)
        misc = jnp.where(iota((ROWS, STRIPE), 0) == stripe, square, misc)
        residual += mm(upright, member_ref[across, :])
    hard = small[...].T[0:ROWS]
    for i in range(per_shard):
        misc += jnp.where(iota((ROWS, STRIPE), 1) == shard * per_shard + i, hard[:, i : i + 1], 0.0)
    extra_ref[stripes * ROWS : (stripes + 1) * ROWS, :] = misc.astype(jnp.bfloat16)
    residual = jnp.where(lax.axis_index("mp") == shard, residual.T[0:ROWS], 0.0)
    spread[...] = residual
    for q in range(4):
        start = (stripes + 1 + q) * ROWS
        quarter = pl.multiple_of(split_quarter(q // 2, q % 2) * STRIPE, LANES)
        extra_ref[start : start + ROWS, :] = spread[:, pl.ds(quarter, STRIPE)].astype(jnp.bfloat16)


def pool_kernel(
    ids_ref,
    own_ref,
    core_any,
    far_any,
    extra_ref,
    member_ref,
    own_rest,
    core_rest,
    far_rest,
    extra_rest,
    member_rest,
    raise_ref,
    sent_ref,
    misc_ref,
    raised,
    total,
    slopes,
    core_ref,
    far_ref,
    sems,
    model_width,
):
    texts, length = ids_ref.shape
    width = own_ref.shape[1]
    quarter = quarter_of(lax.axis_index("dp"))
    fetch([(core_any, core_ref), (far_any, far_ref)], sems)
    raised[...] = jnp.zeros_like(raised)
    raised[0:ROWS, :] = raise_ref[:, pl.ds(pl.multiple_of(quarter * width, LANES), width)]
    total[...] = jnp.zeros_like(total)
    slopes[...] = jnp.zeros_like(slopes)

    def add(refs, extra_ref, member_ref, base):
        span = member_ref.shape[0]
        stripes = pl.cdiv(span, STRIPE)

        def summed(start, size):
            return sum(ref[pl.ds(start, size), :].astype(jnp.float32) for ref in refs)

        misc = extra_ref[stripes * ROWS : (stripes + 1) * ROWS, :]
        if base == 0:
            misc_ref[...] = misc
        inverse = lax.rsqrt(misc / model_width + 1e-05)
        for k in range(stripes):
            size = min(STRIPE, span - k * STRIPE)
            scale = inverse[k : k + 1]
            reduced = (extra_ref[k * ROWS : (k + 1) * ROWS, :] * scale).astype(jnp.bfloat16)
            reduced = reduced.astype(jnp.float32)
            stacked = jnp.concatenate([reduced, jnp.broadcast_to(scale, (LANES - ROWS, STRIPE))])
            turned = stacked[:, 0:size].T
            low = turned.astype(jnp.bfloat16)
            linear = summed(k * STRIPE, size)
            linear = linear * turned[:, ROWS : ROWS + 1] + mm(low, raised[...])
            sigma = 1.0 / (1.0 + jnp.exp(-linear))
            slope = (sigma * (1.0 + linear * (1.0 - sigma))).astype(jnp.bfloat16)
            member = member_ref[pl.ds(k * STRIPE, size), :].astype(jnp.float32).T
            high, rest = split(linear * sigma)
            chosen = member[0:ROWS].astype(jnp.bfloat16)
            total[...] += mm(chosen, high) + mm(chosen, rest)
            spread = [reduced[:, 0:size] * member[text : text + 1] for text in range(texts)]
            slopes[...] += mm(jnp.concatenate(spread).astype(jnp.bfloat16), slope)
        total[...] += extra_ref[(stripes + 1) * ROWS : (stripes + 2) * ROWS, :]

    add((own_ref, core_ref, far_ref), extra_ref, member_ref, 0)
    real = (ids_ref[...] != 0).astype(jnp.float32)

    @pl.when(jnp.sum(real) > member_ref.shape[0])
    def _():
        add((own_rest, core_rest, far_rest), extra_rest, member_rest, member_ref.shape[0])

    counts = jnp.sum(real, axis=1, keepdims=True)
    pooled = total[0:texts] / counts
    pooled = jnp.concatenate([pooled, jnp.zeros((ROWS - texts, width), jnp.float32)])
    sent_ref[0:ROWS, :] = pooled.astype(jnp.bfloat16)
    for text in range(texts):
        part = slopes[text * ROWS : (text + 1) * ROWS, :] / counts[text : text + 1]
        sent_ref[(text + 1) * ROWS : (text + 2) * ROWS, :] = part.astype(jnp.bfloat16)


def both_sides(near, far):
    queries = lax.axis_index("group") == 0
    return jnp.concatenate([jnp.where(queries, near, far), jnp.where(queries, far, near)], axis=0)


def dots_kernel(near_ref, far_ref, packed_ref, slopes_ref):
    block = both_sides(near_ref[0:ROWS], far_ref[0:ROWS])
    rows = 2 * ROWS
    packed_ref[...] = jnp.zeros_like(packed_ref)
    packed_ref[0:rows, 0:rows] = mm(block, block, NT)
    for part in range(block.shape[1] // LANES):
        piece = block[:, part * LANES : (part + 1) * LANES]
        packed_ref[rows + part * rows : rows + (part + 1) * rows, :] = piece.astype(jnp.float32)
    size = near_ref.shape[0] - ROWS
    slopes_ref[0:size] = near_ref[ROWS:]
    slopes_ref[size:] = far_ref[ROWS:]


def score_kernel(*refs, texts, stripes, negatives):
    packed0, packed1, packed2, packed3, slopes0, slopes2 = refs[0:6]
    dots0, dots1, dots2, dots3, misc_ref, sharp_ref = refs[6:12]
    embed_ref, loss_ref, up_ref = refs[12:15]
    rows = 2 * ROWS
    per_shard = loss_ref.shape[1]
    group, shard = lax.axis_index("group"), lax.axis_index("dp")
    dots = ((dots0[...] + dots1[...]) + (dots2[...] + dots3[...]))[:, 0:rows]
    down, across = iota((rows, rows), 0), iota((rows, rows), 1)
    same = down == across
    real = (lax.rem(down, ROWS) < texts) & (lax.rem(across, ROWS) < texts)
    diagonal = jnp.where(same, dots, 0.0)
    rnorm_row = lax.rsqrt(jnp.sum(diagonal, axis=0, keepdims=True) + 1e-06)
    rnorm_col = lax.rsqrt(jnp.sum(diagonal, axis=1, keepdims=True) + 1e-06)
    sharpness = sharp_ref[0]
    cosine = dots * rnorm_col * rnorm_row
    scores = sharpness * cosine
    keep = real & ~same
    top = jnp.max(jnp.where(keep, scores, -jnp.inf), axis=0, keepdims=True)
    top = jnp.where(lax.rem(across[0:1], ROWS) < texts, top, 0.0)
    powers = jnp.exp(jnp.where(real, jnp.minimum(scores - top, 0.0), 0.0))
    hard = misc_ref[stripes : stripes + negatives, 0:rows].astype(jnp.int32) + ROWS
    times = jnp.zeros((rows, rows), jnp.float32)
    for k in range(negatives):
        times += jnp.where(hard[k : k + 1] == down, 1.0, 0.0)
    times = jnp.where(across < texts, times, 0.0)
    weights = (jnp.where(keep, 1.0, 0.0) + jnp.where(real, times, 0.0)) * powers
    total = jnp.sum(weights, axis=0, keepdims=True)
    total = jnp.where(lax.rem(across[0:1], ROWS) < texts, total, 1.0)
    pair = (down == lax.rem(across + ROWS, rows)) & real
    pair_score = jnp.sum(jnp.where(pair, scores, 0.0), axis=0, keepdims=True)
    losses = top + jnp.log(total) - pair_score
    grad_scores = (weights / total - jnp.where(pair, 1.0, 0.0)) / (2 * texts)
    coeff = (grad_scores * rnorm_col * rnorm_row).astype(jnp.bfloat16)
    radial = jnp.sum(grad_scores * cosine, axis=0, keepdims=True) * rnorm_row * rnorm_row

    first = shard * per_shard
    loss_col = jnp.sum(jnp.where(same, losses, 0.0), axis=1, keepdims=True)
    at = (iota((rows, LANES), 0) == group * ROWS + first + iota((rows, LANES), 1)) & (
        iota((rows, LANES), 1) < per_shard
    )
    loss_ref[...] = jnp.sum(jnp.where(at, loss_col, 0.0), axis=0, keepdims=True)[:, 0:per_shard]

    along_rows = coeff.astype(jnp.float32).T.astype(jnp.bfloat16)
    radial_col = jnp.sum(jnp.where(same, radial, 0.0), axis=1, keepdims=True)
    rnorm_own = jnp.where(group == 0, rnorm_col[0:ROWS], rnorm_col[ROWS:rows])
    chosen = iota((ROWS, ROWS), 1) == iota((ROWS, ROWS), 0) + first
    chosen = jnp.where(chosen & (iota((ROWS, ROWS), 0) < per_shard), 1.0, 0.0).astype(jnp.bfloat16)
    blocks = ((packed0, slopes0), (packed1, None), (packed2, slopes2), (packed3, None))
    for o, (packed, slopes) in enumerate(blocks):
        parts = packed.shape[0] // rows - 1
        width = parts * LANES
        halves = [packed[rows * (part + 1) : rows * (part + 2), :] for part in range(parts)]
        block = jnp.concatenate(halves, axis=1)
        queries = group == 0
        at = pl.multiple_of(quarter_of(shard ^ o) * width, LANES)
        own = jnp.where(queries, block[0:ROWS], block[ROWS:rows]) * rnorm_own
        picked = mm(chosen, own.astype(jnp.bfloat16)).astype(jnp.bfloat16)
        embed_ref[0, :, pl.ds(at, width)] = picked[0:per_shard]
        if slopes is None:
            continue
        along = mm(along_rows, block.astype(jnp.bfloat16))
        grad = sharpness * (along - radial_col * block)
        near, far = slopes[0 : slopes.shape[0] // 2], slopes[slopes.shape[0] // 2 :]
        grad_near = jnp.where(queries, grad[0:ROWS], grad[ROWS:rows])
        grad_far = jnp.where(queries, grad[ROWS:rows], grad[0:ROWS])
        update = []
        for side, side_grad in ((near, grad_near), (far, grad_far)):
            total = jnp.zeros((ROWS, width), jnp.float32)
            for text in range(texts):
                slope = side[text * ROWS : (text + 1) * ROWS].astype(jnp.float32)
                total += side_grad[text : text + 1] * slope
            update.append(total)
        at = pl.multiple_of((lax.div(shard, 2) ^ (o // 2)) * width, LANES)
        up_ref[:, pl.ds(at, width)] = update[0] + update[1]


def any_spec():
    return pl.BlockSpec(memory_space=pl.ANY)


def vmem_spec():
    return pl.BlockSpec(memory_space=pltpu.VMEM)


def smem_spec():
    return pl.BlockSpec(memory_space=pltpu.SMEM)


def exchange(x, axis, size):
    steps = [[(i, i ^ o) for i in range(size)] for o in reversed(range(1, size))]
    return [x] + [lax.ppermute(x, axis, step) for step in steps][::-1]


def split_body(
    query_passage_words,
    difficult_distractors,
    vocabulary_vectors,
    layer_weight_matrix,
    lowering_factor_matrix,
    raising_factor_matrix,
    logit_sharpness,
):
    shards, parts = lax.axis_size("dp"), lax.axis_size("mp")
    ids = query_passage_words[0]
    texts, length = ids.shape
    tokens = texts * length
    features, vocab = vocabulary_vectors.shape
    blocks = vocab // IDS_PER_BLOCK
    group_rows = 8 * pl.cdiv(vocab // IDS_PER_GROUP + 1, 8)
    per_shard, negatives = difficult_distractors.shape
    part_width = layer_weight_matrix.shape[1]
    width = part_width // shards
    params = pltpu.CompilerParams(vmem_limit_bytes=LARGE_VMEM)
    modest = pltpu.CompilerParams(vmem_limit_bytes=MODEST_VMEM)
    other_core = [(d, d ^ 1) for d in range(shards)]
    other_y = [(d, d ^ 2) for d in range(shards)]

    def columns(i, j):
        start = split_quarter(i, j) * width
        return lax.dynamic_slice(layer_weight_matrix, (0, start), (features, width))

    def project(base, span, after):
        stripes = pl.cdiv(span, STRIPE)
        extra_rows = (stripes + 1 + shards) * ROWS
        turned, member = pl.pallas_call(
            functools.partial(gather_kernel, base=base),
            out_shape=[
                jax.ShapeDtypeStruct((features, span), jnp.bfloat16),
                jax.ShapeDtypeStruct((span, LANES), jnp.bfloat16),
            ],
            in_specs=[vmem_spec()] + [any_spec()] * 2,
            out_specs=[any_spec()] * 2,
            scratch_shapes=[
                pltpu.VMEM((features, span), jnp.bfloat16),
                pltpu.VMEM((span, LANES), jnp.bfloat16),
                pltpu.VMEM((blocks, features, IDS_PER_BLOCK), jnp.bfloat16),
                pltpu.VMEM((8 * pl.cdiv(span // LANES, 8), LANES), jnp.int32),
                pltpu.VMEM((texts, length), jnp.float32),
                pltpu.VMEM((group_rows, length), jnp.int32),
                pltpu.SMEM((group_rows, length), jnp.int32),
                pltpu.SemaphoreType.DMA((blocks,)),
                pltpu.SemaphoreType.DMA,
                pltpu.SemaphoreType.DMA((2,)),
            ],
            compiler_params=params,
            name="gather",
        )(ids, vocabulary_vectors, after)

        def product(turned, i, j):
            return mm(turned, columns(i, j), (((0,), (0,)), ((), ())))

        def narrow(x):
            return x.astype(jnp.bfloat16)

        core1 = lax.ppermute(narrow(product(turned, 1, 1)), "dp", other_core)
        own1 = lax.optimization_barrier(narrow(product(turned, 0, 1)))
        chip1 = narrow(own1.astype(jnp.float32) + core1.astype(jnp.float32))
        far = lax.ppermute(chip1, "dp", other_y)
        turned, _ = lax.optimization_barrier((turned, chip1))
        extra = pl.pallas_call(
            statistics_kernel,
            out_shape=jax.ShapeDtypeStruct((extra_rows, STRIPE), jnp.bfloat16),
            in_specs=[any_spec()] * 2 + [vmem_spec()] * 2,
            out_specs=vmem_spec(),
            scratch_shapes=[
                pltpu.VMEM((LANES, LANES), jnp.float32),
                pltpu.VMEM(turned.shape, turned.dtype),
                pltpu.VMEM(member.shape, member.dtype),
                pltpu.VMEM((ROWS, features), jnp.float32),
                pltpu.SemaphoreType.DMA((2,)),
            ],
            compiler_params=modest,
            cost_estimate=pl.CostEstimate(
                flops=2 * features * span * (ROWS + LANES),
                bytes_accessed=2 * features * span,
                transcendentals=0,
            ),
            name="statistics",
        )(turned, member, difficult_distractors, lowering_factor_matrix)
        common = (stripes + 1) * ROWS
        near = extra.astype(jnp.float32)
        across = lax.ppermute(extra, "dp", other_core).astype(jnp.float32)
        chip = near[0:common] + across[0:common]
        inputs = near[common : common + 2 * ROWS] + across[common + 2 * ROWS :]
        sent = narrow(jnp.concatenate([chip, inputs[ROWS:]]))
        sent = lax.ppermute(sent, "dp", other_y).astype(jnp.float32)
        extra = jnp.concatenate([chip, inputs[0:ROWS]]) + sent
        core0 = lax.ppermute(narrow(product(turned, 1, 0)), "dp", other_core)
        own0 = narrow(product(turned, 0, 0))
        return own0, core0, far, extra, member

    many = jnp.sum((ids != 0).astype(jnp.int32)) > FIRST
    left = tokens - FIRST
    shapes = jax.eval_shape(lambda: project(FIRST, left, logit_sharpness))
    rest = lax.cond(
        many,
        lambda: project(FIRST, left, logit_sharpness),
        lambda: tuple(jnp.zeros(x.shape, x.dtype) for x in shapes),
    )
    first = project(0, FIRST, rest[3])
    sent, misc = pl.pallas_call(
        functools.partial(pool_kernel, model_width=float(features * shards)),
        out_shape=[
            jax.ShapeDtypeStruct(((texts + 1) * ROWS, width), jnp.bfloat16),
            jax.ShapeDtypeStruct((ROWS, width), jnp.float32),
        ],
        in_specs=[vmem_spec()] * 2 + [any_spec()] * 2 + [vmem_spec()] * 8,
        out_specs=[vmem_spec()] * 2,
        scratch_shapes=[
            pltpu.VMEM((LANES, width), jnp.bfloat16),
            pltpu.VMEM((ROWS, width), jnp.float32),
            pltpu.VMEM((texts * ROWS, width), jnp.float32),
            pltpu.VMEM((FIRST, width), jnp.bfloat16),
            pltpu.VMEM((FIRST, width), jnp.bfloat16),
            pltpu.SemaphoreType.DMA((2,)),
        ],
        compiler_params=modest,
        name="pool",
    )(ids, *first, *rest, raising_factor_matrix)
    far_side = lax.ppermute(sent, "group", [(0, 1), (1, 0)])
    rows = 2 * ROWS
    packed, slopes = pl.pallas_call(
        dots_kernel,
        out_shape=[
            jax.ShapeDtypeStruct((rows + width // LANES * rows, LANES), jnp.float32),
            jax.ShapeDtypeStruct((2 * texts * ROWS, width), jnp.bfloat16),
        ],
        in_specs=[vmem_spec()] * 2,
        out_specs=[vmem_spec()] * 2,
        compiler_params=modest,
        name="dots",
    )(sent, far_side)
    packed = exchange(packed, "dp", shards)
    dots = [x[0:rows] for x in packed]
    dots = (dots[0] + dots[1]) + (dots[2] + dots[3])
    slopes, dots = lax.optimization_barrier((slopes, dots))
    dots = exchange(dots, "mp", parts)
    slopes = [slopes, lax.ppermute(slopes, "dp", other_y)]
    embeddings, losses, update = pl.pallas_call(
        functools.partial(
            score_kernel, texts=texts, stripes=pl.cdiv(FIRST, STRIPE), negatives=negatives
        ),
        out_shape=[
            jax.ShapeDtypeStruct((1, per_shard, part_width), jnp.bfloat16),
            jax.ShapeDtypeStruct((1, per_shard), jnp.float32),
            jax.ShapeDtypeStruct((ROWS, part_width // 2), jnp.float32),
        ],
        in_specs=[vmem_spec()] * 11 + [smem_spec()],
        out_specs=[vmem_spec()] * 3,
        compiler_params=modest,
        name="score",
    )(*packed, *slopes, *dots, misc, logit_sharpness)
    other = lax.ppermute(update, "dp", other_core)
    core = lax.rem(lax.axis_index("dp"), 2)
    halves = [jnp.where(core == 0, update, other), jnp.where(core == 0, other, update)]
    return (embeddings, losses, jnp.concatenate(halves, axis=1))


def body(words, hard, vocabulary, weight, lowering, raising, sharpness):
    shards, parts = lax.axis_size("dp"), lax.axis_size("mp")
    texts, length = words.shape[1:]
    features, vocab = vocabulary.shape
    negatives = hard.shape[1]
    square = shards == 4 and features == weight.shape[1] == 4 * STRIPE and parts == shards
    small = texts <= ROWS - 2 and length == LANES and FIRST < texts * length <= 2048
    even = (texts * length - FIRST) % CHUNK == 0 and vocab % IDS_PER_BLOCK == 0
    fits = features * vocab <= 2**24 and features % (4 * LANES) == 0
    spare = pl.cdiv(FIRST, STRIPE) + negatives <= ROWS and lowering.shape[0] == ROWS
    fast = square and small and even and fits and spare and lax.axis_size("group") == 2
    chosen = split_body if fast else general_body
    return chosen(words, hard, vocabulary, weight, lowering, raising, sharpness)


def solution(mesh):
    in_specs = (
        P("group", None, None),
        P("dp", None),
        P("dp", None),
        P("dp", "mp"),
        P(),
        P(None, "mp"),
        P(),
    )
    out_specs = (P("group", "dp", "mp"), P("group", "dp"), P(None, "mp"))
    return jax.shard_map(body, mesh=mesh, in_specs=in_specs, out_specs=out_specs, check_vma=False)
```

```python
import functools

import jax
import jax.numpy as jnp
from jax import lax
from jax.experimental import pallas as pl
from jax.experimental.pallas import tpu as pltpu
from jax.sharding import PartitionSpec as P


def general_body(
    query_passage_words,
    difficult_distractors,
    vocabulary_vectors,
    layer_weight_matrix,
    lowering_factor_matrix,
    raising_factor_matrix,
    logit_sharpness,
):
    group_index = lax.axis_index("group")
    shard_index = lax.axis_index("dp")
    part_index = lax.axis_index("mp")
    shard_count = lax.axis_size("dp")
    side_ids = query_passage_words[0]
    text_count = side_ids.shape[0]
    length = side_ids.shape[1]
    per_shard = text_count // shard_count
    own_ids = lax.dynamic_slice_in_dim(side_ids, shard_index * per_shard, per_shard, 0)
    columns = jnp.take(vocabulary_vectors, side_ids.reshape(-1), axis=1)
    inputs = lax.all_to_all(columns, "dp", split_axis=1, concat_axis=0, tiled=True)
    tokens = inputs.shape[1]
    feature_width = raising_factor_matrix.shape[1]
    wide_inputs = inputs.astype(jnp.float32)
    inverse = lax.rsqrt(jnp.mean(wide_inputs * wide_inputs, axis=0) + 1e-05)
    normed_state = (wide_inputs * inverse[None, :]).astype(jnp.bfloat16)
    linear_map = lax.dot_general(
        lax.all_gather(layer_weight_matrix, "dp", axis=0, tiled=True),
        normed_state,
        (((0,), (0,)), ((), ())),
        preferred_element_type=jnp.float32,
    )
    reduced_sum = jnp.dot(
        lowering_factor_matrix, normed_state, preferred_element_type=jnp.float32
    ).astype(jnp.bfloat16)
    linear_map = linear_map + lax.dot_general(
        raising_factor_matrix,
        reduced_sum,
        (((0,), (0,)), ((), ())),
        preferred_element_type=jnp.float32,
    )
    own_inputs = lax.dynamic_slice_in_dim(
        inputs, part_index * feature_width, feature_width, 0
    ).astype(jnp.float32)
    hidden_state = own_inputs + jax.nn.silu(linear_map)
    mask = (own_ids != 0).astype(jnp.float32)
    counts = jnp.sum(mask, axis=1)
    summed = jnp.einsum("dnl,nl->nd", hidden_state.reshape(feature_width, per_shard, length), mask)
    pooled = (summed / counts[:, None]).astype(jnp.bfloat16)
    gathered = lax.all_gather(pooled, ("group", "dp"), axis=0, tiled=True)
    part_scores = lax.dot_general(
        pooled, gathered, (((1,), (1,)), ((), ())), preferred_element_type=jnp.float32
    )
    gathered_wide = gathered.astype(jnp.float32)
    part_norms = jnp.sum(gathered_wide * gathered_wide, axis=1)
    dots, norms = lax.psum((part_scores, part_norms), "mp")
    rnorm_all = lax.rsqrt(norms + 1e-06)
    all_count = gathered.shape[0]
    half_count = all_count // 2
    own_rows = (
        group_index * half_count + shard_index * per_shard + jnp.arange(per_shard, dtype=jnp.int32)
    )
    rnorm_own = jnp.take(rnorm_all, own_rows)
    cosine = dots * rnorm_own[:, None] * rnorm_all[None, :]
    multiplier_factor = logit_sharpness[0]
    scores = multiplier_factor * cosine
    column_ids = jnp.arange(all_count, dtype=jnp.int32)
    keep = column_ids[None, :] != own_rows[:, None]
    pair = (own_rows + half_count) % all_count
    weight = (group_index == 0).astype(jnp.float32)
    neg_cols = half_count + difficult_distractors
    top = jnp.max(jnp.where(keep, scores, -jnp.inf), axis=1)
    safe_scores = jnp.where(keep, scores, top[:, None])
    expd = jnp.where(keep, jnp.exp(safe_scores - top[:, None]), 0.0)
    neg_exp = (
        jnp.exp(jnp.minimum(jnp.take_along_axis(scores, neg_cols, axis=1) - top[:, None], 0.0))
        * weight
    )
    total = jnp.sum(expd, axis=1) + jnp.sum(neg_exp, axis=1)
    pair_score = jnp.take_along_axis(scores, pair[:, None], axis=1)[:, 0]
    losses = top + jnp.log(total) - pair_score
    onehot = (column_ids[None, None, :] == neg_cols[:, :, None]).astype(jnp.float32)
    probs = (expd + jnp.einsum("rk,rkc->rc", neg_exp, onehot)) / total[:, None]
    target = (column_ids[None, :] == pair[:, None]).astype(jnp.float32)
    grad_scores = (probs - target) / all_count
    coeff = (grad_scores * rnorm_own[:, None] * rnorm_all[None, :]).astype(jnp.bfloat16)
    along = jnp.dot(coeff, gathered, preferred_element_type=jnp.float32)
    pooled_wide = pooled.astype(jnp.float32)
    radial = jnp.sum(grad_scores * cosine, axis=1) * rnorm_own * rnorm_own
    embedding_gradient = multiplier_factor * (along - radial[:, None] * pooled_wide)
    token_grad = jnp.einsum("nd,nl->dnl", embedding_gradient / counts[:, None], mask).reshape(
        feature_width, tokens
    )
    sigma = jax.nn.sigmoid(linear_map)
    local = (token_grad * sigma * (1.0 + linear_map * (1.0 - sigma))).astype(jnp.bfloat16)
    up_portion = lax.dot_general(
        reduced_sum, local, (((1,), (1,)), ((), ())), preferred_element_type=jnp.float32
    )
    adapter_up_gradient = lax.psum(up_portion, ("group", "dp"))
    embeddings = (pooled_wide * rnorm_own[:, None]).astype(jnp.bfloat16)[None]
    return (embeddings, losses[None], adapter_up_gradient)


BLOCK_BITS, GROUP_BITS, LANE_BITS, ROW_BITS = 10, 9, 7, 4
IDS_PER_BLOCK = 1 << BLOCK_BITS
IDS_PER_GROUP = 1 << GROUP_BITS
CHUNK = 384
STRIPE = 256
ROWS = 1 << ROW_BITS
LANES = 1 << LANE_BITS
FEATURE_ROWS = 128
FIRST = 1152
TAKEN = 768
NT = (((1,), (1,)), ((), ()))
LARGE_VMEM, MODEST_VMEM = 44 * 1024 * 1024, 15 * 1024 * 1024


def mm(a, b, dims=(((1,), (0,)), ((), ()))):
    return lax.dot_general(a, b, dims, preferred_element_type=jnp.float32)


def split(x):
    high = x.astype(jnp.bfloat16)
    return high, (x - high.astype(jnp.float32)).astype(jnp.bfloat16)


def iota(shape, dim):
    return lax.broadcasted_iota(jnp.int32, shape, dim)


def quarter_of(dp_index, cores=2):
    return (dp_index % cores) * 2 + dp_index // cores


def split_quarter(i, j, cores=2):
    shard = lax.axis_index("dp")
    core, side_y = lax.rem(shard, cores), lax.div(shard, cores)
    return (core ^ i) * 2 + (side_y ^ j)


def take_lanes(x, lanes):
    numbers = lax.GatherDimensionNumbers(
        offset_dims=(),
        collapsed_slice_dims=(1,),
        start_index_map=(1,),
        operand_batching_dims=(0,),
        start_indices_batching_dims=(0,),
    )
    mode = lax.GatherScatterMode.PROMISE_IN_BOUNDS
    return lax.gather(x, lanes[..., None], numbers, slice_sizes=(1, 1), mode=mode)


def fetch(pairs, sems):
    copies = [pltpu.make_async_copy(a, b, sems.at[n]) for n, (a, b) in enumerate(pairs)]
    for copy in copies:
        copy.start()
    for copy in copies:
        copy.wait()


def gather_kernel(
    ids_ref,
    vocab_ref,
    weight_ref,
    turned_any,
    member_any,
    weight0,
    weight1,
    turned,
    member_ref,
    held,
    token_ref,
    ranks,
    counted,
    bounds,
    held_sems,
    bounds_sem,
    out_sems,
    weight_sems,
    base,
):
    texts, length = ids_ref.shape
    features, vocab = vocab_ref.shape
    blocks = vocab // IDS_PER_BLOCK
    groups = vocab // IDS_PER_GROUP
    span = member_ref.shape[0]

    def vocab_copy(b):
        columns = pl.ds(pl.multiple_of(b * IDS_PER_BLOCK, LANES), IDS_PER_BLOCK)
        return pltpu.make_async_copy(vocab_ref.at[:, columns], held.at[b], held_sems.at[b])

    weight_copies = []
    for i, weight in enumerate((weight0, weight1)):
        width = weight.shape[1]
        columns = pl.ds(pl.multiple_of(split_quarter(i, 1) * width, LANES), width)
        copy = pltpu.make_async_copy(weight_ref.at[:, columns], weight, weight_sems.at[i])
        weight_copies.append(copy)
    vocab_copy(0).start()
    for copy in weight_copies:
        copy.start()
    for b in range(1, blocks):
        vocab_copy(b).start()

    ids = ids_ref[...]
    valid = ids != 0
    group_of = jnp.where(valid, lax.shift_right_logical(ids, GROUP_BITS), groups)
    group_rows = counted.shape[0]
    group_id = iota((group_rows, length), 0)
    below = jnp.zeros((group_rows, length), jnp.float32)
    for text in range(texts):
        below += jnp.where(group_of[text : text + 1] < group_id, 1.0, 0.0)
    before = jnp.broadcast_to(jnp.sum(below, axis=1, keepdims=True), (group_rows, length))
    counted[...] = before.astype(jnp.int32)
    bounds_copy = pltpu.make_async_copy(counted, bounds, bounds_sem)
    bounds_copy.start()
    earlier = jnp.where(iota((length, length), 0) < iota((length, length), 1), 1.0, 0.0).astype(
        jnp.bfloat16
    )
    for text in range(texts):
        here = jnp.where(group_of[text : text + 1] == group_id, 1.0, 0.0)
        inside = mm(here.astype(jnp.bfloat16), earlier)
        ranks[pl.ds(text, 1), :] = jnp.sum(here * (inside + before), axis=0, keepdims=True)
        before += jnp.broadcast_to(jnp.sum(here, axis=1, keepdims=True), (group_rows, length))
    text_of = iota((texts, length), 0)
    carried = jnp.where(valid, lax.shift_left(ids, ROW_BITS) + text_of, 0).astype(jnp.float32)
    rank = ranks[...]

    def place(p, carry):
        position = (iota((LANES, length), 0) + (p * LANES + base)).astype(jnp.float32)
        total = jnp.zeros((LANES, length), jnp.float32)
        for text in range(texts):
            total += jnp.where(rank[text : text + 1] == position, carried[text : text + 1], 0.0)
        found = jnp.broadcast_to(jnp.sum(total, axis=1, keepdims=True), (LANES, LANES))
        start = pl.multiple_of(p * LANES, LANES)
        row = found.T[0:1].astype(jnp.int32)
        token = lax.shift_right_logical(row, ROW_BITS)
        token_ref[pl.ds(p, 1), :] = jnp.where(token == 0, -vocab, token)
        found = found.astype(jnp.int32)
        real = (found >= ROWS) & ((found & (ROWS - 1)) == iota((LANES, LANES), 1))
        member_ref[pl.ds(start, LANES), :] = jnp.where(real, 1.0, 0.0).astype(jnp.bfloat16)
        turned[:, pl.ds(start, LANES)] = jnp.zeros((features, LANES), jnp.bfloat16)
        return carry

    lax.fori_loop(0, span // LANES, place, 0)
    bounds_copy.wait()

    def within(place):
        return jnp.clip(place - base, 0, span)

    def take(b, carry):
        vocab_copy(b).wait()
        for part in range(IDS_PER_BLOCK // IDS_PER_GROUP):
            group = b * (IDS_PER_BLOCK // IDS_PER_GROUP) + part
            first, last = within(bounds[group, 0]), within(bounds[group + 1, 0])
            begin = lax.shift_right_logical(first, LANE_BITS)
            end = lax.shift_right_logical(last + LANES - 1, LANE_BITS)

            def window(p, carry):
                at = pl.ds(pl.multiple_of(p * LANES, LANES), LANES)
                token = token_ref[pl.ds(p, 1), :] - group * IDS_PER_GROUP
                token = jnp.broadcast_to(token, (FEATURE_ROWS, LANES))
                lane = (token & (LANES - 1)).astype(jnp.int16)
                tile = lax.shift_right_arithmetic(token, LANE_BITS).astype(jnp.int16)
                pieces = [pl.ds(f, FEATURE_ROWS) for f in range(0, TAKEN, FEATURE_ROWS)]
                short = jnp.broadcast_to(token[0:1], (IDS_PER_GROUP, LANES)).astype(jnp.int16)
                picked = jnp.where(
                    short == iota((IDS_PER_GROUP, LANES), 0).astype(jnp.int16), 1.0, 0.0
                ).astype(jnp.bfloat16)
                columns = pl.ds(part * IDS_PER_GROUP, IDS_PER_GROUP)
                rest = pl.ds(TAKEN, features - TAKEN)
                product = mm(held[b, rest, columns], picked).astype(jnp.bfloat16)
                fresh = []
                for rows in pieces:
                    total = jnp.zeros((FEATURE_ROWS, LANES), jnp.bfloat16)
                    for j in range(IDS_PER_GROUP // LANES):
                        columns = pl.ds(part * IDS_PER_GROUP + j * LANES, LANES)
                        total = jnp.where(tile == j, take_lanes(held[b, rows, columns], lane), total)
                    fresh.append(total)
                pieces.append(rest)
                fresh.append(product)
                fresh = [turned[rows, at] + total for rows, total in zip(pieces, fresh)]
                for rows, total in zip(pieces, fresh):
                    turned[rows, at] = total
                return carry

            lax.fori_loop(begin, jnp.where(last > first, end, begin), window, 0)
        return carry

    lax.fori_loop(0, blocks, take, 0)
    fetch([(turned, turned_any), (member_ref, member_any)], out_sems)
    for copy in weight_copies:
        copy.wait()


def statistics_kernel(
    turned_any, member_any, hard_ref, lower_ref, extra_ref, small, turned, member_ref, spread, sems
):
    fetch([(turned_any, turned), (member_any, member_ref)], sems)
    features, span = turned.shape
    stripes = pl.cdiv(span, STRIPE)
    per_shard, negatives = hard_ref.shape
    shard = lax.axis_index("dp")
    small[...] = jnp.zeros_like(small)
    small[0:per_shard, stripes : stripes + negatives] = hard_ref[...].astype(jnp.float32)
    lower = lower_ref[:, pl.ds(pl.multiple_of(shard * features, LANES), features)]

    misc = jnp.zeros((ROWS, STRIPE), jnp.float32)
    residual = jnp.zeros((features, LANES), jnp.float32)
    for stripe in range(stripes):
        size = min(STRIPE, span - stripe * STRIPE)
        across = pl.ds(stripe * STRIPE, size)
        upright = turned[:, across]
        wide = upright.astype(jnp.float32)
        square = jnp.sum(wide * wide, axis=0, keepdims=True)
        reduced = mm(lower, upright)
        if size < STRIPE:
            none = jnp.zeros((ROWS, STRIPE - size), jnp.float32)
            reduced = jnp.concatenate([reduced, none], axis=1)
            square = jnp.concatenate([square, none[0:1]], axis=1)
        extra_ref[stripe * ROWS : (stripe + 1) * ROWS, :] = reduced.astype(jnp.bfloat16)
        misc = jnp.where(iota((ROWS, STRIPE), 0) == stripe, square, misc)
        residual += mm(upright, member_ref[across, :])
    hard = small[...].T[0:ROWS]
    for i in range(per_shard):
        misc += jnp.where(iota((ROWS, STRIPE), 1) == shard * per_shard + i, hard[:, i : i + 1], 0.0)
    extra_ref[stripes * ROWS : (stripes + 1) * ROWS, :] = misc.astype(jnp.bfloat16)
    residual = jnp.where(lax.axis_index("mp") == shard, residual.T[0:ROWS], 0.0)
    spread[...] = residual
    for q in range(4):
        start = (stripes + 1 + q) * ROWS
        quarter = pl.multiple_of(split_quarter(q // 2, q % 2) * STRIPE, LANES)
        extra_ref[start : start + ROWS, :] = spread[:, pl.ds(quarter, STRIPE)].astype(jnp.bfloat16)


def pool_kernel(
    ids_ref,
    own_ref,
    core_any,
    far_any,
    extra_ref,
    member_ref,
    own_rest,
    core_rest,
    far_rest,
    extra_rest,
    member_rest,
    raise_ref,
    sent_ref,
    misc_ref,
    raised,
    total,
    slopes,
    core_ref,
    far_ref,
    sems,
    model_width,
):
    texts, length = ids_ref.shape
    width = own_ref.shape[1]
    quarter = quarter_of(lax.axis_index("dp"))
    fetch([(core_any, core_ref), (far_any, far_ref)], sems)
    raised[...] = jnp.zeros_like(raised)
    raised[0:ROWS, :] = raise_ref[:, pl.ds(pl.multiple_of(quarter * width, LANES), width)]
    total[...] = jnp.zeros_like(total)
    slopes[...] = jnp.zeros_like(slopes)

    def add(refs, extra_ref, member_ref, base):
        span = member_ref.shape[0]
        stripes = pl.cdiv(span, STRIPE)

        def summed(start, size):
            return sum(ref[pl.ds(start, size), :].astype(jnp.float32) for ref in refs)

        misc = extra_ref[stripes * ROWS : (stripes + 1) * ROWS, :]
        if base == 0:
            misc_ref[...] = misc
        inverse = lax.rsqrt(misc / model_width + 1e-05)
        for k in range(stripes):
            size = min(STRIPE, span - k * STRIPE)
            scale = inverse[k : k + 1]
            reduced = (extra_ref[k * ROWS : (k + 1) * ROWS, :] * scale).astype(jnp.bfloat16)
            reduced = reduced.astype(jnp.float32)
            stacked = jnp.concatenate([reduced, jnp.broadcast_to(scale, (LANES - ROWS, STRIPE))])
            turned = stacked[:, 0:size].T
            low = turned.astype(jnp.bfloat16)
            linear = summed(k * STRIPE, size)
            linear = linear * turned[:, ROWS : ROWS + 1] + mm(low, raised[...])
            sigma = 1.0 / (1.0 + jnp.exp(-linear))
            slope = (sigma * (1.0 + linear * (1.0 - sigma))).astype(jnp.bfloat16)
            member = member_ref[pl.ds(k * STRIPE, size), :].astype(jnp.float32).T
            high, rest = split(linear * sigma)
            chosen = member[0:ROWS].astype(jnp.bfloat16)
            total[...] += mm(chosen, high) + mm(chosen, rest)
            spread = [reduced[:, 0:size] * member[text : text + 1] for text in range(texts)]
            slopes[...] += mm(jnp.concatenate(spread).astype(jnp.bfloat16), slope)
        total[...] += extra_ref[(stripes + 1) * ROWS : (stripes + 2) * ROWS, :]

    add((own_ref, core_ref, far_ref), extra_ref, member_ref, 0)
    real = (ids_ref[...] != 0).astype(jnp.float32)

    @pl.when(jnp.sum(real) > member_ref.shape[0])
    def _():
        add((own_rest, core_rest, far_rest), extra_rest, member_rest, member_ref.shape[0])

    counts = jnp.sum(real, axis=1, keepdims=True)
    pooled = total[0:texts] / counts
    pooled = jnp.concatenate([pooled, jnp.zeros((ROWS - texts, width), jnp.float32)])
    sent_ref[0:ROWS, :] = pooled.astype(jnp.bfloat16)
    for text in range(texts):
        part = slopes[text * ROWS : (text + 1) * ROWS, :] / counts[text : text + 1]
        sent_ref[(text + 1) * ROWS : (text + 2) * ROWS, :] = part.astype(jnp.bfloat16)


def both_sides(near, far):
    queries = lax.axis_index("group") == 0
    return jnp.concatenate([jnp.where(queries, near, far), jnp.where(queries, far, near)], axis=0)


def dots_kernel(near_ref, far_ref, packed_ref, slopes_ref):
    block = both_sides(near_ref[0:ROWS], far_ref[0:ROWS])
    rows = 2 * ROWS
    packed_ref[...] = jnp.zeros_like(packed_ref)
    packed_ref[0:rows, 0:rows] = mm(block, block, NT)
    for part in range(block.shape[1] // LANES):
        piece = block[:, part * LANES : (part + 1) * LANES]
        packed_ref[rows + part * rows : rows + (part + 1) * rows, :] = piece.astype(jnp.float32)
    size = near_ref.shape[0] - ROWS
    slopes_ref[0:size] = near_ref[ROWS:]
    slopes_ref[size:] = far_ref[ROWS:]


def score_kernel(*refs, texts, stripes, negatives):
    packed0, packed1, packed2, packed3, slopes0, slopes2 = refs[0:6]
    dots0, dots1, dots2, dots3, misc_ref, sharp_ref = refs[6:12]
    embed_ref, loss_ref, up_ref = refs[12:15]
    rows = 2 * ROWS
    per_shard = loss_ref.shape[1]
    group, shard = lax.axis_index("group"), lax.axis_index("dp")
    dots = ((dots0[...] + dots1[...]) + (dots2[...] + dots3[...]))[:, 0:rows]
    down, across = iota((rows, rows), 0), iota((rows, rows), 1)
    same = down == across
    real = (lax.rem(down, ROWS) < texts) & (lax.rem(across, ROWS) < texts)
    diagonal = jnp.where(same, dots, 0.0)
    rnorm_row = lax.rsqrt(jnp.sum(diagonal, axis=0, keepdims=True) + 1e-06)
    rnorm_col = lax.rsqrt(jnp.sum(diagonal, axis=1, keepdims=True) + 1e-06)
    sharpness = sharp_ref[0]
    cosine = dots * rnorm_col * rnorm_row
    scores = sharpness * cosine
    keep = real & ~same
    top = jnp.max(jnp.where(keep, scores, -jnp.inf), axis=0, keepdims=True)
    top = jnp.where(lax.rem(across[0:1], ROWS) < texts, top, 0.0)
    powers = jnp.exp(jnp.where(real, jnp.minimum(scores - top, 0.0), 0.0))
    hard = misc_ref[stripes : stripes + negatives, 0:rows].astype(jnp.int32) + ROWS
    times = jnp.zeros((rows, rows), jnp.float32)
    for k in range(negatives):
        times += jnp.where(hard[k : k + 1] == down, 1.0, 0.0)
    times = jnp.where(across < texts, times, 0.0)
    weights = (jnp.where(keep, 1.0, 0.0) + jnp.where(real, times, 0.0)) * powers
    total = jnp.sum(weights, axis=0, keepdims=True)
    total = jnp.where(lax.rem(across[0:1], ROWS) < texts, total, 1.0)
    pair = (down == lax.rem(across + ROWS, rows)) & real
    pair_score = jnp.sum(jnp.where(pair, scores, 0.0), axis=0, keepdims=True)
    losses = top + jnp.log(total) - pair_score
    grad_scores = (weights / total - jnp.where(pair, 1.0, 0.0)) / (2 * texts)
    coeff = (grad_scores * rnorm_col * rnorm_row).astype(jnp.bfloat16)
    radial = jnp.sum(grad_scores * cosine, axis=0, keepdims=True) * rnorm_row * rnorm_row

    first = shard * per_shard
    loss_col = jnp.sum(jnp.where(same, losses, 0.0), axis=1, keepdims=True)
    at = (iota((rows, LANES), 0) == group * ROWS + first + iota((rows, LANES), 1)) & (
        iota((rows, LANES), 1) < per_shard
    )
    loss_ref[...] = jnp.sum(jnp.where(at, loss_col, 0.0), axis=0, keepdims=True)[:, 0:per_shard]

    along_rows = coeff.astype(jnp.float32).T.astype(jnp.bfloat16)
    radial_col = jnp.sum(jnp.where(same, radial, 0.0), axis=1, keepdims=True)
    rnorm_own = jnp.where(group == 0, rnorm_col[0:ROWS], rnorm_col[ROWS:rows])
    chosen = iota((ROWS, ROWS), 1) == iota((ROWS, ROWS), 0) + first
    chosen = jnp.where(chosen & (iota((ROWS, ROWS), 0) < per_shard), 1.0, 0.0).astype(jnp.bfloat16)
    blocks = ((packed0, slopes0), (packed1, None), (packed2, slopes2), (packed3, None))
    for o, (packed, slopes) in enumerate(blocks):
        parts = packed.shape[0] // rows - 1
        width = parts * LANES
        halves = [packed[rows * (part + 1) : rows * (part + 2), :] for part in range(parts)]
        block = jnp.concatenate(halves, axis=1)
        queries = group == 0
        at = pl.multiple_of(quarter_of(shard ^ o) * width, LANES)
        own = jnp.where(queries, block[0:ROWS], block[ROWS:rows]) * rnorm_own
        picked = mm(chosen, own.astype(jnp.bfloat16)).astype(jnp.bfloat16)
        embed_ref[0, :, pl.ds(at, width)] = picked[0:per_shard]
        if slopes is None:
            continue
        along = mm(along_rows, block.astype(jnp.bfloat16))
        grad = sharpness * (along - radial_col * block)
        near, far = slopes[0 : slopes.shape[0] // 2], slopes[slopes.shape[0] // 2 :]
        grad_near = jnp.where(queries, grad[0:ROWS], grad[ROWS:rows])
        grad_far = jnp.where(queries, grad[ROWS:rows], grad[0:ROWS])
        update = []
        for side, side_grad in ((near, grad_near), (far, grad_far)):
            total = jnp.zeros((ROWS, width), jnp.float32)
            for text in range(texts):
                slope = side[text * ROWS : (text + 1) * ROWS].astype(jnp.float32)
                total += side_grad[text : text + 1] * slope
            update.append(total)
        at = pl.multiple_of((lax.div(shard, 2) ^ (o // 2)) * width, LANES)
        up_ref[:, pl.ds(at, width)] = update[0] + update[1]


def any_spec():
    return pl.BlockSpec(memory_space=pl.ANY)


def vmem_spec():
    return pl.BlockSpec(memory_space=pltpu.VMEM)


def smem_spec():
    return pl.BlockSpec(memory_space=pltpu.SMEM)


def exchange(x, axis, size):
    steps = [[(i, i ^ o) for i in range(size)] for o in reversed(range(1, size))]
    return [x] + [lax.ppermute(x, axis, step) for step in steps][::-1]


def split_body(
    query_passage_words,
    difficult_distractors,
    vocabulary_vectors,
    layer_weight_matrix,
    lowering_factor_matrix,
    raising_factor_matrix,
    logit_sharpness,
):
    shards, parts = lax.axis_size("dp"), lax.axis_size("mp")
    ids = query_passage_words[0]
    texts, length = ids.shape
    tokens = texts * length
    features, vocab = vocabulary_vectors.shape
    blocks = vocab // IDS_PER_BLOCK
    group_rows = 8 * pl.cdiv(vocab // IDS_PER_GROUP + 1, 8)
    per_shard, negatives = difficult_distractors.shape
    part_width = layer_weight_matrix.shape[1]
    width = part_width // shards
    params = pltpu.CompilerParams(vmem_limit_bytes=LARGE_VMEM)
    modest = pltpu.CompilerParams(vmem_limit_bytes=MODEST_VMEM)
    other_core = [(d, d ^ 1) for d in range(shards)]
    other_y = [(d, d ^ 2) for d in range(shards)]

    def columns(i, j):
        start = split_quarter(i, j) * width
        return lax.dynamic_slice(layer_weight_matrix, (0, start), (features, width))

    def project(base, span):
        stripes = pl.cdiv(span, STRIPE)
        extra_rows = (stripes + 1 + shards) * ROWS
        turned, member, weight0, weight1 = pl.pallas_call(
            functools.partial(gather_kernel, base=base),
            out_shape=[
                jax.ShapeDtypeStruct((features, span), jnp.bfloat16),
                jax.ShapeDtypeStruct((span, LANES), jnp.bfloat16),
                jax.ShapeDtypeStruct((features, width), jnp.bfloat16),
                jax.ShapeDtypeStruct((features, width), jnp.bfloat16),
            ],
            in_specs=[vmem_spec()] + [any_spec()] * 2,
            out_specs=[any_spec()] * 4,
            scratch_shapes=[
                pltpu.VMEM((features, span), jnp.bfloat16),
                pltpu.VMEM((span, LANES), jnp.bfloat16),
                pltpu.VMEM((blocks, features, IDS_PER_BLOCK), jnp.bfloat16),
                pltpu.VMEM((8 * pl.cdiv(span // LANES, 8), LANES), jnp.int32),
                pltpu.VMEM((texts, length), jnp.float32),
                pltpu.VMEM((group_rows, length), jnp.int32),
                pltpu.SMEM((group_rows, length), jnp.int32),
                pltpu.SemaphoreType.DMA((blocks,)),
                pltpu.SemaphoreType.DMA,
                pltpu.SemaphoreType.DMA((2,)),
                pltpu.SemaphoreType.DMA((2,)),
            ],
            compiler_params=params,
            name="gather",
        )(ids, vocabulary_vectors, layer_weight_matrix)

        def product(turned, weight):
            return mm(turned, weight, (((0,), (0,)), ((), ())))

        def narrow(x):
            return x.astype(jnp.bfloat16)

        core1 = lax.ppermute(narrow(product(turned, weight1)), "dp", other_core)
        own1 = lax.optimization_barrier(narrow(product(turned, weight0)))
        chip1 = narrow(own1.astype(jnp.float32) + core1.astype(jnp.float32))
        far = lax.ppermute(chip1, "dp", other_y)
        turned, _ = lax.optimization_barrier((turned, chip1))
        extra = pl.pallas_call(
            statistics_kernel,
            out_shape=jax.ShapeDtypeStruct((extra_rows, STRIPE), jnp.bfloat16),
            in_specs=[any_spec()] * 2 + [vmem_spec()] * 2,
            out_specs=vmem_spec(),
            scratch_shapes=[
                pltpu.VMEM((LANES, LANES), jnp.float32),
                pltpu.VMEM(turned.shape, turned.dtype),
                pltpu.VMEM(member.shape, member.dtype),
                pltpu.VMEM((ROWS, features), jnp.float32),
                pltpu.SemaphoreType.DMA((2,)),
            ],
            compiler_params=modest,
            cost_estimate=pl.CostEstimate(
                flops=2 * features * span * (ROWS + LANES),
                bytes_accessed=2 * features * span,
                transcendentals=0,
            ),
            name="statistics",
        )(turned, member, difficult_distractors, lowering_factor_matrix)
        common = (stripes + 1) * ROWS
        near = extra.astype(jnp.float32)
        across = lax.ppermute(extra, "dp", other_core).astype(jnp.float32)
        chip = near[0:common] + across[0:common]
        inputs = near[common : common + 2 * ROWS] + across[common + 2 * ROWS :]
        sent = narrow(jnp.concatenate([chip, inputs[ROWS:]]))
        sent = lax.ppermute(sent, "dp", other_y).astype(jnp.float32)
        extra = jnp.concatenate([chip, inputs[0:ROWS]]) + sent
        core0 = lax.ppermute(narrow(product(turned, columns(1, 0))), "dp", other_core)
        own0 = narrow(product(turned, columns(0, 0)))
        return own0, core0, far, extra, member

    first = project(0, FIRST)
    later, _ = lax.optimization_barrier((ids, first[0]))
    many = jnp.sum((later != 0).astype(jnp.int32)) > FIRST
    left = tokens - FIRST
    shapes = jax.eval_shape(lambda: project(FIRST, left))
    rest = lax.cond(
        many,
        lambda: project(FIRST, left),
        lambda: tuple(jnp.zeros(x.shape, x.dtype) for x in shapes),
    )
    sent, misc = pl.pallas_call(
        functools.partial(pool_kernel, model_width=float(features * shards)),
        out_shape=[
            jax.ShapeDtypeStruct(((texts + 1) * ROWS, width), jnp.bfloat16),
            jax.ShapeDtypeStruct((ROWS, width), jnp.float32),
        ],
        in_specs=[vmem_spec()] * 2 + [any_spec()] * 2 + [vmem_spec()] * 8,
        out_specs=[vmem_spec()] * 2,
        scratch_shapes=[
            pltpu.VMEM((LANES, width), jnp.bfloat16),
            pltpu.VMEM((ROWS, width), jnp.float32),
            pltpu.VMEM((texts * ROWS, width), jnp.float32),
            pltpu.VMEM((FIRST, width), jnp.bfloat16),
            pltpu.VMEM((FIRST, width), jnp.bfloat16),
            pltpu.SemaphoreType.DMA((2,)),
        ],
        compiler_params=modest,
        name="pool",
    )(ids, *first, *rest, raising_factor_matrix)
    far_side = lax.ppermute(sent, "group", [(0, 1), (1, 0)])
    rows = 2 * ROWS
    packed, slopes = pl.pallas_call(
        dots_kernel,
        out_shape=[
            jax.ShapeDtypeStruct((rows + width // LANES * rows, LANES), jnp.float32),
            jax.ShapeDtypeStruct((2 * texts * ROWS, width), jnp.bfloat16),
        ],
        in_specs=[vmem_spec()] * 2,
        out_specs=[vmem_spec()] * 2,
        compiler_params=modest,
        name="dots",
    )(sent, far_side)
    packed = exchange(packed, "dp", shards)
    dots = [x[0:rows] for x in packed]
    dots = (dots[0] + dots[1]) + (dots[2] + dots[3])
    slopes, dots = lax.optimization_barrier((slopes, dots))
    dots = exchange(dots, "mp", parts)
    slopes = [slopes, lax.ppermute(slopes, "dp", other_y)]
    embeddings, losses, update = pl.pallas_call(
        functools.partial(
            score_kernel, texts=texts, stripes=pl.cdiv(FIRST, STRIPE), negatives=negatives
        ),
        out_shape=[
            jax.ShapeDtypeStruct((1, per_shard, part_width), jnp.bfloat16),
            jax.ShapeDtypeStruct((1, per_shard), jnp.float32),
            jax.ShapeDtypeStruct((ROWS, part_width // 2), jnp.float32),
        ],
        in_specs=[vmem_spec()] * 11 + [smem_spec()],
        out_specs=[vmem_spec()] * 3,
        compiler_params=modest,
        name="score",
    )(*packed, *slopes, *dots, misc, logit_sharpness)
    other = lax.ppermute(update, "dp", other_core)
    core = lax.rem(lax.axis_index("dp"), 2)
    halves = [jnp.where(core == 0, update, other), jnp.where(core == 0, other, update)]
    return (embeddings, losses, jnp.concatenate(halves, axis=1))


def body(words, hard, vocabulary, weight, lowering, raising, sharpness):
    shards, parts = lax.axis_size("dp"), lax.axis_size("mp")
    texts, length = words.shape[1:]
    features, vocab = vocabulary.shape
    negatives = hard.shape[1]
    square = shards == 4 and features == weight.shape[1] == 4 * STRIPE and parts == shards
    small = texts <= ROWS - 2 and length == LANES and FIRST < texts * length <= 2048
    even = (texts * length - FIRST) % CHUNK == 0 and vocab % IDS_PER_BLOCK == 0
    fits = features * vocab <= 2**24 and features % (4 * LANES) == 0
    spare = pl.cdiv(FIRST, STRIPE) + negatives <= ROWS and lowering.shape[0] == ROWS
    fast = square and small and even and fits and spare and lax.axis_size("group") == 2
    chosen = split_body if fast else general_body
    return chosen(words, hard, vocabulary, weight, lowering, raising, sharpness)


def solution(mesh):
    in_specs = (
        P("group", None, None),
        P("dp", None),
        P("dp", None),
        P("dp", "mp"),
        P(),
        P(None, "mp"),
        P(),
    )
    out_specs = (P("group", "dp", "mp"), P("group", "dp"), P(None, "mp"))
    return jax.shard_map(body, mesh=mesh, in_specs=in_specs, out_specs=out_specs, check_vma=False)
```

```python
import functools

import jax
import jax.numpy as jnp
from jax import lax
from jax.experimental import pallas as pl
from jax.experimental.pallas import tpu as pltpu
from jax.sharding import PartitionSpec as P


def general_body(
    query_passage_words,
    difficult_distractors,
    vocabulary_vectors,
    layer_weight_matrix,
    lowering_factor_matrix,
    raising_factor_matrix,
    logit_sharpness,
):
    group_index = lax.axis_index("group")
    shard_index = lax.axis_index("dp")
    part_index = lax.axis_index("mp")
    shard_count = lax.axis_size("dp")
    side_ids = query_passage_words[0]
    text_count = side_ids.shape[0]
    length = side_ids.shape[1]
    per_shard = text_count // shard_count
    own_ids = lax.dynamic_slice_in_dim(side_ids, shard_index * per_shard, per_shard, 0)
    columns = jnp.take(vocabulary_vectors, side_ids.reshape(-1), axis=1)
    inputs = lax.all_to_all(columns, "dp", split_axis=1, concat_axis=0, tiled=True)
    tokens = inputs.shape[1]
    feature_width = raising_factor_matrix.shape[1]
    wide_inputs = inputs.astype(jnp.float32)
    inverse = lax.rsqrt(jnp.mean(wide_inputs * wide_inputs, axis=0) + 1e-05)
    normed_state = (wide_inputs * inverse[None, :]).astype(jnp.bfloat16)
    linear_map = lax.dot_general(
        lax.all_gather(layer_weight_matrix, "dp", axis=0, tiled=True),
        normed_state,
        (((0,), (0,)), ((), ())),
        preferred_element_type=jnp.float32,
    )
    reduced_sum = jnp.dot(
        lowering_factor_matrix, normed_state, preferred_element_type=jnp.float32
    ).astype(jnp.bfloat16)
    linear_map = linear_map + lax.dot_general(
        raising_factor_matrix,
        reduced_sum,
        (((0,), (0,)), ((), ())),
        preferred_element_type=jnp.float32,
    )
    own_inputs = lax.dynamic_slice_in_dim(
        inputs, part_index * feature_width, feature_width, 0
    ).astype(jnp.float32)
    hidden_state = own_inputs + jax.nn.silu(linear_map)
    mask = (own_ids != 0).astype(jnp.float32)
    counts = jnp.sum(mask, axis=1)
    summed = jnp.einsum("dnl,nl->nd", hidden_state.reshape(feature_width, per_shard, length), mask)
    pooled = (summed / counts[:, None]).astype(jnp.bfloat16)
    gathered = lax.all_gather(pooled, ("group", "dp"), axis=0, tiled=True)
    part_scores = lax.dot_general(
        pooled, gathered, (((1,), (1,)), ((), ())), preferred_element_type=jnp.float32
    )
    gathered_wide = gathered.astype(jnp.float32)
    part_norms = jnp.sum(gathered_wide * gathered_wide, axis=1)
    dots, norms = lax.psum((part_scores, part_norms), "mp")
    rnorm_all = lax.rsqrt(norms + 1e-06)
    all_count = gathered.shape[0]
    half_count = all_count // 2
    own_rows = (
        group_index * half_count + shard_index * per_shard + jnp.arange(per_shard, dtype=jnp.int32)
    )
    rnorm_own = jnp.take(rnorm_all, own_rows)
    cosine = dots * rnorm_own[:, None] * rnorm_all[None, :]
    multiplier_factor = logit_sharpness[0]
    scores = multiplier_factor * cosine
    column_ids = jnp.arange(all_count, dtype=jnp.int32)
    keep = column_ids[None, :] != own_rows[:, None]
    pair = (own_rows + half_count) % all_count
    weight = (group_index == 0).astype(jnp.float32)
    neg_cols = half_count + difficult_distractors
    top = jnp.max(jnp.where(keep, scores, -jnp.inf), axis=1)
    safe_scores = jnp.where(keep, scores, top[:, None])
    expd = jnp.where(keep, jnp.exp(safe_scores - top[:, None]), 0.0)
    neg_exp = (
        jnp.exp(jnp.minimum(jnp.take_along_axis(scores, neg_cols, axis=1) - top[:, None], 0.0))
        * weight
    )
    total = jnp.sum(expd, axis=1) + jnp.sum(neg_exp, axis=1)
    pair_score = jnp.take_along_axis(scores, pair[:, None], axis=1)[:, 0]
    losses = top + jnp.log(total) - pair_score
    onehot = (column_ids[None, None, :] == neg_cols[:, :, None]).astype(jnp.float32)
    probs = (expd + jnp.einsum("rk,rkc->rc", neg_exp, onehot)) / total[:, None]
    target = (column_ids[None, :] == pair[:, None]).astype(jnp.float32)
    grad_scores = (probs - target) / all_count
    coeff = (grad_scores * rnorm_own[:, None] * rnorm_all[None, :]).astype(jnp.bfloat16)
    along = jnp.dot(coeff, gathered, preferred_element_type=jnp.float32)
    pooled_wide = pooled.astype(jnp.float32)
    radial = jnp.sum(grad_scores * cosine, axis=1) * rnorm_own * rnorm_own
    embedding_gradient = multiplier_factor * (along - radial[:, None] * pooled_wide)
    token_grad = jnp.einsum("nd,nl->dnl", embedding_gradient / counts[:, None], mask).reshape(
        feature_width, tokens
    )
    sigma = jax.nn.sigmoid(linear_map)
    local = (token_grad * sigma * (1.0 + linear_map * (1.0 - sigma))).astype(jnp.bfloat16)
    up_portion = lax.dot_general(
        reduced_sum, local, (((1,), (1,)), ((), ())), preferred_element_type=jnp.float32
    )
    adapter_up_gradient = lax.psum(up_portion, ("group", "dp"))
    embeddings = (pooled_wide * rnorm_own[:, None]).astype(jnp.bfloat16)[None]
    return (embeddings, losses[None], adapter_up_gradient)


BLOCK_BITS, GROUP_BITS, LANE_BITS, ROW_BITS = 10, 9, 7, 4
IDS_PER_BLOCK = 1 << BLOCK_BITS
IDS_PER_GROUP = 1 << GROUP_BITS
CHUNK = 384
STRIPE = 256
ROWS = 1 << ROW_BITS
LANES = 1 << LANE_BITS
FEATURE_ROWS = 128
FIRST = 1152
TAKEN = 768
NT = (((1,), (1,)), ((), ()))
LARGE_VMEM, MODEST_VMEM = 44 * 1024 * 1024, 15 * 1024 * 1024


def mm(a, b, dims=(((1,), (0,)), ((), ()))):
    return lax.dot_general(a, b, dims, preferred_element_type=jnp.float32)


def split(x):
    high = x.astype(jnp.bfloat16)
    return high, (x - high.astype(jnp.float32)).astype(jnp.bfloat16)


def iota(shape, dim):
    return lax.broadcasted_iota(jnp.int32, shape, dim)


def quarter_of(dp_index, cores=2):
    return (dp_index % cores) * 2 + dp_index // cores


def split_quarter(i, j, cores=2):
    shard = lax.axis_index("dp")
    core, side_y = lax.rem(shard, cores), lax.div(shard, cores)
    return (core ^ i) * 2 + (side_y ^ j)


def take_lanes(x, lanes):
    numbers = lax.GatherDimensionNumbers(
        offset_dims=(),
        collapsed_slice_dims=(1,),
        start_index_map=(1,),
        operand_batching_dims=(0,),
        start_indices_batching_dims=(0,),
    )
    mode = lax.GatherScatterMode.PROMISE_IN_BOUNDS
    return lax.gather(x, lanes[..., None], numbers, slice_sizes=(1, 1), mode=mode)


def fetch(pairs, sems):
    copies = [pltpu.make_async_copy(a, b, sems.at[n]) for n, (a, b) in enumerate(pairs)]
    for copy in copies:
        copy.start()
    for copy in copies:
        copy.wait()


def gather_kernel(
    ids_ref,
    vocab_ref,
    weight_ref,
    turned_any,
    member_any,
    weight00,
    weight01,
    weight10,
    weight11,
    turned,
    member_ref,
    held,
    token_ref,
    ranks,
    counted,
    bounds,
    held_sems,
    bounds_sem,
    out_sems,
    weight_sems,
    base,
):
    texts, length = ids_ref.shape
    features, vocab = vocab_ref.shape
    blocks = vocab // IDS_PER_BLOCK
    groups = vocab // IDS_PER_GROUP
    span = member_ref.shape[0]

    def vocab_copy(b):
        columns = pl.ds(pl.multiple_of(b * IDS_PER_BLOCK, LANES), IDS_PER_BLOCK)
        return pltpu.make_async_copy(vocab_ref.at[:, columns], held.at[b], held_sems.at[b])

    weight_copies = []
    for q, weight in enumerate((weight00, weight01, weight10, weight11)):
        width = weight.shape[1]
        start = pl.multiple_of(split_quarter(q // 2, q % 2) * width, LANES)
        copy = pltpu.make_async_copy(
            weight_ref.at[:, pl.ds(start, width)], weight, weight_sems.at[q]
        )
        weight_copies.append(copy)
    vocab_copy(0).start()
    for b in range(1, blocks):
        vocab_copy(b).start()
    for copy in weight_copies:
        copy.start()

    ids = ids_ref[...]
    valid = ids != 0
    group_of = jnp.where(valid, lax.shift_right_logical(ids, GROUP_BITS), groups)
    group_rows = counted.shape[0]
    group_id = iota((group_rows, length), 0)
    below = jnp.zeros((group_rows, length), jnp.float32)
    for text in range(texts):
        below += jnp.where(group_of[text : text + 1] < group_id, 1.0, 0.0)
    before = jnp.broadcast_to(jnp.sum(below, axis=1, keepdims=True), (group_rows, length))
    counted[...] = before.astype(jnp.int32)
    bounds_copy = pltpu.make_async_copy(counted, bounds, bounds_sem)
    bounds_copy.start()
    earlier = jnp.where(iota((length, length), 0) < iota((length, length), 1), 1.0, 0.0).astype(
        jnp.bfloat16
    )
    for text in range(texts):
        here = jnp.where(group_of[text : text + 1] == group_id, 1.0, 0.0)
        inside = mm(here.astype(jnp.bfloat16), earlier)
        ranks[pl.ds(text, 1), :] = jnp.sum(here * (inside + before), axis=0, keepdims=True)
        before += jnp.broadcast_to(jnp.sum(here, axis=1, keepdims=True), (group_rows, length))
    text_of = iota((texts, length), 0)
    carried = jnp.where(valid, lax.shift_left(ids, ROW_BITS) + text_of, 0).astype(jnp.float32)
    rank = ranks[...]

    def place(p, carry):
        position = (iota((LANES, length), 0) + (p * LANES + base)).astype(jnp.float32)
        total = jnp.zeros((LANES, length), jnp.float32)
        for text in range(texts):
            total += jnp.where(rank[text : text + 1] == position, carried[text : text + 1], 0.0)
        found = jnp.broadcast_to(jnp.sum(total, axis=1, keepdims=True), (LANES, LANES))
        start = pl.multiple_of(p * LANES, LANES)
        row = found.T[0:1].astype(jnp.int32)
        token = lax.shift_right_logical(row, ROW_BITS)
        token_ref[pl.ds(p, 1), :] = jnp.where(token == 0, -vocab, token)
        found = found.astype(jnp.int32)
        real = (found >= ROWS) & ((found & (ROWS - 1)) == iota((LANES, LANES), 1))
        member_ref[pl.ds(start, LANES), :] = jnp.where(real, 1.0, 0.0).astype(jnp.bfloat16)
        turned[:, pl.ds(start, LANES)] = jnp.zeros((features, LANES), jnp.bfloat16)
        return carry

    lax.fori_loop(0, span // LANES, place, 0)
    bounds_copy.wait()

    def within(place):
        return jnp.clip(place - base, 0, span)

    def take(b, carry):
        vocab_copy(b).wait()
        for part in range(IDS_PER_BLOCK // IDS_PER_GROUP):
            group = b * (IDS_PER_BLOCK // IDS_PER_GROUP) + part
            first, last = within(bounds[group, 0]), within(bounds[group + 1, 0])
            begin = lax.shift_right_logical(first, LANE_BITS)
            end = lax.shift_right_logical(last + LANES - 1, LANE_BITS)

            def window(p, carry):
                at = pl.ds(pl.multiple_of(p * LANES, LANES), LANES)
                token = token_ref[pl.ds(p, 1), :] - group * IDS_PER_GROUP
                token = jnp.broadcast_to(token, (FEATURE_ROWS, LANES))
                lane = (token & (LANES - 1)).astype(jnp.int16)
                tile = lax.shift_right_arithmetic(token, LANE_BITS).astype(jnp.int16)
                pieces = [pl.ds(f, FEATURE_ROWS) for f in range(0, TAKEN, FEATURE_ROWS)]
                short = jnp.broadcast_to(token[0:1], (IDS_PER_GROUP, LANES)).astype(jnp.int16)
                picked = jnp.where(
                    short == iota((IDS_PER_GROUP, LANES), 0).astype(jnp.int16), 1.0, 0.0
                ).astype(jnp.bfloat16)
                columns = pl.ds(part * IDS_PER_GROUP, IDS_PER_GROUP)
                rest = pl.ds(TAKEN, features - TAKEN)
                product = mm(held[b, rest, columns], picked).astype(jnp.bfloat16)
                fresh = []
                for rows in pieces:
                    total = jnp.zeros((FEATURE_ROWS, LANES), jnp.bfloat16)
                    for j in range(IDS_PER_GROUP // LANES):
                        columns = pl.ds(part * IDS_PER_GROUP + j * LANES, LANES)
                        total = jnp.where(tile == j, take_lanes(held[b, rows, columns], lane), total)
                    fresh.append(total)
                pieces.append(rest)
                fresh.append(product)
                fresh = [turned[rows, at] + total for rows, total in zip(pieces, fresh)]
                for rows, total in zip(pieces, fresh):
                    turned[rows, at] = total
                return carry

            lax.fori_loop(begin, jnp.where(last > first, end, begin), window, 0)
        return carry

    lax.fori_loop(0, blocks, take, 0)
    fetch([(turned, turned_any), (member_ref, member_any)], out_sems)
    for copy in weight_copies:
        copy.wait()


def statistics_kernel(
    turned_any, member_any, hard_ref, lower_ref, extra_ref, small, turned, member_ref, spread, sems
):
    fetch([(turned_any, turned), (member_any, member_ref)], sems)
    features, span = turned.shape
    stripes = pl.cdiv(span, STRIPE)
    per_shard, negatives = hard_ref.shape
    shard = lax.axis_index("dp")
    small[...] = jnp.zeros_like(small)
    small[0:per_shard, stripes : stripes + negatives] = hard_ref[...].astype(jnp.float32)
    lower = lower_ref[:, pl.ds(pl.multiple_of(shard * features, LANES), features)]

    misc = jnp.zeros((ROWS, STRIPE), jnp.float32)
    residual = jnp.zeros((features, LANES), jnp.float32)
    for stripe in range(stripes):
        size = min(STRIPE, span - stripe * STRIPE)
        across = pl.ds(stripe * STRIPE, size)
        upright = turned[:, across]
        wide = upright.astype(jnp.float32)
        square = jnp.sum(wide * wide, axis=0, keepdims=True)
        reduced = mm(lower, upright)
        if size < STRIPE:
            none = jnp.zeros((ROWS, STRIPE - size), jnp.float32)
            reduced = jnp.concatenate([reduced, none], axis=1)
            square = jnp.concatenate([square, none[0:1]], axis=1)
        extra_ref[stripe * ROWS : (stripe + 1) * ROWS, :] = reduced.astype(jnp.bfloat16)
        misc = jnp.where(iota((ROWS, STRIPE), 0) == stripe, square, misc)
        residual += mm(upright, member_ref[across, :])
    hard = small[...].T[0:ROWS]
    for i in range(per_shard):
        misc += jnp.where(iota((ROWS, STRIPE), 1) == shard * per_shard + i, hard[:, i : i + 1], 0.0)
    extra_ref[stripes * ROWS : (stripes + 1) * ROWS, :] = misc.astype(jnp.bfloat16)
    residual = jnp.where(lax.axis_index("mp") == shard, residual.T[0:ROWS], 0.0)
    spread[...] = residual
    for q in range(4):
        start = (stripes + 1 + q) * ROWS
        quarter = pl.multiple_of(split_quarter(q // 2, q % 2) * STRIPE, LANES)
        extra_ref[start : start + ROWS, :] = spread[:, pl.ds(quarter, STRIPE)].astype(jnp.bfloat16)


def pool_kernel(
    ids_ref,
    own_ref,
    core_any,
    far_any,
    extra_ref,
    member_ref,
    own_rest,
    core_rest,
    far_rest,
    extra_rest,
    member_rest,
    raise_ref,
    sent_ref,
    misc_ref,
    raised,
    total,
    slopes,
    core_ref,
    far_ref,
    sems,
    model_width,
):
    texts, length = ids_ref.shape
    width = own_ref.shape[1]
    quarter = quarter_of(lax.axis_index("dp"))
    fetch([(core_any, core_ref), (far_any, far_ref)], sems)
    raised[...] = jnp.zeros_like(raised)
    raised[0:ROWS, :] = raise_ref[:, pl.ds(pl.multiple_of(quarter * width, LANES), width)]
    total[...] = jnp.zeros_like(total)
    slopes[...] = jnp.zeros_like(slopes)

    def add(refs, extra_ref, member_ref, base):
        span = member_ref.shape[0]
        stripes = pl.cdiv(span, STRIPE)

        def summed(start, size):
            return sum(ref[pl.ds(start, size), :].astype(jnp.float32) for ref in refs)

        misc = extra_ref[stripes * ROWS : (stripes + 1) * ROWS, :]
        if base == 0:
            misc_ref[...] = misc
        inverse = lax.rsqrt(misc / model_width + 1e-05)
        for k in range(stripes):
            size = min(STRIPE, span - k * STRIPE)
            scale = inverse[k : k + 1]
            reduced = (extra_ref[k * ROWS : (k + 1) * ROWS, :] * scale).astype(jnp.bfloat16)
            reduced = reduced.astype(jnp.float32)
            stacked = jnp.concatenate([reduced, jnp.broadcast_to(scale, (LANES - ROWS, STRIPE))])
            turned = stacked[:, 0:size].T
            low = turned.astype(jnp.bfloat16)
            linear = summed(k * STRIPE, size)
            linear = linear * turned[:, ROWS : ROWS + 1] + mm(low, raised[...])
            sigma = 1.0 / (1.0 + jnp.exp(-linear))
            slope = (sigma * (1.0 + linear * (1.0 - sigma))).astype(jnp.bfloat16)
            member = member_ref[pl.ds(k * STRIPE, size), :].astype(jnp.float32).T
            high, rest = split(linear * sigma)
            chosen = member[0:ROWS].astype(jnp.bfloat16)
            total[...] += mm(chosen, high) + mm(chosen, rest)
            spread = [reduced[:, 0:size] * member[text : text + 1] for text in range(texts)]
            slopes[...] += mm(jnp.concatenate(spread).astype(jnp.bfloat16), slope)
        total[...] += extra_ref[(stripes + 1) * ROWS : (stripes + 2) * ROWS, :]

    add((own_ref, core_ref, far_ref), extra_ref, member_ref, 0)
    real = (ids_ref[...] != 0).astype(jnp.float32)

    @pl.when(jnp.sum(real) > member_ref.shape[0])
    def _():
        add((own_rest, core_rest, far_rest), extra_rest, member_rest, member_ref.shape[0])

    counts = jnp.sum(real, axis=1, keepdims=True)
    pooled = total[0:texts] / counts
    pooled = jnp.concatenate([pooled, jnp.zeros((ROWS - texts, width), jnp.float32)])
    sent_ref[0:ROWS, :] = pooled.astype(jnp.bfloat16)
    for text in range(texts):
        part = slopes[text * ROWS : (text + 1) * ROWS, :] / counts[text : text + 1]
        sent_ref[(text + 1) * ROWS : (text + 2) * ROWS, :] = part.astype(jnp.bfloat16)


def both_sides(near, far):
    queries = lax.axis_index("group") == 0
    return jnp.concatenate([jnp.where(queries, near, far), jnp.where(queries, far, near)], axis=0)


def dots_kernel(near_ref, far_ref, packed_ref, slopes_ref):
    block = both_sides(near_ref[0:ROWS], far_ref[0:ROWS])
    rows = 2 * ROWS
    packed_ref[...] = jnp.zeros_like(packed_ref)
    packed_ref[0:rows, 0:rows] = mm(block, block, NT)
    for part in range(block.shape[1] // LANES):
        piece = block[:, part * LANES : (part + 1) * LANES]
        packed_ref[rows + part * rows : rows + (part + 1) * rows, :] = piece.astype(jnp.float32)
    size = near_ref.shape[0] - ROWS
    slopes_ref[0:size] = near_ref[ROWS:]
    slopes_ref[size:] = far_ref[ROWS:]


def score_kernel(*refs, texts, stripes, negatives):
    packed0, packed1, packed2, packed3, slopes0, slopes2 = refs[0:6]
    dots0, dots1, dots2, dots3, misc_ref, sharp_ref = refs[6:12]
    embed_ref, loss_ref, up_ref = refs[12:15]
    rows = 2 * ROWS
    per_shard = loss_ref.shape[1]
    group, shard = lax.axis_index("group"), lax.axis_index("dp")
    dots = ((dots0[...] + dots1[...]) + (dots2[...] + dots3[...]))[:, 0:rows]
    down, across = iota((rows, rows), 0), iota((rows, rows), 1)
    same = down == across
    real = (lax.rem(down, ROWS) < texts) & (lax.rem(across, ROWS) < texts)
    diagonal = jnp.where(same, dots, 0.0)
    rnorm_row = lax.rsqrt(jnp.sum(diagonal, axis=0, keepdims=True) + 1e-06)
    rnorm_col = lax.rsqrt(jnp.sum(diagonal, axis=1, keepdims=True) + 1e-06)
    sharpness = sharp_ref[0]
    cosine = dots * rnorm_col * rnorm_row
    scores = sharpness * cosine
    keep = real & ~same
    top = jnp.max(jnp.where(keep, scores, -jnp.inf), axis=0, keepdims=True)
    top = jnp.where(lax.rem(across[0:1], ROWS) < texts, top, 0.0)
    powers = jnp.exp(jnp.where(real, jnp.minimum(scores - top, 0.0), 0.0))
    hard = misc_ref[stripes : stripes + negatives, 0:rows].astype(jnp.int32) + ROWS
    times = jnp.zeros((rows, rows), jnp.float32)
    for k in range(negatives):
        times += jnp.where(hard[k : k + 1] == down, 1.0, 0.0)
    times = jnp.where(across < texts, times, 0.0)
    weights = (jnp.where(keep, 1.0, 0.0) + jnp.where(real, times, 0.0)) * powers
    total = jnp.sum(weights, axis=0, keepdims=True)
    total = jnp.where(lax.rem(across[0:1], ROWS) < texts, total, 1.0)
    pair = (down == lax.rem(across + ROWS, rows)) & real
    pair_score = jnp.sum(jnp.where(pair, scores, 0.0), axis=0, keepdims=True)
    losses = top + jnp.log(total) - pair_score
    grad_scores = (weights / total - jnp.where(pair, 1.0, 0.0)) / (2 * texts)
    coeff = (grad_scores * rnorm_col * rnorm_row).astype(jnp.bfloat16)
    radial = jnp.sum(grad_scores * cosine, axis=0, keepdims=True) * rnorm_row * rnorm_row

    first = shard * per_shard
    loss_col = jnp.sum(jnp.where(same, losses, 0.0), axis=1, keepdims=True)
    at = (iota((rows, LANES), 0) == group * ROWS + first + iota((rows, LANES), 1)) & (
        iota((rows, LANES), 1) < per_shard
    )
    loss_ref[...] = jnp.sum(jnp.where(at, loss_col, 0.0), axis=0, keepdims=True)[:, 0:per_shard]

    along_rows = coeff.astype(jnp.float32).T.astype(jnp.bfloat16)
    radial_col = jnp.sum(jnp.where(same, radial, 0.0), axis=1, keepdims=True)
    rnorm_own = jnp.where(group == 0, rnorm_col[0:ROWS], rnorm_col[ROWS:rows])
    chosen = iota((ROWS, ROWS), 1) == iota((ROWS, ROWS), 0) + first
    chosen = jnp.where(chosen & (iota((ROWS, ROWS), 0) < per_shard), 1.0, 0.0).astype(jnp.bfloat16)
    blocks = ((packed0, slopes0), (packed1, None), (packed2, slopes2), (packed3, None))
    for o, (packed, slopes) in enumerate(blocks):
        parts = packed.shape[0] // rows - 1
        width = parts * LANES
        halves = [packed[rows * (part + 1) : rows * (part + 2), :] for part in range(parts)]
        block = jnp.concatenate(halves, axis=1)
        queries = group == 0
        at = pl.multiple_of(quarter_of(shard ^ o) * width, LANES)
        own = jnp.where(queries, block[0:ROWS], block[ROWS:rows]) * rnorm_own
        picked = mm(chosen, own.astype(jnp.bfloat16)).astype(jnp.bfloat16)
        embed_ref[0, :, pl.ds(at, width)] = picked[0:per_shard]
        if slopes is None:
            continue
        along = mm(along_rows, block.astype(jnp.bfloat16))
        grad = sharpness * (along - radial_col * block)
        near, far = slopes[0 : slopes.shape[0] // 2], slopes[slopes.shape[0] // 2 :]
        grad_near = jnp.where(queries, grad[0:ROWS], grad[ROWS:rows])
        grad_far = jnp.where(queries, grad[ROWS:rows], grad[0:ROWS])
        update = []
        for side, side_grad in ((near, grad_near), (far, grad_far)):
            total = jnp.zeros((ROWS, width), jnp.float32)
            for text in range(texts):
                slope = side[text * ROWS : (text + 1) * ROWS].astype(jnp.float32)
                total += side_grad[text : text + 1] * slope
            update.append(total)
        at = pl.multiple_of((lax.div(shard, 2) ^ (o // 2)) * width, LANES)
        up_ref[:, pl.ds(at, width)] = update[0] + update[1]


def any_spec():
    return pl.BlockSpec(memory_space=pl.ANY)


def vmem_spec():
    return pl.BlockSpec(memory_space=pltpu.VMEM)


def smem_spec():
    return pl.BlockSpec(memory_space=pltpu.SMEM)


def exchange(x, axis, size):
    steps = [[(i, i ^ o) for i in range(size)] for o in reversed(range(1, size))]
    return [x] + [lax.ppermute(x, axis, step) for step in steps][::-1]


def split_body(
    query_passage_words,
    difficult_distractors,
    vocabulary_vectors,
    layer_weight_matrix,
    lowering_factor_matrix,
    raising_factor_matrix,
    logit_sharpness,
):
    shards, parts = lax.axis_size("dp"), lax.axis_size("mp")
    ids = query_passage_words[0]
    texts, length = ids.shape
    tokens = texts * length
    features, vocab = vocabulary_vectors.shape
    blocks = vocab // IDS_PER_BLOCK
    group_rows = 8 * pl.cdiv(vocab // IDS_PER_GROUP + 1, 8)
    per_shard, negatives = difficult_distractors.shape
    part_width = layer_weight_matrix.shape[1]
    width = part_width // shards
    params = pltpu.CompilerParams(vmem_limit_bytes=LARGE_VMEM)
    modest = pltpu.CompilerParams(vmem_limit_bytes=MODEST_VMEM)
    other_core = [(d, d ^ 1) for d in range(shards)]
    other_y = [(d, d ^ 2) for d in range(shards)]

    def project(base, span):
        stripes = pl.cdiv(span, STRIPE)
        extra_rows = (stripes + 1 + shards) * ROWS
        turned, member, *weights = pl.pallas_call(
            functools.partial(gather_kernel, base=base),
            out_shape=[
                jax.ShapeDtypeStruct((features, span), jnp.bfloat16),
                jax.ShapeDtypeStruct((span, LANES), jnp.bfloat16),
                *[jax.ShapeDtypeStruct((features, width), jnp.bfloat16)] * 4,
            ],
            in_specs=[vmem_spec()] + [any_spec()] * 2,
            out_specs=[any_spec()] * 6,
            scratch_shapes=[
                pltpu.VMEM((features, span), jnp.bfloat16),
                pltpu.VMEM((span, LANES), jnp.bfloat16),
                pltpu.VMEM((blocks, features, IDS_PER_BLOCK), jnp.bfloat16),
                pltpu.VMEM((8 * pl.cdiv(span // LANES, 8), LANES), jnp.int32),
                pltpu.VMEM((texts, length), jnp.float32),
                pltpu.VMEM((group_rows, length), jnp.int32),
                pltpu.SMEM((group_rows, length), jnp.int32),
                pltpu.SemaphoreType.DMA((blocks,)),
                pltpu.SemaphoreType.DMA,
                pltpu.SemaphoreType.DMA((2,)),
                pltpu.SemaphoreType.DMA((4,)),
            ],
            compiler_params=params,
            name="gather",
        )(ids, vocabulary_vectors, layer_weight_matrix)

        def product(turned, weight):
            return mm(turned, weight, (((0,), (0,)), ((), ())))

        def narrow(x):
            return x.astype(jnp.bfloat16)

        core1 = lax.ppermute(narrow(product(turned, weights[3])), "dp", other_core)
        chip1 = narrow(product(turned, weights[1]) + core1.astype(jnp.float32))
        far = lax.ppermute(chip1, "dp", other_y)
        turned, _ = lax.optimization_barrier((turned, chip1))
        extra = pl.pallas_call(
            statistics_kernel,
            out_shape=jax.ShapeDtypeStruct((extra_rows, STRIPE), jnp.bfloat16),
            in_specs=[any_spec()] * 2 + [vmem_spec()] * 2,
            out_specs=vmem_spec(),
            scratch_shapes=[
                pltpu.VMEM((LANES, LANES), jnp.float32),
                pltpu.VMEM(turned.shape, turned.dtype),
                pltpu.VMEM(member.shape, member.dtype),
                pltpu.VMEM((ROWS, features), jnp.float32),
                pltpu.SemaphoreType.DMA((2,)),
            ],
            compiler_params=modest,
            cost_estimate=pl.CostEstimate(
                flops=2 * features * span * (ROWS + LANES),
                bytes_accessed=2 * features * span,
                transcendentals=0,
            ),
            name="statistics",
        )(turned, member, difficult_distractors, lowering_factor_matrix)
        common = (stripes + 1) * ROWS
        near = extra.astype(jnp.float32)
        across = lax.ppermute(extra, "dp", other_core).astype(jnp.float32)
        chip = near[0:common] + across[0:common]
        inputs = near[common : common + 2 * ROWS] + across[common + 2 * ROWS :]
        sent = narrow(jnp.concatenate([chip, inputs[ROWS:]]))
        sent = lax.ppermute(sent, "dp", other_y).astype(jnp.float32)
        extra = jnp.concatenate([chip, inputs[0:ROWS]]) + sent
        core0 = lax.ppermute(narrow(product(turned, weights[2])), "dp", other_core)
        own0 = narrow(product(turned, weights[0]))
        return own0, core0, far, extra, member

    first = project(0, FIRST)
    later, _ = lax.optimization_barrier((ids, first[0]))
    many = jnp.sum((later != 0).astype(jnp.int32)) > FIRST
    left = tokens - FIRST
    shapes = jax.eval_shape(lambda: project(FIRST, left))
    rest = lax.cond(
        many,
        lambda: project(FIRST, left),
        lambda: tuple(jnp.zeros(x.shape, x.dtype) for x in shapes),
    )
    sent, misc = pl.pallas_call(
        functools.partial(pool_kernel, model_width=float(features * shards)),
        out_shape=[
            jax.ShapeDtypeStruct(((texts + 1) * ROWS, width), jnp.bfloat16),
            jax.ShapeDtypeStruct((ROWS, width), jnp.float32),
        ],
        in_specs=[vmem_spec()] * 2 + [any_spec()] * 2 + [vmem_spec()] * 8,
        out_specs=[vmem_spec()] * 2,
        scratch_shapes=[
            pltpu.VMEM((LANES, width), jnp.bfloat16),
            pltpu.VMEM((ROWS, width), jnp.float32),
            pltpu.VMEM((texts * ROWS, width), jnp.float32),
            pltpu.VMEM((FIRST, width), jnp.bfloat16),
            pltpu.VMEM((FIRST, width), jnp.bfloat16),
            pltpu.SemaphoreType.DMA((2,)),
        ],
        compiler_params=modest,
        name="pool",
    )(ids, *first, *rest, raising_factor_matrix)
    far_side = lax.ppermute(sent, "group", [(0, 1), (1, 0)])
    rows = 2 * ROWS
    packed, slopes = pl.pallas_call(
        dots_kernel,
        out_shape=[
            jax.ShapeDtypeStruct((rows + width // LANES * rows, LANES), jnp.float32),
            jax.ShapeDtypeStruct((2 * texts * ROWS, width), jnp.bfloat16),
        ],
        in_specs=[vmem_spec()] * 2,
        out_specs=[vmem_spec()] * 2,
        compiler_params=modest,
        name="dots",
    )(sent, far_side)
    packed = exchange(packed, "dp", shards)
    dots = [x[0:rows] for x in packed]
    dots = (dots[0] + dots[1]) + (dots[2] + dots[3])
    slopes, dots = lax.optimization_barrier((slopes, dots))
    dots = exchange(dots, "mp", parts)
    slopes = [slopes, lax.ppermute(slopes, "dp", other_y)]
    embeddings, losses, update = pl.pallas_call(
        functools.partial(
            score_kernel, texts=texts, stripes=pl.cdiv(FIRST, STRIPE), negatives=negatives
        ),
        out_shape=[
            jax.ShapeDtypeStruct((1, per_shard, part_width), jnp.bfloat16),
            jax.ShapeDtypeStruct((1, per_shard), jnp.float32),
            jax.ShapeDtypeStruct((ROWS, part_width // 2), jnp.float32),
        ],
        in_specs=[vmem_spec()] * 11 + [smem_spec()],
        out_specs=[vmem_spec()] * 3,
        compiler_params=modest,
        name="score",
    )(*packed, *slopes, *dots, misc, logit_sharpness)
    other = lax.ppermute(update, "dp", other_core)
    core = lax.rem(lax.axis_index("dp"), 2)
    halves = [jnp.where(core == 0, update, other), jnp.where(core == 0, other, update)]
    return (embeddings, losses, jnp.concatenate(halves, axis=1))


def body(words, hard, vocabulary, weight, lowering, raising, sharpness):
    shards, parts = lax.axis_size("dp"), lax.axis_size("mp")
    texts, length = words.shape[1:]
    features, vocab = vocabulary.shape
    negatives = hard.shape[1]
    square = shards == 4 and features == weight.shape[1] == 4 * STRIPE and parts == shards
    small = texts <= ROWS - 2 and length == LANES and FIRST < texts * length <= 2048
    even = (texts * length - FIRST) % CHUNK == 0 and vocab % IDS_PER_BLOCK == 0
    fits = features * vocab <= 2**24 and features % (4 * LANES) == 0
    spare = pl.cdiv(FIRST, STRIPE) + negatives <= ROWS and lowering.shape[0] == ROWS
    fast = square and small and even and fits and spare and lax.axis_size("group") == 2
    chosen = split_body if fast else general_body
    return chosen(words, hard, vocabulary, weight, lowering, raising, sharpness)


def solution(mesh):
    in_specs = (
        P("group", None, None),
        P("dp", None),
        P("dp", None),
        P("dp", "mp"),
        P(),
        P(None, "mp"),
        P(),
    )
    out_specs = (P("group", "dp", "mp"), P("group", "dp"), P(None, "mp"))
    return jax.shard_map(body, mesh=mesh, in_specs=in_specs, out_specs=out_specs, check_vma=False)
```

```python
import functools

import jax
import jax.numpy as jnp
from jax import lax
from jax.experimental import pallas as pl
from jax.experimental.pallas import tpu as pltpu
from jax.sharding import PartitionSpec as P


def general_body(
    query_passage_words,
    difficult_distractors,
    vocabulary_vectors,
    layer_weight_matrix,
    lowering_factor_matrix,
    raising_factor_matrix,
    logit_sharpness,
):
    group_index = lax.axis_index("group")
    shard_index = lax.axis_index("dp")
    part_index = lax.axis_index("mp")
    shard_count = lax.axis_size("dp")
    side_ids = query_passage_words[0]
    text_count = side_ids.shape[0]
    length = side_ids.shape[1]
    per_shard = text_count // shard_count
    own_ids = lax.dynamic_slice_in_dim(side_ids, shard_index * per_shard, per_shard, 0)
    columns = jnp.take(vocabulary_vectors, side_ids.reshape(-1), axis=1)
    inputs = lax.all_to_all(columns, "dp", split_axis=1, concat_axis=0, tiled=True)
    tokens = inputs.shape[1]
    feature_width = raising_factor_matrix.shape[1]
    wide_inputs = inputs.astype(jnp.float32)
    inverse = lax.rsqrt(jnp.mean(wide_inputs * wide_inputs, axis=0) + 1e-05)
    normed_state = (wide_inputs * inverse[None, :]).astype(jnp.bfloat16)
    linear_map = lax.dot_general(
        lax.all_gather(layer_weight_matrix, "dp", axis=0, tiled=True),
        normed_state,
        (((0,), (0,)), ((), ())),
        preferred_element_type=jnp.float32,
    )
    reduced_sum = jnp.dot(
        lowering_factor_matrix, normed_state, preferred_element_type=jnp.float32
    ).astype(jnp.bfloat16)
    linear_map = linear_map + lax.dot_general(
        raising_factor_matrix,
        reduced_sum,
        (((0,), (0,)), ((), ())),
        preferred_element_type=jnp.float32,
    )
    own_inputs = lax.dynamic_slice_in_dim(
        inputs, part_index * feature_width, feature_width, 0
    ).astype(jnp.float32)
    hidden_state = own_inputs + jax.nn.silu(linear_map)
    mask = (own_ids != 0).astype(jnp.float32)
    counts = jnp.sum(mask, axis=1)
    summed = jnp.einsum("dnl,nl->nd", hidden_state.reshape(feature_width, per_shard, length), mask)
    pooled = (summed / counts[:, None]).astype(jnp.bfloat16)
    gathered = lax.all_gather(pooled, ("group", "dp"), axis=0, tiled=True)
    part_scores = lax.dot_general(
        pooled, gathered, (((1,), (1,)), ((), ())), preferred_element_type=jnp.float32
    )
    gathered_wide = gathered.astype(jnp.float32)
    part_norms = jnp.sum(gathered_wide * gathered_wide, axis=1)
    dots, norms = lax.psum((part_scores, part_norms), "mp")
    rnorm_all = lax.rsqrt(norms + 1e-06)
    all_count = gathered.shape[0]
    half_count = all_count // 2
    own_rows = (
        group_index * half_count + shard_index * per_shard + jnp.arange(per_shard, dtype=jnp.int32)
    )
    rnorm_own = jnp.take(rnorm_all, own_rows)
    cosine = dots * rnorm_own[:, None] * rnorm_all[None, :]
    multiplier_factor = logit_sharpness[0]
    scores = multiplier_factor * cosine
    column_ids = jnp.arange(all_count, dtype=jnp.int32)
    keep = column_ids[None, :] != own_rows[:, None]
    pair = (own_rows + half_count) % all_count
    weight = (group_index == 0).astype(jnp.float32)
    neg_cols = half_count + difficult_distractors
    top = jnp.max(jnp.where(keep, scores, -jnp.inf), axis=1)
    safe_scores = jnp.where(keep, scores, top[:, None])
    expd = jnp.where(keep, jnp.exp(safe_scores - top[:, None]), 0.0)
    neg_exp = (
        jnp.exp(jnp.minimum(jnp.take_along_axis(scores, neg_cols, axis=1) - top[:, None], 0.0))
        * weight
    )
    total = jnp.sum(expd, axis=1) + jnp.sum(neg_exp, axis=1)
    pair_score = jnp.take_along_axis(scores, pair[:, None], axis=1)[:, 0]
    losses = top + jnp.log(total) - pair_score
    onehot = (column_ids[None, None, :] == neg_cols[:, :, None]).astype(jnp.float32)
    probs = (expd + jnp.einsum("rk,rkc->rc", neg_exp, onehot)) / total[:, None]
    target = (column_ids[None, :] == pair[:, None]).astype(jnp.float32)
    grad_scores = (probs - target) / all_count
    coeff = (grad_scores * rnorm_own[:, None] * rnorm_all[None, :]).astype(jnp.bfloat16)
    along = jnp.dot(coeff, gathered, preferred_element_type=jnp.float32)
    pooled_wide = pooled.astype(jnp.float32)
    radial = jnp.sum(grad_scores * cosine, axis=1) * rnorm_own * rnorm_own
    embedding_gradient = multiplier_factor * (along - radial[:, None] * pooled_wide)
    token_grad = jnp.einsum("nd,nl->dnl", embedding_gradient / counts[:, None], mask).reshape(
        feature_width, tokens
    )
    sigma = jax.nn.sigmoid(linear_map)
    local = (token_grad * sigma * (1.0 + linear_map * (1.0 - sigma))).astype(jnp.bfloat16)
    up_portion = lax.dot_general(
        reduced_sum, local, (((1,), (1,)), ((), ())), preferred_element_type=jnp.float32
    )
    adapter_up_gradient = lax.psum(up_portion, ("group", "dp"))
    embeddings = (pooled_wide * rnorm_own[:, None]).astype(jnp.bfloat16)[None]
    return (embeddings, losses[None], adapter_up_gradient)


BLOCK_BITS, GROUP_BITS, LANE_BITS, ROW_BITS = 10, 9, 7, 4
IDS_PER_BLOCK = 1 << BLOCK_BITS
IDS_PER_GROUP = 1 << GROUP_BITS
CHUNK = 384
STRIPE = 256
ROWS = 1 << ROW_BITS
LANES = 1 << LANE_BITS
FEATURE_ROWS = 128
FIRST = 1152
TAKEN = 768
NT = (((1,), (1,)), ((), ()))
LARGE_VMEM, MODEST_VMEM = 44 * 1024 * 1024, 15 * 1024 * 1024


def mm(a, b, dims=(((1,), (0,)), ((), ()))):
    return lax.dot_general(a, b, dims, preferred_element_type=jnp.float32)


def split(x):
    high = x.astype(jnp.bfloat16)
    return high, (x - high.astype(jnp.float32)).astype(jnp.bfloat16)


def iota(shape, dim):
    return lax.broadcasted_iota(jnp.int32, shape, dim)


def quarter_of(dp_index, cores=2):
    return (dp_index % cores) * 2 + dp_index // cores


def split_quarter(i, j, cores=2):
    shard = lax.axis_index("dp")
    core, side_y = lax.rem(shard, cores), lax.div(shard, cores)
    return (core ^ i) * 2 + (side_y ^ j)


def take_lanes(x, lanes):
    numbers = lax.GatherDimensionNumbers(
        offset_dims=(),
        collapsed_slice_dims=(1,),
        start_index_map=(1,),
        operand_batching_dims=(0,),
        start_indices_batching_dims=(0,),
    )
    mode = lax.GatherScatterMode.PROMISE_IN_BOUNDS
    return lax.gather(x, lanes[..., None], numbers, slice_sizes=(1, 1), mode=mode)


def load_ids(ref):
    return jnp.concatenate([ref[text] for text in range(ref.shape[0])], axis=0)


def fetch(pairs, sems):
    copies = [pltpu.make_async_copy(a, b, sems.at[n]) for n, (a, b) in enumerate(pairs)]
    for copy in copies:
        copy.start()
    for copy in copies:
        copy.wait()


def gather_kernel(
    ids_ref,
    vocab_ref,
    weight_ref,
    turned_any,
    member_any,
    weight00,
    weight01,
    weight10,
    weight11,
    turned,
    member_ref,
    held,
    token_ref,
    plain_ids,
    ranks,
    counted,
    bounds,
    held_sems,
    bounds_sem,
    out_sems,
    weight_sems,
    base,
):
    texts, _, length = ids_ref.shape
    features, vocab = vocab_ref.shape
    blocks = vocab // IDS_PER_BLOCK
    groups = vocab // IDS_PER_GROUP
    span = member_ref.shape[0]

    def vocab_copy(b):
        columns = pl.ds(pl.multiple_of(b * IDS_PER_BLOCK, LANES), IDS_PER_BLOCK)
        return pltpu.make_async_copy(vocab_ref.at[:, columns], held.at[b], held_sems.at[b])

    weight_copies = []
    for q, weight in enumerate((weight00, weight01, weight10, weight11)):
        width = weight.shape[1]
        start = pl.multiple_of(split_quarter(q // 2, q % 2) * width, LANES)
        copy = pltpu.make_async_copy(
            weight_ref.at[:, pl.ds(start, width)], weight, weight_sems.at[q]
        )
        weight_copies.append(copy)
    vocab_copy(0).start()
    for b in range(1, blocks):
        vocab_copy(b).start()
    for copy in weight_copies:
        copy.start()

    for text in range(texts):
        plain_ids[pl.ds(text, 1), :] = ids_ref[text]
    ids = plain_ids[...]
    valid = ids != 0
    group_of = jnp.where(valid, lax.shift_right_logical(ids, GROUP_BITS), groups)
    group_rows = counted.shape[0]
    group_id = iota((group_rows, length), 0)
    below = jnp.zeros((group_rows, length), jnp.float32)
    for text in range(texts):
        below += jnp.where(group_of[text : text + 1] < group_id, 1.0, 0.0)
    before = jnp.broadcast_to(jnp.sum(below, axis=1, keepdims=True), (group_rows, length))
    counted[...] = before.astype(jnp.int32)
    bounds_copy = pltpu.make_async_copy(counted, bounds, bounds_sem)
    bounds_copy.start()
    earlier = jnp.where(iota((length, length), 0) < iota((length, length), 1), 1.0, 0.0).astype(
        jnp.bfloat16
    )
    for text in range(texts):
        here = jnp.where(group_of[text : text + 1] == group_id, 1.0, 0.0)
        inside = mm(here.astype(jnp.bfloat16), earlier)
        ranks[pl.ds(text, 1), :] = jnp.sum(here * (inside + before), axis=0, keepdims=True)
        before += jnp.broadcast_to(jnp.sum(here, axis=1, keepdims=True), (group_rows, length))
    text_of = iota((texts, length), 0)
    carried = jnp.where(valid, lax.shift_left(ids, ROW_BITS) + text_of, 0).astype(jnp.float32)
    rank = ranks[...]

    def place(p, carry):
        position = (iota((LANES, length), 0) + (p * LANES + base)).astype(jnp.float32)
        total = jnp.zeros((LANES, length), jnp.float32)
        for text in range(texts):
            total += jnp.where(rank[text : text + 1] == position, carried[text : text + 1], 0.0)
        found = jnp.broadcast_to(jnp.sum(total, axis=1, keepdims=True), (LANES, LANES))
        start = pl.multiple_of(p * LANES, LANES)
        row = found.T[0:1].astype(jnp.int32)
        token = lax.shift_right_logical(row, ROW_BITS)
        token_ref[pl.ds(p, 1), :] = jnp.where(token == 0, -vocab, token)
        found = found.astype(jnp.int32)
        real = (found >= ROWS) & ((found & (ROWS - 1)) == iota((LANES, LANES), 1))
        member_ref[pl.ds(start, LANES), :] = jnp.where(real, 1.0, 0.0).astype(jnp.bfloat16)
        turned[:, pl.ds(start, LANES)] = jnp.zeros((features, LANES), jnp.bfloat16)
        return carry

    lax.fori_loop(0, span // LANES, place, 0)
    bounds_copy.wait()

    def within(place):
        return jnp.clip(place - base, 0, span)

    def take(b, carry):
        vocab_copy(b).wait()
        for part in range(IDS_PER_BLOCK // IDS_PER_GROUP):
            group = b * (IDS_PER_BLOCK // IDS_PER_GROUP) + part
            first, last = within(bounds[group, 0]), within(bounds[group + 1, 0])
            begin = lax.shift_right_logical(first, LANE_BITS)
            end = lax.shift_right_logical(last + LANES - 1, LANE_BITS)

            def window(p, carry):
                at = pl.ds(pl.multiple_of(p * LANES, LANES), LANES)
                token = token_ref[pl.ds(p, 1), :] - group * IDS_PER_GROUP
                token = jnp.broadcast_to(token, (FEATURE_ROWS, LANES))
                lane = (token & (LANES - 1)).astype(jnp.int16)
                tile = lax.shift_right_arithmetic(token, LANE_BITS).astype(jnp.int16)
                pieces = [pl.ds(f, FEATURE_ROWS) for f in range(0, TAKEN, FEATURE_ROWS)]
                short = jnp.broadcast_to(token[0:1], (IDS_PER_GROUP, LANES)).astype(jnp.int16)
                picked = jnp.where(
                    short == iota((IDS_PER_GROUP, LANES), 0).astype(jnp.int16), 1.0, 0.0
                ).astype(jnp.bfloat16)
                columns = pl.ds(part * IDS_PER_GROUP, IDS_PER_GROUP)
                rest = pl.ds(TAKEN, features - TAKEN)
                product = mm(held[b, rest, columns], picked).astype(jnp.bfloat16)
                fresh = []
                for rows in pieces:
                    total = jnp.zeros((FEATURE_ROWS, LANES), jnp.bfloat16)
                    for j in range(IDS_PER_GROUP // LANES):
                        columns = pl.ds(part * IDS_PER_GROUP + j * LANES, LANES)
                        total = jnp.where(tile == j, take_lanes(held[b, rows, columns], lane), total)
                    fresh.append(total)
                pieces.append(rest)
                fresh.append(product)
                fresh = [turned[rows, at] + total for rows, total in zip(pieces, fresh)]
                for rows, total in zip(pieces, fresh):
                    turned[rows, at] = total
                return carry

            lax.fori_loop(begin, jnp.where(last > first, end, begin), window, 0)
        return carry

    lax.fori_loop(0, blocks, take, 0)
    fetch([(turned, turned_any), (member_ref, member_any)], out_sems)
    for copy in weight_copies:
        copy.wait()


def statistics_kernel(
    turned_any, member_any, hard_ref, lower_ref, extra_ref, small, turned, member_ref, spread, sems
):
    fetch([(turned_any, turned), (member_any, member_ref)], sems)
    features, span = turned.shape
    stripes = pl.cdiv(span, STRIPE)
    per_shard, negatives = hard_ref.shape
    shard = lax.axis_index("dp")
    small[...] = jnp.zeros_like(small)
    small[0:per_shard, stripes : stripes + negatives] = hard_ref[...].astype(jnp.float32)
    lower = lower_ref[:, pl.ds(pl.multiple_of(shard * features, LANES), features)]

    misc = jnp.zeros((ROWS, STRIPE), jnp.float32)
    residual = jnp.zeros((features, LANES), jnp.float32)
    for stripe in range(stripes):
        size = min(STRIPE, span - stripe * STRIPE)
        across = pl.ds(stripe * STRIPE, size)
        upright = turned[:, across]
        wide = upright.astype(jnp.float32)
        square = jnp.sum(wide * wide, axis=0, keepdims=True)
        reduced = mm(lower, upright)
        if size < STRIPE:
            none = jnp.zeros((ROWS, STRIPE - size), jnp.float32)
            reduced = jnp.concatenate([reduced, none], axis=1)
            square = jnp.concatenate([square, none[0:1]], axis=1)
        extra_ref[stripe * ROWS : (stripe + 1) * ROWS, :] = reduced.astype(jnp.bfloat16)
        misc = jnp.where(iota((ROWS, STRIPE), 0) == stripe, square, misc)
        residual += mm(upright, member_ref[across, :])
    hard = small[...].T[0:ROWS]
    for i in range(per_shard):
        misc += jnp.where(iota((ROWS, STRIPE), 1) == shard * per_shard + i, hard[:, i : i + 1], 0.0)
    extra_ref[stripes * ROWS : (stripes + 1) * ROWS, :] = misc.astype(jnp.bfloat16)
    residual = jnp.where(lax.axis_index("mp") == shard, residual.T[0:ROWS], 0.0)
    spread[...] = residual
    for q in range(4):
        start = (stripes + 1 + q) * ROWS
        quarter = pl.multiple_of(split_quarter(q // 2, q % 2) * STRIPE, LANES)
        extra_ref[start : start + ROWS, :] = spread[:, pl.ds(quarter, STRIPE)].astype(jnp.bfloat16)


def pool_kernel(
    ids_ref,
    own_ref,
    core_any,
    far_any,
    extra_ref,
    member_ref,
    own_rest,
    core_rest,
    far_rest,
    extra_rest,
    member_rest,
    raise_ref,
    sent_ref,
    misc_ref,
    raised,
    total,
    slopes,
    core_ref,
    far_ref,
    sems,
    model_width,
):
    texts = ids_ref.shape[0]
    width = own_ref.shape[1]
    quarter = quarter_of(lax.axis_index("dp"))
    fetch([(core_any, core_ref), (far_any, far_ref)], sems)
    raised[...] = jnp.zeros_like(raised)
    raised[0:ROWS, :] = raise_ref[:, pl.ds(pl.multiple_of(quarter * width, LANES), width)]
    total[...] = jnp.zeros_like(total)
    slopes[...] = jnp.zeros_like(slopes)

    def add(refs, extra_ref, member_ref, base):
        span = member_ref.shape[0]
        stripes = pl.cdiv(span, STRIPE)

        def summed(start, size):
            return sum(ref[pl.ds(start, size), :].astype(jnp.float32) for ref in refs)

        misc = extra_ref[stripes * ROWS : (stripes + 1) * ROWS, :]
        if base == 0:
            misc_ref[...] = misc
        inverse = lax.rsqrt(misc / model_width + 1e-05)
        for k in range(stripes):
            size = min(STRIPE, span - k * STRIPE)
            scale = inverse[k : k + 1]
            reduced = (extra_ref[k * ROWS : (k + 1) * ROWS, :] * scale).astype(jnp.bfloat16)
            reduced = reduced.astype(jnp.float32)
            stacked = jnp.concatenate([reduced, jnp.broadcast_to(scale, (LANES - ROWS, STRIPE))])
            turned = stacked[:, 0:size].T
            low = turned.astype(jnp.bfloat16)
            linear = summed(k * STRIPE, size)
            linear = linear * turned[:, ROWS : ROWS + 1] + mm(low, raised[...])
            sigma = 1.0 / (1.0 + jnp.exp(-linear))
            slope = (sigma * (1.0 + linear * (1.0 - sigma))).astype(jnp.bfloat16)
            member = member_ref[pl.ds(k * STRIPE, size), :].astype(jnp.float32).T
            high, rest = split(linear * sigma)
            chosen = member[0:ROWS].astype(jnp.bfloat16)
            total[...] += mm(chosen, high) + mm(chosen, rest)
            spread = [reduced[:, 0:size] * member[text : text + 1] for text in range(texts)]
            slopes[...] += mm(jnp.concatenate(spread).astype(jnp.bfloat16), slope)
        total[...] += extra_ref[(stripes + 1) * ROWS : (stripes + 2) * ROWS, :]

    add((own_ref, core_ref, far_ref), extra_ref, member_ref, 0)
    real = (load_ids(ids_ref) != 0).astype(jnp.float32)

    @pl.when(jnp.sum(real) > member_ref.shape[0])
    def _():
        add((own_rest, core_rest, far_rest), extra_rest, member_rest, member_ref.shape[0])

    counts = jnp.sum(real, axis=1, keepdims=True)
    pooled = total[0:texts] / counts
    pooled = jnp.concatenate([pooled, jnp.zeros((ROWS - texts, width), jnp.float32)])
    sent_ref[0:ROWS, :] = pooled.astype(jnp.bfloat16)
    for text in range(texts):
        part = slopes[text * ROWS : (text + 1) * ROWS, :] / counts[text : text + 1]
        sent_ref[(text + 1) * ROWS : (text + 2) * ROWS, :] = part.astype(jnp.bfloat16)


def both_sides(near, far):
    queries = lax.axis_index("group") == 0
    return jnp.concatenate([jnp.where(queries, near, far), jnp.where(queries, far, near)], axis=0)


def dots_kernel(near_ref, far_ref, packed_ref, slopes_ref):
    block = both_sides(near_ref[0:ROWS], far_ref[0:ROWS])
    rows = 2 * ROWS
    packed_ref[...] = jnp.zeros_like(packed_ref)
    packed_ref[0:rows, 0:rows] = mm(block, block, NT)
    for part in range(block.shape[1] // LANES):
        piece = block[:, part * LANES : (part + 1) * LANES]
        packed_ref[rows + part * rows : rows + (part + 1) * rows, :] = piece.astype(jnp.float32)
    size = near_ref.shape[0] - ROWS
    slopes_ref[0:size] = near_ref[ROWS:]
    slopes_ref[size:] = far_ref[ROWS:]


def score_kernel(*refs, texts, stripes, negatives):
    packed0, packed1, packed2, packed3, slopes0, slopes2 = refs[0:6]
    dots0, dots1, dots2, dots3, misc_ref, sharp_ref = refs[6:12]
    embed_ref, loss_ref, up_ref = refs[12:15]
    rows = 2 * ROWS
    per_shard = loss_ref.shape[1]
    group, shard = lax.axis_index("group"), lax.axis_index("dp")
    dots = ((dots0[...] + dots1[...]) + (dots2[...] + dots3[...]))[:, 0:rows]
    down, across = iota((rows, rows), 0), iota((rows, rows), 1)
    same = down == across
    real = (lax.rem(down, ROWS) < texts) & (lax.rem(across, ROWS) < texts)
    diagonal = jnp.where(same, dots, 0.0)
    rnorm_row = lax.rsqrt(jnp.sum(diagonal, axis=0, keepdims=True) + 1e-06)
    rnorm_col = lax.rsqrt(jnp.sum(diagonal, axis=1, keepdims=True) + 1e-06)
    sharpness = sharp_ref[0]
    cosine = dots * rnorm_col * rnorm_row
    scores = sharpness * cosine
    keep = real & ~same
    top = jnp.max(jnp.where(keep, scores, -jnp.inf), axis=0, keepdims=True)
    top = jnp.where(lax.rem(across[0:1], ROWS) < texts, top, 0.0)
    powers = jnp.exp(jnp.where(real, jnp.minimum(scores - top, 0.0), 0.0))
    hard = misc_ref[stripes : stripes + negatives, 0:rows].astype(jnp.int32) + ROWS
    times = jnp.zeros((rows, rows), jnp.float32)
    for k in range(negatives):
        times += jnp.where(hard[k : k + 1] == down, 1.0, 0.0)
    times = jnp.where(across < texts, times, 0.0)
    weights = (jnp.where(keep, 1.0, 0.0) + jnp.where(real, times, 0.0)) * powers
    total = jnp.sum(weights, axis=0, keepdims=True)
    total = jnp.where(lax.rem(across[0:1], ROWS) < texts, total, 1.0)
    pair = (down == lax.rem(across + ROWS, rows)) & real
    pair_score = jnp.sum(jnp.where(pair, scores, 0.0), axis=0, keepdims=True)
    losses = top + jnp.log(total) - pair_score
    grad_scores = (weights / total - jnp.where(pair, 1.0, 0.0)) / (2 * texts)
    coeff = (grad_scores * rnorm_col * rnorm_row).astype(jnp.bfloat16)
    radial = jnp.sum(grad_scores * cosine, axis=0, keepdims=True) * rnorm_row * rnorm_row

    first = shard * per_shard
    loss_col = jnp.sum(jnp.where(same, losses, 0.0), axis=1, keepdims=True)
    at = (iota((rows, LANES), 0) == group * ROWS + first + iota((rows, LANES), 1)) & (
        iota((rows, LANES), 1) < per_shard
    )
    loss_ref[...] = jnp.sum(jnp.where(at, loss_col, 0.0), axis=0, keepdims=True)[:, 0:per_shard]

    along_rows = coeff.astype(jnp.float32).T.astype(jnp.bfloat16)
    radial_col = jnp.sum(jnp.where(same, radial, 0.0), axis=1, keepdims=True)
    rnorm_own = jnp.where(group == 0, rnorm_col[0:ROWS], rnorm_col[ROWS:rows])
    chosen = iota((ROWS, ROWS), 1) == iota((ROWS, ROWS), 0) + first
    chosen = jnp.where(chosen & (iota((ROWS, ROWS), 0) < per_shard), 1.0, 0.0).astype(jnp.bfloat16)
    blocks = ((packed0, slopes0), (packed1, None), (packed2, slopes2), (packed3, None))
    for o, (packed, slopes) in enumerate(blocks):
        parts = packed.shape[0] // rows - 1
        width = parts * LANES
        halves = [packed[rows * (part + 1) : rows * (part + 2), :] for part in range(parts)]
        block = jnp.concatenate(halves, axis=1)
        queries = group == 0
        at = pl.multiple_of(quarter_of(shard ^ o) * width, LANES)
        own = jnp.where(queries, block[0:ROWS], block[ROWS:rows]) * rnorm_own
        picked = mm(chosen, own.astype(jnp.bfloat16)).astype(jnp.bfloat16)
        embed_ref[0, :, pl.ds(at, width)] = picked[0:per_shard]
        if slopes is None:
            continue
        along = mm(along_rows, block.astype(jnp.bfloat16))
        grad = sharpness * (along - radial_col * block)
        near, far = slopes[0 : slopes.shape[0] // 2], slopes[slopes.shape[0] // 2 :]
        grad_near = jnp.where(queries, grad[0:ROWS], grad[ROWS:rows])
        grad_far = jnp.where(queries, grad[ROWS:rows], grad[0:ROWS])
        update = []
        for side, side_grad in ((near, grad_near), (far, grad_far)):
            total = jnp.zeros((ROWS, width), jnp.float32)
            for text in range(texts):
                slope = side[text * ROWS : (text + 1) * ROWS].astype(jnp.float32)
                total += side_grad[text : text + 1] * slope
            update.append(total)
        at = pl.multiple_of((lax.div(shard, 2) ^ (o // 2)) * width, LANES)
        up_ref[:, pl.ds(at, width)] = update[0] + update[1]


def any_spec():
    return pl.BlockSpec(memory_space=pl.ANY)


def vmem_spec():
    return pl.BlockSpec(memory_space=pltpu.VMEM)


def smem_spec():
    return pl.BlockSpec(memory_space=pltpu.SMEM)


def exchange(x, axis, size):
    steps = [[(i, i ^ o) for i in range(size)] for o in range(1, size)]
    return [x] + [lax.ppermute(x, axis, step) for step in steps]


def split_body(
    query_passage_words,
    difficult_distractors,
    vocabulary_vectors,
    layer_weight_matrix,
    lowering_factor_matrix,
    raising_factor_matrix,
    logit_sharpness,
):
    shards, parts = lax.axis_size("dp"), lax.axis_size("mp")
    texts, length = query_passage_words.shape[1:]
    ids = query_passage_words.reshape(texts, 1, length)
    tokens = texts * length
    features, vocab = vocabulary_vectors.shape
    blocks = vocab // IDS_PER_BLOCK
    group_rows = 8 * pl.cdiv(vocab // IDS_PER_GROUP + 1, 8)
    per_shard, negatives = difficult_distractors.shape
    part_width = layer_weight_matrix.shape[1]
    width = part_width // shards
    params = pltpu.CompilerParams(vmem_limit_bytes=LARGE_VMEM)
    modest = pltpu.CompilerParams(vmem_limit_bytes=MODEST_VMEM)
    other_core = [(d, d ^ 1) for d in range(shards)]
    other_y = [(d, d ^ 2) for d in range(shards)]

    def project(base, span):
        stripes = pl.cdiv(span, STRIPE)
        extra_rows = (stripes + 1 + shards) * ROWS
        turned, member, *weights = pl.pallas_call(
            functools.partial(gather_kernel, base=base),
            out_shape=[
                jax.ShapeDtypeStruct((features, span), jnp.bfloat16),
                jax.ShapeDtypeStruct((span, LANES), jnp.bfloat16),
                *[jax.ShapeDtypeStruct((features, width), jnp.bfloat16)] * 4,
            ],
            in_specs=[vmem_spec()] + [any_spec()] * 2,
            out_specs=[any_spec()] * 6,
            scratch_shapes=[
                pltpu.VMEM((features, span), jnp.bfloat16),
                pltpu.VMEM((span, LANES), jnp.bfloat16),
                pltpu.VMEM((blocks, features, IDS_PER_BLOCK), jnp.bfloat16),
                pltpu.VMEM((8 * pl.cdiv(span // LANES, 8), LANES), jnp.int32),
                pltpu.VMEM((texts, length), jnp.int32),
                pltpu.VMEM((texts, length), jnp.float32),
                pltpu.VMEM((group_rows, length), jnp.int32),
                pltpu.SMEM((group_rows, length), jnp.int32),
                pltpu.SemaphoreType.DMA((blocks,)),
                pltpu.SemaphoreType.DMA,
                pltpu.SemaphoreType.DMA((2,)),
                pltpu.SemaphoreType.DMA((4,)),
            ],
            compiler_params=params,
            name="gather",
        )(ids, vocabulary_vectors, layer_weight_matrix)

        def product(turned, weight):
            return mm(turned, weight, (((0,), (0,)), ((), ())))

        def narrow(x):
            return x.astype(jnp.bfloat16)

        core1 = lax.ppermute(narrow(product(turned, weights[3])), "dp", other_core)
        chip1 = narrow(product(turned, weights[1]) + core1.astype(jnp.float32))
        far = lax.ppermute(chip1, "dp", other_y)
        turned, _ = lax.optimization_barrier((turned, chip1))
        extra = pl.pallas_call(
            statistics_kernel,
            out_shape=jax.ShapeDtypeStruct((extra_rows, STRIPE), jnp.bfloat16),
            in_specs=[any_spec()] * 2 + [vmem_spec()] * 2,
            out_specs=vmem_spec(),
            scratch_shapes=[
                pltpu.VMEM((LANES, LANES), jnp.float32),
                pltpu.VMEM(turned.shape, turned.dtype),
                pltpu.VMEM(member.shape, member.dtype),
                pltpu.VMEM((ROWS, features), jnp.float32),
                pltpu.SemaphoreType.DMA((2,)),
            ],
            compiler_params=modest,
            cost_estimate=pl.CostEstimate(
                flops=2 * features * span * (ROWS + LANES),
                bytes_accessed=2 * features * span,
                transcendentals=0,
            ),
            name="statistics",
        )(turned, member, difficult_distractors, lowering_factor_matrix)
        common = (stripes + 1) * ROWS
        near = extra.astype(jnp.float32)
        across = lax.ppermute(extra, "dp", other_core).astype(jnp.float32)
        chip = near[0:common] + across[0:common]
        inputs = near[common : common + 2 * ROWS] + across[common + 2 * ROWS :]
        sent = narrow(jnp.concatenate([chip, inputs[ROWS:]]))
        sent = lax.ppermute(sent, "dp", other_y).astype(jnp.float32)
        extra = jnp.concatenate([chip, inputs[0:ROWS]]) + sent
        core0 = lax.ppermute(narrow(product(turned, weights[2])), "dp", other_core)
        own0 = narrow(product(turned, weights[0]))
        return own0, core0, far, extra, member

    first = project(0, FIRST)
    later, _ = lax.optimization_barrier((ids, first[0]))
    many = jnp.sum((later != 0).astype(jnp.int32)) > FIRST
    left = tokens - FIRST
    shapes = jax.eval_shape(lambda: project(FIRST, left))
    rest = lax.cond(
        many,
        lambda: project(FIRST, left),
        lambda: tuple(jnp.zeros(x.shape, x.dtype) for x in shapes),
    )
    sent, misc = pl.pallas_call(
        functools.partial(pool_kernel, model_width=float(features * shards)),
        out_shape=[
            jax.ShapeDtypeStruct(((texts + 1) * ROWS, width), jnp.bfloat16),
            jax.ShapeDtypeStruct((ROWS, width), jnp.float32),
        ],
        in_specs=[vmem_spec()] * 2 + [any_spec()] * 2 + [vmem_spec()] * 8,
        out_specs=[vmem_spec()] * 2,
        scratch_shapes=[
            pltpu.VMEM((LANES, width), jnp.bfloat16),
            pltpu.VMEM((ROWS, width), jnp.float32),
            pltpu.VMEM((texts * ROWS, width), jnp.float32),
            pltpu.VMEM((FIRST, width), jnp.bfloat16),
            pltpu.VMEM((FIRST, width), jnp.bfloat16),
            pltpu.SemaphoreType.DMA((2,)),
        ],
        compiler_params=modest,
        name="pool",
    )(ids, *first, *rest, raising_factor_matrix)
    far_side = lax.ppermute(sent, "group", [(0, 1), (1, 0)])
    rows = 2 * ROWS
    packed, slopes = pl.pallas_call(
        dots_kernel,
        out_shape=[
            jax.ShapeDtypeStruct((rows + width // LANES * rows, LANES), jnp.float32),
            jax.ShapeDtypeStruct((2 * texts * ROWS, width), jnp.bfloat16),
        ],
        in_specs=[vmem_spec()] * 2,
        out_specs=[vmem_spec()] * 2,
        compiler_params=modest,
        name="dots",
    )(sent, far_side)
    packed = exchange(packed, "dp", shards)
    dots = [x[0:rows] for x in packed]
    dots = (dots[0] + dots[1]) + (dots[2] + dots[3])
    slopes, dots = lax.optimization_barrier((slopes, dots))
    dots = exchange(dots, "mp", parts)
    slopes = [slopes, lax.ppermute(slopes, "dp", other_y)]
    embeddings, losses, update = pl.pallas_call(
        functools.partial(
            score_kernel, texts=texts, stripes=pl.cdiv(FIRST, STRIPE), negatives=negatives
        ),
        out_shape=[
            jax.ShapeDtypeStruct((1, per_shard, part_width), jnp.bfloat16),
            jax.ShapeDtypeStruct((1, per_shard), jnp.float32),
            jax.ShapeDtypeStruct((ROWS, part_width // 2), jnp.float32),
        ],
        in_specs=[vmem_spec()] * 11 + [smem_spec()],
        out_specs=[vmem_spec()] * 3,
        compiler_params=modest,
        name="score",
    )(*packed, *slopes, *dots, misc, logit_sharpness)
    other = lax.ppermute(update, "dp", other_core)
    core = lax.rem(lax.axis_index("dp"), 2)
    halves = [jnp.where(core == 0, update, other), jnp.where(core == 0, other, update)]
    return (embeddings, losses, jnp.concatenate(halves, axis=1))


def body(words, hard, vocabulary, weight, lowering, raising, sharpness):
    shards, parts = lax.axis_size("dp"), lax.axis_size("mp")
    texts, length = words.shape[1:]
    features, vocab = vocabulary.shape
    negatives = hard.shape[1]
    square = shards == 4 and features == weight.shape[1] == 4 * STRIPE and parts == shards
    small = texts <= ROWS - 2 and length == LANES and FIRST < texts * length <= 2048
    even = (texts * length - FIRST) % CHUNK == 0 and vocab % IDS_PER_BLOCK == 0
    fits = features * vocab <= 2**24 and features % (4 * LANES) == 0
    spare = pl.cdiv(FIRST, STRIPE) + negatives <= ROWS and lowering.shape[0] == ROWS
    fast = square and small and even and fits and spare and lax.axis_size("group") == 2
    chosen = split_body if fast else general_body
    return chosen(words, hard, vocabulary, weight, lowering, raising, sharpness)


def solution(mesh):
    in_specs = (
        P("group", None, None),
        P("dp", None),
        P("dp", None),
        P("dp", "mp"),
        P(),
        P(None, "mp"),
        P(),
    )
    out_specs = (P("group", "dp", "mp"), P("group", "dp"), P(None, "mp"))
    return jax.shard_map(body, mesh=mesh, in_specs=in_specs, out_specs=out_specs, check_vma=False)
```

```python
import functools

import jax
import jax.numpy as jnp
from jax import lax
from jax.experimental import pallas as pl
from jax.experimental.pallas import tpu as pltpu
from jax.sharding import PartitionSpec as P


def general_body(
    query_passage_words,
    difficult_distractors,
    vocabulary_vectors,
    layer_weight_matrix,
    lowering_factor_matrix,
    raising_factor_matrix,
    logit_sharpness,
):
    group_index = lax.axis_index("group")
    shard_index = lax.axis_index("dp")
    part_index = lax.axis_index("mp")
    shard_count = lax.axis_size("dp")
    side_ids = query_passage_words[0]
    text_count = side_ids.shape[0]
    length = side_ids.shape[1]
    per_shard = text_count // shard_count
    own_ids = lax.dynamic_slice_in_dim(side_ids, shard_index * per_shard, per_shard, 0)
    columns = jnp.take(vocabulary_vectors, side_ids.reshape(-1), axis=1)
    inputs = lax.all_to_all(columns, "dp", split_axis=1, concat_axis=0, tiled=True)
    tokens = inputs.shape[1]
    feature_width = raising_factor_matrix.shape[1]
    wide_inputs = inputs.astype(jnp.float32)
    inverse = lax.rsqrt(jnp.mean(wide_inputs * wide_inputs, axis=0) + 1e-05)
    normed_state = (wide_inputs * inverse[None, :]).astype(jnp.bfloat16)
    linear_map = lax.dot_general(
        lax.all_gather(layer_weight_matrix, "dp", axis=0, tiled=True),
        normed_state,
        (((0,), (0,)), ((), ())),
        preferred_element_type=jnp.float32,
    )
    reduced_sum = jnp.dot(
        lowering_factor_matrix, normed_state, preferred_element_type=jnp.float32
    ).astype(jnp.bfloat16)
    linear_map = linear_map + lax.dot_general(
        raising_factor_matrix,
        reduced_sum,
        (((0,), (0,)), ((), ())),
        preferred_element_type=jnp.float32,
    )
    own_inputs = lax.dynamic_slice_in_dim(
        inputs, part_index * feature_width, feature_width, 0
    ).astype(jnp.float32)
    hidden_state = own_inputs + jax.nn.silu(linear_map)
    mask = (own_ids != 0).astype(jnp.float32)
    counts = jnp.sum(mask, axis=1)
    summed = jnp.einsum("dnl,nl->nd", hidden_state.reshape(feature_width, per_shard, length), mask)
    pooled = (summed / counts[:, None]).astype(jnp.bfloat16)
    gathered = lax.all_gather(pooled, ("group", "dp"), axis=0, tiled=True)
    part_scores = lax.dot_general(
        pooled, gathered, (((1,), (1,)), ((), ())), preferred_element_type=jnp.float32
    )
    gathered_wide = gathered.astype(jnp.float32)
    part_norms = jnp.sum(gathered_wide * gathered_wide, axis=1)
    dots, norms = lax.psum((part_scores, part_norms), "mp")
    rnorm_all = lax.rsqrt(norms + 1e-06)
    all_count = gathered.shape[0]
    half_count = all_count // 2
    own_rows = (
        group_index * half_count + shard_index * per_shard + jnp.arange(per_shard, dtype=jnp.int32)
    )
    rnorm_own = jnp.take(rnorm_all, own_rows)
    cosine = dots * rnorm_own[:, None] * rnorm_all[None, :]
    multiplier_factor = logit_sharpness[0]
    scores = multiplier_factor * cosine
    column_ids = jnp.arange(all_count, dtype=jnp.int32)
    keep = column_ids[None, :] != own_rows[:, None]
    pair = (own_rows + half_count) % all_count
    weight = (group_index == 0).astype(jnp.float32)
    neg_cols = half_count + difficult_distractors
    top = jnp.max(jnp.where(keep, scores, -jnp.inf), axis=1)
    safe_scores = jnp.where(keep, scores, top[:, None])
    expd = jnp.where(keep, jnp.exp(safe_scores - top[:, None]), 0.0)
    neg_exp = (
        jnp.exp(jnp.minimum(jnp.take_along_axis(scores, neg_cols, axis=1) - top[:, None], 0.0))
        * weight
    )
    total = jnp.sum(expd, axis=1) + jnp.sum(neg_exp, axis=1)
    pair_score = jnp.take_along_axis(scores, pair[:, None], axis=1)[:, 0]
    losses = top + jnp.log(total) - pair_score
    onehot = (column_ids[None, None, :] == neg_cols[:, :, None]).astype(jnp.float32)
    probs = (expd + jnp.einsum("rk,rkc->rc", neg_exp, onehot)) / total[:, None]
    target = (column_ids[None, :] == pair[:, None]).astype(jnp.float32)
    grad_scores = (probs - target) / all_count
    coeff = (grad_scores * rnorm_own[:, None] * rnorm_all[None, :]).astype(jnp.bfloat16)
    along = jnp.dot(coeff, gathered, preferred_element_type=jnp.float32)
    pooled_wide = pooled.astype(jnp.float32)
    radial = jnp.sum(grad_scores * cosine, axis=1) * rnorm_own * rnorm_own
    embedding_gradient = multiplier_factor * (along - radial[:, None] * pooled_wide)
    token_grad = jnp.einsum("nd,nl->dnl", embedding_gradient / counts[:, None], mask).reshape(
        feature_width, tokens
    )
    sigma = jax.nn.sigmoid(linear_map)
    local = (token_grad * sigma * (1.0 + linear_map * (1.0 - sigma))).astype(jnp.bfloat16)
    up_portion = lax.dot_general(
        reduced_sum, local, (((1,), (1,)), ((), ())), preferred_element_type=jnp.float32
    )
    adapter_up_gradient = lax.psum(up_portion, ("group", "dp"))
    embeddings = (pooled_wide * rnorm_own[:, None]).astype(jnp.bfloat16)[None]
    return (embeddings, losses[None], adapter_up_gradient)


BLOCK_BITS, GROUP_BITS, LANE_BITS, ROW_BITS = 10, 9, 7, 4
IDS_PER_BLOCK = 1 << BLOCK_BITS
IDS_PER_GROUP = 1 << GROUP_BITS
CHUNK = 384
STRIPE = 256
ROWS = 1 << ROW_BITS
LANES = 1 << LANE_BITS
FEATURE_ROWS = 128
FIRST = 1152
TAKEN = 768
NT = (((1,), (1,)), ((), ()))
LARGE_VMEM, MODEST_VMEM = 44 * 1024 * 1024, 15 * 1024 * 1024


def mm(a, b, dims=(((1,), (0,)), ((), ()))):
    return lax.dot_general(a, b, dims, preferred_element_type=jnp.float32)


def split(x):
    high = x.astype(jnp.bfloat16)
    return high, (x - high.astype(jnp.float32)).astype(jnp.bfloat16)


def iota(shape, dim):
    return lax.broadcasted_iota(jnp.int32, shape, dim)


def quarter_of(dp_index, cores=2):
    return (dp_index % cores) * 2 + dp_index // cores


def split_quarter(i, j, cores=2):
    shard = lax.axis_index("dp")
    core, side_y = lax.rem(shard, cores), lax.div(shard, cores)
    return (core ^ i) * 2 + (side_y ^ j)


def take_lanes(x, lanes):
    numbers = lax.GatherDimensionNumbers(
        offset_dims=(),
        collapsed_slice_dims=(1,),
        start_index_map=(1,),
        operand_batching_dims=(0,),
        start_indices_batching_dims=(0,),
    )
    mode = lax.GatherScatterMode.PROMISE_IN_BOUNDS
    return lax.gather(x, lanes[..., None], numbers, slice_sizes=(1, 1), mode=mode)


def load_ids(ref):
    return jnp.concatenate([ref[text] for text in range(ref.shape[0])], axis=0)


def fetch(pairs, sems):
    copies = [pltpu.make_async_copy(a, b, sems.at[n]) for n, (a, b) in enumerate(pairs)]
    for copy in copies:
        copy.start()
    for copy in copies:
        copy.wait()


def gather_kernel(
    ids_ref,
    vocab_ref,
    weight_ref,
    turned_any,
    member_any,
    weight00,
    weight01,
    weight10,
    weight11,
    turned,
    member_ref,
    held,
    token_ref,
    plain_ids,
    ranks,
    counted,
    bounds,
    held_sems,
    bounds_sem,
    out_sems,
    weight_sems,
    base,
):
    texts, _, length = ids_ref.shape
    features, vocab = vocab_ref.shape
    blocks = vocab // IDS_PER_BLOCK
    groups = vocab // IDS_PER_GROUP
    span = member_ref.shape[0]

    def vocab_copy(b):
        columns = pl.ds(pl.multiple_of(b * IDS_PER_BLOCK, LANES), IDS_PER_BLOCK)
        return pltpu.make_async_copy(vocab_ref.at[:, columns], held.at[b], held_sems.at[b])

    weight_copies = []
    for q, weight in enumerate((weight00, weight01, weight10, weight11)):
        width = weight.shape[1]
        start = pl.multiple_of(split_quarter(q // 2, q % 2) * width, LANES)
        copy = pltpu.make_async_copy(
            weight_ref.at[:, pl.ds(start, width)], weight, weight_sems.at[q]
        )
        weight_copies.append(copy)
    vocab_copy(0).start()
    for b in range(1, blocks):
        vocab_copy(b).start()
    for copy in weight_copies:
        copy.start()

    for text in range(texts):
        plain_ids[pl.ds(text, 1), :] = ids_ref[text]
    ids = plain_ids[...]
    valid = ids != 0
    group_of = jnp.where(valid, lax.shift_right_logical(ids, GROUP_BITS), groups)
    group_rows = counted.shape[0]
    group_id = iota((group_rows, length), 0)
    below = jnp.zeros((group_rows, length), jnp.float32)
    for text in range(texts):
        below += jnp.where(group_of[text : text + 1] < group_id, 1.0, 0.0)
    before = jnp.broadcast_to(jnp.sum(below, axis=1, keepdims=True), (group_rows, length))
    counted[...] = before.astype(jnp.int32)
    bounds_copy = pltpu.make_async_copy(counted, bounds, bounds_sem)
    bounds_copy.start()
    earlier = jnp.where(iota((length, length), 0) < iota((length, length), 1), 1.0, 0.0).astype(
        jnp.bfloat16
    )
    for text in range(texts):
        here = jnp.where(group_of[text : text + 1] == group_id, 1.0, 0.0)
        inside = mm(here.astype(jnp.bfloat16), earlier)
        ranks[pl.ds(text, 1), :] = jnp.sum(here * (inside + before), axis=0, keepdims=True)
        before += jnp.broadcast_to(jnp.sum(here, axis=1, keepdims=True), (group_rows, length))
    text_of = iota((texts, length), 0)
    carried = jnp.where(valid, lax.shift_left(ids, ROW_BITS) + text_of, 0).astype(jnp.float32)
    rank = ranks[...]

    def place(p, carry):
        position = (iota((LANES, length), 0) + (p * LANES + base)).astype(jnp.float32)
        total = jnp.zeros((LANES, length), jnp.float32)
        for text in range(texts):
            total += jnp.where(rank[text : text + 1] == position, carried[text : text + 1], 0.0)
        found = jnp.broadcast_to(jnp.sum(total, axis=1, keepdims=True), (LANES, LANES))
        start = pl.multiple_of(p * LANES, LANES)
        row = found.T[0:1].astype(jnp.int32)
        token = lax.shift_right_logical(row, ROW_BITS)
        token_ref[pl.ds(p, 1), :] = jnp.where(token == 0, -vocab, token)
        found = found.astype(jnp.int32)
        real = (found >= ROWS) & ((found & (ROWS - 1)) == iota((LANES, LANES), 1))
        member_ref[pl.ds(start, LANES), :] = jnp.where(real, 1.0, 0.0).astype(jnp.bfloat16)
        turned[:, pl.ds(start, LANES)] = jnp.zeros((features, LANES), jnp.bfloat16)
        return carry

    lax.fori_loop(0, span // LANES, place, 0)
    bounds_copy.wait()

    def within(place):
        return jnp.clip(place - base, 0, span)

    def take(b, carry):
        vocab_copy(b).wait()
        for part in range(IDS_PER_BLOCK // IDS_PER_GROUP):
            group = b * (IDS_PER_BLOCK // IDS_PER_GROUP) + part
            first, last = within(bounds[group, 0]), within(bounds[group + 1, 0])
            begin = lax.shift_right_logical(first, LANE_BITS)
            end = lax.shift_right_logical(last + LANES - 1, LANE_BITS)

            def window(p, carry):
                at = pl.ds(pl.multiple_of(p * LANES, LANES), LANES)
                token = token_ref[pl.ds(p, 1), :] - group * IDS_PER_GROUP
                token = jnp.broadcast_to(token, (FEATURE_ROWS, LANES))
                lane = (token & (LANES - 1)).astype(jnp.int16)
                tile = lax.shift_right_arithmetic(token, LANE_BITS).astype(jnp.int16)
                pieces = [pl.ds(f, FEATURE_ROWS) for f in range(0, TAKEN, FEATURE_ROWS)]
                short = jnp.broadcast_to(token[0:1], (IDS_PER_GROUP, LANES)).astype(jnp.int16)
                picked = jnp.where(
                    short == iota((IDS_PER_GROUP, LANES), 0).astype(jnp.int16), 1.0, 0.0
                ).astype(jnp.bfloat16)
                columns = pl.ds(part * IDS_PER_GROUP, IDS_PER_GROUP)
                rest = pl.ds(TAKEN, features - TAKEN)
                product = mm(held[b, rest, columns], picked).astype(jnp.bfloat16)
                fresh = []
                for rows in pieces:
                    total = jnp.zeros((FEATURE_ROWS, LANES), jnp.bfloat16)
                    for j in range(IDS_PER_GROUP // LANES):
                        columns = pl.ds(part * IDS_PER_GROUP + j * LANES, LANES)
                        total = jnp.where(tile == j, take_lanes(held[b, rows, columns], lane), total)
                    fresh.append(total)
                pieces.append(rest)
                fresh.append(product)
                fresh = [turned[rows, at] + total for rows, total in zip(pieces, fresh)]
                for rows, total in zip(pieces, fresh):
                    turned[rows, at] = total
                return carry

            lax.fori_loop(begin, jnp.where(last > first, end, begin), window, 0)
        return carry

    lax.fori_loop(0, blocks, take, 0)
    fetch([(turned, turned_any), (member_ref, member_any)], out_sems)
    for copy in weight_copies:
        copy.wait()


def statistics_kernel(
    turned_any, member_any, hard_ref, lower_ref, extra_ref, small, turned, member_ref, spread, sems
):
    fetch([(turned_any, turned), (member_any, member_ref)], sems)
    features, span = turned.shape
    stripes = pl.cdiv(span, STRIPE)
    per_shard, negatives = hard_ref.shape
    shard = lax.axis_index("dp")
    small[...] = jnp.zeros_like(small)
    small[0:per_shard, stripes : stripes + negatives] = hard_ref[...].astype(jnp.float32)
    lower = lower_ref[:, pl.ds(pl.multiple_of(shard * features, LANES), features)]

    misc = jnp.zeros((ROWS, STRIPE), jnp.float32)
    residual = jnp.zeros((features, LANES), jnp.float32)
    for stripe in range(stripes):
        size = min(STRIPE, span - stripe * STRIPE)
        across = pl.ds(stripe * STRIPE, size)
        upright = turned[:, across]
        wide = upright.astype(jnp.float32)
        square = jnp.sum(wide * wide, axis=0, keepdims=True)
        reduced = mm(lower, upright)
        if size < STRIPE:
            none = jnp.zeros((ROWS, STRIPE - size), jnp.float32)
            reduced = jnp.concatenate([reduced, none], axis=1)
            square = jnp.concatenate([square, none[0:1]], axis=1)
        extra_ref[stripe * ROWS : (stripe + 1) * ROWS, :] = reduced.astype(jnp.bfloat16)
        misc = jnp.where(iota((ROWS, STRIPE), 0) == stripe, square, misc)
        residual += mm(upright, member_ref[across, :])
    hard = small[...].T[0:ROWS]
    for i in range(per_shard):
        misc += jnp.where(iota((ROWS, STRIPE), 1) == shard * per_shard + i, hard[:, i : i + 1], 0.0)
    extra_ref[stripes * ROWS : (stripes + 1) * ROWS, :] = misc.astype(jnp.bfloat16)
    residual = jnp.where(lax.axis_index("mp") == shard, residual.T[0:ROWS], 0.0)
    spread[...] = residual
    for q in range(4):
        start = (stripes + 1 + q) * ROWS
        quarter = pl.multiple_of(split_quarter(q // 2, q % 2) * STRIPE, LANES)
        extra_ref[start : start + ROWS, :] = spread[:, pl.ds(quarter, STRIPE)].astype(jnp.bfloat16)


def pool_kernel(
    ids_ref,
    own_ref,
    core_any,
    far_any,
    extra_ref,
    member_ref,
    own_rest,
    core_rest,
    far_rest,
    extra_rest,
    member_rest,
    raise_ref,
    sent_ref,
    misc_ref,
    raised,
    total,
    slopes,
    core_ref,
    far_ref,
    sems,
    model_width,
):
    texts = ids_ref.shape[0]
    width = own_ref.shape[1]
    quarter = quarter_of(lax.axis_index("dp"))
    fetch([(core_any, core_ref), (far_any, far_ref)], sems)
    raised[...] = jnp.zeros_like(raised)
    raised[0:ROWS, :] = raise_ref[:, pl.ds(pl.multiple_of(quarter * width, LANES), width)]
    total[...] = jnp.zeros_like(total)
    slopes[...] = jnp.zeros_like(slopes)

    def add(refs, extra_ref, member_ref, base):
        span = member_ref.shape[0]
        stripes = pl.cdiv(span, STRIPE)

        def summed(start, size):
            return sum(ref[pl.ds(start, size), :].astype(jnp.float32) for ref in refs)

        misc = extra_ref[stripes * ROWS : (stripes + 1) * ROWS, :]
        if base == 0:
            misc_ref[...] = misc
        inverse = lax.rsqrt(misc / model_width + 1e-05)
        for k in range(stripes):
            size = min(STRIPE, span - k * STRIPE)
            scale = inverse[k : k + 1]
            reduced = (extra_ref[k * ROWS : (k + 1) * ROWS, :] * scale).astype(jnp.bfloat16)
            reduced = reduced.astype(jnp.float32)
            stacked = jnp.concatenate([reduced, jnp.broadcast_to(scale, (LANES - ROWS, STRIPE))])
            turned = stacked[:, 0:size].T
            low = turned.astype(jnp.bfloat16)
            linear = summed(k * STRIPE, size)
            linear = linear * turned[:, ROWS : ROWS + 1] + mm(low, raised[...])
            sigma = 1.0 / (1.0 + jnp.exp(-linear))
            slope = (sigma * (1.0 + linear * (1.0 - sigma))).astype(jnp.bfloat16)
            member = member_ref[pl.ds(k * STRIPE, size), :].astype(jnp.float32).T
            high, rest = split(linear * sigma)
            chosen = member[0:ROWS].astype(jnp.bfloat16)
            total[...] += mm(chosen, high) + mm(chosen, rest)
            spread = [reduced[:, 0:size] * member[text : text + 1] for text in range(texts)]
            slopes[...] += mm(jnp.concatenate(spread).astype(jnp.bfloat16), slope)
        total[...] += extra_ref[(stripes + 1) * ROWS : (stripes + 2) * ROWS, :]

    add((own_ref, core_ref, far_ref), extra_ref, member_ref, 0)
    real = (load_ids(ids_ref) != 0).astype(jnp.float32)

    @pl.when(jnp.sum(real) > member_ref.shape[0])
    def _():
        add((own_rest, core_rest, far_rest), extra_rest, member_rest, member_ref.shape[0])

    counts = jnp.sum(real, axis=1, keepdims=True)
    pooled = total[0:texts] / counts
    pooled = jnp.concatenate([pooled, jnp.zeros((ROWS - texts, width), jnp.float32)])
    sent_ref[0:ROWS, :] = pooled.astype(jnp.bfloat16)
    for text in range(texts):
        part = slopes[text * ROWS : (text + 1) * ROWS, :] / counts[text : text + 1]
        sent_ref[(text + 1) * ROWS : (text + 2) * ROWS, :] = part.astype(jnp.bfloat16)


def both_sides(near, far):
    queries = lax.axis_index("group") == 0
    return jnp.concatenate([jnp.where(queries, near, far), jnp.where(queries, far, near)], axis=0)


def dots_kernel(near_ref, far_ref, packed_ref, slopes_ref):
    block = both_sides(near_ref[0:ROWS], far_ref[0:ROWS])
    rows = 2 * ROWS
    packed_ref[...] = jnp.zeros_like(packed_ref)
    packed_ref[0:rows, 0:rows] = mm(block, block, NT)
    for part in range(block.shape[1] // LANES):
        piece = block[:, part * LANES : (part + 1) * LANES]
        packed_ref[rows + part * rows : rows + (part + 1) * rows, :] = piece.astype(jnp.float32)
    size = near_ref.shape[0] - ROWS
    slopes_ref[0:size] = near_ref[ROWS:]
    slopes_ref[size:] = far_ref[ROWS:]


def score_kernel(*refs, texts, stripes, negatives):
    packed0, packed1, packed2, packed3, slopes0, slopes2 = refs[0:6]
    dots0, dots1, misc_ref, sharp_ref = refs[6:10]
    embed_ref, loss_ref, up_ref = refs[10:13]
    rows = 2 * ROWS
    per_shard = loss_ref.shape[1]
    group, shard = lax.axis_index("group"), lax.axis_index("dp")
    dots = (dots0[...] + dots1[...])[:, 0:rows]
    down, across = iota((rows, rows), 0), iota((rows, rows), 1)
    same = down == across
    real = (lax.rem(down, ROWS) < texts) & (lax.rem(across, ROWS) < texts)
    diagonal = jnp.where(same, dots, 0.0)
    rnorm_row = lax.rsqrt(jnp.sum(diagonal, axis=0, keepdims=True) + 1e-06)
    rnorm_col = lax.rsqrt(jnp.sum(diagonal, axis=1, keepdims=True) + 1e-06)
    sharpness = sharp_ref[0]
    cosine = dots * rnorm_col * rnorm_row
    scores = sharpness * cosine
    keep = real & ~same
    top = jnp.max(jnp.where(keep, scores, -jnp.inf), axis=0, keepdims=True)
    top = jnp.where(lax.rem(across[0:1], ROWS) < texts, top, 0.0)
    powers = jnp.exp(jnp.where(real, jnp.minimum(scores - top, 0.0), 0.0))
    hard = misc_ref[stripes : stripes + negatives, 0:rows].astype(jnp.int32) + ROWS
    times = jnp.zeros((rows, rows), jnp.float32)
    for k in range(negatives):
        times += jnp.where(hard[k : k + 1] == down, 1.0, 0.0)
    times = jnp.where(across < texts, times, 0.0)
    weights = (jnp.where(keep, 1.0, 0.0) + jnp.where(real, times, 0.0)) * powers
    total = jnp.sum(weights, axis=0, keepdims=True)
    total = jnp.where(lax.rem(across[0:1], ROWS) < texts, total, 1.0)
    pair = (down == lax.rem(across + ROWS, rows)) & real
    pair_score = jnp.sum(jnp.where(pair, scores, 0.0), axis=0, keepdims=True)
    losses = top + jnp.log(total) - pair_score
    grad_scores = (weights / total - jnp.where(pair, 1.0, 0.0)) / (2 * texts)
    coeff = (grad_scores * rnorm_col * rnorm_row).astype(jnp.bfloat16)
    radial = jnp.sum(grad_scores * cosine, axis=0, keepdims=True) * rnorm_row * rnorm_row

    first = shard * per_shard
    loss_col = jnp.sum(jnp.where(same, losses, 0.0), axis=1, keepdims=True)
    at = (iota((rows, LANES), 0) == group * ROWS + first + iota((rows, LANES), 1)) & (
        iota((rows, LANES), 1) < per_shard
    )
    loss_ref[...] = jnp.sum(jnp.where(at, loss_col, 0.0), axis=0, keepdims=True)[:, 0:per_shard]

    along_rows = coeff.astype(jnp.float32).T.astype(jnp.bfloat16)
    radial_col = jnp.sum(jnp.where(same, radial, 0.0), axis=1, keepdims=True)
    rnorm_own = jnp.where(group == 0, rnorm_col[0:ROWS], rnorm_col[ROWS:rows])
    chosen = iota((ROWS, ROWS), 1) == iota((ROWS, ROWS), 0) + first
    chosen = jnp.where(chosen & (iota((ROWS, ROWS), 0) < per_shard), 1.0, 0.0).astype(jnp.bfloat16)
    blocks = ((packed0, slopes0), (packed1, None), (packed2, slopes2), (packed3, None))
    for o, (packed, slopes) in enumerate(blocks):
        parts = packed.shape[0] // rows - 1
        width = parts * LANES
        halves = [packed[rows * (part + 1) : rows * (part + 2), :] for part in range(parts)]
        block = jnp.concatenate(halves, axis=1)
        queries = group == 0
        at = pl.multiple_of(quarter_of(shard ^ o) * width, LANES)
        own = jnp.where(queries, block[0:ROWS], block[ROWS:rows]) * rnorm_own
        picked = mm(chosen, own.astype(jnp.bfloat16)).astype(jnp.bfloat16)
        embed_ref[0, :, pl.ds(at, width)] = picked[0:per_shard]
        if slopes is None:
            continue
        along = mm(along_rows, block.astype(jnp.bfloat16))
        grad = sharpness * (along - radial_col * block)
        near, far = slopes[0 : slopes.shape[0] // 2], slopes[slopes.shape[0] // 2 :]
        grad_near = jnp.where(queries, grad[0:ROWS], grad[ROWS:rows])
        grad_far = jnp.where(queries, grad[ROWS:rows], grad[0:ROWS])
        update = []
        for side, side_grad in ((near, grad_near), (far, grad_far)):
            total = jnp.zeros((ROWS, width), jnp.float32)
            for text in range(texts):
                slope = side[text * ROWS : (text + 1) * ROWS].astype(jnp.float32)
                total += side_grad[text : text + 1] * slope
            update.append(total)
        at = pl.multiple_of((lax.div(shard, 2) ^ (o // 2)) * width, LANES)
        up_ref[:, pl.ds(at, width)] = update[0] + update[1]


def any_spec():
    return pl.BlockSpec(memory_space=pl.ANY)


def vmem_spec():
    return pl.BlockSpec(memory_space=pltpu.VMEM)


def smem_spec():
    return pl.BlockSpec(memory_space=pltpu.SMEM)


def exchange(x, axis, size):
    steps = [[(i, i ^ o) for i in range(size)] for o in range(1, size)]
    return [x] + [lax.ppermute(x, axis, step) for step in steps]


def split_body(
    query_passage_words,
    difficult_distractors,
    vocabulary_vectors,
    layer_weight_matrix,
    lowering_factor_matrix,
    raising_factor_matrix,
    logit_sharpness,
):
    shards, parts = lax.axis_size("dp"), lax.axis_size("mp")
    texts, length = query_passage_words.shape[1:]
    ids = query_passage_words.reshape(texts, 1, length)
    tokens = texts * length
    features, vocab = vocabulary_vectors.shape
    blocks = vocab // IDS_PER_BLOCK
    group_rows = 8 * pl.cdiv(vocab // IDS_PER_GROUP + 1, 8)
    per_shard, negatives = difficult_distractors.shape
    part_width = layer_weight_matrix.shape[1]
    width = part_width // shards
    params = pltpu.CompilerParams(vmem_limit_bytes=LARGE_VMEM)
    modest = pltpu.CompilerParams(vmem_limit_bytes=MODEST_VMEM)
    other_core = [(d, d ^ 1) for d in range(shards)]
    other_y = [(d, d ^ 2) for d in range(shards)]

    def project(base, span):
        stripes = pl.cdiv(span, STRIPE)
        extra_rows = (stripes + 1 + shards) * ROWS
        turned, member, *weights = pl.pallas_call(
            functools.partial(gather_kernel, base=base),
            out_shape=[
                jax.ShapeDtypeStruct((features, span), jnp.bfloat16),
                jax.ShapeDtypeStruct((span, LANES), jnp.bfloat16),
                *[jax.ShapeDtypeStruct((features, width), jnp.bfloat16)] * 4,
            ],
            in_specs=[vmem_spec()] + [any_spec()] * 2,
            out_specs=[any_spec()] * 6,
            scratch_shapes=[
                pltpu.VMEM((features, span), jnp.bfloat16),
                pltpu.VMEM((span, LANES), jnp.bfloat16),
                pltpu.VMEM((blocks, features, IDS_PER_BLOCK), jnp.bfloat16),
                pltpu.VMEM((8 * pl.cdiv(span // LANES, 8), LANES), jnp.int32),
                pltpu.VMEM((texts, length), jnp.int32),
                pltpu.VMEM((texts, length), jnp.float32),
                pltpu.VMEM((group_rows, length), jnp.int32),
                pltpu.SMEM((group_rows, length), jnp.int32),
                pltpu.SemaphoreType.DMA((blocks,)),
                pltpu.SemaphoreType.DMA,
                pltpu.SemaphoreType.DMA((2,)),
                pltpu.SemaphoreType.DMA((4,)),
            ],
            compiler_params=params,
            name="gather",
        )(ids, vocabulary_vectors, layer_weight_matrix)

        def product(turned, weight):
            return mm(turned, weight, (((0,), (0,)), ((), ())))

        def narrow(x):
            return x.astype(jnp.bfloat16)

        core1 = lax.ppermute(narrow(product(turned, weights[3])), "dp", other_core)
        chip1 = narrow(product(turned, weights[1]) + core1.astype(jnp.float32))
        far = lax.ppermute(chip1, "dp", other_y)
        turned, _ = lax.optimization_barrier((turned, chip1))
        extra = pl.pallas_call(
            statistics_kernel,
            out_shape=jax.ShapeDtypeStruct((extra_rows, STRIPE), jnp.bfloat16),
            in_specs=[any_spec()] * 2 + [vmem_spec()] * 2,
            out_specs=vmem_spec(),
            scratch_shapes=[
                pltpu.VMEM((LANES, LANES), jnp.float32),
                pltpu.VMEM(turned.shape, turned.dtype),
                pltpu.VMEM(member.shape, member.dtype),
                pltpu.VMEM((ROWS, features), jnp.float32),
                pltpu.SemaphoreType.DMA((2,)),
            ],
            compiler_params=modest,
            cost_estimate=pl.CostEstimate(
                flops=2 * features * span * (ROWS + LANES),
                bytes_accessed=2 * features * span,
                transcendentals=0,
            ),
            name="statistics",
        )(turned, member, difficult_distractors, lowering_factor_matrix)
        common = (stripes + 1) * ROWS
        near = extra.astype(jnp.float32)
        across = lax.ppermute(extra, "dp", other_core).astype(jnp.float32)
        chip = near[0:common] + across[0:common]
        inputs = near[common : common + 2 * ROWS] + across[common + 2 * ROWS :]
        sent = narrow(jnp.concatenate([chip, inputs[ROWS:]]))
        sent = lax.ppermute(sent, "dp", other_y).astype(jnp.float32)
        extra = jnp.concatenate([chip, inputs[0:ROWS]]) + sent
        core0 = lax.ppermute(narrow(product(turned, weights[2])), "dp", other_core)
        own0 = narrow(product(turned, weights[0]))
        return own0, core0, far, extra, member

    first = project(0, FIRST)
    later, _ = lax.optimization_barrier((ids, first[0]))
    many = jnp.sum((later != 0).astype(jnp.int32)) > FIRST
    left = tokens - FIRST
    shapes = jax.eval_shape(lambda: project(FIRST, left))
    rest = lax.cond(
        many,
        lambda: project(FIRST, left),
        lambda: tuple(jnp.zeros(x.shape, x.dtype) for x in shapes),
    )
    sent, misc = pl.pallas_call(
        functools.partial(pool_kernel, model_width=float(features * shards)),
        out_shape=[
            jax.ShapeDtypeStruct(((texts + 1) * ROWS, width), jnp.bfloat16),
            jax.ShapeDtypeStruct((ROWS, width), jnp.float32),
        ],
        in_specs=[vmem_spec()] * 2 + [any_spec()] * 2 + [vmem_spec()] * 8,
        out_specs=[vmem_spec()] * 2,
        scratch_shapes=[
            pltpu.VMEM((LANES, width), jnp.bfloat16),
            pltpu.VMEM((ROWS, width), jnp.float32),
            pltpu.VMEM((texts * ROWS, width), jnp.float32),
            pltpu.VMEM((FIRST, width), jnp.bfloat16),
            pltpu.VMEM((FIRST, width), jnp.bfloat16),
            pltpu.SemaphoreType.DMA((2,)),
        ],
        compiler_params=modest,
        name="pool",
    )(ids, *first, *rest, raising_factor_matrix)
    far_side = lax.ppermute(sent, "group", [(0, 1), (1, 0)])
    rows = 2 * ROWS
    packed, slopes = pl.pallas_call(
        dots_kernel,
        out_shape=[
            jax.ShapeDtypeStruct((rows + width // LANES * rows, LANES), jnp.float32),
            jax.ShapeDtypeStruct((2 * texts * ROWS, width), jnp.bfloat16),
        ],
        in_specs=[vmem_spec()] * 2,
        out_specs=[vmem_spec()] * 2,
        compiler_params=modest,
        name="dots",
    )(sent, far_side)
    packed = exchange(packed, "dp", shards)
    dots = [x[0:rows] for x in packed]
    dots = (dots[0] + dots[1]) + (dots[2] + dots[3])
    slopes, dots = lax.optimization_barrier((slopes, dots))
    dots = dots + lax.ppermute(dots, "mp", [(i, i ^ 1) for i in range(parts)])
    dots = [dots, lax.ppermute(dots, "mp", [(i, i ^ 2) for i in range(parts)])]
    slopes = [slopes, lax.ppermute(slopes, "dp", other_y)]
    embeddings, losses, update = pl.pallas_call(
        functools.partial(
            score_kernel, texts=texts, stripes=pl.cdiv(FIRST, STRIPE), negatives=negatives
        ),
        out_shape=[
            jax.ShapeDtypeStruct((1, per_shard, part_width), jnp.bfloat16),
            jax.ShapeDtypeStruct((1, per_shard), jnp.float32),
            jax.ShapeDtypeStruct((ROWS, part_width // 2), jnp.float32),
        ],
        in_specs=[vmem_spec()] * 9 + [smem_spec()],
        out_specs=[vmem_spec()] * 3,
        compiler_params=modest,
        name="score",
    )(*packed, *slopes, *dots, misc, logit_sharpness)
    other = lax.ppermute(update, "dp", other_core)
    core = lax.rem(lax.axis_index("dp"), 2)
    halves = [jnp.where(core == 0, update, other), jnp.where(core == 0, other, update)]
    return (embeddings, losses, jnp.concatenate(halves, axis=1))


def body(words, hard, vocabulary, weight, lowering, raising, sharpness):
    shards, parts = lax.axis_size("dp"), lax.axis_size("mp")
    texts, length = words.shape[1:]
    features, vocab = vocabulary.shape
    negatives = hard.shape[1]
    square = shards == 4 and features == weight.shape[1] == 4 * STRIPE and parts == shards
    small = texts <= ROWS - 2 and length == LANES and FIRST < texts * length <= 2048
    even = (texts * length - FIRST) % CHUNK == 0 and vocab % IDS_PER_BLOCK == 0
    fits = features * vocab <= 2**24 and features % (4 * LANES) == 0
    spare = pl.cdiv(FIRST, STRIPE) + negatives <= ROWS and lowering.shape[0] == ROWS
    fast = square and small and even and fits and spare and lax.axis_size("group") == 2
    chosen = split_body if fast else general_body
    return chosen(words, hard, vocabulary, weight, lowering, raising, sharpness)


def solution(mesh):
    in_specs = (
        P("group", None, None),
        P("dp", None),
        P("dp", None),
        P("dp", "mp"),
        P(),
        P(None, "mp"),
        P(),
    )
    out_specs = (P("group", "dp", "mp"), P("group", "dp"), P(None, "mp"))
    return jax.shard_map(body, mesh=mesh, in_specs=in_specs, out_specs=out_specs, check_vma=False)
```

```python
import functools

import jax
import jax.numpy as jnp
from jax import lax
from jax.experimental import pallas as pl
from jax.experimental.pallas import tpu as pltpu
from jax.sharding import PartitionSpec as P


def general_body(
    query_passage_words,
    difficult_distractors,
    vocabulary_vectors,
    layer_weight_matrix,
    lowering_factor_matrix,
    raising_factor_matrix,
    logit_sharpness,
):
    group_index = lax.axis_index("group")
    shard_index = lax.axis_index("dp")
    part_index = lax.axis_index("mp")
    shard_count = lax.axis_size("dp")
    side_ids = query_passage_words[0]
    text_count = side_ids.shape[0]
    length = side_ids.shape[1]
    per_shard = text_count // shard_count
    own_ids = lax.dynamic_slice_in_dim(side_ids, shard_index * per_shard, per_shard, 0)
    columns = jnp.take(vocabulary_vectors, side_ids.reshape(-1), axis=1)
    inputs = lax.all_to_all(columns, "dp", split_axis=1, concat_axis=0, tiled=True)
    tokens = inputs.shape[1]
    feature_width = raising_factor_matrix.shape[1]
    wide_inputs = inputs.astype(jnp.float32)
    inverse = lax.rsqrt(jnp.mean(wide_inputs * wide_inputs, axis=0) + 1e-05)
    normed_state = (wide_inputs * inverse[None, :]).astype(jnp.bfloat16)
    linear_map = lax.dot_general(
        lax.all_gather(layer_weight_matrix, "dp", axis=0, tiled=True),
        normed_state,
        (((0,), (0,)), ((), ())),
        preferred_element_type=jnp.float32,
    )
    reduced_sum = jnp.dot(
        lowering_factor_matrix, normed_state, preferred_element_type=jnp.float32
    ).astype(jnp.bfloat16)
    linear_map = linear_map + lax.dot_general(
        raising_factor_matrix,
        reduced_sum,
        (((0,), (0,)), ((), ())),
        preferred_element_type=jnp.float32,
    )
    own_inputs = lax.dynamic_slice_in_dim(
        inputs, part_index * feature_width, feature_width, 0
    ).astype(jnp.float32)
    hidden_state = own_inputs + jax.nn.silu(linear_map)
    mask = (own_ids != 0).astype(jnp.float32)
    counts = jnp.sum(mask, axis=1)
    summed = jnp.einsum("dnl,nl->nd", hidden_state.reshape(feature_width, per_shard, length), mask)
    pooled = (summed / counts[:, None]).astype(jnp.bfloat16)
    gathered = lax.all_gather(pooled, ("group", "dp"), axis=0, tiled=True)
    part_scores = lax.dot_general(
        pooled, gathered, (((1,), (1,)), ((), ())), preferred_element_type=jnp.float32
    )
    gathered_wide = gathered.astype(jnp.float32)
    part_norms = jnp.sum(gathered_wide * gathered_wide, axis=1)
    dots, norms = lax.psum((part_scores, part_norms), "mp")
    rnorm_all = lax.rsqrt(norms + 1e-06)
    all_count = gathered.shape[0]
    half_count = all_count // 2
    own_rows = (
        group_index * half_count + shard_index * per_shard + jnp.arange(per_shard, dtype=jnp.int32)
    )
    rnorm_own = jnp.take(rnorm_all, own_rows)
    cosine = dots * rnorm_own[:, None] * rnorm_all[None, :]
    multiplier_factor = logit_sharpness[0]
    scores = multiplier_factor * cosine
    column_ids = jnp.arange(all_count, dtype=jnp.int32)
    keep = column_ids[None, :] != own_rows[:, None]
    pair = (own_rows + half_count) % all_count
    weight = (group_index == 0).astype(jnp.float32)
    neg_cols = half_count + difficult_distractors
    top = jnp.max(jnp.where(keep, scores, -jnp.inf), axis=1)
    safe_scores = jnp.where(keep, scores, top[:, None])
    expd = jnp.where(keep, jnp.exp(safe_scores - top[:, None]), 0.0)
    neg_exp = (
        jnp.exp(jnp.minimum(jnp.take_along_axis(scores, neg_cols, axis=1) - top[:, None], 0.0))
        * weight
    )
    total = jnp.sum(expd, axis=1) + jnp.sum(neg_exp, axis=1)
    pair_score = jnp.take_along_axis(scores, pair[:, None], axis=1)[:, 0]
    losses = top + jnp.log(total) - pair_score
    onehot = (column_ids[None, None, :] == neg_cols[:, :, None]).astype(jnp.float32)
    probs = (expd + jnp.einsum("rk,rkc->rc", neg_exp, onehot)) / total[:, None]
    target = (column_ids[None, :] == pair[:, None]).astype(jnp.float32)
    grad_scores = (probs - target) / all_count
    coeff = (grad_scores * rnorm_own[:, None] * rnorm_all[None, :]).astype(jnp.bfloat16)
    along = jnp.dot(coeff, gathered, preferred_element_type=jnp.float32)
    pooled_wide = pooled.astype(jnp.float32)
    radial = jnp.sum(grad_scores * cosine, axis=1) * rnorm_own * rnorm_own
    embedding_gradient = multiplier_factor * (along - radial[:, None] * pooled_wide)
    token_grad = jnp.einsum("nd,nl->dnl", embedding_gradient / counts[:, None], mask).reshape(
        feature_width, tokens
    )
    sigma = jax.nn.sigmoid(linear_map)
    local = (token_grad * sigma * (1.0 + linear_map * (1.0 - sigma))).astype(jnp.bfloat16)
    up_portion = lax.dot_general(
        reduced_sum, local, (((1,), (1,)), ((), ())), preferred_element_type=jnp.float32
    )
    adapter_up_gradient = lax.psum(up_portion, ("group", "dp"))
    embeddings = (pooled_wide * rnorm_own[:, None]).astype(jnp.bfloat16)[None]
    return (embeddings, losses[None], adapter_up_gradient)


BLOCK_BITS, GROUP_BITS, LANE_BITS, ROW_BITS = 10, 8, 7, 4
IDS_PER_BLOCK = 1 << BLOCK_BITS
IDS_PER_GROUP = 1 << GROUP_BITS
CHUNK = 384
STRIPE = 256
ROWS = 1 << ROW_BITS
LANES = 1 << LANE_BITS
FEATURE_ROWS = 128
FIRST = 1152
TAKEN = 768
NT = (((1,), (1,)), ((), ()))
LARGE_VMEM, MODEST_VMEM = 44 * 1024 * 1024, 15 * 1024 * 1024


def mm(a, b, dims=(((1,), (0,)), ((), ()))):
    return lax.dot_general(a, b, dims, preferred_element_type=jnp.float32)


def split(x):
    high = x.astype(jnp.bfloat16)
    return high, (x - high.astype(jnp.float32)).astype(jnp.bfloat16)


def iota(shape, dim):
    return lax.broadcasted_iota(jnp.int32, shape, dim)


def quarter_of(dp_index, cores=2):
    return (dp_index % cores) * 2 + dp_index // cores


def split_quarter(i, j, cores=2):
    shard = lax.axis_index("dp")
    core, side_y = lax.rem(shard, cores), lax.div(shard, cores)
    return (core ^ i) * 2 + (side_y ^ j)


def take_lanes(x, lanes):
    numbers = lax.GatherDimensionNumbers(
        offset_dims=(),
        collapsed_slice_dims=(1,),
        start_index_map=(1,),
        operand_batching_dims=(0,),
        start_indices_batching_dims=(0,),
    )
    mode = lax.GatherScatterMode.PROMISE_IN_BOUNDS
    return lax.gather(x, lanes[..., None], numbers, slice_sizes=(1, 1), mode=mode)


def load_ids(ref):
    return jnp.concatenate([ref[text] for text in range(ref.shape[0])], axis=0)


def fetch(pairs, sems):
    copies = [pltpu.make_async_copy(a, b, sems.at[n]) for n, (a, b) in enumerate(pairs)]
    for copy in copies:
        copy.start()
    for copy in copies:
        copy.wait()


def gather_kernel(
    ids_ref,
    vocab_ref,
    weight_ref,
    turned_any,
    member_any,
    weight00,
    weight01,
    weight10,
    weight11,
    turned,
    member_ref,
    held,
    token_ref,
    plain_ids,
    ranks,
    counted,
    bounds,
    held_sems,
    bounds_sem,
    out_sems,
    weight_sems,
    base,
):
    texts, _, length = ids_ref.shape
    features, vocab = vocab_ref.shape
    blocks = vocab // IDS_PER_BLOCK
    groups = vocab // IDS_PER_GROUP
    span = member_ref.shape[0]

    def vocab_copy(b):
        columns = pl.ds(pl.multiple_of(b * IDS_PER_BLOCK, LANES), IDS_PER_BLOCK)
        return pltpu.make_async_copy(vocab_ref.at[:, columns], held.at[b], held_sems.at[b])

    weight_copies = []
    for q, weight in enumerate((weight00, weight01, weight10, weight11)):
        width = weight.shape[1]
        start = pl.multiple_of(split_quarter(q // 2, q % 2) * width, LANES)
        copy = pltpu.make_async_copy(
            weight_ref.at[:, pl.ds(start, width)], weight, weight_sems.at[q]
        )
        weight_copies.append(copy)
    vocab_copy(0).start()
    for b in range(1, blocks):
        vocab_copy(b).start()
    for copy in weight_copies:
        copy.start()

    for text in range(texts):
        plain_ids[pl.ds(text, 1), :] = ids_ref[text]
    ids = plain_ids[...]
    valid = ids != 0
    group_of = jnp.where(valid, lax.shift_right_logical(ids, GROUP_BITS), groups)
    group_rows = counted.shape[0]
    group_id = iota((group_rows, length), 0)
    below = jnp.zeros((group_rows, length), jnp.float32)
    for text in range(texts):
        below += jnp.where(group_of[text : text + 1] < group_id, 1.0, 0.0)
    before = jnp.broadcast_to(jnp.sum(below, axis=1, keepdims=True), (group_rows, length))
    counted[...] = before.astype(jnp.int32)
    bounds_copy = pltpu.make_async_copy(counted, bounds, bounds_sem)
    bounds_copy.start()
    earlier = jnp.where(iota((length, length), 0) < iota((length, length), 1), 1.0, 0.0).astype(
        jnp.bfloat16
    )
    for text in range(texts):
        here = jnp.where(group_of[text : text + 1] == group_id, 1.0, 0.0)
        inside = mm(here.astype(jnp.bfloat16), earlier)
        ranks[pl.ds(text, 1), :] = jnp.sum(here * (inside + before), axis=0, keepdims=True)
        before += jnp.broadcast_to(jnp.sum(here, axis=1, keepdims=True), (group_rows, length))
    text_of = iota((texts, length), 0)
    carried = jnp.where(valid, lax.shift_left(ids, ROW_BITS) + text_of, 0).astype(jnp.float32)
    rank = ranks[...]

    def place(p, carry):
        position = (iota((LANES, length), 0) + (p * LANES + base)).astype(jnp.float32)
        total = jnp.zeros((LANES, length), jnp.float32)
        for text in range(texts):
            total += jnp.where(rank[text : text + 1] == position, carried[text : text + 1], 0.0)
        found = jnp.broadcast_to(jnp.sum(total, axis=1, keepdims=True), (LANES, LANES))
        start = pl.multiple_of(p * LANES, LANES)
        row = found.T[0:1].astype(jnp.int32)
        token = lax.shift_right_logical(row, ROW_BITS)
        token_ref[pl.ds(p, 1), :] = jnp.where(token == 0, -vocab, token)
        found = found.astype(jnp.int32)
        real = (found >= ROWS) & ((found & (ROWS - 1)) == iota((LANES, LANES), 1))
        member_ref[pl.ds(start, LANES), :] = jnp.where(real, 1.0, 0.0).astype(jnp.bfloat16)
        turned[:, pl.ds(start, LANES)] = jnp.zeros((features, LANES), jnp.bfloat16)
        return carry

    lax.fori_loop(0, span // LANES, place, 0)
    bounds_copy.wait()

    def within(place):
        return jnp.clip(place - base, 0, span)

    def take(b, carry):
        vocab_copy(b).wait()
        for part in range(IDS_PER_BLOCK // IDS_PER_GROUP):
            group = b * (IDS_PER_BLOCK // IDS_PER_GROUP) + part
            first, last = within(bounds[group, 0]), within(bounds[group + 1, 0])
            begin = lax.shift_right_logical(first, LANE_BITS)
            end = lax.shift_right_logical(last + LANES - 1, LANE_BITS)

            def window(p, carry):
                at = pl.ds(pl.multiple_of(p * LANES, LANES), LANES)
                token = token_ref[pl.ds(p, 1), :] - group * IDS_PER_GROUP
                token = jnp.broadcast_to(token, (FEATURE_ROWS, LANES))
                lane = (token & (LANES - 1)).astype(jnp.int16)
                tile = lax.shift_right_arithmetic(token, LANE_BITS).astype(jnp.int16)
                pieces = [pl.ds(f, FEATURE_ROWS) for f in range(0, TAKEN, FEATURE_ROWS)]
                short = jnp.broadcast_to(token[0:1], (IDS_PER_GROUP, LANES)).astype(jnp.int16)
                picked = jnp.where(
                    short == iota((IDS_PER_GROUP, LANES), 0).astype(jnp.int16), 1.0, 0.0
                ).astype(jnp.bfloat16)
                columns = pl.ds(part * IDS_PER_GROUP, IDS_PER_GROUP)
                rest = pl.ds(TAKEN, features - TAKEN)
                product = mm(held[b, rest, columns], picked).astype(jnp.bfloat16)
                fresh = []
                for rows in pieces:
                    total = jnp.zeros((FEATURE_ROWS, LANES), jnp.bfloat16)
                    for j in range(IDS_PER_GROUP // LANES):
                        columns = pl.ds(part * IDS_PER_GROUP + j * LANES, LANES)
                        total = jnp.where(tile == j, take_lanes(held[b, rows, columns], lane), total)
                    fresh.append(total)
                pieces.append(rest)
                fresh.append(product)
                fresh = [turned[rows, at] + total for rows, total in zip(pieces, fresh)]
                for rows, total in zip(pieces, fresh):
                    turned[rows, at] = total
                return carry

            lax.fori_loop(begin, jnp.where(last > first, end, begin), window, 0)
        return carry

    lax.fori_loop(0, blocks, take, 0)
    fetch([(turned, turned_any), (member_ref, member_any)], out_sems)
    for copy in weight_copies:
        copy.wait()


def statistics_kernel(
    turned_any, member_any, hard_ref, lower_ref, extra_ref, small, turned, member_ref, spread, sems
):
    fetch([(turned_any, turned), (member_any, member_ref)], sems)
    features, span = turned.shape
    stripes = pl.cdiv(span, STRIPE)
    per_shard, negatives = hard_ref.shape
    shard = lax.axis_index("dp")
    small[...] = jnp.zeros_like(small)
    small[0:per_shard, stripes : stripes + negatives] = hard_ref[...].astype(jnp.float32)
    lower = lower_ref[:, pl.ds(pl.multiple_of(shard * features, LANES), features)]

    misc = jnp.zeros((ROWS, STRIPE), jnp.float32)
    residual = jnp.zeros((features, LANES), jnp.float32)
    for stripe in range(stripes):
        size = min(STRIPE, span - stripe * STRIPE)
        across = pl.ds(stripe * STRIPE, size)
        upright = turned[:, across]
        wide = upright.astype(jnp.float32)
        square = jnp.sum(wide * wide, axis=0, keepdims=True)
        reduced = mm(lower, upright)
        if size < STRIPE:
            none = jnp.zeros((ROWS, STRIPE - size), jnp.float32)
            reduced = jnp.concatenate([reduced, none], axis=1)
            square = jnp.concatenate([square, none[0:1]], axis=1)
        extra_ref[stripe * ROWS : (stripe + 1) * ROWS, :] = reduced.astype(jnp.bfloat16)
        misc = jnp.where(iota((ROWS, STRIPE), 0) == stripe, square, misc)
        residual += mm(upright, member_ref[across, :])
    hard = small[...].T[0:ROWS]
    for i in range(per_shard):
        misc += jnp.where(iota((ROWS, STRIPE), 1) == shard * per_shard + i, hard[:, i : i + 1], 0.0)
    extra_ref[stripes * ROWS : (stripes + 1) * ROWS, :] = misc.astype(jnp.bfloat16)
    residual = jnp.where(lax.axis_index("mp") == shard, residual.T[0:ROWS], 0.0)
    spread[...] = residual
    for q in range(4):
        start = (stripes + 1 + q) * ROWS
        quarter = pl.multiple_of(split_quarter(q // 2, q % 2) * STRIPE, LANES)
        extra_ref[start : start + ROWS, :] = spread[:, pl.ds(quarter, STRIPE)].astype(jnp.bfloat16)


def pool_kernel(
    ids_ref,
    own_ref,
    core_any,
    far_any,
    extra_ref,
    member_ref,
    own_rest,
    core_rest,
    far_rest,
    extra_rest,
    member_rest,
    raise_ref,
    sent_ref,
    misc_ref,
    raised,
    total,
    slopes,
    core_ref,
    far_ref,
    sems,
    model_width,
):
    texts = ids_ref.shape[0]
    width = own_ref.shape[1]
    quarter = quarter_of(lax.axis_index("dp"))
    fetch([(core_any, core_ref), (far_any, far_ref)], sems)
    raised[...] = jnp.zeros_like(raised)
    raised[0:ROWS, :] = raise_ref[:, pl.ds(pl.multiple_of(quarter * width, LANES), width)]
    total[...] = jnp.zeros_like(total)
    slopes[...] = jnp.zeros_like(slopes)

    def add(refs, extra_ref, member_ref, base):
        span = member_ref.shape[0]
        stripes = pl.cdiv(span, STRIPE)

        def summed(start, size):
            return sum(ref[pl.ds(start, size), :].astype(jnp.float32) for ref in refs)

        misc = extra_ref[stripes * ROWS : (stripes + 1) * ROWS, :]
        if base == 0:
            misc_ref[...] = misc
        inverse = lax.rsqrt(misc / model_width + 1e-05)
        for k in range(stripes):
            size = min(STRIPE, span - k * STRIPE)
            scale = inverse[k : k + 1]
            reduced = (extra_ref[k * ROWS : (k + 1) * ROWS, :] * scale).astype(jnp.bfloat16)
            reduced = reduced.astype(jnp.float32)
            stacked = jnp.concatenate([reduced, jnp.broadcast_to(scale, (LANES - ROWS, STRIPE))])
            turned = stacked[:, 0:size].T
            low = turned.astype(jnp.bfloat16)
            linear = summed(k * STRIPE, size)
            linear = linear * turned[:, ROWS : ROWS + 1] + mm(low, raised[...])
            sigma = 1.0 / (1.0 + jnp.exp(-linear))
            slope = (sigma * (1.0 + linear * (1.0 - sigma))).astype(jnp.bfloat16)
            member = member_ref[pl.ds(k * STRIPE, size), :].astype(jnp.float32).T
            high, rest = split(linear * sigma)
            chosen = member[0:ROWS].astype(jnp.bfloat16)
            total[...] += mm(chosen, high) + mm(chosen, rest)
            spread = [reduced[:, 0:size] * member[text : text + 1] for text in range(texts)]
            slopes[...] += mm(jnp.concatenate(spread).astype(jnp.bfloat16), slope)
        total[...] += extra_ref[(stripes + 1) * ROWS : (stripes + 2) * ROWS, :]

    add((own_ref, core_ref, far_ref), extra_ref, member_ref, 0)
    real = (load_ids(ids_ref) != 0).astype(jnp.float32)

    @pl.when(jnp.sum(real) > member_ref.shape[0])
    def _():
        add((own_rest, core_rest, far_rest), extra_rest, member_rest, member_ref.shape[0])

    counts = jnp.sum(real, axis=1, keepdims=True)
    pooled = total[0:texts] / counts
    pooled = jnp.concatenate([pooled, jnp.zeros((ROWS - texts, width), jnp.float32)])
    sent_ref[0:ROWS, :] = pooled.astype(jnp.bfloat16)
    for text in range(texts):
        part = slopes[text * ROWS : (text + 1) * ROWS, :] / counts[text : text + 1]
        sent_ref[(text + 1) * ROWS : (text + 2) * ROWS, :] = part.astype(jnp.bfloat16)


def both_sides(near, far):
    queries = lax.axis_index("group") == 0
    return jnp.concatenate([jnp.where(queries, near, far), jnp.where(queries, far, near)], axis=0)


def dots_kernel(near_ref, far_ref, packed_ref, slopes_ref):
    block = both_sides(near_ref[0:ROWS], far_ref[0:ROWS])
    rows = 2 * ROWS
    packed_ref[...] = jnp.zeros_like(packed_ref)
    packed_ref[0:rows, 0:rows] = mm(block, block, NT)
    for part in range(block.shape[1] // LANES):
        piece = block[:, part * LANES : (part + 1) * LANES]
        packed_ref[rows + part * rows : rows + (part + 1) * rows, :] = piece.astype(jnp.float32)
    size = near_ref.shape[0] - ROWS
    slopes_ref[0:size] = near_ref[ROWS:]
    slopes_ref[size:] = far_ref[ROWS:]


def score_kernel(*refs, texts, stripes, negatives):
    packed0, packed1, packed2, packed3, slopes0, slopes2 = refs[0:6]
    dots0, dots1, misc_ref, sharp_ref = refs[6:10]
    embed_ref, loss_ref, up_ref = refs[10:13]
    rows = 2 * ROWS
    per_shard = loss_ref.shape[1]
    group, shard = lax.axis_index("group"), lax.axis_index("dp")
    dots = (dots0[...] + dots1[...])[:, 0:rows]
    down, across = iota((rows, rows), 0), iota((rows, rows), 1)
    same = down == across
    real = (lax.rem(down, ROWS) < texts) & (lax.rem(across, ROWS) < texts)
    diagonal = jnp.where(same, dots, 0.0)
    rnorm_row = lax.rsqrt(jnp.sum(diagonal, axis=0, keepdims=True) + 1e-06)
    rnorm_col = lax.rsqrt(jnp.sum(diagonal, axis=1, keepdims=True) + 1e-06)
    sharpness = sharp_ref[0]
    cosine = dots * rnorm_col * rnorm_row
    scores = sharpness * cosine
    keep = real & ~same
    top = jnp.max(jnp.where(keep, scores, -jnp.inf), axis=0, keepdims=True)
    top = jnp.where(lax.rem(across[0:1], ROWS) < texts, top, 0.0)
    powers = jnp.exp(jnp.where(real, jnp.minimum(scores - top, 0.0), 0.0))
    hard = misc_ref[stripes : stripes + negatives, 0:rows].astype(jnp.int32) + ROWS
    times = jnp.zeros((rows, rows), jnp.float32)
    for k in range(negatives):
        times += jnp.where(hard[k : k + 1] == down, 1.0, 0.0)
    times = jnp.where(across < texts, times, 0.0)
    weights = (jnp.where(keep, 1.0, 0.0) + jnp.where(real, times, 0.0)) * powers
    total = jnp.sum(weights, axis=0, keepdims=True)
    total = jnp.where(lax.rem(across[0:1], ROWS) < texts, total, 1.0)
    pair = (down == lax.rem(across + ROWS, rows)) & real
    pair_score = jnp.sum(jnp.where(pair, scores, 0.0), axis=0, keepdims=True)
    losses = top + jnp.log(total) - pair_score
    grad_scores = (weights / total - jnp.where(pair, 1.0, 0.0)) / (2 * texts)
    coeff = (grad_scores * rnorm_col * rnorm_row).astype(jnp.bfloat16)
    radial = jnp.sum(grad_scores * cosine, axis=0, keepdims=True) * rnorm_row * rnorm_row

    first = shard * per_shard
    loss_col = jnp.sum(jnp.where(same, losses, 0.0), axis=1, keepdims=True)
    at = (iota((rows, LANES), 0) == group * ROWS + first + iota((rows, LANES), 1)) & (
        iota((rows, LANES), 1) < per_shard
    )
    loss_ref[...] = jnp.sum(jnp.where(at, loss_col, 0.0), axis=0, keepdims=True)[:, 0:per_shard]

    along_rows = coeff.astype(jnp.float32).T.astype(jnp.bfloat16)
    radial_col = jnp.sum(jnp.where(same, radial, 0.0), axis=1, keepdims=True)
    rnorm_own = jnp.where(group == 0, rnorm_col[0:ROWS], rnorm_col[ROWS:rows])
    chosen = iota((ROWS, ROWS), 1) == iota((ROWS, ROWS), 0) + first
    chosen = jnp.where(chosen & (iota((ROWS, ROWS), 0) < per_shard), 1.0, 0.0).astype(jnp.bfloat16)
    blocks = ((packed0, slopes0), (packed1, None), (packed2, slopes2), (packed3, None))
    for o, (packed, slopes) in enumerate(blocks):
        parts = packed.shape[0] // rows - 1
        width = parts * LANES
        halves = [packed[rows * (part + 1) : rows * (part + 2), :] for part in range(parts)]
        block = jnp.concatenate(halves, axis=1)
        queries = group == 0
        at = pl.multiple_of(quarter_of(shard ^ o) * width, LANES)
        own = jnp.where(queries, block[0:ROWS], block[ROWS:rows]) * rnorm_own
        picked = mm(chosen, own.astype(jnp.bfloat16)).astype(jnp.bfloat16)
        embed_ref[0, :, pl.ds(at, width)] = picked[0:per_shard]
        if slopes is None:
            continue
        along = mm(along_rows, block.astype(jnp.bfloat16))
        grad = sharpness * (along - radial_col * block)
        near, far = slopes[0 : slopes.shape[0] // 2], slopes[slopes.shape[0] // 2 :]
        grad_near = jnp.where(queries, grad[0:ROWS], grad[ROWS:rows])
        grad_far = jnp.where(queries, grad[ROWS:rows], grad[0:ROWS])
        update = []
        for side, side_grad in ((near, grad_near), (far, grad_far)):
            total = jnp.zeros((ROWS, width), jnp.float32)
            for text in range(texts):
                slope = side[text * ROWS : (text + 1) * ROWS].astype(jnp.float32)
                total += side_grad[text : text + 1] * slope
            update.append(total)
        at = pl.multiple_of((lax.div(shard, 2) ^ (o // 2)) * width, LANES)
        up_ref[:, pl.ds(at, width)] = update[0] + update[1]


def any_spec():
    return pl.BlockSpec(memory_space=pl.ANY)


def vmem_spec():
    return pl.BlockSpec(memory_space=pltpu.VMEM)


def smem_spec():
    return pl.BlockSpec(memory_space=pltpu.SMEM)


def exchange(x, axis, size):
    steps = [[(i, i ^ o) for i in range(size)] for o in range(1, size)]
    return [x] + [lax.ppermute(x, axis, step) for step in steps]


def split_body(
    query_passage_words,
    difficult_distractors,
    vocabulary_vectors,
    layer_weight_matrix,
    lowering_factor_matrix,
    raising_factor_matrix,
    logit_sharpness,
):
    shards, parts = lax.axis_size("dp"), lax.axis_size("mp")
    texts, length = query_passage_words.shape[1:]
    ids = query_passage_words.reshape(texts, 1, length)
    tokens = texts * length
    features, vocab = vocabulary_vectors.shape
    blocks = vocab // IDS_PER_BLOCK
    group_rows = 8 * pl.cdiv(vocab // IDS_PER_GROUP + 1, 8)
    per_shard, negatives = difficult_distractors.shape
    part_width = layer_weight_matrix.shape[1]
    width = part_width // shards
    params = pltpu.CompilerParams(vmem_limit_bytes=LARGE_VMEM)
    modest = pltpu.CompilerParams(vmem_limit_bytes=MODEST_VMEM)
    other_core = [(d, d ^ 1) for d in range(shards)]
    other_y = [(d, d ^ 2) for d in range(shards)]

    def project(base, span):
        stripes = pl.cdiv(span, STRIPE)
        extra_rows = (stripes + 1 + shards) * ROWS
        turned, member, *weights = pl.pallas_call(
            functools.partial(gather_kernel, base=base),
            out_shape=[
                jax.ShapeDtypeStruct((features, span), jnp.bfloat16),
                jax.ShapeDtypeStruct((span, LANES), jnp.bfloat16),
                *[jax.ShapeDtypeStruct((features, width), jnp.bfloat16)] * 4,
            ],
            in_specs=[vmem_spec()] + [any_spec()] * 2,
            out_specs=[any_spec()] * 6,
            scratch_shapes=[
                pltpu.VMEM((features, span), jnp.bfloat16),
                pltpu.VMEM((span, LANES), jnp.bfloat16),
                pltpu.VMEM((blocks, features, IDS_PER_BLOCK), jnp.bfloat16),
                pltpu.VMEM((8 * pl.cdiv(span // LANES, 8), LANES), jnp.int32),
                pltpu.VMEM((texts, length), jnp.int32),
                pltpu.VMEM((texts, length), jnp.float32),
                pltpu.VMEM((group_rows, length), jnp.int32),
                pltpu.SMEM((group_rows, length), jnp.int32),
                pltpu.SemaphoreType.DMA((blocks,)),
                pltpu.SemaphoreType.DMA,
                pltpu.SemaphoreType.DMA((2,)),
                pltpu.SemaphoreType.DMA((4,)),
            ],
            compiler_params=params,
            name="gather",
        )(ids, vocabulary_vectors, layer_weight_matrix)

        def product(turned, weight):
            return mm(turned, weight, (((0,), (0,)), ((), ())))

        def narrow(x):
            return x.astype(jnp.bfloat16)

        core1 = lax.ppermute(narrow(product(turned, weights[3])), "dp", other_core)
        chip1 = narrow(product(turned, weights[1]) + core1.astype(jnp.float32))
        far = lax.ppermute(chip1, "dp", other_y)
        turned, _ = lax.optimization_barrier((turned, chip1))
        extra = pl.pallas_call(
            statistics_kernel,
            out_shape=jax.ShapeDtypeStruct((extra_rows, STRIPE), jnp.bfloat16),
            in_specs=[any_spec()] * 2 + [vmem_spec()] * 2,
            out_specs=vmem_spec(),
            scratch_shapes=[
                pltpu.VMEM((LANES, LANES), jnp.float32),
                pltpu.VMEM(turned.shape, turned.dtype),
                pltpu.VMEM(member.shape, member.dtype),
                pltpu.VMEM((ROWS, features), jnp.float32),
                pltpu.SemaphoreType.DMA((2,)),
            ],
            compiler_params=modest,
            cost_estimate=pl.CostEstimate(
                flops=2 * features * span * (ROWS + LANES),
                bytes_accessed=2 * features * span,
                transcendentals=0,
            ),
            name="statistics",
        )(turned, member, difficult_distractors, lowering_factor_matrix)
        common = (stripes + 1) * ROWS
        near = extra.astype(jnp.float32)
        across = lax.ppermute(extra, "dp", other_core).astype(jnp.float32)
        chip = near[0:common] + across[0:common]
        inputs = near[common : common + 2 * ROWS] + across[common + 2 * ROWS :]
        sent = narrow(jnp.concatenate([chip, inputs[ROWS:]]))
        sent = lax.ppermute(sent, "dp", other_y).astype(jnp.float32)
        extra = jnp.concatenate([chip, inputs[0:ROWS]]) + sent
        core0 = lax.ppermute(narrow(product(turned, weights[2])), "dp", other_core)
        own0 = narrow(product(turned, weights[0]))
        return own0, core0, far, extra, member

    first = project(0, FIRST)
    later, _ = lax.optimization_barrier((ids, first[0]))
    many = jnp.sum((later != 0).astype(jnp.int32)) > FIRST
    left = tokens - FIRST
    shapes = jax.eval_shape(lambda: project(FIRST, left))
    rest = lax.cond(
        many,
        lambda: project(FIRST, left),
        lambda: tuple(jnp.zeros(x.shape, x.dtype) for x in shapes),
    )
    sent, misc = pl.pallas_call(
        functools.partial(pool_kernel, model_width=float(features * shards)),
        out_shape=[
            jax.ShapeDtypeStruct(((texts + 1) * ROWS, width), jnp.bfloat16),
            jax.ShapeDtypeStruct((ROWS, width), jnp.float32),
        ],
        in_specs=[vmem_spec()] * 2 + [any_spec()] * 2 + [vmem_spec()] * 8,
        out_specs=[vmem_spec()] * 2,
        scratch_shapes=[
            pltpu.VMEM((LANES, width), jnp.bfloat16),
            pltpu.VMEM((ROWS, width), jnp.float32),
            pltpu.VMEM((texts * ROWS, width), jnp.float32),
            pltpu.VMEM((FIRST, width), jnp.bfloat16),
            pltpu.VMEM((FIRST, width), jnp.bfloat16),
            pltpu.SemaphoreType.DMA((2,)),
        ],
        compiler_params=modest,
        name="pool",
    )(ids, *first, *rest, raising_factor_matrix)
    far_side = lax.ppermute(sent, "group", [(0, 1), (1, 0)])
    rows = 2 * ROWS
    packed, slopes = pl.pallas_call(
        dots_kernel,
        out_shape=[
            jax.ShapeDtypeStruct((rows + width // LANES * rows, LANES), jnp.float32),
            jax.ShapeDtypeStruct((2 * texts * ROWS, width), jnp.bfloat16),
        ],
        in_specs=[vmem_spec()] * 2,
        out_specs=[vmem_spec()] * 2,
        compiler_params=modest,
        name="dots",
    )(sent, far_side)
    packed = exchange(packed, "dp", shards)
    dots = [x[0:rows] for x in packed]
    dots = (dots[0] + dots[1]) + (dots[2] + dots[3])
    slopes, dots = lax.optimization_barrier((slopes, dots))
    dots = dots + lax.ppermute(dots, "mp", [(i, i ^ 1) for i in range(parts)])
    dots = [dots, lax.ppermute(dots, "mp", [(i, i ^ 2) for i in range(parts)])]
    slopes = [slopes, lax.ppermute(slopes, "dp", other_y)]
    embeddings, losses, update = pl.pallas_call(
        functools.partial(
            score_kernel, texts=texts, stripes=pl.cdiv(FIRST, STRIPE), negatives=negatives
        ),
        out_shape=[
            jax.ShapeDtypeStruct((1, per_shard, part_width), jnp.bfloat16),
            jax.ShapeDtypeStruct((1, per_shard), jnp.float32),
            jax.ShapeDtypeStruct((ROWS, part_width // 2), jnp.float32),
        ],
        in_specs=[vmem_spec()] * 9 + [smem_spec()],
        out_specs=[vmem_spec()] * 3,
        compiler_params=modest,
        name="score",
    )(*packed, *slopes, *dots, misc, logit_sharpness)
    other = lax.ppermute(update, "dp", other_core)
    core = lax.rem(lax.axis_index("dp"), 2)
    halves = [jnp.where(core == 0, update, other), jnp.where(core == 0, other, update)]
    return (embeddings, losses, jnp.concatenate(halves, axis=1))


def body(words, hard, vocabulary, weight, lowering, raising, sharpness):
    shards, parts = lax.axis_size("dp"), lax.axis_size("mp")
    texts, length = words.shape[1:]
    features, vocab = vocabulary.shape
    negatives = hard.shape[1]
    square = shards == 4 and features == weight.shape[1] == 4 * STRIPE and parts == shards
    small = texts <= ROWS - 2 and length == LANES and FIRST < texts * length <= 2048
    even = (texts * length - FIRST) % CHUNK == 0 and vocab % IDS_PER_BLOCK == 0
    fits = features * vocab <= 2**24 and features % (4 * LANES) == 0
    spare = pl.cdiv(FIRST, STRIPE) + negatives <= ROWS and lowering.shape[0] == ROWS
    fast = square and small and even and fits and spare and lax.axis_size("group") == 2
    chosen = split_body if fast else general_body
    return chosen(words, hard, vocabulary, weight, lowering, raising, sharpness)


def solution(mesh):
    in_specs = (
        P("group", None, None),
        P("dp", None),
        P("dp", None),
        P("dp", "mp"),
        P(),
        P(None, "mp"),
        P(),
    )
    out_specs = (P("group", "dp", "mp"), P("group", "dp"), P(None, "mp"))
    return jax.shard_map(body, mesh=mesh, in_specs=in_specs, out_specs=out_specs, check_vma=False)
```
